32 devices in a mesh: seq: 16 (over z, y, x), mp: 2 (over core).
Axes of the slice: x: 2, y: 2, z: 4, core: 2. Of those that a mesh axis runs over, the one named last changes fastest.
Arguments:
- byte_states: bfloat16 [4096, 1024], P('seq'), may hold values from -6 to 6
- outer_gain: float32 [1024], replicated, may hold values from 0.1 to 1.9
- mamba_input: bfloat16 [1024, 1024], P(None, 'mp'), may hold values from -0.1875 to 0.1875
- mamba_step: bfloat16 [1024, 1024], P(None, 'mp'), may hold values from -0.1875 to 0.1875
- decay_rate: float32 [1024], P('mp'), as said below
- mixer_weight: bfloat16 [1024, 1024], P('mp'), may hold values from -0.1875 to 0.1875
- boundaries: int32 [16, 128], P('seq'), may hold values from 0 to 256, as said below
- span_counts: int32 [16], replicated, may hold values from 1 to 128, as said below
- up_weight: bfloat16 [1024, 4096], P('seq', 'mp'), may hold values from -0.1875 to 0.1875
- up_bias: float32 [4096], P('mp'), may hold values from -5 to 5
- inner_gain: float32 [4096], replicated, as said below
- query_weight: bfloat16 [4096, 4096], P('seq', 'mp'), as said below
- key_weight: bfloat16 [4096, 1024], P('seq', 'mp'), as said below
- value_weight: bfloat16 [4096, 1024], P('seq', 'mp'), may hold values from -0.09375 to 0.09375
- return_weight: bfloat16 [4096, 1024], P('mp'), may hold values from -0.09375 to 0.09375
Outputs:
- joined: bfloat16 [4096, 1024], P('seq', 'mp')
The draws below stay inside these ranges and needn't reach their ends.
Inputs may be any that keep to these rules, and one draw needn't show every extreme that they name: `boundaries`: row s lists the spans of shard s: its first span_counts[s] entries rise strictly from 0 and are byte positions within the shard; each span runs to the next entry, the last to the shard's end; the other entries equal 256. `span_counts`: the counts sum to 1024; some shard has exactly 128 spans. `decay_rate`: Positive. `inner_gain`: Positive. `query_weight`: Finite. `key_weight`: Finite.
All inputs are finite; a program needn't handle non-finite values.
Results may differ from the reference program's by a relative error of at most 0.01.
Values may be sent and summed in bfloat16 or wider, within the bound.
No kernel may reach another device: no remote copies, remote signals or barrier semaphores. Data moves between devices by JAX's collectives and lax.ppermute only.
A program may use at most 128 MiB of HBM per device.

```python
import math
import jax
import jax.numpy as jnp
from jax import lax

DO = 1024
DI = 4096
HEADS = 32
KV_HEADS = 8
HEAD = 128
ROWS = 256
CAP = 128
TOTAL = 1024
BYTES = 4096
N_SEQ = 16


def span_plan(key):
    plan_key = jax.random.fold_in(key, 71)
    special = jax.random.randint(jax.random.fold_in(plan_key, 1), (), 0, N_SEQ)
    weights = jax.random.randint(jax.random.fold_in(plan_key, 2), (N_SEQ,), 8, 17)
    shard_ids = jnp.arange(N_SEQ, dtype=jnp.int32)
    others = shard_ids != special
    weights = jnp.where(others, weights, 0)
    spare_rows = TOTAL - CAP - (N_SEQ - 1)
    shares = spare_rows * weights // jnp.sum(weights)
    leftover = spare_rows - jnp.sum(shares)
    other_rank = jnp.cumsum(others.astype(jnp.int32)) - 1
    extra_one = (others & (other_rank < leftover)).astype(jnp.int32)
    counts = jnp.where(others, 1 + shares + extra_one, CAP).astype(jnp.int32)

    def one_shard(shard_number, span_total):
        shuffled = jax.random.permutation(jax.random.fold_in(plan_key, 100 + shard_number), ROWS - 1)
        chosen = jnp.concatenate([jnp.ones((1,), bool), shuffled < span_total - 1])
        positions = jnp.where(chosen, jnp.arange(ROWS, dtype=jnp.int32), ROWS)
        return jnp.sort(positions)[:CAP].astype(jnp.int32)
    marks = jax.vmap(one_shard)(shard_ids, counts)
    return (counts, marks)


def draw_boundaries(key, part):
    return span_plan(key)[1]


def draw_span_counts(key, part):
    return span_plan(key)[0]


def draw_decay_rate(key, part):
    choose_slow = jax.random.randint(jax.random.fold_in(key, 3), (DO,), 0, 10)
    slow_mask = choose_slow < 5
    uniform_draw = jax.random.uniform(jax.random.fold_in(key, 4), (DO,), jnp.float32)
    slow_rate = jnp.exp(jnp.log(0.1 / BYTES) + uniform_draw * jnp.log(20.0))
    fast_rate = jnp.exp(jnp.log(1.0 / 50.0) + uniform_draw * jnp.log(50.0 / 30.0))
    return jnp.where(slow_mask, slow_rate, fast_rate).astype(jnp.float32)


def draw_inner_gain(key, part):
    uniform_draw = jax.random.uniform(jax.random.fold_in(key, 5), (DI,), jnp.float32)
    return (0.7 + 0.6 * uniform_draw).astype(jnp.float32)


def draw_up_bias(key, part):
    uniform_draw = jax.random.uniform(jax.random.fold_in(key, 21), (DI,), jnp.float32)
    return (2.0 * uniform_draw - 1.0).astype(jnp.float32)


def projection_base(key):
    return jax.random.truncated_normal(jax.random.fold_in(key, 31), -4.0, 4.0, (DI, KV_HEADS * HEAD), jnp.float32)


def draw_key_weight(key, part):
    return (projection_base(key) / math.sqrt(DI)).astype(jnp.bfloat16)


def draw_query_weight(key, part):
    noise = jax.random.truncated_normal(jax.random.fold_in(key, 32), -4.0, 4.0, (DI, HEADS * HEAD), jnp.float32)
    return (3.0 * noise / math.sqrt(DI)).astype(jnp.bfloat16)


def steps_of(stream_key, dims, cuts, least, largest):
    loudness, own = 1.0, jax.random.fold_in(stream_key, 6)
    for dim, shards_of in cuts:
        draws = jnp.exp(jax.random.uniform(jax.random.fold_in(own, dim), (shards_of,), jnp.float32, least / len(cuts), largest / len(cuts)))
        loudness = loudness * jnp.repeat(draws, dims[dim] // shards_of).reshape([-1 if axis == dim else 1 for axis in range(len(dims))])
    return loudness


def gaussian(key, dims, scale, most, shards=(), held_as=jnp.bfloat16):
    values = jax.random.normal(key, dims, jnp.float32) * scale
    if len(shards) > 0:
        values = steps_of(key, dims, shards, -0.22, 0.18) * values
    return jnp.clip(values, min=-most, max=most).astype(held_as)


def setup_inputs(seed: int = 0) -> dict:
    key_list = jax.random.split(jax.random.key(seed), 16)
    return {
        "byte_states": gaussian(key_list[0], (BYTES, DO), 1.0, 6.0, ((0, 16),)),
        "outer_gain": jnp.clip(1.0 + 0.18 * jax.random.normal(key_list[1], (DO,), jnp.float32), 0.1, 1.9),
        "mamba_input": gaussian(key_list[2], (DO, DO), DO ** -0.5, 0.1875, ((1, 2),)),
        "mamba_step": gaussian(key_list[3], (DO, DO), DO ** -0.5, 0.1875, ((1, 2),)),
        "decay_rate": draw_decay_rate(jax.random.fold_in(key_list[15], 71), 0),
        "mixer_weight": gaussian(key_list[5], (DO, DO), DO ** -0.5, 0.1875, ((0, 2),)),
        "boundaries": draw_boundaries(jax.random.fold_in(key_list[15], 71), 0),
        "span_counts": draw_span_counts(jax.random.fold_in(key_list[15], 71), 0),
        "up_weight": gaussian(key_list[8], (DO, DI), DO ** -0.5, 0.1875, ((0, 16), (1, 2))),
        "up_bias": draw_up_bias(jax.random.fold_in(key_list[15], 71), 0),
        "inner_gain": draw_inner_gain(jax.random.fold_in(key_list[15], 71), 0),
        "query_weight": draw_query_weight(jax.random.fold_in(key_list[15], 71), 0),
        "key_weight": draw_key_weight(jax.random.fold_in(key_list[15], 71), 0),
        "value_weight": gaussian(key_list[13], (DI, KV_HEADS * HEAD), DI ** -0.5, 0.09375, ((0, 16), (1, 2))),
        "return_weight": gaussian(key_list[14], (HEADS * HEAD, DO), (HEADS * HEAD) ** -0.5, 0.09375, ((0, 2),)),
    }


eps = 1e-05
masked = -1e+30

def rms_scale(values, gain):
    values = values.astype(jnp.float32)
    return values * lax.rsqrt(lax.optimization_barrier(jnp.mean(values * values, axis=-1, keepdims=True)) + eps) * gain

def advance(carried, factors):
    carried = factors[0] * carried + factors[1]
    return (carried, carried)

def reference(byte_states, outer_gain, mamba_input, mamba_step, decay_rate, mixer_weight, boundaries, span_counts, up_weight, up_bias, inner_gain, query_weight, key_weight, value_weight, return_weight):
    normed = rms_scale(byte_states, outer_gain).astype(jnp.bfloat16)
    inputs = jnp.dot(normed, mamba_input, preferred_element_type=jnp.float32)
    step_sizes = jax.nn.softplus(jnp.dot(normed, mamba_step, preferred_element_type=jnp.float32))
    rate_steps = step_sizes * decay_rate
    decays = jnp.exp(-rate_steps)
    drives = jnp.sqrt(-jnp.expm1(-2.0 * rate_steps)) * inputs
    _, states = lax.scan(advance, jnp.zeros((DO,), jnp.float32), (decays, drives))
    mixed_sum = jnp.dot(states.astype(jnp.bfloat16), mixer_weight, preferred_element_type=jnp.float32)
    encoded = (byte_states.astype(jnp.float32) + mixed_sum).astype(jnp.bfloat16)
    counts = span_counts.astype(jnp.int32)
    offsets = (jnp.cumsum(counts) - counts).astype(jnp.int32)
    slot_ids = jnp.arange(CAP, dtype=jnp.int32)
    live_slots = slot_ids[None, :] < counts[:, None]
    target = jnp.where(live_slots, offsets[:, None] + slot_ids[None, :], TOTAL).reshape(-1).astype(jnp.int32)
    shard_ids = jnp.arange(N_SEQ, dtype=jnp.int32)
    source_row = (shard_ids[:, None] * ROWS + jnp.minimum(boundaries, ROWS - 1)).reshape(-1).astype(jnp.int32)
    picked = jnp.zeros((TOTAL,), jnp.int32).at[target].set(source_row, mode='drop')
    pooled = encoded[picked]
    widened = (jnp.dot(pooled, up_weight, preferred_element_type=jnp.float32) + up_bias[None, :]).astype(jnp.bfloat16)
    inner_normed = rms_scale(widened, inner_gain).astype(jnp.bfloat16)
    queries = jnp.dot(inner_normed, query_weight, preferred_element_type=jnp.float32).astype(jnp.bfloat16)
    key_rows = jnp.dot(inner_normed, key_weight, preferred_element_type=jnp.float32).astype(jnp.bfloat16)
    value_rows = jnp.dot(inner_normed, value_weight, preferred_element_type=jnp.float32).astype(jnp.bfloat16)
    span_order = jnp.arange(TOTAL, dtype=jnp.int32)
    allowed = span_order[None, :] <= span_order[:, None]
    group_size = HEADS // KV_HEADS
    score_scale = 1.0 / math.sqrt(HEAD)

    def one_head(head_number):
        head_query = lax.dynamic_slice_in_dim(queries, head_number * HEAD, HEAD, 1)
        shared = head_number // group_size
        head_key = lax.dynamic_slice_in_dim(key_rows, shared * HEAD, HEAD, 1)
        head_value = lax.dynamic_slice_in_dim(value_rows, shared * HEAD, HEAD, 1)
        scores = jnp.dot(head_query, head_key.T, preferred_element_type=jnp.float32) * score_scale
        scores = jnp.where(allowed, scores, masked)
        row_peak = lax.optimization_barrier(jnp.max(scores, axis=1, keepdims=True))
        lifted = jnp.exp(scores - row_peak)
        denominator = lax.optimization_barrier(jnp.sum(lifted, axis=1, keepdims=True))
        weighted = jnp.dot(lifted.astype(jnp.bfloat16), head_value, preferred_element_type=jnp.float32)
        return (weighted / denominator).astype(jnp.bfloat16)
    per_head = lax.map(one_head, jnp.arange(HEADS, dtype=jnp.int32))
    attended = jnp.transpose(per_head, (1, 0, 2)).reshape(TOTAL, HEADS * HEAD)
    returned = jnp.dot(attended, return_weight, preferred_element_type=jnp.float32).astype(jnp.bfloat16)
    positions = jnp.arange(ROWS, dtype=jnp.int32)
    passed = lax.optimization_barrier(jnp.sum(((boundaries[:, None, :] <= positions[None, :, None]) & live_slots[:, None, :]).astype(jnp.int32), axis=2))
    span_ids = (offsets[:, None] + passed - 1).reshape(-1).astype(jnp.int32)
    return (encoded.astype(jnp.float32) + returned[span_ids].astype(jnp.float32)).astype(jnp.bfloat16)
```

```python
import functools
import math

import jax
import jax.numpy as jnp
from jax import lax
from jax.experimental import pallas as pl
from jax.experimental.pallas import tpu as pltpu
from jax.sharding import PartitionSpec as P

HEADS = 32
KV_HEADS = 8
HEAD = 128
CH_OWN = 64


eps = 1e-05
masked = -1e30
VMEM_BYTES = 56 * 2**20


def shifted(value, axis, count, step):
    return lax.ppermute(value, axis, [(i, (i + step) % count) for i in range(count)])


def crossed(value, axis, count, mask):
    return lax.ppermute(value, axis, [(i, i ^ mask) for i in range(count)])


def vmem():
    return pl.BlockSpec(memory_space=pltpu.VMEM)


def smem():
    return pl.BlockSpec(memory_space=pltpu.SMEM)


def in_place():
    return pl.BlockSpec(memory_space=pl.ANY)


def params():
    return pltpu.CompilerParams(vmem_limit_bytes=VMEM_BYTES)


def one_minus_exp(u):
    series = jnp.ones_like(u)
    for order in range(9, 1, -1):
        series = 1.0 - u * (1.0 / order) * series
    return jnp.where(u < 0.5, u * series, 1.0 - jnp.exp(-u))


def softplus(v):
    tail = jnp.exp(-jnp.abs(v))
    series = jnp.ones_like(tail)
    for order in range(6, 1, -1):
        series = 1.0 - tail * ((order - 1.0) / order) * series
    return jnp.maximum(v, 0.0) + jnp.where(tail < 0.03, tail * series, jnp.log(1.0 + tail))


def scan_kernel(bytes_ref, gain_ref, input_ref, step_ref, rate_ref, local_ref, through_ref, ends_ref):
    values = bytes_ref[...].astype(jnp.float32)
    scale = lax.rsqrt(jnp.mean(values * values, axis=1, keepdims=True) + eps)
    normed = (values * scale * gain_ref[...]).astype(jnp.bfloat16)
    steps = softplus(jnp.dot(normed, step_ref[...], preferred_element_type=jnp.float32))
    rate_steps = steps * rate_ref[...]
    inputs = jnp.dot(normed, input_ref[...], preferred_element_type=jnp.float32)
    decays = jnp.exp(-rate_steps)
    drives = jnp.sqrt(one_minus_exp(2.0 * rate_steps)) * inputs
    rows, width = decays.shape
    tile = 8
    decays = decays.reshape(rows // tile, tile, width)
    drives = drives.reshape(rows // tile, tile, width)
    place = lax.broadcasted_iota(jnp.int32, decays.shape, 1)
    for reach in (1, 2, 4):
        before_decays = pltpu.roll(decays, reach, 1)
        before_drives = pltpu.roll(drives, reach, 1)
        inside = place >= reach
        drives = jnp.where(inside, decays * before_drives + drives, drives)
        decays = jnp.where(inside, decays * before_decays, decays)
    state = jnp.zeros((1, width), jnp.float32)
    kept = jnp.ones((1, width), jnp.float32)
    for index in range(rows // tile):
        states = decays[index] * state + drives[index]
        passing = decays[index] * kept
        local_ref[pl.ds(index * tile, tile), :] = states
        through_ref[pl.ds(index * tile, tile), :] = passing
        state = states[tile - 1 :, :]
        kept = passing[tile - 1 :, :]
    ends_ref[0:1, :] = kept
    ends_ref[1:2, :] = state


def states_kernel(place_ref, local_ref, through_ref, mixer_ref, *rest):
    earlier, (states_ref, other_ref) = rest[:-2], rest[-2:]
    carry = jnp.zeros((1, local_ref.shape[1]), jnp.float32)
    for piece in earlier:
        carry = piece[0:1, :] * carry + piece[1:2, :]
    states = (local_ref[...] + through_ref[...] * carry).astype(jnp.bfloat16)
    states_ref[...] = states
    half = other_ref.shape[1]
    column = pl.multiple_of((1 - place_ref[1]) * half, half)
    other_ref[...] = jnp.dot(
        states, mixer_ref[:, pl.ds(column, half)], preferred_element_type=jnp.float32
    )


def pool_kernel(place_ref, states_ref, mixer_ref, other_ref, bytes_ref, pick_ref, encoded_ref, out_ref):
    half = other_ref.shape[1]
    column = pl.multiple_of(place_ref[1] * half, half)
    mixed = jnp.dot(
        states_ref[...], mixer_ref[:, pl.ds(column, half)], preferred_element_type=jnp.float32
    )
    skip = bytes_ref[:, pl.ds(column, half)].astype(jnp.float32)
    encoded = (skip + (mixed + other_ref[...])).astype(jnp.bfloat16)
    encoded_ref[...] = encoded
    picked = jnp.dot(pick_ref[...], encoded, preferred_element_type=jnp.float32)
    out_ref[...] = picked.astype(jnp.bfloat16).reshape(out_ref.shape)


def own_kernel(pick_ref, *rest):
    pieces, out_ref = rest[:-1], rest[-1]
    rows = jnp.concatenate([piece[...].astype(jnp.float32) for piece in pieces], axis=0)
    out_ref[...] = jnp.dot(
        pick_ref[...], rows.astype(jnp.bfloat16), preferred_element_type=jnp.float32
    ).astype(jnp.bfloat16)


def inner_kernel(
    shards, plane, place_ref, bias_ref, gain_ref, row_ref, column_ref, dest_ref, *rest
):
    layers = shards // plane
    pooled_own, rest = rest[:plane], rest[plane:]
    pooled_far, rest = rest[:plane], rest[plane:]
    up_own, rest = rest[:plane], rest[plane:]
    up_far, rest = rest[:plane], rest[plane:]
    query_pieces, rest = rest[:shards], rest[shards:]
    pair_pieces, rest = rest[:plane], rest[plane:]
    out_ref, pooled, up, weights, heads, inner, attended, sems = rest
    me, lane = place_ref[0], place_ref[1]
    rows, width = pooled.shape
    half = width // 2
    up_half = up.shape[1] // 2
    piece_rows = width // shards
    block = rows // plane
    weight_rows = weights.shape[0] // shards

    def lane_at(which, size):
        return pl.ds(pl.multiple_of(which * size, size), size)

    def source(cross, layer):
        return lax.rem((me ^ cross) - plane * layer + shards, shards)

    groups = []
    for index, (mine, far) in enumerate(zip(pooled_own, pooled_far)):
        where = pl.ds(index * block, block)
        groups.append((0, mine, pooled.at[where, lane_at(lane, half)]))
        groups.append((0, far, pooled.at[where, lane_at(1 - lane, half)]))
    for cross in range(plane):
        for layer in range(layers):
            where = pl.ds(pl.multiple_of(source(cross, layer) * piece_rows, piece_rows), piece_rows)
            groups.append((1, up_own[cross].at[layer], up.at[where, lane_at(lane, up_half)]))
            groups.append((1, up_far[cross].at[layer], up.at[where, lane_at(1 - lane, up_half)]))
    for step in range(shards):
        origin = lax.rem(me - step + shards, shards)
        where = pl.ds(pl.multiple_of(origin * weight_rows, weight_rows), weight_rows)
        groups.append((2, query_pieces[step], weights.at[where, pl.ds(0, HEAD)]))
    for cross in range(plane):
        for layer in range(layers):
            where = pl.ds(pl.multiple_of(source(cross, layer) * weight_rows, weight_rows), weight_rows)
            groups.append(
                (2, pair_pieces[cross].at[layer], weights.at[where, pl.ds(HEAD, 2 * HEAD)])
            )
    copies = []
    for index, (group, from_ref, to_ref) in enumerate(groups):
        copy = pltpu.make_async_copy(from_ref, to_ref, sems.at[index])
        copy.start()
        copies.append((group, copy))
    for group, copy in copies:
        if group < 2:
            copy.wait()

    part = 1024
    parts = up.shape[1] // part

    def up_block(index, waited):
        where = pl.ds(pl.multiple_of(index * block, block), block)
        left = pooled[where, :]
        total = jnp.zeros((block, 1), jnp.float32)
        for number in range(parts):
            columns = pl.ds(number * part, part)
            widened = jnp.dot(left, up[:, columns], preferred_element_type=jnp.float32)
            widened = (widened + bias_ref[:, columns]).astype(jnp.bfloat16)
            inner[:, columns] = widened
            wide = widened.astype(jnp.float32)
            total = total + jnp.sum(wide * wide, axis=1, keepdims=True)
        scale = lax.rsqrt(total * (1.0 / up.shape[1]) + eps)
        sums = jnp.zeros((block, heads.shape[1]), jnp.float32)
        for number in range(parts):
            columns = pl.ds(number * part, part)
            normed = (inner[:, columns].astype(jnp.float32) * scale * gain_ref[:, columns]).astype(
                jnp.bfloat16
            )
            sums = sums + jnp.dot(
                normed, weights[pl.ds(number * part, part), :], preferred_element_type=jnp.float32
            )
        heads[where, :] = sums.astype(jnp.bfloat16)
        return waited

    for group, copy in copies:
        if group == 2:
            copy.wait()
    lax.fori_loop(0, plane, up_block, 0)

    score_scale = 1.0 / math.sqrt(HEAD)

    def attend_block(index, carried):
        where = pl.ds(pl.multiple_of(index * block, block), block)
        scores = lax.dot_general(
            heads[where, 0:HEAD],
            heads[:, HEAD : 2 * HEAD],
            (((1,), (1,)), ((), ())),
            preferred_element_type=jnp.float32,
        )
        scores = jnp.where(column_ref[...] <= row_ref[where, :], scores * score_scale, masked)
        peak = jnp.max(scores, axis=1, keepdims=True)
        lifted = jnp.exp(scores - peak)
        denominator = jnp.sum(lifted, axis=1, keepdims=True)
        weighted = jnp.dot(
            lifted.astype(jnp.bfloat16),
            heads[:, 2 * HEAD : 3 * HEAD],
            preferred_element_type=jnp.float32,
        )
        attended[where, :] = (weighted / denominator).astype(jnp.bfloat16)
        return carried

    lax.fori_loop(0, plane, attend_block, 0)
    capacity = out_ref.shape[1]

    def send_block(index, carried):
        where = pl.ds(pl.multiple_of(index * capacity, capacity), capacity)
        spots = lax.broadcasted_iota(jnp.int32, (capacity, rows), 1)
        chosen = (spots == dest_ref[where, :]).astype(jnp.float32).astype(jnp.bfloat16)
        out_ref[index] = jnp.dot(
            chosen, attended[...], preferred_element_type=jnp.float32
        ).astype(jnp.bfloat16)
        return carried

    lax.fori_loop(0, shards, send_block, 0)


def return_kernel(shards, place_ref, weight_ref, *rest):
    pieces, (own_ref, other_ref) = rest[:-2], rest[-2:]
    me, lane = place_ref[0], place_ref[1]
    half = own_ref.shape[1]
    total = jnp.zeros((own_ref.shape[0], 2 * half), jnp.float32)
    for step in range(shards):
        head = lax.rem(me - step + shards, shards)
        total = total + jnp.dot(pieces[step][...], weight_ref[head], preferred_element_type=jnp.float32)
    first, second = total[:, :half], total[:, half:]
    at_first = lane == 0
    own_ref[...] = jnp.where(at_first, first, second)
    other_ref[...] = jnp.where(at_first, second, first)


def join_kernel(own_ref, other_ref, encoded_ref, spread_ref, out_ref):
    returned = (own_ref[...] + other_ref[...]).astype(jnp.bfloat16)
    results = jnp.dot(spread_ref[...], returned, preferred_element_type=jnp.float32)
    out_ref[...] = (encoded_ref[...].astype(jnp.float32) + results).astype(jnp.bfloat16)


def one_head_each(
    byte_states,
    outer_gain,
    mamba_input,
    mamba_step,
    decay_rate,
    mixer_weight,
    boundaries,
    span_counts,
    up_weight,
    up_bias,
    inner_gain,
    query_weight,
    key_weight,
    value_weight,
    return_weight,
):
    shards = lax.axis_size("seq")
    me = lax.axis_index("seq")
    lane = lax.axis_index("mp")
    plane = HEADS // KV_HEADS
    layers = shards // plane
    rows_here, width = byte_states.shape
    half = mamba_input.shape[1]
    capacity = boundaries.shape[1]
    slots = capacity // shards
    total_rows = CH_OWN * shards
    place = jnp.stack([me, lane]).astype(jnp.int32)
    f32, bf16 = jnp.float32, jnp.bfloat16

    def over_layers(value):
        return jnp.stack(
            [value] + [shifted(value, "seq", shards, plane * layer) for layer in range(1, layers)]
        )

    def over_plane(value):
        return [value] + [crossed(value, "seq", shards, mask) for mask in range(1, plane)]

    up_layers = over_layers(up_weight)
    up_own = over_plane(up_layers)
    up_far = [crossed(piece, "mp", 2, 1) for piece in up_own]
    own_bias = up_bias[None, :]
    far_bias = crossed(own_bias, "mp", 2, 1)
    bias = jnp.where(
        lane == 0,
        jnp.concatenate([own_bias, far_bias], axis=1),
        jnp.concatenate([far_bias, own_bias], axis=1),
    )

    def columns_of(value, which):
        return lax.dynamic_slice_in_dim(value, which * HEAD, HEAD, 1)

    query_pieces = []
    for step in range(shards):
        piece = columns_of(query_weight, (me + step) % shards)
        query_pieces.append(shifted(piece, "seq", shards, step) if step else piece)
    pair_layers = []
    for layer in range(layers):
        group = (me // plane + layer) % layers
        piece = jnp.concatenate(
            [columns_of(key_weight, group), columns_of(value_weight, group)], axis=1
        )
        pair_layers.append(shifted(piece, "seq", shards, plane * layer) if layer else piece)
    pair_pieces = over_plane(jnp.stack(pair_layers))

    seq_ids = jnp.arange(shards, dtype=jnp.int32)
    offsets = jnp.cumsum(span_counts) - span_counts
    own_offset = jnp.sum(jnp.where(seq_ids == me, offsets, 0))
    own_count = jnp.sum(jnp.where(seq_ids == me, span_counts, 0))
    own_marks = boundaries[0]
    step_ids = jnp.arange(shards, dtype=jnp.int32)
    slot_ids = jnp.arange(slots, dtype=jnp.int32)
    positions = jnp.arange(rows_here, dtype=jnp.int32)
    spans_here = jnp.arange(capacity, dtype=jnp.int32)
    target = (me + step_ids) % shards
    local_span = slot_ids[None, :] * shards + ((target - own_offset) % shards)[:, None]
    local_span = local_span.reshape(-1)
    is_span = spans_here[None, :] == local_span[:, None]
    byte_at = jnp.sum(jnp.where(is_span, jnp.minimum(own_marks, rows_here - 1)[None, :], 0), axis=1)
    pool_pick = (positions[None, :] == byte_at[:, None]).astype(bf16)
    own_spans = me + jnp.arange(CH_OWN, dtype=jnp.int32) * shards
    origin = jnp.sum((offsets[None, :] <= own_spans[:, None]).astype(jnp.int32), axis=1) - 1
    origin_offset = jnp.sum(
        jnp.where(seq_ids[None, :] == origin[:, None], offsets[None, :], 0), axis=1
    )
    own_slot = (own_spans - origin_offset) // shards
    arrived_row = ((me - origin) % shards) * slots + own_slot
    own_pick = (
        jnp.arange(shards * slots, dtype=jnp.int32)[None, :] == arrived_row[:, None]
    ).astype(bf16)
    cross_ids = jnp.arange(plane, dtype=jnp.int32)
    layer_ids = jnp.arange(layers, dtype=jnp.int32)
    holder = ((me ^ cross_ids)[:, None] - plane * layer_ids[None, :]) % shards
    span_of_row = (
        holder.reshape(-1)[:, None] + jnp.arange(CH_OWN, dtype=jnp.int32)[None, :] * shards
    ).reshape(-1)
    back_offset = jnp.sum(jnp.where(seq_ids[None, :] == target[:, None], offsets[None, :], 0), axis=1)
    back_count = jnp.sum(
        jnp.where(seq_ids[None, :] == target[:, None], span_counts[None, :], 0), axis=1
    )
    back_span = back_offset[:, None] + spans_here[None, :]
    owner = back_span % shards
    cross = (me ^ owner) % plane
    layer = (me // plane - owner // plane) % layers
    back_row = (cross * layers + layer) * CH_OWN + back_span // shards
    back_row = jnp.where(spans_here[None, :] < back_count[:, None], back_row, -1).reshape(-1, 1)
    live = spans_here < own_count
    passed = jnp.sum(
        ((own_marks[None, :] <= positions[:, None]) & live[None, :]).astype(jnp.int32), axis=1
    )
    spread = (spans_here[None, :] == (passed - 1)[:, None]).astype(bf16)

    local, through, ends = pl.pallas_call(
        scan_kernel,
        out_shape=(
            jax.ShapeDtypeStruct((rows_here, half), f32),
            jax.ShapeDtypeStruct((rows_here, half), f32),
            jax.ShapeDtypeStruct((2, half), f32),
        ),
        in_specs=[vmem()] * 5,
        out_specs=(vmem(),) * 3,
        compiler_params=params(),
    )(byte_states, outer_gain[None, :], mamba_input, mamba_step, decay_rate[None, :])
    earlier = [
        lax.ppermute(ends, "seq", [(i, i + step) for i in range(shards - step)])
        for step in range(shards - 1, 0, -1)
    ]
    states, other_part = pl.pallas_call(
        states_kernel,
        out_shape=(
            jax.ShapeDtypeStruct((rows_here, half), bf16),
            jax.ShapeDtypeStruct((rows_here, half), f32),
        ),
        in_specs=[smem()] + [vmem()] * (3 + len(earlier)),
        out_specs=(vmem(),) * 2,
        compiler_params=params(),
    )(place, local, through, mixer_weight, *earlier)
    far_part = crossed(other_part, "mp", 2, 1)
    encoded, outgoing = pl.pallas_call(
        pool_kernel,
        out_shape=(
            jax.ShapeDtypeStruct((rows_here, half), bf16),
            jax.ShapeDtypeStruct((shards, slots, half), bf16),
        ),
        in_specs=[smem()] + [vmem()] * 5,
        out_specs=(vmem(),) * 2,
        compiler_params=params(),
    )(place, states, mixer_weight, far_part, byte_states, pool_pick)
    incoming = [
        shifted(outgoing[step], "seq", shards, step) if step else outgoing[0]
        for step in range(shards)
    ]
    own_rows = pl.pallas_call(
        own_kernel,
        out_shape=jax.ShapeDtypeStruct((CH_OWN, half), bf16),
        in_specs=[vmem()] * (1 + shards),
        out_specs=vmem(),
        compiler_params=params(),
    )(own_pick, *incoming)
    pooled_own = over_plane(over_layers(own_rows).reshape(layers * CH_OWN, half))
    pooled_far = [crossed(piece, "mp", 2, 1) for piece in pooled_own]

    pieces = [*pooled_own, *pooled_far, *up_own, *up_far, *query_pieces, *pair_pieces]
    copy_count = 2 * plane + 2 * shards + shards + shards
    inner_width = inner_gain.shape[0]
    leaving = pl.pallas_call(
        functools.partial(inner_kernel, shards, plane),
        out_shape=jax.ShapeDtypeStruct((shards, capacity, HEAD), bf16),
        in_specs=[smem()] + [vmem()] * 5 + [in_place()] * len(pieces),
        out_specs=vmem(),
        scratch_shapes=[
            pltpu.VMEM((total_rows, width), bf16),
            pltpu.VMEM((width, inner_width), bf16),
            pltpu.VMEM((inner_width, 3 * HEAD), bf16),
            pltpu.VMEM((total_rows, 3 * HEAD), bf16),
            pltpu.VMEM((total_rows // plane, inner_width), bf16),
            pltpu.VMEM((total_rows, HEAD), bf16),
            pltpu.SemaphoreType.DMA((copy_count,)),
        ],
        compiler_params=params(),
    )(
        place,
        bias,
        inner_gain[None, :],
        span_of_row[:, None],
        span_of_row[None, :],
        back_row,
        *pieces,
    )
    returned = [
        shifted(leaving[step], "seq", shards, step) if step else leaving[0]
        for step in range(shards)
    ]
    own_back, other_back = pl.pallas_call(
        functools.partial(return_kernel, shards),
        out_shape=(jax.ShapeDtypeStruct((capacity, half), f32),) * 2,
        in_specs=[smem()] + [vmem()] * (1 + shards),
        out_specs=(vmem(),) * 2,
        compiler_params=params(),
    )(place, return_weight.reshape(shards, HEAD, width), *returned)
    far_back = crossed(other_back, "mp", 2, 1)
    return pl.pallas_call(
        join_kernel,
        out_shape=jax.ShapeDtypeStruct((rows_here, half), bf16),
        in_specs=[vmem()] * 4,
        out_specs=vmem(),
        compiler_params=params(),
    )(own_back, far_back, encoded, spread)


def prefix(value, axis, join, neutral):
    count, mine = (lax.axis_size(axis), lax.axis_index(axis))
    pieces = jax.tree.map(lambda part: lax.all_gather(part, axis), value)
    so_far = jax.tree.map(
        lambda part, zero: jnp.full_like(part, 0) + jnp.asarray(zero, part.dtype), value, neutral
    )

    def lap(position, so_far):
        longer = join(so_far, jax.tree.map(lambda part: part[position], pieces))
        return jax.tree.map(lambda new, old: jnp.where(position < mine, new, old), longer, so_far)

    return lax.fori_loop(0, count - 1, lap, so_far)


def rms_scale(values, gain):
    values = values.astype(jnp.float32)
    return values * lax.rsqrt(jnp.mean(values * values, axis=-1, keepdims=True) + eps) * gain


def combine_pairs(earlier, later):
    return (earlier[0] * later[0], later[0] * earlier[1] + later[1])


def pick_table(table, wanted, seq_ids):
    return jnp.sum(jnp.where(seq_ids[None, :] == wanted[:, None], table[None, :], 0), axis=1)


def block_size(piece_rows, shard_rows):
    limit = max(1, 1024 // shard_rows)
    pieces = max(1, piece_rows // shard_rows)
    best_size = 1
    for candidate in range(1, limit + 1):
        if pieces % candidate == 0:
            best_size = candidate
    return min(piece_rows, best_size * shard_rows)


def spread_heads(
    byte_states,
    outer_gain,
    mamba_input,
    mamba_step,
    decay_rate,
    mixer_weight,
    boundaries,
    span_counts,
    up_weight,
    up_bias,
    inner_gain,
    query_weight,
    key_weight,
    value_weight,
    return_weight,
):
    shards = lax.axis_size("seq")
    own_shard = lax.axis_index("seq")
    own_lane = lax.axis_index("mp")
    rows_here = byte_states.shape[0]
    capacity = boundaries.shape[1]
    column_count = mamba_input.shape[1]
    kv_local = key_weight.shape[1] // HEAD
    group_size = HEADS // KV_HEADS
    slot_count = capacity // shards
    offsets = jnp.cumsum(span_counts) - span_counts
    seq_ids = jnp.arange(shards, dtype=jnp.int32)
    own_offset = jnp.sum(jnp.where(seq_ids == own_shard, offsets, 0))
    own_count = jnp.sum(jnp.where(seq_ids == own_shard, span_counts, 0))
    normed = rms_scale(byte_states, outer_gain).astype(jnp.bfloat16)
    inputs = jnp.dot(normed, mamba_input, preferred_element_type=jnp.float32)
    step_sizes = jax.nn.softplus(jnp.dot(normed, mamba_step, preferred_element_type=jnp.float32))
    rate_steps = step_sizes * decay_rate
    decays = jnp.exp(-rate_steps)
    drives = jnp.sqrt(-jnp.expm1(-2.0 * rate_steps)) * inputs
    through, local_states = lax.associative_scan(combine_pairs, (decays, drives), axis=0)
    starting = (jnp.ones((column_count,), jnp.float32), jnp.zeros((column_count,), jnp.float32))
    arriving = prefix((through[-1], local_states[-1]), "seq", combine_pairs, starting)
    states = (local_states + through * arriving[1][None, :]).astype(jnp.bfloat16)
    partial_value = jnp.dot(states, mixer_weight, preferred_element_type=jnp.float32)
    mixed_sum = lax.psum(partial_value, "mp")
    encoded = (byte_states.astype(jnp.float32) + mixed_sum).astype(jnp.bfloat16)
    skip_part = lax.dynamic_slice_in_dim(encoded, own_lane * column_count, column_count, 1)
    own_marks = boundaries[0]
    pooled = encoded[jnp.minimum(own_marks, rows_here - 1)]
    row_width = pooled.shape[1]
    outgoing = jnp.roll(pooled.reshape(slot_count, shards, row_width), own_offset % shards, axis=1)
    incoming = lax.all_to_all(outgoing, "seq", split_axis=1, concat_axis=1, tiled=True)
    position = jnp.arange(CH_OWN, dtype=jnp.int32)
    span_index = own_shard + position * shards
    source = jnp.sum((offsets[None, :] <= span_index[:, None]).astype(jnp.int32), axis=1) - 1
    source_offset = pick_table(offsets, source, seq_ids)
    slot_index = (span_index - source_offset) // shards
    gathered_rows = incoming.reshape(slot_count * shards, row_width)[slot_index * shards + source]
    columns = gathered_rows
    widened_sum = jnp.dot(
        columns,
        lax.all_gather(up_weight, "seq", axis=0, tiled=True),
        preferred_element_type=jnp.float32,
    )
    widened_share = (widened_sum + up_bias[None, :]).astype(jnp.bfloat16)
    widened = lax.all_gather(widened_share, "mp", axis=1, tiled=True)
    inner_normed = rms_scale(widened, inner_gain).astype(jnp.bfloat16)
    columns = inner_normed
    query_part = jnp.dot(
        columns,
        lax.all_gather(query_weight, "seq", axis=0, tiled=True),
        preferred_element_type=jnp.float32,
    )
    key_part = jnp.dot(
        columns,
        lax.all_gather(key_weight, "seq", axis=0, tiled=True),
        preferred_element_type=jnp.float32,
    )
    value_part = jnp.dot(
        columns,
        lax.all_gather(value_weight, "seq", axis=0, tiled=True),
        preferred_element_type=jnp.float32,
    )
    queries = query_part.astype(jnp.bfloat16)
    key_rows = key_part.astype(jnp.bfloat16)
    value_rows = value_part.astype(jnp.bfloat16)
    query_count = queries.shape[0]
    grouped = (
        queries.reshape(query_count, kv_local, group_size, HEAD)
        .transpose(1, 0, 2, 3)
        .reshape(kv_local, query_count * group_size, HEAD)
    )
    row_index = jnp.repeat(span_index, group_size)
    shard_rows = key_rows.shape[0]
    score_scale = 1.0 / math.sqrt(HEAD)

    def key_index(whole_index):
        return whole_index // shard_rows + whole_index % shard_rows * shards

    def attend_block(running, key_block, value_block, index_block):
        row_peak, denominator, weighted = running
        scores = (
            jnp.einsum("hqd,khd->hqk", grouped, key_block, preferred_element_type=jnp.float32)
            * score_scale
        )
        scores = jnp.where(index_block[None, None, :] <= row_index[None, :, None], scores, masked)
        new_peak = jnp.maximum(row_peak, jnp.max(scores, axis=2))
        shrink = jnp.exp(row_peak - new_peak)
        lifted = jnp.exp(scores - new_peak[:, :, None])
        denominator = denominator * shrink + jnp.sum(lifted, axis=2)
        weighted = weighted * shrink[:, :, None] + jnp.einsum(
            "hqk,khd->hqd",
            lifted.astype(jnp.bfloat16),
            value_block,
            preferred_element_type=jnp.float32,
        )
        return (new_peak, denominator, weighted)

    query_total = query_count * group_size
    initial = (
        jnp.full((kv_local, query_total), masked, jnp.float32),
        jnp.zeros((kv_local, query_total), jnp.float32),
        jnp.zeros((kv_local, query_total, HEAD), jnp.float32),
    )
    key_piece = lax.all_gather(key_rows, "seq", axis=0, tiled=True)
    value_piece = lax.all_gather(value_rows, "seq", axis=0, tiled=True)
    piece_rows = key_piece.shape[0]
    block_rows = block_size(piece_rows, shard_rows)
    turn_count = piece_rows // block_rows
    key_blocks = key_piece.reshape(turn_count, block_rows, kv_local, HEAD)
    value_blocks = value_piece.reshape(turn_count, block_rows, kv_local, HEAD)

    def one_turn(turn_index, inner_running):
        whole_index = turn_index * block_rows + jnp.arange(block_rows, dtype=jnp.int32)
        return attend_block(
            inner_running, key_blocks[turn_index], value_blocks[turn_index], key_index(whole_index)
        )

    row_peak, denominator, weighted = lax.fori_loop(0, turn_count, one_turn, initial)
    attended = (weighted / denominator[:, :, None]).astype(jnp.bfloat16)
    attended = (
        attended.reshape(kv_local, query_count, group_size, HEAD)
        .transpose(1, 0, 2, 3)
        .reshape(query_count, kv_local * group_size * HEAD)
    )
    projected = jnp.dot(attended, return_weight, preferred_element_type=jnp.float32)
    returned = lax.psum_scatter(
        projected.astype(jnp.bfloat16), "mp", scatter_dimension=1, tiled=True
    )
    slot_ids = jnp.arange(slot_count, dtype=jnp.int32)
    lead_slot = (own_shard - offsets) % shards
    local_span = slot_ids[:, None] * shards + lead_slot[None, :]
    back_index = (offsets[None, :] + local_span - own_shard) // shards
    alive = local_span < span_counts[None, :]
    back_rows = jnp.where(
        alive[:, :, None],
        returned[jnp.clip(back_index, 0, CH_OWN - 1)],
        jnp.zeros((), jnp.bfloat16),
    )
    arrived = lax.all_to_all(back_rows, "seq", split_axis=1, concat_axis=1, tiled=True)
    span_results = jnp.roll(arrived, -(own_offset % shards), axis=1).reshape(capacity, column_count)
    positions = jnp.arange(rows_here, dtype=jnp.int32)
    live_slots = jnp.arange(capacity, dtype=jnp.int32) < own_count
    passed = jnp.sum(
        ((own_marks[None, :] <= positions[:, None]) & live_slots[None, :]).astype(jnp.int32), axis=1
    )
    return (skip_part.astype(jnp.float32) + span_results[passed - 1].astype(jnp.float32)).astype(
        jnp.bfloat16
    )


def solution(mesh):
    in_specs = (
        P("seq", None),
        P(),
        P(None, "mp"),
        P(None, "mp"),
        P("mp"),
        P("mp", None),
        P("seq", None),
        P(),
        P("seq", "mp"),
        P("mp"),
        P(),
        P("seq", "mp"),
        P("seq", "mp"),
        P("seq", "mp"),
        P("mp", None),
    )
    out_specs = P("seq", "mp")
    def on_device(*arrays):
        heads_here = arrays[11].shape[1] // HEAD
        fits = heads_here == mesh.shape["seq"] and mesh.shape["mp"] == 2
        return (one_head_each if fits else spread_heads)(*arrays)

    return jax.shard_map(
        on_device, mesh=mesh, in_specs=in_specs, out_specs=out_specs, check_vma=False
    )
```

```python
import functools
import math

import jax
import jax.numpy as jnp
from jax import lax
from jax.experimental import pallas as pl
from jax.experimental.pallas import tpu as pltpu
from jax.sharding import PartitionSpec as P

HEADS = 32
KV_HEADS = 8
HEAD = 128
CH_OWN = 64


eps = 1e-05
masked = -1e30
TILE = 16
VMEM_BYTES = 56 * 2**20


def swapped(value):
    return lax.ppermute(value, "mp", [(0, 1), (1, 0)])


def vmem():
    return pl.BlockSpec(memory_space=pltpu.VMEM)


def smem():
    return pl.BlockSpec(memory_space=pltpu.SMEM)


def in_place():
    return pl.BlockSpec(memory_space=pl.ANY)


def params():
    return pltpu.CompilerParams(vmem_limit_bytes=VMEM_BYTES)


def lanes(which, size):
    return pl.ds(pl.multiple_of(which * size, size), size)


def one_minus_exp(u):
    series = jnp.ones_like(u)
    for order in range(9, 1, -1):
        series = 1.0 - u * (1.0 / order) * series
    return jnp.where(u < 0.5, u * series, 1.0 - jnp.exp(-u))


def softplus(v):
    tail = jnp.exp(-jnp.abs(v))
    series = jnp.ones_like(tail)
    for order in range(6, 1, -1):
        series = 1.0 - tail * ((order - 1.0) / order) * series
    return jnp.maximum(v, 0.0) + jnp.where(tail < 0.03, tail * series, jnp.log(1.0 + tail))


def scan_kernel(bytes_ref, gain_ref, input_ref, step_ref, rate_ref, local_ref, through_ref, ends_ref):
    values = bytes_ref[...].astype(jnp.float32)
    scale = lax.rsqrt(jnp.mean(values * values, axis=1, keepdims=True) + eps)
    normed = (values * scale * gain_ref[...]).astype(jnp.bfloat16)
    steps = softplus(jnp.dot(normed, step_ref[...], preferred_element_type=jnp.float32))
    rate_steps = steps * rate_ref[...]
    inputs = jnp.dot(normed, input_ref[...], preferred_element_type=jnp.float32)
    decays = jnp.exp(-rate_steps)
    drives = jnp.sqrt(one_minus_exp(2.0 * rate_steps)) * inputs
    rows, width = decays.shape
    tile = 8
    decays = decays.reshape(rows // tile, tile, width)
    drives = drives.reshape(rows // tile, tile, width)
    place = lax.broadcasted_iota(jnp.int32, decays.shape, 1)
    for reach in (1, 2, 4):
        before_decays = pltpu.roll(decays, reach, 1)
        before_drives = pltpu.roll(drives, reach, 1)
        inside = place >= reach
        drives = jnp.where(inside, decays * before_drives + drives, drives)
        decays = jnp.where(inside, decays * before_decays, decays)
    state = jnp.zeros((1, width), jnp.float32)
    kept = jnp.ones((1, width), jnp.float32)
    for index in range(rows // tile):
        states = decays[index] * state + drives[index]
        passing = decays[index] * kept
        local_ref[pl.ds(index * tile, tile), :] = states
        through_ref[pl.ds(index * tile, tile), :] = passing
        state = states[tile - 1 :, :]
        kept = passing[tile - 1 :, :]
    for index in range(ends_ref.shape[0]):
        ends_ref[index, 0:1, :] = kept
        ends_ref[index, 1:2, :] = state


def states_kernel(place_ref, local_ref, through_ref, mixer_ref, ends_ref, states_ref, other_ref):
    carry = jnp.zeros((1, local_ref.shape[1]), jnp.float32)
    for shard in range(ends_ref.shape[0]):
        later = ends_ref[shard, 0:1, :] * carry + ends_ref[shard, 1:2, :]
        carry = jnp.where(shard < place_ref[0], later, carry)
    states = (local_ref[...] + through_ref[...] * carry).astype(jnp.bfloat16)
    states_ref[...] = states
    half = other_ref.shape[1]
    other_ref[...] = jnp.dot(
        states, mixer_ref[:, lanes(1 - place_ref[1], half)], preferred_element_type=jnp.float32
    )


def pool_kernel(place_ref, states_ref, mixer_ref, other_ref, bytes_ref, pick_ref, encoded_ref, out_ref):
    half = other_ref.shape[1]
    columns = lanes(place_ref[1], half)
    mixed = jnp.dot(states_ref[...], mixer_ref[:, columns], preferred_element_type=jnp.float32)
    skip = bytes_ref[:, columns].astype(jnp.float32)
    encoded = (skip + (mixed + other_ref[...])).astype(jnp.bfloat16)
    encoded_ref[...] = encoded
    picked = jnp.dot(pick_ref[...], encoded, preferred_element_type=jnp.float32)
    picked = picked.astype(jnp.bfloat16)
    for index in range(out_ref.shape[0]):
        out_ref[index] = picked


def inner_kernel(
    place_ref,
    bias_ref,
    gain_ref,
    near_ref,
    far_ref,
    up_ref,
    query_ref,
    far_query_ref,
    pair_ref,
    own_ref,
    other_ref,
    pieces,
    pooled,
    up,
    weights,
    inner,
    sems,
):
    lane = place_ref[1]
    plane, layers, window, half = near_ref.shape
    width = 2 * half
    up_rows = up_ref.shape[2]
    query_rows = query_ref.shape[0]
    pair_rows = pair_ref.shape[3]
    rows, sums_width = own_ref.shape
    span = 3 * HEAD
    early = [
        (near_ref, pieces.at[:, :, :, lanes(lane, half)]),
        (far_ref, pieces.at[:, :, :, lanes(1 - lane, half)]),
    ]
    late = []
    for cross in range(plane):
        for layer in range(layers):
            where = pl.ds((layer * plane + cross) * up_rows, up_rows)
            late.append((up_ref.at[cross, layer], up.at[where, :]))
    late.append((query_ref, weights.at[:, pl.ds(0, HEAD)]))
    late.append((far_query_ref, weights.at[:, pl.ds(span, HEAD)]))
    for cross in range(plane):
        for head in range(2):
            for layer in range(layers // 2):
                where = pl.ds((layer * plane + cross) * pair_rows, pair_rows)
                late.append(
                    (
                        pair_ref.at[cross, head, layer],
                        weights.at[where, pl.ds(head * span + HEAD, 2 * HEAD)],
                    )
                )
    copies = []
    for index, (from_ref, to_ref) in enumerate(early + late):
        copy = pltpu.make_async_copy(from_ref, to_ref, sems.at[index])
        copy.start()
        copies.append(copy)
    pooled[...] = jnp.zeros_like(pooled)
    for copy in copies[: len(early)]:
        copy.wait()
    for layer in range(layers):
        for cross in range(plane):
            first = place_ref[2 + layer * plane + cross]
            where = pl.ds(pl.multiple_of(first * TILE, TILE), window)
            pooled[where, :] = pooled[where, :] + pieces[cross, layer]
    for copy in copies[len(early) :]:
        copy.wait()

    block = inner.shape[0]
    part = min(1024, up.shape[1])
    parts = up.shape[1] // part

    def up_block(index, carried):
        where = pl.ds(pl.multiple_of(index * block, block), block)
        left = pooled[where, :]
        total = jnp.zeros((block, 1), jnp.float32)
        for number in range(parts):
            columns = pl.ds(number * part, part)
            widened = jnp.dot(left, up[:, columns], preferred_element_type=jnp.float32)
            widened = (widened + bias_ref[:, columns]).astype(jnp.bfloat16).astype(jnp.float32)
            inner[:, columns] = (widened * gain_ref[:, columns]).astype(jnp.bfloat16)
            total = total + jnp.sum(widened * widened, axis=1, keepdims=True)
        sums = jnp.dot(inner[...], weights[...], preferred_element_type=jnp.float32)
        spread = jnp.broadcast_to(total, (block, sums_width - span))
        own_ref[where, 0:span] = sums[:, :span]
        own_ref[where, span:] = spread
        other_ref[where, 0:span] = sums[:, span:]
        other_ref[where, span:] = spread
        return carried

    lax.fori_loop(0, rows // block, up_block, 0)


def attend_kernel(features, place_ref, own_ref, other_ref, out_ref, heads, attended):
    rows = own_ref.shape[0]
    span = 3 * HEAD
    window = out_ref.shape[1]
    block = min(256, rows)
    for start in range(0, rows, block):
        where = pl.ds(start, block)
        sums = own_ref[where, :] + other_ref[where, :]
        scale = lax.rsqrt(sums[:, span : span + 1] * (1.0 / features) + eps)
        heads[where, :] = (sums[:, :span] * scale).astype(jnp.bfloat16)
    score_scale = 1.0 / math.sqrt(HEAD)
    for start in range(0, rows, block):
        stop = start + block
        scores = lax.dot_general(
            heads[start:stop, 0:HEAD],
            heads[0:stop, HEAD : 2 * HEAD],
            (((1,), (1,)), ((), ())),
            preferred_element_type=jnp.float32,
        )
        spots = lax.broadcasted_iota(jnp.int32, scores.shape, 1)
        mine = lax.broadcasted_iota(jnp.int32, scores.shape, 0) + start
        scores = jnp.where(spots <= mine, scores * score_scale, masked)
        peak = jnp.max(scores, axis=1, keepdims=True)
        lifted = jnp.exp(scores - peak)
        denominator = jnp.sum(lifted, axis=1, keepdims=True)
        weighted = jnp.dot(
            lifted.astype(jnp.bfloat16),
            heads[0:stop, 2 * HEAD : 3 * HEAD],
            preferred_element_type=jnp.float32,
        )
        attended[start:stop, :] = (weighted / denominator).astype(jnp.bfloat16)
    attended[rows:, :] = jnp.zeros((attended.shape[0] - rows, HEAD), jnp.bfloat16)
    for shard in range(out_ref.shape[0]):
        first = place_ref[2 + shard]
        out_ref[shard] = attended[pl.ds(pl.multiple_of(first * TILE, TILE), window), :]


def return_kernel(place_ref, weight_ref, pieces_ref, own_ref, other_ref, attended):
    half = own_ref.shape[1]
    lane = place_ref[1]
    for head in range(pieces_ref.shape[0]):
        attended[:, head * HEAD : (head + 1) * HEAD] = pieces_ref[head]
    other_ref[...] = jnp.dot(
        attended[...], weight_ref[:, lanes(1 - lane, half)], preferred_element_type=jnp.float32
    )
    own_ref[...] = jnp.dot(
        attended[...], weight_ref[:, lanes(lane, half)], preferred_element_type=jnp.float32
    )


def join_kernel(own_ref, other_ref, encoded_ref, spread_ref, out_ref):
    returned = (own_ref[...] + other_ref[...]).astype(jnp.bfloat16)
    results = jnp.dot(spread_ref[...], returned, preferred_element_type=jnp.float32)
    out_ref[...] = (encoded_ref[...].astype(jnp.float32) + results).astype(jnp.bfloat16)


def one_head_each(
    byte_states,
    outer_gain,
    mamba_input,
    mamba_step,
    decay_rate,
    mixer_weight,
    boundaries,
    span_counts,
    up_weight,
    up_bias,
    inner_gain,
    query_weight,
    key_weight,
    value_weight,
    return_weight,
):
    shards = lax.axis_size("seq")
    me = lax.axis_index("seq")
    lane = lax.axis_index("mp")
    plane = HEADS // KV_HEADS
    layers = shards // plane
    rows_here, width = byte_states.shape
    half = mamba_input.shape[1]
    capacity = boundaries.shape[1]
    window = capacity + TILE
    total_rows = CH_OWN * shards
    inner_width = inner_gain.shape[0]
    inner_half = up_bias.shape[0]
    weight_rows = query_weight.shape[0]
    f32, bf16 = jnp.float32, jnp.bfloat16
    layer_groups = [[first + plane * layer for layer in range(layers)] for first in range(plane)]
    plane_groups = [[first * plane + cross for cross in range(plane)] for first in range(layers)]

    up_layers = lax.all_gather(up_weight, "seq", axis_index_groups=layer_groups)
    up_whole = lax.all_gather(up_layers, "seq", axis_index_groups=plane_groups)
    own_gain = lax.dynamic_slice_in_dim(inner_gain, lane * inner_half, inner_half)[None, :]
    queries = query_weight.reshape(weight_rows, shards, HEAD).transpose(1, 0, 2)
    queries = lax.all_to_all(queries, "seq", 0, 0, tiled=True)
    queries = queries.reshape(2, shards * weight_rows // 2, HEAD)
    own_query = lax.dynamic_index_in_dim(queries, lane, 0, keepdims=False)
    far_query = swapped(lax.dynamic_index_in_dim(queries, 1 - lane, 0, keepdims=False))
    pairs = jnp.concatenate(
        [
            key_weight.reshape(weight_rows, layers, HEAD).transpose(1, 0, 2),
            value_weight.reshape(weight_rows, layers, HEAD).transpose(1, 0, 2),
        ],
        axis=2,
    )
    pairs = lax.all_to_all(pairs, "seq", 0, 0, axis_index_groups=layer_groups, tiled=True)
    pairs = pairs.reshape(2, layers // 2, weight_rows, 2 * HEAD)
    own_pair = lax.dynamic_index_in_dim(pairs, lane, 0, keepdims=False)
    far_pair = swapped(lax.dynamic_index_in_dim(pairs, 1 - lane, 0, keepdims=False))
    pair_whole = lax.all_gather(
        jnp.stack([own_pair, far_pair]), "seq", axis_index_groups=plane_groups
    )

    seq_ids = jnp.arange(shards, dtype=jnp.int32)
    offsets = jnp.cumsum(span_counts) - span_counts
    own_offset = jnp.sum(jnp.where(seq_ids == me, offsets, 0))
    own_count = jnp.sum(jnp.where(seq_ids == me, span_counts, 0))
    place = jnp.concatenate([jnp.stack([me, lane]).astype(jnp.int32), offsets // TILE])
    own_marks = boundaries[0]
    positions = jnp.arange(rows_here, dtype=jnp.int32)
    local_ids = jnp.arange(capacity, dtype=jnp.int32)
    live = local_ids < own_count
    marks = jnp.concatenate([jnp.where(live, own_marks, -1), jnp.full((TILE,), -1, jnp.int32)])
    marks = jnp.roll(marks, own_offset % TILE)
    pool_pick = (positions[None, :] == marks[:, None]).astype(bf16)
    passed = jnp.sum(
        ((own_marks[None, :] <= positions[:, None]) & live[None, :]).astype(jnp.int32), axis=1
    )
    result_row = passed - 1 + own_offset % TILE
    spread = (jnp.arange(window, dtype=jnp.int32)[None, :] == result_row[:, None]).astype(bf16)

    local, through, ends = pl.pallas_call(
        scan_kernel,
        out_shape=(
            jax.ShapeDtypeStruct((rows_here, half), f32),
            jax.ShapeDtypeStruct((rows_here, half), f32),
            jax.ShapeDtypeStruct((shards, 2, half), f32),
        ),
        in_specs=[vmem()] * 5,
        out_specs=(vmem(),) * 3,
        compiler_params=params(),
    )(byte_states, outer_gain[None, :], mamba_input, mamba_step, decay_rate[None, :])
    ends = lax.all_to_all(ends, "seq", 0, 0, tiled=True)
    states, other_part = pl.pallas_call(
        states_kernel,
        out_shape=(
            jax.ShapeDtypeStruct((rows_here, half), bf16),
            jax.ShapeDtypeStruct((rows_here, half), f32),
        ),
        in_specs=[smem()] + [vmem()] * 4,
        out_specs=(vmem(),) * 2,
        compiler_params=params(),
    )(place, local, through, mixer_weight, ends)
    encoded, leaving = pl.pallas_call(
        pool_kernel,
        out_shape=(
            jax.ShapeDtypeStruct((rows_here, half), bf16),
            jax.ShapeDtypeStruct((layers, window, half), bf16),
        ),
        in_specs=[smem()] + [vmem()] * 5,
        out_specs=(vmem(),) * 2,
        compiler_params=params(),
    )(place, states, mixer_weight, swapped(other_part), byte_states, pool_pick)
    near = lax.all_to_all(leaving, "seq", 0, 0, axis_index_groups=layer_groups, tiled=True)
    near = lax.all_to_all(
        jnp.broadcast_to(near[None], (plane, layers, window, half)),
        "seq",
        0,
        0,
        axis_index_groups=plane_groups,
        tiled=True,
    )
    far = swapped(near)

    sums_width = 4 * HEAD
    own_sums, other_sums = pl.pallas_call(
        inner_kernel,
        out_shape=(jax.ShapeDtypeStruct((total_rows, sums_width), f32),) * 2,
        in_specs=[smem()] + [vmem()] * 2 + [in_place()] * 6,
        out_specs=(vmem(),) * 2,
        scratch_shapes=[
            pltpu.VMEM((plane, layers, window, width), bf16),
            pltpu.VMEM((total_rows + window, width), bf16),
            pltpu.VMEM((width, inner_half), bf16),
            pltpu.VMEM((inner_half, 6 * HEAD), bf16),
            pltpu.VMEM((min(256, total_rows), inner_half), bf16),
            pltpu.SemaphoreType.DMA((4 + 2 * shards,)),
        ],
        compiler_params=params(),
    )(place, up_bias[None, :], own_gain, near, far, up_whole, own_query, far_query, pair_whole)
    leaving = pl.pallas_call(
        functools.partial(attend_kernel, inner_width),
        out_shape=jax.ShapeDtypeStruct((shards, window, HEAD), bf16),
        in_specs=[smem()] + [vmem()] * 2,
        out_specs=vmem(),
        scratch_shapes=[
            pltpu.VMEM((total_rows, 3 * HEAD), bf16),
            pltpu.VMEM((total_rows + window, HEAD), bf16),
        ],
        compiler_params=params(),
    )(place, own_sums, swapped(other_sums))
    pieces = lax.all_to_all(leaving, "seq", 0, 0, tiled=True)
    own_back, other_back = pl.pallas_call(
        return_kernel,
        out_shape=(jax.ShapeDtypeStruct((window, half), f32),) * 2,
        in_specs=[smem()] + [vmem()] * 2,
        out_specs=(vmem(),) * 2,
        scratch_shapes=[pltpu.VMEM((window, shards * HEAD), bf16)],
        compiler_params=params(),
    )(place, return_weight, pieces)
    return pl.pallas_call(
        join_kernel,
        out_shape=jax.ShapeDtypeStruct((rows_here, half), bf16),
        in_specs=[vmem()] * 4,
        out_specs=vmem(),
        compiler_params=params(),
    )(own_back, swapped(other_back), encoded, spread)


def prefix(value, axis, join, neutral):
    count, mine = (lax.axis_size(axis), lax.axis_index(axis))
    pieces = jax.tree.map(lambda part: lax.all_gather(part, axis), value)
    so_far = jax.tree.map(
        lambda part, zero: jnp.full_like(part, 0) + jnp.asarray(zero, part.dtype), value, neutral
    )

    def lap(position, so_far):
        longer = join(so_far, jax.tree.map(lambda part: part[position], pieces))
        return jax.tree.map(lambda new, old: jnp.where(position < mine, new, old), longer, so_far)

    return lax.fori_loop(0, count - 1, lap, so_far)


def rms_scale(values, gain):
    values = values.astype(jnp.float32)
    return values * lax.rsqrt(jnp.mean(values * values, axis=-1, keepdims=True) + eps) * gain


def combine_pairs(earlier, later):
    return (earlier[0] * later[0], later[0] * earlier[1] + later[1])


def pick_table(table, wanted, seq_ids):
    return jnp.sum(jnp.where(seq_ids[None, :] == wanted[:, None], table[None, :], 0), axis=1)


def block_size(piece_rows, shard_rows):
    limit = max(1, 1024 // shard_rows)
    pieces = max(1, piece_rows // shard_rows)
    best_size = 1
    for candidate in range(1, limit + 1):
        if pieces % candidate == 0:
            best_size = candidate
    return min(piece_rows, best_size * shard_rows)


def spread_heads(
    byte_states,
    outer_gain,
    mamba_input,
    mamba_step,
    decay_rate,
    mixer_weight,
    boundaries,
    span_counts,
    up_weight,
    up_bias,
    inner_gain,
    query_weight,
    key_weight,
    value_weight,
    return_weight,
):
    shards = lax.axis_size("seq")
    own_shard = lax.axis_index("seq")
    own_lane = lax.axis_index("mp")
    rows_here = byte_states.shape[0]
    capacity = boundaries.shape[1]
    column_count = mamba_input.shape[1]
    kv_local = key_weight.shape[1] // HEAD
    group_size = HEADS // KV_HEADS
    slot_count = capacity // shards
    offsets = jnp.cumsum(span_counts) - span_counts
    seq_ids = jnp.arange(shards, dtype=jnp.int32)
    own_offset = jnp.sum(jnp.where(seq_ids == own_shard, offsets, 0))
    own_count = jnp.sum(jnp.where(seq_ids == own_shard, span_counts, 0))
    normed = rms_scale(byte_states, outer_gain).astype(jnp.bfloat16)
    inputs = jnp.dot(normed, mamba_input, preferred_element_type=jnp.float32)
    step_sizes = jax.nn.softplus(jnp.dot(normed, mamba_step, preferred_element_type=jnp.float32))
    rate_steps = step_sizes * decay_rate
    decays = jnp.exp(-rate_steps)
    drives = jnp.sqrt(-jnp.expm1(-2.0 * rate_steps)) * inputs
    through, local_states = lax.associative_scan(combine_pairs, (decays, drives), axis=0)
    starting = (jnp.ones((column_count,), jnp.float32), jnp.zeros((column_count,), jnp.float32))
    arriving = prefix((through[-1], local_states[-1]), "seq", combine_pairs, starting)
    states = (local_states + through * arriving[1][None, :]).astype(jnp.bfloat16)
    partial_value = jnp.dot(states, mixer_weight, preferred_element_type=jnp.float32)
    mixed_sum = lax.psum(partial_value, "mp")
    encoded = (byte_states.astype(jnp.float32) + mixed_sum).astype(jnp.bfloat16)
    skip_part = lax.dynamic_slice_in_dim(encoded, own_lane * column_count, column_count, 1)
    own_marks = boundaries[0]
    pooled = encoded[jnp.minimum(own_marks, rows_here - 1)]
    row_width = pooled.shape[1]
    outgoing = jnp.roll(pooled.reshape(slot_count, shards, row_width), own_offset % shards, axis=1)
    incoming = lax.all_to_all(outgoing, "seq", split_axis=1, concat_axis=1, tiled=True)
    position = jnp.arange(CH_OWN, dtype=jnp.int32)
    span_index = own_shard + position * shards
    source = jnp.sum((offsets[None, :] <= span_index[:, None]).astype(jnp.int32), axis=1) - 1
    source_offset = pick_table(offsets, source, seq_ids)
    slot_index = (span_index - source_offset) // shards
    gathered_rows = incoming.reshape(slot_count * shards, row_width)[slot_index * shards + source]
    columns = gathered_rows
    widened_sum = jnp.dot(
        columns,
        lax.all_gather(up_weight, "seq", axis=0, tiled=True),
        preferred_element_type=jnp.float32,
    )
    widened_share = (widened_sum + up_bias[None, :]).astype(jnp.bfloat16)
    widened = lax.all_gather(widened_share, "mp", axis=1, tiled=True)
    inner_normed = rms_scale(widened, inner_gain).astype(jnp.bfloat16)
    columns = inner_normed
    query_part = jnp.dot(
        columns,
        lax.all_gather(query_weight, "seq", axis=0, tiled=True),
        preferred_element_type=jnp.float32,
    )
    key_part = jnp.dot(
        columns,
        lax.all_gather(key_weight, "seq", axis=0, tiled=True),
        preferred_element_type=jnp.float32,
    )
    value_part = jnp.dot(
        columns,
        lax.all_gather(value_weight, "seq", axis=0, tiled=True),
        preferred_element_type=jnp.float32,
    )
    queries = query_part.astype(jnp.bfloat16)
    key_rows = key_part.astype(jnp.bfloat16)
    value_rows = value_part.astype(jnp.bfloat16)
    query_count = queries.shape[0]
    grouped = (
        queries.reshape(query_count, kv_local, group_size, HEAD)
        .transpose(1, 0, 2, 3)
        .reshape(kv_local, query_count * group_size, HEAD)
    )
    row_index = jnp.repeat(span_index, group_size)
    shard_rows = key_rows.shape[0]
    score_scale = 1.0 / math.sqrt(HEAD)

    def key_index(whole_index):
        return whole_index // shard_rows + whole_index % shard_rows * shards

    def attend_block(running, key_block, value_block, index_block):
        row_peak, denominator, weighted = running
        scores = (
            jnp.einsum("hqd,khd->hqk", grouped, key_block, preferred_element_type=jnp.float32)
            * score_scale
        )
        scores = jnp.where(index_block[None, None, :] <= row_index[None, :, None], scores, masked)
        new_peak = jnp.maximum(row_peak, jnp.max(scores, axis=2))
        shrink = jnp.exp(row_peak - new_peak)
        lifted = jnp.exp(scores - new_peak[:, :, None])
        denominator = denominator * shrink + jnp.sum(lifted, axis=2)
        weighted = weighted * shrink[:, :, None] + jnp.einsum(
            "hqk,khd->hqd",
            lifted.astype(jnp.bfloat16),
            value_block,
            preferred_element_type=jnp.float32,
        )
        return (new_peak, denominator, weighted)

    query_total = query_count * group_size
    initial = (
        jnp.full((kv_local, query_total), masked, jnp.float32),
        jnp.zeros((kv_local, query_total), jnp.float32),
        jnp.zeros((kv_local, query_total, HEAD), jnp.float32),
    )
    key_piece = lax.all_gather(key_rows, "seq", axis=0, tiled=True)
    value_piece = lax.all_gather(value_rows, "seq", axis=0, tiled=True)
    piece_rows = key_piece.shape[0]
    block_rows = block_size(piece_rows, shard_rows)
    turn_count = piece_rows // block_rows
    key_blocks = key_piece.reshape(turn_count, block_rows, kv_local, HEAD)
    value_blocks = value_piece.reshape(turn_count, block_rows, kv_local, HEAD)

    def one_turn(turn_index, inner_running):
        whole_index = turn_index * block_rows + jnp.arange(block_rows, dtype=jnp.int32)
        return attend_block(
            inner_running, key_blocks[turn_index], value_blocks[turn_index], key_index(whole_index)
        )

    row_peak, denominator, weighted = lax.fori_loop(0, turn_count, one_turn, initial)
    attended = (weighted / denominator[:, :, None]).astype(jnp.bfloat16)
    attended = (
        attended.reshape(kv_local, query_count, group_size, HEAD)
        .transpose(1, 0, 2, 3)
        .reshape(query_count, kv_local * group_size * HEAD)
    )
    projected = jnp.dot(attended, return_weight, preferred_element_type=jnp.float32)
    returned = lax.psum_scatter(
        projected.astype(jnp.bfloat16), "mp", scatter_dimension=1, tiled=True
    )
    slot_ids = jnp.arange(slot_count, dtype=jnp.int32)
    lead_slot = (own_shard - offsets) % shards
    local_span = slot_ids[:, None] * shards + lead_slot[None, :]
    back_index = (offsets[None, :] + local_span - own_shard) // shards
    alive = local_span < span_counts[None, :]
    back_rows = jnp.where(
        alive[:, :, None],
        returned[jnp.clip(back_index, 0, CH_OWN - 1)],
        jnp.zeros((), jnp.bfloat16),
    )
    arrived = lax.all_to_all(back_rows, "seq", split_axis=1, concat_axis=1, tiled=True)
    span_results = jnp.roll(arrived, -(own_offset % shards), axis=1).reshape(capacity, column_count)
    positions = jnp.arange(rows_here, dtype=jnp.int32)
    live_slots = jnp.arange(capacity, dtype=jnp.int32) < own_count
    passed = jnp.sum(
        ((own_marks[None, :] <= positions[:, None]) & live_slots[None, :]).astype(jnp.int32), axis=1
    )
    return (skip_part.astype(jnp.float32) + span_results[passed - 1].astype(jnp.float32)).astype(
        jnp.bfloat16
    )


def solution(mesh):
    in_specs = (
        P("seq", None),
        P(),
        P(None, "mp"),
        P(None, "mp"),
        P("mp"),
        P("mp", None),
        P("seq", None),
        P(),
        P("seq", "mp"),
        P("mp"),
        P(),
        P("seq", "mp"),
        P("seq", "mp"),
        P("seq", "mp"),
        P("mp", None),
    )
    out_specs = P("seq", "mp")
    def on_device(*arrays):
        heads_here = arrays[11].shape[1] // HEAD
        fits = heads_here == mesh.shape["seq"] and mesh.shape["mp"] == 2
        return (one_head_each if fits else spread_heads)(*arrays)

    return jax.shard_map(
        on_device, mesh=mesh, in_specs=in_specs, out_specs=out_specs, check_vma=False
    )
```

```python
import functools
import math

import jax
import jax.numpy as jnp
from jax import lax
from jax.experimental import pallas as pl
from jax.experimental.pallas import tpu as pltpu
from jax.sharding import PartitionSpec as P

HEADS = 32
KV_HEADS = 8
HEAD = 128
CH_OWN = 64


eps = 1e-05
masked = -1e30
TILE = 16
VMEM_BYTES = 56 * 2**20


def swapped(value):
    return lax.ppermute(value, "mp", [(0, 1), (1, 0)])


def vmem():
    return pl.BlockSpec(memory_space=pltpu.VMEM)


def smem():
    return pl.BlockSpec(memory_space=pltpu.SMEM)


def in_place():
    return pl.BlockSpec(memory_space=pl.ANY)


def params():
    return pltpu.CompilerParams(vmem_limit_bytes=VMEM_BYTES)


def lanes(which, size):
    return pl.ds(pl.multiple_of(which * size, size), size)


def one_minus_exp(u):
    series = jnp.ones_like(u)
    for order in range(9, 1, -1):
        series = 1.0 - u * (1.0 / order) * series
    return jnp.where(u < 0.5, u * series, 1.0 - jnp.exp(-u))


def softplus(v):
    tail = jnp.exp(-jnp.abs(v))
    series = jnp.ones_like(tail)
    for order in range(6, 1, -1):
        series = 1.0 - tail * ((order - 1.0) / order) * series
    return jnp.maximum(v, 0.0) + jnp.where(tail < 0.03, tail * series, jnp.log(1.0 + tail))


def scan_kernel(bytes_ref, gain_ref, input_ref, step_ref, rate_ref, local_ref, through_ref, ends_ref):
    values = bytes_ref[...].astype(jnp.float32)
    scale = lax.rsqrt(jnp.mean(values * values, axis=1, keepdims=True) + eps)
    normed = (values * scale * gain_ref[...]).astype(jnp.bfloat16)
    steps = softplus(jnp.dot(normed, step_ref[...], preferred_element_type=jnp.float32))
    rate_steps = steps * rate_ref[...]
    inputs = jnp.dot(normed, input_ref[...], preferred_element_type=jnp.float32)
    decays = jnp.exp(-rate_steps)
    drives = jnp.sqrt(one_minus_exp(2.0 * rate_steps)) * inputs
    rows, width = decays.shape
    tile = 8
    decays = decays.reshape(rows // tile, tile, width)
    drives = drives.reshape(rows // tile, tile, width)
    place = lax.broadcasted_iota(jnp.int32, decays.shape, 1)
    for reach in (1, 2, 4):
        before_decays = pltpu.roll(decays, reach, 1)
        before_drives = pltpu.roll(drives, reach, 1)
        inside = place >= reach
        drives = jnp.where(inside, decays * before_drives + drives, drives)
        decays = jnp.where(inside, decays * before_decays, decays)
    state = jnp.zeros((1, width), jnp.float32)
    kept = jnp.ones((1, width), jnp.float32)
    for index in range(rows // tile):
        states = decays[index] * state + drives[index]
        passing = decays[index] * kept
        local_ref[pl.ds(index * tile, tile), :] = states
        through_ref[pl.ds(index * tile, tile), :] = passing
        state = states[tile - 1 :, :]
        kept = passing[tile - 1 :, :]
    for index in range(ends_ref.shape[0]):
        ends_ref[index, 0:1, :] = kept
        ends_ref[index, 1:2, :] = state


def states_kernel(place_ref, local_ref, through_ref, mixer_ref, ends_ref, states_ref, other_ref):
    carry = jnp.zeros((1, local_ref.shape[1]), jnp.float32)
    for shard in range(ends_ref.shape[0]):
        later = ends_ref[shard, 0:1, :] * carry + ends_ref[shard, 1:2, :]
        carry = jnp.where(shard < place_ref[0], later, carry)
    states = (local_ref[...] + through_ref[...] * carry).astype(jnp.bfloat16)
    states_ref[...] = states
    half = other_ref.shape[1]
    other_ref[...] = jnp.dot(
        states, mixer_ref[:, lanes(1 - place_ref[1], half)], preferred_element_type=jnp.float32
    )


def pool_kernel(place_ref, states_ref, mixer_ref, other_ref, bytes_ref, pick_ref, encoded_ref, out_ref):
    half = other_ref.shape[1]
    columns = lanes(place_ref[1], half)
    mixed = jnp.dot(states_ref[...], mixer_ref[:, columns], preferred_element_type=jnp.float32)
    skip = bytes_ref[:, columns].astype(jnp.float32)
    encoded = (skip + (mixed + other_ref[...])).astype(jnp.bfloat16)
    encoded_ref[...] = encoded
    picked = jnp.dot(pick_ref[...], encoded, preferred_element_type=jnp.float32)
    out_ref[...] = picked.astype(jnp.bfloat16).reshape(out_ref.shape)


def own_kernel(pick_ref, arrived_ref, out_ref):
    shards, slots, half = arrived_ref.shape
    rows = arrived_ref[...].astype(jnp.float32).reshape(shards * slots, half)
    own = jnp.dot(
        pick_ref[...], rows.astype(jnp.bfloat16), preferred_element_type=jnp.float32
    ).astype(jnp.bfloat16)
    for index in range(out_ref.shape[0]):
        out_ref[index] = own


def inner_kernel(
    plane, place_ref, bias_ref, gain_ref, near_ref, far_ref, *rest
):
    up_pieces, rest = rest[: plane + 1], rest[plane + 1 :]
    pair_pieces, rest = rest[:plane], rest[plane:]
    own_ref, other_ref, pooled, up, weights, inner, sems = rest
    me, lane = place_ref[0], place_ref[1]
    layer, cross = me // plane, lax.rem(me, plane)
    half = near_ref.shape[1]
    layers = up_pieces[0].shape[0]
    up_rows = up_pieces[0].shape[1]
    pair_rows = pair_pieces[0].shape[2]
    rows = own_ref.shape[0]
    span = 2 * HEAD
    pairs = [
        (near_ref, pooled.at[:, lanes(lane, half)]),
        (far_ref, pooled.at[:, lanes(1 - lane, half)]),
    ]

    def rows_at(which, size):
        return pl.ds(pl.multiple_of(which * size, size), size)

    for number in range(plane - 1):
        for step in range(layers):
            shard = (layer ^ step) * plane + (cross ^ number)
            pairs.append((up_pieces[number].at[step], up.at[rows_at(shard, up_rows), :]))
    for step in range(layers):
        shard = (layer ^ step) * plane + (cross ^ (plane - 1))
        piece = up_pieces[plane - 1 + step // 2].at[step % 2]
        pairs.append((piece, up.at[rows_at(shard, up_rows), :]))
    for number in range(plane):
        for head in range(2):
            for step in range(layers // 2):
                shard = (lax.rem(layer, 2) ^ step) * plane + (cross ^ number)
                to_ref = weights.at[rows_at(shard, pair_rows), pl.ds(head * span, span)]
                pairs.append((pair_pieces[number].at[head, step], to_ref))
    copies = []
    for index, (from_ref, to_ref) in enumerate(pairs):
        copy = pltpu.make_async_copy(from_ref, to_ref, sems.at[index])
        copy.start()
        copies.append(copy)
    for copy in copies:
        copy.wait()

    block = inner.shape[0]
    part = min(1024, up.shape[1])
    parts = up.shape[1] // part

    def up_block(index, carried):
        where = rows_at(index, block)
        left = pooled[where, :]
        total = jnp.zeros((block, 1), jnp.float32)
        for number in range(parts):
            columns = pl.ds(number * part, part)
            widened = jnp.dot(left, up[:, columns], preferred_element_type=jnp.float32)
            widened = (widened + bias_ref[:, columns]).astype(jnp.bfloat16).astype(jnp.float32)
            inner[:, columns] = (widened * gain_ref[:, columns]).astype(jnp.bfloat16)
            total = total + jnp.sum(widened * widened, axis=1, keepdims=True)
        sums = jnp.dot(inner[...], weights[...], preferred_element_type=jnp.float32)
        spread = jnp.broadcast_to(total, (block, HEAD))
        own_ref[where, 0:span] = sums[:, :span]
        own_ref[where, span:] = spread
        other_ref[where, 0:span] = sums[:, span:]
        other_ref[where, span:] = spread
        return carried

    lax.fori_loop(0, rows // block, up_block, 0)


def heads_kernel(features, plane, own_ref, other_ref, query_ref, pair_ref, queries, pairs):
    rows = own_ref.shape[0]
    span = 2 * HEAD
    shards = rows // CH_OWN
    layers = shards // plane
    for index in range(shards):
        where = pl.ds(index * CH_OWN, CH_OWN)
        sums = own_ref[where, :] + other_ref[where, :]
        scale = lax.rsqrt(sums[:, span:] * (1.0 / features) + eps)
        shard = (index % layers) * plane + index // layers
        natural = pl.ds(shard, CH_OWN, stride=shards)
        queries[natural, :] = sums[:, :HEAD] * scale
        pairs[natural, :] = sums[:, HEAD:span] * scale
    query_ref[...] = queries[...].astype(jnp.bfloat16)
    pair_ref[...] = pairs[...].astype(jnp.bfloat16)


def attend_kernel(place_ref, query_ref, pair_ref, other_ref, out_ref, keys, values, attended):
    rows = query_ref.shape[0]
    window = out_ref.shape[1]
    block = min(256, rows)
    holds_keys = place_ref[2] == 0

    @pl.when(holds_keys)
    def _():
        keys[...] = pair_ref[...]
        values[...] = other_ref[...]

    @pl.when(jnp.logical_not(holds_keys))
    def _():
        keys[...] = other_ref[...]
        values[...] = pair_ref[...]

    score_scale = 1.0 / math.sqrt(HEAD)
    for start in range(0, rows, block):
        stop = start + block
        scores = lax.dot_general(
            query_ref[start:stop, :],
            keys[0:stop, :],
            (((1,), (1,)), ((), ())),
            preferred_element_type=jnp.float32,
        )
        spots = lax.broadcasted_iota(jnp.int32, scores.shape, 1)
        mine = lax.broadcasted_iota(jnp.int32, scores.shape, 0) + start
        scores = jnp.where(spots <= mine, scores * score_scale, masked)
        peak = jnp.max(scores, axis=1, keepdims=True)
        lifted = jnp.exp(scores - peak)
        denominator = jnp.sum(lifted, axis=1, keepdims=True)
        weighted = jnp.dot(
            lifted.astype(jnp.bfloat16), values[0:stop, :], preferred_element_type=jnp.float32
        )
        attended[start:stop, :] = (weighted / denominator).astype(jnp.bfloat16)
    attended[rows:, :] = jnp.zeros((attended.shape[0] - rows, HEAD), jnp.bfloat16)
    for shard in range(out_ref.shape[0]):
        first = place_ref[3 + shard]
        out_ref[shard] = attended[pl.ds(pl.multiple_of(first * TILE, TILE), window), :]


def return_kernel(place_ref, weight_ref, pieces_ref, own_ref, other_ref, attended):
    half = own_ref.shape[1]
    lane = place_ref[1]
    for head in range(pieces_ref.shape[0]):
        attended[:, head * HEAD : (head + 1) * HEAD] = pieces_ref[head]
    other_ref[...] = jnp.dot(
        attended[...], weight_ref[:, lanes(1 - lane, half)], preferred_element_type=jnp.float32
    )
    own_ref[...] = jnp.dot(
        attended[...], weight_ref[:, lanes(lane, half)], preferred_element_type=jnp.float32
    )


def join_kernel(own_ref, other_ref, encoded_ref, spread_ref, out_ref):
    returned = (own_ref[...] + other_ref[...]).astype(jnp.bfloat16)
    results = jnp.dot(spread_ref[...], returned, preferred_element_type=jnp.float32)
    out_ref[...] = (encoded_ref[...].astype(jnp.float32) + results).astype(jnp.bfloat16)


def one_head_each(
    byte_states,
    outer_gain,
    mamba_input,
    mamba_step,
    decay_rate,
    mixer_weight,
    boundaries,
    span_counts,
    up_weight,
    up_bias,
    inner_gain,
    query_weight,
    key_weight,
    value_weight,
    return_weight,
):
    shards = lax.axis_size("seq")
    me = lax.axis_index("seq")
    lane = lax.axis_index("mp")
    plane = HEADS // KV_HEADS
    layers = shards // plane
    rows_here, width = byte_states.shape
    half = mamba_input.shape[1]
    capacity = boundaries.shape[1]
    window = capacity + TILE
    total_rows = CH_OWN * shards
    inner_width = inner_gain.shape[0]
    inner_half = up_bias.shape[0]
    weight_rows = query_weight.shape[0]
    f32, bf16 = jnp.float32, jnp.bfloat16
    layer, cross = me // plane, me % plane
    layer_groups = [[first + plane * step for step in range(layers)] for first in range(plane)]
    plane_groups = [[first * plane + step for step in range(plane)] for first in range(layers)]

    def over(value, mask):
        return lax.ppermute(value, "seq", [(i, i ^ mask) for i in range(shards)])

    def after(value, done):
        return lax.optimization_barrier((value, done))[0]

    own_gain = lax.dynamic_slice_in_dim(inner_gain, lane * inner_half, inner_half)[None, :]
    up_layers = [up_weight] + [over(up_weight, plane * step) for step in range(1, layers)]

    def pair_columns(target):
        return jnp.concatenate(
            [
                lax.dynamic_slice_in_dim(query_weight, target * plane * HEAD, plane * HEAD, 1),
                lax.dynamic_slice_in_dim(key_weight, target * HEAD, HEAD, 1),
                lax.dynamic_slice_in_dim(value_weight, target * HEAD, HEAD, 1),
            ],
            axis=1,
        )

    pair_cuts = [pair_columns(layer ^ step) for step in range(layers)]

    seq_ids = jnp.arange(shards, dtype=jnp.int32)
    offsets = jnp.cumsum(span_counts) - span_counts
    own_offset = jnp.sum(jnp.where(seq_ids == me, offsets, 0))
    own_count = jnp.sum(jnp.where(seq_ids == me, span_counts, 0))
    place = jnp.concatenate([jnp.stack([me, lane, cross // 2]).astype(jnp.int32), offsets // TILE])
    own_marks = boundaries[0]
    positions = jnp.arange(rows_here, dtype=jnp.int32)
    spans_here = jnp.arange(capacity, dtype=jnp.int32)
    live = spans_here < own_count
    slots = capacity // shards
    slot_ids = jnp.arange(slots, dtype=jnp.int32)
    local_span = slot_ids[None, :] * shards + ((seq_ids - own_offset) % shards)[:, None]
    is_span = spans_here[None, :] == local_span.reshape(-1)[:, None]
    byte_at = jnp.sum(jnp.where(is_span, jnp.minimum(own_marks, rows_here - 1)[None, :], 0), axis=1)
    pool_pick = (positions[None, :] == byte_at[:, None]).astype(bf16)
    own_spans = me + jnp.arange(CH_OWN, dtype=jnp.int32) * shards
    origin = jnp.sum((offsets[None, :] <= own_spans[:, None]).astype(jnp.int32), axis=1) - 1
    origin_offset = jnp.sum(
        jnp.where(seq_ids[None, :] == origin[:, None], offsets[None, :], 0), axis=1
    )
    arrived_row = origin * slots + (own_spans - origin_offset) // shards
    own_pick = (
        jnp.arange(shards * slots, dtype=jnp.int32)[None, :] == arrived_row[:, None]
    ).astype(bf16)
    passed = jnp.sum(
        ((own_marks[None, :] <= positions[:, None]) & live[None, :]).astype(jnp.int32), axis=1
    )
    result_row = passed - 1 + own_offset % TILE
    spread = (jnp.arange(window, dtype=jnp.int32)[None, :] == result_row[:, None]).astype(bf16)

    local, through, ends = pl.pallas_call(
        scan_kernel,
        out_shape=(
            jax.ShapeDtypeStruct((rows_here, half), f32),
            jax.ShapeDtypeStruct((rows_here, half), f32),
            jax.ShapeDtypeStruct((shards, 2, half), f32),
        ),
        in_specs=[vmem()] * 5,
        out_specs=(vmem(),) * 3,
        compiler_params=params(),
    )(byte_states, outer_gain[None, :], mamba_input, mamba_step, decay_rate[None, :])
    pair_layers = [pair_cuts[0]] + [
        over(after(pair_cuts[step], ends), plane * step) for step in range(1, layers)
    ]
    ends = lax.all_to_all(ends, "seq", 0, 0, tiled=True)
    states, other_part = pl.pallas_call(
        states_kernel,
        out_shape=(
            jax.ShapeDtypeStruct((rows_here, half), bf16),
            jax.ShapeDtypeStruct((rows_here, half), f32),
        ),
        in_specs=[smem()] + [vmem()] * 4,
        out_specs=(vmem(),) * 2,
        compiler_params=params(),
    )(place, local, through, mixer_weight, ends)
    encoded, leaving = pl.pallas_call(
        pool_kernel,
        out_shape=(
            jax.ShapeDtypeStruct((rows_here, half), bf16),
            jax.ShapeDtypeStruct((shards, slots, half), bf16),
        ),
        in_specs=[smem()] + [vmem()] * 5,
        out_specs=(vmem(),) * 2,
        compiler_params=params(),
    )(place, states, mixer_weight, swapped(other_part), byte_states, pool_pick)
    arrived = lax.all_to_all(leaving, "seq", 0, 0, tiled=True)
    own_rows = pl.pallas_call(
        own_kernel,
        out_shape=jax.ShapeDtypeStruct((layers, CH_OWN, half), bf16),
        in_specs=[vmem()] * 2,
        out_specs=vmem(),
        compiler_params=params(),
    )(own_pick, arrived)
    near_layer = lax.all_to_all(
        own_rows, "seq", 0, 0, axis_index_groups=layer_groups, tiled=True
    )

    up_here = after(jnp.stack(up_layers), own_rows)
    up_beside = over(up_here, 1)
    up_across = over(up_here, 2)
    up_corner = [
        over(after(up_beside[: layers // 2], near_layer), 2),
        over(after(up_across[layers // 2 :], near_layer), 1),
    ]
    low, high = jnp.stack(pair_layers[: layers // 2]), jnp.stack(pair_layers[layers // 2 :])
    low_is_own = layer // (layers // 2) == lane
    low, high = after((low, high), near_layer)
    kept = jnp.where(low_is_own, low, high)
    far_kept = swapped(jnp.where(low_is_own, high, low))
    both = jnp.stack([kept, far_kept])

    def head_columns(target):
        return jnp.concatenate(
            [
                lax.dynamic_slice_in_dim(both, target * HEAD, HEAD, 3),
                lax.dynamic_slice_in_dim(both, (plane + target // 2) * HEAD, HEAD, 3),
            ],
            axis=3,
        )

    pair_pieces = [head_columns(cross)] + [
        over(head_columns(cross ^ mask), mask) for mask in range(1, plane)
    ]
    near = lax.all_to_all(
        jnp.broadcast_to(near_layer[None], (plane, layers, CH_OWN, half)),
        "seq",
        0,
        0,
        axis_index_groups=plane_groups,
        tiled=True,
    ).reshape(total_rows, half)

    up_pieces = [up_here, up_beside, up_across, *up_corner]
    sums_width = 3 * HEAD
    own_sums, other_sums = pl.pallas_call(
        functools.partial(inner_kernel, plane),
        out_shape=(jax.ShapeDtypeStruct((total_rows, sums_width), f32),) * 2,
        in_specs=[smem()] + [vmem()] * 2 + [in_place()] * (2 + len(up_pieces) + plane),
        out_specs=(vmem(),) * 2,
        scratch_shapes=[
            pltpu.VMEM((total_rows, width), bf16),
            pltpu.VMEM((width, inner_half), bf16),
            pltpu.VMEM((inner_half, 4 * HEAD), bf16),
            pltpu.VMEM((min(256, total_rows), inner_half), bf16),
            pltpu.SemaphoreType.DMA((2 + 2 * shards,)),
        ],
        compiler_params=params(),
    )(place, up_bias[None, :], own_gain, near, swapped(near), *up_pieces, *pair_pieces)
    queries, pairs = pl.pallas_call(
        functools.partial(heads_kernel, inner_width, plane),
        out_shape=(jax.ShapeDtypeStruct((total_rows, HEAD), bf16),) * 2,
        in_specs=[vmem()] * 2,
        out_specs=(vmem(),) * 2,
        scratch_shapes=[pltpu.VMEM((total_rows, HEAD), f32)] * 2,
        compiler_params=params(),
    )(own_sums, swapped(other_sums))
    leaving = pl.pallas_call(
        attend_kernel,
        out_shape=jax.ShapeDtypeStruct((shards, window, HEAD), bf16),
        in_specs=[smem()] + [vmem()] * 3,
        out_specs=vmem(),
        scratch_shapes=[
            pltpu.VMEM((total_rows, HEAD), bf16),
            pltpu.VMEM((total_rows, HEAD), bf16),
            pltpu.VMEM((total_rows + window, HEAD), bf16),
        ],
        compiler_params=params(),
    )(place, queries, pairs, over(pairs, 2))
    pieces = lax.all_to_all(leaving, "seq", 0, 0, tiled=True)
    own_back, other_back = pl.pallas_call(
        return_kernel,
        out_shape=(jax.ShapeDtypeStruct((window, half), f32),) * 2,
        in_specs=[smem()] + [vmem()] * 2,
        out_specs=(vmem(),) * 2,
        scratch_shapes=[pltpu.VMEM((window, shards * HEAD), bf16)],
        compiler_params=params(),
    )(place, return_weight, pieces)
    return pl.pallas_call(
        join_kernel,
        out_shape=jax.ShapeDtypeStruct((rows_here, half), bf16),
        in_specs=[vmem()] * 4,
        out_specs=vmem(),
        compiler_params=params(),
    )(own_back, swapped(other_back), encoded, spread)


def prefix(value, axis, join, neutral):
    count, mine = (lax.axis_size(axis), lax.axis_index(axis))
    pieces = jax.tree.map(lambda part: lax.all_gather(part, axis), value)
    so_far = jax.tree.map(
        lambda part, zero: jnp.full_like(part, 0) + jnp.asarray(zero, part.dtype), value, neutral
    )

    def lap(position, so_far):
        longer = join(so_far, jax.tree.map(lambda part: part[position], pieces))
        return jax.tree.map(lambda new, old: jnp.where(position < mine, new, old), longer, so_far)

    return lax.fori_loop(0, count - 1, lap, so_far)


def rms_scale(values, gain):
    values = values.astype(jnp.float32)
    return values * lax.rsqrt(jnp.mean(values * values, axis=-1, keepdims=True) + eps) * gain


def combine_pairs(earlier, later):
    return (earlier[0] * later[0], later[0] * earlier[1] + later[1])


def pick_table(table, wanted, seq_ids):
    return jnp.sum(jnp.where(seq_ids[None, :] == wanted[:, None], table[None, :], 0), axis=1)


def block_size(piece_rows, shard_rows):
    limit = max(1, 1024 // shard_rows)
    pieces = max(1, piece_rows // shard_rows)
    best_size = 1
    for candidate in range(1, limit + 1):
        if pieces % candidate == 0:
            best_size = candidate
    return min(piece_rows, best_size * shard_rows)


def spread_heads(
    byte_states,
    outer_gain,
    mamba_input,
    mamba_step,
    decay_rate,
    mixer_weight,
    boundaries,
    span_counts,
    up_weight,
    up_bias,
    inner_gain,
    query_weight,
    key_weight,
    value_weight,
    return_weight,
):
    shards = lax.axis_size("seq")
    own_shard = lax.axis_index("seq")
    own_lane = lax.axis_index("mp")
    rows_here = byte_states.shape[0]
    capacity = boundaries.shape[1]
    column_count = mamba_input.shape[1]
    kv_local = key_weight.shape[1] // HEAD
    group_size = HEADS // KV_HEADS
    slot_count = capacity // shards
    offsets = jnp.cumsum(span_counts) - span_counts
    seq_ids = jnp.arange(shards, dtype=jnp.int32)
    own_offset = jnp.sum(jnp.where(seq_ids == own_shard, offsets, 0))
    own_count = jnp.sum(jnp.where(seq_ids == own_shard, span_counts, 0))
    normed = rms_scale(byte_states, outer_gain).astype(jnp.bfloat16)
    inputs = jnp.dot(normed, mamba_input, preferred_element_type=jnp.float32)
    step_sizes = jax.nn.softplus(jnp.dot(normed, mamba_step, preferred_element_type=jnp.float32))
    rate_steps = step_sizes * decay_rate
    decays = jnp.exp(-rate_steps)
    drives = jnp.sqrt(-jnp.expm1(-2.0 * rate_steps)) * inputs
    through, local_states = lax.associative_scan(combine_pairs, (decays, drives), axis=0)
    starting = (jnp.ones((column_count,), jnp.float32), jnp.zeros((column_count,), jnp.float32))
    arriving = prefix((through[-1], local_states[-1]), "seq", combine_pairs, starting)
    states = (local_states + through * arriving[1][None, :]).astype(jnp.bfloat16)
    partial_value = jnp.dot(states, mixer_weight, preferred_element_type=jnp.float32)
    mixed_sum = lax.psum(partial_value, "mp")
    encoded = (byte_states.astype(jnp.float32) + mixed_sum).astype(jnp.bfloat16)
    skip_part = lax.dynamic_slice_in_dim(encoded, own_lane * column_count, column_count, 1)
    own_marks = boundaries[0]
    pooled = encoded[jnp.minimum(own_marks, rows_here - 1)]
    row_width = pooled.shape[1]
    outgoing = jnp.roll(pooled.reshape(slot_count, shards, row_width), own_offset % shards, axis=1)
    incoming = lax.all_to_all(outgoing, "seq", split_axis=1, concat_axis=1, tiled=True)
    position = jnp.arange(CH_OWN, dtype=jnp.int32)
    span_index = own_shard + position * shards
    source = jnp.sum((offsets[None, :] <= span_index[:, None]).astype(jnp.int32), axis=1) - 1
    source_offset = pick_table(offsets, source, seq_ids)
    slot_index = (span_index - source_offset) // shards
    gathered_rows = incoming.reshape(slot_count * shards, row_width)[slot_index * shards + source]
    columns = gathered_rows
    widened_sum = jnp.dot(
        columns,
        lax.all_gather(up_weight, "seq", axis=0, tiled=True),
        preferred_element_type=jnp.float32,
    )
    widened_share = (widened_sum + up_bias[None, :]).astype(jnp.bfloat16)
    widened = lax.all_gather(widened_share, "mp", axis=1, tiled=True)
    inner_normed = rms_scale(widened, inner_gain).astype(jnp.bfloat16)
    columns = inner_normed
    query_part = jnp.dot(
        columns,
        lax.all_gather(query_weight, "seq", axis=0, tiled=True),
        preferred_element_type=jnp.float32,
    )
    key_part = jnp.dot(
        columns,
        lax.all_gather(key_weight, "seq", axis=0, tiled=True),
        preferred_element_type=jnp.float32,
    )
    value_part = jnp.dot(
        columns,
        lax.all_gather(value_weight, "seq", axis=0, tiled=True),
        preferred_element_type=jnp.float32,
    )
    queries = query_part.astype(jnp.bfloat16)
    key_rows = key_part.astype(jnp.bfloat16)
    value_rows = value_part.astype(jnp.bfloat16)
    query_count = queries.shape[0]
    grouped = (
        queries.reshape(query_count, kv_local, group_size, HEAD)
        .transpose(1, 0, 2, 3)
        .reshape(kv_local, query_count * group_size, HEAD)
    )
    row_index = jnp.repeat(span_index, group_size)
    shard_rows = key_rows.shape[0]
    score_scale = 1.0 / math.sqrt(HEAD)

    def key_index(whole_index):
        return whole_index // shard_rows + whole_index % shard_rows * shards

    def attend_block(running, key_block, value_block, index_block):
        row_peak, denominator, weighted = running
        scores = (
            jnp.einsum("hqd,khd->hqk", grouped, key_block, preferred_element_type=jnp.float32)
            * score_scale
        )
        scores = jnp.where(index_block[None, None, :] <= row_index[None, :, None], scores, masked)
        new_peak = jnp.maximum(row_peak, jnp.max(scores, axis=2))
        shrink = jnp.exp(row_peak - new_peak)
        lifted = jnp.exp(scores - new_peak[:, :, None])
        denominator = denominator * shrink + jnp.sum(lifted, axis=2)
        weighted = weighted * shrink[:, :, None] + jnp.einsum(
            "hqk,khd->hqd",
            lifted.astype(jnp.bfloat16),
            value_block,
            preferred_element_type=jnp.float32,
        )
        return (new_peak, denominator, weighted)

    query_total = query_count * group_size
    initial = (
        jnp.full((kv_local, query_total), masked, jnp.float32),
        jnp.zeros((kv_local, query_total), jnp.float32),
        jnp.zeros((kv_local, query_total, HEAD), jnp.float32),
    )
    key_piece = lax.all_gather(key_rows, "seq", axis=0, tiled=True)
    value_piece = lax.all_gather(value_rows, "seq", axis=0, tiled=True)
    piece_rows = key_piece.shape[0]
    block_rows = block_size(piece_rows, shard_rows)
    turn_count = piece_rows // block_rows
    key_blocks = key_piece.reshape(turn_count, block_rows, kv_local, HEAD)
    value_blocks = value_piece.reshape(turn_count, block_rows, kv_local, HEAD)

    def one_turn(turn_index, inner_running):
        whole_index = turn_index * block_rows + jnp.arange(block_rows, dtype=jnp.int32)
        return attend_block(
            inner_running, key_blocks[turn_index], value_blocks[turn_index], key_index(whole_index)
        )

    row_peak, denominator, weighted = lax.fori_loop(0, turn_count, one_turn, initial)
    attended = (weighted / denominator[:, :, None]).astype(jnp.bfloat16)
    attended = (
        attended.reshape(kv_local, query_count, group_size, HEAD)
        .transpose(1, 0, 2, 3)
        .reshape(query_count, kv_local * group_size * HEAD)
    )
    projected = jnp.dot(attended, return_weight, preferred_element_type=jnp.float32)
    returned = lax.psum_scatter(
        projected.astype(jnp.bfloat16), "mp", scatter_dimension=1, tiled=True
    )
    slot_ids = jnp.arange(slot_count, dtype=jnp.int32)
    lead_slot = (own_shard - offsets) % shards
    local_span = slot_ids[:, None] * shards + lead_slot[None, :]
    back_index = (offsets[None, :] + local_span - own_shard) // shards
    alive = local_span < span_counts[None, :]
    back_rows = jnp.where(
        alive[:, :, None],
        returned[jnp.clip(back_index, 0, CH_OWN - 1)],
        jnp.zeros((), jnp.bfloat16),
    )
    arrived = lax.all_to_all(back_rows, "seq", split_axis=1, concat_axis=1, tiled=True)
    span_results = jnp.roll(arrived, -(own_offset % shards), axis=1).reshape(capacity, column_count)
    positions = jnp.arange(rows_here, dtype=jnp.int32)
    live_slots = jnp.arange(capacity, dtype=jnp.int32) < own_count
    passed = jnp.sum(
        ((own_marks[None, :] <= positions[:, None]) & live_slots[None, :]).astype(jnp.int32), axis=1
    )
    return (skip_part.astype(jnp.float32) + span_results[passed - 1].astype(jnp.float32)).astype(
        jnp.bfloat16
    )


def solution(mesh):
    in_specs = (
        P("seq", None),
        P(),
        P(None, "mp"),
        P(None, "mp"),
        P("mp"),
        P("mp", None),
        P("seq", None),
        P(),
        P("seq", "mp"),
        P("mp"),
        P(),
        P("seq", "mp"),
        P("seq", "mp"),
        P("seq", "mp"),
        P("mp", None),
    )
    out_specs = P("seq", "mp")
    def on_device(*arrays):
        heads_here = arrays[11].shape[1] // HEAD
        fits = heads_here == mesh.shape["seq"] and mesh.shape["mp"] == 2
        return (one_head_each if fits else spread_heads)(*arrays)

    return jax.shard_map(
        on_device, mesh=mesh, in_specs=in_specs, out_specs=out_specs, check_vma=False
    )
```

```python
import functools
import math

import jax
import jax.numpy as jnp
from jax import lax
from jax.experimental import pallas as pl
from jax.experimental.pallas import tpu as pltpu
from jax.sharding import PartitionSpec as P

HEADS = 32
KV_HEADS = 8
HEAD = 128
CH_OWN = 64


eps = 1e-05
masked = -1e30
TILE = 16


def swapped(value):
    return lax.ppermute(value, "mp", [(0, 1), (1, 0)])


def vmem():
    return pl.BlockSpec(memory_space=pltpu.VMEM)


def smem():
    return pl.BlockSpec(memory_space=pltpu.SMEM)


def in_place():
    return pl.BlockSpec(memory_space=pl.ANY)


def params(mebibytes=24):
    return pltpu.CompilerParams(vmem_limit_bytes=mebibytes * 2**20)


def brief():
    return pl.CostEstimate(flops=1, bytes_accessed=1, transcendentals=0)


def lanes(which, size):
    return pl.ds(pl.multiple_of(which * size, size), size)


def one_minus_exp(u):
    series = jnp.ones_like(u)
    for order in range(9, 1, -1):
        series = 1.0 - u * (1.0 / order) * series
    return jnp.where(u < 0.5, u * series, 1.0 - jnp.exp(-u))


def softplus(v):
    tail = jnp.exp(-jnp.abs(v))
    series = jnp.ones_like(tail)
    for order in range(6, 1, -1):
        series = 1.0 - tail * ((order - 1.0) / order) * series
    return jnp.maximum(v, 0.0) + jnp.where(tail < 0.03, tail * series, jnp.log(1.0 + tail))


def scan_kernel(bytes_ref, gain_ref, input_ref, step_ref, rate_ref, local_ref, through_ref, ends_ref):
    values = bytes_ref[...].astype(jnp.float32)
    scale = lax.rsqrt(jnp.mean(values * values, axis=1, keepdims=True) + eps)
    normed = (values * scale * gain_ref[...]).astype(jnp.bfloat16)
    steps = softplus(jnp.dot(normed, step_ref[...], preferred_element_type=jnp.float32))
    rate_steps = steps * rate_ref[...]
    inputs = jnp.dot(normed, input_ref[...], preferred_element_type=jnp.float32)
    decays = jnp.exp(-rate_steps)
    drives = jnp.sqrt(one_minus_exp(2.0 * rate_steps)) * inputs
    rows, width = decays.shape
    tile = 8
    decays = decays.reshape(rows // tile, tile, width)
    drives = drives.reshape(rows // tile, tile, width)
    place = lax.broadcasted_iota(jnp.int32, decays.shape, 1)
    for reach in (1, 2, 4):
        before_decays = pltpu.roll(decays, reach, 1)
        before_drives = pltpu.roll(drives, reach, 1)
        inside = place >= reach
        drives = jnp.where(inside, decays * before_drives + drives, drives)
        decays = jnp.where(inside, decays * before_decays, decays)
    state = jnp.zeros((1, width), jnp.float32)
    kept = jnp.ones((1, width), jnp.float32)
    for index in range(rows // tile):
        states = decays[index] * state + drives[index]
        passing = decays[index] * kept
        local_ref[pl.ds(index * tile, tile), :] = states
        through_ref[pl.ds(index * tile, tile), :] = passing
        state = states[tile - 1 :, :]
        kept = passing[tile - 1 :, :]
    for index in range(ends_ref.shape[0]):
        ends_ref[index, 0:1, :] = kept
        ends_ref[index, 1:2, :] = state


def states_kernel(place_ref, local_ref, through_ref, mixer_ref, ends_ref, states_ref, other_ref):
    carry = jnp.zeros((1, local_ref.shape[1]), jnp.float32)
    for shard in range(ends_ref.shape[0]):
        later = ends_ref[shard, 0:1, :] * carry + ends_ref[shard, 1:2, :]
        carry = jnp.where(shard < place_ref[0], later, carry)
    states = (local_ref[...] + through_ref[...] * carry).astype(jnp.bfloat16)
    states_ref[...] = states
    half = other_ref.shape[1]
    other_ref[...] = jnp.dot(
        states, mixer_ref[:, lanes(1 - place_ref[1], half)], preferred_element_type=jnp.float32
    )


def pool_kernel(place_ref, states_ref, mixer_ref, other_ref, bytes_ref, pick_ref, encoded_ref, out_ref):
    half = other_ref.shape[1]
    columns = lanes(place_ref[1], half)
    mixed = jnp.dot(states_ref[...], mixer_ref[:, columns], preferred_element_type=jnp.float32)
    skip = bytes_ref[:, columns].astype(jnp.float32)
    encoded = (skip + (mixed + other_ref[...])).astype(jnp.bfloat16)
    encoded_ref[...] = encoded
    picked = jnp.dot(pick_ref[...], encoded, preferred_element_type=jnp.float32)
    out_ref[...] = picked.astype(jnp.bfloat16).reshape(out_ref.shape)


def own_kernel(pick_ref, arrived_ref, out_ref):
    shards, slots, half = arrived_ref.shape
    rows = arrived_ref[...].astype(jnp.float32).reshape(shards * slots, half)
    own = jnp.dot(
        pick_ref[...], rows.astype(jnp.bfloat16), preferred_element_type=jnp.float32
    ).astype(jnp.bfloat16)
    for index in range(out_ref.shape[0]):
        out_ref[index] = own


def rows_at(which, size):
    return pl.ds(pl.multiple_of(which * size, size), size)


def copy_all(pairs, sems):
    copies = []
    for index, (from_ref, to_ref) in enumerate(pairs):
        copy = pltpu.make_async_copy(from_ref, to_ref, sems.at[index])
        copy.start()
        copies.append(copy)
    for copy in copies:
        copy.wait()


def cut_kernel(plane, place_ref, query_ref, key_ref, value_ref, *rest):
    outs, sems = rest[:-1], rest[-1]
    layers = outs[0].shape[0]
    cross = lax.rem(place_ref[0], plane)
    pairs = []
    for mask in range(plane):
        for layer in range(layers):
            column = lanes(layer * plane + (cross ^ mask), HEAD)
            pairs.append((query_ref.at[:, column], outs[mask].at[layer, :, pl.ds(0, HEAD)]))

    def start(far_ref, first_masks):
        for mask in first_masks:
            for layer in range(layers):
                number = mask * layers + layer
                pltpu.make_async_copy(
                    far_ref.at[:, pl.ds(layer * HEAD, HEAD)],
                    outs[mask].at[layer, :, pl.ds(HEAD, HEAD)],
                    sems.at[plane * layers + number],
                ).start()

    here, there = range(plane // 2), range(plane // 2, plane)

    @pl.when(place_ref[2] == 0)
    def _():
        start(key_ref, here)
        start(value_ref, there)

    @pl.when(place_ref[2] != 0)
    def _():
        start(value_ref, here)
        start(key_ref, there)

    copy_all(pairs, sems)
    for mask in range(plane):
        for layer in range(layers):
            number = mask * layers + layer
            pltpu.make_async_copy(
                key_ref.at[:, pl.ds(layer * HEAD, HEAD)],
                outs[mask].at[layer, :, pl.ds(HEAD, HEAD)],
                sems.at[plane * layers + number],
            ).wait()


def regroup_kernel(plane, place_ref, gate_ref, *rest):
    pieces, rest = rest[:plane], rest[plane:]
    layers = pieces[0].shape[0]
    up_pieces, rest = rest[:layers], rest[layers:]
    outs, (up_ref, sems) = rest[:layers], rest[layers:]
    layer = place_ref[0] // plane
    pairs = []
    for step in range(layers):
        pairs.append((up_pieces[step], up_ref.at[step]))
    for step in range(layers):
        for mask in range(plane):
            pairs.append((pieces[mask].at[layer ^ step], outs[step].at[mask]))
    copy_all(pairs, sems)


def up_kernel(
    plane, place_ref, bias_ref, gain_ref, near_ref, far_ref, *rest
):
    up_pieces, rest = rest[: plane + 1], rest[plane + 1 :]
    inner_ref, total_ref, pooled, up, sems = rest
    me, lane = place_ref[0], place_ref[1]
    layer, cross = me // plane, lax.rem(me, plane)
    half = near_ref.shape[1]
    up_rows = up_pieces[0].shape[1]
    rows = inner_ref.shape[0]
    pairs = [
        (near_ref, pooled.at[:, lanes(lane, half)]),
        (far_ref, pooled.at[:, lanes(1 - lane, half)]),
    ]
    layers = up_pieces[0].shape[0]
    for mask in range(plane):
        for step in range(layers):
            shard = (layer ^ step) * plane + (cross ^ mask)
            piece = up_pieces[mask].at[step]
            if mask == plane - 1:
                piece = up_pieces[mask + step // (layers // 2)].at[step % (layers // 2)]
            pairs.append((piece, up.at[rows_at(shard, up_rows), :]))
    copy_all(pairs, sems)
    block = min(256, rows)
    part = min(1024, up.shape[1])

    def up_block(index, carried):
        where = rows_at(index, block)
        left = pooled[where, :]
        total = jnp.zeros((block, 1), jnp.float32)
        for start in range(0, up.shape[1], part):
            columns = pl.ds(start, part)
            widened = jnp.dot(left, up[:, columns], preferred_element_type=jnp.float32)
            widened = (widened + bias_ref[:, columns]).astype(jnp.bfloat16).astype(jnp.float32)
            inner_ref[where, columns] = (widened * gain_ref[:, columns]).astype(jnp.bfloat16)
            total = total + jnp.sum(widened * widened, axis=1, keepdims=True)
        total_ref[where, :] = jnp.broadcast_to(total, (block, HEAD))
        return carried

    lax.fori_loop(0, rows // block, up_block, 0)


def sums_kernel(plane, place_ref, inner_ref, total_ref, *rest):
    layers = (len(rest) - 4) // 2
    mine, far = rest[:layers], rest[layers : 2 * layers]
    own_ref, other_ref, weights, sems = rest[2 * layers :]
    me, lane = place_ref[0], place_ref[1]
    layer, cross = me // plane, lax.rem(me, plane)
    piece_rows = mine[0].shape[1]
    rows = inner_ref.shape[0]
    span = 2 * HEAD
    keep = layers // 2

    def pairs_from(first):
        pairs = []
        for head, pieces in enumerate((mine, far)):
            for step in range(keep):
                for mask in range(plane):
                    shard = (lax.rem(layer, keep) ^ step) * plane + (cross ^ mask)
                    to_ref = weights.at[rows_at(shard, piece_rows), pl.ds(head * span, span)]
                    pairs.append((pieces[first + step].at[mask], to_ref))
        return pairs

    low_is_own = layer // keep == lane

    @pl.when(low_is_own)
    def _():
        copy_all(pairs_from(0), sems)

    @pl.when(jnp.logical_not(low_is_own))
    def _():
        copy_all(pairs_from(keep), sems)

    block = min(256, rows)

    def sums_block(index, carried):
        where = rows_at(index, block)
        sums = jnp.dot(inner_ref[where, :], weights[...], preferred_element_type=jnp.float32)
        own_ref[where, 0:span] = sums[:, :span]
        own_ref[where, span:] = total_ref[where, :]
        other_ref[where, 0:span] = sums[:, span:]
        other_ref[where, span:] = total_ref[where, :]
        return carried

    lax.fori_loop(0, rows // block, sums_block, 0)


def heads_kernel(features, plane, own_ref, other_ref, query_ref, pair_ref, queries, pairs):
    rows = own_ref.shape[0]
    span = 2 * HEAD
    shards = rows // CH_OWN
    layers = shards // plane
    for index in range(shards):
        where = pl.ds(index * CH_OWN, CH_OWN)
        sums = own_ref[where, :] + other_ref[where, :]
        scale = lax.rsqrt(sums[:, span:] * (1.0 / features) + eps)
        shard = (index % layers) * plane + index // layers
        natural = pl.ds(shard, CH_OWN, stride=shards)
        queries[natural, :] = sums[:, :HEAD] * scale
        pairs[natural, :] = sums[:, HEAD:span] * scale
    query_ref[...] = queries[...].astype(jnp.bfloat16)
    pair_ref[...] = pairs[...].astype(jnp.bfloat16)


def attend_kernel(place_ref, query_ref, pair_ref, other_ref, out_ref, keys, values, attended):
    rows = query_ref.shape[0]
    window = out_ref.shape[1]
    block = min(256, rows)
    holds_keys = place_ref[2] == 0

    @pl.when(holds_keys)
    def _():
        keys[...] = pair_ref[...]
        values[...] = other_ref[...]

    @pl.when(jnp.logical_not(holds_keys))
    def _():
        keys[...] = other_ref[...]
        values[...] = pair_ref[...]

    score_scale = 1.0 / math.sqrt(HEAD)
    for start in range(0, rows, block):
        stop = start + block
        scores = lax.dot_general(
            query_ref[start:stop, :],
            keys[0:stop, :],
            (((1,), (1,)), ((), ())),
            preferred_element_type=jnp.float32,
        )
        spots = lax.broadcasted_iota(jnp.int32, scores.shape, 1)
        mine = lax.broadcasted_iota(jnp.int32, scores.shape, 0) + start
        scores = jnp.where(spots <= mine, scores * score_scale, masked)
        peak = jnp.max(scores, axis=1, keepdims=True)
        lifted = jnp.exp(scores - peak)
        denominator = jnp.sum(lifted, axis=1, keepdims=True)
        weighted = jnp.dot(
            lifted.astype(jnp.bfloat16), values[0:stop, :], preferred_element_type=jnp.float32
        )
        attended[start:stop, :] = (weighted / denominator).astype(jnp.bfloat16)
    attended[rows:, :] = jnp.zeros((attended.shape[0] - rows, HEAD), jnp.bfloat16)
    for shard in range(out_ref.shape[0]):
        first = place_ref[3 + shard]
        out_ref[shard] = attended[pl.ds(pl.multiple_of(first * TILE, TILE), window), :]


def return_kernel(place_ref, weight_ref, pieces_ref, own_ref, other_ref, attended):
    half = own_ref.shape[1]
    lane = place_ref[1]
    for head in range(pieces_ref.shape[0]):
        attended[:, head * HEAD : (head + 1) * HEAD] = pieces_ref[head]
    other_ref[...] = jnp.dot(
        attended[...], weight_ref[:, lanes(1 - lane, half)], preferred_element_type=jnp.float32
    )
    own_ref[...] = jnp.dot(
        attended[...], weight_ref[:, lanes(lane, half)], preferred_element_type=jnp.float32
    )


def join_kernel(own_ref, other_ref, encoded_ref, spread_ref, out_ref):
    returned = (own_ref[...] + other_ref[...]).astype(jnp.bfloat16)
    results = jnp.dot(spread_ref[...], returned, preferred_element_type=jnp.float32)
    out_ref[...] = (encoded_ref[...].astype(jnp.float32) + results).astype(jnp.bfloat16)


def one_head_each(
    byte_states,
    outer_gain,
    mamba_input,
    mamba_step,
    decay_rate,
    mixer_weight,
    boundaries,
    span_counts,
    up_weight,
    up_bias,
    inner_gain,
    query_weight,
    key_weight,
    value_weight,
    return_weight,
):
    shards = lax.axis_size("seq")
    me = lax.axis_index("seq")
    lane = lax.axis_index("mp")
    plane = HEADS // KV_HEADS
    layers = shards // plane
    rows_here, width = byte_states.shape
    half = mamba_input.shape[1]
    capacity = boundaries.shape[1]
    window = capacity + TILE
    total_rows = CH_OWN * shards
    inner_width = inner_gain.shape[0]
    inner_half = up_bias.shape[0]
    weight_rows = query_weight.shape[0]
    f32, bf16 = jnp.float32, jnp.bfloat16
    layer, cross = me // plane, me % plane
    layer_groups = [[first + plane * step for step in range(layers)] for first in range(plane)]
    plane_groups = [[first * plane + step for step in range(plane)] for first in range(layers)]

    def over(value, mask):
        return lax.ppermute(value, "seq", [(i, i ^ mask) for i in range(shards)])

    def after(value, done):
        return lax.optimization_barrier((value, done))[0]

    own_gain = lax.dynamic_slice_in_dim(inner_gain, lane * inner_half, inner_half)[None, :]
    seq_ids = jnp.arange(shards, dtype=jnp.int32)
    offsets = jnp.cumsum(span_counts) - span_counts
    own_offset = jnp.sum(jnp.where(seq_ids == me, offsets, 0))
    own_count = jnp.sum(jnp.where(seq_ids == me, span_counts, 0))
    place = jnp.concatenate([jnp.stack([me, lane, cross // 2]).astype(jnp.int32), offsets // TILE])
    own_marks = boundaries[0]
    positions = jnp.arange(rows_here, dtype=jnp.int32)
    spans_here = jnp.arange(capacity, dtype=jnp.int32)
    live = spans_here < own_count
    slots = capacity // shards
    slot_ids = jnp.arange(slots, dtype=jnp.int32)
    local_span = slot_ids[None, :] * shards + ((seq_ids - own_offset) % shards)[:, None]
    is_span = spans_here[None, :] == local_span.reshape(-1)[:, None]
    byte_at = jnp.sum(jnp.where(is_span, jnp.minimum(own_marks, rows_here - 1)[None, :], 0), axis=1)
    pool_pick = (positions[None, :] == byte_at[:, None]).astype(bf16)
    own_spans = me + jnp.arange(CH_OWN, dtype=jnp.int32) * shards
    origin = jnp.sum((offsets[None, :] <= own_spans[:, None]).astype(jnp.int32), axis=1) - 1
    origin_offset = jnp.sum(
        jnp.where(seq_ids[None, :] == origin[:, None], offsets[None, :], 0), axis=1
    )
    arrived_row = origin * slots + (own_spans - origin_offset) // shards
    own_pick = (
        jnp.arange(shards * slots, dtype=jnp.int32)[None, :] == arrived_row[:, None]
    ).astype(bf16)
    passed = jnp.sum(
        ((own_marks[None, :] <= positions[:, None]) & live[None, :]).astype(jnp.int32), axis=1
    )
    result_row = passed - 1 + own_offset % TILE
    spread = (jnp.arange(window, dtype=jnp.int32)[None, :] == result_row[:, None]).astype(bf16)

    up_layers = [up_weight] + [over(up_weight, plane * step) for step in range(1, layers - 1)]
    cuts = pl.pallas_call(
        functools.partial(cut_kernel, plane),
        out_shape=(jax.ShapeDtypeStruct((layers, weight_rows, 2 * HEAD), bf16),) * plane,
        in_specs=[smem()] + [in_place()] * 3,
        out_specs=(in_place(),) * plane,
        scratch_shapes=[pltpu.SemaphoreType.DMA((2 * shards,))],
        cost_estimate=brief(),
        compiler_params=params(),
    )(place, query_weight, key_weight, value_weight)
    pair_planes = [cuts[0]] + [over(cuts[mask], mask) for mask in range(1, plane - 1)]

    local, through, ends = pl.pallas_call(
        scan_kernel,
        out_shape=(
            jax.ShapeDtypeStruct((rows_here, half), f32),
            jax.ShapeDtypeStruct((rows_here, half), f32),
            jax.ShapeDtypeStruct((shards, 2, half), f32),
        ),
        in_specs=[vmem()] * 5,
        out_specs=(vmem(),) * 3,
        cost_estimate=brief(),
        compiler_params=params(),
    )(byte_states, outer_gain[None, :], mamba_input, mamba_step, decay_rate[None, :])
    up_layers.append(over(after(up_weight, ends), plane * (layers - 1)))
    pair_planes.append(over(after(cuts[plane - 1], ends), plane - 1))
    ends = lax.all_to_all(ends, "seq", 0, 0, tiled=True)
    ends, up_layers[1], up_layers[2], pair_planes[1], pair_planes[2] = lax.optimization_barrier(
        (ends, up_layers[1], up_layers[2], pair_planes[1], pair_planes[2])
    )
    states, other_part = pl.pallas_call(
        states_kernel,
        out_shape=(
            jax.ShapeDtypeStruct((rows_here, half), bf16),
            jax.ShapeDtypeStruct((rows_here, half), f32),
        ),
        in_specs=[smem()] + [vmem()] * 4,
        out_specs=(vmem(),) * 2,
        cost_estimate=brief(),
        compiler_params=params(),
    )(place, local, through, mixer_weight, ends)
    encoded, leaving = pl.pallas_call(
        pool_kernel,
        out_shape=(
            jax.ShapeDtypeStruct((rows_here, half), bf16),
            jax.ShapeDtypeStruct((shards, slots, half), bf16),
        ),
        in_specs=[smem()] + [vmem()] * 5,
        out_specs=(vmem(),) * 2,
        cost_estimate=brief(),
        compiler_params=params(),
    )(place, states, mixer_weight, swapped(other_part), byte_states, pool_pick)
    arrived = lax.all_to_all(leaving, "seq", 0, 0, tiled=True)
    *pair_layers, up_here = pl.pallas_call(
        functools.partial(regroup_kernel, plane),
        out_shape=(jax.ShapeDtypeStruct((plane, weight_rows, 2 * HEAD), bf16),) * layers
        + (jax.ShapeDtypeStruct((layers, *up_weight.shape), bf16),),
        in_specs=[smem()] + [in_place()] * (1 + plane + layers),
        out_specs=(in_place(),) * (layers + 1),
        scratch_shapes=[pltpu.SemaphoreType.DMA((shards + layers,))],
        cost_estimate=brief(),
        compiler_params=params(),
    )(place, leaving, *pair_planes, *up_layers)
    up_beside, up_across = over(up_here, 1), over(up_here, 2)
    mine = [pair_layers[0], over(pair_layers[1], plane)]
    own_rows = pl.pallas_call(
        own_kernel,
        out_shape=jax.ShapeDtypeStruct((layers, CH_OWN, half), bf16),
        in_specs=[vmem()] * 2,
        out_specs=vmem(),
        cost_estimate=brief(),
        compiler_params=params(),
    )(own_pick, arrived)
    near_layer = lax.all_to_all(
        own_rows, "seq", 0, 0, axis_index_groups=layer_groups, tiled=True
    )
    mine += [
        over(after(pair_layers[step], own_rows), plane * step) for step in range(2, layers)
    ]
    near_layer, mine[1] = lax.optimization_barrier((near_layer, mine[1]))
    up_corner = [
        over(after(up_beside, near_layer)[: layers // 2], 2),
        over(after(up_across, near_layer)[layers // 2 :], 1),
    ]
    near = lax.all_to_all(
        jnp.broadcast_to(near_layer[None], (plane, layers, CH_OWN, half)),
        "seq",
        0,
        0,
        axis_index_groups=plane_groups,
        tiled=True,
    ).reshape(total_rows, half)

    near, mine[2] = lax.optimization_barrier((near, mine[2]))

    up_pieces = [up_here, up_beside, up_across, *up_corner]
    inner, totals = pl.pallas_call(
        functools.partial(up_kernel, plane),
        out_shape=(
            jax.ShapeDtypeStruct((total_rows, inner_half), bf16),
            jax.ShapeDtypeStruct((total_rows, HEAD), f32),
        ),
        in_specs=[smem()] + [vmem()] * 2 + [in_place()] * (2 + len(up_pieces)),
        out_specs=(vmem(),) * 2,
        scratch_shapes=[
            pltpu.VMEM((total_rows, width), bf16),
            pltpu.VMEM((width, inner_half), bf16),
            pltpu.SemaphoreType.DMA((2 + shards,)),
        ],
        cost_estimate=brief(),
        compiler_params=params(),
    )(place, up_bias[None, :], own_gain, near, swapped(near), *up_pieces)
    mine[layers - 1] = after(mine[layers - 1], totals)
    far = [swapped(piece) for piece in mine]
    own_sums, other_sums = pl.pallas_call(
        functools.partial(sums_kernel, plane),
        out_shape=(jax.ShapeDtypeStruct((total_rows, 3 * HEAD), f32),) * 2,
        in_specs=[smem()] + [vmem()] * 2 + [in_place()] * (2 * layers),
        out_specs=(vmem(),) * 2,
        scratch_shapes=[
            pltpu.VMEM((inner_half, 4 * HEAD), bf16),
            pltpu.SemaphoreType.DMA((shards,)),
        ],
        cost_estimate=brief(),
        compiler_params=params(),
    )(place, inner, totals, *mine, *far)
    queries, pairs = pl.pallas_call(
        functools.partial(heads_kernel, inner_width, plane),
        out_shape=(jax.ShapeDtypeStruct((total_rows, HEAD), bf16),) * 2,
        in_specs=[vmem()] * 2,
        out_specs=(vmem(),) * 2,
        scratch_shapes=[pltpu.VMEM((total_rows, HEAD), f32)] * 2,
        cost_estimate=brief(),
        compiler_params=params(),
    )(own_sums, swapped(other_sums))
    leaving = pl.pallas_call(
        attend_kernel,
        out_shape=jax.ShapeDtypeStruct((shards, window, HEAD), bf16),
        in_specs=[smem()] + [vmem()] * 3,
        out_specs=vmem(),
        scratch_shapes=[
            pltpu.VMEM((total_rows, HEAD), bf16),
            pltpu.VMEM((total_rows, HEAD), bf16),
            pltpu.VMEM((total_rows + window, HEAD), bf16),
        ],
        cost_estimate=brief(),
        compiler_params=params(),
    )(place, queries, pairs, over(pairs, 2))
    pieces = lax.all_to_all(leaving, "seq", 0, 0, tiled=True)
    own_back, other_back = pl.pallas_call(
        return_kernel,
        out_shape=(jax.ShapeDtypeStruct((window, half), f32),) * 2,
        in_specs=[smem()] + [vmem()] * 2,
        out_specs=(vmem(),) * 2,
        scratch_shapes=[pltpu.VMEM((window, shards * HEAD), bf16)],
        cost_estimate=brief(),
        compiler_params=params(),
    )(place, return_weight, pieces)
    return pl.pallas_call(
        join_kernel,
        out_shape=jax.ShapeDtypeStruct((rows_here, half), bf16),
        in_specs=[vmem()] * 4,
        out_specs=vmem(),
        cost_estimate=brief(),
        compiler_params=params(),
    )(own_back, swapped(other_back), encoded, spread)


def prefix(value, axis, join, neutral):
    count, mine = (lax.axis_size(axis), lax.axis_index(axis))
    pieces = jax.tree.map(lambda part: lax.all_gather(part, axis), value)
    so_far = jax.tree.map(
        lambda part, zero: jnp.full_like(part, 0) + jnp.asarray(zero, part.dtype), value, neutral
    )

    def lap(position, so_far):
        longer = join(so_far, jax.tree.map(lambda part: part[position], pieces))
        return jax.tree.map(lambda new, old: jnp.where(position < mine, new, old), longer, so_far)

    return lax.fori_loop(0, count - 1, lap, so_far)


def rms_scale(values, gain):
    values = values.astype(jnp.float32)
    return values * lax.rsqrt(jnp.mean(values * values, axis=-1, keepdims=True) + eps) * gain


def combine_pairs(earlier, later):
    return (earlier[0] * later[0], later[0] * earlier[1] + later[1])


def pick_table(table, wanted, seq_ids):
    return jnp.sum(jnp.where(seq_ids[None, :] == wanted[:, None], table[None, :], 0), axis=1)


def block_size(piece_rows, shard_rows):
    limit = max(1, 1024 // shard_rows)
    pieces = max(1, piece_rows // shard_rows)
    best_size = 1
    for candidate in range(1, limit + 1):
        if pieces % candidate == 0:
            best_size = candidate
    return min(piece_rows, best_size * shard_rows)


def spread_heads(
    byte_states,
    outer_gain,
    mamba_input,
    mamba_step,
    decay_rate,
    mixer_weight,
    boundaries,
    span_counts,
    up_weight,
    up_bias,
    inner_gain,
    query_weight,
    key_weight,
    value_weight,
    return_weight,
):
    shards = lax.axis_size("seq")
    own_shard = lax.axis_index("seq")
    own_lane = lax.axis_index("mp")
    rows_here = byte_states.shape[0]
    capacity = boundaries.shape[1]
    column_count = mamba_input.shape[1]
    kv_local = key_weight.shape[1] // HEAD
    group_size = HEADS // KV_HEADS
    slot_count = capacity // shards
    offsets = jnp.cumsum(span_counts) - span_counts
    seq_ids = jnp.arange(shards, dtype=jnp.int32)
    own_offset = jnp.sum(jnp.where(seq_ids == own_shard, offsets, 0))
    own_count = jnp.sum(jnp.where(seq_ids == own_shard, span_counts, 0))
    normed = rms_scale(byte_states, outer_gain).astype(jnp.bfloat16)
    inputs = jnp.dot(normed, mamba_input, preferred_element_type=jnp.float32)
    step_sizes = jax.nn.softplus(jnp.dot(normed, mamba_step, preferred_element_type=jnp.float32))
    rate_steps = step_sizes * decay_rate
    decays = jnp.exp(-rate_steps)
    drives = jnp.sqrt(-jnp.expm1(-2.0 * rate_steps)) * inputs
    through, local_states = lax.associative_scan(combine_pairs, (decays, drives), axis=0)
    starting = (jnp.ones((column_count,), jnp.float32), jnp.zeros((column_count,), jnp.float32))
    arriving = prefix((through[-1], local_states[-1]), "seq", combine_pairs, starting)
    states = (local_states + through * arriving[1][None, :]).astype(jnp.bfloat16)
    partial_value = jnp.dot(states, mixer_weight, preferred_element_type=jnp.float32)
    mixed_sum = lax.psum(partial_value, "mp")
    encoded = (byte_states.astype(jnp.float32) + mixed_sum).astype(jnp.bfloat16)
    skip_part = lax.dynamic_slice_in_dim(encoded, own_lane * column_count, column_count, 1)
    own_marks = boundaries[0]
    pooled = encoded[jnp.minimum(own_marks, rows_here - 1)]
    row_width = pooled.shape[1]
    outgoing = jnp.roll(pooled.reshape(slot_count, shards, row_width), own_offset % shards, axis=1)
    incoming = lax.all_to_all(outgoing, "seq", split_axis=1, concat_axis=1, tiled=True)
    position = jnp.arange(CH_OWN, dtype=jnp.int32)
    span_index = own_shard + position * shards
    source = jnp.sum((offsets[None, :] <= span_index[:, None]).astype(jnp.int32), axis=1) - 1
    source_offset = pick_table(offsets, source, seq_ids)
    slot_index = (span_index - source_offset) // shards
    gathered_rows = incoming.reshape(slot_count * shards, row_width)[slot_index * shards + source]
    columns = gathered_rows
    widened_sum = jnp.dot(
        columns,
        lax.all_gather(up_weight, "seq", axis=0, tiled=True),
        preferred_element_type=jnp.float32,
    )
    widened_share = (widened_sum + up_bias[None, :]).astype(jnp.bfloat16)
    widened = lax.all_gather(widened_share, "mp", axis=1, tiled=True)
    inner_normed = rms_scale(widened, inner_gain).astype(jnp.bfloat16)
    columns = inner_normed
    query_part = jnp.dot(
        columns,
        lax.all_gather(query_weight, "seq", axis=0, tiled=True),
        preferred_element_type=jnp.float32,
    )
    key_part = jnp.dot(
        columns,
        lax.all_gather(key_weight, "seq", axis=0, tiled=True),
        preferred_element_type=jnp.float32,
    )
    value_part = jnp.dot(
        columns,
        lax.all_gather(value_weight, "seq", axis=0, tiled=True),
        preferred_element_type=jnp.float32,
    )
    queries = query_part.astype(jnp.bfloat16)
    key_rows = key_part.astype(jnp.bfloat16)
    value_rows = value_part.astype(jnp.bfloat16)
    query_count = queries.shape[0]
    grouped = (
        queries.reshape(query_count, kv_local, group_size, HEAD)
        .transpose(1, 0, 2, 3)
        .reshape(kv_local, query_count * group_size, HEAD)
    )
    row_index = jnp.repeat(span_index, group_size)
    shard_rows = key_rows.shape[0]
    score_scale = 1.0 / math.sqrt(HEAD)

    def key_index(whole_index):
        return whole_index // shard_rows + whole_index % shard_rows * shards

    def attend_block(running, key_block, value_block, index_block):
        row_peak, denominator, weighted = running
        scores = (
            jnp.einsum("hqd,khd->hqk", grouped, key_block, preferred_element_type=jnp.float32)
            * score_scale
        )
        scores = jnp.where(index_block[None, None, :] <= row_index[None, :, None], scores, masked)
        new_peak = jnp.maximum(row_peak, jnp.max(scores, axis=2))
        shrink = jnp.exp(row_peak - new_peak)
        lifted = jnp.exp(scores - new_peak[:, :, None])
        denominator = denominator * shrink + jnp.sum(lifted, axis=2)
        weighted = weighted * shrink[:, :, None] + jnp.einsum(
            "hqk,khd->hqd",
            lifted.astype(jnp.bfloat16),
            value_block,
            preferred_element_type=jnp.float32,
        )
        return (new_peak, denominator, weighted)

    query_total = query_count * group_size
    initial = (
        jnp.full((kv_local, query_total), masked, jnp.float32),
        jnp.zeros((kv_local, query_total), jnp.float32),
        jnp.zeros((kv_local, query_total, HEAD), jnp.float32),
    )
    key_piece = lax.all_gather(key_rows, "seq", axis=0, tiled=True)
    value_piece = lax.all_gather(value_rows, "seq", axis=0, tiled=True)
    piece_rows = key_piece.shape[0]
    block_rows = block_size(piece_rows, shard_rows)
    turn_count = piece_rows // block_rows
    key_blocks = key_piece.reshape(turn_count, block_rows, kv_local, HEAD)
    value_blocks = value_piece.reshape(turn_count, block_rows, kv_local, HEAD)

    def one_turn(turn_index, inner_running):
        whole_index = turn_index * block_rows + jnp.arange(block_rows, dtype=jnp.int32)
        return attend_block(
            inner_running, key_blocks[turn_index], value_blocks[turn_index], key_index(whole_index)
        )

    row_peak, denominator, weighted = lax.fori_loop(0, turn_count, one_turn, initial)
    attended = (weighted / denominator[:, :, None]).astype(jnp.bfloat16)
    attended = (
        attended.reshape(kv_local, query_count, group_size, HEAD)
        .transpose(1, 0, 2, 3)
        .reshape(query_count, kv_local * group_size * HEAD)
    )
    projected = jnp.dot(attended, return_weight, preferred_element_type=jnp.float32)
    returned = lax.psum_scatter(
        projected.astype(jnp.bfloat16), "mp", scatter_dimension=1, tiled=True
    )
    slot_ids = jnp.arange(slot_count, dtype=jnp.int32)
    lead_slot = (own_shard - offsets) % shards
    local_span = slot_ids[:, None] * shards + lead_slot[None, :]
    back_index = (offsets[None, :] + local_span - own_shard) // shards
    alive = local_span < span_counts[None, :]
    back_rows = jnp.where(
        alive[:, :, None],
        returned[jnp.clip(back_index, 0, CH_OWN - 1)],
        jnp.zeros((), jnp.bfloat16),
    )
    arrived = lax.all_to_all(back_rows, "seq", split_axis=1, concat_axis=1, tiled=True)
    span_results = jnp.roll(arrived, -(own_offset % shards), axis=1).reshape(capacity, column_count)
    positions = jnp.arange(rows_here, dtype=jnp.int32)
    live_slots = jnp.arange(capacity, dtype=jnp.int32) < own_count
    passed = jnp.sum(
        ((own_marks[None, :] <= positions[:, None]) & live_slots[None, :]).astype(jnp.int32), axis=1
    )
    return (skip_part.astype(jnp.float32) + span_results[passed - 1].astype(jnp.float32)).astype(
        jnp.bfloat16
    )


def solution(mesh):
    in_specs = (
        P("seq", None),
        P(),
        P(None, "mp"),
        P(None, "mp"),
        P("mp"),
        P("mp", None),
        P("seq", None),
        P(),
        P("seq", "mp"),
        P("mp"),
        P(),
        P("seq", "mp"),
        P("seq", "mp"),
        P("seq", "mp"),
        P("mp", None),
    )
    out_specs = P("seq", "mp")
    def on_device(*arrays):
        heads_here = arrays[11].shape[1] // HEAD
        fits = heads_here == mesh.shape["seq"] and mesh.shape["mp"] == 2
        return (one_head_each if fits else spread_heads)(*arrays)

    return jax.shard_map(
        on_device, mesh=mesh, in_specs=in_specs, out_specs=out_specs, check_vma=False
    )
```

```python
import functools
import math

import jax
import jax.numpy as jnp
from jax import lax
from jax.experimental import pallas as pl
from jax.experimental.pallas import tpu as pltpu
from jax.sharding import PartitionSpec as P

HEADS = 32
KV_HEADS = 8
HEAD = 128
CH_OWN = 64


eps = 1e-05
masked = -1e30
TILE = 16


def swapped(value):
    return lax.ppermute(value, "mp", [(0, 1), (1, 0)])


def vmem():
    return pl.BlockSpec(memory_space=pltpu.VMEM)


def smem():
    return pl.BlockSpec(memory_space=pltpu.SMEM)


def in_place():
    return pl.BlockSpec(memory_space=pl.ANY)


def in_hbm():
    return pl.BlockSpec(memory_space=pltpu.HBM)


def seat():
    return lax.axis_index("seq"), lax.axis_index("mp")


def params(mebibytes=24):
    return pltpu.CompilerParams(vmem_limit_bytes=mebibytes * 2**20)


def brief():
    return pl.CostEstimate(flops=1, bytes_accessed=1, transcendentals=0)


def lanes(which, size):
    return pl.ds(pl.multiple_of(which * size, size), size)


def one_minus_exp(u):
    series = jnp.ones_like(u)
    for order in range(9, 1, -1):
        series = 1.0 - u * (1.0 / order) * series
    return jnp.where(u < 0.5, u * series, 1.0 - jnp.exp(-u))


def softplus(v):
    tail = jnp.exp(-jnp.abs(v))
    series = jnp.ones_like(tail)
    for order in range(6, 1, -1):
        series = 1.0 - tail * ((order - 1.0) / order) * series
    return jnp.maximum(v, 0.0) + jnp.where(tail < 0.03, tail * series, jnp.log(1.0 + tail))


def scan_kernel(bytes_ref, gain_ref, input_ref, step_ref, rate_ref, local_ref, through_ref, ends_ref):
    values = bytes_ref[...].astype(jnp.float32)
    scale = lax.rsqrt(jnp.mean(values * values, axis=1, keepdims=True) + eps)
    normed = (values * scale * gain_ref[...]).astype(jnp.bfloat16)
    steps = softplus(jnp.dot(normed, step_ref[...], preferred_element_type=jnp.float32))
    rate_steps = steps * rate_ref[...]
    inputs = jnp.dot(normed, input_ref[...], preferred_element_type=jnp.float32)
    decays = jnp.exp(-rate_steps)
    drives = jnp.sqrt(one_minus_exp(2.0 * rate_steps)) * inputs
    rows, width = decays.shape
    tile = 8
    decays = decays.reshape(rows // tile, tile, width)
    drives = drives.reshape(rows // tile, tile, width)
    place = lax.broadcasted_iota(jnp.int32, decays.shape, 1)
    for reach in (1, 2, 4):
        before_decays = pltpu.roll(decays, reach, 1)
        before_drives = pltpu.roll(drives, reach, 1)
        inside = place >= reach
        drives = jnp.where(inside, decays * before_drives + drives, drives)
        decays = jnp.where(inside, decays * before_decays, decays)
    state = jnp.zeros((1, width), jnp.float32)
    kept = jnp.ones((1, width), jnp.float32)
    for index in range(rows // tile):
        states = decays[index] * state + drives[index]
        passing = decays[index] * kept
        local_ref[pl.ds(index * tile, tile), :] = states
        through_ref[pl.ds(index * tile, tile), :] = passing
        state = states[tile - 1 :, :]
        kept = passing[tile - 1 :, :]
    for index in range(ends_ref.shape[0]):
        ends_ref[index, 0:1, :] = kept
        ends_ref[index, 1:2, :] = state


def states_kernel(local_ref, through_ref, mixer_ref, ends_ref, states_ref, other_ref):
    me, lane = seat()
    carry = jnp.zeros((1, local_ref.shape[1]), jnp.float32)
    for shard in range(ends_ref.shape[0]):
        later = ends_ref[shard, 0:1, :] * carry + ends_ref[shard, 1:2, :]
        carry = jnp.where(shard < me, later, carry)
    states = (local_ref[...] + through_ref[...] * carry).astype(jnp.bfloat16)
    states_ref[...] = states
    half = other_ref.shape[1]
    other_ref[...] = jnp.dot(
        states, mixer_ref[:, lanes(1 - lane, half)], preferred_element_type=jnp.float32
    )


def pool_kernel(states_ref, mixer_ref, other_ref, bytes_ref, pick_ref, encoded_ref, out_ref):
    half = other_ref.shape[1]
    columns = lanes(seat()[1], half)
    mixed = jnp.dot(states_ref[...], mixer_ref[:, columns], preferred_element_type=jnp.float32)
    skip = bytes_ref[:, columns].astype(jnp.float32)
    encoded = (skip + (mixed + other_ref[...])).astype(jnp.bfloat16)
    encoded_ref[...] = encoded
    picked = jnp.dot(pick_ref[...], encoded, preferred_element_type=jnp.float32)
    out_ref[...] = picked.astype(jnp.bfloat16).reshape(out_ref.shape)


def own_kernel(pick_ref, arrived_ref, out_ref):
    shards, slots, half = arrived_ref.shape
    rows = arrived_ref[...].astype(jnp.float32).reshape(shards * slots, half)
    own = jnp.dot(
        pick_ref[...], rows.astype(jnp.bfloat16), preferred_element_type=jnp.float32
    ).astype(jnp.bfloat16)
    for index in range(out_ref.shape[0]):
        out_ref[index] = own


def rows_at(which, size):
    return pl.ds(pl.multiple_of(which * size, size), size)


def copy_all(pairs, sems):
    copies = []
    for index, (from_ref, to_ref) in enumerate(pairs):
        copy = pltpu.make_async_copy(from_ref, to_ref, sems.at[index])
        copy.start()
        copies.append(copy)
    for copy in copies:
        copy.wait()


def cut_kernel(plane, query_ref, key_ref, value_ref, *rest):
    outs, sems = rest[:-1], rest[-1]
    layers = outs[0].shape[0]
    cross = lax.rem(seat()[0], plane)
    pairs = []
    for mask in range(plane):
        for layer in range(layers):
            column = lanes(layer * plane + (cross ^ mask), HEAD)
            pairs.append((query_ref.at[:, column], outs[mask].at[layer, :, pl.ds(0, HEAD)]))

    def start(far_ref, first_masks):
        for mask in first_masks:
            for layer in range(layers):
                number = mask * layers + layer
                pltpu.make_async_copy(
                    far_ref.at[:, pl.ds(layer * HEAD, HEAD)],
                    outs[mask].at[layer, :, pl.ds(HEAD, HEAD)],
                    sems.at[plane * layers + number],
                ).start()

    here, there = range(plane // 2), range(plane // 2, plane)

    @pl.when(cross < plane // 2)
    def _():
        start(key_ref, here)
        start(value_ref, there)

    @pl.when(cross >= plane // 2)
    def _():
        start(value_ref, here)
        start(key_ref, there)

    copy_all(pairs, sems)
    for mask in range(plane):
        for layer in range(layers):
            number = mask * layers + layer
            pltpu.make_async_copy(
                key_ref.at[:, pl.ds(layer * HEAD, HEAD)],
                outs[mask].at[layer, :, pl.ds(HEAD, HEAD)],
                sems.at[plane * layers + number],
            ).wait()


def regroup_kernel(plane, gate_ref, *rest):
    pieces, rest = rest[:plane], rest[plane:]
    layers = pieces[0].shape[0]
    up_pieces, rest = rest[:layers], rest[layers:]
    outs, (up_ref, sems) = rest[:layers], rest[layers:]
    layer = seat()[0] // plane
    pairs = []
    for step in range(layers):
        pairs.append((up_pieces[step], up_ref.at[step]))
    for step in range(layers):
        for mask in range(plane):
            pairs.append((pieces[mask].at[layer ^ step], outs[step].at[mask]))
    copy_all(pairs, sems)


def up_kernel(plane, bias_ref, gain_ref, near_ref, far_ref, *rest):
    up_pieces, rest = rest[: plane + 1], rest[plane + 1 :]
    inner_ref, total_ref, pooled, up, sems = rest
    me, lane = seat()
    layer, cross = me // plane, lax.rem(me, plane)
    half = near_ref.shape[1]
    up_rows = up_pieces[0].shape[1]
    rows = inner_ref.shape[0]
    pairs = [
        (near_ref, pooled.at[:, lanes(lane, half)]),
        (far_ref, pooled.at[:, lanes(1 - lane, half)]),
    ]
    layers = up_pieces[0].shape[0]
    for mask in range(plane):
        for step in range(layers):
            shard = (layer ^ step) * plane + (cross ^ mask)
            piece = up_pieces[mask].at[step]
            if mask == plane - 1:
                piece = up_pieces[mask + step // (layers // 2)].at[step % (layers // 2)]
            pairs.append((piece, up.at[rows_at(shard, up_rows), :]))
    copy_all(pairs, sems)
    block = min(256, rows)
    part = min(1024, up.shape[1])

    def up_block(index, carried):
        where = rows_at(index, block)
        left = pooled[where, :]
        total = jnp.zeros((block, 1), jnp.float32)
        for start in range(0, up.shape[1], part):
            columns = pl.ds(start, part)
            widened = jnp.dot(left, up[:, columns], preferred_element_type=jnp.float32)
            widened = (widened + bias_ref[:, columns]).astype(jnp.bfloat16).astype(jnp.float32)
            inner_ref[where, columns] = (widened * gain_ref[:, columns]).astype(jnp.bfloat16)
            total = total + jnp.sum(widened * widened, axis=1, keepdims=True)
        total_ref[where, :] = jnp.broadcast_to(total, (block, HEAD))
        return carried

    lax.fori_loop(0, rows // block, up_block, 0)


def sums_kernel(plane, inner_ref, total_ref, *rest):
    layers = (len(rest) - 4) // 2
    mine, far = rest[:layers], rest[layers : 2 * layers]
    own_ref, other_ref, weights, sems = rest[2 * layers :]
    me, lane = seat()
    layer, cross = me // plane, lax.rem(me, plane)
    piece_rows = mine[0].shape[1]
    rows = inner_ref.shape[0]
    span = 2 * HEAD
    keep = layers // 2

    def pairs_from(first):
        pairs = []
        for head, pieces in enumerate((mine, far)):
            for step in range(keep):
                for mask in range(plane):
                    shard = (lax.rem(layer, keep) ^ step) * plane + (cross ^ mask)
                    to_ref = weights.at[rows_at(shard, piece_rows), pl.ds(head * span, span)]
                    pairs.append((pieces[first + step].at[mask], to_ref))
        return pairs

    low_is_own = layer // keep == lane

    @pl.when(low_is_own)
    def _():
        copy_all(pairs_from(0), sems)

    @pl.when(jnp.logical_not(low_is_own))
    def _():
        copy_all(pairs_from(keep), sems)

    block = min(256, rows)

    def sums_block(index, carried):
        where = rows_at(index, block)
        sums = jnp.dot(inner_ref[where, :], weights[...], preferred_element_type=jnp.float32)
        own_ref[where, 0:span] = sums[:, :span]
        own_ref[where, span:] = total_ref[where, :]
        other_ref[where, 0:span] = sums[:, span:]
        other_ref[where, span:] = total_ref[where, :]
        return carried

    lax.fori_loop(0, rows // block, sums_block, 0)


def heads_kernel(features, plane, own_ref, other_ref, query_ref, pair_ref, queries, pairs):
    rows = own_ref.shape[0]
    span = 2 * HEAD
    shards = rows // CH_OWN
    layers = shards // plane
    for index in range(shards):
        where = pl.ds(index * CH_OWN, CH_OWN)
        sums = own_ref[where, :] + other_ref[where, :]
        scale = lax.rsqrt(sums[:, span:] * (1.0 / features) + eps)
        shard = (index % layers) * plane + index // layers
        natural = pl.ds(shard, CH_OWN, stride=shards)
        queries[natural, :] = sums[:, :HEAD] * scale
        pairs[natural, :] = sums[:, HEAD:span] * scale
    query_ref[...] = queries[...].astype(jnp.bfloat16)
    pair_ref[...] = pairs[...].astype(jnp.bfloat16)


def attend_kernel(plane, place_ref, query_ref, pair_ref, other_ref, out_ref, keys, values, attended):
    rows = query_ref.shape[0]
    window = out_ref.shape[1]
    block = min(256, rows)
    holds_keys = lax.rem(seat()[0], plane) < plane // 2

    @pl.when(holds_keys)
    def _():
        keys[...] = pair_ref[...]
        values[...] = other_ref[...]

    @pl.when(jnp.logical_not(holds_keys))
    def _():
        keys[...] = other_ref[...]
        values[...] = pair_ref[...]

    score_scale = 1.0 / math.sqrt(HEAD)
    for start in range(0, rows, block):
        stop = start + block
        scores = lax.dot_general(
            query_ref[start:stop, :],
            keys[0:stop, :],
            (((1,), (1,)), ((), ())),
            preferred_element_type=jnp.float32,
        )
        spots = lax.broadcasted_iota(jnp.int32, scores.shape, 1)
        mine = lax.broadcasted_iota(jnp.int32, scores.shape, 0) + start
        scores = jnp.where(spots <= mine, scores * score_scale, masked)
        peak = jnp.max(scores, axis=1, keepdims=True)
        lifted = jnp.exp(scores - peak)
        denominator = jnp.sum(lifted, axis=1, keepdims=True)
        weighted = jnp.dot(
            lifted.astype(jnp.bfloat16), values[0:stop, :], preferred_element_type=jnp.float32
        )
        attended[start:stop, :] = (weighted / denominator).astype(jnp.bfloat16)
    attended[rows:, :] = jnp.zeros((attended.shape[0] - rows, HEAD), jnp.bfloat16)
    for shard in range(out_ref.shape[0]):
        first = place_ref[shard]
        out_ref[shard] = attended[pl.ds(pl.multiple_of(first * TILE, TILE), window), :]


def return_kernel(weight_ref, pieces_ref, own_ref, other_ref, attended):
    half = own_ref.shape[1]
    lane = seat()[1]
    for head in range(pieces_ref.shape[0]):
        attended[:, head * HEAD : (head + 1) * HEAD] = pieces_ref[head]
    other_ref[...] = jnp.dot(
        attended[...], weight_ref[:, lanes(1 - lane, half)], preferred_element_type=jnp.float32
    )
    own_ref[...] = jnp.dot(
        attended[...], weight_ref[:, lanes(lane, half)], preferred_element_type=jnp.float32
    )


def join_kernel(own_ref, other_ref, encoded_ref, spread_ref, out_ref):
    returned = (own_ref[...] + other_ref[...]).astype(jnp.bfloat16)
    results = jnp.dot(spread_ref[...], returned, preferred_element_type=jnp.float32)
    out_ref[...] = (encoded_ref[...].astype(jnp.float32) + results).astype(jnp.bfloat16)


def one_head_each(
    byte_states,
    outer_gain,
    mamba_input,
    mamba_step,
    decay_rate,
    mixer_weight,
    boundaries,
    span_counts,
    up_weight,
    up_bias,
    inner_gain,
    query_weight,
    key_weight,
    value_weight,
    return_weight,
):
    shards = lax.axis_size("seq")
    me = lax.axis_index("seq")
    lane = lax.axis_index("mp")
    plane = HEADS // KV_HEADS
    layers = shards // plane
    rows_here, width = byte_states.shape
    half = mamba_input.shape[1]
    capacity = boundaries.shape[1]
    window = capacity + TILE
    total_rows = CH_OWN * shards
    inner_width = inner_gain.shape[0]
    inner_half = up_bias.shape[0]
    weight_rows = query_weight.shape[0]
    f32, bf16 = jnp.float32, jnp.bfloat16
    layer, cross = me // plane, me % plane
    layer_groups = [[first + plane * step for step in range(layers)] for first in range(plane)]
    plane_groups = [[first * plane + step for step in range(plane)] for first in range(layers)]

    def over(value, mask):
        return lax.ppermute(value, "seq", [(i, i ^ mask) for i in range(shards)])

    def after(value, done):
        return lax.optimization_barrier((value, done))[0]

    own_gain = lax.dynamic_slice_in_dim(inner_gain, lane * inner_half, inner_half)[None, :]
    seq_ids = jnp.arange(shards, dtype=jnp.int32)
    offsets = jnp.cumsum(span_counts) - span_counts
    own_offset = jnp.sum(jnp.where(seq_ids == me, offsets, 0))
    own_count = jnp.sum(jnp.where(seq_ids == me, span_counts, 0))
    place = offsets // TILE
    own_marks = boundaries[0]
    positions = jnp.arange(rows_here, dtype=jnp.int32)
    spans_here = jnp.arange(capacity, dtype=jnp.int32)
    live = spans_here < own_count
    slots = capacity // shards
    slot_ids = jnp.arange(slots, dtype=jnp.int32)
    local_span = slot_ids[None, :] * shards + ((seq_ids - own_offset) % shards)[:, None]
    is_span = spans_here[None, :] == local_span.reshape(-1)[:, None]
    byte_at = jnp.sum(jnp.where(is_span, jnp.minimum(own_marks, rows_here - 1)[None, :], 0), axis=1)
    pool_pick = (positions[None, :] == byte_at[:, None]).astype(bf16)
    own_spans = me + jnp.arange(CH_OWN, dtype=jnp.int32) * shards
    origin = jnp.sum((offsets[None, :] <= own_spans[:, None]).astype(jnp.int32), axis=1) - 1
    origin_offset = jnp.sum(
        jnp.where(seq_ids[None, :] == origin[:, None], offsets[None, :], 0), axis=1
    )
    arrived_row = origin * slots + (own_spans - origin_offset) // shards
    own_pick = (
        jnp.arange(shards * slots, dtype=jnp.int32)[None, :] == arrived_row[:, None]
    ).astype(bf16)
    passed = jnp.sum(
        ((own_marks[None, :] <= positions[:, None]) & live[None, :]).astype(jnp.int32), axis=1
    )
    result_row = passed - 1 + own_offset % TILE
    spread = (jnp.arange(window, dtype=jnp.int32)[None, :] == result_row[:, None]).astype(bf16)

    local, through, ends = pl.pallas_call(
        scan_kernel,
        out_shape=(
            jax.ShapeDtypeStruct((rows_here, half), f32),
            jax.ShapeDtypeStruct((rows_here, half), f32),
            jax.ShapeDtypeStruct((shards, 2, half), f32),
        ),
        in_specs=[vmem()] * 5,
        out_specs=(vmem(),) * 3,
        cost_estimate=brief(),
        compiler_params=params(),
    )(byte_states, outer_gain[None, :], mamba_input, mamba_step, decay_rate[None, :])
    cuts = pl.pallas_call(
        functools.partial(cut_kernel, plane),
        out_shape=(jax.ShapeDtypeStruct((layers, weight_rows, 2 * HEAD), bf16),) * plane,
        in_specs=[in_hbm()] * 3,
        out_specs=(vmem(),) * plane,
        scratch_shapes=[pltpu.SemaphoreType.DMA((2 * shards,))],
        cost_estimate=brief(),
        compiler_params=params(),
    )(*after((query_weight, key_weight, value_weight), ends))
    behind = after(up_weight, ends)
    up_layers = [up_weight] + [over(behind, plane * step) for step in range(1, layers - 1)]
    pair_planes = [cuts[0]] + [over(cuts[mask], mask) for mask in range(1, plane - 1)]
    ends = lax.all_to_all(ends, "seq", 0, 0, tiled=True)
    states, other_part = pl.pallas_call(
        states_kernel,
        out_shape=(
            jax.ShapeDtypeStruct((rows_here, half), bf16),
            jax.ShapeDtypeStruct((rows_here, half), f32),
        ),
        in_specs=[vmem()] * 4,
        out_specs=(vmem(),) * 2,
        cost_estimate=brief(),
        compiler_params=params(),
    )(local, through, mixer_weight, ends)
    encoded, leaving = pl.pallas_call(
        pool_kernel,
        out_shape=(
            jax.ShapeDtypeStruct((rows_here, half), bf16),
            jax.ShapeDtypeStruct((shards, slots, half), bf16),
        ),
        in_specs=[vmem()] * 5,
        out_specs=(vmem(),) * 2,
        cost_estimate=brief(),
        compiler_params=params(),
    )(states, mixer_weight, swapped(other_part), byte_states, pool_pick)
    arrived = lax.all_to_all(leaving, "seq", 0, 0, tiled=True)
    up_layers.append(over(after(up_weight, leaving), plane * (layers - 1)))
    pair_planes.append(over(after(cuts[plane - 1], leaving), plane - 1))
    *pair_layers, up_here = pl.pallas_call(
        functools.partial(regroup_kernel, plane),
        out_shape=(jax.ShapeDtypeStruct((plane, weight_rows, 2 * HEAD), bf16),) * layers
        + (jax.ShapeDtypeStruct((layers, *up_weight.shape), bf16),),
        in_specs=[in_place()] * (1 + plane + layers),
        out_specs=(vmem(),) * (layers + 1),
        scratch_shapes=[pltpu.SemaphoreType.DMA((shards + layers,))],
        cost_estimate=brief(),
        compiler_params=params(),
    )(leaving, *pair_planes, *up_layers)
    up_beside, up_across = over(up_here, 1), over(up_here, 2)
    mine = [pair_layers[0], over(pair_layers[1], plane)]
    own_rows = pl.pallas_call(
        own_kernel,
        out_shape=jax.ShapeDtypeStruct((layers, CH_OWN, half), bf16),
        in_specs=[vmem()] * 2,
        out_specs=vmem(),
        cost_estimate=brief(),
        compiler_params=params(),
    )(own_pick, arrived)
    near_layer = lax.all_to_all(
        own_rows, "seq", 0, 0, axis_index_groups=layer_groups, tiled=True
    )
    mine += [
        over(after(pair_layers[step], own_rows), plane * step) for step in range(2, layers)
    ]
    near_layer, mine[1], up_beside, up_across = lax.optimization_barrier(
        (near_layer, mine[1], up_beside, up_across)
    )
    up_corner = [
        over(after(up_beside, near_layer)[: layers // 2], 2),
        over(after(up_across, near_layer)[layers // 2 :], 1),
    ]
    near = lax.all_to_all(
        jnp.broadcast_to(near_layer[None], (plane, layers, CH_OWN, half)),
        "seq",
        0,
        0,
        axis_index_groups=plane_groups,
        tiled=True,
    ).reshape(total_rows, half)

    near, mine[2] = lax.optimization_barrier((near, mine[2]))

    up_pieces = [up_here, up_beside, up_across, *up_corner]
    inner, totals = pl.pallas_call(
        functools.partial(up_kernel, plane),
        out_shape=(
            jax.ShapeDtypeStruct((total_rows, inner_half), bf16),
            jax.ShapeDtypeStruct((total_rows, HEAD), f32),
        ),
        in_specs=[vmem()] * 2 + [in_place()] * (2 + len(up_pieces)),
        out_specs=(vmem(),) * 2,
        scratch_shapes=[
            pltpu.VMEM((total_rows, width), bf16),
            pltpu.VMEM((width, inner_half), bf16),
            pltpu.SemaphoreType.DMA((2 + shards,)),
        ],
        cost_estimate=brief(),
        compiler_params=params(),
    )(up_bias[None, :], own_gain, near, swapped(near), *up_pieces)
    mine[layers - 1] = after(mine[layers - 1], totals)
    far = [swapped(piece) for piece in mine]
    own_sums, other_sums = pl.pallas_call(
        functools.partial(sums_kernel, plane),
        out_shape=(jax.ShapeDtypeStruct((total_rows, 3 * HEAD), f32),) * 2,
        in_specs=[vmem()] * 2 + [in_place()] * (2 * layers),
        out_specs=(vmem(),) * 2,
        scratch_shapes=[
            pltpu.VMEM((inner_half, 4 * HEAD), bf16),
            pltpu.SemaphoreType.DMA((shards,)),
        ],
        cost_estimate=brief(),
        compiler_params=params(),
    )(inner, totals, *mine, *far)
    queries, pairs = pl.pallas_call(
        functools.partial(heads_kernel, inner_width, plane),
        out_shape=(jax.ShapeDtypeStruct((total_rows, HEAD), bf16),) * 2,
        in_specs=[vmem()] * 2,
        out_specs=(vmem(),) * 2,
        scratch_shapes=[pltpu.VMEM((total_rows, HEAD), f32)] * 2,
        cost_estimate=brief(),
        compiler_params=params(),
    )(own_sums, swapped(other_sums))
    leaving = pl.pallas_call(
        functools.partial(attend_kernel, plane),
        out_shape=jax.ShapeDtypeStruct((shards, window, HEAD), bf16),
        in_specs=[smem()] + [vmem()] * 3,
        out_specs=vmem(),
        scratch_shapes=[
            pltpu.VMEM((total_rows, HEAD), bf16),
            pltpu.VMEM((total_rows, HEAD), bf16),
            pltpu.VMEM((total_rows + window, HEAD), bf16),
        ],
        cost_estimate=brief(),
        compiler_params=params(),
    )(place, queries, pairs, over(pairs, 2))
    pieces = lax.all_to_all(leaving, "seq", 0, 0, tiled=True)
    own_back, other_back = pl.pallas_call(
        return_kernel,
        out_shape=(jax.ShapeDtypeStruct((window, half), f32),) * 2,
        in_specs=[vmem()] * 2,
        out_specs=(vmem(),) * 2,
        scratch_shapes=[pltpu.VMEM((window, shards * HEAD), bf16)],
        cost_estimate=brief(),
        compiler_params=params(),
    )(return_weight, pieces)
    return pl.pallas_call(
        join_kernel,
        out_shape=jax.ShapeDtypeStruct((rows_here, half), bf16),
        in_specs=[vmem()] * 4,
        out_specs=vmem(),
        cost_estimate=brief(),
        compiler_params=params(),
    )(own_back, swapped(other_back), encoded, spread)


def prefix(value, axis, join, neutral):
    count, mine = (lax.axis_size(axis), lax.axis_index(axis))
    pieces = jax.tree.map(lambda part: lax.all_gather(part, axis), value)
    so_far = jax.tree.map(
        lambda part, zero: jnp.full_like(part, 0) + jnp.asarray(zero, part.dtype), value, neutral
    )

    def lap(position, so_far):
        longer = join(so_far, jax.tree.map(lambda part: part[position], pieces))
        return jax.tree.map(lambda new, old: jnp.where(position < mine, new, old), longer, so_far)

    return lax.fori_loop(0, count - 1, lap, so_far)


def rms_scale(values, gain):
    values = values.astype(jnp.float32)
    return values * lax.rsqrt(jnp.mean(values * values, axis=-1, keepdims=True) + eps) * gain


def combine_pairs(earlier, later):
    return (earlier[0] * later[0], later[0] * earlier[1] + later[1])


def pick_table(table, wanted, seq_ids):
    return jnp.sum(jnp.where(seq_ids[None, :] == wanted[:, None], table[None, :], 0), axis=1)


def block_size(piece_rows, shard_rows):
    limit = max(1, 1024 // shard_rows)
    pieces = max(1, piece_rows // shard_rows)
    best_size = 1
    for candidate in range(1, limit + 1):
        if pieces % candidate == 0:
            best_size = candidate
    return min(piece_rows, best_size * shard_rows)


def spread_heads(
    byte_states,
    outer_gain,
    mamba_input,
    mamba_step,
    decay_rate,
    mixer_weight,
    boundaries,
    span_counts,
    up_weight,
    up_bias,
    inner_gain,
    query_weight,
    key_weight,
    value_weight,
    return_weight,
):
    shards = lax.axis_size("seq")
    own_shard = lax.axis_index("seq")
    own_lane = lax.axis_index("mp")
    rows_here = byte_states.shape[0]
    capacity = boundaries.shape[1]
    column_count = mamba_input.shape[1]
    kv_local = key_weight.shape[1] // HEAD
    group_size = HEADS // KV_HEADS
    slot_count = capacity // shards
    offsets = jnp.cumsum(span_counts) - span_counts
    seq_ids = jnp.arange(shards, dtype=jnp.int32)
    own_offset = jnp.sum(jnp.where(seq_ids == own_shard, offsets, 0))
    own_count = jnp.sum(jnp.where(seq_ids == own_shard, span_counts, 0))
    normed = rms_scale(byte_states, outer_gain).astype(jnp.bfloat16)
    inputs = jnp.dot(normed, mamba_input, preferred_element_type=jnp.float32)
    step_sizes = jax.nn.softplus(jnp.dot(normed, mamba_step, preferred_element_type=jnp.float32))
    rate_steps = step_sizes * decay_rate
    decays = jnp.exp(-rate_steps)
    drives = jnp.sqrt(-jnp.expm1(-2.0 * rate_steps)) * inputs
    through, local_states = lax.associative_scan(combine_pairs, (decays, drives), axis=0)
    starting = (jnp.ones((column_count,), jnp.float32), jnp.zeros((column_count,), jnp.float32))
    arriving = prefix((through[-1], local_states[-1]), "seq", combine_pairs, starting)
    states = (local_states + through * arriving[1][None, :]).astype(jnp.bfloat16)
    partial_value = jnp.dot(states, mixer_weight, preferred_element_type=jnp.float32)
    mixed_sum = lax.psum(partial_value, "mp")
    encoded = (byte_states.astype(jnp.float32) + mixed_sum).astype(jnp.bfloat16)
    skip_part = lax.dynamic_slice_in_dim(encoded, own_lane * column_count, column_count, 1)
    own_marks = boundaries[0]
    pooled = encoded[jnp.minimum(own_marks, rows_here - 1)]
    row_width = pooled.shape[1]
    outgoing = jnp.roll(pooled.reshape(slot_count, shards, row_width), own_offset % shards, axis=1)
    incoming = lax.all_to_all(outgoing, "seq", split_axis=1, concat_axis=1, tiled=True)
    position = jnp.arange(CH_OWN, dtype=jnp.int32)
    span_index = own_shard + position * shards
    source = jnp.sum((offsets[None, :] <= span_index[:, None]).astype(jnp.int32), axis=1) - 1
    source_offset = pick_table(offsets, source, seq_ids)
    slot_index = (span_index - source_offset) // shards
    gathered_rows = incoming.reshape(slot_count * shards, row_width)[slot_index * shards + source]
    columns = gathered_rows
    widened_sum = jnp.dot(
        columns,
        lax.all_gather(up_weight, "seq", axis=0, tiled=True),
        preferred_element_type=jnp.float32,
    )
    widened_share = (widened_sum + up_bias[None, :]).astype(jnp.bfloat16)
    widened = lax.all_gather(widened_share, "mp", axis=1, tiled=True)
    inner_normed = rms_scale(widened, inner_gain).astype(jnp.bfloat16)
    columns = inner_normed
    query_part = jnp.dot(
        columns,
        lax.all_gather(query_weight, "seq", axis=0, tiled=True),
        preferred_element_type=jnp.float32,
    )
    key_part = jnp.dot(
        columns,
        lax.all_gather(key_weight, "seq", axis=0, tiled=True),
        preferred_element_type=jnp.float32,
    )
    value_part = jnp.dot(
        columns,
        lax.all_gather(value_weight, "seq", axis=0, tiled=True),
        preferred_element_type=jnp.float32,
    )
    queries = query_part.astype(jnp.bfloat16)
    key_rows = key_part.astype(jnp.bfloat16)
    value_rows = value_part.astype(jnp.bfloat16)
    query_count = queries.shape[0]
    grouped = (
        queries.reshape(query_count, kv_local, group_size, HEAD)
        .transpose(1, 0, 2, 3)
        .reshape(kv_local, query_count * group_size, HEAD)
    )
    row_index = jnp.repeat(span_index, group_size)
    shard_rows = key_rows.shape[0]
    score_scale = 1.0 / math.sqrt(HEAD)

    def key_index(whole_index):
        return whole_index // shard_rows + whole_index % shard_rows * shards

    def attend_block(running, key_block, value_block, index_block):
        row_peak, denominator, weighted = running
        scores = (
            jnp.einsum("hqd,khd->hqk", grouped, key_block, preferred_element_type=jnp.float32)
            * score_scale
        )
        scores = jnp.where(index_block[None, None, :] <= row_index[None, :, None], scores, masked)
        new_peak = jnp.maximum(row_peak, jnp.max(scores, axis=2))
        shrink = jnp.exp(row_peak - new_peak)
        lifted = jnp.exp(scores - new_peak[:, :, None])
        denominator = denominator * shrink + jnp.sum(lifted, axis=2)
        weighted = weighted * shrink[:, :, None] + jnp.einsum(
            "hqk,khd->hqd",
            lifted.astype(jnp.bfloat16),
            value_block,
            preferred_element_type=jnp.float32,
        )
        return (new_peak, denominator, weighted)

    query_total = query_count * group_size
    initial = (
        jnp.full((kv_local, query_total), masked, jnp.float32),
        jnp.zeros((kv_local, query_total), jnp.float32),
        jnp.zeros((kv_local, query_total, HEAD), jnp.float32),
    )
    key_piece = lax.all_gather(key_rows, "seq", axis=0, tiled=True)
    value_piece = lax.all_gather(value_rows, "seq", axis=0, tiled=True)
    piece_rows = key_piece.shape[0]
    block_rows = block_size(piece_rows, shard_rows)
    turn_count = piece_rows // block_rows
    key_blocks = key_piece.reshape(turn_count, block_rows, kv_local, HEAD)
    value_blocks = value_piece.reshape(turn_count, block_rows, kv_local, HEAD)

    def one_turn(turn_index, inner_running):
        whole_index = turn_index * block_rows + jnp.arange(block_rows, dtype=jnp.int32)
        return attend_block(
            inner_running, key_blocks[turn_index], value_blocks[turn_index], key_index(whole_index)
        )

    row_peak, denominator, weighted = lax.fori_loop(0, turn_count, one_turn, initial)
    attended = (weighted / denominator[:, :, None]).astype(jnp.bfloat16)
    attended = (
        attended.reshape(kv_local, query_count, group_size, HEAD)
        .transpose(1, 0, 2, 3)
        .reshape(query_count, kv_local * group_size * HEAD)
    )
    projected = jnp.dot(attended, return_weight, preferred_element_type=jnp.float32)
    returned = lax.psum_scatter(
        projected.astype(jnp.bfloat16), "mp", scatter_dimension=1, tiled=True
    )
    slot_ids = jnp.arange(slot_count, dtype=jnp.int32)
    lead_slot = (own_shard - offsets) % shards
    local_span = slot_ids[:, None] * shards + lead_slot[None, :]
    back_index = (offsets[None, :] + local_span - own_shard) // shards
    alive = local_span < span_counts[None, :]
    back_rows = jnp.where(
        alive[:, :, None],
        returned[jnp.clip(back_index, 0, CH_OWN - 1)],
        jnp.zeros((), jnp.bfloat16),
    )
    arrived = lax.all_to_all(back_rows, "seq", split_axis=1, concat_axis=1, tiled=True)
    span_results = jnp.roll(arrived, -(own_offset % shards), axis=1).reshape(capacity, column_count)
    positions = jnp.arange(rows_here, dtype=jnp.int32)
    live_slots = jnp.arange(capacity, dtype=jnp.int32) < own_count
    passed = jnp.sum(
        ((own_marks[None, :] <= positions[:, None]) & live_slots[None, :]).astype(jnp.int32), axis=1
    )
    return (skip_part.astype(jnp.float32) + span_results[passed - 1].astype(jnp.float32)).astype(
        jnp.bfloat16
    )


def solution(mesh):
    in_specs = (
        P("seq", None),
        P(),
        P(None, "mp"),
        P(None, "mp"),
        P("mp"),
        P("mp", None),
        P("seq", None),
        P(),
        P("seq", "mp"),
        P("mp"),
        P(),
        P("seq", "mp"),
        P("seq", "mp"),
        P("seq", "mp"),
        P("mp", None),
    )
    out_specs = P("seq", "mp")
    def on_device(*arrays):
        heads_here = arrays[11].shape[1] // HEAD
        fits = heads_here == mesh.shape["seq"] and mesh.shape["mp"] == 2
        return (one_head_each if fits else spread_heads)(*arrays)

    return jax.shard_map(
        on_device, mesh=mesh, in_specs=in_specs, out_specs=out_specs, check_vma=False
    )
```

```python
import functools
import math

import jax
import jax.numpy as jnp
from jax import lax
from jax.experimental import pallas as pl
from jax.experimental.pallas import tpu as pltpu
from jax.sharding import PartitionSpec as P

HEADS = 32
KV_HEADS = 8
HEAD = 128
CH_OWN = 64


eps = 1e-05
masked = -1e30
TILE = 16


def swapped(value):
    return lax.ppermute(value, "mp", [(0, 1), (1, 0)])


def vmem():
    return pl.BlockSpec(memory_space=pltpu.VMEM)


def smem():
    return pl.BlockSpec(memory_space=pltpu.SMEM)


def in_place():
    return pl.BlockSpec(memory_space=pl.ANY)


def in_hbm():
    return pl.BlockSpec(memory_space=pltpu.HBM)


def seat():
    return lax.axis_index("seq"), lax.axis_index("mp")


def params(mebibytes=24):
    return pltpu.CompilerParams(vmem_limit_bytes=mebibytes * 2**20)


def brief():
    return pl.CostEstimate(flops=1, bytes_accessed=1, transcendentals=0)


def lanes(which, size):
    return pl.ds(pl.multiple_of(which * size, size), size)


def one_minus_exp(u):
    series = jnp.ones_like(u)
    for order in range(9, 1, -1):
        series = 1.0 - u * (1.0 / order) * series
    return jnp.where(u < 0.5, u * series, 1.0 - jnp.exp(-u))


def softplus(v):
    tail = jnp.exp(-jnp.abs(v))
    series = jnp.ones_like(tail)
    for order in range(6, 1, -1):
        series = 1.0 - tail * ((order - 1.0) / order) * series
    return jnp.maximum(v, 0.0) + jnp.where(tail < 0.03, tail * series, jnp.log(1.0 + tail))


def scan_kernel(
    bytes_hbm,
    gain_ref,
    input_hbm,
    step_hbm,
    rate_ref,
    local_ref,
    through_ref,
    ends_ref,
    bytes_ref,
    input_ref,
    step_ref,
    sems,
):
    fetches = []
    for index, pair in enumerate(
        ((bytes_hbm, bytes_ref), (step_hbm, step_ref), (input_hbm, input_ref))
    ):
        fetches.append(pltpu.make_async_copy(*pair, sems.at[index]))
        fetches[-1].start()
    fetches[0].wait()
    values = bytes_ref[...].astype(jnp.float32)
    scale = lax.rsqrt(jnp.mean(values * values, axis=1, keepdims=True) + eps)
    normed = (values * scale * gain_ref[...]).astype(jnp.bfloat16)
    fetches[1].wait()
    steps = softplus(jnp.dot(normed, step_ref[...], preferred_element_type=jnp.float32))
    rate_steps = steps * rate_ref[...]
    fetches[2].wait()
    inputs = jnp.dot(normed, input_ref[...], preferred_element_type=jnp.float32)
    decays = jnp.exp(-rate_steps)
    drives = jnp.sqrt(one_minus_exp(2.0 * rate_steps)) * inputs
    rows, width = decays.shape
    tile = 8
    decays = decays.reshape(rows // tile, tile, width)
    drives = drives.reshape(rows // tile, tile, width)
    place = lax.broadcasted_iota(jnp.int32, decays.shape, 1)
    for reach in (1, 2, 4):
        before_decays = pltpu.roll(decays, reach, 1)
        before_drives = pltpu.roll(drives, reach, 1)
        inside = place >= reach
        drives = jnp.where(inside, decays * before_drives + drives, drives)
        decays = jnp.where(inside, decays * before_decays, decays)
    state = jnp.zeros((1, width), jnp.float32)
    kept = jnp.ones((1, width), jnp.float32)
    for index in range(rows // tile):
        states = decays[index] * state + drives[index]
        passing = decays[index] * kept
        local_ref[pl.ds(index * tile, tile), :] = states
        through_ref[pl.ds(index * tile, tile), :] = passing
        state = states[tile - 1 :, :]
        kept = passing[tile - 1 :, :]
    for index in range(ends_ref.shape[0]):
        ends_ref[index, 0:1, :] = kept
        ends_ref[index, 1:2, :] = state


def states_kernel(local_ref, through_ref, mixer_ref, ends_ref, states_ref, other_ref):
    me, lane = seat()
    carry = jnp.zeros((1, local_ref.shape[1]), jnp.float32)
    for shard in range(ends_ref.shape[0]):
        later = ends_ref[shard, 0:1, :] * carry + ends_ref[shard, 1:2, :]
        carry = jnp.where(shard < me, later, carry)
    states = (local_ref[...] + through_ref[...] * carry).astype(jnp.bfloat16)
    states_ref[...] = states
    half = other_ref.shape[1]
    other_ref[...] = jnp.dot(
        states, mixer_ref[:, lanes(1 - lane, half)], preferred_element_type=jnp.float32
    )


def pool_kernel(states_ref, mixer_ref, other_ref, bytes_ref, pick_ref, encoded_ref, out_ref):
    half = other_ref.shape[1]
    columns = lanes(seat()[1], half)
    mixed = jnp.dot(states_ref[...], mixer_ref[:, columns], preferred_element_type=jnp.float32)
    skip = bytes_ref[:, columns].astype(jnp.float32)
    encoded = (skip + (mixed + other_ref[...])).astype(jnp.bfloat16)
    encoded_ref[...] = encoded
    picked = jnp.dot(pick_ref[...], encoded, preferred_element_type=jnp.float32)
    out_ref[...] = picked.astype(jnp.bfloat16).reshape(out_ref.shape)


def own_kernel(pick_ref, arrived_ref, out_ref):
    shards, slots, half = arrived_ref.shape
    rows = arrived_ref[...].astype(jnp.float32).reshape(shards * slots, half)
    own = jnp.dot(
        pick_ref[...], rows.astype(jnp.bfloat16), preferred_element_type=jnp.float32
    ).astype(jnp.bfloat16)
    for index in range(out_ref.shape[0]):
        out_ref[index] = own


def rows_at(which, size):
    return pl.ds(pl.multiple_of(which * size, size), size)


def copy_all(pairs, sems):
    copies = []
    for index, (from_ref, to_ref) in enumerate(pairs):
        copy = pltpu.make_async_copy(from_ref, to_ref, sems.at[index])
        copy.start()
        copies.append(copy)
    for copy in copies:
        copy.wait()


def cut_kernel(plane, query_ref, key_ref, value_ref, *rest):
    outs, sems = rest[:-1], rest[-1]
    layers = outs[0].shape[0]
    cross = lax.rem(seat()[0], plane)
    pairs = []
    for mask in range(plane):
        for layer in range(layers):
            column = lanes(layer * plane + (cross ^ mask), HEAD)
            pairs.append((query_ref.at[:, column], outs[mask].at[layer, :, pl.ds(0, HEAD)]))

    def start(far_ref, first_masks):
        for mask in first_masks:
            for layer in range(layers):
                number = mask * layers + layer
                pltpu.make_async_copy(
                    far_ref.at[:, pl.ds(layer * HEAD, HEAD)],
                    outs[mask].at[layer, :, pl.ds(HEAD, HEAD)],
                    sems.at[plane * layers + number],
                ).start()

    here, there = range(plane // 2), range(plane // 2, plane)

    @pl.when(cross < plane // 2)
    def _():
        start(key_ref, here)
        start(value_ref, there)

    @pl.when(cross >= plane // 2)
    def _():
        start(value_ref, here)
        start(key_ref, there)

    copy_all(pairs, sems)
    for mask in range(plane):
        for layer in range(layers):
            number = mask * layers + layer
            pltpu.make_async_copy(
                key_ref.at[:, pl.ds(layer * HEAD, HEAD)],
                outs[mask].at[layer, :, pl.ds(HEAD, HEAD)],
                sems.at[plane * layers + number],
            ).wait()


def stack_kernel(gate_ref, *rest):
    pieces, (out_ref, sems) = rest[:-2], rest[-2:]
    copy_all([(piece, out_ref.at[step]) for step, piece in enumerate(pieces)], sems)


def regroup_kernel(plane, gate_ref, *rest):
    pieces, outs, sems = rest[:plane], rest[plane:-1], rest[-1]
    layer = seat()[0] // plane
    pairs = []
    for step, out_ref in enumerate(outs):
        for mask in range(plane):
            pairs.append((pieces[mask].at[layer ^ step], out_ref.at[mask]))
    copy_all(pairs, sems)


def up_kernel(plane, bias_ref, gain_ref, near_ref, far_ref, *rest):
    up_pieces, rest = rest[: plane + 1], rest[plane + 1 :]
    inner_ref, total_ref, pooled, up, sems = rest
    me, lane = seat()
    layer, cross = me // plane, lax.rem(me, plane)
    half = near_ref.shape[1]
    up_rows = up_pieces[0].shape[1]
    rows = inner_ref.shape[0]
    pairs = [
        (near_ref, pooled.at[:, lanes(lane, half)]),
        (far_ref, pooled.at[:, lanes(1 - lane, half)]),
    ]
    layers = up_pieces[0].shape[0]
    for mask in range(plane):
        for step in range(layers):
            shard = (layer ^ step) * plane + (cross ^ mask)
            piece = up_pieces[mask].at[step]
            if mask == plane - 1:
                piece = up_pieces[mask + step // (layers // 2)].at[step % (layers // 2)]
            pairs.append((piece, up.at[rows_at(shard, up_rows), :]))
    copy_all(pairs, sems)
    block = min(256, rows)
    part = min(1024, up.shape[1])

    def up_block(index, carried):
        where = rows_at(index, block)
        left = pooled[where, :]
        total = jnp.zeros((block, 1), jnp.float32)
        for start in range(0, up.shape[1], part):
            columns = pl.ds(start, part)
            widened = jnp.dot(left, up[:, columns], preferred_element_type=jnp.float32)
            widened = (widened + bias_ref[:, columns]).astype(jnp.bfloat16).astype(jnp.float32)
            inner_ref[where, columns] = (widened * gain_ref[:, columns]).astype(jnp.bfloat16)
            total = total + jnp.sum(widened * widened, axis=1, keepdims=True)
        total_ref[where, :] = jnp.broadcast_to(total, (block, HEAD))
        return carried

    lax.fori_loop(0, rows // block, up_block, 0)


def sums_kernel(plane, inner_ref, total_ref, *rest):
    layers = (len(rest) - 4) // 2
    mine, far = rest[:layers], rest[layers : 2 * layers]
    own_ref, other_ref, weights, sems = rest[2 * layers :]
    me, lane = seat()
    layer, cross = me // plane, lax.rem(me, plane)
    piece_rows = mine[0].shape[1]
    rows = inner_ref.shape[0]
    span = 2 * HEAD
    keep = layers // 2

    def pairs_from(first):
        pairs = []
        for head, pieces in enumerate((mine, far)):
            for step in range(keep):
                for mask in range(plane):
                    shard = (lax.rem(layer, keep) ^ step) * plane + (cross ^ mask)
                    to_ref = weights.at[rows_at(shard, piece_rows), pl.ds(head * span, span)]
                    pairs.append((pieces[first + step].at[mask], to_ref))
        return pairs

    low_is_own = layer // keep == lane

    @pl.when(low_is_own)
    def _():
        copy_all(pairs_from(0), sems)

    @pl.when(jnp.logical_not(low_is_own))
    def _():
        copy_all(pairs_from(keep), sems)

    block = min(256, rows)

    def sums_block(index, carried):
        where = rows_at(index, block)
        sums = jnp.dot(inner_ref[where, :], weights[...], preferred_element_type=jnp.float32)
        own_ref[where, 0:span] = sums[:, :span]
        own_ref[where, span:] = total_ref[where, :]
        other_ref[where, 0:span] = sums[:, span:]
        other_ref[where, span:] = total_ref[where, :]
        return carried

    lax.fori_loop(0, rows // block, sums_block, 0)


def heads_kernel(features, plane, own_ref, other_ref, query_ref, pair_ref, queries, pairs):
    rows = own_ref.shape[0]
    span = 2 * HEAD
    shards = rows // CH_OWN
    layers = shards // plane
    for index in range(shards):
        where = pl.ds(index * CH_OWN, CH_OWN)
        sums = own_ref[where, :] + other_ref[where, :]
        scale = lax.rsqrt(sums[:, span:] * (1.0 / features) + eps)
        shard = (index % layers) * plane + index // layers
        natural = pl.ds(shard, CH_OWN, stride=shards)
        queries[natural, :] = sums[:, :HEAD] * scale
        pairs[natural, :] = sums[:, HEAD:span] * scale
    query_ref[...] = queries[...].astype(jnp.bfloat16)
    pair_ref[...] = pairs[...].astype(jnp.bfloat16)


def attend_kernel(plane, place_ref, query_ref, pair_ref, other_ref, out_ref, keys, values, attended):
    rows = query_ref.shape[0]
    window = out_ref.shape[1]
    block = min(256, rows)
    holds_keys = lax.rem(seat()[0], plane) < plane // 2

    @pl.when(holds_keys)
    def _():
        keys[...] = pair_ref[...]
        values[...] = other_ref[...]

    @pl.when(jnp.logical_not(holds_keys))
    def _():
        keys[...] = other_ref[...]
        values[...] = pair_ref[...]

    score_scale = 1.0 / math.sqrt(HEAD)
    for start in range(0, rows, block):
        stop = start + block
        scores = lax.dot_general(
            query_ref[start:stop, :],
            keys[0:stop, :],
            (((1,), (1,)), ((), ())),
            preferred_element_type=jnp.float32,
        )
        spots = lax.broadcasted_iota(jnp.int32, scores.shape, 1)
        mine = lax.broadcasted_iota(jnp.int32, scores.shape, 0) + start
        scores = jnp.where(spots <= mine, scores * score_scale, masked)
        peak = jnp.max(scores, axis=1, keepdims=True)
        lifted = jnp.exp(scores - peak)
        denominator = jnp.sum(lifted, axis=1, keepdims=True)
        weighted = jnp.dot(
            lifted.astype(jnp.bfloat16), values[0:stop, :], preferred_element_type=jnp.float32
        )
        attended[start:stop, :] = (weighted / denominator).astype(jnp.bfloat16)
    attended[rows:, :] = jnp.zeros((attended.shape[0] - rows, HEAD), jnp.bfloat16)
    for shard in range(out_ref.shape[0]):
        first = place_ref[shard]
        out_ref[shard] = attended[pl.ds(pl.multiple_of(first * TILE, TILE), window), :]


def return_kernel(weight_ref, pieces_ref, own_ref, other_ref, attended):
    half = own_ref.shape[1]
    lane = seat()[1]
    for head in range(pieces_ref.shape[0]):
        attended[:, head * HEAD : (head + 1) * HEAD] = pieces_ref[head]
    other_ref[...] = jnp.dot(
        attended[...], weight_ref[:, lanes(1 - lane, half)], preferred_element_type=jnp.float32
    )
    own_ref[...] = jnp.dot(
        attended[...], weight_ref[:, lanes(lane, half)], preferred_element_type=jnp.float32
    )


def join_kernel(own_ref, other_ref, encoded_ref, spread_ref, out_ref):
    returned = (own_ref[...] + other_ref[...]).astype(jnp.bfloat16)
    results = jnp.dot(spread_ref[...], returned, preferred_element_type=jnp.float32)
    out_ref[...] = (encoded_ref[...].astype(jnp.float32) + results).astype(jnp.bfloat16)


def one_head_each(
    byte_states,
    outer_gain,
    mamba_input,
    mamba_step,
    decay_rate,
    mixer_weight,
    boundaries,
    span_counts,
    up_weight,
    up_bias,
    inner_gain,
    query_weight,
    key_weight,
    value_weight,
    return_weight,
):
    shards = lax.axis_size("seq")
    me = lax.axis_index("seq")
    lane = lax.axis_index("mp")
    plane = HEADS // KV_HEADS
    layers = shards // plane
    rows_here, width = byte_states.shape
    half = mamba_input.shape[1]
    capacity = boundaries.shape[1]
    window = capacity + TILE
    total_rows = CH_OWN * shards
    inner_width = inner_gain.shape[0]
    inner_half = up_bias.shape[0]
    weight_rows = query_weight.shape[0]
    f32, bf16 = jnp.float32, jnp.bfloat16
    layer, cross = me // plane, me % plane
    layer_groups = [[first + plane * step for step in range(layers)] for first in range(plane)]
    plane_groups = [[first * plane + step for step in range(plane)] for first in range(layers)]

    def over(value, mask):
        return lax.ppermute(value, "seq", [(i, i ^ mask) for i in range(shards)])

    def after(value, done):
        return lax.optimization_barrier((value, done))[0]

    own_gain = lax.dynamic_slice_in_dim(inner_gain, lane * inner_half, inner_half)[None, :]
    seq_ids = jnp.arange(shards, dtype=jnp.int32)
    offsets = jnp.cumsum(span_counts) - span_counts
    own_offset = jnp.sum(jnp.where(seq_ids == me, offsets, 0))
    own_count = jnp.sum(jnp.where(seq_ids == me, span_counts, 0))
    place = offsets // TILE
    own_marks = boundaries[0]
    positions = jnp.arange(rows_here, dtype=jnp.int32)
    spans_here = jnp.arange(capacity, dtype=jnp.int32)
    live = spans_here < own_count
    slots = capacity // shards
    slot_ids = jnp.arange(slots, dtype=jnp.int32)
    local_span = slot_ids[None, :] * shards + ((seq_ids - own_offset) % shards)[:, None]
    is_span = spans_here[None, :] == local_span.reshape(-1)[:, None]
    byte_at = jnp.sum(jnp.where(is_span, jnp.minimum(own_marks, rows_here - 1)[None, :], 0), axis=1)
    pool_pick = (positions[None, :] == byte_at[:, None]).astype(bf16)
    own_spans = me + jnp.arange(CH_OWN, dtype=jnp.int32) * shards
    origin = jnp.sum((offsets[None, :] <= own_spans[:, None]).astype(jnp.int32), axis=1) - 1
    origin_offset = jnp.sum(
        jnp.where(seq_ids[None, :] == origin[:, None], offsets[None, :], 0), axis=1
    )
    arrived_row = origin * slots + (own_spans - origin_offset) // shards
    own_pick = (
        jnp.arange(shards * slots, dtype=jnp.int32)[None, :] == arrived_row[:, None]
    ).astype(bf16)
    passed = jnp.sum(
        ((own_marks[None, :] <= positions[:, None]) & live[None, :]).astype(jnp.int32), axis=1
    )
    result_row = passed - 1 + own_offset % TILE
    spread = (jnp.arange(window, dtype=jnp.int32)[None, :] == result_row[:, None]).astype(bf16)

    local, through, ends = pl.pallas_call(
        scan_kernel,
        out_shape=(
            jax.ShapeDtypeStruct((rows_here, half), f32),
            jax.ShapeDtypeStruct((rows_here, half), f32),
            jax.ShapeDtypeStruct((shards, 2, half), f32),
        ),
        in_specs=[in_hbm(), vmem(), in_hbm(), in_hbm(), vmem()],
        out_specs=(vmem(),) * 3,
        scratch_shapes=[
            pltpu.VMEM(byte_states.shape, bf16),
            pltpu.VMEM(mamba_input.shape, bf16),
            pltpu.VMEM(mamba_step.shape, bf16),
            pltpu.SemaphoreType.DMA((3,)),
        ],
        cost_estimate=brief(),
        compiler_params=params(20),
    )(byte_states, outer_gain[None, :], mamba_input, mamba_step, decay_rate[None, :])
    cuts = pl.pallas_call(
        functools.partial(cut_kernel, plane),
        out_shape=(jax.ShapeDtypeStruct((layers, weight_rows, 2 * HEAD), bf16),) * plane,
        in_specs=[in_hbm()] * 3,
        out_specs=(vmem(),) * plane,
        scratch_shapes=[pltpu.SemaphoreType.DMA((2 * shards,))],
        cost_estimate=brief(),
        compiler_params=params(8),
    )(*after((query_weight, key_weight, value_weight), ends))
    behind = after(up_weight, ends)
    up_layers = [up_weight] + [over(behind, plane * step) for step in range(1, layers - 1)]
    pair_planes = [cuts[0]] + [over(cuts[mask], mask) for mask in range(1, plane - 1)]
    ends = lax.all_to_all(ends, "seq", 0, 0, tiled=True)
    states, other_part = pl.pallas_call(
        states_kernel,
        out_shape=(
            jax.ShapeDtypeStruct((rows_here, half), bf16),
            jax.ShapeDtypeStruct((rows_here, half), f32),
        ),
        in_specs=[vmem()] * 4,
        out_specs=(vmem(),) * 2,
        cost_estimate=brief(),
        compiler_params=params(8),
    )(local, through, mixer_weight, ends)
    encoded, leaving = pl.pallas_call(
        pool_kernel,
        out_shape=(
            jax.ShapeDtypeStruct((rows_here, half), bf16),
            jax.ShapeDtypeStruct((shards, slots, half), bf16),
        ),
        in_specs=[vmem()] * 5,
        out_specs=(vmem(),) * 2,
        cost_estimate=brief(),
        compiler_params=params(8),
    )(states, mixer_weight, swapped(other_part), byte_states, pool_pick)
    arrived = lax.all_to_all(leaving, "seq", 0, 0, tiled=True)
    up_layers.append(over(after(up_weight, leaving), plane * (layers - 1)))
    pair_planes.append(over(after(cuts[plane - 1], leaving), plane - 1))
    own_rows = pl.pallas_call(
        own_kernel,
        out_shape=jax.ShapeDtypeStruct((layers, CH_OWN, half), bf16),
        in_specs=[vmem()] * 2,
        out_specs=vmem(),
        cost_estimate=brief(),
        compiler_params=params(8),
    )(own_pick, arrived)
    near_layer = lax.all_to_all(
        own_rows, "seq", 0, 0, axis_index_groups=layer_groups, tiled=True
    )
    up_here = pl.pallas_call(
        stack_kernel,
        out_shape=jax.ShapeDtypeStruct((layers, *up_weight.shape), bf16),
        in_specs=[in_place()] + [in_hbm()] * layers,
        out_specs=vmem(),
        scratch_shapes=[pltpu.SemaphoreType.DMA((layers,))],
        cost_estimate=brief(),
        compiler_params=params(8),
    )(own_rows, *up_layers)
    up_beside, up_across = over(up_here, 1), over(up_here, 2)
    pair_layers = pl.pallas_call(
        functools.partial(regroup_kernel, plane),
        out_shape=(jax.ShapeDtypeStruct((plane, weight_rows, 2 * HEAD), bf16),) * layers,
        in_specs=[in_place()] * 2 + [in_hbm()] * (plane - 1),
        out_specs=(vmem(),) * layers,
        scratch_shapes=[pltpu.SemaphoreType.DMA((shards,))],
        cost_estimate=brief(),
        compiler_params=params(8),
    )(near_layer, *pair_planes)
    mine = [pair_layers[0]] + [over(pair_layers[step], plane * step) for step in range(1, layers)]
    up_beside, up_across, mine[1] = lax.optimization_barrier((up_beside, up_across, mine[1]))
    up_corner = [
        over(up_beside[: layers // 2], 2),
        over(up_across[layers // 2 :], 1),
    ]
    near = lax.all_to_all(
        jnp.broadcast_to(near_layer[None], (plane, layers, CH_OWN, half)),
        "seq",
        0,
        0,
        axis_index_groups=plane_groups,
        tiled=True,
    ).reshape(total_rows, half)

    near, mine[2] = lax.optimization_barrier((near, mine[2]))

    up_pieces = [up_here, up_beside, up_across, *up_corner]
    inner, totals = pl.pallas_call(
        functools.partial(up_kernel, plane),
        out_shape=(
            jax.ShapeDtypeStruct((total_rows, inner_half), bf16),
            jax.ShapeDtypeStruct((total_rows, HEAD), f32),
        ),
        in_specs=[vmem()] * 2 + [in_place()] * 3 + [in_hbm()] * (len(up_pieces) - 1),
        out_specs=(vmem(),) * 2,
        scratch_shapes=[
            pltpu.VMEM((total_rows, width), bf16),
            pltpu.VMEM((width, inner_half), bf16),
            pltpu.SemaphoreType.DMA((2 + shards,)),
        ],
        cost_estimate=brief(),
        compiler_params=params(28),
    )(up_bias[None, :], own_gain, near, swapped(near), *up_pieces)
    mine[layers - 1] = after(mine[layers - 1], totals)
    far = [swapped(piece) for piece in mine]
    own_sums, other_sums = pl.pallas_call(
        functools.partial(sums_kernel, plane),
        out_shape=(jax.ShapeDtypeStruct((total_rows, 3 * HEAD), f32),) * 2,
        in_specs=[vmem()] * 2 + [in_place()] * (2 * layers),
        out_specs=(vmem(),) * 2,
        scratch_shapes=[
            pltpu.VMEM((inner_half, 4 * HEAD), bf16),
            pltpu.SemaphoreType.DMA((shards,)),
        ],
        cost_estimate=brief(),
        compiler_params=params(16),
    )(inner, totals, *mine, *far)
    queries, pairs = pl.pallas_call(
        functools.partial(heads_kernel, inner_width, plane),
        out_shape=(jax.ShapeDtypeStruct((total_rows, HEAD), bf16),) * 2,
        in_specs=[vmem()] * 2,
        out_specs=(vmem(),) * 2,
        scratch_shapes=[pltpu.VMEM((total_rows, HEAD), f32)] * 2,
        cost_estimate=brief(),
        compiler_params=params(8),
    )(own_sums, swapped(other_sums))
    leaving = pl.pallas_call(
        functools.partial(attend_kernel, plane),
        out_shape=jax.ShapeDtypeStruct((shards, window, HEAD), bf16),
        in_specs=[smem()] + [vmem()] * 3,
        out_specs=vmem(),
        scratch_shapes=[
            pltpu.VMEM((total_rows, HEAD), bf16),
            pltpu.VMEM((total_rows, HEAD), bf16),
            pltpu.VMEM((total_rows + window, HEAD), bf16),
        ],
        cost_estimate=brief(),
        compiler_params=params(12),
    )(place, queries, pairs, over(pairs, 2))
    pieces = lax.all_to_all(leaving, "seq", 0, 0, tiled=True)
    own_back, other_back = pl.pallas_call(
        return_kernel,
        out_shape=(jax.ShapeDtypeStruct((window, half), f32),) * 2,
        in_specs=[vmem()] * 2,
        out_specs=(vmem(),) * 2,
        scratch_shapes=[pltpu.VMEM((window, shards * HEAD), bf16)],
        cost_estimate=brief(),
        compiler_params=params(12),
    )(return_weight, pieces)
    return pl.pallas_call(
        join_kernel,
        out_shape=jax.ShapeDtypeStruct((rows_here, half), bf16),
        in_specs=[vmem()] * 4,
        out_specs=vmem(),
        cost_estimate=brief(),
        compiler_params=params(8),
    )(own_back, swapped(other_back), encoded, spread)


def prefix(value, axis, join, neutral):
    count, mine = (lax.axis_size(axis), lax.axis_index(axis))
    pieces = jax.tree.map(lambda part: lax.all_gather(part, axis), value)
    so_far = jax.tree.map(
        lambda part, zero: jnp.full_like(part, 0) + jnp.asarray(zero, part.dtype), value, neutral
    )

    def lap(position, so_far):
        longer = join(so_far, jax.tree.map(lambda part: part[position], pieces))
        return jax.tree.map(lambda new, old: jnp.where(position < mine, new, old), longer, so_far)

    return lax.fori_loop(0, count - 1, lap, so_far)


def rms_scale(values, gain):
    values = values.astype(jnp.float32)
    return values * lax.rsqrt(jnp.mean(values * values, axis=-1, keepdims=True) + eps) * gain


def combine_pairs(earlier, later):
    return (earlier[0] * later[0], later[0] * earlier[1] + later[1])


def pick_table(table, wanted, seq_ids):
    return jnp.sum(jnp.where(seq_ids[None, :] == wanted[:, None], table[None, :], 0), axis=1)


def block_size(piece_rows, shard_rows):
    limit = max(1, 1024 // shard_rows)
    pieces = max(1, piece_rows // shard_rows)
    best_size = 1
    for candidate in range(1, limit + 1):
        if pieces % candidate == 0:
            best_size = candidate
    return min(piece_rows, best_size * shard_rows)


def spread_heads(
    byte_states,
    outer_gain,
    mamba_input,
    mamba_step,
    decay_rate,
    mixer_weight,
    boundaries,
    span_counts,
    up_weight,
    up_bias,
    inner_gain,
    query_weight,
    key_weight,
    value_weight,
    return_weight,
):
    shards = lax.axis_size("seq")
    own_shard = lax.axis_index("seq")
    own_lane = lax.axis_index("mp")
    rows_here = byte_states.shape[0]
    capacity = boundaries.shape[1]
    column_count = mamba_input.shape[1]
    kv_local = key_weight.shape[1] // HEAD
    group_size = HEADS // KV_HEADS
    slot_count = capacity // shards
    offsets = jnp.cumsum(span_counts) - span_counts
    seq_ids = jnp.arange(shards, dtype=jnp.int32)
    own_offset = jnp.sum(jnp.where(seq_ids == own_shard, offsets, 0))
    own_count = jnp.sum(jnp.where(seq_ids == own_shard, span_counts, 0))
    normed = rms_scale(byte_states, outer_gain).astype(jnp.bfloat16)
    inputs = jnp.dot(normed, mamba_input, preferred_element_type=jnp.float32)
    step_sizes = jax.nn.softplus(jnp.dot(normed, mamba_step, preferred_element_type=jnp.float32))
    rate_steps = step_sizes * decay_rate
    decays = jnp.exp(-rate_steps)
    drives = jnp.sqrt(-jnp.expm1(-2.0 * rate_steps)) * inputs
    through, local_states = lax.associative_scan(combine_pairs, (decays, drives), axis=0)
    starting = (jnp.ones((column_count,), jnp.float32), jnp.zeros((column_count,), jnp.float32))
    arriving = prefix((through[-1], local_states[-1]), "seq", combine_pairs, starting)
    states = (local_states + through * arriving[1][None, :]).astype(jnp.bfloat16)
    partial_value = jnp.dot(states, mixer_weight, preferred_element_type=jnp.float32)
    mixed_sum = lax.psum(partial_value, "mp")
    encoded = (byte_states.astype(jnp.float32) + mixed_sum).astype(jnp.bfloat16)
    skip_part = lax.dynamic_slice_in_dim(encoded, own_lane * column_count, column_count, 1)
    own_marks = boundaries[0]
    pooled = encoded[jnp.minimum(own_marks, rows_here - 1)]
    row_width = pooled.shape[1]
    outgoing = jnp.roll(pooled.reshape(slot_count, shards, row_width), own_offset % shards, axis=1)
    incoming = lax.all_to_all(outgoing, "seq", split_axis=1, concat_axis=1, tiled=True)
    position = jnp.arange(CH_OWN, dtype=jnp.int32)
    span_index = own_shard + position * shards
    source = jnp.sum((offsets[None, :] <= span_index[:, None]).astype(jnp.int32), axis=1) - 1
    source_offset = pick_table(offsets, source, seq_ids)
    slot_index = (span_index - source_offset) // shards
    gathered_rows = incoming.reshape(slot_count * shards, row_width)[slot_index * shards + source]
    columns = gathered_rows
    widened_sum = jnp.dot(
        columns,
        lax.all_gather(up_weight, "seq", axis=0, tiled=True),
        preferred_element_type=jnp.float32,
    )
    widened_share = (widened_sum + up_bias[None, :]).astype(jnp.bfloat16)
    widened = lax.all_gather(widened_share, "mp", axis=1, tiled=True)
    inner_normed = rms_scale(widened, inner_gain).astype(jnp.bfloat16)
    columns = inner_normed
    query_part = jnp.dot(
        columns,
        lax.all_gather(query_weight, "seq", axis=0, tiled=True),
        preferred_element_type=jnp.float32,
    )
    key_part = jnp.dot(
        columns,
        lax.all_gather(key_weight, "seq", axis=0, tiled=True),
        preferred_element_type=jnp.float32,
    )
    value_part = jnp.dot(
        columns,
        lax.all_gather(value_weight, "seq", axis=0, tiled=True),
        preferred_element_type=jnp.float32,
    )
    queries = query_part.astype(jnp.bfloat16)
    key_rows = key_part.astype(jnp.bfloat16)
    value_rows = value_part.astype(jnp.bfloat16)
    query_count = queries.shape[0]
    grouped = (
        queries.reshape(query_count, kv_local, group_size, HEAD)
        .transpose(1, 0, 2, 3)
        .reshape(kv_local, query_count * group_size, HEAD)
    )
    row_index = jnp.repeat(span_index, group_size)
    shard_rows = key_rows.shape[0]
    score_scale = 1.0 / math.sqrt(HEAD)

    def key_index(whole_index):
        return whole_index // shard_rows + whole_index % shard_rows * shards

    def attend_block(running, key_block, value_block, index_block):
        row_peak, denominator, weighted = running
        scores = (
            jnp.einsum("hqd,khd->hqk", grouped, key_block, preferred_element_type=jnp.float32)
            * score_scale
        )
        scores = jnp.where(index_block[None, None, :] <= row_index[None, :, None], scores, masked)
        new_peak = jnp.maximum(row_peak, jnp.max(scores, axis=2))
        shrink = jnp.exp(row_peak - new_peak)
        lifted = jnp.exp(scores - new_peak[:, :, None])
        denominator = denominator * shrink + jnp.sum(lifted, axis=2)
        weighted = weighted * shrink[:, :, None] + jnp.einsum(
            "hqk,khd->hqd",
            lifted.astype(jnp.bfloat16),
            value_block,
            preferred_element_type=jnp.float32,
        )
        return (new_peak, denominator, weighted)

    query_total = query_count * group_size
    initial = (
        jnp.full((kv_local, query_total), masked, jnp.float32),
        jnp.zeros((kv_local, query_total), jnp.float32),
        jnp.zeros((kv_local, query_total, HEAD), jnp.float32),
    )
    key_piece = lax.all_gather(key_rows, "seq", axis=0, tiled=True)
    value_piece = lax.all_gather(value_rows, "seq", axis=0, tiled=True)
    piece_rows = key_piece.shape[0]
    block_rows = block_size(piece_rows, shard_rows)
    turn_count = piece_rows // block_rows
    key_blocks = key_piece.reshape(turn_count, block_rows, kv_local, HEAD)
    value_blocks = value_piece.reshape(turn_count, block_rows, kv_local, HEAD)

    def one_turn(turn_index, inner_running):
        whole_index = turn_index * block_rows + jnp.arange(block_rows, dtype=jnp.int32)
        return attend_block(
            inner_running, key_blocks[turn_index], value_blocks[turn_index], key_index(whole_index)
        )

    row_peak, denominator, weighted = lax.fori_loop(0, turn_count, one_turn, initial)
    attended = (weighted / denominator[:, :, None]).astype(jnp.bfloat16)
    attended = (
        attended.reshape(kv_local, query_count, group_size, HEAD)
        .transpose(1, 0, 2, 3)
        .reshape(query_count, kv_local * group_size * HEAD)
    )
    projected = jnp.dot(attended, return_weight, preferred_element_type=jnp.float32)
    returned = lax.psum_scatter(
        projected.astype(jnp.bfloat16), "mp", scatter_dimension=1, tiled=True
    )
    slot_ids = jnp.arange(slot_count, dtype=jnp.int32)
    lead_slot = (own_shard - offsets) % shards
    local_span = slot_ids[:, None] * shards + lead_slot[None, :]
    back_index = (offsets[None, :] + local_span - own_shard) // shards
    alive = local_span < span_counts[None, :]
    back_rows = jnp.where(
        alive[:, :, None],
        returned[jnp.clip(back_index, 0, CH_OWN - 1)],
        jnp.zeros((), jnp.bfloat16),
    )
    arrived = lax.all_to_all(back_rows, "seq", split_axis=1, concat_axis=1, tiled=True)
    span_results = jnp.roll(arrived, -(own_offset % shards), axis=1).reshape(capacity, column_count)
    positions = jnp.arange(rows_here, dtype=jnp.int32)
    live_slots = jnp.arange(capacity, dtype=jnp.int32) < own_count
    passed = jnp.sum(
        ((own_marks[None, :] <= positions[:, None]) & live_slots[None, :]).astype(jnp.int32), axis=1
    )
    return (skip_part.astype(jnp.float32) + span_results[passed - 1].astype(jnp.float32)).astype(
        jnp.bfloat16
    )


def solution(mesh):
    in_specs = (
        P("seq", None),
        P(),
        P(None, "mp"),
        P(None, "mp"),
        P("mp"),
        P("mp", None),
        P("seq", None),
        P(),
        P("seq", "mp"),
        P("mp"),
        P(),
        P("seq", "mp"),
        P("seq", "mp"),
        P("seq", "mp"),
        P("mp", None),
    )
    out_specs = P("seq", "mp")
    def on_device(*arrays):
        heads_here = arrays[11].shape[1] // HEAD
        fits = heads_here == mesh.shape["seq"] and mesh.shape["mp"] == 2
        return (one_head_each if fits else spread_heads)(*arrays)

    return jax.shard_map(
        on_device, mesh=mesh, in_specs=in_specs, out_specs=out_specs, check_vma=False
    )
```

```python
import functools
import math

import jax
import jax.numpy as jnp
from jax import lax
from jax.experimental import pallas as pl
from jax.experimental.pallas import tpu as pltpu
from jax.sharding import PartitionSpec as P

HEADS = 32
KV_HEADS = 8
HEAD = 128
CH_OWN = 64


eps = 1e-05
masked = -1e30
TILE = 16


def swapped(value):
    return lax.ppermute(value, "mp", [(0, 1), (1, 0)])


def vmem():
    return pl.BlockSpec(memory_space=pltpu.VMEM)


def smem():
    return pl.BlockSpec(memory_space=pltpu.SMEM)


def in_place():
    return pl.BlockSpec(memory_space=pl.ANY)


def in_hbm():
    return pl.BlockSpec(memory_space=pltpu.HBM)


def seat():
    return lax.axis_index("seq"), lax.axis_index("mp")


def params(mebibytes=24):
    return pltpu.CompilerParams(vmem_limit_bytes=mebibytes * 2**20)


def brief():
    return pl.CostEstimate(flops=1, bytes_accessed=1, transcendentals=0)


def lanes(which, size):
    return pl.ds(pl.multiple_of(which * size, size), size)


def one_minus_exp(u):
    series = jnp.ones_like(u)
    for order in range(9, 1, -1):
        series = 1.0 - u * (1.0 / order) * series
    return jnp.where(u < 0.5, u * series, 1.0 - jnp.exp(-u))


def softplus(v):
    tail = jnp.exp(-jnp.abs(v))
    series = jnp.ones_like(tail)
    for order in range(6, 1, -1):
        series = 1.0 - tail * ((order - 1.0) / order) * series
    return jnp.maximum(v, 0.0) + jnp.where(tail < 0.03, tail * series, jnp.log(1.0 + tail))


def scan_kernel(
    bytes_hbm,
    gain_ref,
    input_hbm,
    step_hbm,
    rate_ref,
    local_ref,
    through_ref,
    ends_ref,
    bytes_ref,
    input_ref,
    step_ref,
    sems,
):
    fetches = []
    for index, pair in enumerate(
        ((bytes_hbm, bytes_ref), (step_hbm, step_ref), (input_hbm, input_ref))
    ):
        fetches.append(pltpu.make_async_copy(*pair, sems.at[index]))
        fetches[-1].start()
    fetches[0].wait()
    values = bytes_ref[...].astype(jnp.float32)
    scale = lax.rsqrt(jnp.mean(values * values, axis=1, keepdims=True) + eps)
    normed = (values * scale * gain_ref[...]).astype(jnp.bfloat16)
    fetches[1].wait()
    steps = softplus(jnp.dot(normed, step_ref[...], preferred_element_type=jnp.float32))
    rate_steps = steps * rate_ref[...]
    fetches[2].wait()
    inputs = jnp.dot(normed, input_ref[...], preferred_element_type=jnp.float32)
    decays = jnp.exp(-rate_steps)
    drives = jnp.sqrt(one_minus_exp(2.0 * rate_steps)) * inputs
    rows, width = decays.shape
    tile = 8
    decays = decays.reshape(rows // tile, tile, width)
    drives = drives.reshape(rows // tile, tile, width)
    place = lax.broadcasted_iota(jnp.int32, decays.shape, 1)
    for reach in (1, 2, 4):
        before_decays = pltpu.roll(decays, reach, 1)
        before_drives = pltpu.roll(drives, reach, 1)
        inside = place >= reach
        drives = jnp.where(inside, decays * before_drives + drives, drives)
        decays = jnp.where(inside, decays * before_decays, decays)
    state = jnp.zeros((1, width), jnp.float32)
    kept = jnp.ones((1, width), jnp.float32)
    for index in range(rows // tile):
        states = decays[index] * state + drives[index]
        passing = decays[index] * kept
        local_ref[pl.ds(index * tile, tile), :] = states
        through_ref[pl.ds(index * tile, tile), :] = passing
        state = states[tile - 1 :, :]
        kept = passing[tile - 1 :, :]
    for index in range(ends_ref.shape[0]):
        ends_ref[index, 0:1, :] = kept
        ends_ref[index, 1:2, :] = state


def states_kernel(local_ref, through_ref, mixer_ref, ends_ref, states_ref, other_ref):
    me, lane = seat()
    carry = jnp.zeros((1, local_ref.shape[1]), jnp.float32)
    for shard in range(ends_ref.shape[0]):
        later = ends_ref[shard, 0:1, :] * carry + ends_ref[shard, 1:2, :]
        carry = jnp.where(shard < me, later, carry)
    states = (local_ref[...] + through_ref[...] * carry).astype(jnp.bfloat16)
    states_ref[...] = states
    half = other_ref.shape[1]
    other_ref[...] = jnp.dot(
        states, mixer_ref[:, lanes(1 - lane, half)], preferred_element_type=jnp.float32
    )


def pool_kernel(states_ref, mixer_ref, other_ref, bytes_ref, pick_ref, encoded_ref, out_ref):
    half = other_ref.shape[1]
    columns = lanes(seat()[1], half)
    mixed = jnp.dot(states_ref[...], mixer_ref[:, columns], preferred_element_type=jnp.float32)
    skip = bytes_ref[:, columns].astype(jnp.float32)
    encoded = (skip + (mixed + other_ref[...])).astype(jnp.bfloat16)
    encoded_ref[...] = encoded
    picked = jnp.dot(pick_ref[...], encoded, preferred_element_type=jnp.float32)
    out_ref[...] = picked.astype(jnp.bfloat16).reshape(out_ref.shape)


def own_kernel(pick_ref, arrived_ref, out_ref):
    shards, slots, half = arrived_ref.shape
    rows = arrived_ref[...].astype(jnp.float32).reshape(shards * slots, half)
    own = jnp.dot(
        pick_ref[...], rows.astype(jnp.bfloat16), preferred_element_type=jnp.float32
    ).astype(jnp.bfloat16)
    for index in range(out_ref.shape[0]):
        out_ref[index] = own


def rows_at(which, size):
    return pl.ds(pl.multiple_of(which * size, size), size)


def copy_all(pairs, sems):
    copies = []
    for index, (from_ref, to_ref) in enumerate(pairs):
        copy = pltpu.make_async_copy(from_ref, to_ref, sems.at[index])
        copy.start()
        copies.append(copy)
    for copy in copies:
        copy.wait()


def cut_kernel(plane, query_ref, key_ref, value_ref, *rest):
    outs, sems = rest[:-1], rest[-1]
    layers = outs[0].shape[0]
    cross = lax.rem(seat()[0], plane)
    pairs = []
    for mask in range(plane):
        for layer in range(layers):
            column = lanes(layer * plane + (cross ^ mask), HEAD)
            pairs.append((query_ref.at[:, column], outs[mask].at[layer, :, pl.ds(0, HEAD)]))

    def start(far_ref, first_masks):
        for mask in first_masks:
            for layer in range(layers):
                number = mask * layers + layer
                pltpu.make_async_copy(
                    far_ref.at[:, pl.ds(layer * HEAD, HEAD)],
                    outs[mask].at[layer, :, pl.ds(HEAD, HEAD)],
                    sems.at[plane * layers + number],
                ).start()

    here, there = range(plane // 2), range(plane // 2, plane)

    @pl.when(cross < plane // 2)
    def _():
        start(key_ref, here)
        start(value_ref, there)

    @pl.when(cross >= plane // 2)
    def _():
        start(value_ref, here)
        start(key_ref, there)

    copy_all(pairs, sems)
    for mask in range(plane):
        for layer in range(layers):
            number = mask * layers + layer
            pltpu.make_async_copy(
                key_ref.at[:, pl.ds(layer * HEAD, HEAD)],
                outs[mask].at[layer, :, pl.ds(HEAD, HEAD)],
                sems.at[plane * layers + number],
            ).wait()


def stack_kernel(gate_ref, *rest):
    pieces, (out_ref, sems) = rest[:-2], rest[-2:]
    copy_all([(piece, out_ref.at[step]) for step, piece in enumerate(pieces)], sems)


def regroup_kernel(plane, gate_ref, *rest):
    pieces, outs, sems = rest[:plane], rest[plane:-1], rest[-1]
    layer = seat()[0] // plane
    pairs = []
    for step, out_ref in enumerate(outs):
        for mask in range(plane):
            pairs.append((pieces[mask].at[layer ^ step], out_ref.at[mask]))
    copy_all(pairs, sems)


def up_kernel(plane, bias_ref, gain_ref, near_ref, far_ref, *rest):
    up_pieces, rest = rest[: plane + 1], rest[plane + 1 :]
    inner_ref, total_ref, pooled, up, sems = rest
    me, lane = seat()
    layer, cross = me // plane, lax.rem(me, plane)
    half = near_ref.shape[1]
    up_rows = up_pieces[0].shape[1]
    rows = inner_ref.shape[0]
    pairs = [
        (near_ref, pooled.at[:, lanes(lane, half)]),
        (far_ref, pooled.at[:, lanes(1 - lane, half)]),
    ]
    layers = up_pieces[0].shape[0]
    for mask in range(plane):
        for step in range(layers):
            shard = (layer ^ step) * plane + (cross ^ mask)
            piece = up_pieces[mask].at[step]
            if mask == plane - 1:
                piece = up_pieces[mask + step // (layers // 2)].at[step % (layers // 2)]
            pairs.append((piece, up.at[rows_at(shard, up_rows), :]))
    copy_all(pairs, sems)
    block = min(256, rows)
    part = min(1024, up.shape[1])

    def up_block(index, carried):
        where = rows_at(index, block)
        left = pooled[where, :]
        total = jnp.zeros((block, 1), jnp.float32)
        for start in range(0, up.shape[1], part):
            columns = pl.ds(start, part)
            widened = jnp.dot(left, up[:, columns], preferred_element_type=jnp.float32)
            widened = (widened + bias_ref[:, columns]).astype(jnp.bfloat16).astype(jnp.float32)
            inner_ref[where, columns] = (widened * gain_ref[:, columns]).astype(jnp.bfloat16)
            total = total + jnp.sum(widened * widened, axis=1, keepdims=True)
        total_ref[where, :] = jnp.broadcast_to(total, (block, HEAD))
        return carried

    lax.fori_loop(0, rows // block, up_block, 0)


def sums_kernel(plane, inner_ref, total_ref, *rest):
    layers = (len(rest) - 4) // 2
    mine, far = rest[:layers], rest[layers : 2 * layers]
    own_ref, other_ref, weights, sems = rest[2 * layers :]
    me, lane = seat()
    layer, cross = me // plane, lax.rem(me, plane)
    piece_rows = mine[0].shape[1]
    rows = inner_ref.shape[0]
    span = 2 * HEAD
    keep = layers // 2

    def pairs_from(first):
        pairs = []
        for head, pieces in enumerate((mine, far)):
            for step in range(keep):
                for mask in range(plane):
                    shard = (lax.rem(layer, keep) ^ step) * plane + (cross ^ mask)
                    to_ref = weights.at[rows_at(shard, piece_rows), pl.ds(head * span, span)]
                    pairs.append((pieces[first + step].at[mask], to_ref))
        return pairs

    low_is_own = layer // keep == lane

    @pl.when(low_is_own)
    def _():
        copy_all(pairs_from(0), sems)

    @pl.when(jnp.logical_not(low_is_own))
    def _():
        copy_all(pairs_from(keep), sems)

    block = min(256, rows)

    def sums_block(index, carried):
        where = rows_at(index, block)
        sums = jnp.dot(inner_ref[where, :], weights[...], preferred_element_type=jnp.float32)
        own_ref[where, 0:span] = sums[:, :span]
        own_ref[where, span:] = total_ref[where, :]
        other_ref[where, 0:span] = sums[:, span:]
        other_ref[where, span:] = total_ref[where, :]
        return carried

    lax.fori_loop(0, rows // block, sums_block, 0)


def heads_kernel(features, plane, own_ref, other_ref, query_ref, pair_ref, queries, pairs):
    rows = own_ref.shape[0]
    span = 2 * HEAD
    shards = rows // CH_OWN
    layers = shards // plane
    for index in range(shards):
        where = pl.ds(index * CH_OWN, CH_OWN)
        sums = own_ref[where, :] + other_ref[where, :]
        scale = lax.rsqrt(sums[:, span:] * (1.0 / features) + eps)
        shard = (index % layers) * plane + index // layers
        natural = pl.ds(shard, CH_OWN, stride=shards)
        queries[natural, :] = sums[:, :HEAD] * scale
        pairs[natural, :] = sums[:, HEAD:span] * scale
    query_ref[...] = queries[...].astype(jnp.bfloat16)
    pair_ref[...] = pairs[...].astype(jnp.bfloat16)


def attend_kernel(plane, place_ref, query_ref, pair_ref, other_ref, out_ref, keys, values, attended):
    rows = query_ref.shape[0]
    window = out_ref.shape[1]
    block = min(256, rows)
    holds_keys = lax.rem(seat()[0], plane) < plane // 2

    @pl.when(holds_keys)
    def _():
        keys[...] = pair_ref[...]
        values[...] = other_ref[...]

    @pl.when(jnp.logical_not(holds_keys))
    def _():
        keys[...] = other_ref[...]
        values[...] = pair_ref[...]

    score_scale = 1.0 / math.sqrt(HEAD)
    for start in range(0, rows, block):
        stop = start + block
        scores = lax.dot_general(
            query_ref[start:stop, :],
            keys[0:stop, :],
            (((1,), (1,)), ((), ())),
            preferred_element_type=jnp.float32,
        )
        spots = lax.broadcasted_iota(jnp.int32, scores.shape, 1)
        mine = lax.broadcasted_iota(jnp.int32, scores.shape, 0) + start
        scores = jnp.where(spots <= mine, scores * score_scale, masked)
        peak = jnp.max(scores, axis=1, keepdims=True)
        lifted = jnp.exp(scores - peak)
        denominator = jnp.sum(lifted, axis=1, keepdims=True)
        weighted = jnp.dot(
            lifted.astype(jnp.bfloat16), values[0:stop, :], preferred_element_type=jnp.float32
        )
        attended[start:stop, :] = (weighted / denominator).astype(jnp.bfloat16)
    attended[rows:, :] = jnp.zeros((attended.shape[0] - rows, HEAD), jnp.bfloat16)
    for shard in range(out_ref.shape[0]):
        first = place_ref[shard]
        out_ref[shard] = attended[pl.ds(pl.multiple_of(first * TILE, TILE), window), :]


def return_kernel(weight_hbm, pieces_ref, own_ref, other_ref, attended, weight_ref, sems):
    half = own_ref.shape[1]
    lane = seat()[1]
    fetches = []
    for index, which in enumerate((1 - lane, lane)):
        columns = lanes(which, half)
        copy = pltpu.make_async_copy(
            weight_hbm.at[:, columns], weight_ref.at[:, columns], sems.at[index]
        )
        copy.start()
        fetches.append(copy)
    for head in range(pieces_ref.shape[0]):
        attended[:, head * HEAD : (head + 1) * HEAD] = pieces_ref[head]
    fetches[0].wait()
    other_ref[...] = jnp.dot(
        attended[...], weight_ref[:, lanes(1 - lane, half)], preferred_element_type=jnp.float32
    )
    fetches[1].wait()
    own_ref[...] = jnp.dot(
        attended[...], weight_ref[:, lanes(lane, half)], preferred_element_type=jnp.float32
    )


def join_kernel(own_ref, other_ref, encoded_ref, spread_ref, out_ref):
    returned = (own_ref[...] + other_ref[...]).astype(jnp.bfloat16)
    results = jnp.dot(spread_ref[...], returned, preferred_element_type=jnp.float32)
    out_ref[...] = (encoded_ref[...].astype(jnp.float32) + results).astype(jnp.bfloat16)


def one_head_each(
    byte_states,
    outer_gain,
    mamba_input,
    mamba_step,
    decay_rate,
    mixer_weight,
    boundaries,
    span_counts,
    up_weight,
    up_bias,
    inner_gain,
    query_weight,
    key_weight,
    value_weight,
    return_weight,
):
    shards = lax.axis_size("seq")
    me = lax.axis_index("seq")
    lane = lax.axis_index("mp")
    plane = HEADS // KV_HEADS
    layers = shards // plane
    rows_here, width = byte_states.shape
    half = mamba_input.shape[1]
    capacity = boundaries.shape[1]
    window = capacity + TILE
    total_rows = CH_OWN * shards
    inner_width = inner_gain.shape[0]
    inner_half = up_bias.shape[0]
    weight_rows = query_weight.shape[0]
    f32, bf16 = jnp.float32, jnp.bfloat16
    layer, cross = me // plane, me % plane
    layer_groups = [[first + plane * step for step in range(layers)] for first in range(plane)]
    plane_groups = [[first * plane + step for step in range(plane)] for first in range(layers)]

    def over(value, mask):
        return lax.ppermute(value, "seq", [(i, i ^ mask) for i in range(shards)])

    def after(value, done):
        return lax.optimization_barrier((value, done))[0]

    own_gain = lax.dynamic_slice_in_dim(inner_gain, lane * inner_half, inner_half)[None, :]
    seq_ids = jnp.arange(shards, dtype=jnp.int32)
    offsets = jnp.cumsum(span_counts) - span_counts
    own_offset = jnp.sum(jnp.where(seq_ids == me, offsets, 0))
    own_count = jnp.sum(jnp.where(seq_ids == me, span_counts, 0))
    place = offsets // TILE
    own_marks = boundaries[0]
    positions = jnp.arange(rows_here, dtype=jnp.int32)
    spans_here = jnp.arange(capacity, dtype=jnp.int32)
    live = spans_here < own_count
    slots = capacity // shards
    slot_ids = jnp.arange(slots, dtype=jnp.int32)
    local_span = slot_ids[None, :] * shards + ((seq_ids - own_offset) % shards)[:, None]
    is_span = spans_here[None, :] == local_span.reshape(-1)[:, None]
    byte_at = jnp.sum(jnp.where(is_span, jnp.minimum(own_marks, rows_here - 1)[None, :], 0), axis=1)
    pool_pick = (positions[None, :] == byte_at[:, None]).astype(bf16)
    own_spans = me + jnp.arange(CH_OWN, dtype=jnp.int32) * shards
    origin = jnp.sum((offsets[None, :] <= own_spans[:, None]).astype(jnp.int32), axis=1) - 1
    origin_offset = jnp.sum(
        jnp.where(seq_ids[None, :] == origin[:, None], offsets[None, :], 0), axis=1
    )
    arrived_row = origin * slots + (own_spans - origin_offset) // shards
    own_pick = (
        jnp.arange(shards * slots, dtype=jnp.int32)[None, :] == arrived_row[:, None]
    ).astype(bf16)
    passed = jnp.sum(
        ((own_marks[None, :] <= positions[:, None]) & live[None, :]).astype(jnp.int32), axis=1
    )
    result_row = passed - 1 + own_offset % TILE
    spread = (jnp.arange(window, dtype=jnp.int32)[None, :] == result_row[:, None]).astype(bf16)

    up_layers = [up_weight, None] + [over(up_weight, plane * step) for step in range(2, layers)]
    cuts = pl.pallas_call(
        functools.partial(cut_kernel, plane),
        out_shape=(jax.ShapeDtypeStruct((layers, weight_rows, 2 * HEAD), bf16),) * plane,
        in_specs=[in_hbm()] * 3,
        out_specs=(vmem(),) * plane,
        scratch_shapes=[pltpu.SemaphoreType.DMA((2 * shards,))],
        cost_estimate=brief(),
        compiler_params=params(60),
    )(query_weight, key_weight, value_weight)
    pair_planes = [cuts[0]] + [over(cuts[mask], mask) for mask in range(1, plane - 1)] + [None]

    local, through, ends = pl.pallas_call(
        scan_kernel,
        out_shape=(
            jax.ShapeDtypeStruct((rows_here, half), f32),
            jax.ShapeDtypeStruct((rows_here, half), f32),
            jax.ShapeDtypeStruct((shards, 2, half), f32),
        ),
        in_specs=[in_hbm(), vmem(), in_hbm(), in_hbm(), vmem()],
        out_specs=(vmem(),) * 3,
        scratch_shapes=[
            pltpu.VMEM(byte_states.shape, bf16),
            pltpu.VMEM(mamba_input.shape, bf16),
            pltpu.VMEM(mamba_step.shape, bf16),
            pltpu.SemaphoreType.DMA((3,)),
        ],
        cost_estimate=brief(),
        compiler_params=params(62),
    )(byte_states, outer_gain[None, :], mamba_input, mamba_step, decay_rate[None, :])
    up_layers[1] = over(after(up_weight, ends), plane)
    pair_planes[plane - 1] = over(after(cuts[plane - 1], ends), plane - 1)
    ends = lax.all_to_all(ends, "seq", 0, 0, tiled=True)
    ends, up_layers[2:], pair_planes[1 : plane - 1] = lax.optimization_barrier(
        (ends, up_layers[2:], pair_planes[1 : plane - 1])
    )
    states, other_part = pl.pallas_call(
        states_kernel,
        out_shape=(
            jax.ShapeDtypeStruct((rows_here, half), bf16),
            jax.ShapeDtypeStruct((rows_here, half), f32),
        ),
        in_specs=[vmem()] * 4,
        out_specs=(vmem(),) * 2,
        cost_estimate=brief(),
        compiler_params=params(8),
    )(local, through, mixer_weight, ends)
    encoded, leaving = pl.pallas_call(
        pool_kernel,
        out_shape=(
            jax.ShapeDtypeStruct((rows_here, half), bf16),
            jax.ShapeDtypeStruct((shards, slots, half), bf16),
        ),
        in_specs=[vmem()] * 5,
        out_specs=(vmem(),) * 2,
        cost_estimate=brief(),
        compiler_params=params(8),
    )(states, mixer_weight, swapped(other_part), byte_states, pool_pick)
    arrived = lax.all_to_all(leaving, "seq", 0, 0, tiled=True)
    own_rows = pl.pallas_call(
        own_kernel,
        out_shape=jax.ShapeDtypeStruct((layers, CH_OWN, half), bf16),
        in_specs=[vmem()] * 2,
        out_specs=vmem(),
        cost_estimate=brief(),
        compiler_params=params(8),
    )(own_pick, arrived)
    near_layer = lax.all_to_all(
        own_rows, "seq", 0, 0, axis_index_groups=layer_groups, tiled=True
    )
    up_here = pl.pallas_call(
        stack_kernel,
        out_shape=jax.ShapeDtypeStruct((layers, *up_weight.shape), bf16),
        in_specs=[in_place()] * (1 + layers),
        out_specs=vmem(),
        scratch_shapes=[pltpu.SemaphoreType.DMA((layers,))],
        cost_estimate=brief(),
        compiler_params=params(8),
    )(leaving, *up_layers)
    up_beside, up_across = over(up_here, 1), over(up_here, 2)
    pair_layers = pl.pallas_call(
        functools.partial(regroup_kernel, plane),
        out_shape=(jax.ShapeDtypeStruct((plane, weight_rows, 2 * HEAD), bf16),) * layers,
        in_specs=[in_place()] * (1 + plane),
        out_specs=(vmem(),) * layers,
        scratch_shapes=[pltpu.SemaphoreType.DMA((shards,))],
        cost_estimate=brief(),
        compiler_params=params(8),
    )(leaving, *pair_planes)
    mine = [
        over(pair_layers[step] if step == 2 else after(pair_layers[step], own_rows), plane * step)
        if step
        else pair_layers[0]
        for step in range(layers)
    ]
    up_corner = [
        over(up_beside[: layers // 2], 2),
        over(up_across[layers // 2 :], 1),
    ]
    near = lax.all_to_all(
        jnp.broadcast_to(near_layer[None], (plane, layers, CH_OWN, half)),
        "seq",
        0,
        0,
        axis_index_groups=plane_groups,
        tiled=True,
    ).reshape(total_rows, half)

    near, mine[2] = lax.optimization_barrier((near, mine[2]))

    up_pieces = [up_here, up_beside, up_across, *up_corner]
    inner, totals = pl.pallas_call(
        functools.partial(up_kernel, plane),
        out_shape=(
            jax.ShapeDtypeStruct((total_rows, inner_half), bf16),
            jax.ShapeDtypeStruct((total_rows, HEAD), f32),
        ),
        in_specs=[vmem()] * 2 + [in_place()] * (2 + len(up_pieces)),
        out_specs=(vmem(),) * 2,
        scratch_shapes=[
            pltpu.VMEM((total_rows, width), bf16),
            pltpu.VMEM((width, inner_half), bf16),
            pltpu.SemaphoreType.DMA((2 + shards,)),
        ],
        cost_estimate=brief(),
        compiler_params=params(28),
    )(up_bias[None, :], own_gain, near, swapped(near), *up_pieces)
    mine[layers - 1] = after(mine[layers - 1], totals)
    far = [swapped(piece) for piece in mine]
    own_sums, other_sums = pl.pallas_call(
        functools.partial(sums_kernel, plane),
        out_shape=(jax.ShapeDtypeStruct((total_rows, 3 * HEAD), f32),) * 2,
        in_specs=[vmem()] * 2 + [in_place()] * (2 * layers),
        out_specs=(vmem(),) * 2,
        scratch_shapes=[
            pltpu.VMEM((inner_half, 4 * HEAD), bf16),
            pltpu.SemaphoreType.DMA((shards,)),
        ],
        cost_estimate=brief(),
        compiler_params=params(16),
    )(inner, totals, *mine, *far)
    queries, pairs = pl.pallas_call(
        functools.partial(heads_kernel, inner_width, plane),
        out_shape=(jax.ShapeDtypeStruct((total_rows, HEAD), bf16),) * 2,
        in_specs=[vmem()] * 2,
        out_specs=(vmem(),) * 2,
        scratch_shapes=[pltpu.VMEM((total_rows, HEAD), f32)] * 2,
        cost_estimate=brief(),
        compiler_params=params(8),
    )(own_sums, swapped(other_sums))
    leaving = pl.pallas_call(
        functools.partial(attend_kernel, plane),
        out_shape=jax.ShapeDtypeStruct((shards, window, HEAD), bf16),
        in_specs=[smem()] + [vmem()] * 3,
        out_specs=vmem(),
        scratch_shapes=[
            pltpu.VMEM((total_rows, HEAD), bf16),
            pltpu.VMEM((total_rows, HEAD), bf16),
            pltpu.VMEM((total_rows + window, HEAD), bf16),
        ],
        cost_estimate=brief(),
        compiler_params=params(12),
    )(place, queries, pairs, over(pairs, 2))
    pieces = lax.all_to_all(leaving, "seq", 0, 0, tiled=True)
    own_back, other_back = pl.pallas_call(
        return_kernel,
        out_shape=(jax.ShapeDtypeStruct((window, half), f32),) * 2,
        in_specs=[in_hbm(), vmem()],
        out_specs=(vmem(),) * 2,
        scratch_shapes=[
            pltpu.VMEM((window, shards * HEAD), bf16),
            pltpu.VMEM(return_weight.shape, bf16),
            pltpu.SemaphoreType.DMA((2,)),
        ],
        cost_estimate=brief(),
        compiler_params=params(62),
    )(return_weight, pieces)
    return pl.pallas_call(
        join_kernel,
        out_shape=jax.ShapeDtypeStruct((rows_here, half), bf16),
        in_specs=[vmem()] * 4,
        out_specs=vmem(),
        cost_estimate=brief(),
        compiler_params=params(8),
    )(own_back, swapped(other_back), encoded, spread)


def prefix(value, axis, join, neutral):
    count, mine = (lax.axis_size(axis), lax.axis_index(axis))
    pieces = jax.tree.map(lambda part: lax.all_gather(part, axis), value)
    so_far = jax.tree.map(
        lambda part, zero: jnp.full_like(part, 0) + jnp.asarray(zero, part.dtype), value, neutral
    )

    def lap(position, so_far):
        longer = join(so_far, jax.tree.map(lambda part: part[position], pieces))
        return jax.tree.map(lambda new, old: jnp.where(position < mine, new, old), longer, so_far)

    return lax.fori_loop(0, count - 1, lap, so_far)


def rms_scale(values, gain):
    values = values.astype(jnp.float32)
    return values * lax.rsqrt(jnp.mean(values * values, axis=-1, keepdims=True) + eps) * gain


def combine_pairs(earlier, later):
    return (earlier[0] * later[0], later[0] * earlier[1] + later[1])


def pick_table(table, wanted, seq_ids):
    return jnp.sum(jnp.where(seq_ids[None, :] == wanted[:, None], table[None, :], 0), axis=1)


def block_size(piece_rows, shard_rows):
    limit = max(1, 1024 // shard_rows)
    pieces = max(1, piece_rows // shard_rows)
    best_size = 1
    for candidate in range(1, limit + 1):
        if pieces % candidate == 0:
            best_size = candidate
    return min(piece_rows, best_size * shard_rows)


def spread_heads(
    byte_states,
    outer_gain,
    mamba_input,
    mamba_step,
    decay_rate,
    mixer_weight,
    boundaries,
    span_counts,
    up_weight,
    up_bias,
    inner_gain,
    query_weight,
    key_weight,
    value_weight,
    return_weight,
):
    shards = lax.axis_size("seq")
    own_shard = lax.axis_index("seq")
    own_lane = lax.axis_index("mp")
    rows_here = byte_states.shape[0]
    capacity = boundaries.shape[1]
    column_count = mamba_input.shape[1]
    kv_local = key_weight.shape[1] // HEAD
    group_size = HEADS // KV_HEADS
    slot_count = capacity // shards
    offsets = jnp.cumsum(span_counts) - span_counts
    seq_ids = jnp.arange(shards, dtype=jnp.int32)
    own_offset = jnp.sum(jnp.where(seq_ids == own_shard, offsets, 0))
    own_count = jnp.sum(jnp.where(seq_ids == own_shard, span_counts, 0))
    normed = rms_scale(byte_states, outer_gain).astype(jnp.bfloat16)
    inputs = jnp.dot(normed, mamba_input, preferred_element_type=jnp.float32)
    step_sizes = jax.nn.softplus(jnp.dot(normed, mamba_step, preferred_element_type=jnp.float32))
    rate_steps = step_sizes * decay_rate
    decays = jnp.exp(-rate_steps)
    drives = jnp.sqrt(-jnp.expm1(-2.0 * rate_steps)) * inputs
    through, local_states = lax.associative_scan(combine_pairs, (decays, drives), axis=0)
    starting = (jnp.ones((column_count,), jnp.float32), jnp.zeros((column_count,), jnp.float32))
    arriving = prefix((through[-1], local_states[-1]), "seq", combine_pairs, starting)
    states = (local_states + through * arriving[1][None, :]).astype(jnp.bfloat16)
    partial_value = jnp.dot(states, mixer_weight, preferred_element_type=jnp.float32)
    mixed_sum = lax.psum(partial_value, "mp")
    encoded = (byte_states.astype(jnp.float32) + mixed_sum).astype(jnp.bfloat16)
    skip_part = lax.dynamic_slice_in_dim(encoded, own_lane * column_count, column_count, 1)
    own_marks = boundaries[0]
    pooled = encoded[jnp.minimum(own_marks, rows_here - 1)]
    row_width = pooled.shape[1]
    outgoing = jnp.roll(pooled.reshape(slot_count, shards, row_width), own_offset % shards, axis=1)
    incoming = lax.all_to_all(outgoing, "seq", split_axis=1, concat_axis=1, tiled=True)
    position = jnp.arange(CH_OWN, dtype=jnp.int32)
    span_index = own_shard + position * shards
    source = jnp.sum((offsets[None, :] <= span_index[:, None]).astype(jnp.int32), axis=1) - 1
    source_offset = pick_table(offsets, source, seq_ids)
    slot_index = (span_index - source_offset) // shards
    gathered_rows = incoming.reshape(slot_count * shards, row_width)[slot_index * shards + source]
    columns = gathered_rows
    widened_sum = jnp.dot(
        columns,
        lax.all_gather(up_weight, "seq", axis=0, tiled=True),
        preferred_element_type=jnp.float32,
    )
    widened_share = (widened_sum + up_bias[None, :]).astype(jnp.bfloat16)
    widened = lax.all_gather(widened_share, "mp", axis=1, tiled=True)
    inner_normed = rms_scale(widened, inner_gain).astype(jnp.bfloat16)
    columns = inner_normed
    query_part = jnp.dot(
        columns,
        lax.all_gather(query_weight, "seq", axis=0, tiled=True),
        preferred_element_type=jnp.float32,
    )
    key_part = jnp.dot(
        columns,
        lax.all_gather(key_weight, "seq", axis=0, tiled=True),
        preferred_element_type=jnp.float32,
    )
    value_part = jnp.dot(
        columns,
        lax.all_gather(value_weight, "seq", axis=0, tiled=True),
        preferred_element_type=jnp.float32,
    )
    queries = query_part.astype(jnp.bfloat16)
    key_rows = key_part.astype(jnp.bfloat16)
    value_rows = value_part.astype(jnp.bfloat16)
    query_count = queries.shape[0]
    grouped = (
        queries.reshape(query_count, kv_local, group_size, HEAD)
        .transpose(1, 0, 2, 3)
        .reshape(kv_local, query_count * group_size, HEAD)
    )
    row_index = jnp.repeat(span_index, group_size)
    shard_rows = key_rows.shape[0]
    score_scale = 1.0 / math.sqrt(HEAD)

    def key_index(whole_index):
        return whole_index // shard_rows + whole_index % shard_rows * shards

    def attend_block(running, key_block, value_block, index_block):
        row_peak, denominator, weighted = running
        scores = (
            jnp.einsum("hqd,khd->hqk", grouped, key_block, preferred_element_type=jnp.float32)
            * score_scale
        )
        scores = jnp.where(index_block[None, None, :] <= row_index[None, :, None], scores, masked)
        new_peak = jnp.maximum(row_peak, jnp.max(scores, axis=2))
        shrink = jnp.exp(row_peak - new_peak)
        lifted = jnp.exp(scores - new_peak[:, :, None])
        denominator = denominator * shrink + jnp.sum(lifted, axis=2)
        weighted = weighted * shrink[:, :, None] + jnp.einsum(
            "hqk,khd->hqd",
            lifted.astype(jnp.bfloat16),
            value_block,
            preferred_element_type=jnp.float32,
        )
        return (new_peak, denominator, weighted)

    query_total = query_count * group_size
    initial = (
        jnp.full((kv_local, query_total), masked, jnp.float32),
        jnp.zeros((kv_local, query_total), jnp.float32),
        jnp.zeros((kv_local, query_total, HEAD), jnp.float32),
    )
    key_piece = lax.all_gather(key_rows, "seq", axis=0, tiled=True)
    value_piece = lax.all_gather(value_rows, "seq", axis=0, tiled=True)
    piece_rows = key_piece.shape[0]
    block_rows = block_size(piece_rows, shard_rows)
    turn_count = piece_rows // block_rows
    key_blocks = key_piece.reshape(turn_count, block_rows, kv_local, HEAD)
    value_blocks = value_piece.reshape(turn_count, block_rows, kv_local, HEAD)

    def one_turn(turn_index, inner_running):
        whole_index = turn_index * block_rows + jnp.arange(block_rows, dtype=jnp.int32)
        return attend_block(
            inner_running, key_blocks[turn_index], value_blocks[turn_index], key_index(whole_index)
        )

    row_peak, denominator, weighted = lax.fori_loop(0, turn_count, one_turn, initial)
    attended = (weighted / denominator[:, :, None]).astype(jnp.bfloat16)
    attended = (
        attended.reshape(kv_local, query_count, group_size, HEAD)
        .transpose(1, 0, 2, 3)
        .reshape(query_count, kv_local * group_size * HEAD)
    )
    projected = jnp.dot(attended, return_weight, preferred_element_type=jnp.float32)
    returned = lax.psum_scatter(
        projected.astype(jnp.bfloat16), "mp", scatter_dimension=1, tiled=True
    )
    slot_ids = jnp.arange(slot_count, dtype=jnp.int32)
    lead_slot = (own_shard - offsets) % shards
    local_span = slot_ids[:, None] * shards + lead_slot[None, :]
    back_index = (offsets[None, :] + local_span - own_shard) // shards
    alive = local_span < span_counts[None, :]
    back_rows = jnp.where(
        alive[:, :, None],
        returned[jnp.clip(back_index, 0, CH_OWN - 1)],
        jnp.zeros((), jnp.bfloat16),
    )
    arrived = lax.all_to_all(back_rows, "seq", split_axis=1, concat_axis=1, tiled=True)
    span_results = jnp.roll(arrived, -(own_offset % shards), axis=1).reshape(capacity, column_count)
    positions = jnp.arange(rows_here, dtype=jnp.int32)
    live_slots = jnp.arange(capacity, dtype=jnp.int32) < own_count
    passed = jnp.sum(
        ((own_marks[None, :] <= positions[:, None]) & live_slots[None, :]).astype(jnp.int32), axis=1
    )
    return (skip_part.astype(jnp.float32) + span_results[passed - 1].astype(jnp.float32)).astype(
        jnp.bfloat16
    )


def solution(mesh):
    in_specs = (
        P("seq", None),
        P(),
        P(None, "mp"),
        P(None, "mp"),
        P("mp"),
        P("mp", None),
        P("seq", None),
        P(),
        P("seq", "mp"),
        P("mp"),
        P(),
        P("seq", "mp"),
        P("seq", "mp"),
        P("seq", "mp"),
        P("mp", None),
    )
    out_specs = P("seq", "mp")
    def on_device(*arrays):
        heads_here = arrays[11].shape[1] // HEAD
        fits = heads_here == mesh.shape["seq"] and mesh.shape["mp"] == 2
        return (one_head_each if fits else spread_heads)(*arrays)

    return jax.shard_map(
        on_device, mesh=mesh, in_specs=in_specs, out_specs=out_specs, check_vma=False
    )
```

```python
import functools
import math

import jax
import jax.numpy as jnp
from jax import lax
from jax.experimental import pallas as pl
from jax.experimental.pallas import tpu as pltpu
from jax.sharding import PartitionSpec as P

HEADS = 32
KV_HEADS = 8
HEAD = 128
CH_OWN = 64


eps = 1e-05
masked = -1e30
TILE = 16


def swapped(value):
    return lax.ppermute(value, "mp", [(0, 1), (1, 0)])


def vmem():
    return pl.BlockSpec(memory_space=pltpu.VMEM)


def smem():
    return pl.BlockSpec(memory_space=pltpu.SMEM)


def in_place():
    return pl.BlockSpec(memory_space=pl.ANY)


def in_hbm():
    return pl.BlockSpec(memory_space=pltpu.HBM)


def seat():
    return lax.axis_index("seq"), lax.axis_index("mp")


def params(mebibytes=24):
    return pltpu.CompilerParams(vmem_limit_bytes=mebibytes * 2**20)


def brief():
    return pl.CostEstimate(flops=1, bytes_accessed=1, transcendentals=0)


def lanes(which, size):
    return pl.ds(pl.multiple_of(which * size, size), size)


def rows_at(which, size):
    return pl.ds(pl.multiple_of(which * size, size), size)


def start_all(pairs, sems):
    copies = []
    for index, (from_ref, to_ref) in enumerate(pairs):
        copy = pltpu.make_async_copy(from_ref, to_ref, sems.at[index])
        copy.start()
        copies.append(copy)
    return copies


def copy_all(pairs, sems):
    for copy in start_all(pairs, sems):
        copy.wait()


def one_minus_exp(u):
    series = jnp.ones_like(u)
    for order in range(9, 1, -1):
        series = 1.0 - u * (1.0 / order) * series
    return jnp.where(u < 0.5, u * series, 1.0 - jnp.exp(-u))


def softplus(v):
    tail = jnp.exp(-jnp.abs(v))
    series = jnp.ones_like(tail)
    for order in range(6, 1, -1):
        series = 1.0 - tail * ((order - 1.0) / order) * series
    return jnp.maximum(v, 0.0) + jnp.where(tail < 0.03, tail * series, jnp.log(1.0 + tail))


def start_cuts(plane, query_ref, key_ref, value_ref, outs, sems):
    layers = outs[0].shape[0]
    cross = lax.rem(seat()[0], plane)
    copies = []
    for mask in range(plane):
        for layer in range(layers):
            column = lanes(layer * plane + (cross ^ mask), HEAD)
            copies.append(
                pltpu.make_async_copy(
                    query_ref.at[:, column],
                    outs[mask].at[layer, :, pl.ds(0, HEAD)],
                    sems.at[len(copies)],
                )
            )
    for copy in copies:
        copy.start()

    def pair_copies(here_ref, there_ref):
        pairs = []
        for mask in range(plane):
            from_ref = here_ref if mask < plane // 2 else there_ref
            for layer in range(layers):
                pairs.append(
                    pltpu.make_async_copy(
                        from_ref.at[:, pl.ds(layer * HEAD, HEAD)],
                        outs[mask].at[layer, :, pl.ds(HEAD, HEAD)],
                        sems.at[len(copies) + len(pairs)],
                    )
                )
        return pairs

    with_keys = pair_copies(key_ref, value_ref)
    with_values = pair_copies(value_ref, key_ref)

    @pl.when(cross < plane // 2)
    def _():
        for copy in with_keys:
            copy.start()

    @pl.when(cross >= plane // 2)
    def _():
        for copy in with_values:
            copy.start()

    return copies + with_keys


def scan_kernel(plane, *refs):
    bytes_hbm, gain_ref, input_hbm, step_hbm, rate_ref, query_hbm, key_hbm, value_hbm = refs[:8]
    local_ref, through_ref, ends_ref = refs[8:11]
    cut_refs, refs = refs[11 : 11 + plane], refs[11 + plane :]
    bytes_ref, input_ref, step_ref, query_ref, key_ref, value_ref, sems, cut_sems = refs
    fetches = []
    for index, pair in enumerate(
        (
            (bytes_hbm, bytes_ref),
            (step_hbm, step_ref),
            (input_hbm, input_ref),
            (query_hbm, query_ref),
            (key_hbm, key_ref),
            (value_hbm, value_ref),
        )
    ):
        fetches.append(pltpu.make_async_copy(*pair, sems.at[index]))
        fetches[-1].start()
    fetches[0].wait()
    values = bytes_ref[...].astype(jnp.float32)
    scale = lax.rsqrt(jnp.mean(values * values, axis=1, keepdims=True) + eps)
    normed = (values * scale * gain_ref[...]).astype(jnp.bfloat16)
    fetches[1].wait()
    steps = softplus(jnp.dot(normed, step_ref[...], preferred_element_type=jnp.float32))
    rate_steps = steps * rate_ref[...]
    fetches[2].wait()
    inputs = jnp.dot(normed, input_ref[...], preferred_element_type=jnp.float32)
    for fetch in fetches[3:]:
        fetch.wait()
    cuts = start_cuts(plane, query_ref, key_ref, value_ref, cut_refs, cut_sems)
    decays = jnp.exp(-rate_steps)
    drives = jnp.sqrt(one_minus_exp(2.0 * rate_steps)) * inputs
    rows, width = decays.shape
    tile = 8
    decays = decays.reshape(rows // tile, tile, width)
    drives = drives.reshape(rows // tile, tile, width)
    place = lax.broadcasted_iota(jnp.int32, decays.shape, 1)
    for reach in (1, 2, 4):
        before_decays = pltpu.roll(decays, reach, 1)
        before_drives = pltpu.roll(drives, reach, 1)
        inside = place >= reach
        drives = jnp.where(inside, decays * before_drives + drives, drives)
        decays = jnp.where(inside, decays * before_decays, decays)
    state = jnp.zeros((1, width), jnp.float32)
    kept = jnp.ones((1, width), jnp.float32)
    for index in range(rows // tile):
        states = decays[index] * state + drives[index]
        passing = decays[index] * kept
        local_ref[pl.ds(index * tile, tile), :] = states
        through_ref[pl.ds(index * tile, tile), :] = passing
        state = states[tile - 1 :, :]
        kept = passing[tile - 1 :, :]
    for index in range(ends_ref.shape[0]):
        ends_ref[index, 0:1, :] = kept
        ends_ref[index, 1:2, :] = state
    for cut in cuts:
        cut.wait()


def states_kernel(local_ref, through_ref, mixer_ref, ends_ref, states_ref, other_ref):
    me, lane = seat()
    carry = jnp.zeros((1, local_ref.shape[1]), jnp.float32)
    for shard in range(ends_ref.shape[0]):
        later = ends_ref[shard, 0:1, :] * carry + ends_ref[shard, 1:2, :]
        carry = jnp.where(shard < me, later, carry)
    states = (local_ref[...] + through_ref[...] * carry).astype(jnp.bfloat16)
    states_ref[...] = states
    half = other_ref.shape[1]
    other_ref[...] = jnp.dot(
        states, mixer_ref[:, lanes(1 - lane, half)], preferred_element_type=jnp.float32
    )


def pool_kernel(plane, *refs):
    states_ref, mixer_ref, other_ref, bytes_ref, pick_ref = refs[:5]
    layers = (len(refs) - 5 - plane - 4) // 2
    pieces, refs = refs[5 : 5 + plane], refs[5 + plane :]
    up_pieces, refs = refs[:layers], refs[layers:]
    encoded_ref, out_ref, up_ref, *pair_refs, sems = refs
    layer = seat()[0] // plane
    pairs = [(piece, up_ref.at[step]) for step, piece in enumerate(up_pieces)]
    for step, pair_ref in enumerate(pair_refs):
        for mask in range(plane):
            pairs.append((pieces[mask].at[layer ^ step], pair_ref.at[mask]))
    copies = start_all(pairs, sems)
    half = other_ref.shape[1]
    columns = lanes(seat()[1], half)
    mixed = jnp.dot(states_ref[...], mixer_ref[:, columns], preferred_element_type=jnp.float32)
    skip = bytes_ref[:, columns].astype(jnp.float32)
    encoded = (skip + (mixed + other_ref[...])).astype(jnp.bfloat16)
    encoded_ref[...] = encoded
    picked = jnp.dot(pick_ref[...], encoded, preferred_element_type=jnp.float32)
    out_ref[...] = picked.astype(jnp.bfloat16).reshape(out_ref.shape)
    for copy in copies:
        copy.wait()


def own_kernel(pick_ref, arrived_ref, out_ref):
    shards, slots, half = arrived_ref.shape
    rows = arrived_ref[...].astype(jnp.float32).reshape(shards * slots, half)
    own = jnp.dot(
        pick_ref[...], rows.astype(jnp.bfloat16), preferred_element_type=jnp.float32
    ).astype(jnp.bfloat16)
    for index in range(out_ref.shape[0]):
        out_ref[index] = own


def up_kernel(plane, bias_ref, gain_ref, near_ref, far_ref, *rest):
    up_pieces, rest = rest[: plane + 1], rest[plane + 1 :]
    inner_ref, total_ref, pooled, up, sems = rest
    me, lane = seat()
    layer, cross = me // plane, lax.rem(me, plane)
    half = near_ref.shape[1]
    up_rows = up_pieces[0].shape[1]
    rows = inner_ref.shape[0]
    pairs = [
        (near_ref, pooled.at[:, lanes(lane, half)]),
        (far_ref, pooled.at[:, lanes(1 - lane, half)]),
    ]
    layers = up_pieces[0].shape[0]
    for mask in range(plane):
        for step in range(layers):
            shard = (layer ^ step) * plane + (cross ^ mask)
            piece = up_pieces[mask].at[step]
            if mask == plane - 1:
                piece = up_pieces[mask + step // (layers // 2)].at[step % (layers // 2)]
            pairs.append((piece, up.at[rows_at(shard, up_rows), :]))
    copy_all(pairs, sems)
    block = min(256, rows)
    part = min(1024, up.shape[1])

    def up_block(index, carried):
        where = rows_at(index, block)
        left = pooled[where, :]
        total = jnp.zeros((block, 1), jnp.float32)
        for start in range(0, up.shape[1], part):
            columns = pl.ds(start, part)
            widened = jnp.dot(left, up[:, columns], preferred_element_type=jnp.float32)
            widened = (widened + bias_ref[:, columns]).astype(jnp.bfloat16).astype(jnp.float32)
            inner_ref[where, columns] = (widened * gain_ref[:, columns]).astype(jnp.bfloat16)
            total = total + jnp.sum(widened * widened, axis=1, keepdims=True)
        total_ref[where, :] = jnp.broadcast_to(total, (block, HEAD))
        return carried

    lax.fori_loop(0, rows // block, up_block, 0)


def sums_kernel(plane, inner_ref, total_ref, *rest):
    layers = (len(rest) - 4) // 2
    mine, far = rest[:layers], rest[layers : 2 * layers]
    own_ref, other_ref, weights, sems = rest[2 * layers :]
    me, lane = seat()
    layer, cross = me // plane, lax.rem(me, plane)
    piece_rows = mine[0].shape[1]
    rows = inner_ref.shape[0]
    span = 2 * HEAD
    keep = layers // 2

    def pairs_from(first):
        pairs = []
        for head, pieces in enumerate((mine, far)):
            for step in range(keep):
                for mask in range(plane):
                    shard = (lax.rem(layer, keep) ^ step) * plane + (cross ^ mask)
                    to_ref = weights.at[rows_at(shard, piece_rows), pl.ds(head * span, span)]
                    pairs.append((pieces[first + step].at[mask], to_ref))
        return pairs

    low_is_own = layer // keep == lane

    @pl.when(low_is_own)
    def _():
        copy_all(pairs_from(0), sems)

    @pl.when(jnp.logical_not(low_is_own))
    def _():
        copy_all(pairs_from(keep), sems)

    block = min(256, rows)

    def sums_block(index, carried):
        where = rows_at(index, block)
        sums = jnp.dot(inner_ref[where, :], weights[...], preferred_element_type=jnp.float32)
        own_ref[where, 0:span] = sums[:, :span]
        own_ref[where, span:] = total_ref[where, :]
        other_ref[where, 0:span] = sums[:, span:]
        other_ref[where, span:] = total_ref[where, :]
        return carried

    lax.fori_loop(0, rows // block, sums_block, 0)


def heads_kernel(features, plane, own_ref, other_ref, query_ref, pair_ref, queries, pairs):
    rows = own_ref.shape[0]
    span = 2 * HEAD
    shards = rows // CH_OWN
    layers = shards // plane
    for index in range(shards):
        where = pl.ds(index * CH_OWN, CH_OWN)
        sums = own_ref[where, :] + other_ref[where, :]
        scale = lax.rsqrt(sums[:, span:] * (1.0 / features) + eps)
        shard = (index % layers) * plane + index // layers
        natural = pl.ds(shard, CH_OWN, stride=shards)
        queries[natural, :] = sums[:, :HEAD] * scale
        pairs[natural, :] = sums[:, HEAD:span] * scale
    query_ref[...] = queries[...].astype(jnp.bfloat16)
    pair_ref[...] = pairs[...].astype(jnp.bfloat16)


def attend_kernel(plane, place_ref, query_ref, pair_ref, other_ref, out_ref, keys, values, attended):
    rows = query_ref.shape[0]
    window = out_ref.shape[1]
    block = min(256, rows)
    holds_keys = lax.rem(seat()[0], plane) < plane // 2

    @pl.when(holds_keys)
    def _():
        keys[...] = pair_ref[...]
        values[...] = other_ref[...]

    @pl.when(jnp.logical_not(holds_keys))
    def _():
        keys[...] = other_ref[...]
        values[...] = pair_ref[...]

    score_scale = 1.0 / math.sqrt(HEAD)
    for start in range(0, rows, block):
        stop = start + block
        scores = lax.dot_general(
            query_ref[start:stop, :],
            keys[0:stop, :],
            (((1,), (1,)), ((), ())),
            preferred_element_type=jnp.float32,
        )
        spots = lax.broadcasted_iota(jnp.int32, scores.shape, 1)
        mine = lax.broadcasted_iota(jnp.int32, scores.shape, 0) + start
        scores = jnp.where(spots <= mine, scores * score_scale, masked)
        peak = jnp.max(scores, axis=1, keepdims=True)
        lifted = jnp.exp(scores - peak)
        denominator = jnp.sum(lifted, axis=1, keepdims=True)
        weighted = jnp.dot(
            lifted.astype(jnp.bfloat16), values[0:stop, :], preferred_element_type=jnp.float32
        )
        attended[start:stop, :] = (weighted / denominator).astype(jnp.bfloat16)
    attended[rows:, :] = jnp.zeros((attended.shape[0] - rows, HEAD), jnp.bfloat16)
    for shard in range(out_ref.shape[0]):
        first = place_ref[shard]
        out_ref[shard] = attended[pl.ds(pl.multiple_of(first * TILE, TILE), window), :]


def return_kernel(weight_ref, pieces_ref, own_ref, other_ref, attended):
    half = own_ref.shape[1]
    lane = seat()[1]
    for head in range(pieces_ref.shape[0]):
        attended[:, head * HEAD : (head + 1) * HEAD] = pieces_ref[head]
    other_ref[...] = jnp.dot(
        attended[...], weight_ref[:, lanes(1 - lane, half)], preferred_element_type=jnp.float32
    )
    own_ref[...] = jnp.dot(
        attended[...], weight_ref[:, lanes(lane, half)], preferred_element_type=jnp.float32
    )


def join_kernel(own_ref, other_ref, encoded_ref, spread_ref, out_ref):
    returned = (own_ref[...] + other_ref[...]).astype(jnp.bfloat16)
    results = jnp.dot(spread_ref[...], returned, preferred_element_type=jnp.float32)
    out_ref[...] = (encoded_ref[...].astype(jnp.float32) + results).astype(jnp.bfloat16)


def one_head_each(
    byte_states,
    outer_gain,
    mamba_input,
    mamba_step,
    decay_rate,
    mixer_weight,
    boundaries,
    span_counts,
    up_weight,
    up_bias,
    inner_gain,
    query_weight,
    key_weight,
    value_weight,
    return_weight,
):
    shards = lax.axis_size("seq")
    me = lax.axis_index("seq")
    lane = lax.axis_index("mp")
    plane = HEADS // KV_HEADS
    layers = shards // plane
    rows_here, width = byte_states.shape
    half = mamba_input.shape[1]
    capacity = boundaries.shape[1]
    window = capacity + TILE
    total_rows = CH_OWN * shards
    inner_width = inner_gain.shape[0]
    inner_half = up_bias.shape[0]
    weight_rows = query_weight.shape[0]
    f32, bf16 = jnp.float32, jnp.bfloat16
    layer, cross = me // plane, me % plane
    layer_groups = [[first + plane * step for step in range(layers)] for first in range(plane)]
    plane_groups = [[first * plane + step for step in range(plane)] for first in range(layers)]

    def over(value, mask):
        return lax.ppermute(value, "seq", [(i, i ^ mask) for i in range(shards)])

    def after(value, done):
        return lax.optimization_barrier((value, done))[0]

    own_gain = lax.dynamic_slice_in_dim(inner_gain, lane * inner_half, inner_half)[None, :]
    seq_ids = jnp.arange(shards, dtype=jnp.int32)
    offsets = jnp.cumsum(span_counts) - span_counts
    own_offset = jnp.sum(jnp.where(seq_ids == me, offsets, 0))
    own_count = jnp.sum(jnp.where(seq_ids == me, span_counts, 0))
    place = offsets // TILE
    own_marks = boundaries[0]
    positions = jnp.arange(rows_here, dtype=jnp.int32)
    spans_here = jnp.arange(capacity, dtype=jnp.int32)
    live = spans_here < own_count
    slots = capacity // shards
    slot_ids = jnp.arange(slots, dtype=jnp.int32)
    local_span = slot_ids[None, :] * shards + ((seq_ids - own_offset) % shards)[:, None]
    is_span = spans_here[None, :] == local_span.reshape(-1)[:, None]
    byte_at = jnp.sum(jnp.where(is_span, jnp.minimum(own_marks, rows_here - 1)[None, :], 0), axis=1)
    pool_pick = (positions[None, :] == byte_at[:, None]).astype(bf16)
    own_spans = me + jnp.arange(CH_OWN, dtype=jnp.int32) * shards
    origin = jnp.sum((offsets[None, :] <= own_spans[:, None]).astype(jnp.int32), axis=1) - 1
    origin_offset = jnp.sum(
        jnp.where(seq_ids[None, :] == origin[:, None], offsets[None, :], 0), axis=1
    )
    arrived_row = origin * slots + (own_spans - origin_offset) // shards
    own_pick = (
        jnp.arange(shards * slots, dtype=jnp.int32)[None, :] == arrived_row[:, None]
    ).astype(bf16)
    passed = jnp.sum(
        ((own_marks[None, :] <= positions[:, None]) & live[None, :]).astype(jnp.int32), axis=1
    )
    result_row = passed - 1 + own_offset % TILE
    spread = (jnp.arange(window, dtype=jnp.int32)[None, :] == result_row[:, None]).astype(bf16)

    up_layers = [up_weight, None] + [over(up_weight, plane * step) for step in range(2, layers)]

    cut_shape = (layers, weight_rows, 2 * HEAD)
    local, through, ends, *cuts = pl.pallas_call(
        functools.partial(scan_kernel, plane),
        out_shape=(
            jax.ShapeDtypeStruct((rows_here, half), f32),
            jax.ShapeDtypeStruct((rows_here, half), f32),
            jax.ShapeDtypeStruct((shards, 2, half), f32),
        )
        + (jax.ShapeDtypeStruct(cut_shape, bf16),) * plane,
        in_specs=[in_hbm(), vmem(), in_hbm(), in_hbm(), vmem()] + [in_hbm()] * 3,
        out_specs=(vmem(),) * 3 + (in_place(),) * plane,
        scratch_shapes=[
            pltpu.VMEM(array.shape, bf16)
            for array in (
                byte_states, mamba_input, mamba_step, query_weight, key_weight, value_weight
            )
        ]
        + [pltpu.SemaphoreType.DMA((6,)), pltpu.SemaphoreType.DMA((2 * shards,))],
        cost_estimate=brief(),
        compiler_params=params(62),
    )(
        byte_states,
        outer_gain[None, :],
        mamba_input,
        mamba_step,
        decay_rate[None, :],
        query_weight,
        key_weight,
        value_weight,
    )
    pair_planes = [cuts[0]] + [over(cuts[mask], mask) for mask in range(1, plane - 1)] + [None]
    up_layers[1] = over(after(up_weight, ends), plane)
    pair_planes[plane - 1] = over(after(cuts[plane - 1], ends), plane - 1)
    ends = lax.all_to_all(ends, "seq", 0, 0, tiled=True)
    ends, up_layers[2:], pair_planes[1 : plane - 1] = lax.optimization_barrier(
        (ends, up_layers[2:], pair_planes[1 : plane - 1])
    )
    states, other_part = pl.pallas_call(
        states_kernel,
        out_shape=(
            jax.ShapeDtypeStruct((rows_here, half), bf16),
            jax.ShapeDtypeStruct((rows_here, half), f32),
        ),
        in_specs=[vmem()] * 4,
        out_specs=(vmem(),) * 2,
        cost_estimate=brief(),
        compiler_params=params(8),
    )(local, through, mixer_weight, ends)
    encoded, leaving, up_here, *pair_layers = pl.pallas_call(
        functools.partial(pool_kernel, plane),
        out_shape=(
            jax.ShapeDtypeStruct((rows_here, half), bf16),
            jax.ShapeDtypeStruct((shards, slots, half), bf16),
            jax.ShapeDtypeStruct((layers, *up_weight.shape), bf16),
        )
        + (jax.ShapeDtypeStruct((plane, weight_rows, 2 * HEAD), bf16),) * layers,
        in_specs=[vmem()] * 5 + [in_place()] * (plane + layers),
        out_specs=(vmem(),) * (3 + layers),
        scratch_shapes=[pltpu.SemaphoreType.DMA((layers + shards,))],
        cost_estimate=brief(),
        compiler_params=params(16),
    )(
        states,
        mixer_weight,
        swapped(other_part),
        byte_states,
        pool_pick,
        *pair_planes,
        *up_layers,
    )
    arrived = lax.all_to_all(leaving, "seq", 0, 0, tiled=True)
    up_beside, up_across = over(up_here, 1), over(up_here, 2)
    mine = [pair_layers[0], None, over(pair_layers[2], 2 * plane), None]
    own_rows = pl.pallas_call(
        own_kernel,
        out_shape=jax.ShapeDtypeStruct((layers, CH_OWN, half), bf16),
        in_specs=[vmem()] * 2,
        out_specs=vmem(),
        cost_estimate=brief(),
        compiler_params=params(8),
    )(own_pick, arrived)
    own_rows, up_beside, up_across, mine[2] = lax.optimization_barrier(
        (own_rows, up_beside, up_across, mine[2])
    )
    near_layer = lax.all_to_all(
        own_rows, "seq", 0, 0, axis_index_groups=layer_groups, tiled=True
    )
    for step in (1, 3):
        mine[step] = over(after(pair_layers[step], own_rows), plane * step)
    up_corner = [over(up_beside[: layers // 2], 2), over(up_across[layers // 2 :], 1)]
    near_layer, up_corner = lax.optimization_barrier((near_layer, up_corner))
    near = lax.all_to_all(
        jnp.broadcast_to(near_layer[None], (plane, layers, CH_OWN, half)),
        "seq",
        0,
        0,
        axis_index_groups=plane_groups,
        tiled=True,
    ).reshape(total_rows, half)
    near, mine = lax.optimization_barrier((near, mine))

    up_pieces = [up_here, up_beside, up_across, *up_corner]
    inner, totals = pl.pallas_call(
        functools.partial(up_kernel, plane),
        out_shape=(
            jax.ShapeDtypeStruct((total_rows, inner_half), bf16),
            jax.ShapeDtypeStruct((total_rows, HEAD), f32),
        ),
        in_specs=[vmem()] * 2 + [in_place()] * (2 + len(up_pieces)),
        out_specs=(vmem(),) * 2,
        scratch_shapes=[
            pltpu.VMEM((total_rows, width), bf16),
            pltpu.VMEM((width, inner_half), bf16),
            pltpu.SemaphoreType.DMA((2 + shards,)),
        ],
        cost_estimate=brief(),
        compiler_params=params(28),
    )(up_bias[None, :], own_gain, near, swapped(near), *up_pieces)
    far = [swapped(piece) for piece in mine]
    own_sums, other_sums = pl.pallas_call(
        functools.partial(sums_kernel, plane),
        out_shape=(jax.ShapeDtypeStruct((total_rows, 3 * HEAD), f32),) * 2,
        in_specs=[vmem()] * 2 + [in_place()] * (2 * layers),
        out_specs=(vmem(),) * 2,
        scratch_shapes=[
            pltpu.VMEM((inner_half, 4 * HEAD), bf16),
            pltpu.SemaphoreType.DMA((shards,)),
        ],
        cost_estimate=brief(),
        compiler_params=params(16),
    )(inner, totals, *mine, *far)
    queries, pairs = pl.pallas_call(
        functools.partial(heads_kernel, inner_width, plane),
        out_shape=(jax.ShapeDtypeStruct((total_rows, HEAD), bf16),) * 2,
        in_specs=[vmem()] * 2,
        out_specs=(vmem(),) * 2,
        scratch_shapes=[pltpu.VMEM((total_rows, HEAD), f32)] * 2,
        cost_estimate=brief(),
        compiler_params=params(8),
    )(own_sums, swapped(other_sums))
    leaving = pl.pallas_call(
        functools.partial(attend_kernel, plane),
        out_shape=jax.ShapeDtypeStruct((shards, window, HEAD), bf16),
        in_specs=[smem()] + [vmem()] * 3,
        out_specs=vmem(),
        scratch_shapes=[
            pltpu.VMEM((total_rows, HEAD), bf16),
            pltpu.VMEM((total_rows, HEAD), bf16),
            pltpu.VMEM((total_rows + window, HEAD), bf16),
        ],
        cost_estimate=brief(),
        compiler_params=params(12),
    )(place, queries, pairs, over(pairs, 2))
    pieces = lax.all_to_all(leaving, "seq", 0, 0, tiled=True)
    own_back, other_back = pl.pallas_call(
        return_kernel,
        out_shape=(jax.ShapeDtypeStruct((window, half), f32),) * 2,
        in_specs=[vmem()] * 2,
        out_specs=(vmem(),) * 2,
        scratch_shapes=[pltpu.VMEM((window, shards * HEAD), bf16)],
        cost_estimate=brief(),
        compiler_params=params(12),
    )(return_weight, pieces)
    return pl.pallas_call(
        join_kernel,
        out_shape=jax.ShapeDtypeStruct((rows_here, half), bf16),
        in_specs=[vmem()] * 4,
        out_specs=vmem(),
        cost_estimate=brief(),
        compiler_params=params(8),
    )(own_back, swapped(other_back), encoded, spread)


def prefix(value, axis, join, neutral):
    count, mine = (lax.axis_size(axis), lax.axis_index(axis))
    pieces = jax.tree.map(lambda part: lax.all_gather(part, axis), value)
    so_far = jax.tree.map(
        lambda part, zero: jnp.full_like(part, 0) + jnp.asarray(zero, part.dtype), value, neutral
    )

    def lap(position, so_far):
        longer = join(so_far, jax.tree.map(lambda part: part[position], pieces))
        return jax.tree.map(lambda new, old: jnp.where(position < mine, new, old), longer, so_far)

    return lax.fori_loop(0, count - 1, lap, so_far)


def rms_scale(values, gain):
    values = values.astype(jnp.float32)
    return values * lax.rsqrt(jnp.mean(values * values, axis=-1, keepdims=True) + eps) * gain


def combine_pairs(earlier, later):
    return (earlier[0] * later[0], later[0] * earlier[1] + later[1])


def pick_table(table, wanted, seq_ids):
    return jnp.sum(jnp.where(seq_ids[None, :] == wanted[:, None], table[None, :], 0), axis=1)


def block_size(piece_rows, shard_rows):
    limit = max(1, 1024 // shard_rows)
    pieces = max(1, piece_rows // shard_rows)
    best_size = 1
    for candidate in range(1, limit + 1):
        if pieces % candidate == 0:
            best_size = candidate
    return min(piece_rows, best_size * shard_rows)


def spread_heads(
    byte_states,
    outer_gain,
    mamba_input,
    mamba_step,
    decay_rate,
    mixer_weight,
    boundaries,
    span_counts,
    up_weight,
    up_bias,
    inner_gain,
    query_weight,
    key_weight,
    value_weight,
    return_weight,
):
    shards = lax.axis_size("seq")
    own_shard = lax.axis_index("seq")
    own_lane = lax.axis_index("mp")
    rows_here = byte_states.shape[0]
    capacity = boundaries.shape[1]
    column_count = mamba_input.shape[1]
    kv_local = key_weight.shape[1] // HEAD
    group_size = HEADS // KV_HEADS
    slot_count = capacity // shards
    offsets = jnp.cumsum(span_counts) - span_counts
    seq_ids = jnp.arange(shards, dtype=jnp.int32)
    own_offset = jnp.sum(jnp.where(seq_ids == own_shard, offsets, 0))
    own_count = jnp.sum(jnp.where(seq_ids == own_shard, span_counts, 0))
    normed = rms_scale(byte_states, outer_gain).astype(jnp.bfloat16)
    inputs = jnp.dot(normed, mamba_input, preferred_element_type=jnp.float32)
    step_sizes = jax.nn.softplus(jnp.dot(normed, mamba_step, preferred_element_type=jnp.float32))
    rate_steps = step_sizes * decay_rate
    decays = jnp.exp(-rate_steps)
    drives = jnp.sqrt(-jnp.expm1(-2.0 * rate_steps)) * inputs
    through, local_states = lax.associative_scan(combine_pairs, (decays, drives), axis=0)
    starting = (jnp.ones((column_count,), jnp.float32), jnp.zeros((column_count,), jnp.float32))
    arriving = prefix((through[-1], local_states[-1]), "seq", combine_pairs, starting)
    states = (local_states + through * arriving[1][None, :]).astype(jnp.bfloat16)
    partial_value = jnp.dot(states, mixer_weight, preferred_element_type=jnp.float32)
    mixed_sum = lax.psum(partial_value, "mp")
    encoded = (byte_states.astype(jnp.float32) + mixed_sum).astype(jnp.bfloat16)
    skip_part = lax.dynamic_slice_in_dim(encoded, own_lane * column_count, column_count, 1)
    own_marks = boundaries[0]
    pooled = encoded[jnp.minimum(own_marks, rows_here - 1)]
    row_width = pooled.shape[1]
    outgoing = jnp.roll(pooled.reshape(slot_count, shards, row_width), own_offset % shards, axis=1)
    incoming = lax.all_to_all(outgoing, "seq", split_axis=1, concat_axis=1, tiled=True)
    position = jnp.arange(CH_OWN, dtype=jnp.int32)
    span_index = own_shard + position * shards
    source = jnp.sum((offsets[None, :] <= span_index[:, None]).astype(jnp.int32), axis=1) - 1
    source_offset = pick_table(offsets, source, seq_ids)
    slot_index = (span_index - source_offset) // shards
    gathered_rows = incoming.reshape(slot_count * shards, row_width)[slot_index * shards + source]
    columns = gathered_rows
    widened_sum = jnp.dot(
        columns,
        lax.all_gather(up_weight, "seq", axis=0, tiled=True),
        preferred_element_type=jnp.float32,
    )
    widened_share = (widened_sum + up_bias[None, :]).astype(jnp.bfloat16)
    widened = lax.all_gather(widened_share, "mp", axis=1, tiled=True)
    inner_normed = rms_scale(widened, inner_gain).astype(jnp.bfloat16)
    columns = inner_normed
    query_part = jnp.dot(
        columns,
        lax.all_gather(query_weight, "seq", axis=0, tiled=True),
        preferred_element_type=jnp.float32,
    )
    key_part = jnp.dot(
        columns,
        lax.all_gather(key_weight, "seq", axis=0, tiled=True),
        preferred_element_type=jnp.float32,
    )
    value_part = jnp.dot(
        columns,
        lax.all_gather(value_weight, "seq", axis=0, tiled=True),
        preferred_element_type=jnp.float32,
    )
    queries = query_part.astype(jnp.bfloat16)
    key_rows = key_part.astype(jnp.bfloat16)
    value_rows = value_part.astype(jnp.bfloat16)
    query_count = queries.shape[0]
    grouped = (
        queries.reshape(query_count, kv_local, group_size, HEAD)
        .transpose(1, 0, 2, 3)
        .reshape(kv_local, query_count * group_size, HEAD)
    )
    row_index = jnp.repeat(span_index, group_size)
    shard_rows = key_rows.shape[0]
    score_scale = 1.0 / math.sqrt(HEAD)

    def key_index(whole_index):
        return whole_index // shard_rows + whole_index % shard_rows * shards

    def attend_block(running, key_block, value_block, index_block):
        row_peak, denominator, weighted = running
        scores = (
            jnp.einsum("hqd,khd->hqk", grouped, key_block, preferred_element_type=jnp.float32)
            * score_scale
        )
        scores = jnp.where(index_block[None, None, :] <= row_index[None, :, None], scores, masked)
        new_peak = jnp.maximum(row_peak, jnp.max(scores, axis=2))
        shrink = jnp.exp(row_peak - new_peak)
        lifted = jnp.exp(scores - new_peak[:, :, None])
        denominator = denominator * shrink + jnp.sum(lifted, axis=2)
        weighted = weighted * shrink[:, :, None] + jnp.einsum(
            "hqk,khd->hqd",
            lifted.astype(jnp.bfloat16),
            value_block,
            preferred_element_type=jnp.float32,
        )
        return (new_peak, denominator, weighted)

    query_total = query_count * group_size
    initial = (
        jnp.full((kv_local, query_total), masked, jnp.float32),
        jnp.zeros((kv_local, query_total), jnp.float32),
        jnp.zeros((kv_local, query_total, HEAD), jnp.float32),
    )
    key_piece = lax.all_gather(key_rows, "seq", axis=0, tiled=True)
    value_piece = lax.all_gather(value_rows, "seq", axis=0, tiled=True)
    piece_rows = key_piece.shape[0]
    block_rows = block_size(piece_rows, shard_rows)
    turn_count = piece_rows // block_rows
    key_blocks = key_piece.reshape(turn_count, block_rows, kv_local, HEAD)
    value_blocks = value_piece.reshape(turn_count, block_rows, kv_local, HEAD)

    def one_turn(turn_index, inner_running):
        whole_index = turn_index * block_rows + jnp.arange(block_rows, dtype=jnp.int32)
        return attend_block(
            inner_running, key_blocks[turn_index], value_blocks[turn_index], key_index(whole_index)
        )

    row_peak, denominator, weighted = lax.fori_loop(0, turn_count, one_turn, initial)
    attended = (weighted / denominator[:, :, None]).astype(jnp.bfloat16)
    attended = (
        attended.reshape(kv_local, query_count, group_size, HEAD)
        .transpose(1, 0, 2, 3)
        .reshape(query_count, kv_local * group_size * HEAD)
    )
    projected = jnp.dot(attended, return_weight, preferred_element_type=jnp.float32)
    returned = lax.psum_scatter(
        projected.astype(jnp.bfloat16), "mp", scatter_dimension=1, tiled=True
    )
    slot_ids = jnp.arange(slot_count, dtype=jnp.int32)
    lead_slot = (own_shard - offsets) % shards
    local_span = slot_ids[:, None] * shards + lead_slot[None, :]
    back_index = (offsets[None, :] + local_span - own_shard) // shards
    alive = local_span < span_counts[None, :]
    back_rows = jnp.where(
        alive[:, :, None],
        returned[jnp.clip(back_index, 0, CH_OWN - 1)],
        jnp.zeros((), jnp.bfloat16),
    )
    arrived = lax.all_to_all(back_rows, "seq", split_axis=1, concat_axis=1, tiled=True)
    span_results = jnp.roll(arrived, -(own_offset % shards), axis=1).reshape(capacity, column_count)
    positions = jnp.arange(rows_here, dtype=jnp.int32)
    live_slots = jnp.arange(capacity, dtype=jnp.int32) < own_count
    passed = jnp.sum(
        ((own_marks[None, :] <= positions[:, None]) & live_slots[None, :]).astype(jnp.int32), axis=1
    )
    return (skip_part.astype(jnp.float32) + span_results[passed - 1].astype(jnp.float32)).astype(
        jnp.bfloat16
    )


def solution(mesh):
    in_specs = (
        P("seq", None),
        P(),
        P(None, "mp"),
        P(None, "mp"),
        P("mp"),
        P("mp", None),
        P("seq", None),
        P(),
        P("seq", "mp"),
        P("mp"),
        P(),
        P("seq", "mp"),
        P("seq", "mp"),
        P("seq", "mp"),
        P("mp", None),
    )
    out_specs = P("seq", "mp")
    def on_device(*arrays):
        heads_here = arrays[11].shape[1] // HEAD
        fits = heads_here == mesh.shape["seq"] and mesh.shape["mp"] == 2
        return (one_head_each if fits else spread_heads)(*arrays)

    return jax.shard_map(
        on_device, mesh=mesh, in_specs=in_specs, out_specs=out_specs, check_vma=False
    )
```

```python
import functools
import math

import jax
import jax.numpy as jnp
from jax import lax
from jax.experimental import pallas as pl
from jax.experimental.pallas import tpu as pltpu
from jax.sharding import PartitionSpec as P

HEADS = 32
KV_HEADS = 8
HEAD = 128
CH_OWN = 64


eps = 1e-05
masked = -1e30
TILE = 16


def swapped(value):
    return lax.ppermute(value, "mp", [(0, 1), (1, 0)])


def vmem():
    return pl.BlockSpec(memory_space=pltpu.VMEM)


def smem():
    return pl.BlockSpec(memory_space=pltpu.SMEM)


def in_place():
    return pl.BlockSpec(memory_space=pl.ANY)


def in_hbm():
    return pl.BlockSpec(memory_space=pltpu.HBM)


def seat():
    return lax.axis_index("seq"), lax.axis_index("mp")


def params(mebibytes=24):
    return pltpu.CompilerParams(vmem_limit_bytes=mebibytes * 2**20)


def brief():
    return pl.CostEstimate(flops=1, bytes_accessed=1, transcendentals=0)


def lanes(which, size):
    return pl.ds(pl.multiple_of(which * size, size), size)


def rows_at(which, size):
    return pl.ds(pl.multiple_of(which * size, size), size)


def start_all(pairs, sems):
    copies = []
    for index, (from_ref, to_ref) in enumerate(pairs):
        copy = pltpu.make_async_copy(from_ref, to_ref, sems.at[index])
        copy.start()
        copies.append(copy)
    return copies


def copy_all(pairs, sems):
    for copy in start_all(pairs, sems):
        copy.wait()


def one_minus_exp(u):
    series = jnp.ones_like(u)
    for order in range(9, 1, -1):
        series = 1.0 - u * (1.0 / order) * series
    return jnp.where(u < 0.5, u * series, 1.0 - jnp.exp(-u))


def softplus(v):
    tail = jnp.exp(-jnp.abs(v))
    series = jnp.ones_like(tail)
    for order in range(6, 1, -1):
        series = 1.0 - tail * ((order - 1.0) / order) * series
    return jnp.maximum(v, 0.0) + jnp.where(tail < 0.03, tail * series, jnp.log(1.0 + tail))


def start_cuts(plane, query_ref, key_ref, value_ref, up_ref, pair_outs, up_outs, sems):
    layers = len(pair_outs)
    me, _ = seat()
    layer, cross = me // plane, lax.rem(me, plane)
    group = plane * HEAD
    pairs = []
    for step, out_ref in enumerate(pair_outs):
        target = layer ^ step
        pairs.append((query_ref.at[:, lanes(target, group)], out_ref.at[:, pl.ds(0, group)]))
        pairs.append((key_ref.at[:, lanes(target, HEAD)], out_ref.at[:, pl.ds(group, HEAD)]))
        pairs.append(
            (value_ref.at[:, lanes(target, HEAD)], out_ref.at[:, pl.ds(group + HEAD, HEAD)])
        )
    for mask, out_ref in enumerate(up_outs):
        size = 2 * out_ref.shape[1] // layers
        for step in range(layers // 2):
            from_ref = up_ref.at[:, lanes(step * plane + (cross ^ mask), size)]
            pairs.append((from_ref, out_ref.at[:, pl.ds(step * size, size)]))
    return start_all(pairs, sems)


def scan_kernel(plane, layers, *refs):
    bytes_hbm, gain_ref, input_hbm, step_hbm, rate_ref = refs[:5]
    others, refs = refs[5:9], refs[9:]
    local_ref, through_ref, ends_ref = refs[:3]
    pair_outs, refs = refs[3 : 3 + layers], refs[3 + layers :]
    up_outs, refs = refs[:plane], refs[plane:]
    bytes_ref, input_ref, step_ref, *held, sems, cut_sems = refs
    fetches = start_all(
        [(bytes_hbm, bytes_ref), (step_hbm, step_ref), (input_hbm, input_ref), *zip(others, held)],
        sems,
    )
    fetches[0].wait()
    values = bytes_ref[...].astype(jnp.float32)
    scale = lax.rsqrt(jnp.mean(values * values, axis=1, keepdims=True) + eps)
    normed = (values * scale * gain_ref[...]).astype(jnp.bfloat16)
    fetches[1].wait()
    steps = softplus(jnp.dot(normed, step_ref[...], preferred_element_type=jnp.float32))
    rate_steps = steps * rate_ref[...]
    fetches[2].wait()
    inputs = jnp.dot(normed, input_ref[...], preferred_element_type=jnp.float32)
    for fetch in fetches[3:]:
        fetch.wait()
    cuts = start_cuts(plane, *held, pair_outs, up_outs, cut_sems)
    decays = jnp.exp(-rate_steps)
    drives = jnp.sqrt(one_minus_exp(2.0 * rate_steps)) * inputs
    rows, width = decays.shape
    tile = 8
    decays = decays.reshape(rows // tile, tile, width)
    drives = drives.reshape(rows // tile, tile, width)
    place = lax.broadcasted_iota(jnp.int32, decays.shape, 1)
    for reach in (1, 2, 4):
        before_decays = pltpu.roll(decays, reach, 1)
        before_drives = pltpu.roll(drives, reach, 1)
        inside = place >= reach
        drives = jnp.where(inside, decays * before_drives + drives, drives)
        decays = jnp.where(inside, decays * before_decays, decays)
    state = jnp.zeros((1, width), jnp.float32)
    kept = jnp.ones((1, width), jnp.float32)
    for index in range(rows // tile):
        states = decays[index] * state + drives[index]
        passing = decays[index] * kept
        local_ref[pl.ds(index * tile, tile), :] = states
        through_ref[pl.ds(index * tile, tile), :] = passing
        state = states[tile - 1 :, :]
        kept = passing[tile - 1 :, :]
    for index in range(ends_ref.shape[0]):
        ends_ref[index, 0:1, :] = kept
        ends_ref[index, 1:2, :] = state
    for cut in cuts:
        cut.wait()


def states_kernel(local_ref, through_ref, mixer_ref, ends_ref, states_ref, other_ref):
    me, lane = seat()
    carry = jnp.zeros((1, local_ref.shape[1]), jnp.float32)
    for shard in range(ends_ref.shape[0]):
        later = ends_ref[shard, 0:1, :] * carry + ends_ref[shard, 1:2, :]
        carry = jnp.where(shard < me, later, carry)
    states = (local_ref[...] + through_ref[...] * carry).astype(jnp.bfloat16)
    states_ref[...] = states
    half = other_ref.shape[1]
    other_ref[...] = jnp.dot(
        states, mixer_ref[:, lanes(1 - lane, half)], preferred_element_type=jnp.float32
    )


def pool_kernel(plane, *refs):
    states_ref, mixer_ref, other_ref, bytes_ref, pick_ref = refs[:5]
    up_pieces, (encoded_ref, out_ref, up_ref, sems) = refs[5 : 5 + plane], refs[5 + plane :]
    copies = start_all([(piece, up_ref.at[mask]) for mask, piece in enumerate(up_pieces)], sems)
    half = other_ref.shape[1]
    columns = lanes(seat()[1], half)
    mixed = jnp.dot(states_ref[...], mixer_ref[:, columns], preferred_element_type=jnp.float32)
    skip = bytes_ref[:, columns].astype(jnp.float32)
    encoded = (skip + (mixed + other_ref[...])).astype(jnp.bfloat16)
    encoded_ref[...] = encoded
    picked = jnp.dot(pick_ref[...], encoded, preferred_element_type=jnp.float32)
    out_ref[...] = picked.astype(jnp.bfloat16).reshape(out_ref.shape)
    for copy in copies:
        copy.wait()


def own_kernel(pick_ref, arrived_ref, out_ref):
    shards, slots, half = arrived_ref.shape
    rows = arrived_ref[...].astype(jnp.float32).reshape(shards * slots, half)
    own = jnp.dot(
        pick_ref[...], rows.astype(jnp.bfloat16), preferred_element_type=jnp.float32
    ).astype(jnp.bfloat16)
    for index in range(out_ref.shape[0]):
        out_ref[index] = own


def inner_kernel(plane, layers, bias_ref, gain_ref, near_ref, far_ref, *refs):
    up_own, refs = refs[:layers], refs[layers:]
    up_far, refs = refs[:layers], refs[layers:]
    pieces, refs = refs[:layers], refs[layers:]
    out_ref, pooled, up, weights, squares, sems = refs
    me, lane = seat()
    layer, cross = me // plane, lax.rem(me, plane)
    half = near_ref.shape[1]
    up_rows, up_half = up_own[0].shape[1:]
    pairs = [
        (near_ref, pooled.at[:, lanes(lane, half)]),
        (far_ref, pooled.at[:, lanes(1 - lane, half)]),
    ]
    for step in range(layers):
        for mask in range(plane):
            where = rows_at((layer ^ step) * plane + (cross ^ mask), up_rows)
            pairs.append((up_own[step].at[mask], up.at[where, lanes(lane, up_half)]))
            pairs.append((up_far[step].at[mask], up.at[where, lanes(1 - lane, up_half)]))
    for step, piece in enumerate(pieces):
        pairs.append((piece, weights.at[rows_at(layer ^ step, piece.shape[0]), :]))
    copies = start_all(pairs, sems)
    for copy in copies[:-layers]:
        copy.wait()
    rows = pooled.shape[0]
    block = rows // plane
    ones = jnp.ones((8, up.shape[1]), jnp.bfloat16)
    for index in range(plane):
        where = pl.ds(index * block, block)
        widened = jnp.dot(pooled[where, :], up[...], preferred_element_type=jnp.float32)
        widened = (widened + bias_ref[...]).astype(jnp.bfloat16).astype(jnp.float32)
        inner = (widened * gain_ref[...]).astype(jnp.bfloat16)
        square = widened * widened
        coarse = square.astype(jnp.bfloat16)
        fine = (square - coarse.astype(jnp.float32)).astype(jnp.bfloat16)
        squares[:, where] = sum(
            lax.dot_general(
                ones, part, (((1,), (1,)), ((), ())), preferred_element_type=jnp.float32
            )
            for part in (coarse, fine)
        )
        if index == 0:
            for copy in copies[-layers:]:
                copy.wait()
        sums = jnp.dot(inner, weights[...], preferred_element_type=jnp.float32)
        sums = sums.astype(jnp.bfloat16)
        for head in range(plane):
            out_ref[head, where, :] = sums[:, head * HEAD : (head + 1) * HEAD]
        for number in range(2):
            start = (plane + number) * HEAD
            out_ref[index, pl.ds(rows + number * block, block), :] = sums[:, start : start + HEAD]
    total = jnp.concatenate(
        [squares[0:1, start : start + HEAD] for start in range(0, rows, HEAD)], axis=0
    )
    coarse = total.astype(jnp.bfloat16).astype(jnp.float32)
    both = jnp.concatenate([coarse, total - coarse], axis=0).astype(jnp.bfloat16)
    for index in range(plane):
        out_ref[index, pl.ds(rows + 2 * block, both.shape[0]), :] = both


def heads_kernel(features, got_ref, query_ref, pair_ref, queries):
    plane = got_ref.shape[0]
    rows = query_ref.shape[0]
    block = rows // plane
    lines = rows // HEAD
    shards = rows // CH_OWN
    layers = shards // plane
    first = rows + 2 * block

    def added(start, size):
        parts = [got_ref[index, start : start + size, :].astype(jnp.float32) for index in range(plane)]
        return sum(parts[1:], parts[0])

    both = added(first, 2 * lines)
    total = both[:lines, :] + both[lines:, :]
    scale = jnp.transpose(lax.rsqrt(total * (1.0 / features) + eps))
    for line in range(lines):
        scaled = added(line * HEAD, HEAD) * scale[:, line : line + 1]
        for start in range(0, HEAD, CH_OWN):
            index = (line * HEAD + start) // CH_OWN
            shard = (index % layers) * plane + index // layers
            queries[pl.ds(shard, CH_OWN, stride=shards), :] = scaled[start : start + CH_OWN, :]
    query_ref[...] = queries[...].astype(jnp.bfloat16)
    cross = lax.rem(seat()[0], plane)
    per_block = block // HEAD
    for line in range(per_block):
        mine = scale[:, line : line + 1]
        for index in range(1, plane):
            column = index * per_block + line
            mine = jnp.where(cross == index, scale[:, column : column + 1], mine)
        for number in range(2):
            start = number * block + line * HEAD
            pair = (added(rows + start, HEAD) * mine).astype(jnp.bfloat16)
            for index in range(plane):
                pair_ref[index, pl.ds(start, HEAD), :] = pair


def attend_kernel(place_ref, query_ref, pair_ref, out_ref, natural, keys, values, attended):
    rows = query_ref.shape[0]
    window = out_ref.shape[1]
    plane = pair_ref.shape[0]
    part = rows // plane
    shards = rows // CH_OWN
    layers = shards // plane
    for number, held in enumerate((keys, values)):
        for cross in range(plane):
            for layer in range(layers):
                piece = pair_ref[cross, pl.ds(number * part + layer * CH_OWN, CH_OWN), :]
                where = pl.ds(layer * plane + cross, CH_OWN, stride=shards)
                natural[where, :] = piece.astype(jnp.float32)
        held[...] = natural[...].astype(jnp.bfloat16)
    block = min(256, rows)
    score_scale = 1.0 / math.sqrt(HEAD)
    for start in range(0, rows, block):
        stop = start + block
        scores = lax.dot_general(
            query_ref[start:stop, :],
            keys[0:stop, :],
            (((1,), (1,)), ((), ())),
            preferred_element_type=jnp.float32,
        )
        spots = lax.broadcasted_iota(jnp.int32, scores.shape, 1)
        mine = lax.broadcasted_iota(jnp.int32, scores.shape, 0) + start
        scores = jnp.where(spots <= mine, scores * score_scale, masked)
        peak = jnp.max(scores, axis=1, keepdims=True)
        lifted = jnp.exp(scores - peak)
        denominator = jnp.sum(lifted, axis=1, keepdims=True)
        weighted = jnp.dot(
            lifted.astype(jnp.bfloat16), values[0:stop, :], preferred_element_type=jnp.float32
        )
        attended[start:stop, :] = (weighted / denominator).astype(jnp.bfloat16)
    attended[rows:, :] = jnp.zeros((attended.shape[0] - rows, HEAD), jnp.bfloat16)
    for shard in range(out_ref.shape[0]):
        first = place_ref[shard]
        out_ref[shard] = attended[pl.ds(pl.multiple_of(first * TILE, TILE), window), :]


def return_kernel(weight_ref, pieces_ref, own_ref, other_ref, attended):
    half = own_ref.shape[1]
    lane = seat()[1]
    for head in range(pieces_ref.shape[0]):
        attended[:, head * HEAD : (head + 1) * HEAD] = pieces_ref[head]
    other_ref[...] = jnp.dot(
        attended[...], weight_ref[:, lanes(1 - lane, half)], preferred_element_type=jnp.float32
    )
    own_ref[...] = jnp.dot(
        attended[...], weight_ref[:, lanes(lane, half)], preferred_element_type=jnp.float32
    )


def join_kernel(own_ref, other_ref, encoded_ref, spread_ref, out_ref):
    returned = (own_ref[...] + other_ref[...]).astype(jnp.bfloat16)
    results = jnp.dot(spread_ref[...], returned, preferred_element_type=jnp.float32)
    out_ref[...] = (encoded_ref[...].astype(jnp.float32) + results).astype(jnp.bfloat16)


def one_head_each(
    byte_states,
    outer_gain,
    mamba_input,
    mamba_step,
    decay_rate,
    mixer_weight,
    boundaries,
    span_counts,
    up_weight,
    up_bias,
    inner_gain,
    query_weight,
    key_weight,
    value_weight,
    return_weight,
):
    shards = lax.axis_size("seq")
    me = lax.axis_index("seq")
    lane = lax.axis_index("mp")
    plane = HEADS // KV_HEADS
    layers = shards // plane
    rows_here, width = byte_states.shape
    half = mamba_input.shape[1]
    capacity = boundaries.shape[1]
    window = capacity + TILE
    total_rows = CH_OWN * shards
    inner_width = inner_gain.shape[0]
    inner_half = up_bias.shape[0]
    weight_rows = query_weight.shape[0]
    f32, bf16 = jnp.float32, jnp.bfloat16
    layer, cross = me // plane, me % plane
    layer_groups = [[first + plane * step for step in range(layers)] for first in range(plane)]
    plane_groups = [[first * plane + step for step in range(plane)] for first in range(layers)]

    def over(value, mask):
        return lax.ppermute(value, "seq", [(i, i ^ mask) for i in range(shards)])

    def after(value, done):
        return lax.optimization_barrier((value, done))[0]

    own_bias = up_bias.reshape(layers // 2, plane, weight_rows)
    own_bias = lax.dynamic_index_in_dim(own_bias, cross, 1, keepdims=False).reshape(1, -1)
    own_gain = inner_gain.reshape(layers, plane, weight_rows)
    own_gain = lax.dynamic_index_in_dim(own_gain, cross, 1, keepdims=False).reshape(1, -1)

    seq_ids = jnp.arange(shards, dtype=jnp.int32)
    offsets = jnp.cumsum(span_counts) - span_counts
    own_offset = jnp.sum(jnp.where(seq_ids == me, offsets, 0))
    own_count = jnp.sum(jnp.where(seq_ids == me, span_counts, 0))
    place = offsets // TILE
    own_marks = boundaries[0]
    positions = jnp.arange(rows_here, dtype=jnp.int32)
    spans_here = jnp.arange(capacity, dtype=jnp.int32)
    live = spans_here < own_count
    slots = capacity // shards
    slot_ids = jnp.arange(slots, dtype=jnp.int32)
    local_span = slot_ids[None, :] * shards + ((seq_ids - own_offset) % shards)[:, None]
    is_span = spans_here[None, :] == local_span.reshape(-1)[:, None]
    byte_at = jnp.sum(jnp.where(is_span, jnp.minimum(own_marks, rows_here - 1)[None, :], 0), axis=1)
    pool_pick = (positions[None, :] == byte_at[:, None]).astype(bf16)
    own_spans = me + jnp.arange(CH_OWN, dtype=jnp.int32) * shards
    origin = jnp.sum((offsets[None, :] <= own_spans[:, None]).astype(jnp.int32), axis=1) - 1
    origin_offset = jnp.sum(
        jnp.where(seq_ids[None, :] == origin[:, None], offsets[None, :], 0), axis=1
    )
    arrived_row = origin * slots + (own_spans - origin_offset) // shards
    own_pick = (
        jnp.arange(shards * slots, dtype=jnp.int32)[None, :] == arrived_row[:, None]
    ).astype(bf16)
    passed = jnp.sum(
        ((own_marks[None, :] <= positions[:, None]) & live[None, :]).astype(jnp.int32), axis=1
    )
    result_row = passed - 1 + own_offset % TILE
    spread = (jnp.arange(window, dtype=jnp.int32)[None, :] == result_row[:, None]).astype(bf16)

    up_half = inner_half // plane
    local, through, ends, *cuts = pl.pallas_call(
        functools.partial(scan_kernel, plane, layers),
        out_shape=(
            jax.ShapeDtypeStruct((rows_here, half), f32),
            jax.ShapeDtypeStruct((rows_here, half), f32),
            jax.ShapeDtypeStruct((shards, 2, half), f32),
        )
        + (jax.ShapeDtypeStruct((weight_rows, (plane + 2) * HEAD), bf16),) * layers
        + (jax.ShapeDtypeStruct((up_weight.shape[0], up_half), bf16),) * plane,
        in_specs=[in_hbm(), vmem(), in_hbm(), in_hbm(), vmem()] + [in_hbm()] * 4,
        out_specs=(vmem(),) * 3 + (in_place(),) * (layers + plane),
        scratch_shapes=[
            pltpu.VMEM(array.shape, bf16)
            for array in (
                byte_states,
                mamba_input,
                mamba_step,
                query_weight,
                key_weight,
                value_weight,
                up_weight,
            )
        ]
        + [
            pltpu.SemaphoreType.DMA((7,)),
            pltpu.SemaphoreType.DMA((3 * layers + plane * layers // 2,)),
        ],
        cost_estimate=brief(),
        compiler_params=params(62),
    )(
        byte_states,
        outer_gain[None, :],
        mamba_input,
        mamba_step,
        decay_rate[None, :],
        query_weight,
        key_weight,
        value_weight,
        up_weight,
    )
    pair_cuts, up_cuts = cuts[:layers], cuts[layers:]
    ends = lax.all_to_all(ends, "seq", 0, 0, tiled=True)
    up_parts = [up_cuts[0]] + [over(up_cuts[mask], mask) for mask in range(1, plane)]
    pieces = [pair_cuts[0], None, over(pair_cuts[2], 2 * plane), None]
    states, other_part = pl.pallas_call(
        states_kernel,
        out_shape=(
            jax.ShapeDtypeStruct((rows_here, half), bf16),
            jax.ShapeDtypeStruct((rows_here, half), f32),
        ),
        in_specs=[vmem()] * 4,
        out_specs=(vmem(),) * 2,
        cost_estimate=brief(),
        compiler_params=params(8),
    )(local, through, mixer_weight, ends)
    far_part, up_parts, pieces[2] = lax.optimization_barrier(
        (swapped(other_part), up_parts, pieces[2])
    )
    encoded, leaving, up_here = pl.pallas_call(
        functools.partial(pool_kernel, plane),
        out_shape=(
            jax.ShapeDtypeStruct((rows_here, half), bf16),
            jax.ShapeDtypeStruct((shards, slots, half), bf16),
            jax.ShapeDtypeStruct((plane, up_weight.shape[0], up_half), bf16),
        ),
        in_specs=[vmem()] * 5 + [in_place()] * plane,
        out_specs=(vmem(),) * 3,
        scratch_shapes=[pltpu.SemaphoreType.DMA((plane,))],
        cost_estimate=brief(),
        compiler_params=params(10),
    )(states, mixer_weight, far_part, byte_states, pool_pick, *up_parts)
    arrived = lax.all_to_all(leaving, "seq", 0, 0, tiled=True)
    for step in (1, 3):
        pieces[step] = over(after(pair_cuts[step], leaving), plane * step)
    arrived, pieces = lax.optimization_barrier((arrived, pieces))
    own_rows = pl.pallas_call(
        own_kernel,
        out_shape=jax.ShapeDtypeStruct((layers, CH_OWN, half), bf16),
        in_specs=[vmem()] * 2,
        out_specs=vmem(),
        cost_estimate=brief(),
        compiler_params=params(8),
    )(own_pick, arrived)
    near_layer = lax.all_to_all(
        own_rows, "seq", 0, 0, axis_index_groups=layer_groups, tiled=True
    )
    up_behind = after(up_here, own_rows)
    up_own = [up_here] + [over(up_behind, plane * step) for step in range(1, layers)]
    near = lax.all_to_all(
        jnp.broadcast_to(near_layer[None], (plane, layers, CH_OWN, half)),
        "seq",
        0,
        0,
        axis_index_groups=plane_groups,
        tiled=True,
    ).reshape(total_rows, half)
    near, up_own = lax.optimization_barrier((near, up_own))
    up_far = [swapped(piece) for piece in up_own]
    far_bias = swapped(own_bias)
    bias = jnp.where(
        lane == 0,
        jnp.concatenate([own_bias, far_bias], axis=1),
        jnp.concatenate([far_bias, own_bias], axis=1),
    )

    features = own_gain.shape[1]
    block = total_rows // plane
    sent_rows = total_rows + 2 * block + 2 * (total_rows // HEAD)
    partial_sums = pl.pallas_call(
        functools.partial(inner_kernel, plane, layers),
        out_shape=jax.ShapeDtypeStruct((plane, sent_rows, HEAD), bf16),
        in_specs=[vmem()] * 2 + [in_place()] * (2 + 3 * layers),
        out_specs=vmem(),
        scratch_shapes=[
            pltpu.VMEM((total_rows, width), bf16),
            pltpu.VMEM((width, features), bf16),
            pltpu.VMEM((features, (plane + 2) * HEAD), bf16),
            pltpu.VMEM((8, total_rows), f32),
            pltpu.SemaphoreType.DMA((2 + 2 * shards + layers,)),
        ],
        cost_estimate=brief(),
        compiler_params=params(28),
    )(bias, own_gain, near, swapped(near), *up_own, *up_far, *pieces)
    got = lax.all_to_all(
        partial_sums, "seq", 0, 0, axis_index_groups=plane_groups, tiled=True
    )
    queries, pairs = pl.pallas_call(
        functools.partial(heads_kernel, inner_width),
        out_shape=(
            jax.ShapeDtypeStruct((total_rows, HEAD), bf16),
            jax.ShapeDtypeStruct((plane, 2 * block, HEAD), bf16),
        ),
        in_specs=[vmem()],
        out_specs=(vmem(),) * 2,
        scratch_shapes=[pltpu.VMEM((total_rows, HEAD), f32)],
        cost_estimate=brief(),
        compiler_params=params(10),
    )(got)
    pairs = lax.all_to_all(pairs, "seq", 0, 0, axis_index_groups=plane_groups, tiled=True)
    leaving = pl.pallas_call(
        attend_kernel,
        out_shape=jax.ShapeDtypeStruct((shards, window, HEAD), bf16),
        in_specs=[smem()] + [vmem()] * 2,
        out_specs=vmem(),
        scratch_shapes=[
            pltpu.VMEM((total_rows, HEAD), f32),
            pltpu.VMEM((total_rows, HEAD), bf16),
            pltpu.VMEM((total_rows, HEAD), bf16),
            pltpu.VMEM((total_rows + window, HEAD), bf16),
        ],
        cost_estimate=brief(),
        compiler_params=params(12),
    )(place, queries, pairs)
    pieces = lax.all_to_all(leaving, "seq", 0, 0, tiled=True)
    own_back, other_back = pl.pallas_call(
        return_kernel,
        out_shape=(jax.ShapeDtypeStruct((window, half), f32),) * 2,
        in_specs=[vmem()] * 2,
        out_specs=(vmem(),) * 2,
        scratch_shapes=[pltpu.VMEM((window, shards * HEAD), bf16)],
        cost_estimate=brief(),
        compiler_params=params(12),
    )(return_weight, pieces)
    return pl.pallas_call(
        join_kernel,
        out_shape=jax.ShapeDtypeStruct((rows_here, half), bf16),
        in_specs=[vmem()] * 4,
        out_specs=vmem(),
        cost_estimate=brief(),
        compiler_params=params(8),
    )(own_back, swapped(other_back), encoded, spread)


def prefix(value, axis, join, neutral):
    count, mine = (lax.axis_size(axis), lax.axis_index(axis))
    pieces = jax.tree.map(lambda part: lax.all_gather(part, axis), value)
    so_far = jax.tree.map(
        lambda part, zero: jnp.full_like(part, 0) + jnp.asarray(zero, part.dtype), value, neutral
    )

    def lap(position, so_far):
        longer = join(so_far, jax.tree.map(lambda part: part[position], pieces))
        return jax.tree.map(lambda new, old: jnp.where(position < mine, new, old), longer, so_far)

    return lax.fori_loop(0, count - 1, lap, so_far)


def rms_scale(values, gain):
    values = values.astype(jnp.float32)
    return values * lax.rsqrt(jnp.mean(values * values, axis=-1, keepdims=True) + eps) * gain


def combine_pairs(earlier, later):
    return (earlier[0] * later[0], later[0] * earlier[1] + later[1])


def pick_table(table, wanted, seq_ids):
    return jnp.sum(jnp.where(seq_ids[None, :] == wanted[:, None], table[None, :], 0), axis=1)


def block_size(piece_rows, shard_rows):
    limit = max(1, 1024 // shard_rows)
    pieces = max(1, piece_rows // shard_rows)
    best_size = 1
    for candidate in range(1, limit + 1):
        if pieces % candidate == 0:
            best_size = candidate
    return min(piece_rows, best_size * shard_rows)


def spread_heads(
    byte_states,
    outer_gain,
    mamba_input,
    mamba_step,
    decay_rate,
    mixer_weight,
    boundaries,
    span_counts,
    up_weight,
    up_bias,
    inner_gain,
    query_weight,
    key_weight,
    value_weight,
    return_weight,
):
    shards = lax.axis_size("seq")
    own_shard = lax.axis_index("seq")
    own_lane = lax.axis_index("mp")
    rows_here = byte_states.shape[0]
    capacity = boundaries.shape[1]
    column_count = mamba_input.shape[1]
    kv_local = key_weight.shape[1] // HEAD
    group_size = HEADS // KV_HEADS
    slot_count = capacity // shards
    offsets = jnp.cumsum(span_counts) - span_counts
    seq_ids = jnp.arange(shards, dtype=jnp.int32)
    own_offset = jnp.sum(jnp.where(seq_ids == own_shard, offsets, 0))
    own_count = jnp.sum(jnp.where(seq_ids == own_shard, span_counts, 0))
    normed = rms_scale(byte_states, outer_gain).astype(jnp.bfloat16)
    inputs = jnp.dot(normed, mamba_input, preferred_element_type=jnp.float32)
    step_sizes = jax.nn.softplus(jnp.dot(normed, mamba_step, preferred_element_type=jnp.float32))
    rate_steps = step_sizes * decay_rate
    decays = jnp.exp(-rate_steps)
    drives = jnp.sqrt(-jnp.expm1(-2.0 * rate_steps)) * inputs
    through, local_states = lax.associative_scan(combine_pairs, (decays, drives), axis=0)
    starting = (jnp.ones((column_count,), jnp.float32), jnp.zeros((column_count,), jnp.float32))
    arriving = prefix((through[-1], local_states[-1]), "seq", combine_pairs, starting)
    states = (local_states + through * arriving[1][None, :]).astype(jnp.bfloat16)
    partial_value = jnp.dot(states, mixer_weight, preferred_element_type=jnp.float32)
    mixed_sum = lax.psum(partial_value, "mp")
    encoded = (byte_states.astype(jnp.float32) + mixed_sum).astype(jnp.bfloat16)
    skip_part = lax.dynamic_slice_in_dim(encoded, own_lane * column_count, column_count, 1)
    own_marks = boundaries[0]
    pooled = encoded[jnp.minimum(own_marks, rows_here - 1)]
    row_width = pooled.shape[1]
    outgoing = jnp.roll(pooled.reshape(slot_count, shards, row_width), own_offset % shards, axis=1)
    incoming = lax.all_to_all(outgoing, "seq", split_axis=1, concat_axis=1, tiled=True)
    position = jnp.arange(CH_OWN, dtype=jnp.int32)
    span_index = own_shard + position * shards
    source = jnp.sum((offsets[None, :] <= span_index[:, None]).astype(jnp.int32), axis=1) - 1
    source_offset = pick_table(offsets, source, seq_ids)
    slot_index = (span_index - source_offset) // shards
    gathered_rows = incoming.reshape(slot_count * shards, row_width)[slot_index * shards + source]
    columns = gathered_rows
    widened_sum = jnp.dot(
        columns,
        lax.all_gather(up_weight, "seq", axis=0, tiled=True),
        preferred_element_type=jnp.float32,
    )
    widened_share = (widened_sum + up_bias[None, :]).astype(jnp.bfloat16)
    widened = lax.all_gather(widened_share, "mp", axis=1, tiled=True)
    inner_normed = rms_scale(widened, inner_gain).astype(jnp.bfloat16)
    columns = inner_normed
    query_part = jnp.dot(
        columns,
        lax.all_gather(query_weight, "seq", axis=0, tiled=True),
        preferred_element_type=jnp.float32,
    )
    key_part = jnp.dot(
        columns,
        lax.all_gather(key_weight, "seq", axis=0, tiled=True),
        preferred_element_type=jnp.float32,
    )
    value_part = jnp.dot(
        columns,
        lax.all_gather(value_weight, "seq", axis=0, tiled=True),
        preferred_element_type=jnp.float32,
    )
    queries = query_part.astype(jnp.bfloat16)
    key_rows = key_part.astype(jnp.bfloat16)
    value_rows = value_part.astype(jnp.bfloat16)
    query_count = queries.shape[0]
    grouped = (
        queries.reshape(query_count, kv_local, group_size, HEAD)
        .transpose(1, 0, 2, 3)
        .reshape(kv_local, query_count * group_size, HEAD)
    )
    row_index = jnp.repeat(span_index, group_size)
    shard_rows = key_rows.shape[0]
    score_scale = 1.0 / math.sqrt(HEAD)

    def key_index(whole_index):
        return whole_index // shard_rows + whole_index % shard_rows * shards

    def attend_block(running, key_block, value_block, index_block):
        row_peak, denominator, weighted = running
        scores = (
            jnp.einsum("hqd,khd->hqk", grouped, key_block, preferred_element_type=jnp.float32)
            * score_scale
        )
        scores = jnp.where(index_block[None, None, :] <= row_index[None, :, None], scores, masked)
        new_peak = jnp.maximum(row_peak, jnp.max(scores, axis=2))
        shrink = jnp.exp(row_peak - new_peak)
        lifted = jnp.exp(scores - new_peak[:, :, None])
        denominator = denominator * shrink + jnp.sum(lifted, axis=2)
        weighted = weighted * shrink[:, :, None] + jnp.einsum(
            "hqk,khd->hqd",
            lifted.astype(jnp.bfloat16),
            value_block,
            preferred_element_type=jnp.float32,
        )
        return (new_peak, denominator, weighted)

    query_total = query_count * group_size
    initial = (
        jnp.full((kv_local, query_total), masked, jnp.float32),
        jnp.zeros((kv_local, query_total), jnp.float32),
        jnp.zeros((kv_local, query_total, HEAD), jnp.float32),
    )
    key_piece = lax.all_gather(key_rows, "seq", axis=0, tiled=True)
    value_piece = lax.all_gather(value_rows, "seq", axis=0, tiled=True)
    piece_rows = key_piece.shape[0]
    block_rows = block_size(piece_rows, shard_rows)
    turn_count = piece_rows // block_rows
    key_blocks = key_piece.reshape(turn_count, block_rows, kv_local, HEAD)
    value_blocks = value_piece.reshape(turn_count, block_rows, kv_local, HEAD)

    def one_turn(turn_index, inner_running):
        whole_index = turn_index * block_rows + jnp.arange(block_rows, dtype=jnp.int32)
        return attend_block(
            inner_running, key_blocks[turn_index], value_blocks[turn_index], key_index(whole_index)
        )

    row_peak, denominator, weighted = lax.fori_loop(0, turn_count, one_turn, initial)
    attended = (weighted / denominator[:, :, None]).astype(jnp.bfloat16)
    attended = (
        attended.reshape(kv_local, query_count, group_size, HEAD)
        .transpose(1, 0, 2, 3)
        .reshape(query_count, kv_local * group_size * HEAD)
    )
    projected = jnp.dot(attended, return_weight, preferred_element_type=jnp.float32)
    returned = lax.psum_scatter(
        projected.astype(jnp.bfloat16), "mp", scatter_dimension=1, tiled=True
    )
    slot_ids = jnp.arange(slot_count, dtype=jnp.int32)
    lead_slot = (own_shard - offsets) % shards
    local_span = slot_ids[:, None] * shards + lead_slot[None, :]
    back_index = (offsets[None, :] + local_span - own_shard) // shards
    alive = local_span < span_counts[None, :]
    back_rows = jnp.where(
        alive[:, :, None],
        returned[jnp.clip(back_index, 0, CH_OWN - 1)],
        jnp.zeros((), jnp.bfloat16),
    )
    arrived = lax.all_to_all(back_rows, "seq", split_axis=1, concat_axis=1, tiled=True)
    span_results = jnp.roll(arrived, -(own_offset % shards), axis=1).reshape(capacity, column_count)
    positions = jnp.arange(rows_here, dtype=jnp.int32)
    live_slots = jnp.arange(capacity, dtype=jnp.int32) < own_count
    passed = jnp.sum(
        ((own_marks[None, :] <= positions[:, None]) & live_slots[None, :]).astype(jnp.int32), axis=1
    )
    return (skip_part.astype(jnp.float32) + span_results[passed - 1].astype(jnp.float32)).astype(
        jnp.bfloat16
    )


def solution(mesh):
    in_specs = (
        P("seq", None),
        P(),
        P(None, "mp"),
        P(None, "mp"),
        P("mp"),
        P("mp", None),
        P("seq", None),
        P(),
        P("seq", "mp"),
        P("mp"),
        P(),
        P("seq", "mp"),
        P("seq", "mp"),
        P("seq", "mp"),
        P("mp", None),
    )
    out_specs = P("seq", "mp")
    def on_device(*arrays):
        heads_here = arrays[11].shape[1] // HEAD
        fits = heads_here == mesh.shape["seq"] and mesh.shape["mp"] == 2
        return (one_head_each if fits else spread_heads)(*arrays)

    return jax.shard_map(
        on_device, mesh=mesh, in_specs=in_specs, out_specs=out_specs, check_vma=False
    )
```

```python
import functools
import math

import jax
import jax.numpy as jnp
from jax import lax
from jax.experimental import pallas as pl
from jax.experimental.pallas import tpu as pltpu
from jax.sharding import PartitionSpec as P

HEADS = 32
KV_HEADS = 8
HEAD = 128
CH_OWN = 64


eps = 1e-05
masked = -1e30
TILE = 16


def swapped(value):
    return lax.ppermute(value, "mp", [(0, 1), (1, 0)])


def vmem():
    return pl.BlockSpec(memory_space=pltpu.VMEM)


def smem():
    return pl.BlockSpec(memory_space=pltpu.SMEM)


def in_place():
    return pl.BlockSpec(memory_space=pl.ANY)


def in_hbm():
    return pl.BlockSpec(memory_space=pltpu.HBM)


def seat():
    return lax.axis_index("seq"), lax.axis_index("mp")


def params(mebibytes=24):
    return pltpu.CompilerParams(vmem_limit_bytes=mebibytes * 2**20)


def brief():
    return pl.CostEstimate(flops=1, bytes_accessed=1, transcendentals=0)


def lanes(which, size):
    return pl.ds(pl.multiple_of(which * size, size), size)


def rows_at(which, size):
    return pl.ds(pl.multiple_of(which * size, size), size)


def start_all(pairs, sems):
    copies = []
    for index, (from_ref, to_ref) in enumerate(pairs):
        copy = pltpu.make_async_copy(from_ref, to_ref, sems.at[index])
        copy.start()
        copies.append(copy)
    return copies


def copy_all(pairs, sems):
    for copy in start_all(pairs, sems):
        copy.wait()


def one_minus_exp(u):
    series = jnp.ones_like(u)
    for order in range(9, 1, -1):
        series = 1.0 - u * (1.0 / order) * series
    return jnp.where(u < 0.5, u * series, 1.0 - jnp.exp(-u))


def softplus(v):
    tail = jnp.exp(-jnp.abs(v))
    series = jnp.ones_like(tail)
    for order in range(6, 1, -1):
        series = 1.0 - tail * ((order - 1.0) / order) * series
    return jnp.maximum(v, 0.0) + jnp.where(tail < 0.03, tail * series, jnp.log(1.0 + tail))


def start_cuts(plane, query_ref, key_ref, value_ref, pair_outs, sems):
    layers = len(pair_outs)
    me, _ = seat()
    layer = me // plane
    group = plane * HEAD
    pairs = []
    for step, out_ref in enumerate(pair_outs):
        target = layer ^ step
        pairs.append((query_ref.at[:, lanes(target, group)], out_ref.at[:, pl.ds(0, group)]))
        pairs.append((key_ref.at[:, lanes(target, HEAD)], out_ref.at[:, pl.ds(group, HEAD)]))
        pairs.append(
            (value_ref.at[:, lanes(target, HEAD)], out_ref.at[:, pl.ds(group + HEAD, HEAD)])
        )
    return start_all(pairs, sems)


def scan_kernel(plane, layers, *refs):
    bytes_hbm, gain_ref, input_hbm, step_hbm, rate_ref = refs[:5]
    others, refs = refs[5:8], refs[8:]
    local_ref, through_ref, ends_ref = refs[:3]
    pair_outs, refs = refs[3 : 3 + layers], refs[3 + layers :]
    bytes_ref, input_ref, step_ref, *held, sems, cut_sems = refs
    fetches = start_all(
        [(bytes_hbm, bytes_ref), (step_hbm, step_ref), (input_hbm, input_ref), *zip(others, held)],
        sems,
    )
    fetches[0].wait()
    values = bytes_ref[...].astype(jnp.float32)
    scale = lax.rsqrt(jnp.mean(values * values, axis=1, keepdims=True) + eps)
    normed = (values * scale * gain_ref[...]).astype(jnp.bfloat16)
    fetches[1].wait()
    steps = softplus(jnp.dot(normed, step_ref[...], preferred_element_type=jnp.float32))
    rate_steps = steps * rate_ref[...]
    fetches[2].wait()
    inputs = jnp.dot(normed, input_ref[...], preferred_element_type=jnp.float32)
    for fetch in fetches[3:]:
        fetch.wait()
    cuts = start_cuts(plane, *held, pair_outs, cut_sems)
    decays = jnp.exp(-rate_steps)
    drives = jnp.sqrt(one_minus_exp(2.0 * rate_steps)) * inputs
    rows, width = decays.shape
    tile = 8
    decays = decays.reshape(rows // tile, tile, width)
    drives = drives.reshape(rows // tile, tile, width)
    place = lax.broadcasted_iota(jnp.int32, decays.shape, 1)
    for reach in (1, 2, 4):
        before_decays = pltpu.roll(decays, reach, 1)
        before_drives = pltpu.roll(drives, reach, 1)
        inside = place >= reach
        drives = jnp.where(inside, decays * before_drives + drives, drives)
        decays = jnp.where(inside, decays * before_decays, decays)
    state = jnp.zeros((1, width), jnp.float32)
    kept = jnp.ones((1, width), jnp.float32)
    for index in range(rows // tile):
        states = decays[index] * state + drives[index]
        passing = decays[index] * kept
        local_ref[pl.ds(index * tile, tile), :] = states
        through_ref[pl.ds(index * tile, tile), :] = passing
        state = states[tile - 1 :, :]
        kept = passing[tile - 1 :, :]
    for index in range(ends_ref.shape[0]):
        ends_ref[index, 0:1, :] = kept
        ends_ref[index, 1:2, :] = state
    for cut in cuts:
        cut.wait()


def states_kernel(local_ref, through_ref, mixer_ref, ends_ref, states_ref, other_ref):
    me, lane = seat()
    carry = jnp.zeros((1, local_ref.shape[1]), jnp.float32)
    for shard in range(ends_ref.shape[0]):
        later = ends_ref[shard, 0:1, :] * carry + ends_ref[shard, 1:2, :]
        carry = jnp.where(shard < me, later, carry)
    states = (local_ref[...] + through_ref[...] * carry).astype(jnp.bfloat16)
    states_ref[...] = states
    half = other_ref.shape[1]
    other_ref[...] = jnp.dot(
        states, mixer_ref[:, lanes(1 - lane, half)], preferred_element_type=jnp.float32
    )


def pool_kernel(plane, *refs):
    states_ref, mixer_ref, other_ref, bytes_ref, pick_ref = refs[:5]
    layers = len(refs) - 8 - plane
    up_pieces, (encoded_ref, out_ref, *up_refs, sems) = refs[5 : 5 + layers], refs[5 + layers :]
    cross = lax.rem(seat()[0], plane)
    pairs = []
    for mask, up_ref in enumerate(up_refs):
        size = 2 * up_ref.shape[2] // layers
        for step, piece in enumerate(up_pieces):
            for number in range(layers // 2):
                columns = lanes(number * plane + (cross ^ mask), size)
                pairs.append((piece.at[:, columns], up_ref.at[step, :, pl.ds(number * size, size)]))
    copies = start_all(pairs, sems)
    half = other_ref.shape[1]
    columns = lanes(seat()[1], half)
    mixed = jnp.dot(states_ref[...], mixer_ref[:, columns], preferred_element_type=jnp.float32)
    skip = bytes_ref[:, columns].astype(jnp.float32)
    encoded = (skip + (mixed + other_ref[...])).astype(jnp.bfloat16)
    encoded_ref[...] = encoded
    picked = jnp.dot(pick_ref[...], encoded, preferred_element_type=jnp.float32)
    out_ref[...] = picked.astype(jnp.bfloat16).reshape(out_ref.shape)
    for copy in copies:
        copy.wait()


def own_kernel(pick_ref, arrived_ref, out_ref):
    shards, slots, half = arrived_ref.shape
    rows = arrived_ref[...].astype(jnp.float32).reshape(shards * slots, half)
    own = jnp.dot(
        pick_ref[...], rows.astype(jnp.bfloat16), preferred_element_type=jnp.float32
    ).astype(jnp.bfloat16)
    for index in range(out_ref.shape[0]):
        out_ref[index] = own


def inner_kernel(plane, layers, bias_ref, gain_ref, near_ref, far_ref, *refs):
    up_own, refs = refs[:plane], refs[plane:]
    up_far, refs = refs[:plane], refs[plane:]
    pieces, refs = refs[:layers], refs[layers:]
    out_ref, pooled, up, weights, squares, sems = refs
    me, lane = seat()
    layer, cross = me // plane, lax.rem(me, plane)
    half = near_ref.shape[1]
    up_rows, up_half = up_own[0].shape[1:]
    pairs = [
        (near_ref, pooled.at[:, lanes(lane, half)]),
        (far_ref, pooled.at[:, lanes(1 - lane, half)]),
    ]
    for step in range(layers):
        for mask in range(plane):
            where = rows_at((layer ^ step) * plane + (cross ^ mask), up_rows)
            pairs.append((up_own[mask].at[step], up.at[where, lanes(lane, up_half)]))
            pairs.append((up_far[mask].at[step], up.at[where, lanes(1 - lane, up_half)]))
    for step, piece in enumerate(pieces):
        pairs.append((piece, weights.at[rows_at(layer ^ step, piece.shape[0]), :]))
    copies = start_all(pairs, sems)
    for copy in copies[:-layers]:
        copy.wait()
    rows = pooled.shape[0]
    block = rows // plane
    ones = jnp.ones((8, up.shape[1]), jnp.bfloat16)
    for index in range(plane):
        where = pl.ds(index * block, block)
        widened = jnp.dot(pooled[where, :], up[...], preferred_element_type=jnp.float32)
        widened = (widened + bias_ref[...]).astype(jnp.bfloat16).astype(jnp.float32)
        inner = (widened * gain_ref[...]).astype(jnp.bfloat16)
        square = widened * widened
        coarse = square.astype(jnp.bfloat16)
        fine = (square - coarse.astype(jnp.float32)).astype(jnp.bfloat16)
        squares[:, where] = sum(
            lax.dot_general(
                ones, part, (((1,), (1,)), ((), ())), preferred_element_type=jnp.float32
            )
            for part in (coarse, fine)
        )
        if index == 0:
            for copy in copies[-layers:]:
                copy.wait()
        sums = jnp.dot(inner, weights[...], preferred_element_type=jnp.float32)
        sums = sums.astype(jnp.bfloat16)
        for head in range(plane):
            out_ref[head, where, :] = sums[:, head * HEAD : (head + 1) * HEAD]
        for number in range(2):
            start = (plane + number) * HEAD
            out_ref[index, pl.ds(rows + number * block, block), :] = sums[:, start : start + HEAD]
    total = jnp.concatenate(
        [squares[0:1, start : start + HEAD] for start in range(0, rows, HEAD)], axis=0
    )
    coarse = total.astype(jnp.bfloat16).astype(jnp.float32)
    both = jnp.concatenate([coarse, total - coarse], axis=0).astype(jnp.bfloat16)
    for index in range(plane):
        out_ref[index, pl.ds(rows + 2 * block, both.shape[0]), :] = both


def heads_kernel(features, got_ref, query_ref, pair_ref, queries):
    plane = got_ref.shape[0]
    rows = query_ref.shape[0]
    block = rows // plane
    lines = rows // HEAD
    shards = rows // CH_OWN
    layers = shards // plane
    first = rows + 2 * block

    def added(start, size):
        parts = [got_ref[index, start : start + size, :].astype(jnp.float32) for index in range(plane)]
        return sum(parts[1:], parts[0])

    both = added(first, 2 * lines)
    total = both[:lines, :] + both[lines:, :]
    scale = jnp.transpose(lax.rsqrt(total * (1.0 / features) + eps))
    for line in range(lines):
        scaled = added(line * HEAD, HEAD) * scale[:, line : line + 1]
        for start in range(0, HEAD, CH_OWN):
            index = (line * HEAD + start) // CH_OWN
            shard = (index % layers) * plane + index // layers
            queries[pl.ds(shard, CH_OWN, stride=shards), :] = scaled[start : start + CH_OWN, :]
    query_ref[...] = queries[...].astype(jnp.bfloat16)
    cross = lax.rem(seat()[0], plane)
    per_block = block // HEAD
    for line in range(per_block):
        mine = scale[:, line : line + 1]
        for index in range(1, plane):
            column = index * per_block + line
            mine = jnp.where(cross == index, scale[:, column : column + 1], mine)
        for number in range(2):
            start = number * block + line * HEAD
            pair = (added(rows + start, HEAD) * mine).astype(jnp.bfloat16)
            for index in range(plane):
                pair_ref[index, pl.ds(start, HEAD), :] = pair


def attend_kernel(place_ref, query_ref, pair_ref, out_ref, natural, keys, values, attended):
    rows = query_ref.shape[0]
    window = out_ref.shape[1]
    plane = pair_ref.shape[0]
    part = rows // plane
    shards = rows // CH_OWN
    layers = shards // plane
    for number, held in enumerate((keys, values)):
        for cross in range(plane):
            for layer in range(layers):
                piece = pair_ref[cross, pl.ds(number * part + layer * CH_OWN, CH_OWN), :]
                where = pl.ds(layer * plane + cross, CH_OWN, stride=shards)
                natural[where, :] = piece.astype(jnp.float32)
        held[...] = natural[...].astype(jnp.bfloat16)
    block = min(256, rows)
    score_scale = 1.0 / math.sqrt(HEAD)
    for start in range(0, rows, block):
        stop = start + block
        scores = lax.dot_general(
            query_ref[start:stop, :],
            keys[0:stop, :],
            (((1,), (1,)), ((), ())),
            preferred_element_type=jnp.float32,
        )
        spots = lax.broadcasted_iota(jnp.int32, scores.shape, 1)
        mine = lax.broadcasted_iota(jnp.int32, scores.shape, 0) + start
        scores = jnp.where(spots <= mine, scores * score_scale, masked)
        peak = jnp.max(scores, axis=1, keepdims=True)
        lifted = jnp.exp(scores - peak)
        denominator = jnp.sum(lifted, axis=1, keepdims=True)
        weighted = jnp.dot(
            lifted.astype(jnp.bfloat16), values[0:stop, :], preferred_element_type=jnp.float32
        )
        attended[start:stop, :] = (weighted / denominator).astype(jnp.bfloat16)
    attended[rows:, :] = jnp.zeros((attended.shape[0] - rows, HEAD), jnp.bfloat16)
    for shard in range(out_ref.shape[0]):
        first = place_ref[shard]
        out_ref[shard] = attended[pl.ds(pl.multiple_of(first * TILE, TILE), window), :]


def fetch_kernel(from_ref, to_ref, sem):
    copy = pltpu.make_async_copy(from_ref, to_ref, sem)
    copy.start()
    copy.wait()


def return_kernel(weight_ref, pieces_ref, own_ref, other_ref, attended):
    half = own_ref.shape[1]
    lane = seat()[1]
    for head in range(pieces_ref.shape[0]):
        attended[:, head * HEAD : (head + 1) * HEAD] = pieces_ref[head]
    other_ref[...] = jnp.dot(
        attended[...], weight_ref[:, lanes(1 - lane, half)], preferred_element_type=jnp.float32
    )
    own_ref[...] = jnp.dot(
        attended[...], weight_ref[:, lanes(lane, half)], preferred_element_type=jnp.float32
    )


def join_kernel(own_ref, other_ref, encoded_ref, spread_ref, out_ref):
    returned = (own_ref[...] + other_ref[...]).astype(jnp.bfloat16)
    results = jnp.dot(spread_ref[...], returned, preferred_element_type=jnp.float32)
    out_ref[...] = (encoded_ref[...].astype(jnp.float32) + results).astype(jnp.bfloat16)


def one_head_each(
    byte_states,
    outer_gain,
    mamba_input,
    mamba_step,
    decay_rate,
    mixer_weight,
    boundaries,
    span_counts,
    up_weight,
    up_bias,
    inner_gain,
    query_weight,
    key_weight,
    value_weight,
    return_weight,
):
    shards = lax.axis_size("seq")
    me = lax.axis_index("seq")
    lane = lax.axis_index("mp")
    plane = HEADS // KV_HEADS
    layers = shards // plane
    rows_here, width = byte_states.shape
    half = mamba_input.shape[1]
    capacity = boundaries.shape[1]
    window = capacity + TILE
    total_rows = CH_OWN * shards
    inner_width = inner_gain.shape[0]
    inner_half = up_bias.shape[0]
    weight_rows = query_weight.shape[0]
    f32, bf16 = jnp.float32, jnp.bfloat16
    layer, cross = me // plane, me % plane
    layer_groups = [[first + plane * step for step in range(layers)] for first in range(plane)]
    plane_groups = [[first * plane + step for step in range(plane)] for first in range(layers)]

    def over(value, mask):
        return lax.ppermute(value, "seq", [(i, i ^ mask) for i in range(shards)])

    def after(value, done):
        return lax.optimization_barrier((value, done))[0]

    own_bias = up_bias.reshape(layers // 2, plane, weight_rows)
    own_bias = lax.dynamic_index_in_dim(own_bias, cross, 1, keepdims=False).reshape(1, -1)
    own_gain = inner_gain.reshape(layers, plane, weight_rows)
    own_gain = lax.dynamic_index_in_dim(own_gain, cross, 1, keepdims=False).reshape(1, -1)

    seq_ids = jnp.arange(shards, dtype=jnp.int32)
    offsets = jnp.cumsum(span_counts) - span_counts
    own_offset = jnp.sum(jnp.where(seq_ids == me, offsets, 0))
    own_count = jnp.sum(jnp.where(seq_ids == me, span_counts, 0))
    place = offsets // TILE
    own_marks = boundaries[0]
    positions = jnp.arange(rows_here, dtype=jnp.int32)
    spans_here = jnp.arange(capacity, dtype=jnp.int32)
    live = spans_here < own_count
    slots = capacity // shards
    slot_ids = jnp.arange(slots, dtype=jnp.int32)
    local_span = slot_ids[None, :] * shards + ((seq_ids - own_offset) % shards)[:, None]
    is_span = spans_here[None, :] == local_span.reshape(-1)[:, None]
    byte_at = jnp.sum(jnp.where(is_span, jnp.minimum(own_marks, rows_here - 1)[None, :], 0), axis=1)
    pool_pick = (positions[None, :] == byte_at[:, None]).astype(bf16)
    own_spans = me + jnp.arange(CH_OWN, dtype=jnp.int32) * shards
    origin = jnp.sum((offsets[None, :] <= own_spans[:, None]).astype(jnp.int32), axis=1) - 1
    origin_offset = jnp.sum(
        jnp.where(seq_ids[None, :] == origin[:, None], offsets[None, :], 0), axis=1
    )
    arrived_row = origin * slots + (own_spans - origin_offset) // shards
    own_pick = (
        jnp.arange(shards * slots, dtype=jnp.int32)[None, :] == arrived_row[:, None]
    ).astype(bf16)
    passed = jnp.sum(
        ((own_marks[None, :] <= positions[:, None]) & live[None, :]).astype(jnp.int32), axis=1
    )
    result_row = passed - 1 + own_offset % TILE
    spread = (jnp.arange(window, dtype=jnp.int32)[None, :] == result_row[:, None]).astype(bf16)

    up_half = inner_half // plane
    up_layers = [up_weight] + [over(up_weight, plane * step) for step in range(1, layers)]

    local, through, ends, *pair_cuts = pl.pallas_call(
        functools.partial(scan_kernel, plane, layers),
        out_shape=(
            jax.ShapeDtypeStruct((rows_here, half), f32),
            jax.ShapeDtypeStruct((rows_here, half), f32),
            jax.ShapeDtypeStruct((shards, 2, half), f32),
        )
        + (jax.ShapeDtypeStruct((weight_rows, (plane + 2) * HEAD), bf16),) * layers,
        in_specs=[in_hbm(), vmem(), in_hbm(), in_hbm(), vmem()] + [in_hbm()] * 3,
        out_specs=(vmem(),) * 3 + (in_place(),) * layers,
        scratch_shapes=[
            pltpu.VMEM(array.shape, bf16)
            for array in (
                byte_states,
                mamba_input,
                mamba_step,
                query_weight,
                key_weight,
                value_weight,
            )
        ]
        + [pltpu.SemaphoreType.DMA((6,)), pltpu.SemaphoreType.DMA((3 * layers,))],
        cost_estimate=brief(),
        compiler_params=params(62),
    )(
        byte_states,
        outer_gain[None, :],
        mamba_input,
        mamba_step,
        decay_rate[None, :],
        query_weight,
        key_weight,
        value_weight,
    )
    ends = lax.all_to_all(ends, "seq", 0, 0, tiled=True)
    ends, up_layers = lax.optimization_barrier((ends, up_layers))
    pieces = [pair_cuts[0]] + [over(pair_cuts[step], plane * step) for step in (1, 2)]
    states, other_part = pl.pallas_call(
        states_kernel,
        out_shape=(
            jax.ShapeDtypeStruct((rows_here, half), bf16),
            jax.ShapeDtypeStruct((rows_here, half), f32),
        ),
        in_specs=[vmem()] * 4,
        out_specs=(vmem(),) * 2,
        cost_estimate=brief(),
        compiler_params=params(8),
    )(local, through, mixer_weight, ends)
    far_bias = swapped(own_bias)
    bias = jnp.where(
        lane == 0,
        jnp.concatenate([own_bias, far_bias], axis=1),
        jnp.concatenate([far_bias, own_bias], axis=1),
    )
    far_part, pieces, bias = lax.optimization_barrier((swapped(other_part), pieces, bias))
    encoded, leaving, *up_cuts = pl.pallas_call(
        functools.partial(pool_kernel, plane),
        out_shape=(
            jax.ShapeDtypeStruct((rows_here, half), bf16),
            jax.ShapeDtypeStruct((shards, slots, half), bf16),
        )
        + (jax.ShapeDtypeStruct((layers, up_weight.shape[0], up_half), bf16),) * plane,
        in_specs=[vmem()] * 5 + [in_place()] * layers,
        out_specs=(vmem(),) * (2 + plane),
        scratch_shapes=[pltpu.SemaphoreType.DMA((plane * layers * layers // 2,))],
        cost_estimate=brief(),
        compiler_params=params(10),
    )(states, mixer_weight, far_part, byte_states, pool_pick, *up_layers)
    arrived = lax.all_to_all(leaving, "seq", 0, 0, tiled=True)
    pieces.append(over(after(pair_cuts[3], states), 3 * plane))
    up_own = [up_cuts[0]] + [over(up_cuts[mask], mask) for mask in range(1, plane)]
    arrived, pieces = lax.optimization_barrier((arrived, pieces))
    own_rows = pl.pallas_call(
        own_kernel,
        out_shape=jax.ShapeDtypeStruct((layers, CH_OWN, half), bf16),
        in_specs=[vmem()] * 2,
        out_specs=vmem(),
        cost_estimate=brief(),
        compiler_params=params(8),
    )(own_pick, arrived)
    own_rows, up_own = lax.optimization_barrier((own_rows, up_own))
    near_layer = lax.all_to_all(
        own_rows, "seq", 0, 0, axis_index_groups=layer_groups, tiled=True
    )
    near = lax.all_to_all(
        jnp.broadcast_to(near_layer[None], (plane, layers, CH_OWN, half)),
        "seq",
        0,
        0,
        axis_index_groups=plane_groups,
        tiled=True,
    ).reshape(total_rows, half)
    up_far = [swapped(piece) for piece in up_own]

    features = own_gain.shape[1]
    block = total_rows // plane
    sent_rows = total_rows + 2 * block + 2 * (total_rows // HEAD)
    partial_sums = pl.pallas_call(
        functools.partial(inner_kernel, plane, layers),
        out_shape=jax.ShapeDtypeStruct((plane, sent_rows, HEAD), bf16),
        in_specs=[vmem()] * 2 + [in_place()] * (2 + 2 * plane + layers),
        out_specs=vmem(),
        scratch_shapes=[
            pltpu.VMEM((total_rows, width), bf16),
            pltpu.VMEM((width, features), bf16),
            pltpu.VMEM((features, (plane + 2) * HEAD), bf16),
            pltpu.VMEM((8, total_rows), f32),
            pltpu.SemaphoreType.DMA((2 + 2 * shards + layers,)),
        ],
        cost_estimate=brief(),
        compiler_params=params(20),
    )(bias, own_gain, near, swapped(near), *up_own, *up_far, *pieces)
    got = lax.all_to_all(
        partial_sums, "seq", 0, 0, axis_index_groups=plane_groups, tiled=True
    )
    queries, pairs = pl.pallas_call(
        functools.partial(heads_kernel, inner_width),
        out_shape=(
            jax.ShapeDtypeStruct((total_rows, HEAD), bf16),
            jax.ShapeDtypeStruct((plane, 2 * block, HEAD), bf16),
        ),
        in_specs=[vmem()],
        out_specs=(vmem(),) * 2,
        scratch_shapes=[pltpu.VMEM((total_rows, HEAD), f32)],
        cost_estimate=brief(),
        compiler_params=params(10),
    )(got)
    pairs = lax.all_to_all(pairs, "seq", 0, 0, axis_index_groups=plane_groups, tiled=True)
    leaving = pl.pallas_call(
        attend_kernel,
        out_shape=jax.ShapeDtypeStruct((shards, window, HEAD), bf16),
        in_specs=[smem()] + [vmem()] * 2,
        out_specs=vmem(),
        scratch_shapes=[
            pltpu.VMEM((total_rows, HEAD), f32),
            pltpu.VMEM((total_rows, HEAD), bf16),
            pltpu.VMEM((total_rows, HEAD), bf16),
            pltpu.VMEM((total_rows + window, HEAD), bf16),
        ],
        cost_estimate=brief(),
        compiler_params=params(12),
    )(place, queries, pairs)
    pieces = lax.all_to_all(leaving, "seq", 0, 0, tiled=True)
    fetched = pl.pallas_call(
        fetch_kernel,
        out_shape=jax.ShapeDtypeStruct(return_weight.shape, bf16),
        in_specs=[in_hbm()],
        out_specs=vmem(),
        scratch_shapes=[pltpu.SemaphoreType.DMA],
        cost_estimate=brief(),
        compiler_params=params(8),
    )(after(return_weight, leaving))
    own_back, other_back = pl.pallas_call(
        return_kernel,
        out_shape=(jax.ShapeDtypeStruct((window, half), f32),) * 2,
        in_specs=[vmem()] * 2,
        out_specs=(vmem(),) * 2,
        scratch_shapes=[pltpu.VMEM((window, shards * HEAD), bf16)],
        cost_estimate=brief(),
        compiler_params=params(12),
    )(fetched, pieces)
    return pl.pallas_call(
        join_kernel,
        out_shape=jax.ShapeDtypeStruct((rows_here, half), bf16),
        in_specs=[vmem()] * 4,
        out_specs=vmem(),
        cost_estimate=brief(),
        compiler_params=params(8),
    )(own_back, swapped(other_back), encoded, spread)


def prefix(value, axis, join, neutral):
    count, mine = (lax.axis_size(axis), lax.axis_index(axis))
    pieces = jax.tree.map(lambda part: lax.all_gather(part, axis), value)
    so_far = jax.tree.map(
        lambda part, zero: jnp.full_like(part, 0) + jnp.asarray(zero, part.dtype), value, neutral
    )

    def lap(position, so_far):
        longer = join(so_far, jax.tree.map(lambda part: part[position], pieces))
        return jax.tree.map(lambda new, old: jnp.where(position < mine, new, old), longer, so_far)

    return lax.fori_loop(0, count - 1, lap, so_far)


def rms_scale(values, gain):
    values = values.astype(jnp.float32)
    return values * lax.rsqrt(jnp.mean(values * values, axis=-1, keepdims=True) + eps) * gain


def combine_pairs(earlier, later):
    return (earlier[0] * later[0], later[0] * earlier[1] + later[1])


def pick_table(table, wanted, seq_ids):
    return jnp.sum(jnp.where(seq_ids[None, :] == wanted[:, None], table[None, :], 0), axis=1)


def block_size(piece_rows, shard_rows):
    limit = max(1, 1024 // shard_rows)
    pieces = max(1, piece_rows // shard_rows)
    best_size = 1
    for candidate in range(1, limit + 1):
        if pieces % candidate == 0:
            best_size = candidate
    return min(piece_rows, best_size * shard_rows)


def spread_heads(
    byte_states,
    outer_gain,
    mamba_input,
    mamba_step,
    decay_rate,
    mixer_weight,
    boundaries,
    span_counts,
    up_weight,
    up_bias,
    inner_gain,
    query_weight,
    key_weight,
    value_weight,
    return_weight,
):
    shards = lax.axis_size("seq")
    own_shard = lax.axis_index("seq")
    own_lane = lax.axis_index("mp")
    rows_here = byte_states.shape[0]
    capacity = boundaries.shape[1]
    column_count = mamba_input.shape[1]
    kv_local = key_weight.shape[1] // HEAD
    group_size = HEADS // KV_HEADS
    slot_count = capacity // shards
    offsets = jnp.cumsum(span_counts) - span_counts
    seq_ids = jnp.arange(shards, dtype=jnp.int32)
    own_offset = jnp.sum(jnp.where(seq_ids == own_shard, offsets, 0))
    own_count = jnp.sum(jnp.where(seq_ids == own_shard, span_counts, 0))
    normed = rms_scale(byte_states, outer_gain).astype(jnp.bfloat16)
    inputs = jnp.dot(normed, mamba_input, preferred_element_type=jnp.float32)
    step_sizes = jax.nn.softplus(jnp.dot(normed, mamba_step, preferred_element_type=jnp.float32))
    rate_steps = step_sizes * decay_rate
    decays = jnp.exp(-rate_steps)
    drives = jnp.sqrt(-jnp.expm1(-2.0 * rate_steps)) * inputs
    through, local_states = lax.associative_scan(combine_pairs, (decays, drives), axis=0)
    starting = (jnp.ones((column_count,), jnp.float32), jnp.zeros((column_count,), jnp.float32))
    arriving = prefix((through[-1], local_states[-1]), "seq", combine_pairs, starting)
    states = (local_states + through * arriving[1][None, :]).astype(jnp.bfloat16)
    partial_value = jnp.dot(states, mixer_weight, preferred_element_type=jnp.float32)
    mixed_sum = lax.psum(partial_value, "mp")
    encoded = (byte_states.astype(jnp.float32) + mixed_sum).astype(jnp.bfloat16)
    skip_part = lax.dynamic_slice_in_dim(encoded, own_lane * column_count, column_count, 1)
    own_marks = boundaries[0]
    pooled = encoded[jnp.minimum(own_marks, rows_here - 1)]
    row_width = pooled.shape[1]
    outgoing = jnp.roll(pooled.reshape(slot_count, shards, row_width), own_offset % shards, axis=1)
    incoming = lax.all_to_all(outgoing, "seq", split_axis=1, concat_axis=1, tiled=True)
    position = jnp.arange(CH_OWN, dtype=jnp.int32)
    span_index = own_shard + position * shards
    source = jnp.sum((offsets[None, :] <= span_index[:, None]).astype(jnp.int32), axis=1) - 1
    source_offset = pick_table(offsets, source, seq_ids)
    slot_index = (span_index - source_offset) // shards
    gathered_rows = incoming.reshape(slot_count * shards, row_width)[slot_index * shards + source]
    columns = gathered_rows
    widened_sum = jnp.dot(
        columns,
        lax.all_gather(up_weight, "seq", axis=0, tiled=True),
        preferred_element_type=jnp.float32,
    )
    widened_share = (widened_sum + up_bias[None, :]).astype(jnp.bfloat16)
    widened = lax.all_gather(widened_share, "mp", axis=1, tiled=True)
    inner_normed = rms_scale(widened, inner_gain).astype(jnp.bfloat16)
    columns = inner_normed
    query_part = jnp.dot(
        columns,
        lax.all_gather(query_weight, "seq", axis=0, tiled=True),
        preferred_element_type=jnp.float32,
    )
    key_part = jnp.dot(
        columns,
        lax.all_gather(key_weight, "seq", axis=0, tiled=True),
        preferred_element_type=jnp.float32,
    )
    value_part = jnp.dot(
        columns,
        lax.all_gather(value_weight, "seq", axis=0, tiled=True),
        preferred_element_type=jnp.float32,
    )
    queries = query_part.astype(jnp.bfloat16)
    key_rows = key_part.astype(jnp.bfloat16)
    value_rows = value_part.astype(jnp.bfloat16)
    query_count = queries.shape[0]
    grouped = (
        queries.reshape(query_count, kv_local, group_size, HEAD)
        .transpose(1, 0, 2, 3)
        .reshape(kv_local, query_count * group_size, HEAD)
    )
    row_index = jnp.repeat(span_index, group_size)
    shard_rows = key_rows.shape[0]
    score_scale = 1.0 / math.sqrt(HEAD)

    def key_index(whole_index):
        return whole_index // shard_rows + whole_index % shard_rows * shards

    def attend_block(running, key_block, value_block, index_block):
        row_peak, denominator, weighted = running
        scores = (
            jnp.einsum("hqd,khd->hqk", grouped, key_block, preferred_element_type=jnp.float32)
            * score_scale
        )
        scores = jnp.where(index_block[None, None, :] <= row_index[None, :, None], scores, masked)
        new_peak = jnp.maximum(row_peak, jnp.max(scores, axis=2))
        shrink = jnp.exp(row_peak - new_peak)
        lifted = jnp.exp(scores - new_peak[:, :, None])
        denominator = denominator * shrink + jnp.sum(lifted, axis=2)
        weighted = weighted * shrink[:, :, None] + jnp.einsum(
            "hqk,khd->hqd",
            lifted.astype(jnp.bfloat16),
            value_block,
            preferred_element_type=jnp.float32,
        )
        return (new_peak, denominator, weighted)

    query_total = query_count * group_size
    initial = (
        jnp.full((kv_local, query_total), masked, jnp.float32),
        jnp.zeros((kv_local, query_total), jnp.float32),
        jnp.zeros((kv_local, query_total, HEAD), jnp.float32),
    )
    key_piece = lax.all_gather(key_rows, "seq", axis=0, tiled=True)
    value_piece = lax.all_gather(value_rows, "seq", axis=0, tiled=True)
    piece_rows = key_piece.shape[0]
    block_rows = block_size(piece_rows, shard_rows)
    turn_count = piece_rows // block_rows
    key_blocks = key_piece.reshape(turn_count, block_rows, kv_local, HEAD)
    value_blocks = value_piece.reshape(turn_count, block_rows, kv_local, HEAD)

    def one_turn(turn_index, inner_running):
        whole_index = turn_index * block_rows + jnp.arange(block_rows, dtype=jnp.int32)
        return attend_block(
            inner_running, key_blocks[turn_index], value_blocks[turn_index], key_index(whole_index)
        )

    row_peak, denominator, weighted = lax.fori_loop(0, turn_count, one_turn, initial)
    attended = (weighted / denominator[:, :, None]).astype(jnp.bfloat16)
    attended = (
        attended.reshape(kv_local, query_count, group_size, HEAD)
        .transpose(1, 0, 2, 3)
        .reshape(query_count, kv_local * group_size * HEAD)
    )
    projected = jnp.dot(attended, return_weight, preferred_element_type=jnp.float32)
    returned = lax.psum_scatter(
        projected.astype(jnp.bfloat16), "mp", scatter_dimension=1, tiled=True
    )
    slot_ids = jnp.arange(slot_count, dtype=jnp.int32)
    lead_slot = (own_shard - offsets) % shards
    local_span = slot_ids[:, None] * shards + lead_slot[None, :]
    back_index = (offsets[None, :] + local_span - own_shard) // shards
    alive = local_span < span_counts[None, :]
    back_rows = jnp.where(
        alive[:, :, None],
        returned[jnp.clip(back_index, 0, CH_OWN - 1)],
        jnp.zeros((), jnp.bfloat16),
    )
    arrived = lax.all_to_all(back_rows, "seq", split_axis=1, concat_axis=1, tiled=True)
    span_results = jnp.roll(arrived, -(own_offset % shards), axis=1).reshape(capacity, column_count)
    positions = jnp.arange(rows_here, dtype=jnp.int32)
    live_slots = jnp.arange(capacity, dtype=jnp.int32) < own_count
    passed = jnp.sum(
        ((own_marks[None, :] <= positions[:, None]) & live_slots[None, :]).astype(jnp.int32), axis=1
    )
    return (skip_part.astype(jnp.float32) + span_results[passed - 1].astype(jnp.float32)).astype(
        jnp.bfloat16
    )


def solution(mesh):
    in_specs = (
        P("seq", None),
        P(),
        P(None, "mp"),
        P(None, "mp"),
        P("mp"),
        P("mp", None),
        P("seq", None),
        P(),
        P("seq", "mp"),
        P("mp"),
        P(),
        P("seq", "mp"),
        P("seq", "mp"),
        P("seq", "mp"),
        P("mp", None),
    )
    out_specs = P("seq", "mp")
    def on_device(*arrays):
        heads_here = arrays[11].shape[1] // HEAD
        fits = heads_here == mesh.shape["seq"] and mesh.shape["mp"] == 2
        return (one_head_each if fits else spread_heads)(*arrays)

    return jax.shard_map(
        on_device, mesh=mesh, in_specs=in_specs, out_specs=out_specs, check_vma=False
    )
```

```python
import functools
import math

import jax
import jax.numpy as jnp
from jax import lax
from jax.experimental import pallas as pl
from jax.experimental.pallas import tpu as pltpu
from jax.sharding import PartitionSpec as P

HEADS = 32
KV_HEADS = 8
HEAD = 128
CH_OWN = 64


eps = 1e-05
masked = -1e30
TILE = 16


def swapped(value):
    return lax.ppermute(value, "mp", [(0, 1), (1, 0)])


def vmem():
    return pl.BlockSpec(memory_space=pltpu.VMEM)


def smem():
    return pl.BlockSpec(memory_space=pltpu.SMEM)


def in_place():
    return pl.BlockSpec(memory_space=pl.ANY)


def in_hbm():
    return pl.BlockSpec(memory_space=pltpu.HBM)


def seat():
    return lax.axis_index("seq"), lax.axis_index("mp")


def params(mebibytes=24):
    return pltpu.CompilerParams(vmem_limit_bytes=mebibytes * 2**20)


def brief():
    return pl.CostEstimate(flops=1, bytes_accessed=1, transcendentals=0)


def lanes(which, size):
    return pl.ds(pl.multiple_of(which * size, size), size)


def rows_at(which, size):
    return pl.ds(pl.multiple_of(which * size, size), size)


def start_all(pairs, sems):
    copies = []
    for index, (from_ref, to_ref) in enumerate(pairs):
        copy = pltpu.make_async_copy(from_ref, to_ref, sems.at[index])
        copy.start()
        copies.append(copy)
    return copies


def copy_all(pairs, sems):
    for copy in start_all(pairs, sems):
        copy.wait()


def one_minus_exp(u):
    series = jnp.ones_like(u)
    for order in range(9, 1, -1):
        series = 1.0 - u * (1.0 / order) * series
    return jnp.where(u < 0.5, u * series, 1.0 - jnp.exp(-u))


def softplus(v):
    tail = jnp.exp(-jnp.abs(v))
    series = jnp.ones_like(tail)
    for order in range(6, 1, -1):
        series = 1.0 - tail * ((order - 1.0) / order) * series
    return jnp.maximum(v, 0.0) + jnp.where(tail < 0.03, tail * series, jnp.log(1.0 + tail))


def start_cuts(plane, query_ref, key_ref, value_ref, pair_outs, sems):
    layers = len(pair_outs)
    me, _ = seat()
    layer = me // plane
    group = plane * HEAD
    pairs = []
    for step, out_ref in enumerate(pair_outs):
        target = layer ^ step
        pairs.append((query_ref.at[:, lanes(target, group)], out_ref.at[:, pl.ds(0, group)]))
        pairs.append((key_ref.at[:, lanes(target, HEAD)], out_ref.at[:, pl.ds(group, HEAD)]))
        pairs.append(
            (value_ref.at[:, lanes(target, HEAD)], out_ref.at[:, pl.ds(group + HEAD, HEAD)])
        )
    return start_all(pairs, sems)


def scan_kernel(plane, layers, *refs):
    bytes_hbm, gain_ref, input_hbm, step_hbm, rate_ref = refs[:5]
    others, refs = refs[5:8], refs[8:]
    local_ref, through_ref, ends_ref = refs[:3]
    pair_outs, refs = refs[3 : 3 + layers], refs[3 + layers :]
    bytes_ref, input_ref, step_ref, *held, sems, cut_sems = refs
    fetches = start_all(
        [(bytes_hbm, bytes_ref), (step_hbm, step_ref), (input_hbm, input_ref), *zip(others, held)],
        sems,
    )
    fetches[0].wait()
    values = bytes_ref[...].astype(jnp.float32)
    scale = lax.rsqrt(jnp.mean(values * values, axis=1, keepdims=True) + eps)
    normed = (values * scale * gain_ref[...]).astype(jnp.bfloat16)
    fetches[1].wait()
    steps = softplus(jnp.dot(normed, step_ref[...], preferred_element_type=jnp.float32))
    rate_steps = steps * rate_ref[...]
    fetches[2].wait()
    inputs = jnp.dot(normed, input_ref[...], preferred_element_type=jnp.float32)
    for fetch in fetches[3:]:
        fetch.wait()
    cuts = start_cuts(plane, *held, pair_outs, cut_sems)
    decays = jnp.exp(-rate_steps)
    drives = jnp.sqrt(one_minus_exp(2.0 * rate_steps)) * inputs
    rows, width = decays.shape
    tile = 8
    decays = decays.reshape(rows // tile, tile, width)
    drives = drives.reshape(rows // tile, tile, width)
    place = lax.broadcasted_iota(jnp.int32, decays.shape, 1)
    for reach in (1, 2, 4):
        before_decays = pltpu.roll(decays, reach, 1)
        before_drives = pltpu.roll(drives, reach, 1)
        inside = place >= reach
        drives = jnp.where(inside, decays * before_drives + drives, drives)
        decays = jnp.where(inside, decays * before_decays, decays)
    state = jnp.zeros((1, width), jnp.float32)
    kept = jnp.ones((1, width), jnp.float32)
    for index in range(rows // tile):
        states = decays[index] * state + drives[index]
        passing = decays[index] * kept
        local_ref[pl.ds(index * tile, tile), :] = states
        through_ref[pl.ds(index * tile, tile), :] = passing
        state = states[tile - 1 :, :]
        kept = passing[tile - 1 :, :]
    for index in range(ends_ref.shape[0]):
        ends_ref[index, 0:1, :] = kept
        ends_ref[index, 1:2, :] = state
    for cut in cuts:
        cut.wait()


def states_kernel(local_ref, through_ref, mixer_ref, ends_ref, states_ref, other_ref):
    me, lane = seat()
    carry = jnp.zeros((1, local_ref.shape[1]), jnp.float32)
    for shard in range(ends_ref.shape[0]):
        later = ends_ref[shard, 0:1, :] * carry + ends_ref[shard, 1:2, :]
        carry = jnp.where(shard < me, later, carry)
    states = (local_ref[...] + through_ref[...] * carry).astype(jnp.bfloat16)
    states_ref[...] = states
    half = other_ref.shape[1]
    other_ref[...] = jnp.dot(
        states, mixer_ref[:, lanes(1 - lane, half)], preferred_element_type=jnp.float32
    )


def pool_kernel(plane, *refs):
    states_ref, mixer_ref, other_ref, bytes_ref, pick_ref = refs[:5]
    layers = len(refs) - 8 - plane
    up_pieces, (encoded_ref, out_ref, *up_refs, sems) = refs[5 : 5 + layers], refs[5 + layers :]
    cross = lax.rem(seat()[0], plane)
    pairs = []
    for mask, up_ref in enumerate(up_refs):
        size = 2 * up_ref.shape[2] // layers
        for step, piece in enumerate(up_pieces):
            for number in range(layers // 2):
                columns = lanes(number * plane + (cross ^ mask), size)
                pairs.append((piece.at[:, columns], up_ref.at[step, :, pl.ds(number * size, size)]))
    copies = start_all(pairs, sems)
    half = other_ref.shape[1]
    columns = lanes(seat()[1], half)
    mixed = jnp.dot(states_ref[...], mixer_ref[:, columns], preferred_element_type=jnp.float32)
    skip = bytes_ref[:, columns].astype(jnp.float32)
    encoded = (skip + (mixed + other_ref[...])).astype(jnp.bfloat16)
    encoded_ref[...] = encoded
    picked = jnp.dot(pick_ref[...], encoded, preferred_element_type=jnp.float32)
    out_ref[...] = picked.astype(jnp.bfloat16).reshape(out_ref.shape)
    for copy in copies:
        copy.wait()


def own_kernel(pick_ref, arrived_ref, out_ref):
    shards, slots, half = arrived_ref.shape
    rows = arrived_ref[...].astype(jnp.float32).reshape(shards * slots, half)
    own = jnp.dot(
        pick_ref[...], rows.astype(jnp.bfloat16), preferred_element_type=jnp.float32
    ).astype(jnp.bfloat16)
    for index in range(out_ref.shape[0]):
        out_ref[index] = own


def assemble_kernel(plane, layers, *refs):
    up_own, refs = refs[:plane], refs[plane:]
    up_far, refs = refs[:plane], refs[plane:]
    pieces, (up_ref, weights_ref, sems) = refs[:layers], refs[layers:]
    me, lane = seat()
    layer, cross = me // plane, lax.rem(me, plane)
    up_rows, up_half = up_own[0].shape[1:]
    pairs = []
    for step in range(layers):
        for mask in range(plane):
            where = rows_at((layer ^ step) * plane + (cross ^ mask), up_rows)
            pairs.append((up_own[mask].at[step], up_ref.at[where, lanes(lane, up_half)]))
            pairs.append((up_far[mask].at[step], up_ref.at[where, lanes(1 - lane, up_half)]))
    for step, piece in enumerate(pieces):
        pairs.append((piece, weights_ref.at[rows_at(layer ^ step, piece.shape[0]), :]))
    copy_all(pairs, sems)


def inner_kernel(
    plane, bias_ref, gain_ref, near_ref, far_ref, up, weights, out_ref, squares
):
    lane = seat()[1]
    rows, half = near_ref.shape
    block = rows // plane
    ones = jnp.ones((8, up.shape[1]), jnp.bfloat16)
    for index in range(plane):
        where = pl.ds(index * block, block)
        widened = jnp.dot(
            near_ref[where, :], up[rows_at(lane, half), :], preferred_element_type=jnp.float32
        ) + jnp.dot(
            far_ref[where, :], up[rows_at(1 - lane, half), :], preferred_element_type=jnp.float32
        )
        widened = (widened + bias_ref[...]).astype(jnp.bfloat16).astype(jnp.float32)
        inner = (widened * gain_ref[...]).astype(jnp.bfloat16)
        square = widened * widened
        coarse = square.astype(jnp.bfloat16)
        fine = (square - coarse.astype(jnp.float32)).astype(jnp.bfloat16)
        squares[:, where] = sum(
            lax.dot_general(
                ones, part, (((1,), (1,)), ((), ())), preferred_element_type=jnp.float32
            )
            for part in (coarse, fine)
        )
        sums = jnp.dot(inner, weights[...], preferred_element_type=jnp.float32)
        sums = sums.astype(jnp.bfloat16)
        for head in range(plane):
            out_ref[head, where, :] = sums[:, head * HEAD : (head + 1) * HEAD]
        for number in range(2):
            start = (plane + number) * HEAD
            out_ref[index, pl.ds(rows + number * block, block), :] = sums[:, start : start + HEAD]
    total = jnp.concatenate(
        [squares[0:1, start : start + HEAD] for start in range(0, rows, HEAD)], axis=0
    )
    coarse = total.astype(jnp.bfloat16).astype(jnp.float32)
    both = jnp.concatenate([coarse, total - coarse], axis=0).astype(jnp.bfloat16)
    for index in range(plane):
        out_ref[index, pl.ds(rows + 2 * block, both.shape[0]), :] = both


def heads_kernel(features, got_ref, query_ref, pair_ref, queries):
    plane = got_ref.shape[0]
    rows = query_ref.shape[0]
    block = rows // plane
    lines = rows // HEAD
    shards = rows // CH_OWN
    layers = shards // plane
    first = rows + 2 * block

    def added(start, size):
        parts = [got_ref[index, start : start + size, :].astype(jnp.float32) for index in range(plane)]
        return sum(parts[1:], parts[0])

    both = added(first, 2 * lines)
    total = both[:lines, :] + both[lines:, :]
    scale = jnp.transpose(lax.rsqrt(total * (1.0 / features) + eps))
    for line in range(lines):
        scaled = added(line * HEAD, HEAD) * scale[:, line : line + 1]
        for start in range(0, HEAD, CH_OWN):
            index = (line * HEAD + start) // CH_OWN
            shard = (index % layers) * plane + index // layers
            queries[pl.ds(shard, CH_OWN, stride=shards), :] = scaled[start : start + CH_OWN, :]
    query_ref[...] = queries[...].astype(jnp.bfloat16)
    cross = lax.rem(seat()[0], plane)
    per_block = block // HEAD
    for line in range(per_block):
        mine = scale[:, line : line + 1]
        for index in range(1, plane):
            column = index * per_block + line
            mine = jnp.where(cross == index, scale[:, column : column + 1], mine)
        for number in range(2):
            start = number * block + line * HEAD
            pair = (added(rows + start, HEAD) * mine).astype(jnp.bfloat16)
            for index in range(plane):
                pair_ref[index, pl.ds(start, HEAD), :] = pair


def attend_kernel(place_ref, query_ref, pair_ref, out_ref, natural, keys, values, attended):
    rows = query_ref.shape[0]
    window = out_ref.shape[1]
    plane = pair_ref.shape[0]
    part = rows // plane
    shards = rows // CH_OWN
    layers = shards // plane
    for number, held in enumerate((keys, values)):
        for cross in range(plane):
            for layer in range(layers):
                piece = pair_ref[cross, pl.ds(number * part + layer * CH_OWN, CH_OWN), :]
                where = pl.ds(layer * plane + cross, CH_OWN, stride=shards)
                natural[where, :] = piece.astype(jnp.float32)
        held[...] = natural[...].astype(jnp.bfloat16)
    block = min(256, rows)
    score_scale = 1.0 / math.sqrt(HEAD)
    for start in range(0, rows, block):
        stop = start + block
        scores = lax.dot_general(
            query_ref[start:stop, :],
            keys[0:stop, :],
            (((1,), (1,)), ((), ())),
            preferred_element_type=jnp.float32,
        )
        spots = lax.broadcasted_iota(jnp.int32, scores.shape, 1)
        mine = lax.broadcasted_iota(jnp.int32, scores.shape, 0) + start
        scores = jnp.where(spots <= mine, scores * score_scale, masked)
        peak = jnp.max(scores, axis=1, keepdims=True)
        lifted = jnp.exp(scores - peak)
        denominator = jnp.sum(lifted, axis=1, keepdims=True)
        weighted = jnp.dot(
            lifted.astype(jnp.bfloat16), values[0:stop, :], preferred_element_type=jnp.float32
        )
        attended[start:stop, :] = (weighted / denominator).astype(jnp.bfloat16)
    attended[rows:, :] = jnp.zeros((attended.shape[0] - rows, HEAD), jnp.bfloat16)
    for shard in range(out_ref.shape[0]):
        first = place_ref[shard]
        out_ref[shard] = attended[pl.ds(pl.multiple_of(first * TILE, TILE), window), :]


def return_kernel(weight_ref, pieces_ref, own_ref, other_ref, attended):
    half = own_ref.shape[1]
    lane = seat()[1]
    for head in range(pieces_ref.shape[0]):
        attended[:, head * HEAD : (head + 1) * HEAD] = pieces_ref[head]
    other_ref[...] = jnp.dot(
        attended[...], weight_ref[:, lanes(1 - lane, half)], preferred_element_type=jnp.float32
    )
    own_ref[...] = jnp.dot(
        attended[...], weight_ref[:, lanes(lane, half)], preferred_element_type=jnp.float32
    )


def join_kernel(own_ref, other_ref, encoded_ref, spread_ref, out_ref):
    returned = (own_ref[...] + other_ref[...]).astype(jnp.bfloat16)
    results = jnp.dot(spread_ref[...], returned, preferred_element_type=jnp.float32)
    out_ref[...] = (encoded_ref[...].astype(jnp.float32) + results).astype(jnp.bfloat16)


def one_head_each(
    byte_states,
    outer_gain,
    mamba_input,
    mamba_step,
    decay_rate,
    mixer_weight,
    boundaries,
    span_counts,
    up_weight,
    up_bias,
    inner_gain,
    query_weight,
    key_weight,
    value_weight,
    return_weight,
):
    shards = lax.axis_size("seq")
    me = lax.axis_index("seq")
    lane = lax.axis_index("mp")
    plane = HEADS // KV_HEADS
    layers = shards // plane
    rows_here, width = byte_states.shape
    half = mamba_input.shape[1]
    capacity = boundaries.shape[1]
    window = capacity + TILE
    total_rows = CH_OWN * shards
    inner_width = inner_gain.shape[0]
    inner_half = up_bias.shape[0]
    weight_rows = query_weight.shape[0]
    f32, bf16 = jnp.float32, jnp.bfloat16
    layer, cross = me // plane, me % plane
    layer_groups = [[first + plane * step for step in range(layers)] for first in range(plane)]
    plane_groups = [[first * plane + step for step in range(plane)] for first in range(layers)]

    def over(value, mask):
        return lax.ppermute(value, "seq", [(i, i ^ mask) for i in range(shards)])

    def after(value, done):
        return lax.optimization_barrier((value, done))[0]

    own_bias = up_bias.reshape(layers // 2, plane, weight_rows)
    own_bias = lax.dynamic_index_in_dim(own_bias, cross, 1, keepdims=False).reshape(1, -1)
    own_gain = inner_gain.reshape(layers, plane, weight_rows)
    own_gain = lax.dynamic_index_in_dim(own_gain, cross, 1, keepdims=False).reshape(1, -1)

    seq_ids = jnp.arange(shards, dtype=jnp.int32)
    offsets = jnp.cumsum(span_counts) - span_counts
    own_offset = jnp.sum(jnp.where(seq_ids == me, offsets, 0))
    own_count = jnp.sum(jnp.where(seq_ids == me, span_counts, 0))
    place = offsets // TILE
    own_marks = boundaries[0]
    positions = jnp.arange(rows_here, dtype=jnp.int32)
    spans_here = jnp.arange(capacity, dtype=jnp.int32)
    live = spans_here < own_count
    slots = capacity // shards
    slot_ids = jnp.arange(slots, dtype=jnp.int32)
    local_span = slot_ids[None, :] * shards + ((seq_ids - own_offset) % shards)[:, None]
    is_span = spans_here[None, :] == local_span.reshape(-1)[:, None]
    byte_at = jnp.sum(jnp.where(is_span, jnp.minimum(own_marks, rows_here - 1)[None, :], 0), axis=1)
    pool_pick = (positions[None, :] == byte_at[:, None]).astype(bf16)
    own_spans = me + jnp.arange(CH_OWN, dtype=jnp.int32) * shards
    origin = jnp.sum((offsets[None, :] <= own_spans[:, None]).astype(jnp.int32), axis=1) - 1
    origin_offset = jnp.sum(
        jnp.where(seq_ids[None, :] == origin[:, None], offsets[None, :], 0), axis=1
    )
    arrived_row = origin * slots + (own_spans - origin_offset) // shards
    own_pick = (
        jnp.arange(shards * slots, dtype=jnp.int32)[None, :] == arrived_row[:, None]
    ).astype(bf16)
    passed = jnp.sum(
        ((own_marks[None, :] <= positions[:, None]) & live[None, :]).astype(jnp.int32), axis=1
    )
    result_row = passed - 1 + own_offset % TILE
    spread = (jnp.arange(window, dtype=jnp.int32)[None, :] == result_row[:, None]).astype(bf16)

    up_half = inner_half // plane
    up_layers = [up_weight]
    for bit in range(layers.bit_length() - 2, -1, -1):
        up_layers += [over(piece, plane << bit) for piece in up_layers]
    order = [0]
    for bit in range(layers.bit_length() - 2, -1, -1):
        order += [step ^ (1 << bit) for step in order]
    up_layers = [up_layers[order.index(step)] for step in range(layers)]

    local, through, ends, *pair_cuts = pl.pallas_call(
        functools.partial(scan_kernel, plane, layers),
        out_shape=(
            jax.ShapeDtypeStruct((rows_here, half), f32),
            jax.ShapeDtypeStruct((rows_here, half), f32),
            jax.ShapeDtypeStruct((shards, 2, half), f32),
        )
        + (jax.ShapeDtypeStruct((weight_rows, (plane + 2) * HEAD), bf16),) * layers,
        in_specs=[in_hbm(), vmem(), in_hbm(), in_hbm(), vmem()] + [in_hbm()] * 3,
        out_specs=(vmem(),) * 3 + (in_place(),) * layers,
        scratch_shapes=[
            pltpu.VMEM(array.shape, bf16)
            for array in (
                byte_states,
                mamba_input,
                mamba_step,
                query_weight,
                key_weight,
                value_weight,
            )
        ]
        + [pltpu.SemaphoreType.DMA((6,)), pltpu.SemaphoreType.DMA((3 * layers,))],
        cost_estimate=brief(),
        compiler_params=params(62),
    )(
        byte_states,
        outer_gain[None, :],
        mamba_input,
        mamba_step,
        decay_rate[None, :],
        query_weight,
        key_weight,
        value_weight,
    )
    ends = lax.all_to_all(ends, "seq", 0, 0, tiled=True)
    ends, up_layers = lax.optimization_barrier((ends, up_layers))
    pieces = [pair_cuts[0]] + [over(pair_cuts[step], plane * step) for step in range(1, layers)]
    states, other_part = pl.pallas_call(
        states_kernel,
        out_shape=(
            jax.ShapeDtypeStruct((rows_here, half), bf16),
            jax.ShapeDtypeStruct((rows_here, half), f32),
        ),
        in_specs=[vmem()] * 4,
        out_specs=(vmem(),) * 2,
        cost_estimate=brief(),
        compiler_params=params(8),
    )(local, through, mixer_weight, ends)
    far_bias = swapped(own_bias)
    bias = jnp.where(
        lane == 0,
        jnp.concatenate([own_bias, far_bias], axis=1),
        jnp.concatenate([far_bias, own_bias], axis=1),
    )
    far_part, bias, pieces[1] = lax.optimization_barrier((swapped(other_part), bias, pieces[1]))
    encoded, leaving, *up_cuts = pl.pallas_call(
        functools.partial(pool_kernel, plane),
        out_shape=(
            jax.ShapeDtypeStruct((rows_here, half), bf16),
            jax.ShapeDtypeStruct((shards, slots, half), bf16),
        )
        + (jax.ShapeDtypeStruct((layers, up_weight.shape[0], up_half), bf16),) * plane,
        in_specs=[vmem()] * 5 + [in_place()] * layers,
        out_specs=(vmem(),) * (2 + plane),
        scratch_shapes=[pltpu.SemaphoreType.DMA((plane * layers * layers // 2,))],
        cost_estimate=brief(),
        compiler_params=params(10),
    )(states, mixer_weight, far_part, byte_states, pool_pick, *up_layers)
    arrived = lax.all_to_all(leaving, "seq", 0, 0, tiled=True)
    up_own = [up_cuts[0]] + [over(up_cuts[mask], mask) for mask in range(1, plane)]
    arrived, pieces = lax.optimization_barrier((arrived, pieces))
    own_rows = pl.pallas_call(
        own_kernel,
        out_shape=jax.ShapeDtypeStruct((layers, CH_OWN, half), bf16),
        in_specs=[vmem()] * 2,
        out_specs=vmem(),
        cost_estimate=brief(),
        compiler_params=params(8),
    )(own_pick, arrived)
    own_rows, up_own = lax.optimization_barrier((own_rows, up_own))
    near_layer = lax.all_to_all(
        own_rows, "seq", 0, 0, axis_index_groups=layer_groups, tiled=True
    )
    features = own_gain.shape[1]
    up_far = [swapped(piece) for piece in up_own]
    up_all, weights = pl.pallas_call(
        functools.partial(assemble_kernel, plane, layers),
        out_shape=(
            jax.ShapeDtypeStruct((width, features), bf16),
            jax.ShapeDtypeStruct((features, (plane + 2) * HEAD), bf16),
        ),
        in_specs=[in_place()] * (2 * plane + layers),
        out_specs=(vmem(),) * 2,
        scratch_shapes=[pltpu.SemaphoreType.DMA((2 * shards + layers,))],
        cost_estimate=brief(),
        compiler_params=params(8),
    )(*up_own, *up_far, *pieces)
    near_layer, up_all, weights = lax.optimization_barrier((near_layer, up_all, weights))
    near = lax.all_to_all(
        jnp.broadcast_to(near_layer[None], (plane, layers, CH_OWN, half)),
        "seq",
        0,
        0,
        axis_index_groups=plane_groups,
        tiled=True,
    ).reshape(total_rows, half)

    block = total_rows // plane
    sent_rows = total_rows + 2 * block + 2 * (total_rows // HEAD)
    partial_sums = pl.pallas_call(
        functools.partial(inner_kernel, plane),
        out_shape=jax.ShapeDtypeStruct((plane, sent_rows, HEAD), bf16),
        in_specs=[vmem()] * 6,
        out_specs=vmem(),
        scratch_shapes=[pltpu.VMEM((8, total_rows), f32)],
        cost_estimate=brief(),
        compiler_params=params(18),
    )(bias, own_gain, near, swapped(near), up_all, weights)
    got = lax.all_to_all(
        partial_sums, "seq", 0, 0, axis_index_groups=plane_groups, tiled=True
    )
    queries, pairs = pl.pallas_call(
        functools.partial(heads_kernel, inner_width),
        out_shape=(
            jax.ShapeDtypeStruct((total_rows, HEAD), bf16),
            jax.ShapeDtypeStruct((plane, 2 * block, HEAD), bf16),
        ),
        in_specs=[vmem()],
        out_specs=(vmem(),) * 2,
        scratch_shapes=[pltpu.VMEM((total_rows, HEAD), f32)],
        cost_estimate=brief(),
        compiler_params=params(10),
    )(got)
    pairs = lax.all_to_all(pairs, "seq", 0, 0, axis_index_groups=plane_groups, tiled=True)
    leaving = pl.pallas_call(
        attend_kernel,
        out_shape=jax.ShapeDtypeStruct((shards, window, HEAD), bf16),
        in_specs=[smem()] + [vmem()] * 2,
        out_specs=vmem(),
        scratch_shapes=[
            pltpu.VMEM((total_rows, HEAD), f32),
            pltpu.VMEM((total_rows, HEAD), bf16),
            pltpu.VMEM((total_rows, HEAD), bf16),
            pltpu.VMEM((total_rows + window, HEAD), bf16),
        ],
        cost_estimate=brief(),
        compiler_params=params(12),
    )(place, queries, pairs)
    pieces = lax.all_to_all(leaving, "seq", 0, 0, tiled=True)
    own_back, other_back = pl.pallas_call(
        return_kernel,
        out_shape=(jax.ShapeDtypeStruct((window, half), f32),) * 2,
        in_specs=[vmem()] * 2,
        out_specs=(vmem(),) * 2,
        scratch_shapes=[pltpu.VMEM((window, shards * HEAD), bf16)],
        cost_estimate=brief(),
        compiler_params=params(12),
    )(return_weight, pieces)
    return pl.pallas_call(
        join_kernel,
        out_shape=jax.ShapeDtypeStruct((rows_here, half), bf16),
        in_specs=[vmem()] * 4,
        out_specs=vmem(),
        cost_estimate=brief(),
        compiler_params=params(8),
    )(own_back, swapped(other_back), encoded, spread)


def prefix(value, axis, join, neutral):
    count, mine = (lax.axis_size(axis), lax.axis_index(axis))
    pieces = jax.tree.map(lambda part: lax.all_gather(part, axis), value)
    so_far = jax.tree.map(
        lambda part, zero: jnp.full_like(part, 0) + jnp.asarray(zero, part.dtype), value, neutral
    )

    def lap(position, so_far):
        longer = join(so_far, jax.tree.map(lambda part: part[position], pieces))
        return jax.tree.map(lambda new, old: jnp.where(position < mine, new, old), longer, so_far)

    return lax.fori_loop(0, count - 1, lap, so_far)


def rms_scale(values, gain):
    values = values.astype(jnp.float32)
    return values * lax.rsqrt(jnp.mean(values * values, axis=-1, keepdims=True) + eps) * gain


def combine_pairs(earlier, later):
    return (earlier[0] * later[0], later[0] * earlier[1] + later[1])


def pick_table(table, wanted, seq_ids):
    return jnp.sum(jnp.where(seq_ids[None, :] == wanted[:, None], table[None, :], 0), axis=1)


def block_size(piece_rows, shard_rows):
    limit = max(1, 1024 // shard_rows)
    pieces = max(1, piece_rows // shard_rows)
    best_size = 1
    for candidate in range(1, limit + 1):
        if pieces % candidate == 0:
            best_size = candidate
    return min(piece_rows, best_size * shard_rows)


def spread_heads(
    byte_states,
    outer_gain,
    mamba_input,
    mamba_step,
    decay_rate,
    mixer_weight,
    boundaries,
    span_counts,
    up_weight,
    up_bias,
    inner_gain,
    query_weight,
    key_weight,
    value_weight,
    return_weight,
):
    shards = lax.axis_size("seq")
    own_shard = lax.axis_index("seq")
    own_lane = lax.axis_index("mp")
    rows_here = byte_states.shape[0]
    capacity = boundaries.shape[1]
    column_count = mamba_input.shape[1]
    kv_local = key_weight.shape[1] // HEAD
    group_size = HEADS // KV_HEADS
    slot_count = capacity // shards
    offsets = jnp.cumsum(span_counts) - span_counts
    seq_ids = jnp.arange(shards, dtype=jnp.int32)
    own_offset = jnp.sum(jnp.where(seq_ids == own_shard, offsets, 0))
    own_count = jnp.sum(jnp.where(seq_ids == own_shard, span_counts, 0))
    normed = rms_scale(byte_states, outer_gain).astype(jnp.bfloat16)
    inputs = jnp.dot(normed, mamba_input, preferred_element_type=jnp.float32)
    step_sizes = jax.nn.softplus(jnp.dot(normed, mamba_step, preferred_element_type=jnp.float32))
    rate_steps = step_sizes * decay_rate
    decays = jnp.exp(-rate_steps)
    drives = jnp.sqrt(-jnp.expm1(-2.0 * rate_steps)) * inputs
    through, local_states = lax.associative_scan(combine_pairs, (decays, drives), axis=0)
    starting = (jnp.ones((column_count,), jnp.float32), jnp.zeros((column_count,), jnp.float32))
    arriving = prefix((through[-1], local_states[-1]), "seq", combine_pairs, starting)
    states = (local_states + through * arriving[1][None, :]).astype(jnp.bfloat16)
    partial_value = jnp.dot(states, mixer_weight, preferred_element_type=jnp.float32)
    mixed_sum = lax.psum(partial_value, "mp")
    encoded = (byte_states.astype(jnp.float32) + mixed_sum).astype(jnp.bfloat16)
    skip_part = lax.dynamic_slice_in_dim(encoded, own_lane * column_count, column_count, 1)
    own_marks = boundaries[0]
    pooled = encoded[jnp.minimum(own_marks, rows_here - 1)]
    row_width = pooled.shape[1]
    outgoing = jnp.roll(pooled.reshape(slot_count, shards, row_width), own_offset % shards, axis=1)
    incoming = lax.all_to_all(outgoing, "seq", split_axis=1, concat_axis=1, tiled=True)
    position = jnp.arange(CH_OWN, dtype=jnp.int32)
    span_index = own_shard + position * shards
    source = jnp.sum((offsets[None, :] <= span_index[:, None]).astype(jnp.int32), axis=1) - 1
    source_offset = pick_table(offsets, source, seq_ids)
    slot_index = (span_index - source_offset) // shards
    gathered_rows = incoming.reshape(slot_count * shards, row_width)[slot_index * shards + source]
    columns = gathered_rows
    widened_sum = jnp.dot(
        columns,
        lax.all_gather(up_weight, "seq", axis=0, tiled=True),
        preferred_element_type=jnp.float32,
    )
    widened_share = (widened_sum + up_bias[None, :]).astype(jnp.bfloat16)
    widened = lax.all_gather(widened_share, "mp", axis=1, tiled=True)
    inner_normed = rms_scale(widened, inner_gain).astype(jnp.bfloat16)
    columns = inner_normed
    query_part = jnp.dot(
        columns,
        lax.all_gather(query_weight, "seq", axis=0, tiled=True),
        preferred_element_type=jnp.float32,
    )
    key_part = jnp.dot(
        columns,
        lax.all_gather(key_weight, "seq", axis=0, tiled=True),
        preferred_element_type=jnp.float32,
    )
    value_part = jnp.dot(
        columns,
        lax.all_gather(value_weight, "seq", axis=0, tiled=True),
        preferred_element_type=jnp.float32,
    )
    queries = query_part.astype(jnp.bfloat16)
    key_rows = key_part.astype(jnp.bfloat16)
    value_rows = value_part.astype(jnp.bfloat16)
    query_count = queries.shape[0]
    grouped = (
        queries.reshape(query_count, kv_local, group_size, HEAD)
        .transpose(1, 0, 2, 3)
        .reshape(kv_local, query_count * group_size, HEAD)
    )
    row_index = jnp.repeat(span_index, group_size)
    shard_rows = key_rows.shape[0]
    score_scale = 1.0 / math.sqrt(HEAD)

    def key_index(whole_index):
        return whole_index // shard_rows + whole_index % shard_rows * shards

    def attend_block(running, key_block, value_block, index_block):
        row_peak, denominator, weighted = running
        scores = (
            jnp.einsum("hqd,khd->hqk", grouped, key_block, preferred_element_type=jnp.float32)
            * score_scale
        )
        scores = jnp.where(index_block[None, None, :] <= row_index[None, :, None], scores, masked)
        new_peak = jnp.maximum(row_peak, jnp.max(scores, axis=2))
        shrink = jnp.exp(row_peak - new_peak)
        lifted = jnp.exp(scores - new_peak[:, :, None])
        denominator = denominator * shrink + jnp.sum(lifted, axis=2)
        weighted = weighted * shrink[:, :, None] + jnp.einsum(
            "hqk,khd->hqd",
            lifted.astype(jnp.bfloat16),
            value_block,
            preferred_element_type=jnp.float32,
        )
        return (new_peak, denominator, weighted)

    query_total = query_count * group_size
    initial = (
        jnp.full((kv_local, query_total), masked, jnp.float32),
        jnp.zeros((kv_local, query_total), jnp.float32),
        jnp.zeros((kv_local, query_total, HEAD), jnp.float32),
    )
    key_piece = lax.all_gather(key_rows, "seq", axis=0, tiled=True)
    value_piece = lax.all_gather(value_rows, "seq", axis=0, tiled=True)
    piece_rows = key_piece.shape[0]
    block_rows = block_size(piece_rows, shard_rows)
    turn_count = piece_rows // block_rows
    key_blocks = key_piece.reshape(turn_count, block_rows, kv_local, HEAD)
    value_blocks = value_piece.reshape(turn_count, block_rows, kv_local, HEAD)

    def one_turn(turn_index, inner_running):
        whole_index = turn_index * block_rows + jnp.arange(block_rows, dtype=jnp.int32)
        return attend_block(
            inner_running, key_blocks[turn_index], value_blocks[turn_index], key_index(whole_index)
        )

    row_peak, denominator, weighted = lax.fori_loop(0, turn_count, one_turn, initial)
    attended = (weighted / denominator[:, :, None]).astype(jnp.bfloat16)
    attended = (
        attended.reshape(kv_local, query_count, group_size, HEAD)
        .transpose(1, 0, 2, 3)
        .reshape(query_count, kv_local * group_size * HEAD)
    )
    projected = jnp.dot(attended, return_weight, preferred_element_type=jnp.float32)
    returned = lax.psum_scatter(
        projected.astype(jnp.bfloat16), "mp", scatter_dimension=1, tiled=True
    )
    slot_ids = jnp.arange(slot_count, dtype=jnp.int32)
    lead_slot = (own_shard - offsets) % shards
    local_span = slot_ids[:, None] * shards + lead_slot[None, :]
    back_index = (offsets[None, :] + local_span - own_shard) // shards
    alive = local_span < span_counts[None, :]
    back_rows = jnp.where(
        alive[:, :, None],
        returned[jnp.clip(back_index, 0, CH_OWN - 1)],
        jnp.zeros((), jnp.bfloat16),
    )
    arrived = lax.all_to_all(back_rows, "seq", split_axis=1, concat_axis=1, tiled=True)
    span_results = jnp.roll(arrived, -(own_offset % shards), axis=1).reshape(capacity, column_count)
    positions = jnp.arange(rows_here, dtype=jnp.int32)
    live_slots = jnp.arange(capacity, dtype=jnp.int32) < own_count
    passed = jnp.sum(
        ((own_marks[None, :] <= positions[:, None]) & live_slots[None, :]).astype(jnp.int32), axis=1
    )
    return (skip_part.astype(jnp.float32) + span_results[passed - 1].astype(jnp.float32)).astype(
        jnp.bfloat16
    )


def solution(mesh):
    in_specs = (
        P("seq", None),
        P(),
        P(None, "mp"),
        P(None, "mp"),
        P("mp"),
        P("mp", None),
        P("seq", None),
        P(),
        P("seq", "mp"),
        P("mp"),
        P(),
        P("seq", "mp"),
        P("seq", "mp"),
        P("seq", "mp"),
        P("mp", None),
    )
    out_specs = P("seq", "mp")
    def on_device(*arrays):
        heads_here = arrays[11].shape[1] // HEAD
        fits = heads_here == mesh.shape["seq"] and mesh.shape["mp"] == 2
        return (one_head_each if fits else spread_heads)(*arrays)

    return jax.shard_map(
        on_device, mesh=mesh, in_specs=in_specs, out_specs=out_specs, check_vma=False
    )
```

```python
import functools
import math

import jax
import jax.numpy as jnp
from jax import lax
from jax.experimental import pallas as pl
from jax.experimental.pallas import tpu as pltpu
from jax.sharding import PartitionSpec as P

HEADS = 32
KV_HEADS = 8
HEAD = 128
CH_OWN = 64


eps = 1e-05
masked = -1e30
TILE = 16


def swapped(value):
    return lax.ppermute(value, "mp", [(0, 1), (1, 0)])


def vmem():
    return pl.BlockSpec(memory_space=pltpu.VMEM)


def smem():
    return pl.BlockSpec(memory_space=pltpu.SMEM)


def in_place():
    return pl.BlockSpec(memory_space=pl.ANY)


def in_hbm():
    return pl.BlockSpec(memory_space=pltpu.HBM)


def seat():
    return lax.axis_index("seq"), lax.axis_index("mp")


def params(mebibytes=24):
    return pltpu.CompilerParams(vmem_limit_bytes=mebibytes * 2**20)


def brief():
    return pl.CostEstimate(flops=1, bytes_accessed=1, transcendentals=0)


def lanes(which, size):
    return pl.ds(pl.multiple_of(which * size, size), size)


def rows_at(which, size):
    return pl.ds(pl.multiple_of(which * size, size), size)


def start_all(pairs, sems):
    copies = []
    for index, (from_ref, to_ref) in enumerate(pairs):
        copy = pltpu.make_async_copy(from_ref, to_ref, sems.at[index])
        copy.start()
        copies.append(copy)
    return copies


def copy_all(pairs, sems):
    for copy in start_all(pairs, sems):
        copy.wait()


def one_minus_exp(u):
    series = jnp.ones_like(u)
    for order in range(9, 1, -1):
        series = 1.0 - u * (1.0 / order) * series
    return jnp.where(u < 0.5, u * series, 1.0 - jnp.exp(-u))


def softplus(v):
    tail = jnp.exp(-jnp.abs(v))
    series = jnp.ones_like(tail)
    for order in range(6, 1, -1):
        series = 1.0 - tail * ((order - 1.0) / order) * series
    return jnp.maximum(v, 0.0) + jnp.where(tail < 0.03, tail * series, jnp.log(1.0 + tail))


def start_cuts(plane, query_ref, key_ref, value_ref, pair_outs, sems):
    layers = len(pair_outs)
    me, _ = seat()
    layer = me // plane
    group = plane * HEAD
    pairs = []
    for step, out_ref in enumerate(pair_outs):
        target = layer ^ step
        pairs.append((query_ref.at[:, lanes(target, group)], out_ref.at[:, pl.ds(0, group)]))
        pairs.append((key_ref.at[:, lanes(target, HEAD)], out_ref.at[:, pl.ds(group, HEAD)]))
        pairs.append(
            (value_ref.at[:, lanes(target, HEAD)], out_ref.at[:, pl.ds(group + HEAD, HEAD)])
        )
    return start_all(pairs, sems)


def scan_kernel(plane, layers, *refs):
    bytes_hbm, gain_ref, input_hbm, step_hbm, rate_ref = refs[:5]
    others, refs = refs[5:8], refs[8:]
    local_ref, through_ref, ends_ref = refs[:3]
    pair_outs, refs = refs[3 : 3 + layers], refs[3 + layers :]
    bytes_ref, input_ref, step_ref, *held, sems, cut_sems = refs
    fetches = start_all(
        [(bytes_hbm, bytes_ref), (step_hbm, step_ref), (input_hbm, input_ref), *zip(others, held)],
        sems,
    )
    fetches[0].wait()
    values = bytes_ref[...].astype(jnp.float32)
    scale = lax.rsqrt(jnp.mean(values * values, axis=1, keepdims=True) + eps)
    normed = (values * scale * gain_ref[...]).astype(jnp.bfloat16)
    fetches[1].wait()
    steps = softplus(jnp.dot(normed, step_ref[...], preferred_element_type=jnp.float32))
    rate_steps = steps * rate_ref[...]
    fetches[2].wait()
    inputs = jnp.dot(normed, input_ref[...], preferred_element_type=jnp.float32)
    for fetch in fetches[3:]:
        fetch.wait()
    cuts = start_cuts(plane, *held, pair_outs, cut_sems)
    decays = jnp.exp(-rate_steps)
    drives = jnp.sqrt(one_minus_exp(2.0 * rate_steps)) * inputs
    rows, width = decays.shape
    tile = 8
    decays = decays.reshape(rows // tile, tile, width)
    drives = drives.reshape(rows // tile, tile, width)
    place = lax.broadcasted_iota(jnp.int32, decays.shape, 1)
    for reach in (1, 2, 4):
        before_decays = pltpu.roll(decays, reach, 1)
        before_drives = pltpu.roll(drives, reach, 1)
        inside = place >= reach
        drives = jnp.where(inside, decays * before_drives + drives, drives)
        decays = jnp.where(inside, decays * before_decays, decays)
    state = jnp.zeros((1, width), jnp.float32)
    kept = jnp.ones((1, width), jnp.float32)
    for index in range(rows // tile):
        states = decays[index] * state + drives[index]
        passing = decays[index] * kept
        local_ref[pl.ds(index * tile, tile), :] = states
        through_ref[pl.ds(index * tile, tile), :] = passing
        state = states[tile - 1 :, :]
        kept = passing[tile - 1 :, :]
    for index in range(ends_ref.shape[0]):
        ends_ref[index, 0:1, :] = kept
        ends_ref[index, 1:2, :] = state
    for cut in cuts:
        cut.wait()


def states_kernel(local_ref, through_ref, mixer_ref, ends_ref, states_ref, other_ref):
    me, lane = seat()
    carry = jnp.zeros((1, local_ref.shape[1]), jnp.float32)
    for shard in range(ends_ref.shape[0]):
        later = ends_ref[shard, 0:1, :] * carry + ends_ref[shard, 1:2, :]
        carry = jnp.where(shard < me, later, carry)
    states = (local_ref[...] + through_ref[...] * carry).astype(jnp.bfloat16)
    states_ref[...] = states
    half = other_ref.shape[1]
    other_ref[...] = jnp.dot(
        states, mixer_ref[:, lanes(1 - lane, half)], preferred_element_type=jnp.float32
    )


def pool_kernel(plane, *refs):
    states_ref, mixer_ref, other_ref, bytes_ref, pick_ref = refs[:5]
    layers = len(refs) - 8 - plane
    up_pieces, (encoded_ref, out_ref, *up_refs, sems) = refs[5 : 5 + layers], refs[5 + layers :]
    cross = lax.rem(seat()[0], plane)
    pairs = []
    for mask, up_ref in enumerate(up_refs):
        size = 2 * up_ref.shape[2] // layers
        for step, piece in enumerate(up_pieces):
            for number in range(layers // 2):
                columns = lanes(number * plane + (cross ^ mask), size)
                pairs.append((piece.at[:, columns], up_ref.at[step, :, pl.ds(number * size, size)]))
    copies = start_all(pairs, sems)
    half = other_ref.shape[1]
    columns = lanes(seat()[1], half)
    mixed = jnp.dot(states_ref[...], mixer_ref[:, columns], preferred_element_type=jnp.float32)
    skip = bytes_ref[:, columns].astype(jnp.float32)
    encoded = (skip + (mixed + other_ref[...])).astype(jnp.bfloat16)
    encoded_ref[...] = encoded
    picked = jnp.dot(pick_ref[...], encoded, preferred_element_type=jnp.float32)
    out_ref[...] = picked.astype(jnp.bfloat16).reshape(out_ref.shape)
    for copy in copies:
        copy.wait()


def own_kernel(pick_ref, arrived_ref, out_ref):
    shards, slots, half = arrived_ref.shape
    rows = arrived_ref[...].astype(jnp.float32).reshape(shards * slots, half)
    own = jnp.dot(
        pick_ref[...], rows.astype(jnp.bfloat16), preferred_element_type=jnp.float32
    ).astype(jnp.bfloat16)
    for index in range(out_ref.shape[0]):
        out_ref[index] = own


def assemble_kernel(plane, layers, *refs):
    up_own, refs = refs[:plane], refs[plane:]
    up_far, refs = refs[:plane], refs[plane:]
    pieces, (up_ref, weights_ref, sems) = refs[:layers], refs[layers:]
    me, lane = seat()
    layer, cross = me // plane, lax.rem(me, plane)
    up_rows, up_half = up_own[0].shape[1:]
    pairs = []
    for step in range(layers):
        for mask in range(plane):
            where = rows_at((layer ^ step) * plane + (cross ^ mask), up_rows)
            pairs.append((up_own[mask].at[step], up_ref.at[where, lanes(lane, up_half)]))
            pairs.append((up_far[mask].at[step], up_ref.at[where, lanes(1 - lane, up_half)]))
    for step, piece in enumerate(pieces):
        pairs.append((piece, weights_ref.at[rows_at(layer ^ step, piece.shape[0]), :]))
    copy_all(pairs, sems)


def inner_kernel(
    plane, bias_ref, gain_ref, near_ref, far_ref, up, weights, out_ref, squares
):
    lane = seat()[1]
    rows, half = near_ref.shape
    block = rows // plane
    ones = jnp.ones((8, up.shape[1]), jnp.bfloat16)
    for index in range(plane):
        where = pl.ds(index * block, block)
        widened = jnp.dot(
            near_ref[where, :], up[rows_at(lane, half), :], preferred_element_type=jnp.float32
        ) + jnp.dot(
            far_ref[where, :], up[rows_at(1 - lane, half), :], preferred_element_type=jnp.float32
        )
        widened = (widened + bias_ref[...]).astype(jnp.bfloat16).astype(jnp.float32)
        inner = (widened * gain_ref[...]).astype(jnp.bfloat16)
        square = widened * widened
        coarse = square.astype(jnp.bfloat16)
        fine = (square - coarse.astype(jnp.float32)).astype(jnp.bfloat16)
        squares[:, where] = sum(
            lax.dot_general(
                ones, part, (((1,), (1,)), ((), ())), preferred_element_type=jnp.float32
            )
            for part in (coarse, fine)
        )
        sums = jnp.dot(inner, weights[...], preferred_element_type=jnp.float32)
        sums = sums.astype(jnp.bfloat16)
        for head in range(plane):
            out_ref[head, where, :] = sums[:, head * HEAD : (head + 1) * HEAD]
        for number in range(2):
            start = (plane + number) * HEAD
            out_ref[index, pl.ds(rows + number * block, block), :] = sums[:, start : start + HEAD]
    total = jnp.concatenate(
        [squares[0:1, start : start + HEAD] for start in range(0, rows, HEAD)], axis=0
    )
    coarse = total.astype(jnp.bfloat16).astype(jnp.float32)
    both = jnp.concatenate([coarse, total - coarse], axis=0).astype(jnp.bfloat16)
    for index in range(plane):
        out_ref[index, pl.ds(rows + 2 * block, both.shape[0]), :] = both


def heads_kernel(features, got_ref, query_ref, pair_ref, queries):
    plane = got_ref.shape[0]
    rows = query_ref.shape[0]
    block = rows // plane
    lines = rows // HEAD
    shards = rows // CH_OWN
    layers = shards // plane
    first = rows + 2 * block

    def added(start, size):
        parts = [got_ref[index, start : start + size, :].astype(jnp.float32) for index in range(plane)]
        return sum(parts[1:], parts[0])

    both = added(first, 2 * lines)
    total = both[:lines, :] + both[lines:, :]
    scale = jnp.transpose(lax.rsqrt(total * (1.0 / features) + eps))
    for line in range(lines):
        scaled = added(line * HEAD, HEAD) * scale[:, line : line + 1]
        for start in range(0, HEAD, CH_OWN):
            index = (line * HEAD + start) // CH_OWN
            shard = (index % layers) * plane + index // layers
            queries[pl.ds(shard, CH_OWN, stride=shards), :] = scaled[start : start + CH_OWN, :]
    query_ref[...] = queries[...].astype(jnp.bfloat16)
    cross = lax.rem(seat()[0], plane)
    per_block = block // HEAD
    for line in range(per_block):
        mine = scale[:, line : line + 1]
        for index in range(1, plane):
            column = index * per_block + line
            mine = jnp.where(cross == index, scale[:, column : column + 1], mine)
        for number in range(2):
            start = number * block + line * HEAD
            pair = (added(rows + start, HEAD) * mine).astype(jnp.bfloat16)
            for index in range(plane):
                pair_ref[index, pl.ds(start, HEAD), :] = pair


def attend_kernel(place_ref, query_ref, pair_ref, out_ref, natural, keys, values, attended):
    rows = query_ref.shape[0]
    window = out_ref.shape[1]
    plane = pair_ref.shape[0]
    part = rows // plane
    shards = rows // CH_OWN
    layers = shards // plane
    for number, held in enumerate((keys, values)):
        for cross in range(plane):
            for layer in range(layers):
                piece = pair_ref[cross, pl.ds(number * part + layer * CH_OWN, CH_OWN), :]
                where = pl.ds(layer * plane + cross, CH_OWN, stride=shards)
                natural[where, :] = piece.astype(jnp.float32)
        held[...] = natural[...].astype(jnp.bfloat16)
    block = min(256, rows)
    score_scale = 1.0 / math.sqrt(HEAD)
    for start in range(0, rows, block):
        stop = start + block
        scores = lax.dot_general(
            query_ref[start:stop, :],
            keys[0:stop, :],
            (((1,), (1,)), ((), ())),
            preferred_element_type=jnp.float32,
        )
        spots = lax.broadcasted_iota(jnp.int32, scores.shape, 1)
        mine = lax.broadcasted_iota(jnp.int32, scores.shape, 0) + start
        scores = jnp.where(spots <= mine, scores * score_scale, masked)
        peak = jnp.max(scores, axis=1, keepdims=True)
        lifted = jnp.exp(scores - peak)
        denominator = jnp.sum(lifted, axis=1, keepdims=True)
        weighted = jnp.dot(
            lifted.astype(jnp.bfloat16), values[0:stop, :], preferred_element_type=jnp.float32
        )
        attended[start:stop, :] = (weighted / denominator).astype(jnp.bfloat16)
    attended[rows:, :] = jnp.zeros((attended.shape[0] - rows, HEAD), jnp.bfloat16)
    for shard in range(out_ref.shape[0]):
        first = place_ref[shard]
        out_ref[shard] = attended[pl.ds(pl.multiple_of(first * TILE, TILE), window), :]


def return_kernel(weight_ref, pieces_ref, own_ref, other_ref, attended):
    half = own_ref.shape[1]
    lane = seat()[1]
    for head in range(pieces_ref.shape[0]):
        attended[:, head * HEAD : (head + 1) * HEAD] = pieces_ref[head]
    other_ref[...] = jnp.dot(
        attended[...], weight_ref[:, lanes(1 - lane, half)], preferred_element_type=jnp.float32
    )
    own_ref[...] = jnp.dot(
        attended[...], weight_ref[:, lanes(lane, half)], preferred_element_type=jnp.float32
    )


def join_kernel(own_ref, other_ref, encoded_ref, spread_ref, out_ref):
    returned = (own_ref[...] + other_ref[...]).astype(jnp.bfloat16)
    results = jnp.dot(spread_ref[...], returned, preferred_element_type=jnp.float32)
    out_ref[...] = (encoded_ref[...].astype(jnp.float32) + results).astype(jnp.bfloat16)


def one_head_each(
    byte_states,
    outer_gain,
    mamba_input,
    mamba_step,
    decay_rate,
    mixer_weight,
    boundaries,
    span_counts,
    up_weight,
    up_bias,
    inner_gain,
    query_weight,
    key_weight,
    value_weight,
    return_weight,
):
    shards = lax.axis_size("seq")
    me = lax.axis_index("seq")
    lane = lax.axis_index("mp")
    plane = HEADS // KV_HEADS
    layers = shards // plane
    rows_here, width = byte_states.shape
    half = mamba_input.shape[1]
    capacity = boundaries.shape[1]
    window = capacity + TILE
    total_rows = CH_OWN * shards
    inner_width = inner_gain.shape[0]
    inner_half = up_bias.shape[0]
    weight_rows = query_weight.shape[0]
    f32, bf16 = jnp.float32, jnp.bfloat16
    layer, cross = me // plane, me % plane
    layer_groups = [[first + plane * step for step in range(layers)] for first in range(plane)]
    plane_groups = [[first * plane + step for step in range(plane)] for first in range(layers)]

    def over(value, mask):
        return lax.ppermute(value, "seq", [(i, i ^ mask) for i in range(shards)])

    def after(value, done):
        return lax.optimization_barrier((value, done))[0]

    own_bias = up_bias.reshape(layers // 2, plane, weight_rows)
    own_bias = lax.dynamic_index_in_dim(own_bias, cross, 1, keepdims=False).reshape(1, -1)
    own_gain = inner_gain.reshape(layers, plane, weight_rows)
    own_gain = lax.dynamic_index_in_dim(own_gain, cross, 1, keepdims=False).reshape(1, -1)

    seq_ids = jnp.arange(shards, dtype=jnp.int32)
    offsets = jnp.cumsum(span_counts) - span_counts
    own_offset = jnp.sum(jnp.where(seq_ids == me, offsets, 0))
    own_count = jnp.sum(jnp.where(seq_ids == me, span_counts, 0))
    place = offsets // TILE
    own_marks = boundaries[0]
    positions = jnp.arange(rows_here, dtype=jnp.int32)
    spans_here = jnp.arange(capacity, dtype=jnp.int32)
    live = spans_here < own_count
    slots = capacity // shards
    slot_ids = jnp.arange(slots, dtype=jnp.int32)
    local_span = slot_ids[None, :] * shards + ((seq_ids - own_offset) % shards)[:, None]
    is_span = spans_here[None, :] == local_span.reshape(-1)[:, None]
    byte_at = jnp.sum(jnp.where(is_span, jnp.minimum(own_marks, rows_here - 1)[None, :], 0), axis=1)
    pool_pick = (positions[None, :] == byte_at[:, None]).astype(bf16)
    own_spans = me + jnp.arange(CH_OWN, dtype=jnp.int32) * shards
    origin = jnp.sum((offsets[None, :] <= own_spans[:, None]).astype(jnp.int32), axis=1) - 1
    origin_offset = jnp.sum(
        jnp.where(seq_ids[None, :] == origin[:, None], offsets[None, :], 0), axis=1
    )
    arrived_row = origin * slots + (own_spans - origin_offset) // shards
    own_pick = (
        jnp.arange(shards * slots, dtype=jnp.int32)[None, :] == arrived_row[:, None]
    ).astype(bf16)
    passed = jnp.sum(
        ((own_marks[None, :] <= positions[:, None]) & live[None, :]).astype(jnp.int32), axis=1
    )
    result_row = passed - 1 + own_offset % TILE
    spread = (jnp.arange(window, dtype=jnp.int32)[None, :] == result_row[:, None]).astype(bf16)

    up_half = inner_half // plane
    up_layers = [up_weight]
    for bit in range(layers.bit_length() - 2, -1, -1):
        up_layers += [over(piece, plane << bit) for piece in up_layers]
    order = [0]
    for bit in range(layers.bit_length() - 2, -1, -1):
        order += [step ^ (1 << bit) for step in order]
    up_layers = [up_layers[order.index(step)] for step in range(layers)]

    local, through, ends, *pair_cuts = pl.pallas_call(
        functools.partial(scan_kernel, plane, layers),
        out_shape=(
            jax.ShapeDtypeStruct((rows_here, half), f32),
            jax.ShapeDtypeStruct((rows_here, half), f32),
            jax.ShapeDtypeStruct((shards, 2, half), f32),
        )
        + (jax.ShapeDtypeStruct((weight_rows, (plane + 2) * HEAD), bf16),) * layers,
        in_specs=[in_hbm(), vmem(), in_hbm(), in_hbm(), vmem()] + [in_hbm()] * 3,
        out_specs=(vmem(),) * 3 + (in_place(),) * layers,
        scratch_shapes=[
            pltpu.VMEM(array.shape, bf16)
            for array in (
                byte_states,
                mamba_input,
                mamba_step,
                query_weight,
                key_weight,
                value_weight,
            )
        ]
        + [pltpu.SemaphoreType.DMA((6,)), pltpu.SemaphoreType.DMA((3 * layers,))],
        cost_estimate=brief(),
        compiler_params=params(16),
    )(
        byte_states,
        outer_gain[None, :],
        mamba_input,
        mamba_step,
        decay_rate[None, :],
        query_weight,
        key_weight,
        value_weight,
    )
    ends = lax.all_to_all(ends, "seq", 0, 0, tiled=True)
    pair_cuts = lax.optimization_barrier((pair_cuts, up_layers[layers // 2]))[0]
    ends, up_layers = lax.optimization_barrier((ends, up_layers))
    pieces = [pair_cuts[0]] + [over(pair_cuts[step], plane * step) for step in range(1, layers)]
    states, other_part = pl.pallas_call(
        states_kernel,
        out_shape=(
            jax.ShapeDtypeStruct((rows_here, half), bf16),
            jax.ShapeDtypeStruct((rows_here, half), f32),
        ),
        in_specs=[vmem()] * 4,
        out_specs=(vmem(),) * 2,
        cost_estimate=brief(),
        compiler_params=params(8),
    )(local, through, mixer_weight, ends)
    far_bias = swapped(own_bias)
    bias = jnp.where(
        lane == 0,
        jnp.concatenate([own_bias, far_bias], axis=1),
        jnp.concatenate([far_bias, own_bias], axis=1),
    )
    far_part, bias, pieces[1] = lax.optimization_barrier((swapped(other_part), bias, pieces[1]))
    encoded, leaving, *up_cuts = pl.pallas_call(
        functools.partial(pool_kernel, plane),
        out_shape=(
            jax.ShapeDtypeStruct((rows_here, half), bf16),
            jax.ShapeDtypeStruct((shards, slots, half), bf16),
        )
        + (jax.ShapeDtypeStruct((layers, up_weight.shape[0], up_half), bf16),) * plane,
        in_specs=[vmem()] * 5 + [in_place()] * layers,
        out_specs=(vmem(),) * (2 + plane),
        scratch_shapes=[pltpu.SemaphoreType.DMA((plane * layers * layers // 2,))],
        cost_estimate=brief(),
        compiler_params=params(10),
    )(states, mixer_weight, far_part, byte_states, pool_pick, *up_layers)
    arrived = lax.all_to_all(leaving, "seq", 0, 0, tiled=True)
    up_own = [up_cuts[0]] + [over(up_cuts[mask], mask) for mask in range(1, plane)]
    arrived, pieces = lax.optimization_barrier((arrived, pieces))
    own_rows = pl.pallas_call(
        own_kernel,
        out_shape=jax.ShapeDtypeStruct((layers, CH_OWN, half), bf16),
        in_specs=[vmem()] * 2,
        out_specs=vmem(),
        cost_estimate=brief(),
        compiler_params=params(8),
    )(own_pick, arrived)
    near_layer = lax.all_to_all(
        own_rows, "seq", 0, 0, axis_index_groups=layer_groups, tiled=True
    )
    features = own_gain.shape[1]
    up_far = [swapped(piece) for piece in up_own]
    up_all, weights = pl.pallas_call(
        functools.partial(assemble_kernel, plane, layers),
        out_shape=(
            jax.ShapeDtypeStruct((width, features), bf16),
            jax.ShapeDtypeStruct((features, (plane + 2) * HEAD), bf16),
        ),
        in_specs=[in_place()] * (2 * plane + layers),
        out_specs=(vmem(),) * 2,
        scratch_shapes=[pltpu.SemaphoreType.DMA((2 * shards + layers,))],
        cost_estimate=brief(),
        compiler_params=params(8),
    )(*up_own, *up_far, *pieces)
    near_layer, up_all, weights = lax.optimization_barrier((near_layer, up_all, weights))
    near = lax.all_to_all(
        jnp.broadcast_to(near_layer[None], (plane, layers, CH_OWN, half)),
        "seq",
        0,
        0,
        axis_index_groups=plane_groups,
        tiled=True,
    ).reshape(total_rows, half)

    block = total_rows // plane
    sent_rows = total_rows + 2 * block + 2 * (total_rows // HEAD)
    partial_sums = pl.pallas_call(
        functools.partial(inner_kernel, plane),
        out_shape=jax.ShapeDtypeStruct((plane, sent_rows, HEAD), bf16),
        in_specs=[vmem()] * 6,
        out_specs=vmem(),
        scratch_shapes=[pltpu.VMEM((8, total_rows), f32)],
        cost_estimate=brief(),
        compiler_params=params(18),
    )(bias, own_gain, near, swapped(near), up_all, weights)
    got = lax.all_to_all(
        partial_sums, "seq", 0, 0, axis_index_groups=plane_groups, tiled=True
    )
    queries, pairs = pl.pallas_call(
        functools.partial(heads_kernel, inner_width),
        out_shape=(
            jax.ShapeDtypeStruct((total_rows, HEAD), bf16),
            jax.ShapeDtypeStruct((plane, 2 * block, HEAD), bf16),
        ),
        in_specs=[vmem()],
        out_specs=(vmem(),) * 2,
        scratch_shapes=[pltpu.VMEM((total_rows, HEAD), f32)],
        cost_estimate=brief(),
        compiler_params=params(10),
    )(got)
    pairs = lax.all_to_all(pairs, "seq", 0, 0, axis_index_groups=plane_groups, tiled=True)
    leaving = pl.pallas_call(
        attend_kernel,
        out_shape=jax.ShapeDtypeStruct((shards, window, HEAD), bf16),
        in_specs=[smem()] + [vmem()] * 2,
        out_specs=vmem(),
        scratch_shapes=[
            pltpu.VMEM((total_rows, HEAD), f32),
            pltpu.VMEM((total_rows, HEAD), bf16),
            pltpu.VMEM((total_rows, HEAD), bf16),
            pltpu.VMEM((total_rows + window, HEAD), bf16),
        ],
        cost_estimate=brief(),
        compiler_params=params(12),
    )(place, queries, pairs)
    pieces = lax.all_to_all(leaving, "seq", 0, 0, tiled=True)
    own_back, other_back = pl.pallas_call(
        return_kernel,
        out_shape=(jax.ShapeDtypeStruct((window, half), f32),) * 2,
        in_specs=[vmem()] * 2,
        out_specs=(vmem(),) * 2,
        scratch_shapes=[pltpu.VMEM((window, shards * HEAD), bf16)],
        cost_estimate=brief(),
        compiler_params=params(12),
    )(return_weight, pieces)
    return pl.pallas_call(
        join_kernel,
        out_shape=jax.ShapeDtypeStruct((rows_here, half), bf16),
        in_specs=[vmem()] * 4,
        out_specs=vmem(),
        cost_estimate=brief(),
        compiler_params=params(8),
    )(own_back, swapped(other_back), encoded, spread)


def prefix(value, axis, join, neutral):
    count, mine = (lax.axis_size(axis), lax.axis_index(axis))
    pieces = jax.tree.map(lambda part: lax.all_gather(part, axis), value)
    so_far = jax.tree.map(
        lambda part, zero: jnp.full_like(part, 0) + jnp.asarray(zero, part.dtype), value, neutral
    )

    def lap(position, so_far):
        longer = join(so_far, jax.tree.map(lambda part: part[position], pieces))
        return jax.tree.map(lambda new, old: jnp.where(position < mine, new, old), longer, so_far)

    return lax.fori_loop(0, count - 1, lap, so_far)


def rms_scale(values, gain):
    values = values.astype(jnp.float32)
    return values * lax.rsqrt(jnp.mean(values * values, axis=-1, keepdims=True) + eps) * gain


def combine_pairs(earlier, later):
    return (earlier[0] * later[0], later[0] * earlier[1] + later[1])


def pick_table(table, wanted, seq_ids):
    return jnp.sum(jnp.where(seq_ids[None, :] == wanted[:, None], table[None, :], 0), axis=1)


def block_size(piece_rows, shard_rows):
    limit = max(1, 1024 // shard_rows)
    pieces = max(1, piece_rows // shard_rows)
    best_size = 1
    for candidate in range(1, limit + 1):
        if pieces % candidate == 0:
            best_size = candidate
    return min(piece_rows, best_size * shard_rows)


def spread_heads(
    byte_states,
    outer_gain,
    mamba_input,
    mamba_step,
    decay_rate,
    mixer_weight,
    boundaries,
    span_counts,
    up_weight,
    up_bias,
    inner_gain,
    query_weight,
    key_weight,
    value_weight,
    return_weight,
):
    shards = lax.axis_size("seq")
    own_shard = lax.axis_index("seq")
    own_lane = lax.axis_index("mp")
    rows_here = byte_states.shape[0]
    capacity = boundaries.shape[1]
    column_count = mamba_input.shape[1]
    kv_local = key_weight.shape[1] // HEAD
    group_size = HEADS // KV_HEADS
    slot_count = capacity // shards
    offsets = jnp.cumsum(span_counts) - span_counts
    seq_ids = jnp.arange(shards, dtype=jnp.int32)
    own_offset = jnp.sum(jnp.where(seq_ids == own_shard, offsets, 0))
    own_count = jnp.sum(jnp.where(seq_ids == own_shard, span_counts, 0))
    normed = rms_scale(byte_states, outer_gain).astype(jnp.bfloat16)
    inputs = jnp.dot(normed, mamba_input, preferred_element_type=jnp.float32)
    step_sizes = jax.nn.softplus(jnp.dot(normed, mamba_step, preferred_element_type=jnp.float32))
    rate_steps = step_sizes * decay_rate
    decays = jnp.exp(-rate_steps)
    drives = jnp.sqrt(-jnp.expm1(-2.0 * rate_steps)) * inputs
    through, local_states = lax.associative_scan(combine_pairs, (decays, drives), axis=0)
    starting = (jnp.ones((column_count,), jnp.float32), jnp.zeros((column_count,), jnp.float32))
    arriving = prefix((through[-1], local_states[-1]), "seq", combine_pairs, starting)
    states = (local_states + through * arriving[1][None, :]).astype(jnp.bfloat16)
    partial_value = jnp.dot(states, mixer_weight, preferred_element_type=jnp.float32)
    mixed_sum = lax.psum(partial_value, "mp")
    encoded = (byte_states.astype(jnp.float32) + mixed_sum).astype(jnp.bfloat16)
    skip_part = lax.dynamic_slice_in_dim(encoded, own_lane * column_count, column_count, 1)
    own_marks = boundaries[0]
    pooled = encoded[jnp.minimum(own_marks, rows_here - 1)]
    row_width = pooled.shape[1]
    outgoing = jnp.roll(pooled.reshape(slot_count, shards, row_width), own_offset % shards, axis=1)
    incoming = lax.all_to_all(outgoing, "seq", split_axis=1, concat_axis=1, tiled=True)
    position = jnp.arange(CH_OWN, dtype=jnp.int32)
    span_index = own_shard + position * shards
    source = jnp.sum((offsets[None, :] <= span_index[:, None]).astype(jnp.int32), axis=1) - 1
    source_offset = pick_table(offsets, source, seq_ids)
    slot_index = (span_index - source_offset) // shards
    gathered_rows = incoming.reshape(slot_count * shards, row_width)[slot_index * shards + source]
    columns = gathered_rows
    widened_sum = jnp.dot(
        columns,
        lax.all_gather(up_weight, "seq", axis=0, tiled=True),
        preferred_element_type=jnp.float32,
    )
    widened_share = (widened_sum + up_bias[None, :]).astype(jnp.bfloat16)
    widened = lax.all_gather(widened_share, "mp", axis=1, tiled=True)
    inner_normed = rms_scale(widened, inner_gain).astype(jnp.bfloat16)
    columns = inner_normed
    query_part = jnp.dot(
        columns,
        lax.all_gather(query_weight, "seq", axis=0, tiled=True),
        preferred_element_type=jnp.float32,
    )
    key_part = jnp.dot(
        columns,
        lax.all_gather(key_weight, "seq", axis=0, tiled=True),
        preferred_element_type=jnp.float32,
    )
    value_part = jnp.dot(
        columns,
        lax.all_gather(value_weight, "seq", axis=0, tiled=True),
        preferred_element_type=jnp.float32,
    )
    queries = query_part.astype(jnp.bfloat16)
    key_rows = key_part.astype(jnp.bfloat16)
    value_rows = value_part.astype(jnp.bfloat16)
    query_count = queries.shape[0]
    grouped = (
        queries.reshape(query_count, kv_local, group_size, HEAD)
        .transpose(1, 0, 2, 3)
        .reshape(kv_local, query_count * group_size, HEAD)
    )
    row_index = jnp.repeat(span_index, group_size)
    shard_rows = key_rows.shape[0]
    score_scale = 1.0 / math.sqrt(HEAD)

    def key_index(whole_index):
        return whole_index // shard_rows + whole_index % shard_rows * shards

    def attend_block(running, key_block, value_block, index_block):
        row_peak, denominator, weighted = running
        scores = (
            jnp.einsum("hqd,khd->hqk", grouped, key_block, preferred_element_type=jnp.float32)
            * score_scale
        )
        scores = jnp.where(index_block[None, None, :] <= row_index[None, :, None], scores, masked)
        new_peak = jnp.maximum(row_peak, jnp.max(scores, axis=2))
        shrink = jnp.exp(row_peak - new_peak)
        lifted = jnp.exp(scores - new_peak[:, :, None])
        denominator = denominator * shrink + jnp.sum(lifted, axis=2)
        weighted = weighted * shrink[:, :, None] + jnp.einsum(
            "hqk,khd->hqd",
            lifted.astype(jnp.bfloat16),
            value_block,
            preferred_element_type=jnp.float32,
        )
        return (new_peak, denominator, weighted)

    query_total = query_count * group_size
    initial = (
        jnp.full((kv_local, query_total), masked, jnp.float32),
        jnp.zeros((kv_local, query_total), jnp.float32),
        jnp.zeros((kv_local, query_total, HEAD), jnp.float32),
    )
    key_piece = lax.all_gather(key_rows, "seq", axis=0, tiled=True)
    value_piece = lax.all_gather(value_rows, "seq", axis=0, tiled=True)
    piece_rows = key_piece.shape[0]
    block_rows = block_size(piece_rows, shard_rows)
    turn_count = piece_rows // block_rows
    key_blocks = key_piece.reshape(turn_count, block_rows, kv_local, HEAD)
    value_blocks = value_piece.reshape(turn_count, block_rows, kv_local, HEAD)

    def one_turn(turn_index, inner_running):
        whole_index = turn_index * block_rows + jnp.arange(block_rows, dtype=jnp.int32)
        return attend_block(
            inner_running, key_blocks[turn_index], value_blocks[turn_index], key_index(whole_index)
        )

    row_peak, denominator, weighted = lax.fori_loop(0, turn_count, one_turn, initial)
    attended = (weighted / denominator[:, :, None]).astype(jnp.bfloat16)
    attended = (
        attended.reshape(kv_local, query_count, group_size, HEAD)
        .transpose(1, 0, 2, 3)
        .reshape(query_count, kv_local * group_size * HEAD)
    )
    projected = jnp.dot(attended, return_weight, preferred_element_type=jnp.float32)
    returned = lax.psum_scatter(
        projected.astype(jnp.bfloat16), "mp", scatter_dimension=1, tiled=True
    )
    slot_ids = jnp.arange(slot_count, dtype=jnp.int32)
    lead_slot = (own_shard - offsets) % shards
    local_span = slot_ids[:, None] * shards + lead_slot[None, :]
    back_index = (offsets[None, :] + local_span - own_shard) // shards
    alive = local_span < span_counts[None, :]
    back_rows = jnp.where(
        alive[:, :, None],
        returned[jnp.clip(back_index, 0, CH_OWN - 1)],
        jnp.zeros((), jnp.bfloat16),
    )
    arrived = lax.all_to_all(back_rows, "seq", split_axis=1, concat_axis=1, tiled=True)
    span_results = jnp.roll(arrived, -(own_offset % shards), axis=1).reshape(capacity, column_count)
    positions = jnp.arange(rows_here, dtype=jnp.int32)
    live_slots = jnp.arange(capacity, dtype=jnp.int32) < own_count
    passed = jnp.sum(
        ((own_marks[None, :] <= positions[:, None]) & live_slots[None, :]).astype(jnp.int32), axis=1
    )
    return (skip_part.astype(jnp.float32) + span_results[passed - 1].astype(jnp.float32)).astype(
        jnp.bfloat16
    )


def solution(mesh):
    in_specs = (
        P("seq", None),
        P(),
        P(None, "mp"),
        P(None, "mp"),
        P("mp"),
        P("mp", None),
        P("seq", None),
        P(),
        P("seq", "mp"),
        P("mp"),
        P(),
        P("seq", "mp"),
        P("seq", "mp"),
        P("seq", "mp"),
        P("mp", None),
    )
    out_specs = P("seq", "mp")
    def on_device(*arrays):
        heads_here = arrays[11].shape[1] // HEAD
        fits = heads_here == mesh.shape["seq"] and mesh.shape["mp"] == 2
        return (one_head_each if fits else spread_heads)(*arrays)

    return jax.shard_map(
        on_device, mesh=mesh, in_specs=in_specs, out_specs=out_specs, check_vma=False
    )
```

```python
import functools
import math

import jax
import jax.numpy as jnp
from jax import lax
from jax.experimental import pallas as pl
from jax.experimental.pallas import tpu as pltpu
from jax.sharding import PartitionSpec as P

HEADS = 32
KV_HEADS = 8
HEAD = 128
CH_OWN = 64


eps = 1e-05
masked = -1e30
TILE = 16


def swapped(value):
    return lax.ppermute(value, "mp", [(0, 1), (1, 0)])


def vmem():
    return pl.BlockSpec(memory_space=pltpu.VMEM)


def smem():
    return pl.BlockSpec(memory_space=pltpu.SMEM)


def in_place():
    return pl.BlockSpec(memory_space=pl.ANY)


def in_hbm():
    return pl.BlockSpec(memory_space=pltpu.HBM)


def seat():
    return lax.axis_index("seq"), lax.axis_index("mp")


def params(mebibytes=24):
    return pltpu.CompilerParams(vmem_limit_bytes=mebibytes * 2**20)


def brief():
    return pl.CostEstimate(flops=1, bytes_accessed=1, transcendentals=0)


def lanes(which, size):
    return pl.ds(pl.multiple_of(which * size, size), size)


def rows_at(which, size):
    return pl.ds(pl.multiple_of(which * size, size), size)


def start_all(pairs, sems):
    copies = []
    for index, (from_ref, to_ref) in enumerate(pairs):
        copy = pltpu.make_async_copy(from_ref, to_ref, sems.at[index])
        copy.start()
        copies.append(copy)
    return copies


def copy_all(pairs, sems):
    for copy in start_all(pairs, sems):
        copy.wait()


def one_minus_exp(u):
    series = jnp.ones_like(u)
    for order in range(9, 1, -1):
        series = 1.0 - u * (1.0 / order) * series
    return jnp.where(u < 0.5, u * series, 1.0 - jnp.exp(-u))


def softplus(v):
    tail = jnp.exp(-jnp.abs(v))
    series = jnp.ones_like(tail)
    for order in range(6, 1, -1):
        series = 1.0 - tail * ((order - 1.0) / order) * series
    return jnp.maximum(v, 0.0) + jnp.where(tail < 0.03, tail * series, jnp.log(1.0 + tail))


def start_cuts(plane, query_ref, key_ref, value_ref, pair_outs, sems):
    layers = len(pair_outs)
    me, _ = seat()
    layer = me // plane
    group = plane * HEAD
    pairs = []
    for step, out_ref in enumerate(pair_outs):
        target = layer ^ step
        pairs.append((query_ref.at[:, lanes(target, group)], out_ref.at[:, pl.ds(0, group)]))
        pairs.append((key_ref.at[:, lanes(target, HEAD)], out_ref.at[:, pl.ds(group, HEAD)]))
        pairs.append(
            (value_ref.at[:, lanes(target, HEAD)], out_ref.at[:, pl.ds(group + HEAD, HEAD)])
        )
    return start_all(pairs, sems)


def scan_kernel(plane, layers, *refs):
    bytes_hbm, gain_ref, input_hbm, step_hbm, rate_ref = refs[:5]
    others, refs = refs[5:8], refs[8:]
    local_ref, through_ref, ends_ref = refs[:3]
    pair_outs, refs = refs[3 : 3 + layers], refs[3 + layers :]
    bytes_ref, input_ref, step_ref, *held, sems, cut_sems = refs
    fetches = start_all(
        [(bytes_hbm, bytes_ref), (step_hbm, step_ref), (input_hbm, input_ref), *zip(others, held)],
        sems,
    )
    fetches[0].wait()
    values = bytes_ref[...].astype(jnp.float32)
    scale = lax.rsqrt(jnp.mean(values * values, axis=1, keepdims=True) + eps)
    normed = (values * scale * gain_ref[...]).astype(jnp.bfloat16)
    fetches[1].wait()
    steps = softplus(jnp.dot(normed, step_ref[...], preferred_element_type=jnp.float32))
    rate_steps = steps * rate_ref[...]
    fetches[2].wait()
    inputs = jnp.dot(normed, input_ref[...], preferred_element_type=jnp.float32)
    for fetch in fetches[3:]:
        fetch.wait()
    cuts = start_cuts(plane, *held, pair_outs, cut_sems)
    decays = jnp.exp(-rate_steps)
    drives = jnp.sqrt(one_minus_exp(2.0 * rate_steps)) * inputs
    rows, width = decays.shape
    tile = 8
    decays = decays.reshape(rows // tile, tile, width)
    drives = drives.reshape(rows // tile, tile, width)
    place = lax.broadcasted_iota(jnp.int32, decays.shape, 1)
    for reach in (1, 2, 4):
        before_decays = pltpu.roll(decays, reach, 1)
        before_drives = pltpu.roll(drives, reach, 1)
        inside = place >= reach
        drives = jnp.where(inside, decays * before_drives + drives, drives)
        decays = jnp.where(inside, decays * before_decays, decays)
    state = jnp.zeros((1, width), jnp.float32)
    kept = jnp.ones((1, width), jnp.float32)
    for index in range(rows // tile):
        states = decays[index] * state + drives[index]
        passing = decays[index] * kept
        local_ref[pl.ds(index * tile, tile), :] = states
        through_ref[pl.ds(index * tile, tile), :] = passing
        state = states[tile - 1 :, :]
        kept = passing[tile - 1 :, :]
    for index in range(ends_ref.shape[0]):
        ends_ref[index, 0:1, :] = kept
        ends_ref[index, 1:2, :] = state
    for cut in cuts:
        cut.wait()


def states_kernel(local_ref, through_ref, mixer_ref, ends_ref, states_ref, other_ref):
    me, lane = seat()
    carry = jnp.zeros((1, local_ref.shape[1]), jnp.float32)
    for shard in range(ends_ref.shape[0]):
        later = ends_ref[shard, 0:1, :] * carry + ends_ref[shard, 1:2, :]
        carry = jnp.where(shard < me, later, carry)
    states = (local_ref[...] + through_ref[...] * carry).astype(jnp.bfloat16)
    states_ref[...] = states
    half = other_ref.shape[1]
    other_ref[...] = jnp.dot(
        states, mixer_ref[:, lanes(1 - lane, half)], preferred_element_type=jnp.float32
    )


def pool_kernel(plane, *refs):
    states_ref, mixer_ref, other_ref, bytes_ref, pick_ref = refs[:5]
    layers = len(refs) - 8 - plane
    up_pieces, (encoded_ref, out_ref, *up_refs, sems) = refs[5 : 5 + layers], refs[5 + layers :]
    cross = lax.rem(seat()[0], plane)
    pairs = []
    for mask, up_ref in enumerate(up_refs):
        size = 2 * up_ref.shape[2] // layers
        for step, piece in enumerate(up_pieces):
            for number in range(layers // 2):
                columns = lanes(number * plane + (cross ^ mask), size)
                pairs.append((piece.at[:, columns], up_ref.at[step, :, pl.ds(number * size, size)]))
    copies = start_all(pairs, sems)
    half = other_ref.shape[1]
    columns = lanes(seat()[1], half)
    mixed = jnp.dot(states_ref[...], mixer_ref[:, columns], preferred_element_type=jnp.float32)
    skip = bytes_ref[:, columns].astype(jnp.float32)
    encoded = (skip + (mixed + other_ref[...])).astype(jnp.bfloat16)
    encoded_ref[...] = encoded
    picked = jnp.dot(pick_ref[...], encoded, preferred_element_type=jnp.float32)
    out_ref[...] = picked.astype(jnp.bfloat16).reshape(out_ref.shape)
    for copy in copies:
        copy.wait()


def own_kernel(pick_ref, arrived_ref, out_ref):
    shards, slots, half = arrived_ref.shape
    rows = arrived_ref[...].astype(jnp.float32).reshape(shards * slots, half)
    own = jnp.dot(
        pick_ref[...], rows.astype(jnp.bfloat16), preferred_element_type=jnp.float32
    ).astype(jnp.bfloat16)
    for index in range(out_ref.shape[0]):
        out_ref[index] = own


def inner_kernel(plane, layers, bias_ref, gain_ref, near_ref, far_ref, *refs):
    up_own, refs = refs[:plane], refs[plane:]
    up_far, refs = refs[:plane], refs[plane:]
    pieces, refs = refs[:layers], refs[layers:]
    out_ref, pooled, up, weights, squares, sems = refs
    me, lane = seat()
    layer, cross = me // plane, lax.rem(me, plane)
    half = near_ref.shape[1]
    up_rows, up_half = up_own[0].shape[1:]
    pairs = [
        (near_ref, pooled.at[:, lanes(lane, half)]),
        (far_ref, pooled.at[:, lanes(1 - lane, half)]),
    ]
    for step in range(layers):
        for mask in range(plane):
            where = rows_at((layer ^ step) * plane + (cross ^ mask), up_rows)
            pairs.append((up_own[mask].at[step], up.at[where, lanes(lane, up_half)]))
            pairs.append((up_far[mask].at[step], up.at[where, lanes(1 - lane, up_half)]))
    for step, piece in enumerate(pieces):
        pairs.append((piece, weights.at[rows_at(layer ^ step, piece.shape[0]), :]))
    copies = start_all(pairs, sems)
    for copy in copies[:-layers]:
        copy.wait()
    rows = pooled.shape[0]
    block = rows // plane
    ones = jnp.ones((8, up.shape[1]), jnp.bfloat16)
    for index in range(plane):
        where = pl.ds(index * block, block)
        widened = jnp.dot(pooled[where, :], up[...], preferred_element_type=jnp.float32)
        widened = (widened + bias_ref[...]).astype(jnp.bfloat16).astype(jnp.float32)
        inner = (widened * gain_ref[...]).astype(jnp.bfloat16)
        square = widened * widened
        coarse = square.astype(jnp.bfloat16)
        fine = (square - coarse.astype(jnp.float32)).astype(jnp.bfloat16)
        squares[:, where] = sum(
            lax.dot_general(
                ones, part, (((1,), (1,)), ((), ())), preferred_element_type=jnp.float32
            )
            for part in (coarse, fine)
        )
        if index == 0:
            for copy in copies[-layers:]:
                copy.wait()
        sums = jnp.dot(inner, weights[...], preferred_element_type=jnp.float32)
        sums = sums.astype(jnp.bfloat16)
        for head in range(plane):
            out_ref[head, where, :] = sums[:, head * HEAD : (head + 1) * HEAD]
        for number in range(2):
            start = (plane + number) * HEAD
            out_ref[index, pl.ds(rows + number * block, block), :] = sums[:, start : start + HEAD]
    total = jnp.concatenate(
        [squares[0:1, start : start + HEAD] for start in range(0, rows, HEAD)], axis=0
    )
    coarse = total.astype(jnp.bfloat16).astype(jnp.float32)
    both = jnp.concatenate([coarse, total - coarse], axis=0).astype(jnp.bfloat16)
    for index in range(plane):
        out_ref[index, pl.ds(rows + 2 * block, both.shape[0]), :] = both


def heads_kernel(features, got_ref, query_ref, pair_ref, queries):
    plane = got_ref.shape[0]
    rows = query_ref.shape[0]
    block = rows // plane
    lines = rows // HEAD
    shards = rows // CH_OWN
    layers = shards // plane
    first = rows + 2 * block

    def added(start, size):
        parts = [got_ref[index, start : start + size, :].astype(jnp.float32) for index in range(plane)]
        return sum(parts[1:], parts[0])

    both = added(first, 2 * lines)
    total = both[:lines, :] + both[lines:, :]
    scale = jnp.transpose(lax.rsqrt(total * (1.0 / features) + eps))
    for line in range(lines):
        scaled = added(line * HEAD, HEAD) * scale[:, line : line + 1]
        for start in range(0, HEAD, CH_OWN):
            index = (line * HEAD + start) // CH_OWN
            shard = (index % layers) * plane + index // layers
            queries[pl.ds(shard, CH_OWN, stride=shards), :] = scaled[start : start + CH_OWN, :]
    query_ref[...] = queries[...].astype(jnp.bfloat16)
    cross = lax.rem(seat()[0], plane)
    per_block = block // HEAD
    for line in range(per_block):
        mine = scale[:, line : line + 1]
        for index in range(1, plane):
            column = index * per_block + line
            mine = jnp.where(cross == index, scale[:, column : column + 1], mine)
        for number in range(2):
            start = number * block + line * HEAD
            pair = (added(rows + start, HEAD) * mine).astype(jnp.bfloat16)
            for index in range(plane):
                pair_ref[index, pl.ds(start, HEAD), :] = pair


def attend_kernel(place_ref, query_ref, pair_ref, out_ref, natural, keys, values, attended):
    rows = query_ref.shape[0]
    window = out_ref.shape[1]
    plane = pair_ref.shape[0]
    part = rows // plane
    shards = rows // CH_OWN
    layers = shards // plane
    for number, held in enumerate((keys, values)):
        for cross in range(plane):
            for layer in range(layers):
                piece = pair_ref[cross, pl.ds(number * part + layer * CH_OWN, CH_OWN), :]
                where = pl.ds(layer * plane + cross, CH_OWN, stride=shards)
                natural[where, :] = piece.astype(jnp.float32)
        held[...] = natural[...].astype(jnp.bfloat16)
    block = min(256, rows)
    score_scale = 1.0 / math.sqrt(HEAD)
    for start in range(0, rows, block):
        stop = start + block
        scores = lax.dot_general(
            query_ref[start:stop, :],
            keys[0:stop, :],
            (((1,), (1,)), ((), ())),
            preferred_element_type=jnp.float32,
        )
        spots = lax.broadcasted_iota(jnp.int32, scores.shape, 1)
        mine = lax.broadcasted_iota(jnp.int32, scores.shape, 0) + start
        scores = jnp.where(spots <= mine, scores * score_scale, masked)
        peak = jnp.max(scores, axis=1, keepdims=True)
        lifted = jnp.exp(scores - peak)
        denominator = jnp.sum(lifted, axis=1, keepdims=True)
        weighted = jnp.dot(
            lifted.astype(jnp.bfloat16), values[0:stop, :], preferred_element_type=jnp.float32
        )
        attended[start:stop, :] = (weighted / denominator).astype(jnp.bfloat16)
    attended[rows:, :] = jnp.zeros((attended.shape[0] - rows, HEAD), jnp.bfloat16)
    for shard in range(out_ref.shape[0]):
        first = place_ref[shard]
        out_ref[shard] = attended[pl.ds(pl.multiple_of(first * TILE, TILE), window), :]


def return_kernel(weight_ref, pieces_ref, own_ref, other_ref, attended):
    half = own_ref.shape[1]
    lane = seat()[1]
    for head in range(pieces_ref.shape[0]):
        attended[:, head * HEAD : (head + 1) * HEAD] = pieces_ref[head]
    other_ref[...] = jnp.dot(
        attended[...], weight_ref[:, lanes(1 - lane, half)], preferred_element_type=jnp.float32
    )
    own_ref[...] = jnp.dot(
        attended[...], weight_ref[:, lanes(lane, half)], preferred_element_type=jnp.float32
    )


def join_kernel(own_ref, other_ref, encoded_ref, spread_ref, out_ref):
    returned = (own_ref[...] + other_ref[...]).astype(jnp.bfloat16)
    results = jnp.dot(spread_ref[...], returned, preferred_element_type=jnp.float32)
    out_ref[...] = (encoded_ref[...].astype(jnp.float32) + results).astype(jnp.bfloat16)


def one_head_each(
    byte_states,
    outer_gain,
    mamba_input,
    mamba_step,
    decay_rate,
    mixer_weight,
    boundaries,
    span_counts,
    up_weight,
    up_bias,
    inner_gain,
    query_weight,
    key_weight,
    value_weight,
    return_weight,
):
    shards = lax.axis_size("seq")
    me = lax.axis_index("seq")
    lane = lax.axis_index("mp")
    plane = HEADS // KV_HEADS
    layers = shards // plane
    rows_here, width = byte_states.shape
    half = mamba_input.shape[1]
    capacity = boundaries.shape[1]
    window = capacity + TILE
    total_rows = CH_OWN * shards
    inner_width = inner_gain.shape[0]
    inner_half = up_bias.shape[0]
    weight_rows = query_weight.shape[0]
    f32, bf16 = jnp.float32, jnp.bfloat16
    layer, cross = me // plane, me % plane
    layer_groups = [[first + plane * step for step in range(layers)] for first in range(plane)]
    plane_groups = [[first * plane + step for step in range(plane)] for first in range(layers)]

    def over(value, mask):
        return lax.ppermute(value, "seq", [(i, i ^ mask) for i in range(shards)])

    def after(value, done):
        return lax.optimization_barrier((value, done))[0]

    own_bias = up_bias.reshape(layers // 2, plane, weight_rows)
    own_bias = lax.dynamic_index_in_dim(own_bias, cross, 1, keepdims=False).reshape(1, -1)
    own_gain = inner_gain.reshape(layers, plane, weight_rows)
    own_gain = lax.dynamic_index_in_dim(own_gain, cross, 1, keepdims=False).reshape(1, -1)

    seq_ids = jnp.arange(shards, dtype=jnp.int32)
    offsets = jnp.cumsum(span_counts) - span_counts
    own_offset = jnp.sum(jnp.where(seq_ids == me, offsets, 0))
    own_count = jnp.sum(jnp.where(seq_ids == me, span_counts, 0))
    place = offsets // TILE
    own_marks = boundaries[0]
    positions = jnp.arange(rows_here, dtype=jnp.int32)
    spans_here = jnp.arange(capacity, dtype=jnp.int32)
    live = spans_here < own_count
    slots = capacity // shards
    slot_ids = jnp.arange(slots, dtype=jnp.int32)
    local_span = slot_ids[None, :] * shards + ((seq_ids - own_offset) % shards)[:, None]
    is_span = spans_here[None, :] == local_span.reshape(-1)[:, None]
    byte_at = jnp.sum(jnp.where(is_span, jnp.minimum(own_marks, rows_here - 1)[None, :], 0), axis=1)
    pool_pick = (positions[None, :] == byte_at[:, None]).astype(bf16)
    own_spans = me + jnp.arange(CH_OWN, dtype=jnp.int32) * shards
    origin = jnp.sum((offsets[None, :] <= own_spans[:, None]).astype(jnp.int32), axis=1) - 1
    origin_offset = jnp.sum(
        jnp.where(seq_ids[None, :] == origin[:, None], offsets[None, :], 0), axis=1
    )
    arrived_row = origin * slots + (own_spans - origin_offset) // shards
    own_pick = (
        jnp.arange(shards * slots, dtype=jnp.int32)[None, :] == arrived_row[:, None]
    ).astype(bf16)
    passed = jnp.sum(
        ((own_marks[None, :] <= positions[:, None]) & live[None, :]).astype(jnp.int32), axis=1
    )
    result_row = passed - 1 + own_offset % TILE
    spread = (jnp.arange(window, dtype=jnp.int32)[None, :] == result_row[:, None]).astype(bf16)

    up_half = inner_half // plane
    up_layers = [up_weight]
    for bit in range(layers.bit_length() - 2, -1, -1):
        up_layers += [over(piece, plane << bit) for piece in up_layers]
    order = [0]
    for bit in range(layers.bit_length() - 2, -1, -1):
        order += [step ^ (1 << bit) for step in order]
    up_layers = [up_layers[order.index(step)] for step in range(layers)]

    local, through, ends, *pair_cuts = pl.pallas_call(
        functools.partial(scan_kernel, plane, layers),
        out_shape=(
            jax.ShapeDtypeStruct((rows_here, half), f32),
            jax.ShapeDtypeStruct((rows_here, half), f32),
            jax.ShapeDtypeStruct((shards, 2, half), f32),
        )
        + (jax.ShapeDtypeStruct((weight_rows, (plane + 2) * HEAD), bf16),) * layers,
        in_specs=[in_hbm(), vmem(), in_hbm(), in_hbm(), vmem()] + [in_hbm()] * 3,
        out_specs=(vmem(),) * 3 + (in_place(),) * layers,
        scratch_shapes=[
            pltpu.VMEM(array.shape, bf16)
            for array in (
                byte_states,
                mamba_input,
                mamba_step,
                query_weight,
                key_weight,
                value_weight,
            )
        ]
        + [pltpu.SemaphoreType.DMA((6,)), pltpu.SemaphoreType.DMA((3 * layers,))],
        cost_estimate=brief(),
        compiler_params=params(56),
    )(
        byte_states,
        outer_gain[None, :],
        mamba_input,
        mamba_step,
        decay_rate[None, :],
        query_weight,
        key_weight,
        value_weight,
    )
    ends = lax.all_to_all(ends, "seq", 0, 0, tiled=True)
    pair_cuts = lax.optimization_barrier((pair_cuts, up_layers[layers // 2]))[0]
    ends, up_layers = lax.optimization_barrier((ends, up_layers))
    pieces = [pair_cuts[0]] + [over(pair_cuts[step], plane * step) for step in range(1, layers)]
    states, other_part = pl.pallas_call(
        states_kernel,
        out_shape=(
            jax.ShapeDtypeStruct((rows_here, half), bf16),
            jax.ShapeDtypeStruct((rows_here, half), f32),
        ),
        in_specs=[vmem()] * 4,
        out_specs=(vmem(),) * 2,
        cost_estimate=brief(),
        compiler_params=params(56),
    )(local, through, mixer_weight, ends)
    far_bias = swapped(own_bias)
    bias = jnp.where(
        lane == 0,
        jnp.concatenate([own_bias, far_bias], axis=1),
        jnp.concatenate([far_bias, own_bias], axis=1),
    )
    far_part, bias = lax.optimization_barrier((swapped(other_part), bias))
    encoded, leaving, *up_cuts = pl.pallas_call(
        functools.partial(pool_kernel, plane),
        out_shape=(
            jax.ShapeDtypeStruct((rows_here, half), bf16),
            jax.ShapeDtypeStruct((shards, slots, half), bf16),
        )
        + (jax.ShapeDtypeStruct((layers, up_weight.shape[0], up_half), bf16),) * plane,
        in_specs=[vmem()] * 5 + [in_place()] * layers,
        out_specs=(vmem(),) * (2 + plane),
        scratch_shapes=[pltpu.SemaphoreType.DMA((plane * layers * layers // 2,))],
        cost_estimate=brief(),
        compiler_params=params(56),
    )(states, mixer_weight, far_part, byte_states, pool_pick, *up_layers)
    arrived = lax.all_to_all(leaving, "seq", 0, 0, tiled=True)
    up_own = [up_cuts[0]] + [over(up_cuts[mask], mask) for mask in range(1, plane)]
    arrived, pieces = lax.optimization_barrier((arrived, pieces))
    own_rows = pl.pallas_call(
        own_kernel,
        out_shape=jax.ShapeDtypeStruct((layers, CH_OWN, half), bf16),
        in_specs=[vmem()] * 2,
        out_specs=vmem(),
        cost_estimate=brief(),
        compiler_params=params(56),
    )(own_pick, arrived)
    near_layer = lax.all_to_all(
        own_rows, "seq", 0, 0, axis_index_groups=layer_groups, tiled=True
    )
    up_far = [swapped(piece) for piece in up_own]
    near_layer, up_far = lax.optimization_barrier((near_layer, up_far))
    near = lax.all_to_all(
        jnp.broadcast_to(near_layer[None], (plane, layers, CH_OWN, half)),
        "seq",
        0,
        0,
        axis_index_groups=plane_groups,
        tiled=True,
    ).reshape(total_rows, half)

    features = own_gain.shape[1]
    block = total_rows // plane
    sent_rows = total_rows + 2 * block + 2 * (total_rows // HEAD)
    partial_sums = pl.pallas_call(
        functools.partial(inner_kernel, plane, layers),
        out_shape=jax.ShapeDtypeStruct((plane, sent_rows, HEAD), bf16),
        in_specs=[vmem()] * 2 + [in_place()] * (2 + 2 * plane + layers),
        out_specs=vmem(),
        scratch_shapes=[
            pltpu.VMEM((total_rows, width), bf16),
            pltpu.VMEM((width, features), bf16),
            pltpu.VMEM((features, (plane + 2) * HEAD), bf16),
            pltpu.VMEM((8, total_rows), f32),
            pltpu.SemaphoreType.DMA((2 + 2 * shards + layers,)),
        ],
        cost_estimate=brief(),
        compiler_params=params(56),
    )(bias, own_gain, near, swapped(near), *up_own, *up_far, *pieces)
    got = lax.all_to_all(
        partial_sums, "seq", 0, 0, axis_index_groups=plane_groups, tiled=True
    )
    queries, pairs = pl.pallas_call(
        functools.partial(heads_kernel, inner_width),
        out_shape=(
            jax.ShapeDtypeStruct((total_rows, HEAD), bf16),
            jax.ShapeDtypeStruct((plane, 2 * block, HEAD), bf16),
        ),
        in_specs=[vmem()],
        out_specs=(vmem(),) * 2,
        scratch_shapes=[pltpu.VMEM((total_rows, HEAD), f32)],
        cost_estimate=brief(),
        compiler_params=params(10),
    )(got)
    pairs = lax.all_to_all(pairs, "seq", 0, 0, axis_index_groups=plane_groups, tiled=True)
    leaving = pl.pallas_call(
        attend_kernel,
        out_shape=jax.ShapeDtypeStruct((shards, window, HEAD), bf16),
        in_specs=[smem()] + [vmem()] * 2,
        out_specs=vmem(),
        scratch_shapes=[
            pltpu.VMEM((total_rows, HEAD), f32),
            pltpu.VMEM((total_rows, HEAD), bf16),
            pltpu.VMEM((total_rows, HEAD), bf16),
            pltpu.VMEM((total_rows + window, HEAD), bf16),
        ],
        cost_estimate=brief(),
        compiler_params=params(12),
    )(place, queries, pairs)
    pieces = lax.all_to_all(leaving, "seq", 0, 0, tiled=True)
    own_back, other_back = pl.pallas_call(
        return_kernel,
        out_shape=(jax.ShapeDtypeStruct((window, half), f32),) * 2,
        in_specs=[vmem()] * 2,
        out_specs=(vmem(),) * 2,
        scratch_shapes=[pltpu.VMEM((window, shards * HEAD), bf16)],
        cost_estimate=brief(),
        compiler_params=params(12),
    )(return_weight, pieces)
    return pl.pallas_call(
        join_kernel,
        out_shape=jax.ShapeDtypeStruct((rows_here, half), bf16),
        in_specs=[vmem()] * 4,
        out_specs=vmem(),
        cost_estimate=brief(),
        compiler_params=params(8),
    )(own_back, swapped(other_back), encoded, spread)


def prefix(value, axis, join, neutral):
    count, mine = (lax.axis_size(axis), lax.axis_index(axis))
    pieces = jax.tree.map(lambda part: lax.all_gather(part, axis), value)
    so_far = jax.tree.map(
        lambda part, zero: jnp.full_like(part, 0) + jnp.asarray(zero, part.dtype), value, neutral
    )

    def lap(position, so_far):
        longer = join(so_far, jax.tree.map(lambda part: part[position], pieces))
        return jax.tree.map(lambda new, old: jnp.where(position < mine, new, old), longer, so_far)

    return lax.fori_loop(0, count - 1, lap, so_far)


def rms_scale(values, gain):
    values = values.astype(jnp.float32)
    return values * lax.rsqrt(jnp.mean(values * values, axis=-1, keepdims=True) + eps) * gain


def combine_pairs(earlier, later):
    return (earlier[0] * later[0], later[0] * earlier[1] + later[1])


def pick_table(table, wanted, seq_ids):
    return jnp.sum(jnp.where(seq_ids[None, :] == wanted[:, None], table[None, :], 0), axis=1)


def block_size(piece_rows, shard_rows):
    limit = max(1, 1024 // shard_rows)
    pieces = max(1, piece_rows // shard_rows)
    best_size = 1
    for candidate in range(1, limit + 1):
        if pieces % candidate == 0:
            best_size = candidate
    return min(piece_rows, best_size * shard_rows)


def spread_heads(
    byte_states,
    outer_gain,
    mamba_input,
    mamba_step,
    decay_rate,
    mixer_weight,
    boundaries,
    span_counts,
    up_weight,
    up_bias,
    inner_gain,
    query_weight,
    key_weight,
    value_weight,
    return_weight,
):
    shards = lax.axis_size("seq")
    own_shard = lax.axis_index("seq")
    own_lane = lax.axis_index("mp")
    rows_here = byte_states.shape[0]
    capacity = boundaries.shape[1]
    column_count = mamba_input.shape[1]
    kv_local = key_weight.shape[1] // HEAD
    group_size = HEADS // KV_HEADS
    slot_count = capacity // shards
    offsets = jnp.cumsum(span_counts) - span_counts
    seq_ids = jnp.arange(shards, dtype=jnp.int32)
    own_offset = jnp.sum(jnp.where(seq_ids == own_shard, offsets, 0))
    own_count = jnp.sum(jnp.where(seq_ids == own_shard, span_counts, 0))
    normed = rms_scale(byte_states, outer_gain).astype(jnp.bfloat16)
    inputs = jnp.dot(normed, mamba_input, preferred_element_type=jnp.float32)
    step_sizes = jax.nn.softplus(jnp.dot(normed, mamba_step, preferred_element_type=jnp.float32))
    rate_steps = step_sizes * decay_rate
    decays = jnp.exp(-rate_steps)
    drives = jnp.sqrt(-jnp.expm1(-2.0 * rate_steps)) * inputs
    through, local_states = lax.associative_scan(combine_pairs, (decays, drives), axis=0)
    starting = (jnp.ones((column_count,), jnp.float32), jnp.zeros((column_count,), jnp.float32))
    arriving = prefix((through[-1], local_states[-1]), "seq", combine_pairs, starting)
    states = (local_states + through * arriving[1][None, :]).astype(jnp.bfloat16)
    partial_value = jnp.dot(states, mixer_weight, preferred_element_type=jnp.float32)
    mixed_sum = lax.psum(partial_value, "mp")
    encoded = (byte_states.astype(jnp.float32) + mixed_sum).astype(jnp.bfloat16)
    skip_part = lax.dynamic_slice_in_dim(encoded, own_lane * column_count, column_count, 1)
    own_marks = boundaries[0]
    pooled = encoded[jnp.minimum(own_marks, rows_here - 1)]
    row_width = pooled.shape[1]
    outgoing = jnp.roll(pooled.reshape(slot_count, shards, row_width), own_offset % shards, axis=1)
    incoming = lax.all_to_all(outgoing, "seq", split_axis=1, concat_axis=1, tiled=True)
    position = jnp.arange(CH_OWN, dtype=jnp.int32)
    span_index = own_shard + position * shards
    source = jnp.sum((offsets[None, :] <= span_index[:, None]).astype(jnp.int32), axis=1) - 1
    source_offset = pick_table(offsets, source, seq_ids)
    slot_index = (span_index - source_offset) // shards
    gathered_rows = incoming.reshape(slot_count * shards, row_width)[slot_index * shards + source]
    columns = gathered_rows
    widened_sum = jnp.dot(
        columns,
        lax.all_gather(up_weight, "seq", axis=0, tiled=True),
        preferred_element_type=jnp.float32,
    )
    widened_share = (widened_sum + up_bias[None, :]).astype(jnp.bfloat16)
    widened = lax.all_gather(widened_share, "mp", axis=1, tiled=True)
    inner_normed = rms_scale(widened, inner_gain).astype(jnp.bfloat16)
    columns = inner_normed
    query_part = jnp.dot(
        columns,
        lax.all_gather(query_weight, "seq", axis=0, tiled=True),
        preferred_element_type=jnp.float32,
    )
    key_part = jnp.dot(
        columns,
        lax.all_gather(key_weight, "seq", axis=0, tiled=True),
        preferred_element_type=jnp.float32,
    )
    value_part = jnp.dot(
        columns,
        lax.all_gather(value_weight, "seq", axis=0, tiled=True),
        preferred_element_type=jnp.float32,
    )
    queries = query_part.astype(jnp.bfloat16)
    key_rows = key_part.astype(jnp.bfloat16)
    value_rows = value_part.astype(jnp.bfloat16)
    query_count = queries.shape[0]
    grouped = (
        queries.reshape(query_count, kv_local, group_size, HEAD)
        .transpose(1, 0, 2, 3)
        .reshape(kv_local, query_count * group_size, HEAD)
    )
    row_index = jnp.repeat(span_index, group_size)
    shard_rows = key_rows.shape[0]
    score_scale = 1.0 / math.sqrt(HEAD)

    def key_index(whole_index):
        return whole_index // shard_rows + whole_index % shard_rows * shards

    def attend_block(running, key_block, value_block, index_block):
        row_peak, denominator, weighted = running
        scores = (
            jnp.einsum("hqd,khd->hqk", grouped, key_block, preferred_element_type=jnp.float32)
            * score_scale
        )
        scores = jnp.where(index_block[None, None, :] <= row_index[None, :, None], scores, masked)
        new_peak = jnp.maximum(row_peak, jnp.max(scores, axis=2))
        shrink = jnp.exp(row_peak - new_peak)
        lifted = jnp.exp(scores - new_peak[:, :, None])
        denominator = denominator * shrink + jnp.sum(lifted, axis=2)
        weighted = weighted * shrink[:, :, None] + jnp.einsum(
            "hqk,khd->hqd",
            lifted.astype(jnp.bfloat16),
            value_block,
            preferred_element_type=jnp.float32,
        )
        return (new_peak, denominator, weighted)

    query_total = query_count * group_size
    initial = (
        jnp.full((kv_local, query_total), masked, jnp.float32),
        jnp.zeros((kv_local, query_total), jnp.float32),
        jnp.zeros((kv_local, query_total, HEAD), jnp.float32),
    )
    key_piece = lax.all_gather(key_rows, "seq", axis=0, tiled=True)
    value_piece = lax.all_gather(value_rows, "seq", axis=0, tiled=True)
    piece_rows = key_piece.shape[0]
    block_rows = block_size(piece_rows, shard_rows)
    turn_count = piece_rows // block_rows
    key_blocks = key_piece.reshape(turn_count, block_rows, kv_local, HEAD)
    value_blocks = value_piece.reshape(turn_count, block_rows, kv_local, HEAD)

    def one_turn(turn_index, inner_running):
        whole_index = turn_index * block_rows + jnp.arange(block_rows, dtype=jnp.int32)
        return attend_block(
            inner_running, key_blocks[turn_index], value_blocks[turn_index], key_index(whole_index)
        )

    row_peak, denominator, weighted = lax.fori_loop(0, turn_count, one_turn, initial)
    attended = (weighted / denominator[:, :, None]).astype(jnp.bfloat16)
    attended = (
        attended.reshape(kv_local, query_count, group_size, HEAD)
        .transpose(1, 0, 2, 3)
        .reshape(query_count, kv_local * group_size * HEAD)
    )
    projected = jnp.dot(attended, return_weight, preferred_element_type=jnp.float32)
    returned = lax.psum_scatter(
        projected.astype(jnp.bfloat16), "mp", scatter_dimension=1, tiled=True
    )
    slot_ids = jnp.arange(slot_count, dtype=jnp.int32)
    lead_slot = (own_shard - offsets) % shards
    local_span = slot_ids[:, None] * shards + lead_slot[None, :]
    back_index = (offsets[None, :] + local_span - own_shard) // shards
    alive = local_span < span_counts[None, :]
    back_rows = jnp.where(
        alive[:, :, None],
        returned[jnp.clip(back_index, 0, CH_OWN - 1)],
        jnp.zeros((), jnp.bfloat16),
    )
    arrived = lax.all_to_all(back_rows, "seq", split_axis=1, concat_axis=1, tiled=True)
    span_results = jnp.roll(arrived, -(own_offset % shards), axis=1).reshape(capacity, column_count)
    positions = jnp.arange(rows_here, dtype=jnp.int32)
    live_slots = jnp.arange(capacity, dtype=jnp.int32) < own_count
    passed = jnp.sum(
        ((own_marks[None, :] <= positions[:, None]) & live_slots[None, :]).astype(jnp.int32), axis=1
    )
    return (skip_part.astype(jnp.float32) + span_results[passed - 1].astype(jnp.float32)).astype(
        jnp.bfloat16
    )


def solution(mesh):
    in_specs = (
        P("seq", None),
        P(),
        P(None, "mp"),
        P(None, "mp"),
        P("mp"),
        P("mp", None),
        P("seq", None),
        P(),
        P("seq", "mp"),
        P("mp"),
        P(),
        P("seq", "mp"),
        P("seq", "mp"),
        P("seq", "mp"),
        P("mp", None),
    )
    out_specs = P("seq", "mp")
    def on_device(*arrays):
        heads_here = arrays[11].shape[1] // HEAD
        fits = heads_here == mesh.shape["seq"] and mesh.shape["mp"] == 2
        return (one_head_each if fits else spread_heads)(*arrays)

    return jax.shard_map(
        on_device, mesh=mesh, in_specs=in_specs, out_specs=out_specs, check_vma=False
    )
```

```python
import functools
import math

import jax
import jax.numpy as jnp
from jax import lax
from jax.experimental import pallas as pl
from jax.experimental.pallas import tpu as pltpu
from jax.sharding import PartitionSpec as P

HEADS = 32
KV_HEADS = 8
HEAD = 128
CH_OWN = 64


eps = 1e-05
masked = -1e30
TILE = 16


def swapped(value):
    return lax.ppermute(value, "mp", [(0, 1), (1, 0)])


def vmem():
    return pl.BlockSpec(memory_space=pltpu.VMEM)


def smem():
    return pl.BlockSpec(memory_space=pltpu.SMEM)


def in_place():
    return pl.BlockSpec(memory_space=pl.ANY)


def in_hbm():
    return pl.BlockSpec(memory_space=pltpu.HBM)


def seat():
    return lax.axis_index("seq"), lax.axis_index("mp")


def params(mebibytes=24):
    return pltpu.CompilerParams(vmem_limit_bytes=mebibytes * 2**20)


def brief():
    return pl.CostEstimate(flops=1, bytes_accessed=1, transcendentals=0)


def lanes(which, size):
    return pl.ds(pl.multiple_of(which * size, size), size)


def rows_at(which, size):
    return pl.ds(pl.multiple_of(which * size, size), size)


def start_all(pairs, sems):
    copies = []
    for index, (from_ref, to_ref) in enumerate(pairs):
        copy = pltpu.make_async_copy(from_ref, to_ref, sems.at[index])
        copy.start()
        copies.append(copy)
    return copies


def copy_all(pairs, sems):
    for copy in start_all(pairs, sems):
        copy.wait()


def one_minus_exp(u):
    series = jnp.ones_like(u)
    for order in range(9, 1, -1):
        series = 1.0 - u * (1.0 / order) * series
    return jnp.where(u < 0.5, u * series, 1.0 - jnp.exp(-u))


def softplus(v):
    tail = jnp.exp(-jnp.abs(v))
    series = jnp.ones_like(tail)
    for order in range(6, 1, -1):
        series = 1.0 - tail * ((order - 1.0) / order) * series
    return jnp.maximum(v, 0.0) + jnp.where(tail < 0.03, tail * series, jnp.log(1.0 + tail))


def start_cuts(plane, query_ref, key_ref, value_ref, pair_outs, sems):
    layers = len(pair_outs)
    me, _ = seat()
    layer = me // plane
    group = plane * HEAD
    pairs = []
    for step, out_ref in enumerate(pair_outs):
        target = layer ^ step
        pairs.append((query_ref.at[:, lanes(target, group)], out_ref.at[:, pl.ds(0, group)]))
        pairs.append((key_ref.at[:, lanes(target, HEAD)], out_ref.at[:, pl.ds(group, HEAD)]))
        pairs.append(
            (value_ref.at[:, lanes(target, HEAD)], out_ref.at[:, pl.ds(group + HEAD, HEAD)])
        )
    return start_all(pairs, sems)


def scan_kernel(plane, layers, *refs):
    bytes_hbm, gain_ref, input_hbm, step_hbm, rate_ref = refs[:5]
    others, refs = refs[5:8], refs[8:]
    local_ref, through_ref, ends_ref = refs[:3]
    pair_outs, refs = refs[3 : 3 + layers], refs[3 + layers :]
    bytes_ref, input_ref, step_ref, *held, sems, cut_sems = refs
    fetches = start_all(
        [(bytes_hbm, bytes_ref), (step_hbm, step_ref), (input_hbm, input_ref), *zip(others, held)],
        sems,
    )
    fetches[0].wait()
    values = bytes_ref[...].astype(jnp.float32)
    scale = lax.rsqrt(jnp.mean(values * values, axis=1, keepdims=True) + eps)
    normed = (values * scale * gain_ref[...]).astype(jnp.bfloat16)
    fetches[1].wait()
    steps = softplus(jnp.dot(normed, step_ref[...], preferred_element_type=jnp.float32))
    rate_steps = steps * rate_ref[...]
    fetches[2].wait()
    inputs = jnp.dot(normed, input_ref[...], preferred_element_type=jnp.float32)
    for fetch in fetches[3:]:
        fetch.wait()
    cuts = start_cuts(plane, *held, pair_outs, cut_sems)
    decays = jnp.exp(-rate_steps)
    drives = jnp.sqrt(one_minus_exp(2.0 * rate_steps)) * inputs
    rows, width = decays.shape
    tile = 8
    decays = decays.reshape(rows // tile, tile, width)
    drives = drives.reshape(rows // tile, tile, width)
    place = lax.broadcasted_iota(jnp.int32, decays.shape, 1)
    for reach in (1, 2, 4):
        before_decays = pltpu.roll(decays, reach, 1)
        before_drives = pltpu.roll(drives, reach, 1)
        inside = place >= reach
        drives = jnp.where(inside, decays * before_drives + drives, drives)
        decays = jnp.where(inside, decays * before_decays, decays)
    state = jnp.zeros((1, width), jnp.float32)
    kept = jnp.ones((1, width), jnp.float32)
    for index in range(rows // tile):
        states = decays[index] * state + drives[index]
        passing = decays[index] * kept
        local_ref[pl.ds(index * tile, tile), :] = states
        through_ref[pl.ds(index * tile, tile), :] = passing
        state = states[tile - 1 :, :]
        kept = passing[tile - 1 :, :]
    for index in range(ends_ref.shape[0]):
        ends_ref[index, 0:1, :] = kept
        ends_ref[index, 1:2, :] = state
    for cut in cuts:
        cut.wait()


def states_kernel(local_ref, through_ref, mixer_ref, ends_ref, states_ref, other_ref):
    me, lane = seat()
    carry = jnp.zeros((1, local_ref.shape[1]), jnp.float32)
    for shard in range(ends_ref.shape[0]):
        later = ends_ref[shard, 0:1, :] * carry + ends_ref[shard, 1:2, :]
        carry = jnp.where(shard < me, later, carry)
    states = (local_ref[...] + through_ref[...] * carry).astype(jnp.bfloat16)
    states_ref[...] = states
    half = other_ref.shape[1]
    other_ref[...] = jnp.dot(
        states, mixer_ref[:, lanes(1 - lane, half)], preferred_element_type=jnp.float32
    )


def pool_kernel(plane, *refs):
    states_ref, mixer_ref, other_ref, bytes_ref, pick_ref = refs[:5]
    layers = len(refs) - 8 - plane
    up_pieces, (encoded_ref, out_ref, *up_refs, sems) = refs[5 : 5 + layers], refs[5 + layers :]
    cross = lax.rem(seat()[0], plane)
    pairs = []
    for mask, up_ref in enumerate(up_refs):
        size = 2 * up_ref.shape[2] // layers
        for step, piece in enumerate(up_pieces):
            for number in range(layers // 2):
                columns = lanes(number * plane + (cross ^ mask), size)
                pairs.append((piece.at[:, columns], up_ref.at[step, :, pl.ds(number * size, size)]))
    copies = start_all(pairs, sems)
    half = other_ref.shape[1]
    columns = lanes(seat()[1], half)
    mixed = jnp.dot(states_ref[...], mixer_ref[:, columns], preferred_element_type=jnp.float32)
    skip = bytes_ref[:, columns].astype(jnp.float32)
    encoded = (skip + (mixed + other_ref[...])).astype(jnp.bfloat16)
    encoded_ref[...] = encoded
    picked = jnp.dot(pick_ref[...], encoded, preferred_element_type=jnp.float32)
    out_ref[...] = picked.astype(jnp.bfloat16).reshape(out_ref.shape)
    for copy in copies:
        copy.wait()


def own_kernel(pick_ref, arrived_ref, out_ref):
    shards, slots, half = arrived_ref.shape
    rows = arrived_ref[...].astype(jnp.float32).reshape(shards * slots, half)
    own = jnp.dot(
        pick_ref[...], rows.astype(jnp.bfloat16), preferred_element_type=jnp.float32
    ).astype(jnp.bfloat16)
    for index in range(out_ref.shape[0]):
        out_ref[index] = own


def inner_kernel(plane, layers, bias_ref, gain_ref, near_ref, far_ref, *refs):
    up_own, refs = refs[:plane], refs[plane:]
    up_far, refs = refs[:plane], refs[plane:]
    pieces, refs = refs[:layers], refs[layers:]
    out_ref, pooled, up, weights, squares, sems = refs
    me, lane = seat()
    layer, cross = me // plane, lax.rem(me, plane)
    half = near_ref.shape[1]
    up_rows, up_half = up_own[0].shape[1:]
    pairs = [
        (near_ref, pooled.at[:, lanes(lane, half)]),
        (far_ref, pooled.at[:, lanes(1 - lane, half)]),
    ]
    for step in range(layers):
        for mask in range(plane):
            where = rows_at((layer ^ step) * plane + (cross ^ mask), up_rows)
            pairs.append((up_own[mask].at[step], up.at[where, lanes(lane, up_half)]))
            pairs.append((up_far[mask].at[step], up.at[where, lanes(1 - lane, up_half)]))
    for step, piece in enumerate(pieces):
        pairs.append((piece, weights.at[rows_at(layer ^ step, piece.shape[0]), :]))
    copies = start_all(pairs, sems)
    for copy in copies[:-layers]:
        copy.wait()
    rows = pooled.shape[0]
    block = rows // plane
    ones = jnp.ones((8, up.shape[1]), jnp.bfloat16)
    for index in range(plane):
        where = pl.ds(index * block, block)
        widened = jnp.dot(pooled[where, :], up[...], preferred_element_type=jnp.float32)
        widened = (widened + bias_ref[...]).astype(jnp.bfloat16).astype(jnp.float32)
        inner = (widened * gain_ref[...]).astype(jnp.bfloat16)
        square = widened * widened
        coarse = square.astype(jnp.bfloat16)
        fine = (square - coarse.astype(jnp.float32)).astype(jnp.bfloat16)
        squares[:, where] = sum(
            lax.dot_general(
                ones, part, (((1,), (1,)), ((), ())), preferred_element_type=jnp.float32
            )
            for part in (coarse, fine)
        )
        if index == 0:
            for copy in copies[-layers:]:
                copy.wait()
        sums = jnp.dot(inner, weights[...], preferred_element_type=jnp.float32)
        sums = sums.astype(jnp.bfloat16)
        for head in range(plane):
            out_ref[head, where, :] = sums[:, head * HEAD : (head + 1) * HEAD]
        for number in range(2):
            start = (plane + number) * HEAD
            out_ref[index, pl.ds(rows + number * block, block), :] = sums[:, start : start + HEAD]
    total = jnp.concatenate(
        [squares[0:1, start : start + HEAD] for start in range(0, rows, HEAD)], axis=0
    )
    coarse = total.astype(jnp.bfloat16).astype(jnp.float32)
    both = jnp.concatenate([coarse, total - coarse], axis=0).astype(jnp.bfloat16)
    for index in range(plane):
        out_ref[index, pl.ds(rows + 2 * block, both.shape[0]), :] = both


def heads_kernel(features, got_ref, query_ref, pair_ref, queries):
    plane = got_ref.shape[0]
    rows = query_ref.shape[0]
    block = rows // plane
    lines = rows // HEAD
    shards = rows // CH_OWN
    layers = shards // plane
    first = rows + 2 * block

    def added(start, size):
        parts = [got_ref[index, start : start + size, :].astype(jnp.float32) for index in range(plane)]
        return sum(parts[1:], parts[0])

    both = added(first, 2 * lines)
    total = both[:lines, :] + both[lines:, :]
    scale = jnp.transpose(lax.rsqrt(total * (1.0 / features) + eps))
    for line in range(lines):
        scaled = added(line * HEAD, HEAD) * scale[:, line : line + 1]
        for start in range(0, HEAD, CH_OWN):
            index = (line * HEAD + start) // CH_OWN
            shard = (index % layers) * plane + index // layers
            queries[pl.ds(shard, CH_OWN, stride=shards), :] = scaled[start : start + CH_OWN, :]
    query_ref[...] = queries[...].astype(jnp.bfloat16)
    cross = lax.rem(seat()[0], plane)
    per_block = block // HEAD
    for line in range(per_block):
        mine = scale[:, line : line + 1]
        for index in range(1, plane):
            column = index * per_block + line
            mine = jnp.where(cross == index, scale[:, column : column + 1], mine)
        for number in range(2):
            start = number * block + line * HEAD
            pair = (added(rows + start, HEAD) * mine).astype(jnp.bfloat16)
            for index in range(plane):
                pair_ref[index, pl.ds(start, HEAD), :] = pair


def attend_kernel(place_ref, query_ref, pair_ref, out_ref, natural, keys, values, attended):
    rows = query_ref.shape[0]
    window = out_ref.shape[1]
    plane = pair_ref.shape[0]
    part = rows // plane
    shards = rows // CH_OWN
    layers = shards // plane
    for number, held in enumerate((keys, values)):
        for cross in range(plane):
            for layer in range(layers):
                piece = pair_ref[cross, pl.ds(number * part + layer * CH_OWN, CH_OWN), :]
                where = pl.ds(layer * plane + cross, CH_OWN, stride=shards)
                natural[where, :] = piece.astype(jnp.float32)
        held[...] = natural[...].astype(jnp.bfloat16)
    block = min(256, rows)
    score_scale = 1.0 / math.sqrt(HEAD)
    for start in range(0, rows, block):
        stop = start + block
        scores = lax.dot_general(
            query_ref[start:stop, :],
            keys[0:stop, :],
            (((1,), (1,)), ((), ())),
            preferred_element_type=jnp.float32,
        )
        spots = lax.broadcasted_iota(jnp.int32, scores.shape, 1)
        mine = lax.broadcasted_iota(jnp.int32, scores.shape, 0) + start
        scores = jnp.where(spots <= mine, scores * score_scale, masked)
        peak = jnp.max(scores, axis=1, keepdims=True)
        lifted = jnp.exp(scores - peak)
        denominator = jnp.sum(lifted, axis=1, keepdims=True)
        weighted = jnp.dot(
            lifted.astype(jnp.bfloat16), values[0:stop, :], preferred_element_type=jnp.float32
        )
        attended[start:stop, :] = (weighted / denominator).astype(jnp.bfloat16)
    attended[rows:, :] = jnp.zeros((attended.shape[0] - rows, HEAD), jnp.bfloat16)
    for shard in range(out_ref.shape[0]):
        first = place_ref[shard]
        out_ref[shard] = attended[pl.ds(pl.multiple_of(first * TILE, TILE), window), :]


def return_kernel(weight_ref, pieces_ref, own_ref, other_ref, attended):
    half = own_ref.shape[1]
    lane = seat()[1]
    for head in range(pieces_ref.shape[0]):
        attended[:, head * HEAD : (head + 1) * HEAD] = pieces_ref[head]
    other_ref[...] = jnp.dot(
        attended[...], weight_ref[:, lanes(1 - lane, half)], preferred_element_type=jnp.float32
    )
    own_ref[...] = jnp.dot(
        attended[...], weight_ref[:, lanes(lane, half)], preferred_element_type=jnp.float32
    )


def join_kernel(own_ref, other_ref, encoded_ref, spread_ref, out_ref):
    returned = (own_ref[...] + other_ref[...]).astype(jnp.bfloat16)
    results = jnp.dot(spread_ref[...], returned, preferred_element_type=jnp.float32)
    out_ref[...] = (encoded_ref[...].astype(jnp.float32) + results).astype(jnp.bfloat16)


def one_head_each(
    byte_states,
    outer_gain,
    mamba_input,
    mamba_step,
    decay_rate,
    mixer_weight,
    boundaries,
    span_counts,
    up_weight,
    up_bias,
    inner_gain,
    query_weight,
    key_weight,
    value_weight,
    return_weight,
):
    shards = lax.axis_size("seq")
    me = lax.axis_index("seq")
    lane = lax.axis_index("mp")
    plane = HEADS // KV_HEADS
    layers = shards // plane
    rows_here, width = byte_states.shape
    half = mamba_input.shape[1]
    capacity = boundaries.shape[1]
    window = capacity + TILE
    total_rows = CH_OWN * shards
    inner_width = inner_gain.shape[0]
    inner_half = up_bias.shape[0]
    weight_rows = query_weight.shape[0]
    f32, bf16 = jnp.float32, jnp.bfloat16
    layer, cross = me // plane, me % plane
    layer_groups = [[first + plane * step for step in range(layers)] for first in range(plane)]
    plane_groups = [[first * plane + step for step in range(plane)] for first in range(layers)]

    def over(value, mask):
        return lax.ppermute(value, "seq", [(i, i ^ mask) for i in range(shards)])

    def after(value, done):
        return lax.optimization_barrier((value, done))[0]

    own_bias = up_bias.reshape(layers // 2, plane, weight_rows)
    own_bias = lax.dynamic_index_in_dim(own_bias, cross, 1, keepdims=False).reshape(1, -1)
    own_gain = inner_gain.reshape(layers, plane, weight_rows)
    own_gain = lax.dynamic_index_in_dim(own_gain, cross, 1, keepdims=False).reshape(1, -1)

    seq_ids = jnp.arange(shards, dtype=jnp.int32)
    offsets = jnp.cumsum(span_counts) - span_counts
    own_offset = jnp.sum(jnp.where(seq_ids == me, offsets, 0))
    own_count = jnp.sum(jnp.where(seq_ids == me, span_counts, 0))
    place = offsets // TILE
    own_marks = boundaries[0]
    positions = jnp.arange(rows_here, dtype=jnp.int32)
    spans_here = jnp.arange(capacity, dtype=jnp.int32)
    live = spans_here < own_count
    slots = capacity // shards
    slot_ids = jnp.arange(slots, dtype=jnp.int32)
    local_span = slot_ids[None, :] * shards + ((seq_ids - own_offset) % shards)[:, None]
    is_span = spans_here[None, :] == local_span.reshape(-1)[:, None]
    byte_at = jnp.sum(jnp.where(is_span, jnp.minimum(own_marks, rows_here - 1)[None, :], 0), axis=1)
    pool_pick = (positions[None, :] == byte_at[:, None]).astype(bf16)
    own_spans = me + jnp.arange(CH_OWN, dtype=jnp.int32) * shards
    origin = jnp.sum((offsets[None, :] <= own_spans[:, None]).astype(jnp.int32), axis=1) - 1
    origin_offset = jnp.sum(
        jnp.where(seq_ids[None, :] == origin[:, None], offsets[None, :], 0), axis=1
    )
    arrived_row = origin * slots + (own_spans - origin_offset) // shards
    own_pick = (
        jnp.arange(shards * slots, dtype=jnp.int32)[None, :] == arrived_row[:, None]
    ).astype(bf16)
    passed = jnp.sum(
        ((own_marks[None, :] <= positions[:, None]) & live[None, :]).astype(jnp.int32), axis=1
    )
    result_row = passed - 1 + own_offset % TILE
    spread = (jnp.arange(window, dtype=jnp.int32)[None, :] == result_row[:, None]).astype(bf16)

    up_half = inner_half // plane
    up_layers = [up_weight]
    for bit in range(layers.bit_length() - 2, -1, -1):
        up_layers += [over(piece, plane << bit) for piece in up_layers]
    order = [0]
    for bit in range(layers.bit_length() - 2, -1, -1):
        order += [step ^ (1 << bit) for step in order]
    up_layers = [up_layers[order.index(step)] for step in range(layers)]

    local, through, ends, *pair_cuts = pl.pallas_call(
        functools.partial(scan_kernel, plane, layers),
        out_shape=(
            jax.ShapeDtypeStruct((rows_here, half), f32),
            jax.ShapeDtypeStruct((rows_here, half), f32),
            jax.ShapeDtypeStruct((shards, 2, half), f32),
        )
        + (jax.ShapeDtypeStruct((weight_rows, (plane + 2) * HEAD), bf16),) * layers,
        in_specs=[in_hbm(), vmem(), in_hbm(), in_hbm(), vmem()] + [in_hbm()] * 3,
        out_specs=(vmem(),) * 3 + (in_place(),) * layers,
        scratch_shapes=[
            pltpu.VMEM(array.shape, bf16)
            for array in (
                byte_states,
                mamba_input,
                mamba_step,
                query_weight,
                key_weight,
                value_weight,
            )
        ]
        + [pltpu.SemaphoreType.DMA((6,)), pltpu.SemaphoreType.DMA((3 * layers,))],
        cost_estimate=brief(),
        compiler_params=params(56),
    )(
        byte_states,
        outer_gain[None, :],
        mamba_input,
        mamba_step,
        decay_rate[None, :],
        query_weight,
        key_weight,
        value_weight,
    )
    ends = lax.all_to_all(ends, "seq", 0, 0, tiled=True)
    pair_cuts = lax.optimization_barrier((pair_cuts, up_layers[layers // 2]))[0]
    ends, up_layers = lax.optimization_barrier((ends, up_layers))
    pieces = [pair_cuts[0]] + [over(pair_cuts[step], plane * step) for step in (1, 2)]
    states, other_part = pl.pallas_call(
        states_kernel,
        out_shape=(
            jax.ShapeDtypeStruct((rows_here, half), bf16),
            jax.ShapeDtypeStruct((rows_here, half), f32),
        ),
        in_specs=[vmem()] * 4,
        out_specs=(vmem(),) * 2,
        cost_estimate=brief(),
        compiler_params=params(56),
    )(local, through, mixer_weight, ends)
    far_bias = swapped(own_bias)
    bias = jnp.where(
        lane == 0,
        jnp.concatenate([own_bias, far_bias], axis=1),
        jnp.concatenate([far_bias, own_bias], axis=1),
    )
    far_part, bias, pieces = lax.optimization_barrier((swapped(other_part), bias, pieces))
    encoded, leaving, *up_cuts = pl.pallas_call(
        functools.partial(pool_kernel, plane),
        out_shape=(
            jax.ShapeDtypeStruct((rows_here, half), bf16),
            jax.ShapeDtypeStruct((shards, slots, half), bf16),
        )
        + (jax.ShapeDtypeStruct((layers, up_weight.shape[0], up_half), bf16),) * plane,
        in_specs=[vmem()] * 5 + [in_place()] * layers,
        out_specs=(vmem(),) * (2 + plane),
        scratch_shapes=[pltpu.SemaphoreType.DMA((plane * layers * layers // 2,))],
        cost_estimate=brief(),
        compiler_params=params(56),
    )(states, mixer_weight, far_part, byte_states, pool_pick, *up_layers)
    arrived = lax.all_to_all(leaving, "seq", 0, 0, tiled=True)
    up_own = [up_cuts[0]] + [over(up_cuts[mask], mask) for mask in range(1, plane)]
    own_rows = pl.pallas_call(
        own_kernel,
        out_shape=jax.ShapeDtypeStruct((layers, CH_OWN, half), bf16),
        in_specs=[vmem()] * 2,
        out_specs=vmem(),
        cost_estimate=brief(),
        compiler_params=params(56),
    )(own_pick, arrived)
    pieces.append(over(after(pair_cuts[3], own_rows), 3 * plane))
    near_layer = lax.all_to_all(
        own_rows, "seq", 0, 0, axis_index_groups=layer_groups, tiled=True
    )
    up_far = [swapped(piece) for piece in up_own]
    near_layer, up_far = lax.optimization_barrier((near_layer, up_far))
    near = lax.all_to_all(
        jnp.broadcast_to(near_layer[None], (plane, layers, CH_OWN, half)),
        "seq",
        0,
        0,
        axis_index_groups=plane_groups,
        tiled=True,
    ).reshape(total_rows, half)

    features = own_gain.shape[1]
    block = total_rows // plane
    sent_rows = total_rows + 2 * block + 2 * (total_rows // HEAD)
    partial_sums = pl.pallas_call(
        functools.partial(inner_kernel, plane, layers),
        out_shape=jax.ShapeDtypeStruct((plane, sent_rows, HEAD), bf16),
        in_specs=[vmem()] * 2 + [in_place()] * (2 + 2 * plane + layers),
        out_specs=vmem(),
        scratch_shapes=[
            pltpu.VMEM((total_rows, width), bf16),
            pltpu.VMEM((width, features), bf16),
            pltpu.VMEM((features, (plane + 2) * HEAD), bf16),
            pltpu.VMEM((8, total_rows), f32),
            pltpu.SemaphoreType.DMA((2 + 2 * shards + layers,)),
        ],
        cost_estimate=brief(),
        compiler_params=params(56),
    )(bias, own_gain, near, swapped(near), *up_own, *up_far, *pieces)
    got = lax.all_to_all(
        partial_sums, "seq", 0, 0, axis_index_groups=plane_groups, tiled=True
    )
    queries, pairs = pl.pallas_call(
        functools.partial(heads_kernel, inner_width),
        out_shape=(
            jax.ShapeDtypeStruct((total_rows, HEAD), bf16),
            jax.ShapeDtypeStruct((plane, 2 * block, HEAD), bf16),
        ),
        in_specs=[vmem()],
        out_specs=(vmem(),) * 2,
        scratch_shapes=[pltpu.VMEM((total_rows, HEAD), f32)],
        cost_estimate=brief(),
        compiler_params=params(10),
    )(got)
    pairs = lax.all_to_all(pairs, "seq", 0, 0, axis_index_groups=plane_groups, tiled=True)
    leaving = pl.pallas_call(
        attend_kernel,
        out_shape=jax.ShapeDtypeStruct((shards, window, HEAD), bf16),
        in_specs=[smem()] + [vmem()] * 2,
        out_specs=vmem(),
        scratch_shapes=[
            pltpu.VMEM((total_rows, HEAD), f32),
            pltpu.VMEM((total_rows, HEAD), bf16),
            pltpu.VMEM((total_rows, HEAD), bf16),
            pltpu.VMEM((total_rows + window, HEAD), bf16),
        ],
        cost_estimate=brief(),
        compiler_params=params(12),
    )(place, queries, pairs)
    pieces = lax.all_to_all(leaving, "seq", 0, 0, tiled=True)
    own_back, other_back = pl.pallas_call(
        return_kernel,
        out_shape=(jax.ShapeDtypeStruct((window, half), f32),) * 2,
        in_specs=[vmem()] * 2,
        out_specs=(vmem(),) * 2,
        scratch_shapes=[pltpu.VMEM((window, shards * HEAD), bf16)],
        cost_estimate=brief(),
        compiler_params=params(12),
    )(return_weight, pieces)
    return pl.pallas_call(
        join_kernel,
        out_shape=jax.ShapeDtypeStruct((rows_here, half), bf16),
        in_specs=[vmem()] * 4,
        out_specs=vmem(),
        cost_estimate=brief(),
        compiler_params=params(8),
    )(own_back, swapped(other_back), encoded, spread)


def prefix(value, axis, join, neutral):
    count, mine = (lax.axis_size(axis), lax.axis_index(axis))
    pieces = jax.tree.map(lambda part: lax.all_gather(part, axis), value)
    so_far = jax.tree.map(
        lambda part, zero: jnp.full_like(part, 0) + jnp.asarray(zero, part.dtype), value, neutral
    )

    def lap(position, so_far):
        longer = join(so_far, jax.tree.map(lambda part: part[position], pieces))
        return jax.tree.map(lambda new, old: jnp.where(position < mine, new, old), longer, so_far)

    return lax.fori_loop(0, count - 1, lap, so_far)


def rms_scale(values, gain):
    values = values.astype(jnp.float32)
    return values * lax.rsqrt(jnp.mean(values * values, axis=-1, keepdims=True) + eps) * gain


def combine_pairs(earlier, later):
    return (earlier[0] * later[0], later[0] * earlier[1] + later[1])


def pick_table(table, wanted, seq_ids):
    return jnp.sum(jnp.where(seq_ids[None, :] == wanted[:, None], table[None, :], 0), axis=1)


def block_size(piece_rows, shard_rows):
    limit = max(1, 1024 // shard_rows)
    pieces = max(1, piece_rows // shard_rows)
    best_size = 1
    for candidate in range(1, limit + 1):
        if pieces % candidate == 0:
            best_size = candidate
    return min(piece_rows, best_size * shard_rows)


def spread_heads(
    byte_states,
    outer_gain,
    mamba_input,
    mamba_step,
    decay_rate,
    mixer_weight,
    boundaries,
    span_counts,
    up_weight,
    up_bias,
    inner_gain,
    query_weight,
    key_weight,
    value_weight,
    return_weight,
):
    shards = lax.axis_size("seq")
    own_shard = lax.axis_index("seq")
    own_lane = lax.axis_index("mp")
    rows_here = byte_states.shape[0]
    capacity = boundaries.shape[1]
    column_count = mamba_input.shape[1]
    kv_local = key_weight.shape[1] // HEAD
    group_size = HEADS // KV_HEADS
    slot_count = capacity // shards
    offsets = jnp.cumsum(span_counts) - span_counts
    seq_ids = jnp.arange(shards, dtype=jnp.int32)
    own_offset = jnp.sum(jnp.where(seq_ids == own_shard, offsets, 0))
    own_count = jnp.sum(jnp.where(seq_ids == own_shard, span_counts, 0))
    normed = rms_scale(byte_states, outer_gain).astype(jnp.bfloat16)
    inputs = jnp.dot(normed, mamba_input, preferred_element_type=jnp.float32)
    step_sizes = jax.nn.softplus(jnp.dot(normed, mamba_step, preferred_element_type=jnp.float32))
    rate_steps = step_sizes * decay_rate
    decays = jnp.exp(-rate_steps)
    drives = jnp.sqrt(-jnp.expm1(-2.0 * rate_steps)) * inputs
    through, local_states = lax.associative_scan(combine_pairs, (decays, drives), axis=0)
    starting = (jnp.ones((column_count,), jnp.float32), jnp.zeros((column_count,), jnp.float32))
    arriving = prefix((through[-1], local_states[-1]), "seq", combine_pairs, starting)
    states = (local_states + through * arriving[1][None, :]).astype(jnp.bfloat16)
    partial_value = jnp.dot(states, mixer_weight, preferred_element_type=jnp.float32)
    mixed_sum = lax.psum(partial_value, "mp")
    encoded = (byte_states.astype(jnp.float32) + mixed_sum).astype(jnp.bfloat16)
    skip_part = lax.dynamic_slice_in_dim(encoded, own_lane * column_count, column_count, 1)
    own_marks = boundaries[0]
    pooled = encoded[jnp.minimum(own_marks, rows_here - 1)]
    row_width = pooled.shape[1]
    outgoing = jnp.roll(pooled.reshape(slot_count, shards, row_width), own_offset % shards, axis=1)
    incoming = lax.all_to_all(outgoing, "seq", split_axis=1, concat_axis=1, tiled=True)
    position = jnp.arange(CH_OWN, dtype=jnp.int32)
    span_index = own_shard + position * shards
    source = jnp.sum((offsets[None, :] <= span_index[:, None]).astype(jnp.int32), axis=1) - 1
    source_offset = pick_table(offsets, source, seq_ids)
    slot_index = (span_index - source_offset) // shards
    gathered_rows = incoming.reshape(slot_count * shards, row_width)[slot_index * shards + source]
    columns = gathered_rows
    widened_sum = jnp.dot(
        columns,
        lax.all_gather(up_weight, "seq", axis=0, tiled=True),
        preferred_element_type=jnp.float32,
    )
    widened_share = (widened_sum + up_bias[None, :]).astype(jnp.bfloat16)
    widened = lax.all_gather(widened_share, "mp", axis=1, tiled=True)
    inner_normed = rms_scale(widened, inner_gain).astype(jnp.bfloat16)
    columns = inner_normed
    query_part = jnp.dot(
        columns,
        lax.all_gather(query_weight, "seq", axis=0, tiled=True),
        preferred_element_type=jnp.float32,
    )
    key_part = jnp.dot(
        columns,
        lax.all_gather(key_weight, "seq", axis=0, tiled=True),
        preferred_element_type=jnp.float32,
    )
    value_part = jnp.dot(
        columns,
        lax.all_gather(value_weight, "seq", axis=0, tiled=True),
        preferred_element_type=jnp.float32,
    )
    queries = query_part.astype(jnp.bfloat16)
    key_rows = key_part.astype(jnp.bfloat16)
    value_rows = value_part.astype(jnp.bfloat16)
    query_count = queries.shape[0]
    grouped = (
        queries.reshape(query_count, kv_local, group_size, HEAD)
        .transpose(1, 0, 2, 3)
        .reshape(kv_local, query_count * group_size, HEAD)
    )
    row_index = jnp.repeat(span_index, group_size)
    shard_rows = key_rows.shape[0]
    score_scale = 1.0 / math.sqrt(HEAD)

    def key_index(whole_index):
        return whole_index // shard_rows + whole_index % shard_rows * shards

    def attend_block(running, key_block, value_block, index_block):
        row_peak, denominator, weighted = running
        scores = (
            jnp.einsum("hqd,khd->hqk", grouped, key_block, preferred_element_type=jnp.float32)
            * score_scale
        )
        scores = jnp.where(index_block[None, None, :] <= row_index[None, :, None], scores, masked)
        new_peak = jnp.maximum(row_peak, jnp.max(scores, axis=2))
        shrink = jnp.exp(row_peak - new_peak)
        lifted = jnp.exp(scores - new_peak[:, :, None])
        denominator = denominator * shrink + jnp.sum(lifted, axis=2)
        weighted = weighted * shrink[:, :, None] + jnp.einsum(
            "hqk,khd->hqd",
            lifted.astype(jnp.bfloat16),
            value_block,
            preferred_element_type=jnp.float32,
        )
        return (new_peak, denominator, weighted)

    query_total = query_count * group_size
    initial = (
        jnp.full((kv_local, query_total), masked, jnp.float32),
        jnp.zeros((kv_local, query_total), jnp.float32),
        jnp.zeros((kv_local, query_total, HEAD), jnp.float32),
    )
    key_piece = lax.all_gather(key_rows, "seq", axis=0, tiled=True)
    value_piece = lax.all_gather(value_rows, "seq", axis=0, tiled=True)
    piece_rows = key_piece.shape[0]
    block_rows = block_size(piece_rows, shard_rows)
    turn_count = piece_rows // block_rows
    key_blocks = key_piece.reshape(turn_count, block_rows, kv_local, HEAD)
    value_blocks = value_piece.reshape(turn_count, block_rows, kv_local, HEAD)

    def one_turn(turn_index, inner_running):
        whole_index = turn_index * block_rows + jnp.arange(block_rows, dtype=jnp.int32)
        return attend_block(
            inner_running, key_blocks[turn_index], value_blocks[turn_index], key_index(whole_index)
        )

    row_peak, denominator, weighted = lax.fori_loop(0, turn_count, one_turn, initial)
    attended = (weighted / denominator[:, :, None]).astype(jnp.bfloat16)
    attended = (
        attended.reshape(kv_local, query_count, group_size, HEAD)
        .transpose(1, 0, 2, 3)
        .reshape(query_count, kv_local * group_size * HEAD)
    )
    projected = jnp.dot(attended, return_weight, preferred_element_type=jnp.float32)
    returned = lax.psum_scatter(
        projected.astype(jnp.bfloat16), "mp", scatter_dimension=1, tiled=True
    )
    slot_ids = jnp.arange(slot_count, dtype=jnp.int32)
    lead_slot = (own_shard - offsets) % shards
    local_span = slot_ids[:, None] * shards + lead_slot[None, :]
    back_index = (offsets[None, :] + local_span - own_shard) // shards
    alive = local_span < span_counts[None, :]
    back_rows = jnp.where(
        alive[:, :, None],
        returned[jnp.clip(back_index, 0, CH_OWN - 1)],
        jnp.zeros((), jnp.bfloat16),
    )
    arrived = lax.all_to_all(back_rows, "seq", split_axis=1, concat_axis=1, tiled=True)
    span_results = jnp.roll(arrived, -(own_offset % shards), axis=1).reshape(capacity, column_count)
    positions = jnp.arange(rows_here, dtype=jnp.int32)
    live_slots = jnp.arange(capacity, dtype=jnp.int32) < own_count
    passed = jnp.sum(
        ((own_marks[None, :] <= positions[:, None]) & live_slots[None, :]).astype(jnp.int32), axis=1
    )
    return (skip_part.astype(jnp.float32) + span_results[passed - 1].astype(jnp.float32)).astype(
        jnp.bfloat16
    )


def solution(mesh):
    in_specs = (
        P("seq", None),
        P(),
        P(None, "mp"),
        P(None, "mp"),
        P("mp"),
        P("mp", None),
        P("seq", None),
        P(),
        P("seq", "mp"),
        P("mp"),
        P(),
        P("seq", "mp"),
        P("seq", "mp"),
        P("seq", "mp"),
        P("mp", None),
    )
    out_specs = P("seq", "mp")
    def on_device(*arrays):
        heads_here = arrays[11].shape[1] // HEAD
        fits = heads_here == mesh.shape["seq"] and mesh.shape["mp"] == 2
        return (one_head_each if fits else spread_heads)(*arrays)

    return jax.shard_map(
        on_device, mesh=mesh, in_specs=in_specs, out_specs=out_specs, check_vma=False
    )
```

```python
import functools
import math

import jax
import jax.numpy as jnp
from jax import lax
from jax.experimental import pallas as pl
from jax.experimental.pallas import tpu as pltpu
from jax.sharding import PartitionSpec as P

HEADS = 32
KV_HEADS = 8
HEAD = 128
CH_OWN = 64


eps = 1e-05
masked = -1e30
TILE = 16


def swapped(value):
    return lax.ppermute(value, "mp", [(0, 1), (1, 0)])


def vmem():
    return pl.BlockSpec(memory_space=pltpu.VMEM)


def smem():
    return pl.BlockSpec(memory_space=pltpu.SMEM)


def in_place():
    return pl.BlockSpec(memory_space=pl.ANY)


def in_hbm():
    return pl.BlockSpec(memory_space=pltpu.HBM)


def seat():
    return lax.axis_index("seq"), lax.axis_index("mp")


def params(mebibytes=24):
    return pltpu.CompilerParams(vmem_limit_bytes=mebibytes * 2**20)


def brief():
    return pl.CostEstimate(flops=1, bytes_accessed=1, transcendentals=0)


def lanes(which, size):
    return pl.ds(pl.multiple_of(which * size, size), size)


def rows_at(which, size):
    return pl.ds(pl.multiple_of(which * size, size), size)


def start_all(pairs, sems):
    copies = []
    for index, (from_ref, to_ref) in enumerate(pairs):
        copy = pltpu.make_async_copy(from_ref, to_ref, sems.at[index])
        copy.start()
        copies.append(copy)
    return copies


def copy_all(pairs, sems):
    for copy in start_all(pairs, sems):
        copy.wait()


def one_minus_exp(u):
    series = jnp.ones_like(u)
    for order in range(9, 1, -1):
        series = 1.0 - u * (1.0 / order) * series
    return jnp.where(u < 0.5, u * series, 1.0 - jnp.exp(-u))


def softplus(v):
    tail = jnp.exp(-jnp.abs(v))
    series = jnp.ones_like(tail)
    for order in range(6, 1, -1):
        series = 1.0 - tail * ((order - 1.0) / order) * series
    return jnp.maximum(v, 0.0) + jnp.where(tail < 0.03, tail * series, jnp.log(1.0 + tail))


def start_cuts(plane, query_ref, key_ref, value_ref, pair_outs, sems):
    layers = len(pair_outs)
    me, _ = seat()
    layer = me // plane
    group = plane * HEAD
    pairs = []
    for step, out_ref in enumerate(pair_outs):
        target = layer ^ step
        pairs.append((query_ref.at[:, lanes(target, group)], out_ref.at[:, pl.ds(0, group)]))
        pairs.append((key_ref.at[:, lanes(target, HEAD)], out_ref.at[:, pl.ds(group, HEAD)]))
        pairs.append(
            (value_ref.at[:, lanes(target, HEAD)], out_ref.at[:, pl.ds(group + HEAD, HEAD)])
        )
    return start_all(pairs, sems)


def scan_kernel(plane, layers, *refs):
    bytes_hbm, gain_ref, input_hbm, step_hbm, rate_ref = refs[:5]
    others, refs = refs[5:8], refs[8:]
    local_ref, through_ref, ends_ref = refs[:3]
    pair_outs, refs = refs[3 : 3 + layers], refs[3 + layers :]
    bytes_ref, input_ref, step_ref, *held, sems, cut_sems = refs
    fetches = start_all(
        [(bytes_hbm, bytes_ref), (step_hbm, step_ref), (input_hbm, input_ref), *zip(others, held)],
        sems,
    )
    fetches[0].wait()
    values = bytes_ref[...].astype(jnp.float32)
    scale = lax.rsqrt(jnp.mean(values * values, axis=1, keepdims=True) + eps)
    normed = (values * scale * gain_ref[...]).astype(jnp.bfloat16)
    fetches[1].wait()
    steps = softplus(jnp.dot(normed, step_ref[...], preferred_element_type=jnp.float32))
    rate_steps = steps * rate_ref[...]
    fetches[2].wait()
    inputs = jnp.dot(normed, input_ref[...], preferred_element_type=jnp.float32)
    for fetch in fetches[3:]:
        fetch.wait()
    cuts = start_cuts(plane, *held, pair_outs, cut_sems)
    decays = jnp.exp(-rate_steps)
    drives = jnp.sqrt(one_minus_exp(2.0 * rate_steps)) * inputs
    rows, width = decays.shape
    tile = 8
    decays = decays.reshape(rows // tile, tile, width)
    drives = drives.reshape(rows // tile, tile, width)
    place = lax.broadcasted_iota(jnp.int32, decays.shape, 1)
    for reach in (1, 2, 4):
        before_decays = pltpu.roll(decays, reach, 1)
        before_drives = pltpu.roll(drives, reach, 1)
        inside = place >= reach
        drives = jnp.where(inside, decays * before_drives + drives, drives)
        decays = jnp.where(inside, decays * before_decays, decays)
    state = jnp.zeros((1, width), jnp.float32)
    kept = jnp.ones((1, width), jnp.float32)
    for index in range(rows // tile):
        states = decays[index] * state + drives[index]
        passing = decays[index] * kept
        local_ref[pl.ds(index * tile, tile), :] = states
        through_ref[pl.ds(index * tile, tile), :] = passing
        state = states[tile - 1 :, :]
        kept = passing[tile - 1 :, :]
    for index in range(ends_ref.shape[0]):
        ends_ref[index, 0:1, :] = kept
        ends_ref[index, 1:2, :] = state
    for cut in cuts:
        cut.wait()


def states_kernel(local_ref, through_ref, mixer_ref, ends_ref, states_ref, other_ref):
    me, lane = seat()
    carry = jnp.zeros((1, local_ref.shape[1]), jnp.float32)
    for shard in range(ends_ref.shape[0]):
        later = ends_ref[shard, 0:1, :] * carry + ends_ref[shard, 1:2, :]
        carry = jnp.where(shard < me, later, carry)
    states = (local_ref[...] + through_ref[...] * carry).astype(jnp.bfloat16)
    states_ref[...] = states
    half = other_ref.shape[1]
    other_ref[...] = jnp.dot(
        states, mixer_ref[:, lanes(1 - lane, half)], preferred_element_type=jnp.float32
    )


def pool_kernel(plane, *refs):
    states_ref, mixer_ref, other_ref, bytes_ref, pick_ref = refs[:5]
    layers = len(refs) - 8 - plane
    up_pieces, (encoded_ref, out_ref, *up_refs, sems) = refs[5 : 5 + layers], refs[5 + layers :]
    cross = lax.rem(seat()[0], plane)
    pairs = []
    for mask, up_ref in enumerate(up_refs):
        size = 2 * up_ref.shape[2] // layers
        for step, piece in enumerate(up_pieces):
            for number in range(layers // 2):
                columns = lanes(number * plane + (cross ^ mask), size)
                pairs.append((piece.at[:, columns], up_ref.at[step, :, pl.ds(number * size, size)]))
    copies = start_all(pairs, sems)
    half = other_ref.shape[1]
    columns = lanes(seat()[1], half)
    mixed = jnp.dot(states_ref[...], mixer_ref[:, columns], preferred_element_type=jnp.float32)
    skip = bytes_ref[:, columns].astype(jnp.float32)
    encoded = (skip + (mixed + other_ref[...])).astype(jnp.bfloat16)
    encoded_ref[...] = encoded
    picked = jnp.dot(pick_ref[...], encoded, preferred_element_type=jnp.float32)
    out_ref[...] = picked.astype(jnp.bfloat16).reshape(out_ref.shape)
    for copy in copies:
        copy.wait()


def own_kernel(pick_ref, arrived_ref, out_ref):
    shards, slots, half = arrived_ref.shape
    rows = arrived_ref[...].astype(jnp.float32).reshape(shards * slots, half)
    own = jnp.dot(
        pick_ref[...], rows.astype(jnp.bfloat16), preferred_element_type=jnp.float32
    ).astype(jnp.bfloat16)
    for index in range(out_ref.shape[0]):
        out_ref[index] = own


def inner_kernel(plane, layers, bias_ref, gain_ref, near_ref, far_ref, *refs):
    up_own, refs = refs[:plane], refs[plane:]
    up_far, refs = refs[:plane], refs[plane:]
    pieces, refs = refs[:layers], refs[layers:]
    out_ref, pooled, up, weights, squares, sems = refs
    me, lane = seat()
    layer, cross = me // plane, lax.rem(me, plane)
    half = near_ref.shape[1]
    up_rows, up_half = up_own[0].shape[1:]
    pairs = [
        (near_ref, pooled.at[:, lanes(lane, half)]),
        (far_ref, pooled.at[:, lanes(1 - lane, half)]),
    ]
    for step in range(layers):
        for mask in range(plane):
            where = rows_at((layer ^ step) * plane + (cross ^ mask), up_rows)
            pairs.append((up_own[mask].at[step], up.at[where, lanes(lane, up_half)]))
            pairs.append((up_far[mask].at[step], up.at[where, lanes(1 - lane, up_half)]))
    for step, piece in enumerate(pieces):
        pairs.append((piece, weights.at[rows_at(layer ^ step, piece.shape[0]), :]))
    copies = start_all(pairs, sems)
    for copy in copies[:-layers]:
        copy.wait()
    rows = pooled.shape[0]
    block = rows // plane
    ones = jnp.ones((8, up.shape[1]), jnp.bfloat16)
    for index in range(plane):
        where = pl.ds(index * block, block)
        widened = jnp.dot(pooled[where, :], up[...], preferred_element_type=jnp.float32)
        widened = (widened + bias_ref[...]).astype(jnp.bfloat16).astype(jnp.float32)
        inner = (widened * gain_ref[...]).astype(jnp.bfloat16)
        square = widened * widened
        coarse = square.astype(jnp.bfloat16)
        fine = (square - coarse.astype(jnp.float32)).astype(jnp.bfloat16)
        squares[:, where] = sum(
            lax.dot_general(
                ones, part, (((1,), (1,)), ((), ())), preferred_element_type=jnp.float32
            )
            for part in (coarse, fine)
        )
        if index == 0:
            for copy in copies[-layers:]:
                copy.wait()
        sums = jnp.dot(inner, weights[...], preferred_element_type=jnp.float32)
        sums = sums.astype(jnp.bfloat16)
        for head in range(plane):
            out_ref[head, where, :] = sums[:, head * HEAD : (head + 1) * HEAD]
        for number in range(2):
            start = (plane + number) * HEAD
            out_ref[index, pl.ds(rows + number * block, block), :] = sums[:, start : start + HEAD]
    total = jnp.concatenate(
        [squares[0:1, start : start + HEAD] for start in range(0, rows, HEAD)], axis=0
    )
    coarse = total.astype(jnp.bfloat16).astype(jnp.float32)
    both = jnp.concatenate([coarse, total - coarse], axis=0).astype(jnp.bfloat16)
    for index in range(plane):
        out_ref[index, pl.ds(rows + 2 * block, both.shape[0]), :] = both


def heads_kernel(features, got_ref, query_ref, pair_ref, queries):
    plane = got_ref.shape[0]
    rows = query_ref.shape[0]
    block = rows // plane
    lines = rows // HEAD
    shards = rows // CH_OWN
    layers = shards // plane
    first = rows + 2 * block

    def added(start, size):
        parts = [got_ref[index, start : start + size, :].astype(jnp.float32) for index in range(plane)]
        return sum(parts[1:], parts[0])

    both = added(first, 2 * lines)
    total = both[:lines, :] + both[lines:, :]
    scale = jnp.transpose(lax.rsqrt(total * (1.0 / features) + eps))
    for line in range(lines):
        scaled = added(line * HEAD, HEAD) * scale[:, line : line + 1]
        for start in range(0, HEAD, CH_OWN):
            index = (line * HEAD + start) // CH_OWN
            shard = (index % layers) * plane + index // layers
            queries[pl.ds(shard, CH_OWN, stride=shards), :] = scaled[start : start + CH_OWN, :]
    query_ref[...] = queries[...].astype(jnp.bfloat16)
    cross = lax.rem(seat()[0], plane)
    per_block = block // HEAD
    for line in range(per_block):
        mine = scale[:, line : line + 1]
        for index in range(1, plane):
            column = index * per_block + line
            mine = jnp.where(cross == index, scale[:, column : column + 1], mine)
        for number in range(2):
            start = number * block + line * HEAD
            pair = (added(rows + start, HEAD) * mine).astype(jnp.bfloat16)
            for index in range(plane):
                pair_ref[index, pl.ds(start, HEAD), :] = pair


def attend_kernel(place_ref, query_ref, pair_ref, out_ref, natural, keys, values, attended):
    rows = query_ref.shape[0]
    window = out_ref.shape[1]
    plane = pair_ref.shape[0]
    part = rows // plane
    shards = rows // CH_OWN
    layers = shards // plane
    for number, held in enumerate((keys, values)):
        for cross in range(plane):
            for layer in range(layers):
                piece = pair_ref[cross, pl.ds(number * part + layer * CH_OWN, CH_OWN), :]
                where = pl.ds(layer * plane + cross, CH_OWN, stride=shards)
                natural[where, :] = piece.astype(jnp.float32)
        held[...] = natural[...].astype(jnp.bfloat16)
    block = min(256, rows)
    score_scale = 1.0 / math.sqrt(HEAD)
    for start in range(0, rows, block):
        stop = start + block
        scores = lax.dot_general(
            query_ref[start:stop, :],
            keys[0:stop, :],
            (((1,), (1,)), ((), ())),
            preferred_element_type=jnp.float32,
        )
        spots = lax.broadcasted_iota(jnp.int32, scores.shape, 1)
        mine = lax.broadcasted_iota(jnp.int32, scores.shape, 0) + start
        scores = jnp.where(spots <= mine, scores * score_scale, masked)
        peak = jnp.max(scores, axis=1, keepdims=True)
        lifted = jnp.exp(scores - peak)
        denominator = jnp.sum(lifted, axis=1, keepdims=True)
        weighted = jnp.dot(
            lifted.astype(jnp.bfloat16), values[0:stop, :], preferred_element_type=jnp.float32
        )
        attended[start:stop, :] = (weighted / denominator).astype(jnp.bfloat16)
    attended[rows:, :] = jnp.zeros((attended.shape[0] - rows, HEAD), jnp.bfloat16)
    for shard in range(out_ref.shape[0]):
        first = place_ref[shard]
        out_ref[shard] = attended[pl.ds(pl.multiple_of(first * TILE, TILE), window), :]


def return_kernel(weight_ref, pieces_ref, own_ref, other_ref, attended):
    half = own_ref.shape[1]
    lane = seat()[1]
    for head in range(pieces_ref.shape[0]):
        attended[:, head * HEAD : (head + 1) * HEAD] = pieces_ref[head]
    other_ref[...] = jnp.dot(
        attended[...], weight_ref[:, lanes(1 - lane, half)], preferred_element_type=jnp.float32
    )
    own_ref[...] = jnp.dot(
        attended[...], weight_ref[:, lanes(lane, half)], preferred_element_type=jnp.float32
    )


def join_kernel(own_ref, other_ref, encoded_ref, spread_ref, out_ref):
    returned = (own_ref[...] + other_ref[...]).astype(jnp.bfloat16)
    results = jnp.dot(spread_ref[...], returned, preferred_element_type=jnp.float32)
    out_ref[...] = (encoded_ref[...].astype(jnp.float32) + results).astype(jnp.bfloat16)


def one_head_each(
    byte_states,
    outer_gain,
    mamba_input,
    mamba_step,
    decay_rate,
    mixer_weight,
    boundaries,
    span_counts,
    up_weight,
    up_bias,
    inner_gain,
    query_weight,
    key_weight,
    value_weight,
    return_weight,
):
    shards = lax.axis_size("seq")
    me = lax.axis_index("seq")
    lane = lax.axis_index("mp")
    plane = HEADS // KV_HEADS
    layers = shards // plane
    rows_here, width = byte_states.shape
    half = mamba_input.shape[1]
    capacity = boundaries.shape[1]
    window = capacity + TILE
    total_rows = CH_OWN * shards
    inner_width = inner_gain.shape[0]
    inner_half = up_bias.shape[0]
    weight_rows = query_weight.shape[0]
    f32, bf16 = jnp.float32, jnp.bfloat16
    layer, cross = me // plane, me % plane
    layer_groups = [[first + plane * step for step in range(layers)] for first in range(plane)]
    plane_groups = [[first * plane + step for step in range(plane)] for first in range(layers)]

    def over(value, mask):
        return lax.ppermute(value, "seq", [(i, i ^ mask) for i in range(shards)])

    def after(value, done):
        return lax.optimization_barrier((value, done))[0]

    own_bias = up_bias.reshape(layers // 2, plane, weight_rows)
    own_bias = lax.dynamic_index_in_dim(own_bias, cross, 1, keepdims=False).reshape(1, -1)
    own_gain = inner_gain.reshape(layers, plane, weight_rows)
    own_gain = lax.dynamic_index_in_dim(own_gain, cross, 1, keepdims=False).reshape(1, -1)

    seq_ids = jnp.arange(shards, dtype=jnp.int32)
    offsets = jnp.cumsum(span_counts) - span_counts
    own_offset = jnp.sum(jnp.where(seq_ids == me, offsets, 0))
    own_count = jnp.sum(jnp.where(seq_ids == me, span_counts, 0))
    place = offsets // TILE
    own_marks = boundaries[0]
    positions = jnp.arange(rows_here, dtype=jnp.int32)
    spans_here = jnp.arange(capacity, dtype=jnp.int32)
    live = spans_here < own_count
    slots = capacity // shards
    slot_ids = jnp.arange(slots, dtype=jnp.int32)
    local_span = slot_ids[None, :] * shards + ((seq_ids - own_offset) % shards)[:, None]
    is_span = spans_here[None, :] == local_span.reshape(-1)[:, None]
    byte_at = jnp.sum(jnp.where(is_span, jnp.minimum(own_marks, rows_here - 1)[None, :], 0), axis=1)
    pool_pick = (positions[None, :] == byte_at[:, None]).astype(bf16)
    own_spans = me + jnp.arange(CH_OWN, dtype=jnp.int32) * shards
    origin = jnp.sum((offsets[None, :] <= own_spans[:, None]).astype(jnp.int32), axis=1) - 1
    origin_offset = jnp.sum(
        jnp.where(seq_ids[None, :] == origin[:, None], offsets[None, :], 0), axis=1
    )
    arrived_row = origin * slots + (own_spans - origin_offset) // shards
    own_pick = (
        jnp.arange(shards * slots, dtype=jnp.int32)[None, :] == arrived_row[:, None]
    ).astype(bf16)
    passed = jnp.sum(
        ((own_marks[None, :] <= positions[:, None]) & live[None, :]).astype(jnp.int32), axis=1
    )
    result_row = passed - 1 + own_offset % TILE
    spread = (jnp.arange(window, dtype=jnp.int32)[None, :] == result_row[:, None]).astype(bf16)

    up_half = inner_half // plane
    up_layers = [up_weight]
    for bit in range(layers.bit_length() - 2, -1, -1):
        up_layers += [over(piece, plane << bit) for piece in up_layers]
    order = [0]
    for bit in range(layers.bit_length() - 2, -1, -1):
        order += [step ^ (1 << bit) for step in order]
    up_layers = [up_layers[order.index(step)] for step in range(layers)]

    local, through, ends, *pair_cuts = pl.pallas_call(
        functools.partial(scan_kernel, plane, layers),
        out_shape=(
            jax.ShapeDtypeStruct((rows_here, half), f32),
            jax.ShapeDtypeStruct((rows_here, half), f32),
            jax.ShapeDtypeStruct((shards, 2, half), f32),
        )
        + (jax.ShapeDtypeStruct((weight_rows, (plane + 2) * HEAD), bf16),) * layers,
        in_specs=[in_hbm(), vmem(), in_hbm(), in_hbm(), vmem()] + [in_hbm()] * 3,
        out_specs=(vmem(),) * 3 + (in_place(),) * layers,
        scratch_shapes=[
            pltpu.VMEM(array.shape, bf16)
            for array in (
                byte_states,
                mamba_input,
                mamba_step,
                query_weight,
                key_weight,
                value_weight,
            )
        ]
        + [pltpu.SemaphoreType.DMA((6,)), pltpu.SemaphoreType.DMA((3 * layers,))],
        cost_estimate=brief(),
        compiler_params=params(56),
    )(
        byte_states,
        outer_gain[None, :],
        mamba_input,
        mamba_step,
        decay_rate[None, :],
        query_weight,
        key_weight,
        value_weight,
    )
    ends = lax.all_to_all(ends, "seq", 0, 0, tiled=True)
    ends, up_layers[1], up_layers[2] = lax.optimization_barrier(
        (ends, up_layers[1], up_layers[2])
    )
    pieces = [pair_cuts[0]] + [over(pair_cuts[step], plane * step) for step in range(1, layers)]
    states, other_part = pl.pallas_call(
        states_kernel,
        out_shape=(
            jax.ShapeDtypeStruct((rows_here, half), bf16),
            jax.ShapeDtypeStruct((rows_here, half), f32),
        ),
        in_specs=[vmem()] * 4,
        out_specs=(vmem(),) * 2,
        cost_estimate=brief(),
        compiler_params=params(56),
    )(local, through, mixer_weight, ends)
    far_bias = swapped(own_bias)
    bias = jnp.where(
        lane == 0,
        jnp.concatenate([own_bias, far_bias], axis=1),
        jnp.concatenate([far_bias, own_bias], axis=1),
    )
    far_part, bias, pieces = lax.optimization_barrier((swapped(other_part), bias, pieces))
    encoded, leaving, *up_cuts = pl.pallas_call(
        functools.partial(pool_kernel, plane),
        out_shape=(
            jax.ShapeDtypeStruct((rows_here, half), bf16),
            jax.ShapeDtypeStruct((shards, slots, half), bf16),
        )
        + (jax.ShapeDtypeStruct((layers, up_weight.shape[0], up_half), bf16),) * plane,
        in_specs=[vmem()] * 5 + [in_place()] * layers,
        out_specs=(vmem(),) * (2 + plane),
        scratch_shapes=[pltpu.SemaphoreType.DMA((plane * layers * layers // 2,))],
        cost_estimate=brief(),
        compiler_params=params(56),
    )(states, mixer_weight, far_part, byte_states, pool_pick, *up_layers)
    arrived = lax.all_to_all(leaving, "seq", 0, 0, tiled=True)
    up_own = [up_cuts[0]] + [over(up_cuts[mask], mask) for mask in range(1, plane)]
    own_rows = pl.pallas_call(
        own_kernel,
        out_shape=jax.ShapeDtypeStruct((layers, CH_OWN, half), bf16),
        in_specs=[vmem()] * 2,
        out_specs=vmem(),
        cost_estimate=brief(),
        compiler_params=params(56),
    )(own_pick, arrived)
    near_layer = lax.all_to_all(
        own_rows, "seq", 0, 0, axis_index_groups=layer_groups, tiled=True
    )
    up_far = [swapped(piece) for piece in up_own]
    near_layer, up_far = lax.optimization_barrier((near_layer, up_far))
    near = lax.all_to_all(
        jnp.broadcast_to(near_layer[None], (plane, layers, CH_OWN, half)),
        "seq",
        0,
        0,
        axis_index_groups=plane_groups,
        tiled=True,
    ).reshape(total_rows, half)

    features = own_gain.shape[1]
    block = total_rows // plane
    sent_rows = total_rows + 2 * block + 2 * (total_rows // HEAD)
    partial_sums = pl.pallas_call(
        functools.partial(inner_kernel, plane, layers),
        out_shape=jax.ShapeDtypeStruct((plane, sent_rows, HEAD), bf16),
        in_specs=[vmem()] * 2 + [in_place()] * (2 + 2 * plane + layers),
        out_specs=vmem(),
        scratch_shapes=[
            pltpu.VMEM((total_rows, width), bf16),
            pltpu.VMEM((width, features), bf16),
            pltpu.VMEM((features, (plane + 2) * HEAD), bf16),
            pltpu.VMEM((8, total_rows), f32),
            pltpu.SemaphoreType.DMA((2 + 2 * shards + layers,)),
        ],
        cost_estimate=brief(),
        compiler_params=params(56),
    )(bias, own_gain, near, swapped(near), *up_own, *up_far, *pieces)
    got = lax.all_to_all(
        partial_sums, "seq", 0, 0, axis_index_groups=plane_groups, tiled=True
    )
    queries, pairs = pl.pallas_call(
        functools.partial(heads_kernel, inner_width),
        out_shape=(
            jax.ShapeDtypeStruct((total_rows, HEAD), bf16),
            jax.ShapeDtypeStruct((plane, 2 * block, HEAD), bf16),
        ),
        in_specs=[vmem()],
        out_specs=(vmem(),) * 2,
        scratch_shapes=[pltpu.VMEM((total_rows, HEAD), f32)],
        cost_estimate=brief(),
        compiler_params=params(10),
    )(got)
    pairs = lax.all_to_all(pairs, "seq", 0, 0, axis_index_groups=plane_groups, tiled=True)
    leaving = pl.pallas_call(
        attend_kernel,
        out_shape=jax.ShapeDtypeStruct((shards, window, HEAD), bf16),
        in_specs=[smem()] + [vmem()] * 2,
        out_specs=vmem(),
        scratch_shapes=[
            pltpu.VMEM((total_rows, HEAD), f32),
            pltpu.VMEM((total_rows, HEAD), bf16),
            pltpu.VMEM((total_rows, HEAD), bf16),
            pltpu.VMEM((total_rows + window, HEAD), bf16),
        ],
        cost_estimate=brief(),
        compiler_params=params(12),
    )(place, queries, pairs)
    pieces = lax.all_to_all(leaving, "seq", 0, 0, tiled=True)
    own_back, other_back = pl.pallas_call(
        return_kernel,
        out_shape=(jax.ShapeDtypeStruct((window, half), f32),) * 2,
        in_specs=[vmem()] * 2,
        out_specs=(vmem(),) * 2,
        scratch_shapes=[pltpu.VMEM((window, shards * HEAD), bf16)],
        cost_estimate=brief(),
        compiler_params=params(12),
    )(return_weight, pieces)
    return pl.pallas_call(
        join_kernel,
        out_shape=jax.ShapeDtypeStruct((rows_here, half), bf16),
        in_specs=[vmem()] * 4,
        out_specs=vmem(),
        cost_estimate=brief(),
        compiler_params=params(8),
    )(own_back, swapped(other_back), encoded, spread)


def prefix(value, axis, join, neutral):
    count, mine = (lax.axis_size(axis), lax.axis_index(axis))
    pieces = jax.tree.map(lambda part: lax.all_gather(part, axis), value)
    so_far = jax.tree.map(
        lambda part, zero: jnp.full_like(part, 0) + jnp.asarray(zero, part.dtype), value, neutral
    )

    def lap(position, so_far):
        longer = join(so_far, jax.tree.map(lambda part: part[position], pieces))
        return jax.tree.map(lambda new, old: jnp.where(position < mine, new, old), longer, so_far)

    return lax.fori_loop(0, count - 1, lap, so_far)


def rms_scale(values, gain):
    values = values.astype(jnp.float32)
    return values * lax.rsqrt(jnp.mean(values * values, axis=-1, keepdims=True) + eps) * gain


def combine_pairs(earlier, later):
    return (earlier[0] * later[0], later[0] * earlier[1] + later[1])


def pick_table(table, wanted, seq_ids):
    return jnp.sum(jnp.where(seq_ids[None, :] == wanted[:, None], table[None, :], 0), axis=1)


def block_size(piece_rows, shard_rows):
    limit = max(1, 1024 // shard_rows)
    pieces = max(1, piece_rows // shard_rows)
    best_size = 1
    for candidate in range(1, limit + 1):
        if pieces % candidate == 0:
            best_size = candidate
    return min(piece_rows, best_size * shard_rows)


def spread_heads(
    byte_states,
    outer_gain,
    mamba_input,
    mamba_step,
    decay_rate,
    mixer_weight,
    boundaries,
    span_counts,
    up_weight,
    up_bias,
    inner_gain,
    query_weight,
    key_weight,
    value_weight,
    return_weight,
):
    shards = lax.axis_size("seq")
    own_shard = lax.axis_index("seq")
    own_lane = lax.axis_index("mp")
    rows_here = byte_states.shape[0]
    capacity = boundaries.shape[1]
    column_count = mamba_input.shape[1]
    kv_local = key_weight.shape[1] // HEAD
    group_size = HEADS // KV_HEADS
    slot_count = capacity // shards
    offsets = jnp.cumsum(span_counts) - span_counts
    seq_ids = jnp.arange(shards, dtype=jnp.int32)
    own_offset = jnp.sum(jnp.where(seq_ids == own_shard, offsets, 0))
    own_count = jnp.sum(jnp.where(seq_ids == own_shard, span_counts, 0))
    normed = rms_scale(byte_states, outer_gain).astype(jnp.bfloat16)
    inputs = jnp.dot(normed, mamba_input, preferred_element_type=jnp.float32)
    step_sizes = jax.nn.softplus(jnp.dot(normed, mamba_step, preferred_element_type=jnp.float32))
    rate_steps = step_sizes * decay_rate
    decays = jnp.exp(-rate_steps)
    drives = jnp.sqrt(-jnp.expm1(-2.0 * rate_steps)) * inputs
    through, local_states = lax.associative_scan(combine_pairs, (decays, drives), axis=0)
    starting = (jnp.ones((column_count,), jnp.float32), jnp.zeros((column_count,), jnp.float32))
    arriving = prefix((through[-1], local_states[-1]), "seq", combine_pairs, starting)
    states = (local_states + through * arriving[1][None, :]).astype(jnp.bfloat16)
    partial_value = jnp.dot(states, mixer_weight, preferred_element_type=jnp.float32)
    mixed_sum = lax.psum(partial_value, "mp")
    encoded = (byte_states.astype(jnp.float32) + mixed_sum).astype(jnp.bfloat16)
    skip_part = lax.dynamic_slice_in_dim(encoded, own_lane * column_count, column_count, 1)
    own_marks = boundaries[0]
    pooled = encoded[jnp.minimum(own_marks, rows_here - 1)]
    row_width = pooled.shape[1]
    outgoing = jnp.roll(pooled.reshape(slot_count, shards, row_width), own_offset % shards, axis=1)
    incoming = lax.all_to_all(outgoing, "seq", split_axis=1, concat_axis=1, tiled=True)
    position = jnp.arange(CH_OWN, dtype=jnp.int32)
    span_index = own_shard + position * shards
    source = jnp.sum((offsets[None, :] <= span_index[:, None]).astype(jnp.int32), axis=1) - 1
    source_offset = pick_table(offsets, source, seq_ids)
    slot_index = (span_index - source_offset) // shards
    gathered_rows = incoming.reshape(slot_count * shards, row_width)[slot_index * shards + source]
    columns = gathered_rows
    widened_sum = jnp.dot(
        columns,
        lax.all_gather(up_weight, "seq", axis=0, tiled=True),
        preferred_element_type=jnp.float32,
    )
    widened_share = (widened_sum + up_bias[None, :]).astype(jnp.bfloat16)
    widened = lax.all_gather(widened_share, "mp", axis=1, tiled=True)
    inner_normed = rms_scale(widened, inner_gain).astype(jnp.bfloat16)
    columns = inner_normed
    query_part = jnp.dot(
        columns,
        lax.all_gather(query_weight, "seq", axis=0, tiled=True),
        preferred_element_type=jnp.float32,
    )
    key_part = jnp.dot(
        columns,
        lax.all_gather(key_weight, "seq", axis=0, tiled=True),
        preferred_element_type=jnp.float32,
    )
    value_part = jnp.dot(
        columns,
        lax.all_gather(value_weight, "seq", axis=0, tiled=True),
        preferred_element_type=jnp.float32,
    )
    queries = query_part.astype(jnp.bfloat16)
    key_rows = key_part.astype(jnp.bfloat16)
    value_rows = value_part.astype(jnp.bfloat16)
    query_count = queries.shape[0]
    grouped = (
        queries.reshape(query_count, kv_local, group_size, HEAD)
        .transpose(1, 0, 2, 3)
        .reshape(kv_local, query_count * group_size, HEAD)
    )
    row_index = jnp.repeat(span_index, group_size)
    shard_rows = key_rows.shape[0]
    score_scale = 1.0 / math.sqrt(HEAD)

    def key_index(whole_index):
        return whole_index // shard_rows + whole_index % shard_rows * shards

    def attend_block(running, key_block, value_block, index_block):
        row_peak, denominator, weighted = running
        scores = (
            jnp.einsum("hqd,khd->hqk", grouped, key_block, preferred_element_type=jnp.float32)
            * score_scale
        )
        scores = jnp.where(index_block[None, None, :] <= row_index[None, :, None], scores, masked)
        new_peak = jnp.maximum(row_peak, jnp.max(scores, axis=2))
        shrink = jnp.exp(row_peak - new_peak)
        lifted = jnp.exp(scores - new_peak[:, :, None])
        denominator = denominator * shrink + jnp.sum(lifted, axis=2)
        weighted = weighted * shrink[:, :, None] + jnp.einsum(
            "hqk,khd->hqd",
            lifted.astype(jnp.bfloat16),
            value_block,
            preferred_element_type=jnp.float32,
        )
        return (new_peak, denominator, weighted)

    query_total = query_count * group_size
    initial = (
        jnp.full((kv_local, query_total), masked, jnp.float32),
        jnp.zeros((kv_local, query_total), jnp.float32),
        jnp.zeros((kv_local, query_total, HEAD), jnp.float32),
    )
    key_piece = lax.all_gather(key_rows, "seq", axis=0, tiled=True)
    value_piece = lax.all_gather(value_rows, "seq", axis=0, tiled=True)
    piece_rows = key_piece.shape[0]
    block_rows = block_size(piece_rows, shard_rows)
    turn_count = piece_rows // block_rows
    key_blocks = key_piece.reshape(turn_count, block_rows, kv_local, HEAD)
    value_blocks = value_piece.reshape(turn_count, block_rows, kv_local, HEAD)

    def one_turn(turn_index, inner_running):
        whole_index = turn_index * block_rows + jnp.arange(block_rows, dtype=jnp.int32)
        return attend_block(
            inner_running, key_blocks[turn_index], value_blocks[turn_index], key_index(whole_index)
        )

    row_peak, denominator, weighted = lax.fori_loop(0, turn_count, one_turn, initial)
    attended = (weighted / denominator[:, :, None]).astype(jnp.bfloat16)
    attended = (
        attended.reshape(kv_local, query_count, group_size, HEAD)
        .transpose(1, 0, 2, 3)
        .reshape(query_count, kv_local * group_size * HEAD)
    )
    projected = jnp.dot(attended, return_weight, preferred_element_type=jnp.float32)
    returned = lax.psum_scatter(
        projected.astype(jnp.bfloat16), "mp", scatter_dimension=1, tiled=True
    )
    slot_ids = jnp.arange(slot_count, dtype=jnp.int32)
    lead_slot = (own_shard - offsets) % shards
    local_span = slot_ids[:, None] * shards + lead_slot[None, :]
    back_index = (offsets[None, :] + local_span - own_shard) // shards
    alive = local_span < span_counts[None, :]
    back_rows = jnp.where(
        alive[:, :, None],
        returned[jnp.clip(back_index, 0, CH_OWN - 1)],
        jnp.zeros((), jnp.bfloat16),
    )
    arrived = lax.all_to_all(back_rows, "seq", split_axis=1, concat_axis=1, tiled=True)
    span_results = jnp.roll(arrived, -(own_offset % shards), axis=1).reshape(capacity, column_count)
    positions = jnp.arange(rows_here, dtype=jnp.int32)
    live_slots = jnp.arange(capacity, dtype=jnp.int32) < own_count
    passed = jnp.sum(
        ((own_marks[None, :] <= positions[:, None]) & live_slots[None, :]).astype(jnp.int32), axis=1
    )
    return (skip_part.astype(jnp.float32) + span_results[passed - 1].astype(jnp.float32)).astype(
        jnp.bfloat16
    )


def solution(mesh):
    in_specs = (
        P("seq", None),
        P(),
        P(None, "mp"),
        P(None, "mp"),
        P("mp"),
        P("mp", None),
        P("seq", None),
        P(),
        P("seq", "mp"),
        P("mp"),
        P(),
        P("seq", "mp"),
        P("seq", "mp"),
        P("seq", "mp"),
        P("mp", None),
    )
    out_specs = P("seq", "mp")
    def on_device(*arrays):
        heads_here = arrays[11].shape[1] // HEAD
        fits = heads_here == mesh.shape["seq"] and mesh.shape["mp"] == 2
        return (one_head_each if fits else spread_heads)(*arrays)

    return jax.shard_map(
        on_device, mesh=mesh, in_specs=in_specs, out_specs=out_specs, check_vma=False
    )
```

```python
import functools
import math

import jax
import jax.numpy as jnp
from jax import lax
from jax.experimental import pallas as pl
from jax.experimental.pallas import tpu as pltpu
from jax.sharding import PartitionSpec as P

HEADS = 32
KV_HEADS = 8
HEAD = 128
CH_OWN = 64


eps = 1e-05
masked = -1e30
TILE = 16


def swapped(value):
    return lax.ppermute(value, "mp", [(0, 1), (1, 0)])


def vmem():
    return pl.BlockSpec(memory_space=pltpu.VMEM)


def smem():
    return pl.BlockSpec(memory_space=pltpu.SMEM)


def in_place():
    return pl.BlockSpec(memory_space=pl.ANY)


def in_hbm():
    return pl.BlockSpec(memory_space=pltpu.HBM)


def seat():
    return lax.axis_index("seq"), lax.axis_index("mp")


def params(mebibytes=24):
    return pltpu.CompilerParams(vmem_limit_bytes=mebibytes * 2**20)


def brief():
    return pl.CostEstimate(flops=1, bytes_accessed=1, transcendentals=0)


def lanes(which, size):
    return pl.ds(pl.multiple_of(which * size, size), size)


def rows_at(which, size):
    return pl.ds(pl.multiple_of(which * size, size), size)


def start_all(pairs, sems):
    copies = []
    for index, (from_ref, to_ref) in enumerate(pairs):
        copy = pltpu.make_async_copy(from_ref, to_ref, sems.at[index])
        copy.start()
        copies.append(copy)
    return copies


def copy_all(pairs, sems):
    for copy in start_all(pairs, sems):
        copy.wait()


def one_minus_exp(u):
    series = jnp.ones_like(u)
    for order in range(9, 1, -1):
        series = 1.0 - u * (1.0 / order) * series
    return jnp.where(u < 0.5, u * series, 1.0 - jnp.exp(-u))


def softplus(v):
    tail = jnp.exp(-jnp.abs(v))
    series = jnp.ones_like(tail)
    for order in range(6, 1, -1):
        series = 1.0 - tail * ((order - 1.0) / order) * series
    return jnp.maximum(v, 0.0) + jnp.where(tail < 0.03, tail * series, jnp.log(1.0 + tail))


def start_cuts(plane, query_ref, key_ref, value_ref, pair_outs, sems):
    layers = len(pair_outs)
    me, _ = seat()
    layer = me // plane
    group = plane * HEAD
    pairs = []
    for step, out_ref in enumerate(pair_outs):
        target = layer ^ step
        pairs.append((query_ref.at[:, lanes(target, group)], out_ref.at[:, pl.ds(0, group)]))
        pairs.append((key_ref.at[:, lanes(target, HEAD)], out_ref.at[:, pl.ds(group, HEAD)]))
        pairs.append(
            (value_ref.at[:, lanes(target, HEAD)], out_ref.at[:, pl.ds(group + HEAD, HEAD)])
        )
    return start_all(pairs, sems)


def scan_kernel(plane, layers, *refs):
    bytes_hbm, gain_ref, input_hbm, step_hbm, rate_ref = refs[:5]
    others, refs = refs[5:8], refs[8:]
    local_ref, through_ref, ends_ref = refs[:3]
    pair_outs, refs = refs[3 : 3 + layers], refs[3 + layers :]
    bytes_ref, input_ref, step_ref, *held, sems, cut_sems = refs
    fetches = start_all(
        [(bytes_hbm, bytes_ref), (step_hbm, step_ref), (input_hbm, input_ref), *zip(others, held)],
        sems,
    )
    fetches[0].wait()
    values = bytes_ref[...].astype(jnp.float32)
    scale = lax.rsqrt(jnp.mean(values * values, axis=1, keepdims=True) + eps)
    normed = (values * scale * gain_ref[...]).astype(jnp.bfloat16)
    fetches[1].wait()
    steps = softplus(jnp.dot(normed, step_ref[...], preferred_element_type=jnp.float32))
    rate_steps = steps * rate_ref[...]
    fetches[2].wait()
    inputs = jnp.dot(normed, input_ref[...], preferred_element_type=jnp.float32)
    for fetch in fetches[3:]:
        fetch.wait()
    cuts = start_cuts(plane, *held, pair_outs, cut_sems)
    decays = jnp.exp(-rate_steps)
    drives = jnp.sqrt(one_minus_exp(2.0 * rate_steps)) * inputs
    rows, width = decays.shape
    tile = 8
    decays = decays.reshape(rows // tile, tile, width)
    drives = drives.reshape(rows // tile, tile, width)
    place = lax.broadcasted_iota(jnp.int32, decays.shape, 1)
    for reach in (1, 2, 4):
        before_decays = pltpu.roll(decays, reach, 1)
        before_drives = pltpu.roll(drives, reach, 1)
        inside = place >= reach
        drives = jnp.where(inside, decays * before_drives + drives, drives)
        decays = jnp.where(inside, decays * before_decays, decays)
    state = jnp.zeros((1, width), jnp.float32)
    kept = jnp.ones((1, width), jnp.float32)
    for index in range(rows // tile):
        states = decays[index] * state + drives[index]
        passing = decays[index] * kept
        local_ref[pl.ds(index * tile, tile), :] = states
        through_ref[pl.ds(index * tile, tile), :] = passing
        state = states[tile - 1 :, :]
        kept = passing[tile - 1 :, :]
    for index in range(ends_ref.shape[0]):
        ends_ref[index, 0:1, :] = kept
        ends_ref[index, 1:2, :] = state
    for cut in cuts:
        cut.wait()


def states_kernel(local_ref, through_ref, mixer_ref, ends_ref, states_ref, other_ref):
    me, lane = seat()
    carry = jnp.zeros((1, local_ref.shape[1]), jnp.float32)
    for shard in range(ends_ref.shape[0]):
        later = ends_ref[shard, 0:1, :] * carry + ends_ref[shard, 1:2, :]
        carry = jnp.where(shard < me, later, carry)
    states = (local_ref[...] + through_ref[...] * carry).astype(jnp.bfloat16)
    states_ref[...] = states
    half = other_ref.shape[1]
    other_ref[...] = jnp.dot(
        states, mixer_ref[:, lanes(1 - lane, half)], preferred_element_type=jnp.float32
    )


def pool_kernel(plane, *refs):
    states_ref, mixer_ref, other_ref, bytes_ref, pick_ref = refs[:5]
    layers = len(refs) - 8 - plane
    up_pieces, (encoded_ref, out_ref, *up_refs, sems) = refs[5 : 5 + layers], refs[5 + layers :]
    cross = lax.rem(seat()[0], plane)
    pairs = []
    for mask, up_ref in enumerate(up_refs):
        size = 2 * up_ref.shape[2] // layers
        for step, piece in enumerate(up_pieces):
            for number in range(layers // 2):
                columns = lanes(number * plane + (cross ^ mask), size)
                pairs.append((piece.at[:, columns], up_ref.at[step, :, pl.ds(number * size, size)]))
    copies = start_all(pairs, sems)
    half = other_ref.shape[1]
    columns = lanes(seat()[1], half)
    mixed = jnp.dot(states_ref[...], mixer_ref[:, columns], preferred_element_type=jnp.float32)
    skip = bytes_ref[:, columns].astype(jnp.float32)
    encoded = (skip + (mixed + other_ref[...])).astype(jnp.bfloat16)
    encoded_ref[...] = encoded
    picked = jnp.dot(pick_ref[...], encoded, preferred_element_type=jnp.float32)
    picked = picked.astype(jnp.bfloat16)
    size = out_ref.shape[1]
    for target in range(out_ref.shape[0]):
        start = target % plane * size
        out_ref[target] = picked[start : start + size, :]
    for copy in copies:
        copy.wait()


def own_kernel(pick_ref, arrived_ref, out_ref):
    shards, slots, half = arrived_ref.shape
    rows = arrived_ref[...].reshape(shards * slots, half)
    own = jnp.dot(pick_ref[...], rows, preferred_element_type=jnp.float32).astype(jnp.bfloat16)
    for index in range(out_ref.shape[0]):
        out_ref[index] = own


def inner_kernel(plane, layers, bias_ref, gain_ref, near_ref, far_ref, *refs):
    up_own, refs = refs[:plane], refs[plane:]
    up_far, refs = refs[:plane], refs[plane:]
    pieces, refs = refs[:layers], refs[layers:]
    out_ref, pooled, up, weights, squares, sems = refs
    me, lane = seat()
    layer, cross = me // plane, lax.rem(me, plane)
    half = near_ref.shape[1]
    up_rows, up_half = up_own[0].shape[1:]
    pairs = [
        (near_ref, pooled.at[:, lanes(lane, half)]),
        (far_ref, pooled.at[:, lanes(1 - lane, half)]),
    ]
    for step in range(layers):
        for mask in range(plane):
            where = rows_at((layer ^ step) * plane + (cross ^ mask), up_rows)
            pairs.append((up_own[mask].at[step], up.at[where, lanes(lane, up_half)]))
            pairs.append((up_far[mask].at[step], up.at[where, lanes(1 - lane, up_half)]))
    for step, piece in enumerate(pieces):
        pairs.append((piece, weights.at[rows_at(layer ^ step, piece.shape[0]), :]))
    copies = start_all(pairs, sems)
    for copy in copies[:-layers]:
        copy.wait()
    rows = pooled.shape[0]
    block = rows // plane
    ones = jnp.ones((8, up.shape[1]), jnp.bfloat16)
    for index in range(plane):
        where = pl.ds(index * block, block)
        widened = jnp.dot(pooled[where, :], up[...], preferred_element_type=jnp.float32)
        widened = (widened + bias_ref[...]).astype(jnp.bfloat16).astype(jnp.float32)
        inner = (widened * gain_ref[...]).astype(jnp.bfloat16)
        square = widened * widened
        coarse = square.astype(jnp.bfloat16)
        fine = (square - coarse.astype(jnp.float32)).astype(jnp.bfloat16)
        squares[:, where] = sum(
            lax.dot_general(
                ones, part, (((1,), (1,)), ((), ())), preferred_element_type=jnp.float32
            )
            for part in (coarse, fine)
        )
        if index == 0:
            for copy in copies[-layers:]:
                copy.wait()
        sums = jnp.dot(inner, weights[...], preferred_element_type=jnp.float32)
        sums = sums.astype(jnp.bfloat16)
        for head in range(plane):
            out_ref[head, where, :] = sums[:, head * HEAD : (head + 1) * HEAD]
        for number in range(2):
            start = (plane + number) * HEAD
            out_ref[index, pl.ds(rows + number * block, block), :] = sums[:, start : start + HEAD]
    total = jnp.concatenate(
        [squares[0:1, start : start + HEAD] for start in range(0, rows, HEAD)], axis=0
    )
    coarse = total.astype(jnp.bfloat16).astype(jnp.float32)
    both = jnp.concatenate([coarse, total - coarse], axis=0).astype(jnp.bfloat16)
    for index in range(plane):
        out_ref[index, pl.ds(rows + 2 * block, both.shape[0]), :] = both


def heads_kernel(features, got_ref, query_ref, pair_ref, queries):
    plane = got_ref.shape[0]
    rows = query_ref.shape[0]
    block = rows // plane
    lines = rows // HEAD
    shards = rows // CH_OWN
    layers = shards // plane
    first = rows + 2 * block

    def added(start, size):
        parts = [got_ref[index, start : start + size, :].astype(jnp.float32) for index in range(plane)]
        return sum(parts[1:], parts[0])

    both = added(first, 2 * lines)
    total = both[:lines, :] + both[lines:, :]
    scale = jnp.transpose(lax.rsqrt(total * (1.0 / features) + eps))
    for line in range(lines):
        scaled = added(line * HEAD, HEAD) * scale[:, line : line + 1]
        for start in range(0, HEAD, CH_OWN):
            index = (line * HEAD + start) // CH_OWN
            shard = (index % layers) * plane + index // layers
            queries[pl.ds(shard, CH_OWN, stride=shards), :] = scaled[start : start + CH_OWN, :]
    query_ref[...] = queries[...].astype(jnp.bfloat16)
    cross = lax.rem(seat()[0], plane)
    per_block = block // HEAD
    for line in range(per_block):
        mine = scale[:, line : line + 1]
        for index in range(1, plane):
            column = index * per_block + line
            mine = jnp.where(cross == index, scale[:, column : column + 1], mine)
        for number in range(2):
            start = number * block + line * HEAD
            pair = (added(rows + start, HEAD) * mine).astype(jnp.bfloat16)
            for index in range(plane):
                pair_ref[index, pl.ds(start, HEAD), :] = pair


def attend_kernel(place_ref, query_ref, pair_ref, out_ref, natural, keys, values, attended):
    rows = query_ref.shape[0]
    window = out_ref.shape[1]
    plane = pair_ref.shape[0]
    part = rows // plane
    shards = rows // CH_OWN
    layers = shards // plane
    for number, held in enumerate((keys, values)):
        for cross in range(plane):
            for layer in range(layers):
                piece = pair_ref[cross, pl.ds(number * part + layer * CH_OWN, CH_OWN), :]
                where = pl.ds(layer * plane + cross, CH_OWN, stride=shards)
                natural[where, :] = piece.astype(jnp.float32)
        held[...] = natural[...].astype(jnp.bfloat16)
    block = min(256, rows)
    score_scale = 1.0 / math.sqrt(HEAD)
    for start in range(0, rows, block):
        stop = start + block
        scores = lax.dot_general(
            query_ref[start:stop, :],
            keys[0:stop, :],
            (((1,), (1,)), ((), ())),
            preferred_element_type=jnp.float32,
        )
        spots = lax.broadcasted_iota(jnp.int32, scores.shape, 1)
        mine = lax.broadcasted_iota(jnp.int32, scores.shape, 0) + start
        scores = jnp.where(spots <= mine, scores * score_scale, masked)
        peak = jnp.max(scores, axis=1, keepdims=True)
        lifted = jnp.exp(scores - peak)
        denominator = jnp.sum(lifted, axis=1, keepdims=True)
        weighted = jnp.dot(
            lifted.astype(jnp.bfloat16), values[0:stop, :], preferred_element_type=jnp.float32
        )
        attended[start:stop, :] = (weighted / denominator).astype(jnp.bfloat16)
    attended[rows:, :] = jnp.zeros((attended.shape[0] - rows, HEAD), jnp.bfloat16)
    for shard in range(out_ref.shape[0]):
        first = place_ref[shard]
        out_ref[shard] = attended[pl.ds(pl.multiple_of(first * TILE, TILE), window), :]


def return_kernel(weight_ref, pieces_ref, own_ref, other_ref, attended):
    half = own_ref.shape[1]
    lane = seat()[1]
    for head in range(pieces_ref.shape[0]):
        attended[:, head * HEAD : (head + 1) * HEAD] = pieces_ref[head]
    other_ref[...] = jnp.dot(
        attended[...], weight_ref[:, lanes(1 - lane, half)], preferred_element_type=jnp.float32
    )
    own_ref[...] = jnp.dot(
        attended[...], weight_ref[:, lanes(lane, half)], preferred_element_type=jnp.float32
    )


def join_kernel(own_ref, other_ref, encoded_ref, spread_ref, out_ref):
    returned = (own_ref[...] + other_ref[...]).astype(jnp.bfloat16)
    results = jnp.dot(spread_ref[...], returned, preferred_element_type=jnp.float32)
    out_ref[...] = (encoded_ref[...].astype(jnp.float32) + results).astype(jnp.bfloat16)


def one_head_each(
    byte_states,
    outer_gain,
    mamba_input,
    mamba_step,
    decay_rate,
    mixer_weight,
    boundaries,
    span_counts,
    up_weight,
    up_bias,
    inner_gain,
    query_weight,
    key_weight,
    value_weight,
    return_weight,
):
    shards = lax.axis_size("seq")
    me = lax.axis_index("seq")
    lane = lax.axis_index("mp")
    plane = HEADS // KV_HEADS
    layers = shards // plane
    rows_here, width = byte_states.shape
    half = mamba_input.shape[1]
    capacity = boundaries.shape[1]
    window = capacity + TILE
    total_rows = CH_OWN * shards
    inner_width = inner_gain.shape[0]
    inner_half = up_bias.shape[0]
    weight_rows = query_weight.shape[0]
    f32, bf16 = jnp.float32, jnp.bfloat16
    layer, cross = me // plane, me % plane
    plane_groups = [[first * plane + step for step in range(plane)] for first in range(layers)]

    def over(value, mask):
        return lax.ppermute(value, "seq", [(i, i ^ mask) for i in range(shards)])

    def after(value, done):
        return lax.optimization_barrier((value, done))[0]

    own_bias = up_bias.reshape(layers // 2, plane, weight_rows)
    own_bias = lax.dynamic_index_in_dim(own_bias, cross, 1, keepdims=False).reshape(1, -1)
    own_gain = inner_gain.reshape(layers, plane, weight_rows)
    own_gain = lax.dynamic_index_in_dim(own_gain, cross, 1, keepdims=False).reshape(1, -1)

    seq_ids = jnp.arange(shards, dtype=jnp.int32)
    offsets = jnp.cumsum(span_counts) - span_counts
    own_offset = jnp.sum(jnp.where(seq_ids == me, offsets, 0))
    own_count = jnp.sum(jnp.where(seq_ids == me, span_counts, 0))
    place = offsets // TILE
    own_marks = boundaries[0]
    positions = jnp.arange(rows_here, dtype=jnp.int32)
    spans_here = jnp.arange(capacity, dtype=jnp.int32)
    live = spans_here < own_count
    slots = capacity // shards
    slot_ids = jnp.arange(slots, dtype=jnp.int32)
    owners = seq_ids.reshape(layers, plane).T
    local_span = slot_ids * shards + ((owners - own_offset) % shards)[:, :, None]
    is_span = spans_here[None, :] == local_span.reshape(-1)[:, None]
    byte_at = jnp.sum(jnp.where(is_span, jnp.minimum(own_marks, rows_here - 1)[None, :], 0), axis=1)
    pool_pick = (positions[None, :] == byte_at[:, None]).astype(bf16)
    near_owner = jnp.arange(layers, dtype=jnp.int32) * plane + cross
    near_spans = near_owner[:, None] + jnp.arange(CH_OWN, dtype=jnp.int32)[None, :] * shards
    origin = jnp.sum((offsets <= near_spans[:, :, None]).astype(jnp.int32), axis=2) - 1
    origin_offset = jnp.sum(jnp.where(seq_ids == origin[:, :, None], offsets, 0), axis=2)
    arrived_row = (
        origin * (layers * slots)
        + jnp.arange(layers, dtype=jnp.int32)[:, None] * slots
        + (near_spans - origin_offset) // shards
    ).reshape(-1)
    near_pick = (
        jnp.arange(shards * layers * slots, dtype=jnp.int32)[None, :] == arrived_row[:, None]
    ).astype(bf16)
    passed = jnp.sum(
        ((own_marks[None, :] <= positions[:, None]) & live[None, :]).astype(jnp.int32), axis=1
    )
    result_row = passed - 1 + own_offset % TILE
    spread = (jnp.arange(window, dtype=jnp.int32)[None, :] == result_row[:, None]).astype(bf16)

    up_half = inner_half // plane
    up_layers = [up_weight]
    for bit in range(layers.bit_length() - 2, -1, -1):
        up_layers += [over(piece, plane << bit) for piece in up_layers]
    order = [0]
    for bit in range(layers.bit_length() - 2, -1, -1):
        order += [step ^ (1 << bit) for step in order]
    up_layers = [up_layers[order.index(step)] for step in range(layers)]

    local, through, ends, *pair_cuts = pl.pallas_call(
        functools.partial(scan_kernel, plane, layers),
        out_shape=(
            jax.ShapeDtypeStruct((rows_here, half), f32),
            jax.ShapeDtypeStruct((rows_here, half), f32),
            jax.ShapeDtypeStruct((shards, 2, half), f32),
        )
        + (jax.ShapeDtypeStruct((weight_rows, (plane + 2) * HEAD), bf16),) * layers,
        in_specs=[in_hbm(), vmem(), in_hbm(), in_hbm(), vmem()] + [in_hbm()] * 3,
        out_specs=(vmem(),) * 3 + (in_place(),) * layers,
        scratch_shapes=[
            pltpu.VMEM(array.shape, bf16)
            for array in (
                byte_states,
                mamba_input,
                mamba_step,
                query_weight,
                key_weight,
                value_weight,
            )
        ]
        + [pltpu.SemaphoreType.DMA((6,)), pltpu.SemaphoreType.DMA((3 * layers,))],
        cost_estimate=brief(),
        compiler_params=params(56),
    )(
        byte_states,
        outer_gain[None, :],
        mamba_input,
        mamba_step,
        decay_rate[None, :],
        query_weight,
        key_weight,
        value_weight,
    )
    ends = lax.all_to_all(ends, "seq", 0, 0, tiled=True)
    ends, up_layers[1], up_layers[2] = lax.optimization_barrier(
        (ends, up_layers[1], up_layers[2])
    )
    pieces = [pair_cuts[0]] + [over(pair_cuts[step], plane * step) for step in range(1, layers)]
    states, other_part = pl.pallas_call(
        states_kernel,
        out_shape=(
            jax.ShapeDtypeStruct((rows_here, half), bf16),
            jax.ShapeDtypeStruct((rows_here, half), f32),
        ),
        in_specs=[vmem()] * 4,
        out_specs=(vmem(),) * 2,
        cost_estimate=brief(),
        compiler_params=params(56),
    )(local, through, mixer_weight, ends)
    far_bias = swapped(own_bias)
    bias = jnp.where(
        lane == 0,
        jnp.concatenate([own_bias, far_bias], axis=1),
        jnp.concatenate([far_bias, own_bias], axis=1),
    )
    far_part, bias, pieces = lax.optimization_barrier((swapped(other_part), bias, pieces))
    encoded, leaving, *up_cuts = pl.pallas_call(
        functools.partial(pool_kernel, plane),
        out_shape=(
            jax.ShapeDtypeStruct((rows_here, half), bf16),
            jax.ShapeDtypeStruct((shards, layers * slots, half), bf16),
        )
        + (jax.ShapeDtypeStruct((layers, up_weight.shape[0], up_half), bf16),) * plane,
        in_specs=[vmem()] * 5 + [in_place()] * layers,
        out_specs=(vmem(),) * (2 + plane),
        scratch_shapes=[pltpu.SemaphoreType.DMA((plane * layers * layers // 2,))],
        cost_estimate=brief(),
        compiler_params=params(56),
    )(states, mixer_weight, far_part, byte_states, pool_pick, *up_layers)
    arrived = lax.all_to_all(leaving, "seq", 0, 0, tiled=True)
    up_own = [up_cuts[0]] + [over(up_cuts[mask], mask) for mask in range(1, plane)]
    near_rows = pl.pallas_call(
        own_kernel,
        out_shape=jax.ShapeDtypeStruct((plane, layers * CH_OWN, half), bf16),
        in_specs=[vmem()] * 2,
        out_specs=vmem(),
        cost_estimate=brief(),
        compiler_params=params(56),
    )(near_pick, arrived)
    up_far = [swapped(piece) for piece in up_own]
    near = lax.all_to_all(
        near_rows, "seq", 0, 0, axis_index_groups=plane_groups, tiled=True
    ).reshape(total_rows, half)

    features = own_gain.shape[1]
    block = total_rows // plane
    sent_rows = total_rows + 2 * block + 2 * (total_rows // HEAD)
    partial_sums = pl.pallas_call(
        functools.partial(inner_kernel, plane, layers),
        out_shape=jax.ShapeDtypeStruct((plane, sent_rows, HEAD), bf16),
        in_specs=[vmem()] * 2 + [in_place()] * (2 + 2 * plane + layers),
        out_specs=vmem(),
        scratch_shapes=[
            pltpu.VMEM((total_rows, width), bf16),
            pltpu.VMEM((width, features), bf16),
            pltpu.VMEM((features, (plane + 2) * HEAD), bf16),
            pltpu.VMEM((8, total_rows), f32),
            pltpu.SemaphoreType.DMA((2 + 2 * shards + layers,)),
        ],
        cost_estimate=brief(),
        compiler_params=params(56),
    )(bias, own_gain, near, swapped(near), *up_own, *up_far, *pieces)
    got = lax.all_to_all(
        partial_sums, "seq", 0, 0, axis_index_groups=plane_groups, tiled=True
    )
    queries, pairs = pl.pallas_call(
        functools.partial(heads_kernel, inner_width),
        out_shape=(
            jax.ShapeDtypeStruct((total_rows, HEAD), bf16),
            jax.ShapeDtypeStruct((plane, 2 * block, HEAD), bf16),
        ),
        in_specs=[vmem()],
        out_specs=(vmem(),) * 2,
        scratch_shapes=[pltpu.VMEM((total_rows, HEAD), f32)],
        cost_estimate=brief(),
        compiler_params=params(10),
    )(got)
    pairs = lax.all_to_all(pairs, "seq", 0, 0, axis_index_groups=plane_groups, tiled=True)
    leaving = pl.pallas_call(
        attend_kernel,
        out_shape=jax.ShapeDtypeStruct((shards, window, HEAD), bf16),
        in_specs=[smem()] + [vmem()] * 2,
        out_specs=vmem(),
        scratch_shapes=[
            pltpu.VMEM((total_rows, HEAD), f32),
            pltpu.VMEM((total_rows, HEAD), bf16),
            pltpu.VMEM((total_rows, HEAD), bf16),
            pltpu.VMEM((total_rows + window, HEAD), bf16),
        ],
        cost_estimate=brief(),
        compiler_params=params(12),
    )(place, queries, pairs)
    pieces = lax.all_to_all(leaving, "seq", 0, 0, tiled=True)
    own_back, other_back = pl.pallas_call(
        return_kernel,
        out_shape=(jax.ShapeDtypeStruct((window, half), f32),) * 2,
        in_specs=[vmem()] * 2,
        out_specs=(vmem(),) * 2,
        scratch_shapes=[pltpu.VMEM((window, shards * HEAD), bf16)],
        cost_estimate=brief(),
        compiler_params=params(12),
    )(return_weight, pieces)
    return pl.pallas_call(
        join_kernel,
        out_shape=jax.ShapeDtypeStruct((rows_here, half), bf16),
        in_specs=[vmem()] * 4,
        out_specs=vmem(),
        cost_estimate=brief(),
        compiler_params=params(8),
    )(own_back, swapped(other_back), encoded, spread)


def prefix(value, axis, join, neutral):
    count, mine = (lax.axis_size(axis), lax.axis_index(axis))
    pieces = jax.tree.map(lambda part: lax.all_gather(part, axis), value)
    so_far = jax.tree.map(
        lambda part, zero: jnp.full_like(part, 0) + jnp.asarray(zero, part.dtype), value, neutral
    )

    def lap(position, so_far):
        longer = join(so_far, jax.tree.map(lambda part: part[position], pieces))
        return jax.tree.map(lambda new, old: jnp.where(position < mine, new, old), longer, so_far)

    return lax.fori_loop(0, count - 1, lap, so_far)


def rms_scale(values, gain):
    values = values.astype(jnp.float32)
    return values * lax.rsqrt(jnp.mean(values * values, axis=-1, keepdims=True) + eps) * gain


def combine_pairs(earlier, later):
    return (earlier[0] * later[0], later[0] * earlier[1] + later[1])


def pick_table(table, wanted, seq_ids):
    return jnp.sum(jnp.where(seq_ids[None, :] == wanted[:, None], table[None, :], 0), axis=1)


def block_size(piece_rows, shard_rows):
    limit = max(1, 1024 // shard_rows)
    pieces = max(1, piece_rows // shard_rows)
    best_size = 1
    for candidate in range(1, limit + 1):
        if pieces % candidate == 0:
            best_size = candidate
    return min(piece_rows, best_size * shard_rows)


def spread_heads(
    byte_states,
    outer_gain,
    mamba_input,
    mamba_step,
    decay_rate,
    mixer_weight,
    boundaries,
    span_counts,
    up_weight,
    up_bias,
    inner_gain,
    query_weight,
    key_weight,
    value_weight,
    return_weight,
):
    shards = lax.axis_size("seq")
    own_shard = lax.axis_index("seq")
    own_lane = lax.axis_index("mp")
    rows_here = byte_states.shape[0]
    capacity = boundaries.shape[1]
    column_count = mamba_input.shape[1]
    kv_local = key_weight.shape[1] // HEAD
    group_size = HEADS // KV_HEADS
    slot_count = capacity // shards
    offsets = jnp.cumsum(span_counts) - span_counts
    seq_ids = jnp.arange(shards, dtype=jnp.int32)
    own_offset = jnp.sum(jnp.where(seq_ids == own_shard, offsets, 0))
    own_count = jnp.sum(jnp.where(seq_ids == own_shard, span_counts, 0))
    normed = rms_scale(byte_states, outer_gain).astype(jnp.bfloat16)
    inputs = jnp.dot(normed, mamba_input, preferred_element_type=jnp.float32)
    step_sizes = jax.nn.softplus(jnp.dot(normed, mamba_step, preferred_element_type=jnp.float32))
    rate_steps = step_sizes * decay_rate
    decays = jnp.exp(-rate_steps)
    drives = jnp.sqrt(-jnp.expm1(-2.0 * rate_steps)) * inputs
    through, local_states = lax.associative_scan(combine_pairs, (decays, drives), axis=0)
    starting = (jnp.ones((column_count,), jnp.float32), jnp.zeros((column_count,), jnp.float32))
    arriving = prefix((through[-1], local_states[-1]), "seq", combine_pairs, starting)
    states = (local_states + through * arriving[1][None, :]).astype(jnp.bfloat16)
    partial_value = jnp.dot(states, mixer_weight, preferred_element_type=jnp.float32)
    mixed_sum = lax.psum(partial_value, "mp")
    encoded = (byte_states.astype(jnp.float32) + mixed_sum).astype(jnp.bfloat16)
    skip_part = lax.dynamic_slice_in_dim(encoded, own_lane * column_count, column_count, 1)
    own_marks = boundaries[0]
    pooled = encoded[jnp.minimum(own_marks, rows_here - 1)]
    row_width = pooled.shape[1]
    outgoing = jnp.roll(pooled.reshape(slot_count, shards, row_width), own_offset % shards, axis=1)
    incoming = lax.all_to_all(outgoing, "seq", split_axis=1, concat_axis=1, tiled=True)
    position = jnp.arange(CH_OWN, dtype=jnp.int32)
    span_index = own_shard + position * shards
    source = jnp.sum((offsets[None, :] <= span_index[:, None]).astype(jnp.int32), axis=1) - 1
    source_offset = pick_table(offsets, source, seq_ids)
    slot_index = (span_index - source_offset) // shards
    gathered_rows = incoming.reshape(slot_count * shards, row_width)[slot_index * shards + source]
    columns = gathered_rows
    widened_sum = jnp.dot(
        columns,
        lax.all_gather(up_weight, "seq", axis=0, tiled=True),
        preferred_element_type=jnp.float32,
    )
    widened_share = (widened_sum + up_bias[None, :]).astype(jnp.bfloat16)
    widened = lax.all_gather(widened_share, "mp", axis=1, tiled=True)
    inner_normed = rms_scale(widened, inner_gain).astype(jnp.bfloat16)
    columns = inner_normed
    query_part = jnp.dot(
        columns,
        lax.all_gather(query_weight, "seq", axis=0, tiled=True),
        preferred_element_type=jnp.float32,
    )
    key_part = jnp.dot(
        columns,
        lax.all_gather(key_weight, "seq", axis=0, tiled=True),
        preferred_element_type=jnp.float32,
    )
    value_part = jnp.dot(
        columns,
        lax.all_gather(value_weight, "seq", axis=0, tiled=True),
        preferred_element_type=jnp.float32,
    )
    queries = query_part.astype(jnp.bfloat16)
    key_rows = key_part.astype(jnp.bfloat16)
    value_rows = value_part.astype(jnp.bfloat16)
    query_count = queries.shape[0]
    grouped = (
        queries.reshape(query_count, kv_local, group_size, HEAD)
        .transpose(1, 0, 2, 3)
        .reshape(kv_local, query_count * group_size, HEAD)
    )
    row_index = jnp.repeat(span_index, group_size)
    shard_rows = key_rows.shape[0]
    score_scale = 1.0 / math.sqrt(HEAD)

    def key_index(whole_index):
        return whole_index // shard_rows + whole_index % shard_rows * shards

    def attend_block(running, key_block, value_block, index_block):
        row_peak, denominator, weighted = running
        scores = (
            jnp.einsum("hqd,khd->hqk", grouped, key_block, preferred_element_type=jnp.float32)
            * score_scale
        )
        scores = jnp.where(index_block[None, None, :] <= row_index[None, :, None], scores, masked)
        new_peak = jnp.maximum(row_peak, jnp.max(scores, axis=2))
        shrink = jnp.exp(row_peak - new_peak)
        lifted = jnp.exp(scores - new_peak[:, :, None])
        denominator = denominator * shrink + jnp.sum(lifted, axis=2)
        weighted = weighted * shrink[:, :, None] + jnp.einsum(
            "hqk,khd->hqd",
            lifted.astype(jnp.bfloat16),
            value_block,
            preferred_element_type=jnp.float32,
        )
        return (new_peak, denominator, weighted)

    query_total = query_count * group_size
    initial = (
        jnp.full((kv_local, query_total), masked, jnp.float32),
        jnp.zeros((kv_local, query_total), jnp.float32),
        jnp.zeros((kv_local, query_total, HEAD), jnp.float32),
    )
    key_piece = lax.all_gather(key_rows, "seq", axis=0, tiled=True)
    value_piece = lax.all_gather(value_rows, "seq", axis=0, tiled=True)
    piece_rows = key_piece.shape[0]
    block_rows = block_size(piece_rows, shard_rows)
    turn_count = piece_rows // block_rows
    key_blocks = key_piece.reshape(turn_count, block_rows, kv_local, HEAD)
    value_blocks = value_piece.reshape(turn_count, block_rows, kv_local, HEAD)

    def one_turn(turn_index, inner_running):
        whole_index = turn_index * block_rows + jnp.arange(block_rows, dtype=jnp.int32)
        return attend_block(
            inner_running, key_blocks[turn_index], value_blocks[turn_index], key_index(whole_index)
        )

    row_peak, denominator, weighted = lax.fori_loop(0, turn_count, one_turn, initial)
    attended = (weighted / denominator[:, :, None]).astype(jnp.bfloat16)
    attended = (
        attended.reshape(kv_local, query_count, group_size, HEAD)
        .transpose(1, 0, 2, 3)
        .reshape(query_count, kv_local * group_size * HEAD)
    )
    projected = jnp.dot(attended, return_weight, preferred_element_type=jnp.float32)
    returned = lax.psum_scatter(
        projected.astype(jnp.bfloat16), "mp", scatter_dimension=1, tiled=True
    )
    slot_ids = jnp.arange(slot_count, dtype=jnp.int32)
    lead_slot = (own_shard - offsets) % shards
    local_span = slot_ids[:, None] * shards + lead_slot[None, :]
    back_index = (offsets[None, :] + local_span - own_shard) // shards
    alive = local_span < span_counts[None, :]
    back_rows = jnp.where(
        alive[:, :, None],
        returned[jnp.clip(back_index, 0, CH_OWN - 1)],
        jnp.zeros((), jnp.bfloat16),
    )
    arrived = lax.all_to_all(back_rows, "seq", split_axis=1, concat_axis=1, tiled=True)
    span_results = jnp.roll(arrived, -(own_offset % shards), axis=1).reshape(capacity, column_count)
    positions = jnp.arange(rows_here, dtype=jnp.int32)
    live_slots = jnp.arange(capacity, dtype=jnp.int32) < own_count
    passed = jnp.sum(
        ((own_marks[None, :] <= positions[:, None]) & live_slots[None, :]).astype(jnp.int32), axis=1
    )
    return (skip_part.astype(jnp.float32) + span_results[passed - 1].astype(jnp.float32)).astype(
        jnp.bfloat16
    )


def solution(mesh):
    in_specs = (
        P("seq", None),
        P(),
        P(None, "mp"),
        P(None, "mp"),
        P("mp"),
        P("mp", None),
        P("seq", None),
        P(),
        P("seq", "mp"),
        P("mp"),
        P(),
        P("seq", "mp"),
        P("seq", "mp"),
        P("seq", "mp"),
        P("mp", None),
    )
    out_specs = P("seq", "mp")
    def on_device(*arrays):
        heads_here = arrays[11].shape[1] // HEAD
        fits = heads_here == mesh.shape["seq"] and mesh.shape["mp"] == 2
        return (one_head_each if fits else spread_heads)(*arrays)

    return jax.shard_map(
        on_device, mesh=mesh, in_specs=in_specs, out_specs=out_specs, check_vma=False
    )
```

```python
import functools
import math

import jax
import jax.numpy as jnp
from jax import lax
from jax.experimental import pallas as pl
from jax.experimental.pallas import tpu as pltpu
from jax.sharding import PartitionSpec as P

HEADS = 32
KV_HEADS = 8
HEAD = 128
CH_OWN = 64


eps = 1e-05
masked = -1e30
TILE = 16


def swapped(value):
    return lax.ppermute(value, "mp", [(0, 1), (1, 0)])


def vmem():
    return pl.BlockSpec(memory_space=pltpu.VMEM)


def smem():
    return pl.BlockSpec(memory_space=pltpu.SMEM)


def in_place():
    return pl.BlockSpec(memory_space=pl.ANY)


def in_hbm():
    return pl.BlockSpec(memory_space=pltpu.HBM)


def seat():
    return lax.axis_index("seq"), lax.axis_index("mp")


def params(mebibytes=24):
    return pltpu.CompilerParams(vmem_limit_bytes=mebibytes * 2**20)


def brief():
    return pl.CostEstimate(flops=1, bytes_accessed=1, transcendentals=0)


def lanes(which, size):
    return pl.ds(pl.multiple_of(which * size, size), size)


def rows_at(which, size):
    return pl.ds(pl.multiple_of(which * size, size), size)


def start_all(pairs, sems):
    copies = []
    for index, (from_ref, to_ref) in enumerate(pairs):
        copy = pltpu.make_async_copy(from_ref, to_ref, sems.at[index])
        copy.start()
        copies.append(copy)
    return copies


def copy_all(pairs, sems):
    for copy in start_all(pairs, sems):
        copy.wait()


def one_minus_exp(u):
    series = jnp.ones_like(u)
    for order in range(9, 1, -1):
        series = 1.0 - u * (1.0 / order) * series
    return jnp.where(u < 0.5, u * series, 1.0 - jnp.exp(-u))


def softplus(v):
    tail = jnp.exp(-jnp.abs(v))
    series = jnp.ones_like(tail)
    for order in range(6, 1, -1):
        series = 1.0 - tail * ((order - 1.0) / order) * series
    return jnp.maximum(v, 0.0) + jnp.where(tail < 0.03, tail * series, jnp.log(1.0 + tail))


def start_cuts(plane, query_ref, key_ref, value_ref, pair_outs, sems):
    layers = len(pair_outs)
    me, _ = seat()
    layer = me // plane
    group = plane * HEAD
    pairs = []
    for step, out_ref in enumerate(pair_outs):
        target = layer ^ step
        pairs.append((query_ref.at[:, lanes(target, group)], out_ref.at[:, pl.ds(0, group)]))
        pairs.append((key_ref.at[:, lanes(target, HEAD)], out_ref.at[:, pl.ds(group, HEAD)]))
        pairs.append(
            (value_ref.at[:, lanes(target, HEAD)], out_ref.at[:, pl.ds(group + HEAD, HEAD)])
        )
    return start_all(pairs, sems)


def scan_kernel(plane, layers, *refs):
    bytes_hbm, gain_ref, input_hbm, step_hbm, rate_ref = refs[:5]
    others, refs = refs[5:8], refs[8:]
    local_ref, through_ref, ends_ref = refs[:3]
    pair_outs, refs = refs[3 : 3 + layers], refs[3 + layers :]
    bytes_ref, input_ref, step_ref, *held, sems, cut_sems = refs
    fetches = start_all(
        [(bytes_hbm, bytes_ref), (step_hbm, step_ref), (input_hbm, input_ref), *zip(others, held)],
        sems,
    )
    fetches[0].wait()
    values = bytes_ref[...].astype(jnp.float32)
    scale = lax.rsqrt(jnp.mean(values * values, axis=1, keepdims=True) + eps)
    normed = (values * scale * gain_ref[...]).astype(jnp.bfloat16)
    fetches[1].wait()
    steps = softplus(jnp.dot(normed, step_ref[...], preferred_element_type=jnp.float32))
    rate_steps = steps * rate_ref[...]
    fetches[2].wait()
    inputs = jnp.dot(normed, input_ref[...], preferred_element_type=jnp.float32)
    for fetch in fetches[3:]:
        fetch.wait()
    cuts = start_cuts(plane, *held, pair_outs, cut_sems)
    decays = jnp.exp(-rate_steps)
    drives = jnp.sqrt(one_minus_exp(2.0 * rate_steps)) * inputs
    rows, width = decays.shape
    tile = 8
    decays = decays.reshape(rows // tile, tile, width)
    drives = drives.reshape(rows // tile, tile, width)
    place = lax.broadcasted_iota(jnp.int32, decays.shape, 1)
    for reach in (1, 2, 4):
        before_decays = pltpu.roll(decays, reach, 1)
        before_drives = pltpu.roll(drives, reach, 1)
        inside = place >= reach
        drives = jnp.where(inside, decays * before_drives + drives, drives)
        decays = jnp.where(inside, decays * before_decays, decays)
    state = jnp.zeros((1, width), jnp.float32)
    kept = jnp.ones((1, width), jnp.float32)
    for index in range(rows // tile):
        states = decays[index] * state + drives[index]
        passing = decays[index] * kept
        local_ref[pl.ds(index * tile, tile), :] = states
        through_ref[pl.ds(index * tile, tile), :] = passing
        state = states[tile - 1 :, :]
        kept = passing[tile - 1 :, :]
    for index in range(ends_ref.shape[0]):
        ends_ref[index, 0:1, :] = kept
        ends_ref[index, 1:2, :] = state
    for cut in cuts:
        cut.wait()


def states_kernel(local_ref, through_ref, mixer_ref, ends_ref, states_ref, other_ref):
    me, lane = seat()
    carry = jnp.zeros((1, local_ref.shape[1]), jnp.float32)
    for shard in range(ends_ref.shape[0]):
        later = ends_ref[shard, 0:1, :] * carry + ends_ref[shard, 1:2, :]
        carry = jnp.where(shard < me, later, carry)
    states = (local_ref[...] + through_ref[...] * carry).astype(jnp.bfloat16)
    states_ref[...] = states
    half = other_ref.shape[1]
    other_ref[...] = jnp.dot(
        states, mixer_ref[:, lanes(1 - lane, half)], preferred_element_type=jnp.float32
    )


def pool_kernel(
    plane, states_ref, mixer_ref, other_ref, bytes_ref, pick_ref, encoded_ref, out_ref
):
    half = other_ref.shape[1]
    columns = lanes(seat()[1], half)
    mixed = jnp.dot(states_ref[...], mixer_ref[:, columns], preferred_element_type=jnp.float32)
    skip = bytes_ref[:, columns].astype(jnp.float32)
    encoded = (skip + (mixed + other_ref[...])).astype(jnp.bfloat16)
    encoded_ref[...] = encoded
    picked = jnp.dot(pick_ref[...], encoded, preferred_element_type=jnp.float32)
    picked = picked.astype(jnp.bfloat16)
    size = out_ref.shape[1]
    for target in range(out_ref.shape[0]):
        start = target % plane * size
        out_ref[target] = picked[start : start + size, :]


def cut_kernel(plane, gate_ref, *refs):
    layers = len(refs) - plane - 3
    pieces, (*outs, held, sems, cut_sems) = refs[:layers], refs[layers:]
    copy_all([(piece, held.at[step]) for step, piece in enumerate(pieces)], sems)
    cross = lax.rem(seat()[0], plane)
    pairs = []
    for mask, out_ref in enumerate(outs):
        size = 2 * out_ref.shape[2] // layers
        for number in range(layers // 2):
            columns = lanes(number * plane + (cross ^ mask), size)
            pairs.append((held.at[:, :, columns], out_ref.at[:, :, pl.ds(number * size, size)]))
    copy_all(pairs, cut_sems)


def own_kernel(pick_ref, arrived_ref, out_ref):
    shards, slots, half = arrived_ref.shape
    rows = arrived_ref[...].reshape(shards * slots, half)
    own = jnp.dot(pick_ref[...], rows, preferred_element_type=jnp.float32).astype(jnp.bfloat16)
    for index in range(out_ref.shape[0]):
        out_ref[index] = own


def inner_kernel(plane, layers, bias_ref, gain_ref, near_ref, far_ref, *refs):
    up_own, refs = refs[:plane], refs[plane:]
    up_far, refs = refs[:plane], refs[plane:]
    pieces, refs = refs[:layers], refs[layers:]
    out_ref, pooled, up, weights, squares, sems = refs
    me, lane = seat()
    layer, cross = me // plane, lax.rem(me, plane)
    half = near_ref.shape[1]
    up_rows, up_half = up_own[0].shape[1:]
    pairs = [
        (near_ref, pooled.at[:, lanes(lane, half)]),
        (far_ref, pooled.at[:, lanes(1 - lane, half)]),
    ]
    for step in range(layers):
        for mask in range(plane):
            where = rows_at((layer ^ step) * plane + (cross ^ mask), up_rows)
            pairs.append((up_own[mask].at[step], up.at[where, lanes(lane, up_half)]))
            pairs.append((up_far[mask].at[step], up.at[where, lanes(1 - lane, up_half)]))
    for step, piece in enumerate(pieces):
        pairs.append((piece, weights.at[rows_at(layer ^ step, piece.shape[0]), :]))
    copies = start_all(pairs, sems)
    for copy in copies[:-layers]:
        copy.wait()
    rows = pooled.shape[0]
    block = rows // plane
    ones = jnp.ones((8, up.shape[1]), jnp.bfloat16)
    for index in range(plane):
        where = pl.ds(index * block, block)
        widened = jnp.dot(pooled[where, :], up[...], preferred_element_type=jnp.float32)
        widened = (widened + bias_ref[...]).astype(jnp.bfloat16).astype(jnp.float32)
        inner = (widened * gain_ref[...]).astype(jnp.bfloat16)
        square = widened * widened
        coarse = square.astype(jnp.bfloat16)
        fine = (square - coarse.astype(jnp.float32)).astype(jnp.bfloat16)
        squares[:, where] = sum(
            lax.dot_general(
                ones, part, (((1,), (1,)), ((), ())), preferred_element_type=jnp.float32
            )
            for part in (coarse, fine)
        )
        if index == 0:
            for copy in copies[-layers:]:
                copy.wait()
        sums = jnp.dot(inner, weights[...], preferred_element_type=jnp.float32)
        sums = sums.astype(jnp.bfloat16)
        for head in range(plane):
            out_ref[head, where, :] = sums[:, head * HEAD : (head + 1) * HEAD]
        for number in range(2):
            start = (plane + number) * HEAD
            out_ref[index, pl.ds(rows + number * block, block), :] = sums[:, start : start + HEAD]
    total = jnp.concatenate(
        [squares[0:1, start : start + HEAD] for start in range(0, rows, HEAD)], axis=0
    )
    coarse = total.astype(jnp.bfloat16).astype(jnp.float32)
    both = jnp.concatenate([coarse, total - coarse], axis=0).astype(jnp.bfloat16)
    for index in range(plane):
        out_ref[index, pl.ds(rows + 2 * block, both.shape[0]), :] = both


def heads_kernel(features, got_ref, query_ref, pair_ref, queries):
    plane = got_ref.shape[0]
    rows = query_ref.shape[0]
    block = rows // plane
    lines = rows // HEAD
    shards = rows // CH_OWN
    layers = shards // plane
    first = rows + 2 * block

    def added(start, size):
        parts = [got_ref[index, start : start + size, :].astype(jnp.float32) for index in range(plane)]
        return sum(parts[1:], parts[0])

    both = added(first, 2 * lines)
    total = both[:lines, :] + both[lines:, :]
    scale = jnp.transpose(lax.rsqrt(total * (1.0 / features) + eps))
    for line in range(lines):
        scaled = added(line * HEAD, HEAD) * scale[:, line : line + 1]
        for start in range(0, HEAD, CH_OWN):
            index = (line * HEAD + start) // CH_OWN
            shard = (index % layers) * plane + index // layers
            queries[pl.ds(shard, CH_OWN, stride=shards), :] = scaled[start : start + CH_OWN, :]
    query_ref[...] = queries[...].astype(jnp.bfloat16)
    cross = lax.rem(seat()[0], plane)
    per_block = block // HEAD
    for line in range(per_block):
        mine = scale[:, line : line + 1]
        for index in range(1, plane):
            column = index * per_block + line
            mine = jnp.where(cross == index, scale[:, column : column + 1], mine)
        for number in range(2):
            start = number * block + line * HEAD
            pair = (added(rows + start, HEAD) * mine).astype(jnp.bfloat16)
            for index in range(plane):
                pair_ref[index, pl.ds(start, HEAD), :] = pair


def attend_kernel(place_ref, query_ref, pair_ref, out_ref, natural, keys, values, attended):
    rows = query_ref.shape[0]
    window = out_ref.shape[1]
    plane = pair_ref.shape[0]
    part = rows // plane
    shards = rows // CH_OWN
    layers = shards // plane
    for number, held in enumerate((keys, values)):
        for cross in range(plane):
            for layer in range(layers):
                piece = pair_ref[cross, pl.ds(number * part + layer * CH_OWN, CH_OWN), :]
                where = pl.ds(layer * plane + cross, CH_OWN, stride=shards)
                natural[where, :] = piece.astype(jnp.float32)
        held[...] = natural[...].astype(jnp.bfloat16)
    block = min(256, rows)
    score_scale = 1.0 / math.sqrt(HEAD)
    for start in range(0, rows, block):
        stop = start + block
        scores = lax.dot_general(
            query_ref[start:stop, :],
            keys[0:stop, :],
            (((1,), (1,)), ((), ())),
            preferred_element_type=jnp.float32,
        )
        spots = lax.broadcasted_iota(jnp.int32, scores.shape, 1)
        mine = lax.broadcasted_iota(jnp.int32, scores.shape, 0) + start
        scores = jnp.where(spots <= mine, scores * score_scale, masked)
        peak = jnp.max(scores, axis=1, keepdims=True)
        lifted = jnp.exp(scores - peak)
        denominator = jnp.sum(lifted, axis=1, keepdims=True)
        weighted = jnp.dot(
            lifted.astype(jnp.bfloat16), values[0:stop, :], preferred_element_type=jnp.float32
        )
        attended[start:stop, :] = (weighted / denominator).astype(jnp.bfloat16)
    attended[rows:, :] = jnp.zeros((attended.shape[0] - rows, HEAD), jnp.bfloat16)
    for shard in range(out_ref.shape[0]):
        first = place_ref[shard]
        out_ref[shard] = attended[pl.ds(pl.multiple_of(first * TILE, TILE), window), :]


def return_kernel(weight_ref, pieces_ref, own_ref, other_ref, attended):
    half = own_ref.shape[1]
    lane = seat()[1]
    for head in range(pieces_ref.shape[0]):
        attended[:, head * HEAD : (head + 1) * HEAD] = pieces_ref[head]
    other_ref[...] = jnp.dot(
        attended[...], weight_ref[:, lanes(1 - lane, half)], preferred_element_type=jnp.float32
    )
    own_ref[...] = jnp.dot(
        attended[...], weight_ref[:, lanes(lane, half)], preferred_element_type=jnp.float32
    )


def join_kernel(own_ref, other_ref, encoded_ref, spread_ref, out_ref):
    returned = (own_ref[...] + other_ref[...]).astype(jnp.bfloat16)
    results = jnp.dot(spread_ref[...], returned, preferred_element_type=jnp.float32)
    out_ref[...] = (encoded_ref[...].astype(jnp.float32) + results).astype(jnp.bfloat16)


def one_head_each(
    byte_states,
    outer_gain,
    mamba_input,
    mamba_step,
    decay_rate,
    mixer_weight,
    boundaries,
    span_counts,
    up_weight,
    up_bias,
    inner_gain,
    query_weight,
    key_weight,
    value_weight,
    return_weight,
):
    shards = lax.axis_size("seq")
    me = lax.axis_index("seq")
    lane = lax.axis_index("mp")
    plane = HEADS // KV_HEADS
    layers = shards // plane
    rows_here, width = byte_states.shape
    half = mamba_input.shape[1]
    capacity = boundaries.shape[1]
    window = capacity + TILE
    total_rows = CH_OWN * shards
    inner_width = inner_gain.shape[0]
    inner_half = up_bias.shape[0]
    weight_rows = query_weight.shape[0]
    f32, bf16 = jnp.float32, jnp.bfloat16
    layer, cross = me // plane, me % plane
    plane_groups = [[first * plane + step for step in range(plane)] for first in range(layers)]

    def over(value, mask):
        return lax.ppermute(value, "seq", [(i, i ^ mask) for i in range(shards)])

    def after(value, done):
        return lax.optimization_barrier((value, done))[0]

    own_bias = up_bias.reshape(layers // 2, plane, weight_rows)
    own_bias = lax.dynamic_index_in_dim(own_bias, cross, 1, keepdims=False).reshape(1, -1)
    own_gain = inner_gain.reshape(layers, plane, weight_rows)
    own_gain = lax.dynamic_index_in_dim(own_gain, cross, 1, keepdims=False).reshape(1, -1)

    seq_ids = jnp.arange(shards, dtype=jnp.int32)
    offsets = jnp.cumsum(span_counts) - span_counts
    own_offset = jnp.sum(jnp.where(seq_ids == me, offsets, 0))
    own_count = jnp.sum(jnp.where(seq_ids == me, span_counts, 0))
    place = offsets // TILE
    own_marks = boundaries[0]
    positions = jnp.arange(rows_here, dtype=jnp.int32)
    spans_here = jnp.arange(capacity, dtype=jnp.int32)
    live = spans_here < own_count
    slots = capacity // shards
    slot_ids = jnp.arange(slots, dtype=jnp.int32)
    owners = seq_ids.reshape(layers, plane).T
    local_span = slot_ids * shards + ((owners - own_offset) % shards)[:, :, None]
    is_span = spans_here[None, :] == local_span.reshape(-1)[:, None]
    byte_at = jnp.sum(jnp.where(is_span, jnp.minimum(own_marks, rows_here - 1)[None, :], 0), axis=1)
    pool_pick = (positions[None, :] == byte_at[:, None]).astype(bf16)
    near_owner = jnp.arange(layers, dtype=jnp.int32) * plane + cross
    near_spans = near_owner[:, None] + jnp.arange(CH_OWN, dtype=jnp.int32)[None, :] * shards
    origin = jnp.sum((offsets <= near_spans[:, :, None]).astype(jnp.int32), axis=2) - 1
    origin_offset = jnp.sum(jnp.where(seq_ids == origin[:, :, None], offsets, 0), axis=2)
    arrived_row = (
        origin * (layers * slots)
        + jnp.arange(layers, dtype=jnp.int32)[:, None] * slots
        + (near_spans - origin_offset) // shards
    ).reshape(-1)
    near_pick = (
        jnp.arange(shards * layers * slots, dtype=jnp.int32)[None, :] == arrived_row[:, None]
    ).astype(bf16)
    passed = jnp.sum(
        ((own_marks[None, :] <= positions[:, None]) & live[None, :]).astype(jnp.int32), axis=1
    )
    result_row = passed - 1 + own_offset % TILE
    spread = (jnp.arange(window, dtype=jnp.int32)[None, :] == result_row[:, None]).astype(bf16)

    up_half = inner_half // plane
    up_layers = [up_weight]
    for bit in range(layers.bit_length() - 2, -1, -1):
        up_layers += [over(piece, plane << bit) for piece in up_layers]
    order = [0]
    for bit in range(layers.bit_length() - 2, -1, -1):
        order += [step ^ (1 << bit) for step in order]
    up_layers = [up_layers[order.index(step)] for step in range(layers)]

    local, through, ends, *pair_cuts = pl.pallas_call(
        functools.partial(scan_kernel, plane, layers),
        out_shape=(
            jax.ShapeDtypeStruct((rows_here, half), f32),
            jax.ShapeDtypeStruct((rows_here, half), f32),
            jax.ShapeDtypeStruct((shards, 2, half), f32),
        )
        + (jax.ShapeDtypeStruct((weight_rows, (plane + 2) * HEAD), bf16),) * layers,
        in_specs=[in_hbm(), vmem(), in_hbm(), in_hbm(), vmem()] + [in_hbm()] * 3,
        out_specs=(vmem(),) * 3 + (in_place(),) * layers,
        scratch_shapes=[
            pltpu.VMEM(array.shape, bf16)
            for array in (
                byte_states,
                mamba_input,
                mamba_step,
                query_weight,
                key_weight,
                value_weight,
            )
        ]
        + [pltpu.SemaphoreType.DMA((6,)), pltpu.SemaphoreType.DMA((3 * layers,))],
        cost_estimate=brief(),
        compiler_params=params(56),
    )(
        byte_states,
        outer_gain[None, :],
        mamba_input,
        mamba_step,
        decay_rate[None, :],
        query_weight,
        key_weight,
        value_weight,
    )
    ends = lax.all_to_all(ends, "seq", 0, 0, tiled=True)
    ends, up_layers[1], up_layers[2] = lax.optimization_barrier(
        (ends, up_layers[1], up_layers[2])
    )
    pieces = [pair_cuts[0]] + [over(pair_cuts[step], plane * step) for step in range(1, layers)]
    states, other_part = pl.pallas_call(
        states_kernel,
        out_shape=(
            jax.ShapeDtypeStruct((rows_here, half), bf16),
            jax.ShapeDtypeStruct((rows_here, half), f32),
        ),
        in_specs=[vmem()] * 4,
        out_specs=(vmem(),) * 2,
        cost_estimate=brief(),
        compiler_params=params(56),
    )(local, through, mixer_weight, ends)
    far_bias = swapped(own_bias)
    bias = jnp.where(
        lane == 0,
        jnp.concatenate([own_bias, far_bias], axis=1),
        jnp.concatenate([far_bias, own_bias], axis=1),
    )
    far_part, bias, pieces[1] = lax.optimization_barrier((swapped(other_part), bias, pieces[1]))
    encoded, leaving = pl.pallas_call(
        functools.partial(pool_kernel, plane),
        out_shape=(
            jax.ShapeDtypeStruct((rows_here, half), bf16),
            jax.ShapeDtypeStruct((shards, layers * slots, half), bf16),
        ),
        in_specs=[vmem()] * 5,
        out_specs=(vmem(),) * 2,
        cost_estimate=brief(),
        compiler_params=params(56),
    )(states, mixer_weight, far_part, byte_states, pool_pick)
    arrived = lax.all_to_all(leaving, "seq", 0, 0, tiled=True)
    up_cuts = pl.pallas_call(
        functools.partial(cut_kernel, plane),
        out_shape=(jax.ShapeDtypeStruct((layers, up_weight.shape[0], up_half), bf16),) * plane,
        in_specs=[in_place()] * (1 + layers),
        out_specs=(in_place(),) * plane,
        scratch_shapes=[
            pltpu.VMEM((layers, *up_weight.shape), bf16),
            pltpu.SemaphoreType.DMA((layers,)),
            pltpu.SemaphoreType.DMA((plane * layers // 2,)),
        ],
        cost_estimate=brief(),
        compiler_params=params(56),
    )(leaving, *up_layers)
    up_own = [up_cuts[0]] + [over(up_cuts[mask], mask) for mask in range(1, plane)]
    arrived, pieces, up_own = lax.optimization_barrier((arrived, pieces, up_own))
    near_rows = pl.pallas_call(
        own_kernel,
        out_shape=jax.ShapeDtypeStruct((plane, layers * CH_OWN, half), bf16),
        in_specs=[vmem()] * 2,
        out_specs=vmem(),
        cost_estimate=brief(),
        compiler_params=params(56),
    )(near_pick, arrived)
    near_rows, up_far = lax.optimization_barrier(
        (near_rows, [swapped(piece) for piece in up_own])
    )
    near = lax.all_to_all(
        near_rows, "seq", 0, 0, axis_index_groups=plane_groups, tiled=True
    ).reshape(total_rows, half)

    features = own_gain.shape[1]
    block = total_rows // plane
    sent_rows = total_rows + 2 * block + 2 * (total_rows // HEAD)
    partial_sums = pl.pallas_call(
        functools.partial(inner_kernel, plane, layers),
        out_shape=jax.ShapeDtypeStruct((plane, sent_rows, HEAD), bf16),
        in_specs=[vmem()] * 2 + [in_place()] * (2 + 2 * plane + layers),
        out_specs=vmem(),
        scratch_shapes=[
            pltpu.VMEM((total_rows, width), bf16),
            pltpu.VMEM((width, features), bf16),
            pltpu.VMEM((features, (plane + 2) * HEAD), bf16),
            pltpu.VMEM((8, total_rows), f32),
            pltpu.SemaphoreType.DMA((2 + 2 * shards + layers,)),
        ],
        cost_estimate=brief(),
        compiler_params=params(56),
    )(bias, own_gain, near, swapped(near), *up_own, *up_far, *pieces)
    got = lax.all_to_all(
        partial_sums, "seq", 0, 0, axis_index_groups=plane_groups, tiled=True
    )
    queries, pairs = pl.pallas_call(
        functools.partial(heads_kernel, inner_width),
        out_shape=(
            jax.ShapeDtypeStruct((total_rows, HEAD), bf16),
            jax.ShapeDtypeStruct((plane, 2 * block, HEAD), bf16),
        ),
        in_specs=[vmem()],
        out_specs=(vmem(),) * 2,
        scratch_shapes=[pltpu.VMEM((total_rows, HEAD), f32)],
        cost_estimate=brief(),
        compiler_params=params(10),
    )(got)
    pairs = lax.all_to_all(pairs, "seq", 0, 0, axis_index_groups=plane_groups, tiled=True)
    leaving = pl.pallas_call(
        attend_kernel,
        out_shape=jax.ShapeDtypeStruct((shards, window, HEAD), bf16),
        in_specs=[smem()] + [vmem()] * 2,
        out_specs=vmem(),
        scratch_shapes=[
            pltpu.VMEM((total_rows, HEAD), f32),
            pltpu.VMEM((total_rows, HEAD), bf16),
            pltpu.VMEM((total_rows, HEAD), bf16),
            pltpu.VMEM((total_rows + window, HEAD), bf16),
        ],
        cost_estimate=brief(),
        compiler_params=params(12),
    )(place, queries, pairs)
    pieces = lax.all_to_all(leaving, "seq", 0, 0, tiled=True)
    own_back, other_back = pl.pallas_call(
        return_kernel,
        out_shape=(jax.ShapeDtypeStruct((window, half), f32),) * 2,
        in_specs=[vmem()] * 2,
        out_specs=(vmem(),) * 2,
        scratch_shapes=[pltpu.VMEM((window, shards * HEAD), bf16)],
        cost_estimate=brief(),
        compiler_params=params(12),
    )(return_weight, pieces)
    return pl.pallas_call(
        join_kernel,
        out_shape=jax.ShapeDtypeStruct((rows_here, half), bf16),
        in_specs=[vmem()] * 4,
        out_specs=vmem(),
        cost_estimate=brief(),
        compiler_params=params(8),
    )(own_back, swapped(other_back), encoded, spread)


def prefix(value, axis, join, neutral):
    count, mine = (lax.axis_size(axis), lax.axis_index(axis))
    pieces = jax.tree.map(lambda part: lax.all_gather(part, axis), value)
    so_far = jax.tree.map(
        lambda part, zero: jnp.full_like(part, 0) + jnp.asarray(zero, part.dtype), value, neutral
    )

    def lap(position, so_far):
        longer = join(so_far, jax.tree.map(lambda part: part[position], pieces))
        return jax.tree.map(lambda new, old: jnp.where(position < mine, new, old), longer, so_far)

    return lax.fori_loop(0, count - 1, lap, so_far)


def rms_scale(values, gain):
    values = values.astype(jnp.float32)
    return values * lax.rsqrt(jnp.mean(values * values, axis=-1, keepdims=True) + eps) * gain


def combine_pairs(earlier, later):
    return (earlier[0] * later[0], later[0] * earlier[1] + later[1])


def pick_table(table, wanted, seq_ids):
    return jnp.sum(jnp.where(seq_ids[None, :] == wanted[:, None], table[None, :], 0), axis=1)


def block_size(piece_rows, shard_rows):
    limit = max(1, 1024 // shard_rows)
    pieces = max(1, piece_rows // shard_rows)
    best_size = 1
    for candidate in range(1, limit + 1):
        if pieces % candidate == 0:
            best_size = candidate
    return min(piece_rows, best_size * shard_rows)


def spread_heads(
    byte_states,
    outer_gain,
    mamba_input,
    mamba_step,
    decay_rate,
    mixer_weight,
    boundaries,
    span_counts,
    up_weight,
    up_bias,
    inner_gain,
    query_weight,
    key_weight,
    value_weight,
    return_weight,
):
    shards = lax.axis_size("seq")
    own_shard = lax.axis_index("seq")
    own_lane = lax.axis_index("mp")
    rows_here = byte_states.shape[0]
    capacity = boundaries.shape[1]
    column_count = mamba_input.shape[1]
    kv_local = key_weight.shape[1] // HEAD
    group_size = HEADS // KV_HEADS
    slot_count = capacity // shards
    offsets = jnp.cumsum(span_counts) - span_counts
    seq_ids = jnp.arange(shards, dtype=jnp.int32)
    own_offset = jnp.sum(jnp.where(seq_ids == own_shard, offsets, 0))
    own_count = jnp.sum(jnp.where(seq_ids == own_shard, span_counts, 0))
    normed = rms_scale(byte_states, outer_gain).astype(jnp.bfloat16)
    inputs = jnp.dot(normed, mamba_input, preferred_element_type=jnp.float32)
    step_sizes = jax.nn.softplus(jnp.dot(normed, mamba_step, preferred_element_type=jnp.float32))
    rate_steps = step_sizes * decay_rate
    decays = jnp.exp(-rate_steps)
    drives = jnp.sqrt(-jnp.expm1(-2.0 * rate_steps)) * inputs
    through, local_states = lax.associative_scan(combine_pairs, (decays, drives), axis=0)
    starting = (jnp.ones((column_count,), jnp.float32), jnp.zeros((column_count,), jnp.float32))
    arriving = prefix((through[-1], local_states[-1]), "seq", combine_pairs, starting)
    states = (local_states + through * arriving[1][None, :]).astype(jnp.bfloat16)
    partial_value = jnp.dot(states, mixer_weight, preferred_element_type=jnp.float32)
    mixed_sum = lax.psum(partial_value, "mp")
    encoded = (byte_states.astype(jnp.float32) + mixed_sum).astype(jnp.bfloat16)
    skip_part = lax.dynamic_slice_in_dim(encoded, own_lane * column_count, column_count, 1)
    own_marks = boundaries[0]
    pooled = encoded[jnp.minimum(own_marks, rows_here - 1)]
    row_width = pooled.shape[1]
    outgoing = jnp.roll(pooled.reshape(slot_count, shards, row_width), own_offset % shards, axis=1)
    incoming = lax.all_to_all(outgoing, "seq", split_axis=1, concat_axis=1, tiled=True)
    position = jnp.arange(CH_OWN, dtype=jnp.int32)
    span_index = own_shard + position * shards
    source = jnp.sum((offsets[None, :] <= span_index[:, None]).astype(jnp.int32), axis=1) - 1
    source_offset = pick_table(offsets, source, seq_ids)
    slot_index = (span_index - source_offset) // shards
    gathered_rows = incoming.reshape(slot_count * shards, row_width)[slot_index * shards + source]
    columns = gathered_rows
    widened_sum = jnp.dot(
        columns,
        lax.all_gather(up_weight, "seq", axis=0, tiled=True),
        preferred_element_type=jnp.float32,
    )
    widened_share = (widened_sum + up_bias[None, :]).astype(jnp.bfloat16)
    widened = lax.all_gather(widened_share, "mp", axis=1, tiled=True)
    inner_normed = rms_scale(widened, inner_gain).astype(jnp.bfloat16)
    columns = inner_normed
    query_part = jnp.dot(
        columns,
        lax.all_gather(query_weight, "seq", axis=0, tiled=True),
        preferred_element_type=jnp.float32,
    )
    key_part = jnp.dot(
        columns,
        lax.all_gather(key_weight, "seq", axis=0, tiled=True),
        preferred_element_type=jnp.float32,
    )
    value_part = jnp.dot(
        columns,
        lax.all_gather(value_weight, "seq", axis=0, tiled=True),
        preferred_element_type=jnp.float32,
    )
    queries = query_part.astype(jnp.bfloat16)
    key_rows = key_part.astype(jnp.bfloat16)
    value_rows = value_part.astype(jnp.bfloat16)
    query_count = queries.shape[0]
    grouped = (
        queries.reshape(query_count, kv_local, group_size, HEAD)
        .transpose(1, 0, 2, 3)
        .reshape(kv_local, query_count * group_size, HEAD)
    )
    row_index = jnp.repeat(span_index, group_size)
    shard_rows = key_rows.shape[0]
    score_scale = 1.0 / math.sqrt(HEAD)

    def key_index(whole_index):
        return whole_index // shard_rows + whole_index % shard_rows * shards

    def attend_block(running, key_block, value_block, index_block):
        row_peak, denominator, weighted = running
        scores = (
            jnp.einsum("hqd,khd->hqk", grouped, key_block, preferred_element_type=jnp.float32)
            * score_scale
        )
        scores = jnp.where(index_block[None, None, :] <= row_index[None, :, None], scores, masked)
        new_peak = jnp.maximum(row_peak, jnp.max(scores, axis=2))
        shrink = jnp.exp(row_peak - new_peak)
        lifted = jnp.exp(scores - new_peak[:, :, None])
        denominator = denominator * shrink + jnp.sum(lifted, axis=2)
        weighted = weighted * shrink[:, :, None] + jnp.einsum(
            "hqk,khd->hqd",
            lifted.astype(jnp.bfloat16),
            value_block,
            preferred_element_type=jnp.float32,
        )
        return (new_peak, denominator, weighted)

    query_total = query_count * group_size
    initial = (
        jnp.full((kv_local, query_total), masked, jnp.float32),
        jnp.zeros((kv_local, query_total), jnp.float32),
        jnp.zeros((kv_local, query_total, HEAD), jnp.float32),
    )
    key_piece = lax.all_gather(key_rows, "seq", axis=0, tiled=True)
    value_piece = lax.all_gather(value_rows, "seq", axis=0, tiled=True)
    piece_rows = key_piece.shape[0]
    block_rows = block_size(piece_rows, shard_rows)
    turn_count = piece_rows // block_rows
    key_blocks = key_piece.reshape(turn_count, block_rows, kv_local, HEAD)
    value_blocks = value_piece.reshape(turn_count, block_rows, kv_local, HEAD)

    def one_turn(turn_index, inner_running):
        whole_index = turn_index * block_rows + jnp.arange(block_rows, dtype=jnp.int32)
        return attend_block(
            inner_running, key_blocks[turn_index], value_blocks[turn_index], key_index(whole_index)
        )

    row_peak, denominator, weighted = lax.fori_loop(0, turn_count, one_turn, initial)
    attended = (weighted / denominator[:, :, None]).astype(jnp.bfloat16)
    attended = (
        attended.reshape(kv_local, query_count, group_size, HEAD)
        .transpose(1, 0, 2, 3)
        .reshape(query_count, kv_local * group_size * HEAD)
    )
    projected = jnp.dot(attended, return_weight, preferred_element_type=jnp.float32)
    returned = lax.psum_scatter(
        projected.astype(jnp.bfloat16), "mp", scatter_dimension=1, tiled=True
    )
    slot_ids = jnp.arange(slot_count, dtype=jnp.int32)
    lead_slot = (own_shard - offsets) % shards
    local_span = slot_ids[:, None] * shards + lead_slot[None, :]
    back_index = (offsets[None, :] + local_span - own_shard) // shards
    alive = local_span < span_counts[None, :]
    back_rows = jnp.where(
        alive[:, :, None],
        returned[jnp.clip(back_index, 0, CH_OWN - 1)],
        jnp.zeros((), jnp.bfloat16),
    )
    arrived = lax.all_to_all(back_rows, "seq", split_axis=1, concat_axis=1, tiled=True)
    span_results = jnp.roll(arrived, -(own_offset % shards), axis=1).reshape(capacity, column_count)
    positions = jnp.arange(rows_here, dtype=jnp.int32)
    live_slots = jnp.arange(capacity, dtype=jnp.int32) < own_count
    passed = jnp.sum(
        ((own_marks[None, :] <= positions[:, None]) & live_slots[None, :]).astype(jnp.int32), axis=1
    )
    return (skip_part.astype(jnp.float32) + span_results[passed - 1].astype(jnp.float32)).astype(
        jnp.bfloat16
    )


def solution(mesh):
    in_specs = (
        P("seq", None),
        P(),
        P(None, "mp"),
        P(None, "mp"),
        P("mp"),
        P("mp", None),
        P("seq", None),
        P(),
        P("seq", "mp"),
        P("mp"),
        P(),
        P("seq", "mp"),
        P("seq", "mp"),
        P("seq", "mp"),
        P("mp", None),
    )
    out_specs = P("seq", "mp")
    def on_device(*arrays):
        heads_here = arrays[11].shape[1] // HEAD
        fits = heads_here == mesh.shape["seq"] and mesh.shape["mp"] == 2
        return (one_head_each if fits else spread_heads)(*arrays)

    return jax.shard_map(
        on_device, mesh=mesh, in_specs=in_specs, out_specs=out_specs, check_vma=False
    )
```

```python
import functools
import math

import jax
import jax.numpy as jnp
from jax import lax
from jax.experimental import pallas as pl
from jax.experimental.pallas import tpu as pltpu
from jax.sharding import PartitionSpec as P

HEADS = 32
KV_HEADS = 8
HEAD = 128
CH_OWN = 64


eps = 1e-05
masked = -1e30
TILE = 16


def swapped(value):
    return lax.ppermute(value, "mp", [(0, 1), (1, 0)])


def vmem():
    return pl.BlockSpec(memory_space=pltpu.VMEM)


def smem():
    return pl.BlockSpec(memory_space=pltpu.SMEM)


def in_place():
    return pl.BlockSpec(memory_space=pl.ANY)


def in_hbm():
    return pl.BlockSpec(memory_space=pltpu.HBM)


def seat():
    return lax.axis_index("seq"), lax.axis_index("mp")


def params(mebibytes=24):
    return pltpu.CompilerParams(vmem_limit_bytes=mebibytes * 2**20)


def brief():
    return pl.CostEstimate(flops=1, bytes_accessed=1, transcendentals=0)


def lanes(which, size):
    return pl.ds(pl.multiple_of(which * size, size), size)


def rows_at(which, size):
    return pl.ds(pl.multiple_of(which * size, size), size)


def start_all(pairs, sems):
    copies = []
    for index, (from_ref, to_ref) in enumerate(pairs):
        copy = pltpu.make_async_copy(from_ref, to_ref, sems.at[index])
        copy.start()
        copies.append(copy)
    return copies


def copy_all(pairs, sems):
    for copy in start_all(pairs, sems):
        copy.wait()


def one_minus_exp(u):
    series = jnp.ones_like(u)
    for order in range(9, 1, -1):
        series = 1.0 - u * (1.0 / order) * series
    return jnp.where(u < 0.5, u * series, 1.0 - jnp.exp(-u))


def softplus(v):
    tail = jnp.exp(-jnp.abs(v))
    series = jnp.ones_like(tail)
    for order in range(6, 1, -1):
        series = 1.0 - tail * ((order - 1.0) / order) * series
    return jnp.maximum(v, 0.0) + jnp.where(tail < 0.03, tail * series, jnp.log(1.0 + tail))


def start_cuts(plane, query_ref, key_ref, value_ref, pair_outs, sems):
    layers = len(pair_outs)
    me, _ = seat()
    layer = me // plane
    group = plane * HEAD
    pairs = []
    for step, out_ref in enumerate(pair_outs):
        target = layer ^ step
        pairs.append((query_ref.at[:, lanes(target, group)], out_ref.at[:, pl.ds(0, group)]))
        pairs.append((key_ref.at[:, lanes(target, HEAD)], out_ref.at[:, pl.ds(group, HEAD)]))
        pairs.append(
            (value_ref.at[:, lanes(target, HEAD)], out_ref.at[:, pl.ds(group + HEAD, HEAD)])
        )
    return start_all(pairs, sems)


def scan_kernel(plane, layers, *refs):
    bytes_hbm, gain_ref, input_hbm, step_hbm, rate_ref = refs[:5]
    others, refs = refs[5:8], refs[8:]
    local_ref, through_ref, ends_ref = refs[:3]
    pair_outs, refs = refs[3 : 3 + layers], refs[3 + layers :]
    bytes_ref, input_ref, step_ref, *held, sems, cut_sems = refs
    fetches = start_all(
        [(bytes_hbm, bytes_ref), (step_hbm, step_ref), (input_hbm, input_ref), *zip(others, held)],
        sems,
    )
    fetches[0].wait()
    values = bytes_ref[...].astype(jnp.float32)
    scale = lax.rsqrt(jnp.mean(values * values, axis=1, keepdims=True) + eps)
    normed = (values * scale * gain_ref[...]).astype(jnp.bfloat16)
    fetches[1].wait()
    steps = softplus(jnp.dot(normed, step_ref[...], preferred_element_type=jnp.float32))
    rate_steps = steps * rate_ref[...]
    fetches[2].wait()
    inputs = jnp.dot(normed, input_ref[...], preferred_element_type=jnp.float32)
    for fetch in fetches[3:]:
        fetch.wait()
    cuts = start_cuts(plane, *held, pair_outs, cut_sems)
    decays = jnp.exp(-rate_steps)
    drives = jnp.sqrt(one_minus_exp(2.0 * rate_steps)) * inputs
    rows, width = decays.shape
    tile = 8
    decays = decays.reshape(rows // tile, tile, width)
    drives = drives.reshape(rows // tile, tile, width)
    place = lax.broadcasted_iota(jnp.int32, decays.shape, 1)
    for reach in (1, 2, 4):
        before_decays = pltpu.roll(decays, reach, 1)
        before_drives = pltpu.roll(drives, reach, 1)
        inside = place >= reach
        drives = jnp.where(inside, decays * before_drives + drives, drives)
        decays = jnp.where(inside, decays * before_decays, decays)
    state = jnp.zeros((1, width), jnp.float32)
    kept = jnp.ones((1, width), jnp.float32)
    for index in range(rows // tile):
        states = decays[index] * state + drives[index]
        passing = decays[index] * kept
        local_ref[pl.ds(index * tile, tile), :] = states
        through_ref[pl.ds(index * tile, tile), :] = passing
        state = states[tile - 1 :, :]
        kept = passing[tile - 1 :, :]
    for index in range(ends_ref.shape[0]):
        ends_ref[index, 0:1, :] = kept
        ends_ref[index, 1:2, :] = state
    for cut in cuts:
        cut.wait()


def states_kernel(local_ref, through_ref, mixer_ref, ends_ref, states_ref, other_ref):
    me, lane = seat()
    carry = jnp.zeros((1, local_ref.shape[1]), jnp.float32)
    for shard in range(ends_ref.shape[0]):
        later = ends_ref[shard, 0:1, :] * carry + ends_ref[shard, 1:2, :]
        carry = jnp.where(shard < me, later, carry)
    states = (local_ref[...] + through_ref[...] * carry).astype(jnp.bfloat16)
    states_ref[...] = states
    half = other_ref.shape[1]
    other_ref[...] = jnp.dot(
        states, mixer_ref[:, lanes(1 - lane, half)], preferred_element_type=jnp.float32
    )


def pool_kernel(
    plane, states_ref, mixer_ref, other_ref, bytes_ref, pick_ref, encoded_ref, out_ref
):
    half = other_ref.shape[1]
    columns = lanes(seat()[1], half)
    mixed = jnp.dot(states_ref[...], mixer_ref[:, columns], preferred_element_type=jnp.float32)
    skip = bytes_ref[:, columns].astype(jnp.float32)
    encoded = (skip + (mixed + other_ref[...])).astype(jnp.bfloat16)
    encoded_ref[...] = encoded
    picked = jnp.dot(pick_ref[...], encoded, preferred_element_type=jnp.float32)
    picked = picked.astype(jnp.bfloat16)
    size = out_ref.shape[1]
    for target in range(out_ref.shape[0]):
        start = target % plane * size
        out_ref[target] = picked[start : start + size, :]


def cut_kernel(plane, gate_ref, *refs):
    layers = len(refs) - plane - 3
    pieces, (*outs, held, sems, cut_sems) = refs[:layers], refs[layers:]
    copy_all([(piece, held.at[step]) for step, piece in enumerate(pieces)], sems)
    cross = lax.rem(seat()[0], plane)
    pairs = []
    for mask, out_ref in enumerate(outs):
        size = 2 * out_ref.shape[2] // layers
        for number in range(layers // 2):
            columns = lanes(number * plane + (cross ^ mask), size)
            pairs.append((held.at[:, :, columns], out_ref.at[:, :, pl.ds(number * size, size)]))
    copy_all(pairs, cut_sems)


def own_kernel(pick_ref, arrived_ref, out_ref):
    shards, slots, half = arrived_ref.shape
    rows = arrived_ref[...].reshape(shards * slots, half)
    own = jnp.dot(pick_ref[...], rows, preferred_element_type=jnp.float32).astype(jnp.bfloat16)
    for index in range(out_ref.shape[0]):
        out_ref[index] = own


def inner_kernel(plane, layers, bias_ref, gain_ref, near_ref, far_ref, *refs):
    up_own, refs = refs[:plane], refs[plane:]
    up_far, refs = refs[:plane], refs[plane:]
    pieces, refs = refs[:layers], refs[layers:]
    out_ref, pooled, up, weights, squares, sems = refs
    me, lane = seat()
    layer, cross = me // plane, lax.rem(me, plane)
    half = near_ref.shape[1]
    up_rows, up_half = up_own[0].shape[1:]
    pairs = [
        (near_ref, pooled.at[:, lanes(lane, half)]),
        (far_ref, pooled.at[:, lanes(1 - lane, half)]),
    ]
    for step in range(layers):
        for mask in range(plane):
            where = rows_at((layer ^ step) * plane + (cross ^ mask), up_rows)
            pairs.append((up_own[mask].at[step], up.at[where, lanes(lane, up_half)]))
            pairs.append((up_far[mask].at[step], up.at[where, lanes(1 - lane, up_half)]))
    for step, piece in enumerate(pieces):
        pairs.append((piece, weights.at[rows_at(layer ^ step, piece.shape[0]), :]))
    copies = start_all(pairs, sems)
    for copy in copies[:-layers]:
        copy.wait()
    rows = pooled.shape[0]
    block = rows // plane
    ones = jnp.ones((8, up.shape[1]), jnp.bfloat16)
    for index in range(plane):
        where = pl.ds(index * block, block)
        widened = jnp.dot(pooled[where, :], up[...], preferred_element_type=jnp.float32)
        widened = (widened + bias_ref[...]).astype(jnp.bfloat16).astype(jnp.float32)
        inner = (widened * gain_ref[...]).astype(jnp.bfloat16)
        square = widened * widened
        coarse = square.astype(jnp.bfloat16)
        fine = (square - coarse.astype(jnp.float32)).astype(jnp.bfloat16)
        squares[:, where] = sum(
            lax.dot_general(
                ones, part, (((1,), (1,)), ((), ())), preferred_element_type=jnp.float32
            )
            for part in (coarse, fine)
        )
        if index == 0:
            for copy in copies[-layers:]:
                copy.wait()
        sums = jnp.dot(inner, weights[...], preferred_element_type=jnp.float32)
        sums = sums.astype(jnp.bfloat16)
        for head in range(plane):
            out_ref[head, where, :] = sums[:, head * HEAD : (head + 1) * HEAD]
        for number in range(2):
            start = (plane + number) * HEAD
            out_ref[index, pl.ds(rows + number * block, block), :] = sums[:, start : start + HEAD]
    total = jnp.concatenate(
        [squares[0:1, start : start + HEAD] for start in range(0, rows, HEAD)], axis=0
    )
    coarse = total.astype(jnp.bfloat16).astype(jnp.float32)
    both = jnp.concatenate([coarse, total - coarse], axis=0).astype(jnp.bfloat16)
    for index in range(plane):
        out_ref[index, pl.ds(rows + 2 * block, both.shape[0]), :] = both


def heads_kernel(features, got_ref, query_ref, pair_ref, queries):
    plane = got_ref.shape[0]
    rows = query_ref.shape[0]
    block = rows // plane
    lines = rows // HEAD
    shards = rows // CH_OWN
    layers = shards // plane
    first = rows + 2 * block

    def added(start, size):
        parts = [got_ref[index, start : start + size, :].astype(jnp.float32) for index in range(plane)]
        return sum(parts[1:], parts[0])

    both = added(first, 2 * lines)
    total = both[:lines, :] + both[lines:, :]
    scale = jnp.transpose(lax.rsqrt(total * (1.0 / features) + eps))
    for line in range(lines):
        scaled = added(line * HEAD, HEAD) * scale[:, line : line + 1]
        for start in range(0, HEAD, CH_OWN):
            index = (line * HEAD + start) // CH_OWN
            shard = (index % layers) * plane + index // layers
            queries[pl.ds(shard, CH_OWN, stride=shards), :] = scaled[start : start + CH_OWN, :]
    query_ref[...] = queries[...].astype(jnp.bfloat16)
    cross = lax.rem(seat()[0], plane)
    per_block = block // HEAD
    for line in range(per_block):
        mine = scale[:, line : line + 1]
        for index in range(1, plane):
            column = index * per_block + line
            mine = jnp.where(cross == index, scale[:, column : column + 1], mine)
        for number in range(2):
            start = number * block + line * HEAD
            pair = (added(rows + start, HEAD) * mine).astype(jnp.bfloat16)
            for index in range(plane):
                pair_ref[index, pl.ds(start, HEAD), :] = pair


def attend_kernel(place_ref, query_ref, pair_ref, out_ref, natural, keys, values, attended):
    rows = query_ref.shape[0]
    window = out_ref.shape[1]
    plane = pair_ref.shape[0]
    part = rows // plane
    shards = rows // CH_OWN
    layers = shards // plane
    for number, held in enumerate((keys, values)):
        for cross in range(plane):
            for layer in range(layers):
                piece = pair_ref[cross, pl.ds(number * part + layer * CH_OWN, CH_OWN), :]
                where = pl.ds(layer * plane + cross, CH_OWN, stride=shards)
                natural[where, :] = piece.astype(jnp.float32)
        held[...] = natural[...].astype(jnp.bfloat16)
    block = min(256, rows)
    score_scale = 1.0 / math.sqrt(HEAD)
    for start in range(0, rows, block):
        stop = start + block
        scores = lax.dot_general(
            query_ref[start:stop, :],
            keys[0:stop, :],
            (((1,), (1,)), ((), ())),
            preferred_element_type=jnp.float32,
        )
        spots = lax.broadcasted_iota(jnp.int32, scores.shape, 1)
        mine = lax.broadcasted_iota(jnp.int32, scores.shape, 0) + start
        scores = jnp.where(spots <= mine, scores * score_scale, masked)
        peak = jnp.max(scores, axis=1, keepdims=True)
        lifted = jnp.exp(scores - peak)
        denominator = jnp.sum(lifted, axis=1, keepdims=True)
        weighted = jnp.dot(
            lifted.astype(jnp.bfloat16), values[0:stop, :], preferred_element_type=jnp.float32
        )
        attended[start:stop, :] = (weighted / denominator).astype(jnp.bfloat16)
    attended[rows:, :] = jnp.zeros((attended.shape[0] - rows, HEAD), jnp.bfloat16)
    for shard in range(out_ref.shape[0]):
        first = place_ref[shard]
        out_ref[shard] = attended[pl.ds(pl.multiple_of(first * TILE, TILE), window), :]


def return_kernel(weight_ref, pieces_ref, own_ref, other_ref, attended):
    half = own_ref.shape[1]
    lane = seat()[1]
    for head in range(pieces_ref.shape[0]):
        attended[:, head * HEAD : (head + 1) * HEAD] = pieces_ref[head]
    other_ref[...] = jnp.dot(
        attended[...], weight_ref[:, lanes(1 - lane, half)], preferred_element_type=jnp.float32
    )
    own_ref[...] = jnp.dot(
        attended[...], weight_ref[:, lanes(lane, half)], preferred_element_type=jnp.float32
    )


def join_kernel(own_ref, other_ref, encoded_ref, spread_ref, out_ref):
    returned = (own_ref[...] + other_ref[...]).astype(jnp.bfloat16)
    results = jnp.dot(spread_ref[...], returned, preferred_element_type=jnp.float32)
    out_ref[...] = (encoded_ref[...].astype(jnp.float32) + results).astype(jnp.bfloat16)


def one_head_each(
    byte_states,
    outer_gain,
    mamba_input,
    mamba_step,
    decay_rate,
    mixer_weight,
    boundaries,
    span_counts,
    up_weight,
    up_bias,
    inner_gain,
    query_weight,
    key_weight,
    value_weight,
    return_weight,
):
    shards = lax.axis_size("seq")
    me = lax.axis_index("seq")
    lane = lax.axis_index("mp")
    plane = HEADS // KV_HEADS
    layers = shards // plane
    rows_here, width = byte_states.shape
    half = mamba_input.shape[1]
    capacity = boundaries.shape[1]
    window = capacity + TILE
    total_rows = CH_OWN * shards
    inner_width = inner_gain.shape[0]
    inner_half = up_bias.shape[0]
    weight_rows = query_weight.shape[0]
    f32, bf16 = jnp.float32, jnp.bfloat16
    layer, cross = me // plane, me % plane
    plane_groups = [[first * plane + step for step in range(plane)] for first in range(layers)]

    def over(value, mask):
        return lax.ppermute(value, "seq", [(i, i ^ mask) for i in range(shards)])

    def after(value, done):
        return lax.optimization_barrier((value, done))[0]

    own_bias = up_bias.reshape(layers // 2, plane, weight_rows)
    own_bias = lax.dynamic_index_in_dim(own_bias, cross, 1, keepdims=False).reshape(1, -1)
    own_gain = inner_gain.reshape(layers, plane, weight_rows)
    own_gain = lax.dynamic_index_in_dim(own_gain, cross, 1, keepdims=False).reshape(1, -1)

    seq_ids = jnp.arange(shards, dtype=jnp.int32)
    offsets = jnp.cumsum(span_counts) - span_counts
    own_offset = jnp.sum(jnp.where(seq_ids == me, offsets, 0))
    own_count = jnp.sum(jnp.where(seq_ids == me, span_counts, 0))
    place = offsets // TILE
    own_marks = boundaries[0]
    positions = jnp.arange(rows_here, dtype=jnp.int32)
    spans_here = jnp.arange(capacity, dtype=jnp.int32)
    live = spans_here < own_count
    slots = capacity // shards
    slot_ids = jnp.arange(slots, dtype=jnp.int32)
    owners = seq_ids.reshape(layers, plane).T
    local_span = slot_ids * shards + ((owners - own_offset) % shards)[:, :, None]
    is_span = spans_here[None, :] == local_span.reshape(-1)[:, None]
    byte_at = jnp.sum(jnp.where(is_span, jnp.minimum(own_marks, rows_here - 1)[None, :], 0), axis=1)
    pool_pick = (positions[None, :] == byte_at[:, None]).astype(bf16)
    near_owner = jnp.arange(layers, dtype=jnp.int32) * plane + cross
    near_spans = near_owner[:, None] + jnp.arange(CH_OWN, dtype=jnp.int32)[None, :] * shards
    origin = jnp.sum((offsets <= near_spans[:, :, None]).astype(jnp.int32), axis=2) - 1
    origin_offset = jnp.sum(jnp.where(seq_ids == origin[:, :, None], offsets, 0), axis=2)
    arrived_row = (
        origin * (layers * slots)
        + jnp.arange(layers, dtype=jnp.int32)[:, None] * slots
        + (near_spans - origin_offset) // shards
    ).reshape(-1)
    near_pick = (
        jnp.arange(shards * layers * slots, dtype=jnp.int32)[None, :] == arrived_row[:, None]
    ).astype(bf16)
    passed = jnp.sum(
        ((own_marks[None, :] <= positions[:, None]) & live[None, :]).astype(jnp.int32), axis=1
    )
    result_row = passed - 1 + own_offset % TILE
    spread = (jnp.arange(window, dtype=jnp.int32)[None, :] == result_row[:, None]).astype(bf16)

    up_half = inner_half // plane
    up_layers = [up_weight] + [over(up_weight, plane * step) for step in range(1, layers)]

    local, through, ends, *pair_cuts = pl.pallas_call(
        functools.partial(scan_kernel, plane, layers),
        out_shape=(
            jax.ShapeDtypeStruct((rows_here, half), f32),
            jax.ShapeDtypeStruct((rows_here, half), f32),
            jax.ShapeDtypeStruct((shards, 2, half), f32),
        )
        + (jax.ShapeDtypeStruct((weight_rows, (plane + 2) * HEAD), bf16),) * layers,
        in_specs=[in_hbm(), vmem(), in_hbm(), in_hbm(), vmem()] + [in_hbm()] * 3,
        out_specs=(vmem(),) * 3 + (in_place(),) * layers,
        scratch_shapes=[
            pltpu.VMEM(array.shape, bf16)
            for array in (
                byte_states,
                mamba_input,
                mamba_step,
                query_weight,
                key_weight,
                value_weight,
            )
        ]
        + [pltpu.SemaphoreType.DMA((6,)), pltpu.SemaphoreType.DMA((3 * layers,))],
        cost_estimate=brief(),
        compiler_params=params(56),
    )(
        byte_states,
        outer_gain[None, :],
        mamba_input,
        mamba_step,
        decay_rate[None, :],
        query_weight,
        key_weight,
        value_weight,
    )
    ends = lax.all_to_all(ends, "seq", 0, 0, tiled=True)
    ends, up_layers = lax.optimization_barrier((ends, up_layers))
    pieces = [pair_cuts[0]] + [over(pair_cuts[step], plane * step) for step in range(1, layers)]
    states, other_part = pl.pallas_call(
        states_kernel,
        out_shape=(
            jax.ShapeDtypeStruct((rows_here, half), bf16),
            jax.ShapeDtypeStruct((rows_here, half), f32),
        ),
        in_specs=[vmem()] * 4,
        out_specs=(vmem(),) * 2,
        cost_estimate=brief(),
        compiler_params=params(56),
    )(local, through, mixer_weight, ends)
    far_bias = swapped(own_bias)
    bias = jnp.where(
        lane == 0,
        jnp.concatenate([own_bias, far_bias], axis=1),
        jnp.concatenate([far_bias, own_bias], axis=1),
    )
    far_part, bias, pieces[1] = lax.optimization_barrier((swapped(other_part), bias, pieces[1]))
    encoded, leaving = pl.pallas_call(
        functools.partial(pool_kernel, plane),
        out_shape=(
            jax.ShapeDtypeStruct((rows_here, half), bf16),
            jax.ShapeDtypeStruct((shards, layers * slots, half), bf16),
        ),
        in_specs=[vmem()] * 5,
        out_specs=(vmem(),) * 2,
        cost_estimate=brief(),
        compiler_params=params(56),
    )(states, mixer_weight, far_part, byte_states, pool_pick)
    arrived = lax.all_to_all(leaving, "seq", 0, 0, tiled=True)
    up_cuts = pl.pallas_call(
        functools.partial(cut_kernel, plane),
        out_shape=(jax.ShapeDtypeStruct((layers, up_weight.shape[0], up_half), bf16),) * plane,
        in_specs=[in_place()] * (1 + layers),
        out_specs=(in_place(),) * plane,
        scratch_shapes=[
            pltpu.VMEM((layers, *up_weight.shape), bf16),
            pltpu.SemaphoreType.DMA((layers,)),
            pltpu.SemaphoreType.DMA((plane * layers // 2,)),
        ],
        cost_estimate=brief(),
        compiler_params=params(56),
    )(leaving, *up_layers)
    up_own = [up_cuts[0]] + [over(up_cuts[mask], mask) for mask in range(1, plane)]
    arrived, pieces, up_own = lax.optimization_barrier((arrived, pieces, up_own))
    near_rows = pl.pallas_call(
        own_kernel,
        out_shape=jax.ShapeDtypeStruct((plane, layers * CH_OWN, half), bf16),
        in_specs=[vmem()] * 2,
        out_specs=vmem(),
        cost_estimate=brief(),
        compiler_params=params(56),
    )(near_pick, arrived)
    near_rows, up_far = lax.optimization_barrier(
        (near_rows, [swapped(piece) for piece in up_own])
    )
    near = lax.all_to_all(
        near_rows, "seq", 0, 0, axis_index_groups=plane_groups, tiled=True
    ).reshape(total_rows, half)

    features = own_gain.shape[1]
    block = total_rows // plane
    sent_rows = total_rows + 2 * block + 2 * (total_rows // HEAD)
    partial_sums = pl.pallas_call(
        functools.partial(inner_kernel, plane, layers),
        out_shape=jax.ShapeDtypeStruct((plane, sent_rows, HEAD), bf16),
        in_specs=[vmem()] * 2 + [in_place()] * (2 + 2 * plane + layers),
        out_specs=vmem(),
        scratch_shapes=[
            pltpu.VMEM((total_rows, width), bf16),
            pltpu.VMEM((width, features), bf16),
            pltpu.VMEM((features, (plane + 2) * HEAD), bf16),
            pltpu.VMEM((8, total_rows), f32),
            pltpu.SemaphoreType.DMA((2 + 2 * shards + layers,)),
        ],
        cost_estimate=brief(),
        compiler_params=params(56),
    )(bias, own_gain, near, swapped(near), *up_own, *up_far, *pieces)
    got = lax.all_to_all(
        partial_sums, "seq", 0, 0, axis_index_groups=plane_groups, tiled=True
    )
    queries, pairs = pl.pallas_call(
        functools.partial(heads_kernel, inner_width),
        out_shape=(
            jax.ShapeDtypeStruct((total_rows, HEAD), bf16),
            jax.ShapeDtypeStruct((plane, 2 * block, HEAD), bf16),
        ),
        in_specs=[vmem()],
        out_specs=(vmem(),) * 2,
        scratch_shapes=[pltpu.VMEM((total_rows, HEAD), f32)],
        cost_estimate=brief(),
        compiler_params=params(10),
    )(got)
    pairs = lax.all_to_all(pairs, "seq", 0, 0, axis_index_groups=plane_groups, tiled=True)
    leaving = pl.pallas_call(
        attend_kernel,
        out_shape=jax.ShapeDtypeStruct((shards, window, HEAD), bf16),
        in_specs=[smem()] + [vmem()] * 2,
        out_specs=vmem(),
        scratch_shapes=[
            pltpu.VMEM((total_rows, HEAD), f32),
            pltpu.VMEM((total_rows, HEAD), bf16),
            pltpu.VMEM((total_rows, HEAD), bf16),
            pltpu.VMEM((total_rows + window, HEAD), bf16),
        ],
        cost_estimate=brief(),
        compiler_params=params(12),
    )(place, queries, pairs)
    pieces = lax.all_to_all(leaving, "seq", 0, 0, tiled=True)
    own_back, other_back = pl.pallas_call(
        return_kernel,
        out_shape=(jax.ShapeDtypeStruct((window, half), f32),) * 2,
        in_specs=[vmem()] * 2,
        out_specs=(vmem(),) * 2,
        scratch_shapes=[pltpu.VMEM((window, shards * HEAD), bf16)],
        cost_estimate=brief(),
        compiler_params=params(12),
    )(return_weight, pieces)
    return pl.pallas_call(
        join_kernel,
        out_shape=jax.ShapeDtypeStruct((rows_here, half), bf16),
        in_specs=[vmem()] * 4,
        out_specs=vmem(),
        cost_estimate=brief(),
        compiler_params=params(8),
    )(own_back, swapped(other_back), encoded, spread)


def prefix(value, axis, join, neutral):
    count, mine = (lax.axis_size(axis), lax.axis_index(axis))
    pieces = jax.tree.map(lambda part: lax.all_gather(part, axis), value)
    so_far = jax.tree.map(
        lambda part, zero: jnp.full_like(part, 0) + jnp.asarray(zero, part.dtype), value, neutral
    )

    def lap(position, so_far):
        longer = join(so_far, jax.tree.map(lambda part: part[position], pieces))
        return jax.tree.map(lambda new, old: jnp.where(position < mine, new, old), longer, so_far)

    return lax.fori_loop(0, count - 1, lap, so_far)


def rms_scale(values, gain):
    values = values.astype(jnp.float32)
    return values * lax.rsqrt(jnp.mean(values * values, axis=-1, keepdims=True) + eps) * gain


def combine_pairs(earlier, later):
    return (earlier[0] * later[0], later[0] * earlier[1] + later[1])


def pick_table(table, wanted, seq_ids):
    return jnp.sum(jnp.where(seq_ids[None, :] == wanted[:, None], table[None, :], 0), axis=1)


def block_size(piece_rows, shard_rows):
    limit = max(1, 1024 // shard_rows)
    pieces = max(1, piece_rows // shard_rows)
    best_size = 1
    for candidate in range(1, limit + 1):
        if pieces % candidate == 0:
            best_size = candidate
    return min(piece_rows, best_size * shard_rows)


def spread_heads(
    byte_states,
    outer_gain,
    mamba_input,
    mamba_step,
    decay_rate,
    mixer_weight,
    boundaries,
    span_counts,
    up_weight,
    up_bias,
    inner_gain,
    query_weight,
    key_weight,
    value_weight,
    return_weight,
):
    shards = lax.axis_size("seq")
    own_shard = lax.axis_index("seq")
    own_lane = lax.axis_index("mp")
    rows_here = byte_states.shape[0]
    capacity = boundaries.shape[1]
    column_count = mamba_input.shape[1]
    kv_local = key_weight.shape[1] // HEAD
    group_size = HEADS // KV_HEADS
    slot_count = capacity // shards
    offsets = jnp.cumsum(span_counts) - span_counts
    seq_ids = jnp.arange(shards, dtype=jnp.int32)
    own_offset = jnp.sum(jnp.where(seq_ids == own_shard, offsets, 0))
    own_count = jnp.sum(jnp.where(seq_ids == own_shard, span_counts, 0))
    normed = rms_scale(byte_states, outer_gain).astype(jnp.bfloat16)
    inputs = jnp.dot(normed, mamba_input, preferred_element_type=jnp.float32)
    step_sizes = jax.nn.softplus(jnp.dot(normed, mamba_step, preferred_element_type=jnp.float32))
    rate_steps = step_sizes * decay_rate
    decays = jnp.exp(-rate_steps)
    drives = jnp.sqrt(-jnp.expm1(-2.0 * rate_steps)) * inputs
    through, local_states = lax.associative_scan(combine_pairs, (decays, drives), axis=0)
    starting = (jnp.ones((column_count,), jnp.float32), jnp.zeros((column_count,), jnp.float32))
    arriving = prefix((through[-1], local_states[-1]), "seq", combine_pairs, starting)
    states = (local_states + through * arriving[1][None, :]).astype(jnp.bfloat16)
    partial_value = jnp.dot(states, mixer_weight, preferred_element_type=jnp.float32)
    mixed_sum = lax.psum(partial_value, "mp")
    encoded = (byte_states.astype(jnp.float32) + mixed_sum).astype(jnp.bfloat16)
    skip_part = lax.dynamic_slice_in_dim(encoded, own_lane * column_count, column_count, 1)
    own_marks = boundaries[0]
    pooled = encoded[jnp.minimum(own_marks, rows_here - 1)]
    row_width = pooled.shape[1]
    outgoing = jnp.roll(pooled.reshape(slot_count, shards, row_width), own_offset % shards, axis=1)
    incoming = lax.all_to_all(outgoing, "seq", split_axis=1, concat_axis=1, tiled=True)
    position = jnp.arange(CH_OWN, dtype=jnp.int32)
    span_index = own_shard + position * shards
    source = jnp.sum((offsets[None, :] <= span_index[:, None]).astype(jnp.int32), axis=1) - 1
    source_offset = pick_table(offsets, source, seq_ids)
    slot_index = (span_index - source_offset) // shards
    gathered_rows = incoming.reshape(slot_count * shards, row_width)[slot_index * shards + source]
    columns = gathered_rows
    widened_sum = jnp.dot(
        columns,
        lax.all_gather(up_weight, "seq", axis=0, tiled=True),
        preferred_element_type=jnp.float32,
    )
    widened_share = (widened_sum + up_bias[None, :]).astype(jnp.bfloat16)
    widened = lax.all_gather(widened_share, "mp", axis=1, tiled=True)
    inner_normed = rms_scale(widened, inner_gain).astype(jnp.bfloat16)
    columns = inner_normed
    query_part = jnp.dot(
        columns,
        lax.all_gather(query_weight, "seq", axis=0, tiled=True),
        preferred_element_type=jnp.float32,
    )
    key_part = jnp.dot(
        columns,
        lax.all_gather(key_weight, "seq", axis=0, tiled=True),
        preferred_element_type=jnp.float32,
    )
    value_part = jnp.dot(
        columns,
        lax.all_gather(value_weight, "seq", axis=0, tiled=True),
        preferred_element_type=jnp.float32,
    )
    queries = query_part.astype(jnp.bfloat16)
    key_rows = key_part.astype(jnp.bfloat16)
    value_rows = value_part.astype(jnp.bfloat16)
    query_count = queries.shape[0]
    grouped = (
        queries.reshape(query_count, kv_local, group_size, HEAD)
        .transpose(1, 0, 2, 3)
        .reshape(kv_local, query_count * group_size, HEAD)
    )
    row_index = jnp.repeat(span_index, group_size)
    shard_rows = key_rows.shape[0]
    score_scale = 1.0 / math.sqrt(HEAD)

    def key_index(whole_index):
        return whole_index // shard_rows + whole_index % shard_rows * shards

    def attend_block(running, key_block, value_block, index_block):
        row_peak, denominator, weighted = running
        scores = (
            jnp.einsum("hqd,khd->hqk", grouped, key_block, preferred_element_type=jnp.float32)
            * score_scale
        )
        scores = jnp.where(index_block[None, None, :] <= row_index[None, :, None], scores, masked)
        new_peak = jnp.maximum(row_peak, jnp.max(scores, axis=2))
        shrink = jnp.exp(row_peak - new_peak)
        lifted = jnp.exp(scores - new_peak[:, :, None])
        denominator = denominator * shrink + jnp.sum(lifted, axis=2)
        weighted = weighted * shrink[:, :, None] + jnp.einsum(
            "hqk,khd->hqd",
            lifted.astype(jnp.bfloat16),
            value_block,
            preferred_element_type=jnp.float32,
        )
        return (new_peak, denominator, weighted)

    query_total = query_count * group_size
    initial = (
        jnp.full((kv_local, query_total), masked, jnp.float32),
        jnp.zeros((kv_local, query_total), jnp.float32),
        jnp.zeros((kv_local, query_total, HEAD), jnp.float32),
    )
    key_piece = lax.all_gather(key_rows, "seq", axis=0, tiled=True)
    value_piece = lax.all_gather(value_rows, "seq", axis=0, tiled=True)
    piece_rows = key_piece.shape[0]
    block_rows = block_size(piece_rows, shard_rows)
    turn_count = piece_rows // block_rows
    key_blocks = key_piece.reshape(turn_count, block_rows, kv_local, HEAD)
    value_blocks = value_piece.reshape(turn_count, block_rows, kv_local, HEAD)

    def one_turn(turn_index, inner_running):
        whole_index = turn_index * block_rows + jnp.arange(block_rows, dtype=jnp.int32)
        return attend_block(
            inner_running, key_blocks[turn_index], value_blocks[turn_index], key_index(whole_index)
        )

    row_peak, denominator, weighted = lax.fori_loop(0, turn_count, one_turn, initial)
    attended = (weighted / denominator[:, :, None]).astype(jnp.bfloat16)
    attended = (
        attended.reshape(kv_local, query_count, group_size, HEAD)
        .transpose(1, 0, 2, 3)
        .reshape(query_count, kv_local * group_size * HEAD)
    )
    projected = jnp.dot(attended, return_weight, preferred_element_type=jnp.float32)
    returned = lax.psum_scatter(
        projected.astype(jnp.bfloat16), "mp", scatter_dimension=1, tiled=True
    )
    slot_ids = jnp.arange(slot_count, dtype=jnp.int32)
    lead_slot = (own_shard - offsets) % shards
    local_span = slot_ids[:, None] * shards + lead_slot[None, :]
    back_index = (offsets[None, :] + local_span - own_shard) // shards
    alive = local_span < span_counts[None, :]
    back_rows = jnp.where(
        alive[:, :, None],
        returned[jnp.clip(back_index, 0, CH_OWN - 1)],
        jnp.zeros((), jnp.bfloat16),
    )
    arrived = lax.all_to_all(back_rows, "seq", split_axis=1, concat_axis=1, tiled=True)
    span_results = jnp.roll(arrived, -(own_offset % shards), axis=1).reshape(capacity, column_count)
    positions = jnp.arange(rows_here, dtype=jnp.int32)
    live_slots = jnp.arange(capacity, dtype=jnp.int32) < own_count
    passed = jnp.sum(
        ((own_marks[None, :] <= positions[:, None]) & live_slots[None, :]).astype(jnp.int32), axis=1
    )
    return (skip_part.astype(jnp.float32) + span_results[passed - 1].astype(jnp.float32)).astype(
        jnp.bfloat16
    )


def solution(mesh):
    in_specs = (
        P("seq", None),
        P(),
        P(None, "mp"),
        P(None, "mp"),
        P("mp"),
        P("mp", None),
        P("seq", None),
        P(),
        P("seq", "mp"),
        P("mp"),
        P(),
        P("seq", "mp"),
        P("seq", "mp"),
        P("seq", "mp"),
        P("mp", None),
    )
    out_specs = P("seq", "mp")
    def on_device(*arrays):
        heads_here = arrays[11].shape[1] // HEAD
        fits = heads_here == mesh.shape["seq"] and mesh.shape["mp"] == 2
        return (one_head_each if fits else spread_heads)(*arrays)

    return jax.shard_map(
        on_device, mesh=mesh, in_specs=in_specs, out_specs=out_specs, check_vma=False
    )
```

```python
import functools
import math

import jax
import jax.numpy as jnp
from jax import lax
from jax.experimental import pallas as pl
from jax.experimental.pallas import tpu as pltpu
from jax.sharding import PartitionSpec as P

HEADS = 32
KV_HEADS = 8
HEAD = 128
CH_OWN = 64


eps = 1e-05
masked = -1e30
TILE = 16


def swapped(value):
    return lax.ppermute(value, "mp", [(0, 1), (1, 0)])


def vmem():
    return pl.BlockSpec(memory_space=pltpu.VMEM)


def smem():
    return pl.BlockSpec(memory_space=pltpu.SMEM)


def in_place():
    return pl.BlockSpec(memory_space=pl.ANY)


def in_hbm():
    return pl.BlockSpec(memory_space=pltpu.HBM)


def seat():
    return lax.axis_index("seq"), lax.axis_index("mp")


def params(mebibytes=24):
    return pltpu.CompilerParams(vmem_limit_bytes=mebibytes * 2**20)


def brief():
    return pl.CostEstimate(flops=1, bytes_accessed=1, transcendentals=0)


def lanes(which, size):
    return pl.ds(pl.multiple_of(which * size, size), size)


def rows_at(which, size):
    return pl.ds(pl.multiple_of(which * size, size), size)


def start_all(pairs, sems):
    copies = []
    for index, (from_ref, to_ref) in enumerate(pairs):
        copy = pltpu.make_async_copy(from_ref, to_ref, sems.at[index])
        copy.start()
        copies.append(copy)
    return copies


def copy_all(pairs, sems):
    for copy in start_all(pairs, sems):
        copy.wait()


def one_minus_exp(u):
    series = jnp.ones_like(u)
    for order in range(9, 1, -1):
        series = 1.0 - u * (1.0 / order) * series
    return jnp.where(u < 0.5, u * series, 1.0 - jnp.exp(-u))


def softplus(v):
    tail = jnp.exp(-jnp.abs(v))
    series = jnp.ones_like(tail)
    for order in range(6, 1, -1):
        series = 1.0 - tail * ((order - 1.0) / order) * series
    return jnp.maximum(v, 0.0) + jnp.where(tail < 0.03, tail * series, jnp.log(1.0 + tail))


def start_cuts(plane, query_ref, key_ref, value_ref, pair_outs, sems):
    layers = len(pair_outs)
    me, _ = seat()
    layer = me // plane
    group = plane * HEAD
    pairs = []
    for step, out_ref in enumerate(pair_outs):
        target = layer ^ step
        pairs.append((query_ref.at[:, lanes(target, group)], out_ref.at[:, pl.ds(0, group)]))
        pairs.append((key_ref.at[:, lanes(target, HEAD)], out_ref.at[:, pl.ds(group, HEAD)]))
        pairs.append(
            (value_ref.at[:, lanes(target, HEAD)], out_ref.at[:, pl.ds(group + HEAD, HEAD)])
        )
    return start_all(pairs, sems)


def scan_kernel(plane, layers, *refs):
    bytes_hbm, gain_ref, input_hbm, step_hbm, rate_ref = refs[:5]
    others, refs = refs[5:8], refs[8:]
    local_ref, through_ref, ends_ref = refs[:3]
    pair_outs, refs = refs[3 : 3 + layers], refs[3 + layers :]
    bytes_ref, input_ref, step_ref, *held, sems, cut_sems = refs
    fetches = start_all(
        [(bytes_hbm, bytes_ref), (step_hbm, step_ref), (input_hbm, input_ref), *zip(others, held)],
        sems,
    )
    fetches[0].wait()
    values = bytes_ref[...].astype(jnp.float32)
    scale = lax.rsqrt(jnp.mean(values * values, axis=1, keepdims=True) + eps)
    normed = (values * scale * gain_ref[...]).astype(jnp.bfloat16)
    fetches[1].wait()
    steps = softplus(jnp.dot(normed, step_ref[...], preferred_element_type=jnp.float32))
    rate_steps = steps * rate_ref[...]
    fetches[2].wait()
    inputs = jnp.dot(normed, input_ref[...], preferred_element_type=jnp.float32)
    for fetch in fetches[3:]:
        fetch.wait()
    cuts = start_cuts(plane, *held, pair_outs, cut_sems)
    decays = jnp.exp(-rate_steps)
    drives = jnp.sqrt(one_minus_exp(2.0 * rate_steps)) * inputs
    rows, width = decays.shape
    tile = 8
    decays = decays.reshape(rows // tile, tile, width)
    drives = drives.reshape(rows // tile, tile, width)
    place = lax.broadcasted_iota(jnp.int32, decays.shape, 1)
    for reach in (1, 2, 4):
        before_decays = pltpu.roll(decays, reach, 1)
        before_drives = pltpu.roll(drives, reach, 1)
        inside = place >= reach
        drives = jnp.where(inside, decays * before_drives + drives, drives)
        decays = jnp.where(inside, decays * before_decays, decays)
    state = jnp.zeros((1, width), jnp.float32)
    kept = jnp.ones((1, width), jnp.float32)
    for index in range(rows // tile):
        states = decays[index] * state + drives[index]
        passing = decays[index] * kept
        local_ref[pl.ds(index * tile, tile), :] = states
        through_ref[pl.ds(index * tile, tile), :] = passing
        state = states[tile - 1 :, :]
        kept = passing[tile - 1 :, :]
    for index in range(ends_ref.shape[0]):
        ends_ref[index, 0:1, :] = kept
        ends_ref[index, 1:2, :] = state
    for cut in cuts:
        cut.wait()


def states_kernel(local_ref, through_ref, mixer_ref, ends_ref, states_ref, other_ref):
    me, lane = seat()
    carry = jnp.zeros((1, local_ref.shape[1]), jnp.float32)
    for shard in range(ends_ref.shape[0]):
        later = ends_ref[shard, 0:1, :] * carry + ends_ref[shard, 1:2, :]
        carry = jnp.where(shard < me, later, carry)
    states = (local_ref[...] + through_ref[...] * carry).astype(jnp.bfloat16)
    states_ref[...] = states
    half = other_ref.shape[1]
    other_ref[...] = jnp.dot(
        states, mixer_ref[:, lanes(1 - lane, half)], preferred_element_type=jnp.float32
    )


def pool_kernel(
    plane, states_ref, mixer_ref, other_ref, bytes_ref, pick_ref, encoded_ref, out_ref
):
    half = other_ref.shape[1]
    columns = lanes(seat()[1], half)
    mixed = jnp.dot(states_ref[...], mixer_ref[:, columns], preferred_element_type=jnp.float32)
    skip = bytes_ref[:, columns].astype(jnp.float32)
    encoded = (skip + (mixed + other_ref[...])).astype(jnp.bfloat16)
    encoded_ref[...] = encoded
    picked = jnp.dot(pick_ref[...], encoded, preferred_element_type=jnp.float32)
    picked = picked.astype(jnp.bfloat16)
    size = out_ref.shape[1]
    for target in range(out_ref.shape[0]):
        start = target % plane * size
        out_ref[target] = picked[start : start + size, :]


def cut_kernel(plane, gate_ref, *refs):
    layers = len(refs) - plane - 3
    pieces, (*outs, held, sems, cut_sems) = refs[:layers], refs[layers:]
    copy_all([(piece, held.at[step]) for step, piece in enumerate(pieces)], sems)
    cross = lax.rem(seat()[0], plane)
    pairs = []
    for mask, out_ref in enumerate(outs):
        size = 2 * out_ref.shape[2] // layers
        for number in range(layers // 2):
            columns = lanes(number * plane + (cross ^ mask), size)
            pairs.append((held.at[:, :, columns], out_ref.at[:, :, pl.ds(number * size, size)]))
    copy_all(pairs, cut_sems)


def own_kernel(pick_ref, arrived_ref, out_ref):
    shards, slots, half = arrived_ref.shape
    rows = arrived_ref[...].reshape(shards * slots, half)
    own = jnp.dot(pick_ref[...], rows, preferred_element_type=jnp.float32).astype(jnp.bfloat16)
    for index in range(out_ref.shape[0]):
        out_ref[index] = own


def inner_kernel(plane, layers, bias_ref, gain_ref, near_ref, far_ref, *refs):
    up_own, refs = refs[:plane], refs[plane:]
    up_far, refs = refs[:plane], refs[plane:]
    pieces, refs = refs[:layers], refs[layers:]
    query_ref, *pair_refs, pooled, up, weights, squares, pairs_held, sems, out_sems = refs
    me, lane = seat()
    layer, cross = me // plane, lax.rem(me, plane)
    half = near_ref.shape[1]
    up_rows, up_half = up_own[0].shape[1:]
    pairs = [
        (near_ref, pooled.at[:, lanes(lane, half)]),
        (far_ref, pooled.at[:, lanes(1 - lane, half)]),
    ]
    for step in range(layers):
        for mask in range(plane):
            where = rows_at((layer ^ step) * plane + (cross ^ mask), up_rows)
            pairs.append((up_own[mask].at[step], up.at[where, lanes(lane, up_half)]))
            pairs.append((up_far[mask].at[step], up.at[where, lanes(1 - lane, up_half)]))
    for step, piece in enumerate(pieces):
        pairs.append((piece, weights.at[rows_at(layer ^ step, piece.shape[0]), :]))
    copies = start_all(pairs, sems)
    for copy in copies[:-layers]:
        copy.wait()
    rows = pooled.shape[0]
    block = rows // plane
    ones = jnp.ones((8, up.shape[1]), jnp.bfloat16)
    for index in range(plane):
        where = pl.ds(index * block, block)
        widened = jnp.dot(pooled[where, :], up[...], preferred_element_type=jnp.float32)
        widened = (widened + bias_ref[...]).astype(jnp.bfloat16).astype(jnp.float32)
        inner = (widened * gain_ref[...]).astype(jnp.bfloat16)
        square = widened * widened
        coarse = square.astype(jnp.bfloat16)
        fine = (square - coarse.astype(jnp.float32)).astype(jnp.bfloat16)
        squares[:, where] = sum(
            lax.dot_general(
                ones, part, (((1,), (1,)), ((), ())), preferred_element_type=jnp.float32
            )
            for part in (coarse, fine)
        )
        if index == 0:
            for copy in copies[-layers:]:
                copy.wait()
        sums = jnp.dot(inner, weights[...], preferred_element_type=jnp.float32)
        sums = sums.astype(jnp.bfloat16)
        for head in range(plane):
            query_ref[head, where, :] = sums[:, head * HEAD : (head + 1) * HEAD]
        for number in range(2):
            start = (plane + number) * HEAD
            pairs_held[index, pl.ds(number * block, block), :] = sums[:, start : start + HEAD]
    total = jnp.concatenate(
        [squares[0:1, start : start + HEAD] for start in range(0, rows, HEAD)], axis=0
    )
    coarse = total.astype(jnp.bfloat16).astype(jnp.float32)
    both = jnp.concatenate([coarse, total - coarse], axis=0).astype(jnp.bfloat16)
    for index in range(plane):
        pairs_held[index, pl.ds(2 * block, both.shape[0]), :] = both
    copy_all(
        [(pairs_held.at[cross ^ mask], out_ref) for mask, out_ref in enumerate(pair_refs)], out_sems
    )


def added(refs, start, size):
    parts = [ref[pl.ds(start, size), :].astype(jnp.float32) for ref in refs]
    return sum(parts[1:], parts[0])


def row_scale(features, refs, lines):
    both = added(refs, refs[0].shape[0] - 2 * lines, 2 * lines)
    total = both[:lines, :] + both[lines:, :]
    return jnp.transpose(lax.rsqrt(total * (1.0 / features) + eps))


def pairs_kernel(features, lines, *refs):
    got_refs, pair_ref = refs[:-1], refs[-1]
    scale = row_scale(features, got_refs, lines)
    cross = lax.rem(seat()[0], len(got_refs))
    per_block = lines // len(got_refs)
    for line in range(per_block):
        mine = scale[:, line : line + 1]
        for index in range(1, len(got_refs)):
            column = index * per_block + line
            mine = jnp.where(cross == index, scale[:, column : column + 1], mine)
        for number in range(2):
            start = (number * per_block + line) * HEAD
            pair_ref[pl.ds(start, HEAD), :] = (added(got_refs, start, HEAD) * mine).astype(
                jnp.bfloat16
            )


def queries_kernel(features, got_ref, *refs):
    pair_refs, (query_ref, queries) = refs[:-2], refs[-2:]
    plane, rows, _ = got_ref.shape
    lines = rows // HEAD
    shards = rows // CH_OWN
    layers = shards // plane
    scale = row_scale(features, pair_refs, lines)
    for line in range(lines):
        parts = [got_ref.at[index] for index in range(plane)]
        scaled = added(parts, line * HEAD, HEAD) * scale[:, line : line + 1]
        for start in range(0, HEAD, CH_OWN):
            index = (line * HEAD + start) // CH_OWN
            shard = (index % layers) * plane + index // layers
            queries[pl.ds(shard, CH_OWN, stride=shards), :] = scaled[start : start + CH_OWN, :]
    query_ref[...] = queries[...].astype(jnp.bfloat16)


def attend_kernel(plane, place_ref, query_ref, *refs):
    pair_refs, (out_ref, natural, keys, values, attended) = refs[:plane], refs[plane:]
    rows = query_ref.shape[0]
    window = out_ref.shape[1]
    part = rows // plane
    shards = rows // CH_OWN
    layers = shards // plane
    cross = lax.rem(seat()[0], plane)
    for number, held in enumerate((keys, values)):
        for mask, pair_ref in enumerate(pair_refs):
            for layer in range(layers):
                piece = pair_ref[pl.ds(number * part + layer * CH_OWN, CH_OWN), :]
                where = pl.ds(layer * plane + (cross ^ mask), CH_OWN, stride=shards)
                natural[where, :] = piece.astype(jnp.float32)
        held[...] = natural[...].astype(jnp.bfloat16)
    block = min(256, rows)
    score_scale = 1.0 / math.sqrt(HEAD)
    for start in range(0, rows, block):
        stop = start + block
        scores = lax.dot_general(
            query_ref[start:stop, :],
            keys[0:stop, :],
            (((1,), (1,)), ((), ())),
            preferred_element_type=jnp.float32,
        )
        spots = lax.broadcasted_iota(jnp.int32, scores.shape, 1)
        mine = lax.broadcasted_iota(jnp.int32, scores.shape, 0) + start
        scores = jnp.where(spots <= mine, scores * score_scale, masked)
        peak = jnp.max(scores, axis=1, keepdims=True)
        lifted = jnp.exp(scores - peak)
        denominator = jnp.sum(lifted, axis=1, keepdims=True)
        weighted = jnp.dot(
            lifted.astype(jnp.bfloat16), values[0:stop, :], preferred_element_type=jnp.float32
        )
        attended[start:stop, :] = (weighted / denominator).astype(jnp.bfloat16)
    attended[rows:, :] = jnp.zeros((attended.shape[0] - rows, HEAD), jnp.bfloat16)
    for shard in range(out_ref.shape[0]):
        first = place_ref[shard]
        out_ref[shard] = attended[pl.ds(pl.multiple_of(first * TILE, TILE), window), :]


def return_kernel(weight_ref, pieces_ref, own_ref, other_ref, attended):
    half = own_ref.shape[1]
    lane = seat()[1]
    for head in range(pieces_ref.shape[0]):
        attended[:, head * HEAD : (head + 1) * HEAD] = pieces_ref[head]
    other_ref[...] = jnp.dot(
        attended[...], weight_ref[:, lanes(1 - lane, half)], preferred_element_type=jnp.float32
    )
    own_ref[...] = jnp.dot(
        attended[...], weight_ref[:, lanes(lane, half)], preferred_element_type=jnp.float32
    )


def join_kernel(own_ref, other_ref, encoded_ref, spread_ref, out_ref):
    returned = (own_ref[...] + other_ref[...]).astype(jnp.bfloat16)
    results = jnp.dot(spread_ref[...], returned, preferred_element_type=jnp.float32)
    out_ref[...] = (encoded_ref[...].astype(jnp.float32) + results).astype(jnp.bfloat16)


def one_head_each(
    byte_states,
    outer_gain,
    mamba_input,
    mamba_step,
    decay_rate,
    mixer_weight,
    boundaries,
    span_counts,
    up_weight,
    up_bias,
    inner_gain,
    query_weight,
    key_weight,
    value_weight,
    return_weight,
):
    shards = lax.axis_size("seq")
    me = lax.axis_index("seq")
    lane = lax.axis_index("mp")
    plane = HEADS // KV_HEADS
    layers = shards // plane
    rows_here, width = byte_states.shape
    half = mamba_input.shape[1]
    capacity = boundaries.shape[1]
    window = capacity + TILE
    total_rows = CH_OWN * shards
    inner_width = inner_gain.shape[0]
    inner_half = up_bias.shape[0]
    weight_rows = query_weight.shape[0]
    f32, bf16 = jnp.float32, jnp.bfloat16
    layer, cross = me // plane, me % plane
    plane_groups = [[first * plane + step for step in range(plane)] for first in range(layers)]

    def over(value, mask):
        return lax.ppermute(value, "seq", [(i, i ^ mask) for i in range(shards)])

    def after(value, done):
        return lax.optimization_barrier((value, done))[0]

    own_bias = up_bias.reshape(layers // 2, plane, weight_rows)
    own_bias = lax.dynamic_index_in_dim(own_bias, cross, 1, keepdims=False).reshape(1, -1)
    own_gain = inner_gain.reshape(layers, plane, weight_rows)
    own_gain = lax.dynamic_index_in_dim(own_gain, cross, 1, keepdims=False).reshape(1, -1)

    seq_ids = jnp.arange(shards, dtype=jnp.int32)
    offsets = jnp.cumsum(span_counts) - span_counts
    own_offset = jnp.sum(jnp.where(seq_ids == me, offsets, 0))
    own_count = jnp.sum(jnp.where(seq_ids == me, span_counts, 0))
    place = offsets // TILE
    own_marks = boundaries[0]
    positions = jnp.arange(rows_here, dtype=jnp.int32)
    spans_here = jnp.arange(capacity, dtype=jnp.int32)
    live = spans_here < own_count
    slots = capacity // shards
    slot_ids = jnp.arange(slots, dtype=jnp.int32)
    owners = seq_ids.reshape(layers, plane).T
    local_span = slot_ids * shards + ((owners - own_offset) % shards)[:, :, None]
    is_span = spans_here[None, :] == local_span.reshape(-1)[:, None]
    byte_at = jnp.sum(jnp.where(is_span, jnp.minimum(own_marks, rows_here - 1)[None, :], 0), axis=1)
    pool_pick = (positions[None, :] == byte_at[:, None]).astype(bf16)
    near_owner = jnp.arange(layers, dtype=jnp.int32) * plane + cross
    near_spans = near_owner[:, None] + jnp.arange(CH_OWN, dtype=jnp.int32)[None, :] * shards
    origin = jnp.sum((offsets <= near_spans[:, :, None]).astype(jnp.int32), axis=2) - 1
    origin_offset = jnp.sum(jnp.where(seq_ids == origin[:, :, None], offsets, 0), axis=2)
    arrived_row = (
        origin * (layers * slots)
        + jnp.arange(layers, dtype=jnp.int32)[:, None] * slots
        + (near_spans - origin_offset) // shards
    ).reshape(-1)
    near_pick = (
        jnp.arange(shards * layers * slots, dtype=jnp.int32)[None, :] == arrived_row[:, None]
    ).astype(bf16)
    passed = jnp.sum(
        ((own_marks[None, :] <= positions[:, None]) & live[None, :]).astype(jnp.int32), axis=1
    )
    result_row = passed - 1 + own_offset % TILE
    spread = (jnp.arange(window, dtype=jnp.int32)[None, :] == result_row[:, None]).astype(bf16)

    up_half = inner_half // plane
    up_layers = [up_weight] + [over(up_weight, plane * step) for step in range(1, layers)]

    local, through, ends, *pair_cuts = pl.pallas_call(
        functools.partial(scan_kernel, plane, layers),
        out_shape=(
            jax.ShapeDtypeStruct((rows_here, half), f32),
            jax.ShapeDtypeStruct((rows_here, half), f32),
            jax.ShapeDtypeStruct((shards, 2, half), f32),
        )
        + (jax.ShapeDtypeStruct((weight_rows, (plane + 2) * HEAD), bf16),) * layers,
        in_specs=[in_hbm(), vmem(), in_hbm(), in_hbm(), vmem()] + [in_hbm()] * 3,
        out_specs=(vmem(),) * 3 + (in_place(),) * layers,
        scratch_shapes=[
            pltpu.VMEM(array.shape, bf16)
            for array in (
                byte_states,
                mamba_input,
                mamba_step,
                query_weight,
                key_weight,
                value_weight,
            )
        ]
        + [pltpu.SemaphoreType.DMA((6,)), pltpu.SemaphoreType.DMA((3 * layers,))],
        cost_estimate=brief(),
        compiler_params=params(56),
    )(
        byte_states,
        outer_gain[None, :],
        mamba_input,
        mamba_step,
        decay_rate[None, :],
        query_weight,
        key_weight,
        value_weight,
    )
    ends = lax.all_to_all(ends, "seq", 0, 0, tiled=True)
    ends, up_layers = lax.optimization_barrier((ends, up_layers))
    pieces = [pair_cuts[0]] + [over(pair_cuts[step], plane * step) for step in range(1, layers)]
    states, other_part = pl.pallas_call(
        states_kernel,
        out_shape=(
            jax.ShapeDtypeStruct((rows_here, half), bf16),
            jax.ShapeDtypeStruct((rows_here, half), f32),
        ),
        in_specs=[vmem()] * 4,
        out_specs=(vmem(),) * 2,
        cost_estimate=brief(),
        compiler_params=params(56),
    )(local, through, mixer_weight, ends)
    far_bias = swapped(own_bias)
    bias = jnp.where(
        lane == 0,
        jnp.concatenate([own_bias, far_bias], axis=1),
        jnp.concatenate([far_bias, own_bias], axis=1),
    )
    far_part, bias, pieces[1] = lax.optimization_barrier((swapped(other_part), bias, pieces[1]))
    encoded, leaving = pl.pallas_call(
        functools.partial(pool_kernel, plane),
        out_shape=(
            jax.ShapeDtypeStruct((rows_here, half), bf16),
            jax.ShapeDtypeStruct((shards, layers * slots, half), bf16),
        ),
        in_specs=[vmem()] * 5,
        out_specs=(vmem(),) * 2,
        cost_estimate=brief(),
        compiler_params=params(56),
    )(states, mixer_weight, far_part, byte_states, pool_pick)
    arrived = lax.all_to_all(leaving, "seq", 0, 0, tiled=True)
    up_cuts = pl.pallas_call(
        functools.partial(cut_kernel, plane),
        out_shape=(jax.ShapeDtypeStruct((layers, up_weight.shape[0], up_half), bf16),) * plane,
        in_specs=[in_place()] * (1 + layers),
        out_specs=(in_place(),) * plane,
        scratch_shapes=[
            pltpu.VMEM((layers, *up_weight.shape), bf16),
            pltpu.SemaphoreType.DMA((layers,)),
            pltpu.SemaphoreType.DMA((plane * layers // 2,)),
        ],
        cost_estimate=brief(),
        compiler_params=params(56),
    )(leaving, *up_layers)
    up_own = [up_cuts[0]] + [over(up_cuts[mask], mask) for mask in range(1, plane)]
    arrived, pieces, up_own = lax.optimization_barrier((arrived, pieces, up_own))
    near_rows = pl.pallas_call(
        own_kernel,
        out_shape=jax.ShapeDtypeStruct((plane, layers * CH_OWN, half), bf16),
        in_specs=[vmem()] * 2,
        out_specs=vmem(),
        cost_estimate=brief(),
        compiler_params=params(56),
    )(near_pick, arrived)
    near_rows, up_far = lax.optimization_barrier(
        (near_rows, [swapped(piece) for piece in up_own])
    )
    near = lax.all_to_all(
        near_rows, "seq", 0, 0, axis_index_groups=plane_groups, tiled=True
    ).reshape(total_rows, half)

    features = own_gain.shape[1]
    block = total_rows // plane
    lines = total_rows // HEAD
    pair_rows = 2 * block + 2 * lines
    query_sums, *pair_sums = pl.pallas_call(
        functools.partial(inner_kernel, plane, layers),
        out_shape=(jax.ShapeDtypeStruct((plane, total_rows, HEAD), bf16),)
        + (jax.ShapeDtypeStruct((pair_rows, HEAD), bf16),) * plane,
        in_specs=[vmem()] * 2 + [in_place()] * (2 + 2 * plane + layers),
        out_specs=(vmem(),) + (in_place(),) * plane,
        scratch_shapes=[
            pltpu.VMEM((total_rows, width), bf16),
            pltpu.VMEM((width, features), bf16),
            pltpu.VMEM((features, (plane + 2) * HEAD), bf16),
            pltpu.VMEM((8, total_rows), f32),
            pltpu.VMEM((plane, pair_rows, HEAD), bf16),
            pltpu.SemaphoreType.DMA((2 + 2 * shards + layers,)),
            pltpu.SemaphoreType.DMA((plane,)),
        ],
        cost_estimate=brief(),
        compiler_params=params(56),
    )(bias, own_gain, near, swapped(near), *up_own, *up_far, *pieces)
    got_pairs = [pair_sums[0]] + [over(pair_sums[mask], mask) for mask in range(1, plane)]
    got_queries = lax.all_to_all(
        query_sums, "seq", 0, 0, axis_index_groups=plane_groups, tiled=True
    )
    pairs = pl.pallas_call(
        functools.partial(pairs_kernel, inner_width, lines),
        out_shape=jax.ShapeDtypeStruct((2 * block, HEAD), bf16),
        in_specs=[vmem()] * plane,
        out_specs=vmem(),
        cost_estimate=brief(),
        compiler_params=params(8),
    )(*got_pairs)
    whole_pairs = [pairs] + [over(pairs, mask) for mask in range(1, plane)]
    queries = pl.pallas_call(
        functools.partial(queries_kernel, inner_width),
        out_shape=jax.ShapeDtypeStruct((total_rows, HEAD), bf16),
        in_specs=[vmem()] * (1 + plane),
        out_specs=vmem(),
        scratch_shapes=[pltpu.VMEM((total_rows, HEAD), f32)],
        cost_estimate=brief(),
        compiler_params=params(10),
    )(got_queries, *got_pairs)
    leaving = pl.pallas_call(
        functools.partial(attend_kernel, plane),
        out_shape=jax.ShapeDtypeStruct((shards, window, HEAD), bf16),
        in_specs=[smem()] + [vmem()] * (1 + plane),
        out_specs=vmem(),
        scratch_shapes=[
            pltpu.VMEM((total_rows, HEAD), f32),
            pltpu.VMEM((total_rows, HEAD), bf16),
            pltpu.VMEM((total_rows, HEAD), bf16),
            pltpu.VMEM((total_rows + window, HEAD), bf16),
        ],
        cost_estimate=brief(),
        compiler_params=params(12),
    )(place, queries, *whole_pairs)
    pieces = lax.all_to_all(leaving, "seq", 0, 0, tiled=True)
    own_back, other_back = pl.pallas_call(
        return_kernel,
        out_shape=(jax.ShapeDtypeStruct((window, half), f32),) * 2,
        in_specs=[vmem()] * 2,
        out_specs=(vmem(),) * 2,
        scratch_shapes=[pltpu.VMEM((window, shards * HEAD), bf16)],
        cost_estimate=brief(),
        compiler_params=params(12),
    )(return_weight, pieces)
    return pl.pallas_call(
        join_kernel,
        out_shape=jax.ShapeDtypeStruct((rows_here, half), bf16),
        in_specs=[vmem()] * 4,
        out_specs=vmem(),
        cost_estimate=brief(),
        compiler_params=params(8),
    )(own_back, swapped(other_back), encoded, spread)


def prefix(value, axis, join, neutral):
    count, mine = (lax.axis_size(axis), lax.axis_index(axis))
    pieces = jax.tree.map(lambda part: lax.all_gather(part, axis), value)
    so_far = jax.tree.map(
        lambda part, zero: jnp.full_like(part, 0) + jnp.asarray(zero, part.dtype), value, neutral
    )

    def lap(position, so_far):
        longer = join(so_far, jax.tree.map(lambda part: part[position], pieces))
        return jax.tree.map(lambda new, old: jnp.where(position < mine, new, old), longer, so_far)

    return lax.fori_loop(0, count - 1, lap, so_far)


def rms_scale(values, gain):
    values = values.astype(jnp.float32)
    return values * lax.rsqrt(jnp.mean(values * values, axis=-1, keepdims=True) + eps) * gain


def combine_pairs(earlier, later):
    return (earlier[0] * later[0], later[0] * earlier[1] + later[1])


def pick_table(table, wanted, seq_ids):
    return jnp.sum(jnp.where(seq_ids[None, :] == wanted[:, None], table[None, :], 0), axis=1)


def block_size(piece_rows, shard_rows):
    limit = max(1, 1024 // shard_rows)
    pieces = max(1, piece_rows // shard_rows)
    best_size = 1
    for candidate in range(1, limit + 1):
        if pieces % candidate == 0:
            best_size = candidate
    return min(piece_rows, best_size * shard_rows)


def spread_heads(
    byte_states,
    outer_gain,
    mamba_input,
    mamba_step,
    decay_rate,
    mixer_weight,
    boundaries,
    span_counts,
    up_weight,
    up_bias,
    inner_gain,
    query_weight,
    key_weight,
    value_weight,
    return_weight,
):
    shards = lax.axis_size("seq")
    own_shard = lax.axis_index("seq")
    own_lane = lax.axis_index("mp")
    rows_here = byte_states.shape[0]
    capacity = boundaries.shape[1]
    column_count = mamba_input.shape[1]
    kv_local = key_weight.shape[1] // HEAD
    group_size = HEADS // KV_HEADS
    slot_count = capacity // shards
    offsets = jnp.cumsum(span_counts) - span_counts
    seq_ids = jnp.arange(shards, dtype=jnp.int32)
    own_offset = jnp.sum(jnp.where(seq_ids == own_shard, offsets, 0))
    own_count = jnp.sum(jnp.where(seq_ids == own_shard, span_counts, 0))
    normed = rms_scale(byte_states, outer_gain).astype(jnp.bfloat16)
    inputs = jnp.dot(normed, mamba_input, preferred_element_type=jnp.float32)
    step_sizes = jax.nn.softplus(jnp.dot(normed, mamba_step, preferred_element_type=jnp.float32))
    rate_steps = step_sizes * decay_rate
    decays = jnp.exp(-rate_steps)
    drives = jnp.sqrt(-jnp.expm1(-2.0 * rate_steps)) * inputs
    through, local_states = lax.associative_scan(combine_pairs, (decays, drives), axis=0)
    starting = (jnp.ones((column_count,), jnp.float32), jnp.zeros((column_count,), jnp.float32))
    arriving = prefix((through[-1], local_states[-1]), "seq", combine_pairs, starting)
    states = (local_states + through * arriving[1][None, :]).astype(jnp.bfloat16)
    partial_value = jnp.dot(states, mixer_weight, preferred_element_type=jnp.float32)
    mixed_sum = lax.psum(partial_value, "mp")
    encoded = (byte_states.astype(jnp.float32) + mixed_sum).astype(jnp.bfloat16)
    skip_part = lax.dynamic_slice_in_dim(encoded, own_lane * column_count, column_count, 1)
    own_marks = boundaries[0]
    pooled = encoded[jnp.minimum(own_marks, rows_here - 1)]
    row_width = pooled.shape[1]
    outgoing = jnp.roll(pooled.reshape(slot_count, shards, row_width), own_offset % shards, axis=1)
    incoming = lax.all_to_all(outgoing, "seq", split_axis=1, concat_axis=1, tiled=True)
    position = jnp.arange(CH_OWN, dtype=jnp.int32)
    span_index = own_shard + position * shards
    source = jnp.sum((offsets[None, :] <= span_index[:, None]).astype(jnp.int32), axis=1) - 1
    source_offset = pick_table(offsets, source, seq_ids)
    slot_index = (span_index - source_offset) // shards
    gathered_rows = incoming.reshape(slot_count * shards, row_width)[slot_index * shards + source]
    columns = gathered_rows
    widened_sum = jnp.dot(
        columns,
        lax.all_gather(up_weight, "seq", axis=0, tiled=True),
        preferred_element_type=jnp.float32,
    )
    widened_share = (widened_sum + up_bias[None, :]).astype(jnp.bfloat16)
    widened = lax.all_gather(widened_share, "mp", axis=1, tiled=True)
    inner_normed = rms_scale(widened, inner_gain).astype(jnp.bfloat16)
    columns = inner_normed
    query_part = jnp.dot(
        columns,
        lax.all_gather(query_weight, "seq", axis=0, tiled=True),
        preferred_element_type=jnp.float32,
    )
    key_part = jnp.dot(
        columns,
        lax.all_gather(key_weight, "seq", axis=0, tiled=True),
        preferred_element_type=jnp.float32,
    )
    value_part = jnp.dot(
        columns,
        lax.all_gather(value_weight, "seq", axis=0, tiled=True),
        preferred_element_type=jnp.float32,
    )
    queries = query_part.astype(jnp.bfloat16)
    key_rows = key_part.astype(jnp.bfloat16)
    value_rows = value_part.astype(jnp.bfloat16)
    query_count = queries.shape[0]
    grouped = (
        queries.reshape(query_count, kv_local, group_size, HEAD)
        .transpose(1, 0, 2, 3)
        .reshape(kv_local, query_count * group_size, HEAD)
    )
    row_index = jnp.repeat(span_index, group_size)
    shard_rows = key_rows.shape[0]
    score_scale = 1.0 / math.sqrt(HEAD)

    def key_index(whole_index):
        return whole_index // shard_rows + whole_index % shard_rows * shards

    def attend_block(running, key_block, value_block, index_block):
        row_peak, denominator, weighted = running
        scores = (
            jnp.einsum("hqd,khd->hqk", grouped, key_block, preferred_element_type=jnp.float32)
            * score_scale
        )
        scores = jnp.where(index_block[None, None, :] <= row_index[None, :, None], scores, masked)
        new_peak = jnp.maximum(row_peak, jnp.max(scores, axis=2))
        shrink = jnp.exp(row_peak - new_peak)
        lifted = jnp.exp(scores - new_peak[:, :, None])
        denominator = denominator * shrink + jnp.sum(lifted, axis=2)
        weighted = weighted * shrink[:, :, None] + jnp.einsum(
            "hqk,khd->hqd",
            lifted.astype(jnp.bfloat16),
            value_block,
            preferred_element_type=jnp.float32,
        )
        return (new_peak, denominator, weighted)

    query_total = query_count * group_size
    initial = (
        jnp.full((kv_local, query_total), masked, jnp.float32),
        jnp.zeros((kv_local, query_total), jnp.float32),
        jnp.zeros((kv_local, query_total, HEAD), jnp.float32),
    )
    key_piece = lax.all_gather(key_rows, "seq", axis=0, tiled=True)
    value_piece = lax.all_gather(value_rows, "seq", axis=0, tiled=True)
    piece_rows = key_piece.shape[0]
    block_rows = block_size(piece_rows, shard_rows)
    turn_count = piece_rows // block_rows
    key_blocks = key_piece.reshape(turn_count, block_rows, kv_local, HEAD)
    value_blocks = value_piece.reshape(turn_count, block_rows, kv_local, HEAD)

    def one_turn(turn_index, inner_running):
        whole_index = turn_index * block_rows + jnp.arange(block_rows, dtype=jnp.int32)
        return attend_block(
            inner_running, key_blocks[turn_index], value_blocks[turn_index], key_index(whole_index)
        )

    row_peak, denominator, weighted = lax.fori_loop(0, turn_count, one_turn, initial)
    attended = (weighted / denominator[:, :, None]).astype(jnp.bfloat16)
    attended = (
        attended.reshape(kv_local, query_count, group_size, HEAD)
        .transpose(1, 0, 2, 3)
        .reshape(query_count, kv_local * group_size * HEAD)
    )
    projected = jnp.dot(attended, return_weight, preferred_element_type=jnp.float32)
    returned = lax.psum_scatter(
        projected.astype(jnp.bfloat16), "mp", scatter_dimension=1, tiled=True
    )
    slot_ids = jnp.arange(slot_count, dtype=jnp.int32)
    lead_slot = (own_shard - offsets) % shards
    local_span = slot_ids[:, None] * shards + lead_slot[None, :]
    back_index = (offsets[None, :] + local_span - own_shard) // shards
    alive = local_span < span_counts[None, :]
    back_rows = jnp.where(
        alive[:, :, None],
        returned[jnp.clip(back_index, 0, CH_OWN - 1)],
        jnp.zeros((), jnp.bfloat16),
    )
    arrived = lax.all_to_all(back_rows, "seq", split_axis=1, concat_axis=1, tiled=True)
    span_results = jnp.roll(arrived, -(own_offset % shards), axis=1).reshape(capacity, column_count)
    positions = jnp.arange(rows_here, dtype=jnp.int32)
    live_slots = jnp.arange(capacity, dtype=jnp.int32) < own_count
    passed = jnp.sum(
        ((own_marks[None, :] <= positions[:, None]) & live_slots[None, :]).astype(jnp.int32), axis=1
    )
    return (skip_part.astype(jnp.float32) + span_results[passed - 1].astype(jnp.float32)).astype(
        jnp.bfloat16
    )


def solution(mesh):
    in_specs = (
        P("seq", None),
        P(),
        P(None, "mp"),
        P(None, "mp"),
        P("mp"),
        P("mp", None),
        P("seq", None),
        P(),
        P("seq", "mp"),
        P("mp"),
        P(),
        P("seq", "mp"),
        P("seq", "mp"),
        P("seq", "mp"),
        P("mp", None),
    )
    out_specs = P("seq", "mp")
    def on_device(*arrays):
        heads_here = arrays[11].shape[1] // HEAD
        fits = heads_here == mesh.shape["seq"] and mesh.shape["mp"] == 2
        return (one_head_each if fits else spread_heads)(*arrays)

    return jax.shard_map(
        on_device, mesh=mesh, in_specs=in_specs, out_specs=out_specs, check_vma=False
    )
```

```python
import functools
import math

import jax
import jax.numpy as jnp
from jax import lax
from jax.experimental import pallas as pl
from jax.experimental.pallas import tpu as pltpu
from jax.sharding import PartitionSpec as P

HEADS = 32
KV_HEADS = 8
HEAD = 128
CH_OWN = 64


eps = 1e-05
masked = -1e30
TILE = 16


def swapped(value):
    return lax.ppermute(value, "mp", [(0, 1), (1, 0)])


def vmem():
    return pl.BlockSpec(memory_space=pltpu.VMEM)


def smem():
    return pl.BlockSpec(memory_space=pltpu.SMEM)


def in_place():
    return pl.BlockSpec(memory_space=pl.ANY)


def in_hbm():
    return pl.BlockSpec(memory_space=pltpu.HBM)


def seat():
    return lax.axis_index("seq"), lax.axis_index("mp")


def params(mebibytes=24):
    return pltpu.CompilerParams(vmem_limit_bytes=mebibytes * 2**20)


def brief():
    return pl.CostEstimate(flops=1, bytes_accessed=1, transcendentals=0)


def lanes(which, size):
    return pl.ds(pl.multiple_of(which * size, size), size)


def rows_at(which, size):
    return pl.ds(pl.multiple_of(which * size, size), size)


def start_all(pairs, sems):
    copies = []
    for index, (from_ref, to_ref) in enumerate(pairs):
        copy = pltpu.make_async_copy(from_ref, to_ref, sems.at[index])
        copy.start()
        copies.append(copy)
    return copies


def copy_all(pairs, sems):
    for copy in start_all(pairs, sems):
        copy.wait()


def one_minus_exp(u):
    series = jnp.ones_like(u)
    for order in range(9, 1, -1):
        series = 1.0 - u * (1.0 / order) * series
    return jnp.where(u < 0.5, u * series, 1.0 - jnp.exp(-u))


def softplus(v):
    tail = jnp.exp(-jnp.abs(v))
    series = jnp.ones_like(tail)
    for order in range(6, 1, -1):
        series = 1.0 - tail * ((order - 1.0) / order) * series
    return jnp.maximum(v, 0.0) + jnp.where(tail < 0.03, tail * series, jnp.log(1.0 + tail))


def start_cuts(plane, query_ref, key_ref, value_ref, pair_outs, sems):
    layers = len(pair_outs)
    me, _ = seat()
    layer = me // plane
    group = plane * HEAD
    pairs = []
    for step, out_ref in enumerate(pair_outs):
        target = layer ^ step
        pairs.append((query_ref.at[:, lanes(target, group)], out_ref.at[:, pl.ds(0, group)]))
        pairs.append((key_ref.at[:, lanes(target, HEAD)], out_ref.at[:, pl.ds(group, HEAD)]))
        pairs.append(
            (value_ref.at[:, lanes(target, HEAD)], out_ref.at[:, pl.ds(group + HEAD, HEAD)])
        )
    return start_all(pairs, sems)


def scan_kernel(plane, layers, *refs):
    bytes_hbm, gain_ref, input_hbm, step_hbm, rate_ref = refs[:5]
    others, refs = refs[5:8], refs[8:]
    local_ref, through_ref, ends_ref = refs[:3]
    pair_outs, refs = refs[3 : 3 + layers], refs[3 + layers :]
    bytes_ref, input_ref, step_ref, *held, sems, cut_sems = refs
    fetches = start_all(
        [(bytes_hbm, bytes_ref), (step_hbm, step_ref), (input_hbm, input_ref), *zip(others, held)],
        sems,
    )
    fetches[0].wait()
    values = bytes_ref[...].astype(jnp.float32)
    scale = lax.rsqrt(jnp.mean(values * values, axis=1, keepdims=True) + eps)
    normed = (values * scale * gain_ref[...]).astype(jnp.bfloat16)
    fetches[1].wait()
    steps = softplus(jnp.dot(normed, step_ref[...], preferred_element_type=jnp.float32))
    rate_steps = steps * rate_ref[...]
    fetches[2].wait()
    inputs = jnp.dot(normed, input_ref[...], preferred_element_type=jnp.float32)
    for fetch in fetches[3:]:
        fetch.wait()
    cuts = start_cuts(plane, *held, pair_outs, cut_sems)
    decays = jnp.exp(-rate_steps)
    drives = jnp.sqrt(one_minus_exp(2.0 * rate_steps)) * inputs
    rows, width = decays.shape
    tile = 8
    decays = decays.reshape(rows // tile, tile, width)
    drives = drives.reshape(rows // tile, tile, width)
    place = lax.broadcasted_iota(jnp.int32, decays.shape, 1)
    for reach in (1, 2, 4):
        before_decays = pltpu.roll(decays, reach, 1)
        before_drives = pltpu.roll(drives, reach, 1)
        inside = place >= reach
        drives = jnp.where(inside, decays * before_drives + drives, drives)
        decays = jnp.where(inside, decays * before_decays, decays)
    state = jnp.zeros((1, width), jnp.float32)
    kept = jnp.ones((1, width), jnp.float32)
    for index in range(rows // tile):
        states = decays[index] * state + drives[index]
        passing = decays[index] * kept
        local_ref[pl.ds(index * tile, tile), :] = states
        through_ref[pl.ds(index * tile, tile), :] = passing
        state = states[tile - 1 :, :]
        kept = passing[tile - 1 :, :]
    for index in range(ends_ref.shape[0]):
        ends_ref[index, 0:1, :] = kept
        ends_ref[index, 1:2, :] = state
    for cut in cuts:
        cut.wait()


def states_kernel(local_ref, through_ref, mixer_ref, ends_ref, states_ref, other_ref):
    me, lane = seat()
    carry = jnp.zeros((1, local_ref.shape[1]), jnp.float32)
    for shard in range(ends_ref.shape[0]):
        later = ends_ref[shard, 0:1, :] * carry + ends_ref[shard, 1:2, :]
        carry = jnp.where(shard < me, later, carry)
    states = (local_ref[...] + through_ref[...] * carry).astype(jnp.bfloat16)
    states_ref[...] = states
    half = other_ref.shape[1]
    other_ref[...] = jnp.dot(
        states, mixer_ref[:, lanes(1 - lane, half)], preferred_element_type=jnp.float32
    )


def pool_kernel(
    plane, states_ref, mixer_ref, other_ref, bytes_ref, pick_ref, encoded_ref, out_ref
):
    half = other_ref.shape[1]
    columns = lanes(seat()[1], half)
    mixed = jnp.dot(states_ref[...], mixer_ref[:, columns], preferred_element_type=jnp.float32)
    skip = bytes_ref[:, columns].astype(jnp.float32)
    encoded = (skip + (mixed + other_ref[...])).astype(jnp.bfloat16)
    encoded_ref[...] = encoded
    picked = jnp.dot(pick_ref[...], encoded, preferred_element_type=jnp.float32)
    picked = picked.astype(jnp.bfloat16)
    size = out_ref.shape[1]
    for target in range(out_ref.shape[0]):
        start = target % plane * size
        out_ref[target] = picked[start : start + size, :]


def cut_kernel(plane, gate_ref, *refs):
    layers = len(refs) - plane - 3
    pieces, (*outs, held, sems, cut_sems) = refs[:layers], refs[layers:]
    copy_all([(piece, held.at[step]) for step, piece in enumerate(pieces)], sems)
    cross = lax.rem(seat()[0], plane)
    pairs = []
    for mask, out_ref in enumerate(outs):
        size = 2 * out_ref.shape[2] // layers
        for number in range(layers // 2):
            columns = lanes(number * plane + (cross ^ mask), size)
            pairs.append((held.at[:, :, columns], out_ref.at[:, :, pl.ds(number * size, size)]))
    copy_all(pairs, cut_sems)


def own_kernel(pick_ref, arrived_ref, out_ref):
    shards, slots, half = arrived_ref.shape
    rows = arrived_ref[...].reshape(shards * slots, half)
    own = jnp.dot(pick_ref[...], rows, preferred_element_type=jnp.float32).astype(jnp.bfloat16)
    for index in range(out_ref.shape[0]):
        out_ref[index] = own


def inner_kernel(plane, layers, bias_ref, gain_ref, near_ref, far_ref, *refs):
    up_own, refs = refs[:plane], refs[plane:]
    up_far, refs = refs[:plane], refs[plane:]
    pieces, refs = refs[:layers], refs[layers:]
    query_refs, pair_refs, refs = refs[:plane], refs[plane : 2 * plane], refs[2 * plane :]
    pooled, up, weights, squares, queries_held, pairs_held, sems, out_sems = refs
    me, lane = seat()
    layer, cross = me // plane, lax.rem(me, plane)
    half = near_ref.shape[1]
    up_rows, up_half = up_own[0].shape[1:]
    pairs = [
        (near_ref, pooled.at[:, lanes(lane, half)]),
        (far_ref, pooled.at[:, lanes(1 - lane, half)]),
    ]
    for step in range(layers):
        for mask in range(plane):
            where = rows_at((layer ^ step) * plane + (cross ^ mask), up_rows)
            pairs.append((up_own[mask].at[step], up.at[where, lanes(lane, up_half)]))
            pairs.append((up_far[mask].at[step], up.at[where, lanes(1 - lane, up_half)]))
    for step, piece in enumerate(pieces):
        pairs.append((piece, weights.at[rows_at(layer ^ step, piece.shape[0]), :]))
    copies = start_all(pairs, sems)
    for copy in copies[:-layers]:
        copy.wait()
    rows = pooled.shape[0]
    block = rows // plane
    ones = jnp.ones((8, up.shape[1]), jnp.bfloat16)
    for index in range(plane):
        where = pl.ds(index * block, block)
        widened = jnp.dot(pooled[where, :], up[...], preferred_element_type=jnp.float32)
        widened = (widened + bias_ref[...]).astype(jnp.bfloat16).astype(jnp.float32)
        inner = (widened * gain_ref[...]).astype(jnp.bfloat16)
        square = widened * widened
        coarse = square.astype(jnp.bfloat16)
        fine = (square - coarse.astype(jnp.float32)).astype(jnp.bfloat16)
        squares[:, where] = sum(
            lax.dot_general(
                ones, part, (((1,), (1,)), ((), ())), preferred_element_type=jnp.float32
            )
            for part in (coarse, fine)
        )
        if index == 0:
            for copy in copies[-layers:]:
                copy.wait()
        sums = jnp.dot(inner, weights[...], preferred_element_type=jnp.float32)
        sums = sums.astype(jnp.bfloat16)
        for head in range(plane):
            queries_held[head, where, :] = sums[:, head * HEAD : (head + 1) * HEAD]
        for number in range(2):
            start = (plane + number) * HEAD
            pairs_held[index, pl.ds(number * block, block), :] = sums[:, start : start + HEAD]
    total = jnp.concatenate(
        [squares[0:1, start : start + HEAD] for start in range(0, rows, HEAD)], axis=0
    )
    coarse = total.astype(jnp.bfloat16).astype(jnp.float32)
    both = jnp.concatenate([coarse, total - coarse], axis=0).astype(jnp.bfloat16)
    for index in range(plane):
        pairs_held[index, pl.ds(2 * block, both.shape[0]), :] = both
    outs = [(pairs_held.at[cross ^ mask], out_ref) for mask, out_ref in enumerate(pair_refs)]
    outs += [(queries_held.at[cross ^ mask], out_ref) for mask, out_ref in enumerate(query_refs)]
    copy_all(outs, out_sems)


def added(refs, start, size):
    parts = [ref[pl.ds(start, size), :].astype(jnp.float32) for ref in refs]
    return sum(parts[1:], parts[0])


def row_scale(features, refs, lines):
    both = added(refs, refs[0].shape[0] - 2 * lines, 2 * lines)
    total = both[:lines, :] + both[lines:, :]
    return jnp.transpose(lax.rsqrt(total * (1.0 / features) + eps))


def pairs_kernel(features, lines, *refs):
    got_refs, pair_ref = refs[:-1], refs[-1]
    scale = row_scale(features, got_refs, lines)
    cross = lax.rem(seat()[0], len(got_refs))
    per_block = lines // len(got_refs)
    for line in range(per_block):
        mine = scale[:, line : line + 1]
        for index in range(1, len(got_refs)):
            column = index * per_block + line
            mine = jnp.where(cross == index, scale[:, column : column + 1], mine)
        for number in range(2):
            start = (number * per_block + line) * HEAD
            pair_ref[pl.ds(start, HEAD), :] = (added(got_refs, start, HEAD) * mine).astype(
                jnp.bfloat16
            )


def queries_kernel(features, plane, *refs):
    got_refs, pair_refs, (query_ref, queries) = refs[:plane], refs[plane:-2], refs[-2:]
    rows = query_ref.shape[0]
    lines = rows // HEAD
    shards = rows // CH_OWN
    layers = shards // plane
    scale = row_scale(features, pair_refs, lines)
    for line in range(lines):
        scaled = added(got_refs, line * HEAD, HEAD) * scale[:, line : line + 1]
        for start in range(0, HEAD, CH_OWN):
            index = (line * HEAD + start) // CH_OWN
            shard = (index % layers) * plane + index // layers
            queries[pl.ds(shard, CH_OWN, stride=shards), :] = scaled[start : start + CH_OWN, :]
    query_ref[...] = queries[...].astype(jnp.bfloat16)


def attend_kernel(plane, place_ref, query_ref, *refs):
    pair_refs, (out_ref, natural, keys, values, attended) = refs[:plane], refs[plane:]
    rows = query_ref.shape[0]
    window = out_ref.shape[1]
    part = rows // plane
    shards = rows // CH_OWN
    layers = shards // plane
    cross = lax.rem(seat()[0], plane)
    for number, held in enumerate((keys, values)):
        for mask, pair_ref in enumerate(pair_refs):
            for layer in range(layers):
                piece = pair_ref[pl.ds(number * part + layer * CH_OWN, CH_OWN), :]
                where = pl.ds(layer * plane + (cross ^ mask), CH_OWN, stride=shards)
                natural[where, :] = piece.astype(jnp.float32)
        held[...] = natural[...].astype(jnp.bfloat16)
    block = min(256, rows)
    score_scale = 1.0 / math.sqrt(HEAD)
    for start in range(0, rows, block):
        stop = start + block
        scores = lax.dot_general(
            query_ref[start:stop, :],
            keys[0:stop, :],
            (((1,), (1,)), ((), ())),
            preferred_element_type=jnp.float32,
        )
        spots = lax.broadcasted_iota(jnp.int32, scores.shape, 1)
        mine = lax.broadcasted_iota(jnp.int32, scores.shape, 0) + start
        scores = jnp.where(spots <= mine, scores * score_scale, masked)
        peak = jnp.max(scores, axis=1, keepdims=True)
        lifted = jnp.exp(scores - peak)
        denominator = jnp.sum(lifted, axis=1, keepdims=True)
        weighted = jnp.dot(
            lifted.astype(jnp.bfloat16), values[0:stop, :], preferred_element_type=jnp.float32
        )
        attended[start:stop, :] = (weighted / denominator).astype(jnp.bfloat16)
    attended[rows:, :] = jnp.zeros((attended.shape[0] - rows, HEAD), jnp.bfloat16)
    for shard in range(out_ref.shape[0]):
        first = place_ref[shard]
        out_ref[shard] = attended[pl.ds(pl.multiple_of(first * TILE, TILE), window), :]


def return_kernel(weight_ref, pieces_ref, own_ref, other_ref, attended):
    half = own_ref.shape[1]
    lane = seat()[1]
    for head in range(pieces_ref.shape[0]):
        attended[:, head * HEAD : (head + 1) * HEAD] = pieces_ref[head]
    other_ref[...] = jnp.dot(
        attended[...], weight_ref[:, lanes(1 - lane, half)], preferred_element_type=jnp.float32
    )
    own_ref[...] = jnp.dot(
        attended[...], weight_ref[:, lanes(lane, half)], preferred_element_type=jnp.float32
    )


def join_kernel(own_ref, other_ref, encoded_ref, spread_ref, out_ref):
    returned = (own_ref[...] + other_ref[...]).astype(jnp.bfloat16)
    results = jnp.dot(spread_ref[...], returned, preferred_element_type=jnp.float32)
    out_ref[...] = (encoded_ref[...].astype(jnp.float32) + results).astype(jnp.bfloat16)


def one_head_each(
    byte_states,
    outer_gain,
    mamba_input,
    mamba_step,
    decay_rate,
    mixer_weight,
    boundaries,
    span_counts,
    up_weight,
    up_bias,
    inner_gain,
    query_weight,
    key_weight,
    value_weight,
    return_weight,
):
    shards = lax.axis_size("seq")
    me = lax.axis_index("seq")
    lane = lax.axis_index("mp")
    plane = HEADS // KV_HEADS
    layers = shards // plane
    rows_here, width = byte_states.shape
    half = mamba_input.shape[1]
    capacity = boundaries.shape[1]
    window = capacity + TILE
    total_rows = CH_OWN * shards
    inner_width = inner_gain.shape[0]
    inner_half = up_bias.shape[0]
    weight_rows = query_weight.shape[0]
    f32, bf16 = jnp.float32, jnp.bfloat16
    layer, cross = me // plane, me % plane
    plane_groups = [[first * plane + step for step in range(plane)] for first in range(layers)]

    def over(value, mask):
        return lax.ppermute(value, "seq", [(i, i ^ mask) for i in range(shards)])

    def after(value, done):
        return lax.optimization_barrier((value, done))[0]

    own_bias = up_bias.reshape(layers // 2, plane, weight_rows)
    own_bias = lax.dynamic_index_in_dim(own_bias, cross, 1, keepdims=False).reshape(1, -1)
    own_gain = inner_gain.reshape(layers, plane, weight_rows)
    own_gain = lax.dynamic_index_in_dim(own_gain, cross, 1, keepdims=False).reshape(1, -1)

    seq_ids = jnp.arange(shards, dtype=jnp.int32)
    offsets = jnp.cumsum(span_counts) - span_counts
    own_offset = jnp.sum(jnp.where(seq_ids == me, offsets, 0))
    own_count = jnp.sum(jnp.where(seq_ids == me, span_counts, 0))
    place = offsets // TILE
    own_marks = boundaries[0]
    positions = jnp.arange(rows_here, dtype=jnp.int32)
    spans_here = jnp.arange(capacity, dtype=jnp.int32)
    live = spans_here < own_count
    slots = capacity // shards
    slot_ids = jnp.arange(slots, dtype=jnp.int32)
    owners = seq_ids.reshape(layers, plane).T
    local_span = slot_ids * shards + ((owners - own_offset) % shards)[:, :, None]
    is_span = spans_here[None, :] == local_span.reshape(-1)[:, None]
    byte_at = jnp.sum(jnp.where(is_span, jnp.minimum(own_marks, rows_here - 1)[None, :], 0), axis=1)
    pool_pick = (positions[None, :] == byte_at[:, None]).astype(bf16)
    near_owner = jnp.arange(layers, dtype=jnp.int32) * plane + cross
    near_spans = near_owner[:, None] + jnp.arange(CH_OWN, dtype=jnp.int32)[None, :] * shards
    origin = jnp.sum((offsets <= near_spans[:, :, None]).astype(jnp.int32), axis=2) - 1
    origin_offset = jnp.sum(jnp.where(seq_ids == origin[:, :, None], offsets, 0), axis=2)
    arrived_row = (
        origin * (layers * slots)
        + jnp.arange(layers, dtype=jnp.int32)[:, None] * slots
        + (near_spans - origin_offset) // shards
    ).reshape(-1)
    near_pick = (
        jnp.arange(shards * layers * slots, dtype=jnp.int32)[None, :] == arrived_row[:, None]
    ).astype(bf16)
    passed = jnp.sum(
        ((own_marks[None, :] <= positions[:, None]) & live[None, :]).astype(jnp.int32), axis=1
    )
    result_row = passed - 1 + own_offset % TILE
    spread = (jnp.arange(window, dtype=jnp.int32)[None, :] == result_row[:, None]).astype(bf16)

    up_half = inner_half // plane
    up_layers = [up_weight] + [over(up_weight, plane * step) for step in range(1, layers)]

    local, through, ends, *pair_cuts = pl.pallas_call(
        functools.partial(scan_kernel, plane, layers),
        out_shape=(
            jax.ShapeDtypeStruct((rows_here, half), f32),
            jax.ShapeDtypeStruct((rows_here, half), f32),
            jax.ShapeDtypeStruct((shards, 2, half), f32),
        )
        + (jax.ShapeDtypeStruct((weight_rows, (plane + 2) * HEAD), bf16),) * layers,
        in_specs=[in_hbm(), vmem(), in_hbm(), in_hbm(), vmem()] + [in_hbm()] * 3,
        out_specs=(vmem(),) * 3 + (in_place(),) * layers,
        scratch_shapes=[
            pltpu.VMEM(array.shape, bf16)
            for array in (
                byte_states,
                mamba_input,
                mamba_step,
                query_weight,
                key_weight,
                value_weight,
            )
        ]
        + [pltpu.SemaphoreType.DMA((6,)), pltpu.SemaphoreType.DMA((3 * layers,))],
        cost_estimate=brief(),
        compiler_params=params(56),
    )(
        byte_states,
        outer_gain[None, :],
        mamba_input,
        mamba_step,
        decay_rate[None, :],
        query_weight,
        key_weight,
        value_weight,
    )
    ends = lax.all_to_all(ends, "seq", 0, 0, tiled=True)
    ends, up_layers = lax.optimization_barrier((ends, up_layers))
    pieces = [pair_cuts[0]] + [over(pair_cuts[step], plane * step) for step in range(1, layers)]
    states, other_part = pl.pallas_call(
        states_kernel,
        out_shape=(
            jax.ShapeDtypeStruct((rows_here, half), bf16),
            jax.ShapeDtypeStruct((rows_here, half), f32),
        ),
        in_specs=[vmem()] * 4,
        out_specs=(vmem(),) * 2,
        cost_estimate=brief(),
        compiler_params=params(56),
    )(local, through, mixer_weight, ends)
    far_bias = swapped(own_bias)
    bias = jnp.where(
        lane == 0,
        jnp.concatenate([own_bias, far_bias], axis=1),
        jnp.concatenate([far_bias, own_bias], axis=1),
    )
    far_part, bias, pieces[1] = lax.optimization_barrier((swapped(other_part), bias, pieces[1]))
    encoded, leaving = pl.pallas_call(
        functools.partial(pool_kernel, plane),
        out_shape=(
            jax.ShapeDtypeStruct((rows_here, half), bf16),
            jax.ShapeDtypeStruct((shards, layers * slots, half), bf16),
        ),
        in_specs=[vmem()] * 5,
        out_specs=(vmem(),) * 2,
        cost_estimate=brief(),
        compiler_params=params(56),
    )(states, mixer_weight, far_part, byte_states, pool_pick)
    arrived = lax.all_to_all(leaving, "seq", 0, 0, tiled=True)
    up_cuts = pl.pallas_call(
        functools.partial(cut_kernel, plane),
        out_shape=(jax.ShapeDtypeStruct((layers, up_weight.shape[0], up_half), bf16),) * plane,
        in_specs=[in_place()] * (1 + layers),
        out_specs=(in_place(),) * plane,
        scratch_shapes=[
            pltpu.VMEM((layers, *up_weight.shape), bf16),
            pltpu.SemaphoreType.DMA((layers,)),
            pltpu.SemaphoreType.DMA((plane * layers // 2,)),
        ],
        cost_estimate=brief(),
        compiler_params=params(56),
    )(leaving, *up_layers)
    up_own = [up_cuts[0]] + [over(up_cuts[mask], mask) for mask in range(1, plane)]
    arrived, pieces, up_own = lax.optimization_barrier((arrived, pieces, up_own))
    near_rows = pl.pallas_call(
        own_kernel,
        out_shape=jax.ShapeDtypeStruct((plane, layers * CH_OWN, half), bf16),
        in_specs=[vmem()] * 2,
        out_specs=vmem(),
        cost_estimate=brief(),
        compiler_params=params(56),
    )(near_pick, arrived)
    near_rows, up_far = lax.optimization_barrier(
        (near_rows, [swapped(piece) for piece in up_own])
    )
    near = lax.all_to_all(
        near_rows, "seq", 0, 0, axis_index_groups=plane_groups, tiled=True
    ).reshape(total_rows, half)

    features = own_gain.shape[1]
    block = total_rows // plane
    lines = total_rows // HEAD
    pair_rows = 2 * block + 2 * lines
    partial_sums = pl.pallas_call(
        functools.partial(inner_kernel, plane, layers),
        out_shape=(jax.ShapeDtypeStruct((total_rows, HEAD), bf16),) * plane
        + (jax.ShapeDtypeStruct((pair_rows, HEAD), bf16),) * plane,
        in_specs=[vmem()] * 2 + [in_place()] * (2 + 2 * plane + layers),
        out_specs=(in_place(),) * (2 * plane),
        scratch_shapes=[
            pltpu.VMEM((total_rows, width), bf16),
            pltpu.VMEM((width, features), bf16),
            pltpu.VMEM((features, (plane + 2) * HEAD), bf16),
            pltpu.VMEM((8, total_rows), f32),
            pltpu.VMEM((plane, total_rows, HEAD), bf16),
            pltpu.VMEM((plane, pair_rows, HEAD), bf16),
            pltpu.SemaphoreType.DMA((2 + 2 * shards + layers,)),
            pltpu.SemaphoreType.DMA((2 * plane,)),
        ],
        cost_estimate=brief(),
        compiler_params=params(56),
    )(bias, own_gain, near, swapped(near), *up_own, *up_far, *pieces)
    query_sums, pair_sums = partial_sums[:plane], partial_sums[plane:]
    got_pairs = [pair_sums[0]] + [over(pair_sums[mask], mask) for mask in range(1, plane)]
    got_queries = [query_sums[0]] + [over(query_sums[mask], mask) for mask in range(1, plane)]
    pairs = pl.pallas_call(
        functools.partial(pairs_kernel, inner_width, lines),
        out_shape=jax.ShapeDtypeStruct((2 * block, HEAD), bf16),
        in_specs=[vmem()] * plane,
        out_specs=vmem(),
        cost_estimate=brief(),
        compiler_params=params(8),
    )(*got_pairs)
    whole_pairs = [pairs] + [over(pairs, mask) for mask in range(1, plane)]
    queries = pl.pallas_call(
        functools.partial(queries_kernel, inner_width, plane),
        out_shape=jax.ShapeDtypeStruct((total_rows, HEAD), bf16),
        in_specs=[vmem()] * (2 * plane),
        out_specs=vmem(),
        scratch_shapes=[pltpu.VMEM((total_rows, HEAD), f32)],
        cost_estimate=brief(),
        compiler_params=params(10),
    )(*got_queries, *got_pairs)
    leaving = pl.pallas_call(
        functools.partial(attend_kernel, plane),
        out_shape=jax.ShapeDtypeStruct((shards, window, HEAD), bf16),
        in_specs=[smem()] + [vmem()] * (1 + plane),
        out_specs=vmem(),
        scratch_shapes=[
            pltpu.VMEM((total_rows, HEAD), f32),
            pltpu.VMEM((total_rows, HEAD), bf16),
            pltpu.VMEM((total_rows, HEAD), bf16),
            pltpu.VMEM((total_rows + window, HEAD), bf16),
        ],
        cost_estimate=brief(),
        compiler_params=params(12),
    )(place, queries, *whole_pairs)
    pieces = lax.all_to_all(leaving, "seq", 0, 0, tiled=True)
    own_back, other_back = pl.pallas_call(
        return_kernel,
        out_shape=(jax.ShapeDtypeStruct((window, half), f32),) * 2,
        in_specs=[vmem()] * 2,
        out_specs=(vmem(),) * 2,
        scratch_shapes=[pltpu.VMEM((window, shards * HEAD), bf16)],
        cost_estimate=brief(),
        compiler_params=params(12),
    )(return_weight, pieces)
    return pl.pallas_call(
        join_kernel,
        out_shape=jax.ShapeDtypeStruct((rows_here, half), bf16),
        in_specs=[vmem()] * 4,
        out_specs=vmem(),
        cost_estimate=brief(),
        compiler_params=params(8),
    )(own_back, swapped(other_back), encoded, spread)


def prefix(value, axis, join, neutral):
    count, mine = (lax.axis_size(axis), lax.axis_index(axis))
    pieces = jax.tree.map(lambda part: lax.all_gather(part, axis), value)
    so_far = jax.tree.map(
        lambda part, zero: jnp.full_like(part, 0) + jnp.asarray(zero, part.dtype), value, neutral
    )

    def lap(position, so_far):
        longer = join(so_far, jax.tree.map(lambda part: part[position], pieces))
        return jax.tree.map(lambda new, old: jnp.where(position < mine, new, old), longer, so_far)

    return lax.fori_loop(0, count - 1, lap, so_far)


def rms_scale(values, gain):
    values = values.astype(jnp.float32)
    return values * lax.rsqrt(jnp.mean(values * values, axis=-1, keepdims=True) + eps) * gain


def combine_pairs(earlier, later):
    return (earlier[0] * later[0], later[0] * earlier[1] + later[1])


def pick_table(table, wanted, seq_ids):
    return jnp.sum(jnp.where(seq_ids[None, :] == wanted[:, None], table[None, :], 0), axis=1)


def block_size(piece_rows, shard_rows):
    limit = max(1, 1024 // shard_rows)
    pieces = max(1, piece_rows // shard_rows)
    best_size = 1
    for candidate in range(1, limit + 1):
        if pieces % candidate == 0:
            best_size = candidate
    return min(piece_rows, best_size * shard_rows)


def spread_heads(
    byte_states,
    outer_gain,
    mamba_input,
    mamba_step,
    decay_rate,
    mixer_weight,
    boundaries,
    span_counts,
    up_weight,
    up_bias,
    inner_gain,
    query_weight,
    key_weight,
    value_weight,
    return_weight,
):
    shards = lax.axis_size("seq")
    own_shard = lax.axis_index("seq")
    own_lane = lax.axis_index("mp")
    rows_here = byte_states.shape[0]
    capacity = boundaries.shape[1]
    column_count = mamba_input.shape[1]
    kv_local = key_weight.shape[1] // HEAD
    group_size = HEADS // KV_HEADS
    slot_count = capacity // shards
    offsets = jnp.cumsum(span_counts) - span_counts
    seq_ids = jnp.arange(shards, dtype=jnp.int32)
    own_offset = jnp.sum(jnp.where(seq_ids == own_shard, offsets, 0))
    own_count = jnp.sum(jnp.where(seq_ids == own_shard, span_counts, 0))
    normed = rms_scale(byte_states, outer_gain).astype(jnp.bfloat16)
    inputs = jnp.dot(normed, mamba_input, preferred_element_type=jnp.float32)
    step_sizes = jax.nn.softplus(jnp.dot(normed, mamba_step, preferred_element_type=jnp.float32))
    rate_steps = step_sizes * decay_rate
    decays = jnp.exp(-rate_steps)
    drives = jnp.sqrt(-jnp.expm1(-2.0 * rate_steps)) * inputs
    through, local_states = lax.associative_scan(combine_pairs, (decays, drives), axis=0)
    starting = (jnp.ones((column_count,), jnp.float32), jnp.zeros((column_count,), jnp.float32))
    arriving = prefix((through[-1], local_states[-1]), "seq", combine_pairs, starting)
    states = (local_states + through * arriving[1][None, :]).astype(jnp.bfloat16)
    partial_value = jnp.dot(states, mixer_weight, preferred_element_type=jnp.float32)
    mixed_sum = lax.psum(partial_value, "mp")
    encoded = (byte_states.astype(jnp.float32) + mixed_sum).astype(jnp.bfloat16)
    skip_part = lax.dynamic_slice_in_dim(encoded, own_lane * column_count, column_count, 1)
    own_marks = boundaries[0]
    pooled = encoded[jnp.minimum(own_marks, rows_here - 1)]
    row_width = pooled.shape[1]
    outgoing = jnp.roll(pooled.reshape(slot_count, shards, row_width), own_offset % shards, axis=1)
    incoming = lax.all_to_all(outgoing, "seq", split_axis=1, concat_axis=1, tiled=True)
    position = jnp.arange(CH_OWN, dtype=jnp.int32)
    span_index = own_shard + position * shards
    source = jnp.sum((offsets[None, :] <= span_index[:, None]).astype(jnp.int32), axis=1) - 1
    source_offset = pick_table(offsets, source, seq_ids)
    slot_index = (span_index - source_offset) // shards
    gathered_rows = incoming.reshape(slot_count * shards, row_width)[slot_index * shards + source]
    columns = gathered_rows
    widened_sum = jnp.dot(
        columns,
        lax.all_gather(up_weight, "seq", axis=0, tiled=True),
        preferred_element_type=jnp.float32,
    )
    widened_share = (widened_sum + up_bias[None, :]).astype(jnp.bfloat16)
    widened = lax.all_gather(widened_share, "mp", axis=1, tiled=True)
    inner_normed = rms_scale(widened, inner_gain).astype(jnp.bfloat16)
    columns = inner_normed
    query_part = jnp.dot(
        columns,
        lax.all_gather(query_weight, "seq", axis=0, tiled=True),
        preferred_element_type=jnp.float32,
    )
    key_part = jnp.dot(
        columns,
        lax.all_gather(key_weight, "seq", axis=0, tiled=True),
        preferred_element_type=jnp.float32,
    )
    value_part = jnp.dot(
        columns,
        lax.all_gather(value_weight, "seq", axis=0, tiled=True),
        preferred_element_type=jnp.float32,
    )
    queries = query_part.astype(jnp.bfloat16)
    key_rows = key_part.astype(jnp.bfloat16)
    value_rows = value_part.astype(jnp.bfloat16)
    query_count = queries.shape[0]
    grouped = (
        queries.reshape(query_count, kv_local, group_size, HEAD)
        .transpose(1, 0, 2, 3)
        .reshape(kv_local, query_count * group_size, HEAD)
    )
    row_index = jnp.repeat(span_index, group_size)
    shard_rows = key_rows.shape[0]
    score_scale = 1.0 / math.sqrt(HEAD)

    def key_index(whole_index):
        return whole_index // shard_rows + whole_index % shard_rows * shards

    def attend_block(running, key_block, value_block, index_block):
        row_peak, denominator, weighted = running
        scores = (
            jnp.einsum("hqd,khd->hqk", grouped, key_block, preferred_element_type=jnp.float32)
            * score_scale
        )
        scores = jnp.where(index_block[None, None, :] <= row_index[None, :, None], scores, masked)
        new_peak = jnp.maximum(row_peak, jnp.max(scores, axis=2))
        shrink = jnp.exp(row_peak - new_peak)
        lifted = jnp.exp(scores - new_peak[:, :, None])
        denominator = denominator * shrink + jnp.sum(lifted, axis=2)
        weighted = weighted * shrink[:, :, None] + jnp.einsum(
            "hqk,khd->hqd",
            lifted.astype(jnp.bfloat16),
            value_block,
            preferred_element_type=jnp.float32,
        )
        return (new_peak, denominator, weighted)

    query_total = query_count * group_size
    initial = (
        jnp.full((kv_local, query_total), masked, jnp.float32),
        jnp.zeros((kv_local, query_total), jnp.float32),
        jnp.zeros((kv_local, query_total, HEAD), jnp.float32),
    )
    key_piece = lax.all_gather(key_rows, "seq", axis=0, tiled=True)
    value_piece = lax.all_gather(value_rows, "seq", axis=0, tiled=True)
    piece_rows = key_piece.shape[0]
    block_rows = block_size(piece_rows, shard_rows)
    turn_count = piece_rows // block_rows
    key_blocks = key_piece.reshape(turn_count, block_rows, kv_local, HEAD)
    value_blocks = value_piece.reshape(turn_count, block_rows, kv_local, HEAD)

    def one_turn(turn_index, inner_running):
        whole_index = turn_index * block_rows + jnp.arange(block_rows, dtype=jnp.int32)
        return attend_block(
            inner_running, key_blocks[turn_index], value_blocks[turn_index], key_index(whole_index)
        )

    row_peak, denominator, weighted = lax.fori_loop(0, turn_count, one_turn, initial)
    attended = (weighted / denominator[:, :, None]).astype(jnp.bfloat16)
    attended = (
        attended.reshape(kv_local, query_count, group_size, HEAD)
        .transpose(1, 0, 2, 3)
        .reshape(query_count, kv_local * group_size * HEAD)
    )
    projected = jnp.dot(attended, return_weight, preferred_element_type=jnp.float32)
    returned = lax.psum_scatter(
        projected.astype(jnp.bfloat16), "mp", scatter_dimension=1, tiled=True
    )
    slot_ids = jnp.arange(slot_count, dtype=jnp.int32)
    lead_slot = (own_shard - offsets) % shards
    local_span = slot_ids[:, None] * shards + lead_slot[None, :]
    back_index = (offsets[None, :] + local_span - own_shard) // shards
    alive = local_span < span_counts[None, :]
    back_rows = jnp.where(
        alive[:, :, None],
        returned[jnp.clip(back_index, 0, CH_OWN - 1)],
        jnp.zeros((), jnp.bfloat16),
    )
    arrived = lax.all_to_all(back_rows, "seq", split_axis=1, concat_axis=1, tiled=True)
    span_results = jnp.roll(arrived, -(own_offset % shards), axis=1).reshape(capacity, column_count)
    positions = jnp.arange(rows_here, dtype=jnp.int32)
    live_slots = jnp.arange(capacity, dtype=jnp.int32) < own_count
    passed = jnp.sum(
        ((own_marks[None, :] <= positions[:, None]) & live_slots[None, :]).astype(jnp.int32), axis=1
    )
    return (skip_part.astype(jnp.float32) + span_results[passed - 1].astype(jnp.float32)).astype(
        jnp.bfloat16
    )


def solution(mesh):
    in_specs = (
        P("seq", None),
        P(),
        P(None, "mp"),
        P(None, "mp"),
        P("mp"),
        P("mp", None),
        P("seq", None),
        P(),
        P("seq", "mp"),
        P("mp"),
        P(),
        P("seq", "mp"),
        P("seq", "mp"),
        P("seq", "mp"),
        P("mp", None),
    )
    out_specs = P("seq", "mp")
    def on_device(*arrays):
        heads_here = arrays[11].shape[1] // HEAD
        fits = heads_here == mesh.shape["seq"] and mesh.shape["mp"] == 2
        return (one_head_each if fits else spread_heads)(*arrays)

    return jax.shard_map(
        on_device, mesh=mesh, in_specs=in_specs, out_specs=out_specs, check_vma=False
    )
```

```python
import functools
import math

import jax
import jax.numpy as jnp
from jax import lax
from jax.experimental import pallas as pl
from jax.experimental.pallas import tpu as pltpu
from jax.sharding import PartitionSpec as P

HEADS = 32
KV_HEADS = 8
HEAD = 128
CH_OWN = 64


eps = 1e-05
masked = -1e30
TILE = 16


def swapped(value):
    return lax.ppermute(value, "mp", [(0, 1), (1, 0)])


def vmem():
    return pl.BlockSpec(memory_space=pltpu.VMEM)


def smem():
    return pl.BlockSpec(memory_space=pltpu.SMEM)


def in_place():
    return pl.BlockSpec(memory_space=pl.ANY)


def in_hbm():
    return pl.BlockSpec(memory_space=pltpu.HBM)


def seat():
    return lax.axis_index("seq"), lax.axis_index("mp")


def params(mebibytes=24):
    return pltpu.CompilerParams(vmem_limit_bytes=mebibytes * 2**20)


def brief():
    return pl.CostEstimate(flops=1, bytes_accessed=1, transcendentals=0)


def lanes(which, size):
    return pl.ds(pl.multiple_of(which * size, size), size)


def rows_at(which, size):
    return pl.ds(pl.multiple_of(which * size, size), size)


def start_all(pairs, sems):
    copies = []
    for index, (from_ref, to_ref) in enumerate(pairs):
        copy = pltpu.make_async_copy(from_ref, to_ref, sems.at[index])
        copy.start()
        copies.append(copy)
    return copies


def copy_all(pairs, sems):
    for copy in start_all(pairs, sems):
        copy.wait()


def one_minus_exp(u):
    series = jnp.ones_like(u)
    for order in range(9, 1, -1):
        series = 1.0 - u * (1.0 / order) * series
    return jnp.where(u < 0.5, u * series, 1.0 - jnp.exp(-u))


def softplus(v):
    tail = jnp.exp(-jnp.abs(v))
    series = jnp.ones_like(tail)
    for order in range(6, 1, -1):
        series = 1.0 - tail * ((order - 1.0) / order) * series
    return jnp.maximum(v, 0.0) + jnp.where(tail < 0.03, tail * series, jnp.log(1.0 + tail))


def start_cuts(plane, query_ref, key_ref, value_ref, pair_outs, sems):
    layers = len(pair_outs)
    me, _ = seat()
    layer = me // plane
    group = plane * HEAD
    pairs = []
    for step, out_ref in enumerate(pair_outs):
        target = layer ^ step
        pairs.append((query_ref.at[:, lanes(target, group)], out_ref.at[:, pl.ds(0, group)]))
        pairs.append((key_ref.at[:, lanes(target, HEAD)], out_ref.at[:, pl.ds(group, HEAD)]))
        pairs.append(
            (value_ref.at[:, lanes(target, HEAD)], out_ref.at[:, pl.ds(group + HEAD, HEAD)])
        )
    return start_all(pairs, sems)


def scan_kernel(plane, layers, *refs):
    bytes_hbm, gain_ref, input_hbm, step_hbm, rate_ref = refs[:5]
    others, refs = refs[5:8], refs[8:]
    local_ref, through_ref, ends_ref = refs[:3]
    pair_outs, refs = refs[3 : 3 + layers], refs[3 + layers :]
    bytes_ref, input_ref, step_ref, *held, sems, cut_sems = refs
    fetches = start_all(
        [(bytes_hbm, bytes_ref), (step_hbm, step_ref), (input_hbm, input_ref), *zip(others, held)],
        sems,
    )
    fetches[0].wait()
    values = bytes_ref[...].astype(jnp.float32)
    scale = lax.rsqrt(jnp.mean(values * values, axis=1, keepdims=True) + eps)
    normed = (values * scale * gain_ref[...]).astype(jnp.bfloat16)
    fetches[1].wait()
    steps = softplus(jnp.dot(normed, step_ref[...], preferred_element_type=jnp.float32))
    rate_steps = steps * rate_ref[...]
    fetches[2].wait()
    inputs = jnp.dot(normed, input_ref[...], preferred_element_type=jnp.float32)
    for fetch in fetches[3:]:
        fetch.wait()
    cuts = start_cuts(plane, *held, pair_outs, cut_sems)
    decays = jnp.exp(-rate_steps)
    drives = jnp.sqrt(one_minus_exp(2.0 * rate_steps)) * inputs
    rows, width = decays.shape
    tile = 8
    decays = decays.reshape(rows // tile, tile, width)
    drives = drives.reshape(rows // tile, tile, width)
    place = lax.broadcasted_iota(jnp.int32, decays.shape, 1)
    for reach in (1, 2, 4):
        before_decays = pltpu.roll(decays, reach, 1)
        before_drives = pltpu.roll(drives, reach, 1)
        inside = place >= reach
        drives = jnp.where(inside, decays * before_drives + drives, drives)
        decays = jnp.where(inside, decays * before_decays, decays)
    state = jnp.zeros((1, width), jnp.float32)
    kept = jnp.ones((1, width), jnp.float32)
    for index in range(rows // tile):
        states = decays[index] * state + drives[index]
        passing = decays[index] * kept
        local_ref[pl.ds(index * tile, tile), :] = states
        through_ref[pl.ds(index * tile, tile), :] = passing
        state = states[tile - 1 :, :]
        kept = passing[tile - 1 :, :]
    for index in range(ends_ref.shape[0]):
        ends_ref[index, 0:1, :] = kept
        ends_ref[index, 1:2, :] = state
    for cut in cuts:
        cut.wait()


def states_kernel(local_ref, through_ref, mixer_ref, ends_ref, states_ref, other_ref):
    me, lane = seat()
    carry = jnp.zeros((1, local_ref.shape[1]), jnp.float32)
    for shard in range(ends_ref.shape[0]):
        later = ends_ref[shard, 0:1, :] * carry + ends_ref[shard, 1:2, :]
        carry = jnp.where(shard < me, later, carry)
    states = (local_ref[...] + through_ref[...] * carry).astype(jnp.bfloat16)
    states_ref[...] = states
    half = other_ref.shape[1]
    other_ref[...] = jnp.dot(
        states, mixer_ref[:, lanes(1 - lane, half)], preferred_element_type=jnp.float32
    )


def pool_kernel(
    plane, states_ref, mixer_ref, other_ref, bytes_ref, pick_ref, encoded_ref, out_ref
):
    half = other_ref.shape[1]
    columns = lanes(seat()[1], half)
    mixed = jnp.dot(states_ref[...], mixer_ref[:, columns], preferred_element_type=jnp.float32)
    skip = bytes_ref[:, columns].astype(jnp.float32)
    encoded = (skip + (mixed + other_ref[...])).astype(jnp.bfloat16)
    encoded_ref[...] = encoded
    picked = jnp.dot(pick_ref[...], encoded, preferred_element_type=jnp.float32)
    picked = picked.astype(jnp.bfloat16)
    size = out_ref.shape[1]
    for target in range(out_ref.shape[0]):
        start = target % plane * size
        out_ref[target] = picked[start : start + size, :]


def cut_kernel(plane, gate_ref, *refs):
    layers = len(refs) - plane - 3
    pieces, (*outs, held, sems, cut_sems) = refs[:layers], refs[layers:]
    copy_all([(piece, held.at[step]) for step, piece in enumerate(pieces)], sems)
    cross = lax.rem(seat()[0], plane)
    pairs = []
    for mask, out_ref in enumerate(outs):
        size = 2 * out_ref.shape[2] // layers
        for number in range(layers // 2):
            columns = lanes(number * plane + (cross ^ mask), size)
            pairs.append((held.at[:, :, columns], out_ref.at[:, :, pl.ds(number * size, size)]))
    copy_all(pairs, cut_sems)


def own_kernel(pick_ref, arrived_ref, out_ref):
    shards, slots, half = arrived_ref.shape
    rows = arrived_ref[...].reshape(shards * slots, half)
    own = jnp.dot(pick_ref[...], rows, preferred_element_type=jnp.float32)
    out_ref[...] = own.astype(jnp.bfloat16)


def inner_kernel(plane, layers, bias_ref, gain_ref, *refs):
    near, refs = refs[:plane], refs[plane:]
    far, refs = refs[:plane], refs[plane:]
    up_own, refs = refs[:plane], refs[plane:]
    up_far, refs = refs[:plane], refs[plane:]
    pieces, refs = refs[:layers], refs[layers:]
    query_refs, pair_refs, refs = refs[:plane], refs[plane : 2 * plane], refs[2 * plane :]
    pooled, up, weights, squares, queries_held, pairs_held, sems, out_sems = refs
    me, lane = seat()
    layer, cross = me // plane, lax.rem(me, plane)
    near_rows, half = near[0].shape
    up_rows, up_half = up_own[0].shape[1:]
    pairs = []
    for mask in range(plane):
        where = rows_at(cross ^ mask, near_rows)
        pairs.append((near[mask], pooled.at[where, lanes(lane, half)]))
        pairs.append((far[mask], pooled.at[where, lanes(1 - lane, half)]))
    for step in range(layers):
        for mask in range(plane):
            where = rows_at((layer ^ step) * plane + (cross ^ mask), up_rows)
            pairs.append((up_own[mask].at[step], up.at[where, lanes(lane, up_half)]))
            pairs.append((up_far[mask].at[step], up.at[where, lanes(1 - lane, up_half)]))
    for step, piece in enumerate(pieces):
        pairs.append((piece, weights.at[rows_at(layer ^ step, piece.shape[0]), :]))
    copies = start_all(pairs, sems)
    for copy in copies[:-layers]:
        copy.wait()
    rows = pooled.shape[0]
    block = rows // plane
    ones = jnp.ones((8, up.shape[1]), jnp.bfloat16)
    for index in range(plane):
        where = pl.ds(index * block, block)
        widened = jnp.dot(pooled[where, :], up[...], preferred_element_type=jnp.float32)
        widened = (widened + bias_ref[...]).astype(jnp.bfloat16).astype(jnp.float32)
        inner = (widened * gain_ref[...]).astype(jnp.bfloat16)
        square = widened * widened
        coarse = square.astype(jnp.bfloat16)
        fine = (square - coarse.astype(jnp.float32)).astype(jnp.bfloat16)
        squares[:, where] = sum(
            lax.dot_general(
                ones, part, (((1,), (1,)), ((), ())), preferred_element_type=jnp.float32
            )
            for part in (coarse, fine)
        )
        if index == 0:
            for copy in copies[-layers:]:
                copy.wait()
        sums = jnp.dot(inner, weights[...], preferred_element_type=jnp.float32)
        sums = sums.astype(jnp.bfloat16)
        for head in range(plane):
            queries_held[head, where, :] = sums[:, head * HEAD : (head + 1) * HEAD]
        for number in range(2):
            start = (plane + number) * HEAD
            pairs_held[index, pl.ds(number * block, block), :] = sums[:, start : start + HEAD]
    total = jnp.concatenate(
        [squares[0:1, start : start + HEAD] for start in range(0, rows, HEAD)], axis=0
    )
    coarse = total.astype(jnp.bfloat16).astype(jnp.float32)
    both = jnp.concatenate([coarse, total - coarse], axis=0).astype(jnp.bfloat16)
    for index in range(plane):
        pairs_held[index, pl.ds(2 * block, both.shape[0]), :] = both
    outs = [(pairs_held.at[cross ^ mask], out_ref) for mask, out_ref in enumerate(pair_refs)]
    outs += [(queries_held.at[cross ^ mask], out_ref) for mask, out_ref in enumerate(query_refs)]
    copy_all(outs, out_sems)


def added(refs, start, size):
    parts = [ref[pl.ds(start, size), :].astype(jnp.float32) for ref in refs]
    return sum(parts[1:], parts[0])


def row_scale(features, refs, lines):
    both = added(refs, refs[0].shape[0] - 2 * lines, 2 * lines)
    total = both[:lines, :] + both[lines:, :]
    return jnp.transpose(lax.rsqrt(total * (1.0 / features) + eps))


def pairs_kernel(features, lines, *refs):
    got_refs, pair_ref = refs[:-1], refs[-1]
    scale = row_scale(features, got_refs, lines)
    cross = lax.rem(seat()[0], len(got_refs))
    per_block = lines // len(got_refs)
    for line in range(per_block):
        mine = scale[:, line : line + 1]
        for index in range(1, len(got_refs)):
            column = index * per_block + line
            mine = jnp.where(cross == index, scale[:, column : column + 1], mine)
        for number in range(2):
            start = (number * per_block + line) * HEAD
            pair_ref[pl.ds(start, HEAD), :] = (added(got_refs, start, HEAD) * mine).astype(
                jnp.bfloat16
            )


def queries_kernel(features, plane, *refs):
    got_refs, pair_refs, (query_ref, queries) = refs[:plane], refs[plane:-2], refs[-2:]
    rows = query_ref.shape[0]
    lines = rows // HEAD
    shards = rows // CH_OWN
    layers = shards // plane
    scale = row_scale(features, pair_refs, lines)
    for line in range(lines):
        scaled = added(got_refs, line * HEAD, HEAD) * scale[:, line : line + 1]
        for start in range(0, HEAD, CH_OWN):
            index = (line * HEAD + start) // CH_OWN
            shard = (index % layers) * plane + index // layers
            queries[pl.ds(shard, CH_OWN, stride=shards), :] = scaled[start : start + CH_OWN, :]
    query_ref[...] = queries[...].astype(jnp.bfloat16)


def attend_kernel(plane, place_ref, query_ref, *refs):
    pair_refs, (out_ref, natural, keys, values, attended) = refs[:plane], refs[plane:]
    rows = query_ref.shape[0]
    window = out_ref.shape[1]
    part = rows // plane
    shards = rows // CH_OWN
    layers = shards // plane
    cross = lax.rem(seat()[0], plane)
    for number, held in enumerate((keys, values)):
        for mask, pair_ref in enumerate(pair_refs):
            for layer in range(layers):
                piece = pair_ref[pl.ds(number * part + layer * CH_OWN, CH_OWN), :]
                where = pl.ds(layer * plane + (cross ^ mask), CH_OWN, stride=shards)
                natural[where, :] = piece.astype(jnp.float32)
        held[...] = natural[...].astype(jnp.bfloat16)
    block = min(256, rows)
    score_scale = 1.0 / math.sqrt(HEAD)
    for start in range(0, rows, block):
        stop = start + block
        scores = lax.dot_general(
            query_ref[start:stop, :],
            keys[0:stop, :],
            (((1,), (1,)), ((), ())),
            preferred_element_type=jnp.float32,
        )
        spots = lax.broadcasted_iota(jnp.int32, scores.shape, 1)
        mine = lax.broadcasted_iota(jnp.int32, scores.shape, 0) + start
        scores = jnp.where(spots <= mine, scores * score_scale, masked)
        peak = jnp.max(scores, axis=1, keepdims=True)
        lifted = jnp.exp(scores - peak)
        denominator = jnp.sum(lifted, axis=1, keepdims=True)
        weighted = jnp.dot(
            lifted.astype(jnp.bfloat16), values[0:stop, :], preferred_element_type=jnp.float32
        )
        attended[start:stop, :] = (weighted / denominator).astype(jnp.bfloat16)
    attended[rows:, :] = jnp.zeros((attended.shape[0] - rows, HEAD), jnp.bfloat16)
    for shard in range(out_ref.shape[0]):
        first = place_ref[shard]
        out_ref[shard] = attended[pl.ds(pl.multiple_of(first * TILE, TILE), window), :]


def return_kernel(weight_ref, pieces_ref, own_ref, other_ref, attended):
    half = own_ref.shape[1]
    lane = seat()[1]
    for head in range(pieces_ref.shape[0]):
        attended[:, head * HEAD : (head + 1) * HEAD] = pieces_ref[head]
    other_ref[...] = jnp.dot(
        attended[...], weight_ref[:, lanes(1 - lane, half)], preferred_element_type=jnp.float32
    )
    own_ref[...] = jnp.dot(
        attended[...], weight_ref[:, lanes(lane, half)], preferred_element_type=jnp.float32
    )


def join_kernel(own_ref, other_ref, encoded_ref, spread_ref, out_ref):
    returned = (own_ref[...] + other_ref[...]).astype(jnp.bfloat16)
    results = jnp.dot(spread_ref[...], returned, preferred_element_type=jnp.float32)
    out_ref[...] = (encoded_ref[...].astype(jnp.float32) + results).astype(jnp.bfloat16)


def one_head_each(
    byte_states,
    outer_gain,
    mamba_input,
    mamba_step,
    decay_rate,
    mixer_weight,
    boundaries,
    span_counts,
    up_weight,
    up_bias,
    inner_gain,
    query_weight,
    key_weight,
    value_weight,
    return_weight,
):
    shards = lax.axis_size("seq")
    me = lax.axis_index("seq")
    lane = lax.axis_index("mp")
    plane = HEADS // KV_HEADS
    layers = shards // plane
    rows_here, width = byte_states.shape
    half = mamba_input.shape[1]
    capacity = boundaries.shape[1]
    window = capacity + TILE
    total_rows = CH_OWN * shards
    inner_width = inner_gain.shape[0]
    inner_half = up_bias.shape[0]
    weight_rows = query_weight.shape[0]
    f32, bf16 = jnp.float32, jnp.bfloat16
    layer, cross = me // plane, me % plane

    def over(value, mask):
        return lax.ppermute(value, "seq", [(i, i ^ mask) for i in range(shards)])

    def after(value, done):
        return lax.optimization_barrier((value, done))[0]

    own_bias = up_bias.reshape(layers // 2, plane, weight_rows)
    own_bias = lax.dynamic_index_in_dim(own_bias, cross, 1, keepdims=False).reshape(1, -1)
    own_gain = inner_gain.reshape(layers, plane, weight_rows)
    own_gain = lax.dynamic_index_in_dim(own_gain, cross, 1, keepdims=False).reshape(1, -1)

    seq_ids = jnp.arange(shards, dtype=jnp.int32)
    offsets = jnp.cumsum(span_counts) - span_counts
    own_offset = jnp.sum(jnp.where(seq_ids == me, offsets, 0))
    own_count = jnp.sum(jnp.where(seq_ids == me, span_counts, 0))
    place = offsets // TILE
    own_marks = boundaries[0]
    positions = jnp.arange(rows_here, dtype=jnp.int32)
    spans_here = jnp.arange(capacity, dtype=jnp.int32)
    live = spans_here < own_count
    slots = capacity // shards
    slot_ids = jnp.arange(slots, dtype=jnp.int32)
    owners = seq_ids.reshape(layers, plane).T
    local_span = slot_ids * shards + ((owners - own_offset) % shards)[:, :, None]
    is_span = spans_here[None, :] == local_span.reshape(-1)[:, None]
    byte_at = jnp.sum(jnp.where(is_span, jnp.minimum(own_marks, rows_here - 1)[None, :], 0), axis=1)
    pool_pick = (positions[None, :] == byte_at[:, None]).astype(bf16)
    near_owner = jnp.arange(layers, dtype=jnp.int32) * plane + cross
    near_spans = near_owner[:, None] + jnp.arange(CH_OWN, dtype=jnp.int32)[None, :] * shards
    origin = jnp.sum((offsets <= near_spans[:, :, None]).astype(jnp.int32), axis=2) - 1
    origin_offset = jnp.sum(jnp.where(seq_ids == origin[:, :, None], offsets, 0), axis=2)
    arrived_row = (
        origin * (layers * slots)
        + jnp.arange(layers, dtype=jnp.int32)[:, None] * slots
        + (near_spans - origin_offset) // shards
    ).reshape(-1)
    near_pick = (
        jnp.arange(shards * layers * slots, dtype=jnp.int32)[None, :] == arrived_row[:, None]
    ).astype(bf16)
    passed = jnp.sum(
        ((own_marks[None, :] <= positions[:, None]) & live[None, :]).astype(jnp.int32), axis=1
    )
    result_row = passed - 1 + own_offset % TILE
    spread = (jnp.arange(window, dtype=jnp.int32)[None, :] == result_row[:, None]).astype(bf16)

    up_half = inner_half // plane
    up_layers = [up_weight] + [over(up_weight, plane * step) for step in range(1, layers)]

    local, through, ends, *pair_cuts = pl.pallas_call(
        functools.partial(scan_kernel, plane, layers),
        out_shape=(
            jax.ShapeDtypeStruct((rows_here, half), f32),
            jax.ShapeDtypeStruct((rows_here, half), f32),
            jax.ShapeDtypeStruct((shards, 2, half), f32),
        )
        + (jax.ShapeDtypeStruct((weight_rows, (plane + 2) * HEAD), bf16),) * layers,
        in_specs=[in_hbm(), vmem(), in_hbm(), in_hbm(), vmem()] + [in_hbm()] * 3,
        out_specs=(vmem(),) * 3 + (in_place(),) * layers,
        scratch_shapes=[
            pltpu.VMEM(array.shape, bf16)
            for array in (
                byte_states,
                mamba_input,
                mamba_step,
                query_weight,
                key_weight,
                value_weight,
            )
        ]
        + [pltpu.SemaphoreType.DMA((6,)), pltpu.SemaphoreType.DMA((3 * layers,))],
        cost_estimate=brief(),
        compiler_params=params(56),
    )(
        byte_states,
        outer_gain[None, :],
        mamba_input,
        mamba_step,
        decay_rate[None, :],
        query_weight,
        key_weight,
        value_weight,
    )
    ends = lax.all_to_all(ends, "seq", 0, 0, tiled=True)
    ends, up_layers = lax.optimization_barrier((ends, up_layers))
    pieces = [pair_cuts[0]] + [over(pair_cuts[step], plane * step) for step in range(1, layers)]
    states, other_part = pl.pallas_call(
        states_kernel,
        out_shape=(
            jax.ShapeDtypeStruct((rows_here, half), bf16),
            jax.ShapeDtypeStruct((rows_here, half), f32),
        ),
        in_specs=[vmem()] * 4,
        out_specs=(vmem(),) * 2,
        cost_estimate=brief(),
        compiler_params=params(56),
    )(local, through, mixer_weight, ends)
    far_bias = swapped(own_bias)
    bias = jnp.where(
        lane == 0,
        jnp.concatenate([own_bias, far_bias], axis=1),
        jnp.concatenate([far_bias, own_bias], axis=1),
    )
    far_part, bias, pieces[1] = lax.optimization_barrier((swapped(other_part), bias, pieces[1]))
    encoded, leaving = pl.pallas_call(
        functools.partial(pool_kernel, plane),
        out_shape=(
            jax.ShapeDtypeStruct((rows_here, half), bf16),
            jax.ShapeDtypeStruct((shards, layers * slots, half), bf16),
        ),
        in_specs=[vmem()] * 5,
        out_specs=(vmem(),) * 2,
        cost_estimate=brief(),
        compiler_params=params(56),
    )(states, mixer_weight, far_part, byte_states, pool_pick)
    arrived = lax.all_to_all(leaving, "seq", 0, 0, tiled=True)
    up_cuts = pl.pallas_call(
        functools.partial(cut_kernel, plane),
        out_shape=(jax.ShapeDtypeStruct((layers, up_weight.shape[0], up_half), bf16),) * plane,
        in_specs=[in_place()] * (1 + layers),
        out_specs=(in_place(),) * plane,
        scratch_shapes=[
            pltpu.VMEM((layers, *up_weight.shape), bf16),
            pltpu.SemaphoreType.DMA((layers,)),
            pltpu.SemaphoreType.DMA((plane * layers // 2,)),
        ],
        cost_estimate=brief(),
        compiler_params=params(56),
    )(leaving, *up_layers)
    up_own = [up_cuts[0]] + [over(up_cuts[mask], mask) for mask in range(1, plane)]
    arrived, pieces, up_own = lax.optimization_barrier((arrived, pieces, up_own))
    near_rows = pl.pallas_call(
        own_kernel,
        out_shape=jax.ShapeDtypeStruct((layers * CH_OWN, half), bf16),
        in_specs=[vmem()] * 2,
        out_specs=vmem(),
        cost_estimate=brief(),
        compiler_params=params(56),
    )(near_pick, arrived)
    near_rows, up_far = lax.optimization_barrier(
        (near_rows, [swapped(piece) for piece in up_own])
    )
    near = [near_rows] + [over(near_rows, mask) for mask in range(1, plane)]
    far = [swapped(piece) for piece in near]

    features = own_gain.shape[1]
    block = total_rows // plane
    lines = total_rows // HEAD
    pair_rows = 2 * block + 2 * lines
    partial_sums = pl.pallas_call(
        functools.partial(inner_kernel, plane, layers),
        out_shape=(jax.ShapeDtypeStruct((total_rows, HEAD), bf16),) * plane
        + (jax.ShapeDtypeStruct((pair_rows, HEAD), bf16),) * plane,
        in_specs=[vmem()] * 2 + [in_place()] * (4 * plane + layers),
        out_specs=(in_place(),) * (2 * plane),
        scratch_shapes=[
            pltpu.VMEM((total_rows, width), bf16),
            pltpu.VMEM((width, features), bf16),
            pltpu.VMEM((features, (plane + 2) * HEAD), bf16),
            pltpu.VMEM((8, total_rows), f32),
            pltpu.VMEM((plane, total_rows, HEAD), bf16),
            pltpu.VMEM((plane, pair_rows, HEAD), bf16),
            pltpu.SemaphoreType.DMA((2 * plane + 2 * shards + layers,)),
            pltpu.SemaphoreType.DMA((2 * plane,)),
        ],
        cost_estimate=brief(),
        compiler_params=params(56),
    )(bias, own_gain, *near, *far, *up_own, *up_far, *pieces)
    query_sums, pair_sums = partial_sums[:plane], partial_sums[plane:]
    got_pairs = [pair_sums[0]] + [over(pair_sums[mask], mask) for mask in range(1, plane)]
    got_queries = [query_sums[0]] + [over(query_sums[mask], mask) for mask in range(1, plane)]
    pairs = pl.pallas_call(
        functools.partial(pairs_kernel, inner_width, lines),
        out_shape=jax.ShapeDtypeStruct((2 * block, HEAD), bf16),
        in_specs=[vmem()] * plane,
        out_specs=vmem(),
        cost_estimate=brief(),
        compiler_params=params(8),
    )(*got_pairs)
    whole_pairs = [pairs] + [over(pairs, mask) for mask in range(1, plane)]
    queries = pl.pallas_call(
        functools.partial(queries_kernel, inner_width, plane),
        out_shape=jax.ShapeDtypeStruct((total_rows, HEAD), bf16),
        in_specs=[vmem()] * (2 * plane),
        out_specs=vmem(),
        scratch_shapes=[pltpu.VMEM((total_rows, HEAD), f32)],
        cost_estimate=brief(),
        compiler_params=params(10),
    )(*got_queries, *got_pairs)
    leaving = pl.pallas_call(
        functools.partial(attend_kernel, plane),
        out_shape=jax.ShapeDtypeStruct((shards, window, HEAD), bf16),
        in_specs=[smem()] + [vmem()] * (1 + plane),
        out_specs=vmem(),
        scratch_shapes=[
            pltpu.VMEM((total_rows, HEAD), f32),
            pltpu.VMEM((total_rows, HEAD), bf16),
            pltpu.VMEM((total_rows, HEAD), bf16),
            pltpu.VMEM((total_rows + window, HEAD), bf16),
        ],
        cost_estimate=brief(),
        compiler_params=params(12),
    )(place, queries, *whole_pairs)
    pieces = lax.all_to_all(leaving, "seq", 0, 0, tiled=True)
    own_back, other_back = pl.pallas_call(
        return_kernel,
        out_shape=(jax.ShapeDtypeStruct((window, half), f32),) * 2,
        in_specs=[vmem()] * 2,
        out_specs=(vmem(),) * 2,
        scratch_shapes=[pltpu.VMEM((window, shards * HEAD), bf16)],
        cost_estimate=brief(),
        compiler_params=params(12),
    )(return_weight, pieces)
    return pl.pallas_call(
        join_kernel,
        out_shape=jax.ShapeDtypeStruct((rows_here, half), bf16),
        in_specs=[vmem()] * 4,
        out_specs=vmem(),
        cost_estimate=brief(),
        compiler_params=params(8),
    )(own_back, swapped(other_back), encoded, spread)


def prefix(value, axis, join, neutral):
    count, mine = (lax.axis_size(axis), lax.axis_index(axis))
    pieces = jax.tree.map(lambda part: lax.all_gather(part, axis), value)
    so_far = jax.tree.map(
        lambda part, zero: jnp.full_like(part, 0) + jnp.asarray(zero, part.dtype), value, neutral
    )

    def lap(position, so_far):
        longer = join(so_far, jax.tree.map(lambda part: part[position], pieces))
        return jax.tree.map(lambda new, old: jnp.where(position < mine, new, old), longer, so_far)

    return lax.fori_loop(0, count - 1, lap, so_far)


def rms_scale(values, gain):
    values = values.astype(jnp.float32)
    return values * lax.rsqrt(jnp.mean(values * values, axis=-1, keepdims=True) + eps) * gain


def combine_pairs(earlier, later):
    return (earlier[0] * later[0], later[0] * earlier[1] + later[1])


def pick_table(table, wanted, seq_ids):
    return jnp.sum(jnp.where(seq_ids[None, :] == wanted[:, None], table[None, :], 0), axis=1)


def block_size(piece_rows, shard_rows):
    limit = max(1, 1024 // shard_rows)
    pieces = max(1, piece_rows // shard_rows)
    best_size = 1
    for candidate in range(1, limit + 1):
        if pieces % candidate == 0:
            best_size = candidate
    return min(piece_rows, best_size * shard_rows)


def spread_heads(
    byte_states,
    outer_gain,
    mamba_input,
    mamba_step,
    decay_rate,
    mixer_weight,
    boundaries,
    span_counts,
    up_weight,
    up_bias,
    inner_gain,
    query_weight,
    key_weight,
    value_weight,
    return_weight,
):
    shards = lax.axis_size("seq")
    own_shard = lax.axis_index("seq")
    own_lane = lax.axis_index("mp")
    rows_here = byte_states.shape[0]
    capacity = boundaries.shape[1]
    column_count = mamba_input.shape[1]
    kv_local = key_weight.shape[1] // HEAD
    group_size = HEADS // KV_HEADS
    slot_count = capacity // shards
    offsets = jnp.cumsum(span_counts) - span_counts
    seq_ids = jnp.arange(shards, dtype=jnp.int32)
    own_offset = jnp.sum(jnp.where(seq_ids == own_shard, offsets, 0))
    own_count = jnp.sum(jnp.where(seq_ids == own_shard, span_counts, 0))
    normed = rms_scale(byte_states, outer_gain).astype(jnp.bfloat16)
    inputs = jnp.dot(normed, mamba_input, preferred_element_type=jnp.float32)
    step_sizes = jax.nn.softplus(jnp.dot(normed, mamba_step, preferred_element_type=jnp.float32))
    rate_steps = step_sizes * decay_rate
    decays = jnp.exp(-rate_steps)
    drives = jnp.sqrt(-jnp.expm1(-2.0 * rate_steps)) * inputs
    through, local_states = lax.associative_scan(combine_pairs, (decays, drives), axis=0)
    starting = (jnp.ones((column_count,), jnp.float32), jnp.zeros((column_count,), jnp.float32))
    arriving = prefix((through[-1], local_states[-1]), "seq", combine_pairs, starting)
    states = (local_states + through * arriving[1][None, :]).astype(jnp.bfloat16)
    partial_value = jnp.dot(states, mixer_weight, preferred_element_type=jnp.float32)
    mixed_sum = lax.psum(partial_value, "mp")
    encoded = (byte_states.astype(jnp.float32) + mixed_sum).astype(jnp.bfloat16)
    skip_part = lax.dynamic_slice_in_dim(encoded, own_lane * column_count, column_count, 1)
    own_marks = boundaries[0]
    pooled = encoded[jnp.minimum(own_marks, rows_here - 1)]
    row_width = pooled.shape[1]
    outgoing = jnp.roll(pooled.reshape(slot_count, shards, row_width), own_offset % shards, axis=1)
    incoming = lax.all_to_all(outgoing, "seq", split_axis=1, concat_axis=1, tiled=True)
    position = jnp.arange(CH_OWN, dtype=jnp.int32)
    span_index = own_shard + position * shards
    source = jnp.sum((offsets[None, :] <= span_index[:, None]).astype(jnp.int32), axis=1) - 1
    source_offset = pick_table(offsets, source, seq_ids)
    slot_index = (span_index - source_offset) // shards
    gathered_rows = incoming.reshape(slot_count * shards, row_width)[slot_index * shards + source]
    columns = gathered_rows
    widened_sum = jnp.dot(
        columns,
        lax.all_gather(up_weight, "seq", axis=0, tiled=True),
        preferred_element_type=jnp.float32,
    )
    widened_share = (widened_sum + up_bias[None, :]).astype(jnp.bfloat16)
    widened = lax.all_gather(widened_share, "mp", axis=1, tiled=True)
    inner_normed = rms_scale(widened, inner_gain).astype(jnp.bfloat16)
    columns = inner_normed
    query_part = jnp.dot(
        columns,
        lax.all_gather(query_weight, "seq", axis=0, tiled=True),
        preferred_element_type=jnp.float32,
    )
    key_part = jnp.dot(
        columns,
        lax.all_gather(key_weight, "seq", axis=0, tiled=True),
        preferred_element_type=jnp.float32,
    )
    value_part = jnp.dot(
        columns,
        lax.all_gather(value_weight, "seq", axis=0, tiled=True),
        preferred_element_type=jnp.float32,
    )
    queries = query_part.astype(jnp.bfloat16)
    key_rows = key_part.astype(jnp.bfloat16)
    value_rows = value_part.astype(jnp.bfloat16)
    query_count = queries.shape[0]
    grouped = (
        queries.reshape(query_count, kv_local, group_size, HEAD)
        .transpose(1, 0, 2, 3)
        .reshape(kv_local, query_count * group_size, HEAD)
    )
    row_index = jnp.repeat(span_index, group_size)
    shard_rows = key_rows.shape[0]
    score_scale = 1.0 / math.sqrt(HEAD)

    def key_index(whole_index):
        return whole_index // shard_rows + whole_index % shard_rows * shards

    def attend_block(running, key_block, value_block, index_block):
        row_peak, denominator, weighted = running
        scores = (
            jnp.einsum("hqd,khd->hqk", grouped, key_block, preferred_element_type=jnp.float32)
            * score_scale
        )
        scores = jnp.where(index_block[None, None, :] <= row_index[None, :, None], scores, masked)
        new_peak = jnp.maximum(row_peak, jnp.max(scores, axis=2))
        shrink = jnp.exp(row_peak - new_peak)
        lifted = jnp.exp(scores - new_peak[:, :, None])
        denominator = denominator * shrink + jnp.sum(lifted, axis=2)
        weighted = weighted * shrink[:, :, None] + jnp.einsum(
            "hqk,khd->hqd",
            lifted.astype(jnp.bfloat16),
            value_block,
            preferred_element_type=jnp.float32,
        )
        return (new_peak, denominator, weighted)

    query_total = query_count * group_size
    initial = (
        jnp.full((kv_local, query_total), masked, jnp.float32),
        jnp.zeros((kv_local, query_total), jnp.float32),
        jnp.zeros((kv_local, query_total, HEAD), jnp.float32),
    )
    key_piece = lax.all_gather(key_rows, "seq", axis=0, tiled=True)
    value_piece = lax.all_gather(value_rows, "seq", axis=0, tiled=True)
    piece_rows = key_piece.shape[0]
    block_rows = block_size(piece_rows, shard_rows)
    turn_count = piece_rows // block_rows
    key_blocks = key_piece.reshape(turn_count, block_rows, kv_local, HEAD)
    value_blocks = value_piece.reshape(turn_count, block_rows, kv_local, HEAD)

    def one_turn(turn_index, inner_running):
        whole_index = turn_index * block_rows + jnp.arange(block_rows, dtype=jnp.int32)
        return attend_block(
            inner_running, key_blocks[turn_index], value_blocks[turn_index], key_index(whole_index)
        )

    row_peak, denominator, weighted = lax.fori_loop(0, turn_count, one_turn, initial)
    attended = (weighted / denominator[:, :, None]).astype(jnp.bfloat16)
    attended = (
        attended.reshape(kv_local, query_count, group_size, HEAD)
        .transpose(1, 0, 2, 3)
        .reshape(query_count, kv_local * group_size * HEAD)
    )
    projected = jnp.dot(attended, return_weight, preferred_element_type=jnp.float32)
    returned = lax.psum_scatter(
        projected.astype(jnp.bfloat16), "mp", scatter_dimension=1, tiled=True
    )
    slot_ids = jnp.arange(slot_count, dtype=jnp.int32)
    lead_slot = (own_shard - offsets) % shards
    local_span = slot_ids[:, None] * shards + lead_slot[None, :]
    back_index = (offsets[None, :] + local_span - own_shard) // shards
    alive = local_span < span_counts[None, :]
    back_rows = jnp.where(
        alive[:, :, None],
        returned[jnp.clip(back_index, 0, CH_OWN - 1)],
        jnp.zeros((), jnp.bfloat16),
    )
    arrived = lax.all_to_all(back_rows, "seq", split_axis=1, concat_axis=1, tiled=True)
    span_results = jnp.roll(arrived, -(own_offset % shards), axis=1).reshape(capacity, column_count)
    positions = jnp.arange(rows_here, dtype=jnp.int32)
    live_slots = jnp.arange(capacity, dtype=jnp.int32) < own_count
    passed = jnp.sum(
        ((own_marks[None, :] <= positions[:, None]) & live_slots[None, :]).astype(jnp.int32), axis=1
    )
    return (skip_part.astype(jnp.float32) + span_results[passed - 1].astype(jnp.float32)).astype(
        jnp.bfloat16
    )


def solution(mesh):
    in_specs = (
        P("seq", None),
        P(),
        P(None, "mp"),
        P(None, "mp"),
        P("mp"),
        P("mp", None),
        P("seq", None),
        P(),
        P("seq", "mp"),
        P("mp"),
        P(),
        P("seq", "mp"),
        P("seq", "mp"),
        P("seq", "mp"),
        P("mp", None),
    )
    out_specs = P("seq", "mp")
    def on_device(*arrays):
        heads_here = arrays[11].shape[1] // HEAD
        fits = heads_here == mesh.shape["seq"] and mesh.shape["mp"] == 2
        return (one_head_each if fits else spread_heads)(*arrays)

    return jax.shard_map(
        on_device, mesh=mesh, in_specs=in_specs, out_specs=out_specs, check_vma=False
    )
```

```python
import functools
import math

import jax
import jax.numpy as jnp
from jax import lax
from jax.experimental import pallas as pl
from jax.experimental.pallas import tpu as pltpu
from jax.sharding import PartitionSpec as P

HEADS = 32
KV_HEADS = 8
HEAD = 128
CH_OWN = 64


eps = 1e-05
masked = -1e30
TILE = 16


def swapped(value):
    return lax.ppermute(value, "mp", [(0, 1), (1, 0)])


def vmem():
    return pl.BlockSpec(memory_space=pltpu.VMEM)


def smem():
    return pl.BlockSpec(memory_space=pltpu.SMEM)


def in_place():
    return pl.BlockSpec(memory_space=pl.ANY)


def in_hbm():
    return pl.BlockSpec(memory_space=pltpu.HBM)


def seat():
    return lax.axis_index("seq"), lax.axis_index("mp")


def params(mebibytes=24):
    return pltpu.CompilerParams(vmem_limit_bytes=mebibytes * 2**20)


def brief():
    return pl.CostEstimate(flops=1, bytes_accessed=1, transcendentals=0)


def lanes(which, size):
    return pl.ds(pl.multiple_of(which * size, size), size)


def rows_at(which, size):
    return pl.ds(pl.multiple_of(which * size, size), size)


def start_all(pairs, sems):
    copies = []
    for index, (from_ref, to_ref) in enumerate(pairs):
        copy = pltpu.make_async_copy(from_ref, to_ref, sems.at[index])
        copy.start()
        copies.append(copy)
    return copies


def copy_all(pairs, sems):
    for copy in start_all(pairs, sems):
        copy.wait()


def one_minus_exp(u):
    series = jnp.ones_like(u)
    for order in range(9, 1, -1):
        series = 1.0 - u * (1.0 / order) * series
    return jnp.where(u < 0.5, u * series, 1.0 - jnp.exp(-u))


def softplus(v):
    tail = jnp.exp(-jnp.abs(v))
    series = jnp.ones_like(tail)
    for order in range(6, 1, -1):
        series = 1.0 - tail * ((order - 1.0) / order) * series
    return jnp.maximum(v, 0.0) + jnp.where(tail < 0.03, tail * series, jnp.log(1.0 + tail))


def start_cuts(plane, query_ref, key_ref, value_ref, pair_outs, sems):
    layers = len(pair_outs)
    me, _ = seat()
    layer = me // plane
    group = plane * HEAD
    pairs = []
    for step, out_ref in enumerate(pair_outs):
        target = layer ^ step
        pairs.append((query_ref.at[:, lanes(target, group)], out_ref.at[:, pl.ds(0, group)]))
        pairs.append((key_ref.at[:, lanes(target, HEAD)], out_ref.at[:, pl.ds(group, HEAD)]))
        pairs.append(
            (value_ref.at[:, lanes(target, HEAD)], out_ref.at[:, pl.ds(group + HEAD, HEAD)])
        )
    return start_all(pairs, sems)


def scan_kernel(plane, layers, *refs):
    bytes_hbm, gain_ref, input_hbm, step_hbm, rate_ref = refs[:5]
    others, refs = refs[5:8], refs[8:]
    local_ref, through_ref, ends_ref = refs[:3]
    pair_outs, refs = refs[3 : 3 + layers], refs[3 + layers :]
    bytes_ref, input_ref, step_ref, *held, sems, cut_sems = refs
    fetches = start_all(
        [(bytes_hbm, bytes_ref), (step_hbm, step_ref), (input_hbm, input_ref), *zip(others, held)],
        sems,
    )
    fetches[0].wait()
    values = bytes_ref[...].astype(jnp.float32)
    scale = lax.rsqrt(jnp.mean(values * values, axis=1, keepdims=True) + eps)
    normed = (values * scale * gain_ref[...]).astype(jnp.bfloat16)
    fetches[1].wait()
    steps = softplus(jnp.dot(normed, step_ref[...], preferred_element_type=jnp.float32))
    rate_steps = steps * rate_ref[...]
    fetches[2].wait()
    inputs = jnp.dot(normed, input_ref[...], preferred_element_type=jnp.float32)
    for fetch in fetches[3:]:
        fetch.wait()
    cuts = start_cuts(plane, *held, pair_outs, cut_sems)
    decays = jnp.exp(-rate_steps)
    drives = jnp.sqrt(one_minus_exp(2.0 * rate_steps)) * inputs
    rows, width = decays.shape
    tile = 8
    decays = decays.reshape(rows // tile, tile, width)
    drives = drives.reshape(rows // tile, tile, width)
    place = lax.broadcasted_iota(jnp.int32, decays.shape, 1)
    for reach in (1, 2, 4):
        before_decays = pltpu.roll(decays, reach, 1)
        before_drives = pltpu.roll(drives, reach, 1)
        inside = place >= reach
        drives = jnp.where(inside, decays * before_drives + drives, drives)
        decays = jnp.where(inside, decays * before_decays, decays)
    state = jnp.zeros((1, width), jnp.float32)
    kept = jnp.ones((1, width), jnp.float32)
    for index in range(rows // tile):
        states = decays[index] * state + drives[index]
        passing = decays[index] * kept
        local_ref[pl.ds(index * tile, tile), :] = states
        through_ref[pl.ds(index * tile, tile), :] = passing
        state = states[tile - 1 :, :]
        kept = passing[tile - 1 :, :]
    for index in range(ends_ref.shape[0]):
        ends_ref[index, 0:1, :] = kept
        ends_ref[index, 1:2, :] = state
    for cut in cuts:
        cut.wait()


def states_kernel(local_ref, through_ref, mixer_ref, ends_ref, states_ref, other_ref):
    me, lane = seat()
    carry = jnp.zeros((1, local_ref.shape[1]), jnp.float32)
    for shard in range(ends_ref.shape[0]):
        later = ends_ref[shard, 0:1, :] * carry + ends_ref[shard, 1:2, :]
        carry = jnp.where(shard < me, later, carry)
    states = (local_ref[...] + through_ref[...] * carry).astype(jnp.bfloat16)
    states_ref[...] = states
    half = other_ref.shape[1]
    other_ref[...] = jnp.dot(
        states, mixer_ref[:, lanes(1 - lane, half)], preferred_element_type=jnp.float32
    )


def pool_kernel(
    plane, states_ref, mixer_ref, other_ref, bytes_ref, pick_ref, encoded_ref, out_ref
):
    half = other_ref.shape[1]
    columns = lanes(seat()[1], half)
    mixed = jnp.dot(states_ref[...], mixer_ref[:, columns], preferred_element_type=jnp.float32)
    skip = bytes_ref[:, columns].astype(jnp.float32)
    encoded = (skip + (mixed + other_ref[...])).astype(jnp.bfloat16)
    encoded_ref[...] = encoded
    picked = jnp.dot(pick_ref[...], encoded, preferred_element_type=jnp.float32)
    picked = picked.astype(jnp.bfloat16)
    size = out_ref.shape[1]
    for target in range(out_ref.shape[0]):
        start = target % plane * size
        out_ref[target] = picked[start : start + size, :]


def cut_kernel(plane, gate_ref, *refs):
    layers = len(refs) - plane - 3
    pieces, (*outs, held, sems, cut_sems) = refs[:layers], refs[layers:]
    copy_all([(piece, held.at[step]) for step, piece in enumerate(pieces)], sems)
    cross = lax.rem(seat()[0], plane)
    pairs = []
    for mask, out_ref in enumerate(outs):
        size = 2 * out_ref.shape[2] // layers
        for number in range(layers // 2):
            columns = lanes(number * plane + (cross ^ mask), size)
            pairs.append((held.at[:, :, columns], out_ref.at[:, :, pl.ds(number * size, size)]))
    copy_all(pairs, cut_sems)


def own_kernel(pick_ref, arrived_ref, out_ref):
    shards, slots, half = arrived_ref.shape
    rows = arrived_ref[...].reshape(shards * slots, half)
    own = jnp.dot(pick_ref[...], rows, preferred_element_type=jnp.float32)
    out_ref[...] = own.astype(jnp.bfloat16)


def inner_kernel(plane, layers, bias_ref, gain_ref, *refs):
    near, refs = refs[:plane], refs[plane:]
    far, refs = refs[:plane], refs[plane:]
    up_own, refs = refs[:plane], refs[plane:]
    up_far, refs = refs[:plane], refs[plane:]
    pieces, refs = refs[:layers], refs[layers:]
    query_refs, pair_refs, refs = refs[:plane], refs[plane : 2 * plane], refs[2 * plane :]
    pooled, up, weights, squares, queries_held, pairs_held, sems, out_sems = refs
    me, lane = seat()
    layer, cross = me // plane, lax.rem(me, plane)
    near_rows, half = near[0].shape
    up_rows, up_half = up_own[0].shape[1:]
    pairs = []
    for mask in range(plane):
        where = rows_at(cross ^ mask, near_rows)
        pairs.append((near[mask], pooled.at[where, lanes(lane, half)]))
        pairs.append((far[mask], pooled.at[where, lanes(1 - lane, half)]))
    for step in range(layers):
        for mask in range(plane):
            where = rows_at((layer ^ step) * plane + (cross ^ mask), up_rows)
            pairs.append((up_own[mask].at[step], up.at[where, lanes(lane, up_half)]))
            pairs.append((up_far[mask].at[step], up.at[where, lanes(1 - lane, up_half)]))
    for step, piece in enumerate(pieces):
        pairs.append((piece, weights.at[rows_at(layer ^ step, piece.shape[0]), :]))
    copies = start_all(pairs, sems)
    for copy in copies[:-layers]:
        copy.wait()
    rows = pooled.shape[0]
    block = rows // plane
    ones = jnp.ones((8, up.shape[1]), jnp.bfloat16)
    for index in range(plane):
        where = pl.ds(index * block, block)
        widened = jnp.dot(pooled[where, :], up[...], preferred_element_type=jnp.float32)
        widened = (widened + bias_ref[...]).astype(jnp.bfloat16).astype(jnp.float32)
        inner = (widened * gain_ref[...]).astype(jnp.bfloat16)
        square = widened * widened
        coarse = square.astype(jnp.bfloat16)
        fine = (square - coarse.astype(jnp.float32)).astype(jnp.bfloat16)
        squares[:, where] = sum(
            lax.dot_general(
                ones, part, (((1,), (1,)), ((), ())), preferred_element_type=jnp.float32
            )
            for part in (coarse, fine)
        )
        if index == 0:
            for copy in copies[-layers:]:
                copy.wait()
        sums = jnp.dot(inner, weights[...], preferred_element_type=jnp.float32)
        sums = sums.astype(jnp.bfloat16)
        for head in range(plane):
            queries_held[head, where, :] = sums[:, head * HEAD : (head + 1) * HEAD]
        for number in range(2):
            start = (plane + number) * HEAD
            pairs_held[index, pl.ds(number * block, block), :] = sums[:, start : start + HEAD]
    total = jnp.concatenate(
        [squares[0:1, start : start + HEAD] for start in range(0, rows, HEAD)], axis=0
    )
    coarse = total.astype(jnp.bfloat16).astype(jnp.float32)
    both = jnp.concatenate([coarse, total - coarse], axis=0).astype(jnp.bfloat16)
    for index in range(plane):
        pairs_held[index, pl.ds(2 * block, both.shape[0]), :] = both
    outs = [(pairs_held.at[cross ^ mask], out_ref) for mask, out_ref in enumerate(pair_refs)]
    outs += [(queries_held.at[cross ^ mask], out_ref) for mask, out_ref in enumerate(query_refs)]
    copy_all(outs, out_sems)


def added(refs, start, size):
    parts = [ref[pl.ds(start, size), :].astype(jnp.float32) for ref in refs]
    return sum(parts[1:], parts[0])


def row_scale(features, refs, lines):
    both = added(refs, refs[0].shape[0] - 2 * lines, 2 * lines)
    total = both[:lines, :] + both[lines:, :]
    return jnp.transpose(lax.rsqrt(total * (1.0 / features) + eps))


def pairs_kernel(features, lines, *refs):
    got_refs, pair_ref = refs[:-1], refs[-1]
    scale = row_scale(features, got_refs, lines)
    cross = lax.rem(seat()[0], len(got_refs))
    per_block = lines // len(got_refs)
    for line in range(per_block):
        mine = scale[:, line : line + 1]
        for index in range(1, len(got_refs)):
            column = index * per_block + line
            mine = jnp.where(cross == index, scale[:, column : column + 1], mine)
        for number in range(2):
            start = (number * per_block + line) * HEAD
            pair_ref[pl.ds(start, HEAD), :] = (added(got_refs, start, HEAD) * mine).astype(
                jnp.bfloat16
            )


def queries_kernel(features, plane, *refs):
    got_refs, pair_refs, (query_ref, queries) = refs[:plane], refs[plane:-2], refs[-2:]
    rows = query_ref.shape[0]
    lines = rows // HEAD
    shards = rows // CH_OWN
    layers = shards // plane
    scale = row_scale(features, pair_refs, lines)
    for line in range(lines):
        scaled = added(got_refs, line * HEAD, HEAD) * scale[:, line : line + 1]
        for start in range(0, HEAD, CH_OWN):
            index = (line * HEAD + start) // CH_OWN
            shard = (index % layers) * plane + index // layers
            queries[pl.ds(shard, CH_OWN, stride=shards), :] = scaled[start : start + CH_OWN, :]
    query_ref[...] = queries[...].astype(jnp.bfloat16)


def attend_kernel(plane, place_ref, query_ref, *refs):
    pair_refs, (out_ref, natural, keys, values, attended) = refs[:plane], refs[plane:]
    rows = query_ref.shape[0]
    window = out_ref.shape[1]
    part = rows // plane
    shards = rows // CH_OWN
    layers = shards // plane
    cross = lax.rem(seat()[0], plane)
    for number, held in enumerate((keys, values)):
        for mask, pair_ref in enumerate(pair_refs):
            for layer in range(layers):
                piece = pair_ref[pl.ds(number * part + layer * CH_OWN, CH_OWN), :]
                where = pl.ds(layer * plane + (cross ^ mask), CH_OWN, stride=shards)
                natural[where, :] = piece.astype(jnp.float32)
        held[...] = natural[...].astype(jnp.bfloat16)
    block = min(256, rows)
    score_scale = 1.0 / math.sqrt(HEAD)
    for start in range(0, rows, block):
        stop = start + block
        scores = lax.dot_general(
            query_ref[start:stop, :],
            keys[0:stop, :],
            (((1,), (1,)), ((), ())),
            preferred_element_type=jnp.float32,
        )
        spots = lax.broadcasted_iota(jnp.int32, scores.shape, 1)
        mine = lax.broadcasted_iota(jnp.int32, scores.shape, 0) + start
        scores = jnp.where(spots <= mine, scores * score_scale, masked)
        peak = jnp.max(scores, axis=1, keepdims=True)
        lifted = jnp.exp(scores - peak)
        denominator = jnp.sum(lifted, axis=1, keepdims=True)
        weighted = jnp.dot(
            lifted.astype(jnp.bfloat16), values[0:stop, :], preferred_element_type=jnp.float32
        )
        attended[start:stop, :] = (weighted / denominator).astype(jnp.bfloat16)
    attended[rows:, :] = jnp.zeros((attended.shape[0] - rows, HEAD), jnp.bfloat16)
    for shard in range(out_ref.shape[0]):
        first = place_ref[shard]
        out_ref[shard] = attended[pl.ds(pl.multiple_of(first * TILE, TILE), window), :]


def return_kernel(weight_ref, pieces_ref, own_ref, other_ref, attended):
    half = own_ref.shape[1]
    lane = seat()[1]
    for head in range(pieces_ref.shape[0]):
        attended[:, head * HEAD : (head + 1) * HEAD] = pieces_ref[head]
    other_ref[...] = jnp.dot(
        attended[...], weight_ref[:, lanes(1 - lane, half)], preferred_element_type=jnp.float32
    )
    own_ref[...] = jnp.dot(
        attended[...], weight_ref[:, lanes(lane, half)], preferred_element_type=jnp.float32
    )


def join_kernel(own_ref, other_ref, encoded_ref, spread_ref, out_ref):
    returned = (own_ref[...] + other_ref[...]).astype(jnp.bfloat16)
    results = jnp.dot(spread_ref[...], returned, preferred_element_type=jnp.float32)
    out_ref[...] = (encoded_ref[...].astype(jnp.float32) + results).astype(jnp.bfloat16)


def one_head_each(
    byte_states,
    outer_gain,
    mamba_input,
    mamba_step,
    decay_rate,
    mixer_weight,
    boundaries,
    span_counts,
    up_weight,
    up_bias,
    inner_gain,
    query_weight,
    key_weight,
    value_weight,
    return_weight,
):
    shards = lax.axis_size("seq")
    me = lax.axis_index("seq")
    lane = lax.axis_index("mp")
    plane = HEADS // KV_HEADS
    layers = shards // plane
    rows_here, width = byte_states.shape
    half = mamba_input.shape[1]
    capacity = boundaries.shape[1]
    window = capacity + TILE
    total_rows = CH_OWN * shards
    inner_width = inner_gain.shape[0]
    inner_half = up_bias.shape[0]
    weight_rows = query_weight.shape[0]
    f32, bf16 = jnp.float32, jnp.bfloat16
    layer, cross = me // plane, me % plane

    def over(value, mask):
        return lax.ppermute(value, "seq", [(i, i ^ mask) for i in range(shards)])

    def after(value, done):
        return lax.optimization_barrier((value, done))[0]

    own_bias = up_bias.reshape(layers // 2, plane, weight_rows)
    own_bias = lax.dynamic_index_in_dim(own_bias, cross, 1, keepdims=False).reshape(1, -1)
    own_gain = inner_gain.reshape(layers, plane, weight_rows)
    own_gain = lax.dynamic_index_in_dim(own_gain, cross, 1, keepdims=False).reshape(1, -1)

    seq_ids = jnp.arange(shards, dtype=jnp.int32)
    offsets = jnp.cumsum(span_counts) - span_counts
    own_offset = jnp.sum(jnp.where(seq_ids == me, offsets, 0))
    own_count = jnp.sum(jnp.where(seq_ids == me, span_counts, 0))
    place = offsets // TILE
    own_marks = boundaries[0]
    positions = jnp.arange(rows_here, dtype=jnp.int32)
    spans_here = jnp.arange(capacity, dtype=jnp.int32)
    live = spans_here < own_count
    slots = capacity // shards
    slot_ids = jnp.arange(slots, dtype=jnp.int32)
    owners = seq_ids.reshape(layers, plane).T
    local_span = slot_ids * shards + ((owners - own_offset) % shards)[:, :, None]
    is_span = spans_here[None, :] == local_span.reshape(-1)[:, None]
    byte_at = jnp.sum(jnp.where(is_span, jnp.minimum(own_marks, rows_here - 1)[None, :], 0), axis=1)
    pool_pick = (positions[None, :] == byte_at[:, None]).astype(bf16)
    near_owner = jnp.arange(layers, dtype=jnp.int32) * plane + cross
    near_spans = near_owner[:, None] + jnp.arange(CH_OWN, dtype=jnp.int32)[None, :] * shards
    origin = jnp.sum((offsets <= near_spans[:, :, None]).astype(jnp.int32), axis=2) - 1
    origin_offset = jnp.sum(jnp.where(seq_ids == origin[:, :, None], offsets, 0), axis=2)
    arrived_row = (
        origin * (layers * slots)
        + jnp.arange(layers, dtype=jnp.int32)[:, None] * slots
        + (near_spans - origin_offset) // shards
    ).reshape(-1)
    near_pick = (
        jnp.arange(shards * layers * slots, dtype=jnp.int32)[None, :] == arrived_row[:, None]
    ).astype(bf16)
    passed = jnp.sum(
        ((own_marks[None, :] <= positions[:, None]) & live[None, :]).astype(jnp.int32), axis=1
    )
    result_row = passed - 1 + own_offset % TILE
    spread = (jnp.arange(window, dtype=jnp.int32)[None, :] == result_row[:, None]).astype(bf16)

    up_half = inner_half // plane
    up_layers = [up_weight]
    for bit in range(layers.bit_length() - 2, -1, -1):
        up_layers += [over(piece, plane << bit) for piece in up_layers]
    order = [0]
    for bit in range(layers.bit_length() - 2, -1, -1):
        order += [step ^ (1 << bit) for step in order]
    up_layers = [up_layers[order.index(step)] for step in range(layers)]

    local, through, ends, *pair_cuts = pl.pallas_call(
        functools.partial(scan_kernel, plane, layers),
        out_shape=(
            jax.ShapeDtypeStruct((rows_here, half), f32),
            jax.ShapeDtypeStruct((rows_here, half), f32),
            jax.ShapeDtypeStruct((shards, 2, half), f32),
        )
        + (jax.ShapeDtypeStruct((weight_rows, (plane + 2) * HEAD), bf16),) * layers,
        in_specs=[in_hbm(), vmem(), in_hbm(), in_hbm(), vmem()] + [in_hbm()] * 3,
        out_specs=(vmem(),) * 3 + (in_place(),) * layers,
        scratch_shapes=[
            pltpu.VMEM(array.shape, bf16)
            for array in (
                byte_states,
                mamba_input,
                mamba_step,
                query_weight,
                key_weight,
                value_weight,
            )
        ]
        + [pltpu.SemaphoreType.DMA((6,)), pltpu.SemaphoreType.DMA((3 * layers,))],
        cost_estimate=brief(),
        compiler_params=params(56),
    )(
        byte_states,
        outer_gain[None, :],
        mamba_input,
        mamba_step,
        decay_rate[None, :],
        query_weight,
        key_weight,
        value_weight,
    )
    ends = lax.all_to_all(ends, "seq", 0, 0, tiled=True)
    ends, up_layers[1], up_layers[2] = lax.optimization_barrier(
        (ends, up_layers[1], up_layers[2])
    )
    pieces = [pair_cuts[0]] + [over(pair_cuts[step], plane * step) for step in range(1, layers)]
    states, other_part = pl.pallas_call(
        states_kernel,
        out_shape=(
            jax.ShapeDtypeStruct((rows_here, half), bf16),
            jax.ShapeDtypeStruct((rows_here, half), f32),
        ),
        in_specs=[vmem()] * 4,
        out_specs=(vmem(),) * 2,
        cost_estimate=brief(),
        compiler_params=params(56),
    )(local, through, mixer_weight, ends)
    far_bias = swapped(own_bias)
    bias = jnp.where(
        lane == 0,
        jnp.concatenate([own_bias, far_bias], axis=1),
        jnp.concatenate([far_bias, own_bias], axis=1),
    )
    far_part, bias, own_gain, near_pick, pieces[1], up_layers[3] = lax.optimization_barrier(
        (swapped(other_part), bias, own_gain, near_pick, pieces[1], up_layers[3])
    )
    encoded, leaving = pl.pallas_call(
        functools.partial(pool_kernel, plane),
        out_shape=(
            jax.ShapeDtypeStruct((rows_here, half), bf16),
            jax.ShapeDtypeStruct((shards, layers * slots, half), bf16),
        ),
        in_specs=[vmem()] * 5,
        out_specs=(vmem(),) * 2,
        cost_estimate=brief(),
        compiler_params=params(56),
    )(states, mixer_weight, far_part, byte_states, pool_pick)
    arrived = lax.all_to_all(leaving, "seq", 0, 0, tiled=True)
    up_cuts = pl.pallas_call(
        functools.partial(cut_kernel, plane),
        out_shape=(jax.ShapeDtypeStruct((layers, up_weight.shape[0], up_half), bf16),) * plane,
        in_specs=[in_place()] * (1 + layers),
        out_specs=(in_place(),) * plane,
        scratch_shapes=[
            pltpu.VMEM((layers, *up_weight.shape), bf16),
            pltpu.SemaphoreType.DMA((layers,)),
            pltpu.SemaphoreType.DMA((plane * layers // 2,)),
        ],
        cost_estimate=brief(),
        compiler_params=params(56),
    )(leaving, *up_layers)
    up_own = [up_cuts[0]] + [over(up_cuts[mask], mask) for mask in range(1, plane)]
    arrived, pieces, up_own = lax.optimization_barrier((arrived, pieces, up_own))
    near_rows = pl.pallas_call(
        own_kernel,
        out_shape=jax.ShapeDtypeStruct((layers * CH_OWN, half), bf16),
        in_specs=[vmem()] * 2,
        out_specs=vmem(),
        cost_estimate=brief(),
        compiler_params=params(56),
    )(near_pick, arrived)
    near_rows, up_far = lax.optimization_barrier(
        (near_rows, [swapped(piece) for piece in up_own])
    )
    near = [near_rows] + [over(near_rows, mask) for mask in range(1, plane)]
    far = [swapped(piece) for piece in near]

    features = own_gain.shape[1]
    block = total_rows // plane
    lines = total_rows // HEAD
    pair_rows = 2 * block + 2 * lines
    partial_sums = pl.pallas_call(
        functools.partial(inner_kernel, plane, layers),
        out_shape=(jax.ShapeDtypeStruct((total_rows, HEAD), bf16),) * plane
        + (jax.ShapeDtypeStruct((pair_rows, HEAD), bf16),) * plane,
        in_specs=[vmem()] * 2 + [in_place()] * (4 * plane + layers),
        out_specs=(in_place(),) * (2 * plane),
        scratch_shapes=[
            pltpu.VMEM((total_rows, width), bf16),
            pltpu.VMEM((width, features), bf16),
            pltpu.VMEM((features, (plane + 2) * HEAD), bf16),
            pltpu.VMEM((8, total_rows), f32),
            pltpu.VMEM((plane, total_rows, HEAD), bf16),
            pltpu.VMEM((plane, pair_rows, HEAD), bf16),
            pltpu.SemaphoreType.DMA((2 * plane + 2 * shards + layers,)),
            pltpu.SemaphoreType.DMA((2 * plane,)),
        ],
        cost_estimate=brief(),
        compiler_params=params(56),
    )(bias, own_gain, *near, *far, *up_own, *up_far, *pieces)
    query_sums, pair_sums = partial_sums[:plane], partial_sums[plane:]
    got_pairs = [pair_sums[0]] + [over(pair_sums[mask], mask) for mask in range(1, plane)]
    got_queries = [query_sums[0]] + [over(query_sums[mask], mask) for mask in range(1, plane)]
    pairs = pl.pallas_call(
        functools.partial(pairs_kernel, inner_width, lines),
        out_shape=jax.ShapeDtypeStruct((2 * block, HEAD), bf16),
        in_specs=[vmem()] * plane,
        out_specs=vmem(),
        cost_estimate=brief(),
        compiler_params=params(8),
    )(*got_pairs)
    whole_pairs = [pairs] + [over(pairs, mask) for mask in range(1, plane)]
    queries = pl.pallas_call(
        functools.partial(queries_kernel, inner_width, plane),
        out_shape=jax.ShapeDtypeStruct((total_rows, HEAD), bf16),
        in_specs=[vmem()] * (2 * plane),
        out_specs=vmem(),
        scratch_shapes=[pltpu.VMEM((total_rows, HEAD), f32)],
        cost_estimate=brief(),
        compiler_params=params(10),
    )(*got_queries, *got_pairs)
    leaving = pl.pallas_call(
        functools.partial(attend_kernel, plane),
        out_shape=jax.ShapeDtypeStruct((shards, window, HEAD), bf16),
        in_specs=[smem()] + [vmem()] * (1 + plane),
        out_specs=vmem(),
        scratch_shapes=[
            pltpu.VMEM((total_rows, HEAD), f32),
            pltpu.VMEM((total_rows, HEAD), bf16),
            pltpu.VMEM((total_rows, HEAD), bf16),
            pltpu.VMEM((total_rows + window, HEAD), bf16),
        ],
        cost_estimate=brief(),
        compiler_params=params(12),
    )(place, queries, *whole_pairs)
    pieces = lax.all_to_all(leaving, "seq", 0, 0, tiled=True)
    own_back, other_back = pl.pallas_call(
        return_kernel,
        out_shape=(jax.ShapeDtypeStruct((window, half), f32),) * 2,
        in_specs=[vmem()] * 2,
        out_specs=(vmem(),) * 2,
        scratch_shapes=[pltpu.VMEM((window, shards * HEAD), bf16)],
        cost_estimate=brief(),
        compiler_params=params(12),
    )(return_weight, pieces)
    return pl.pallas_call(
        join_kernel,
        out_shape=jax.ShapeDtypeStruct((rows_here, half), bf16),
        in_specs=[vmem()] * 4,
        out_specs=vmem(),
        cost_estimate=brief(),
        compiler_params=params(8),
    )(own_back, swapped(other_back), encoded, spread)


def prefix(value, axis, join, neutral):
    count, mine = (lax.axis_size(axis), lax.axis_index(axis))
    pieces = jax.tree.map(lambda part: lax.all_gather(part, axis), value)
    so_far = jax.tree.map(
        lambda part, zero: jnp.full_like(part, 0) + jnp.asarray(zero, part.dtype), value, neutral
    )

    def lap(position, so_far):
        longer = join(so_far, jax.tree.map(lambda part: part[position], pieces))
        return jax.tree.map(lambda new, old: jnp.where(position < mine, new, old), longer, so_far)

    return lax.fori_loop(0, count - 1, lap, so_far)


def rms_scale(values, gain):
    values = values.astype(jnp.float32)
    return values * lax.rsqrt(jnp.mean(values * values, axis=-1, keepdims=True) + eps) * gain


def combine_pairs(earlier, later):
    return (earlier[0] * later[0], later[0] * earlier[1] + later[1])


def pick_table(table, wanted, seq_ids):
    return jnp.sum(jnp.where(seq_ids[None, :] == wanted[:, None], table[None, :], 0), axis=1)


def block_size(piece_rows, shard_rows):
    limit = max(1, 1024 // shard_rows)
    pieces = max(1, piece_rows // shard_rows)
    best_size = 1
    for candidate in range(1, limit + 1):
        if pieces % candidate == 0:
            best_size = candidate
    return min(piece_rows, best_size * shard_rows)


def spread_heads(
    byte_states,
    outer_gain,
    mamba_input,
    mamba_step,
    decay_rate,
    mixer_weight,
    boundaries,
    span_counts,
    up_weight,
    up_bias,
    inner_gain,
    query_weight,
    key_weight,
    value_weight,
    return_weight,
):
    shards = lax.axis_size("seq")
    own_shard = lax.axis_index("seq")
    own_lane = lax.axis_index("mp")
    rows_here = byte_states.shape[0]
    capacity = boundaries.shape[1]
    column_count = mamba_input.shape[1]
    kv_local = key_weight.shape[1] // HEAD
    group_size = HEADS // KV_HEADS
    slot_count = capacity // shards
    offsets = jnp.cumsum(span_counts) - span_counts
    seq_ids = jnp.arange(shards, dtype=jnp.int32)
    own_offset = jnp.sum(jnp.where(seq_ids == own_shard, offsets, 0))
    own_count = jnp.sum(jnp.where(seq_ids == own_shard, span_counts, 0))
    normed = rms_scale(byte_states, outer_gain).astype(jnp.bfloat16)
    inputs = jnp.dot(normed, mamba_input, preferred_element_type=jnp.float32)
    step_sizes = jax.nn.softplus(jnp.dot(normed, mamba_step, preferred_element_type=jnp.float32))
    rate_steps = step_sizes * decay_rate
    decays = jnp.exp(-rate_steps)
    drives = jnp.sqrt(-jnp.expm1(-2.0 * rate_steps)) * inputs
    through, local_states = lax.associative_scan(combine_pairs, (decays, drives), axis=0)
    starting = (jnp.ones((column_count,), jnp.float32), jnp.zeros((column_count,), jnp.float32))
    arriving = prefix((through[-1], local_states[-1]), "seq", combine_pairs, starting)
    states = (local_states + through * arriving[1][None, :]).astype(jnp.bfloat16)
    partial_value = jnp.dot(states, mixer_weight, preferred_element_type=jnp.float32)
    mixed_sum = lax.psum(partial_value, "mp")
    encoded = (byte_states.astype(jnp.float32) + mixed_sum).astype(jnp.bfloat16)
    skip_part = lax.dynamic_slice_in_dim(encoded, own_lane * column_count, column_count, 1)
    own_marks = boundaries[0]
    pooled = encoded[jnp.minimum(own_marks, rows_here - 1)]
    row_width = pooled.shape[1]
    outgoing = jnp.roll(pooled.reshape(slot_count, shards, row_width), own_offset % shards, axis=1)
    incoming = lax.all_to_all(outgoing, "seq", split_axis=1, concat_axis=1, tiled=True)
    position = jnp.arange(CH_OWN, dtype=jnp.int32)
    span_index = own_shard + position * shards
    source = jnp.sum((offsets[None, :] <= span_index[:, None]).astype(jnp.int32), axis=1) - 1
    source_offset = pick_table(offsets, source, seq_ids)
    slot_index = (span_index - source_offset) // shards
    gathered_rows = incoming.reshape(slot_count * shards, row_width)[slot_index * shards + source]
    columns = gathered_rows
    widened_sum = jnp.dot(
        columns,
        lax.all_gather(up_weight, "seq", axis=0, tiled=True),
        preferred_element_type=jnp.float32,
    )
    widened_share = (widened_sum + up_bias[None, :]).astype(jnp.bfloat16)
    widened = lax.all_gather(widened_share, "mp", axis=1, tiled=True)
    inner_normed = rms_scale(widened, inner_gain).astype(jnp.bfloat16)
    columns = inner_normed
    query_part = jnp.dot(
        columns,
        lax.all_gather(query_weight, "seq", axis=0, tiled=True),
        preferred_element_type=jnp.float32,
    )
    key_part = jnp.dot(
        columns,
        lax.all_gather(key_weight, "seq", axis=0, tiled=True),
        preferred_element_type=jnp.float32,
    )
    value_part = jnp.dot(
        columns,
        lax.all_gather(value_weight, "seq", axis=0, tiled=True),
        preferred_element_type=jnp.float32,
    )
    queries = query_part.astype(jnp.bfloat16)
    key_rows = key_part.astype(jnp.bfloat16)
    value_rows = value_part.astype(jnp.bfloat16)
    query_count = queries.shape[0]
    grouped = (
        queries.reshape(query_count, kv_local, group_size, HEAD)
        .transpose(1, 0, 2, 3)
        .reshape(kv_local, query_count * group_size, HEAD)
    )
    row_index = jnp.repeat(span_index, group_size)
    shard_rows = key_rows.shape[0]
    score_scale = 1.0 / math.sqrt(HEAD)

    def key_index(whole_index):
        return whole_index // shard_rows + whole_index % shard_rows * shards

    def attend_block(running, key_block, value_block, index_block):
        row_peak, denominator, weighted = running
        scores = (
            jnp.einsum("hqd,khd->hqk", grouped, key_block, preferred_element_type=jnp.float32)
            * score_scale
        )
        scores = jnp.where(index_block[None, None, :] <= row_index[None, :, None], scores, masked)
        new_peak = jnp.maximum(row_peak, jnp.max(scores, axis=2))
        shrink = jnp.exp(row_peak - new_peak)
        lifted = jnp.exp(scores - new_peak[:, :, None])
        denominator = denominator * shrink + jnp.sum(lifted, axis=2)
        weighted = weighted * shrink[:, :, None] + jnp.einsum(
            "hqk,khd->hqd",
            lifted.astype(jnp.bfloat16),
            value_block,
            preferred_element_type=jnp.float32,
        )
        return (new_peak, denominator, weighted)

    query_total = query_count * group_size
    initial = (
        jnp.full((kv_local, query_total), masked, jnp.float32),
        jnp.zeros((kv_local, query_total), jnp.float32),
        jnp.zeros((kv_local, query_total, HEAD), jnp.float32),
    )
    key_piece = lax.all_gather(key_rows, "seq", axis=0, tiled=True)
    value_piece = lax.all_gather(value_rows, "seq", axis=0, tiled=True)
    piece_rows = key_piece.shape[0]
    block_rows = block_size(piece_rows, shard_rows)
    turn_count = piece_rows // block_rows
    key_blocks = key_piece.reshape(turn_count, block_rows, kv_local, HEAD)
    value_blocks = value_piece.reshape(turn_count, block_rows, kv_local, HEAD)

    def one_turn(turn_index, inner_running):
        whole_index = turn_index * block_rows + jnp.arange(block_rows, dtype=jnp.int32)
        return attend_block(
            inner_running, key_blocks[turn_index], value_blocks[turn_index], key_index(whole_index)
        )

    row_peak, denominator, weighted = lax.fori_loop(0, turn_count, one_turn, initial)
    attended = (weighted / denominator[:, :, None]).astype(jnp.bfloat16)
    attended = (
        attended.reshape(kv_local, query_count, group_size, HEAD)
        .transpose(1, 0, 2, 3)
        .reshape(query_count, kv_local * group_size * HEAD)
    )
    projected = jnp.dot(attended, return_weight, preferred_element_type=jnp.float32)
    returned = lax.psum_scatter(
        projected.astype(jnp.bfloat16), "mp", scatter_dimension=1, tiled=True
    )
    slot_ids = jnp.arange(slot_count, dtype=jnp.int32)
    lead_slot = (own_shard - offsets) % shards
    local_span = slot_ids[:, None] * shards + lead_slot[None, :]
    back_index = (offsets[None, :] + local_span - own_shard) // shards
    alive = local_span < span_counts[None, :]
    back_rows = jnp.where(
        alive[:, :, None],
        returned[jnp.clip(back_index, 0, CH_OWN - 1)],
        jnp.zeros((), jnp.bfloat16),
    )
    arrived = lax.all_to_all(back_rows, "seq", split_axis=1, concat_axis=1, tiled=True)
    span_results = jnp.roll(arrived, -(own_offset % shards), axis=1).reshape(capacity, column_count)
    positions = jnp.arange(rows_here, dtype=jnp.int32)
    live_slots = jnp.arange(capacity, dtype=jnp.int32) < own_count
    passed = jnp.sum(
        ((own_marks[None, :] <= positions[:, None]) & live_slots[None, :]).astype(jnp.int32), axis=1
    )
    return (skip_part.astype(jnp.float32) + span_results[passed - 1].astype(jnp.float32)).astype(
        jnp.bfloat16
    )


def solution(mesh):
    in_specs = (
        P("seq", None),
        P(),
        P(None, "mp"),
        P(None, "mp"),
        P("mp"),
        P("mp", None),
        P("seq", None),
        P(),
        P("seq", "mp"),
        P("mp"),
        P(),
        P("seq", "mp"),
        P("seq", "mp"),
        P("seq", "mp"),
        P("mp", None),
    )
    out_specs = P("seq", "mp")
    def on_device(*arrays):
        heads_here = arrays[11].shape[1] // HEAD
        fits = heads_here == mesh.shape["seq"] and mesh.shape["mp"] == 2
        return (one_head_each if fits else spread_heads)(*arrays)

    return jax.shard_map(
        on_device, mesh=mesh, in_specs=in_specs, out_specs=out_specs, check_vma=False
    )
```

```python
import functools
import math

import jax
import jax.numpy as jnp
from jax import lax
from jax.experimental import pallas as pl
from jax.experimental.pallas import tpu as pltpu
from jax.sharding import PartitionSpec as P

HEADS = 32
KV_HEADS = 8
HEAD = 128
CH_OWN = 64


eps = 1e-05
masked = -1e30
TILE = 16


def swapped(value):
    return lax.ppermute(value, "mp", [(0, 1), (1, 0)])


def vmem():
    return pl.BlockSpec(memory_space=pltpu.VMEM)


def smem():
    return pl.BlockSpec(memory_space=pltpu.SMEM)


def in_place():
    return pl.BlockSpec(memory_space=pl.ANY)


def in_hbm():
    return pl.BlockSpec(memory_space=pltpu.HBM)


def seat():
    return lax.axis_index("seq"), lax.axis_index("mp")


def params(mebibytes=24):
    return pltpu.CompilerParams(vmem_limit_bytes=mebibytes * 2**20)


def brief():
    return pl.CostEstimate(flops=1, bytes_accessed=1, transcendentals=0)


def lanes(which, size):
    return pl.ds(pl.multiple_of(which * size, size), size)


def rows_at(which, size):
    return pl.ds(pl.multiple_of(which * size, size), size)


def start_all(pairs, sems):
    copies = []
    for index, (from_ref, to_ref) in enumerate(pairs):
        copy = pltpu.make_async_copy(from_ref, to_ref, sems.at[index])
        copy.start()
        copies.append(copy)
    return copies


def copy_all(pairs, sems):
    for copy in start_all(pairs, sems):
        copy.wait()


def one_minus_exp(u):
    series = jnp.ones_like(u)
    for order in range(9, 1, -1):
        series = 1.0 - u * (1.0 / order) * series
    return jnp.where(u < 0.5, u * series, 1.0 - jnp.exp(-u))


def softplus(v):
    tail = jnp.exp(-jnp.abs(v))
    series = jnp.ones_like(tail)
    for order in range(6, 1, -1):
        series = 1.0 - tail * ((order - 1.0) / order) * series
    return jnp.maximum(v, 0.0) + jnp.where(tail < 0.03, tail * series, jnp.log(1.0 + tail))


def start_cuts(plane, query_ref, key_ref, value_ref, pair_outs, sems):
    layers = len(pair_outs)
    me, _ = seat()
    layer = me // plane
    group = plane * HEAD
    pairs = []
    for step, out_ref in enumerate(pair_outs):
        target = layer ^ step
        pairs.append((query_ref.at[:, lanes(target, group)], out_ref.at[:, pl.ds(0, group)]))
        pairs.append((key_ref.at[:, lanes(target, HEAD)], out_ref.at[:, pl.ds(group, HEAD)]))
        pairs.append(
            (value_ref.at[:, lanes(target, HEAD)], out_ref.at[:, pl.ds(group + HEAD, HEAD)])
        )
    return start_all(pairs, sems)


def scan_kernel(plane, layers, *refs):
    bytes_hbm, gain_ref, input_hbm, step_hbm, rate_ref = refs[:5]
    others, refs = refs[5:8], refs[8:]
    local_ref, through_ref, ends_ref = refs[:3]
    pair_outs, refs = refs[3 : 3 + layers], refs[3 + layers :]
    bytes_ref, input_ref, step_ref, *held, sems, cut_sems = refs
    fetches = start_all(
        [(bytes_hbm, bytes_ref), (step_hbm, step_ref), (input_hbm, input_ref), *zip(others, held)],
        sems,
    )
    fetches[0].wait()
    values = bytes_ref[...].astype(jnp.float32)
    scale = lax.rsqrt(jnp.mean(values * values, axis=1, keepdims=True) + eps)
    normed = (values * scale * gain_ref[...]).astype(jnp.bfloat16)
    fetches[1].wait()
    steps = softplus(jnp.dot(normed, step_ref[...], preferred_element_type=jnp.float32))
    rate_steps = steps * rate_ref[...]
    fetches[2].wait()
    inputs = jnp.dot(normed, input_ref[...], preferred_element_type=jnp.float32)
    for fetch in fetches[3:]:
        fetch.wait()
    cuts = start_cuts(plane, *held, pair_outs, cut_sems)
    decays = jnp.exp(-rate_steps)
    drives = jnp.sqrt(one_minus_exp(2.0 * rate_steps)) * inputs
    rows, width = decays.shape
    tile = 8
    decays = decays.reshape(rows // tile, tile, width)
    drives = drives.reshape(rows // tile, tile, width)
    place = lax.broadcasted_iota(jnp.int32, decays.shape, 1)
    for reach in (1, 2, 4):
        before_decays = pltpu.roll(decays, reach, 1)
        before_drives = pltpu.roll(drives, reach, 1)
        inside = place >= reach
        drives = jnp.where(inside, decays * before_drives + drives, drives)
        decays = jnp.where(inside, decays * before_decays, decays)
    state = jnp.zeros((1, width), jnp.float32)
    kept = jnp.ones((1, width), jnp.float32)
    for index in range(rows // tile):
        states = decays[index] * state + drives[index]
        passing = decays[index] * kept
        local_ref[pl.ds(index * tile, tile), :] = states
        through_ref[pl.ds(index * tile, tile), :] = passing
        state = states[tile - 1 :, :]
        kept = passing[tile - 1 :, :]
    for index in range(ends_ref.shape[0]):
        ends_ref[index, 0:1, :] = kept
        ends_ref[index, 1:2, :] = state
    for cut in cuts:
        cut.wait()


def states_kernel(local_ref, through_ref, mixer_ref, ends_ref, states_ref, other_ref):
    me, lane = seat()
    carry = jnp.zeros((1, local_ref.shape[1]), jnp.float32)
    for shard in range(ends_ref.shape[0]):
        later = ends_ref[shard, 0:1, :] * carry + ends_ref[shard, 1:2, :]
        carry = jnp.where(shard < me, later, carry)
    states = (local_ref[...] + through_ref[...] * carry).astype(jnp.bfloat16)
    states_ref[...] = states
    half = other_ref.shape[1]
    other_ref[...] = jnp.dot(
        states, mixer_ref[:, lanes(1 - lane, half)], preferred_element_type=jnp.float32
    )


def pool_kernel(
    plane, states_ref, mixer_ref, other_ref, bytes_ref, pick_ref, encoded_ref, out_ref
):
    half = other_ref.shape[1]
    columns = lanes(seat()[1], half)
    mixed = jnp.dot(states_ref[...], mixer_ref[:, columns], preferred_element_type=jnp.float32)
    skip = bytes_ref[:, columns].astype(jnp.float32)
    encoded = (skip + (mixed + other_ref[...])).astype(jnp.bfloat16)
    encoded_ref[...] = encoded
    picked = jnp.dot(pick_ref[...], encoded, preferred_element_type=jnp.float32)
    picked = picked.astype(jnp.bfloat16)
    size = out_ref.shape[1]
    for target in range(out_ref.shape[0]):
        start = target % plane * size
        out_ref[target] = picked[start : start + size, :]


def cut_kernel(plane, gate_ref, *refs):
    layers = len(refs) - plane - 3
    pieces, (*outs, held, sems, cut_sems) = refs[:layers], refs[layers:]
    copy_all([(piece, held.at[step]) for step, piece in enumerate(pieces)], sems)
    cross = lax.rem(seat()[0], plane)
    pairs = []
    for mask, out_ref in enumerate(outs):
        size = 2 * out_ref.shape[2] // layers
        for number in range(layers // 2):
            columns = lanes(number * plane + (cross ^ mask), size)
            pairs.append((held.at[:, :, columns], out_ref.at[:, :, pl.ds(number * size, size)]))
    copy_all(pairs, cut_sems)


def own_kernel(pick_ref, arrived_ref, out_ref):
    shards, slots, half = arrived_ref.shape
    rows = arrived_ref[...].reshape(shards * slots, half)
    own = jnp.dot(pick_ref[...], rows, preferred_element_type=jnp.float32)
    out_ref[...] = own.astype(jnp.bfloat16)


def inner_kernel(plane, layers, bias_ref, gain_ref, *refs):
    near, refs = refs[:plane], refs[plane:]
    far, refs = refs[:plane], refs[plane:]
    up_own, refs = refs[:plane], refs[plane:]
    up_far, refs = refs[:plane], refs[plane:]
    pieces, refs = refs[:layers], refs[layers:]
    query_refs, pair_refs, refs = refs[:plane], refs[plane : 2 * plane], refs[2 * plane :]
    pooled, up, weights, squares, queries_held, pairs_held, sems, out_sems = refs
    me, lane = seat()
    layer, cross = me // plane, lax.rem(me, plane)
    near_rows, half = near[0].shape
    up_rows, up_half = up_own[0].shape[1:]
    pairs = []
    for mask in range(plane):
        where = rows_at(cross ^ mask, near_rows)
        pairs.append((near[mask], pooled.at[where, lanes(lane, half)]))
        pairs.append((far[mask], pooled.at[where, lanes(1 - lane, half)]))
    for step in range(layers):
        for mask in range(plane):
            where = rows_at((layer ^ step) * plane + (cross ^ mask), up_rows)
            pairs.append((up_own[mask].at[step], up.at[where, lanes(lane, up_half)]))
            pairs.append((up_far[mask].at[step], up.at[where, lanes(1 - lane, up_half)]))
    for step, piece in enumerate(pieces):
        pairs.append((piece, weights.at[rows_at(layer ^ step, piece.shape[0]), :]))
    copies = start_all(pairs, sems)
    for copy in copies[:-layers]:
        copy.wait()
    rows = pooled.shape[0]
    block = rows // plane
    ones = jnp.ones((8, up.shape[1]), jnp.bfloat16)
    leaving = []
    for index in range(plane):
        where = pl.ds(index * block, block)
        widened = jnp.dot(pooled[where, :], up[...], preferred_element_type=jnp.float32)
        widened = (widened + bias_ref[...]).astype(jnp.bfloat16).astype(jnp.float32)
        inner = (widened * gain_ref[...]).astype(jnp.bfloat16)
        square = widened * widened
        coarse = square.astype(jnp.bfloat16)
        fine = (square - coarse.astype(jnp.float32)).astype(jnp.bfloat16)
        squares[:, where] = sum(
            lax.dot_general(
                ones, part, (((1,), (1,)), ((), ())), preferred_element_type=jnp.float32
            )
            for part in (coarse, fine)
        )
        if index == 0:
            for copy in copies[-layers:]:
                copy.wait()
        sums = jnp.dot(inner, weights[...], preferred_element_type=jnp.float32)
        sums = sums.astype(jnp.bfloat16)
        for head in range(plane):
            queries_held[head, where, :] = sums[:, head * HEAD : (head + 1) * HEAD]
        for number in range(2):
            start = (plane + number) * HEAD
            pairs_held[index, pl.ds(number * block, block), :] = sums[:, start : start + HEAD]
        for mask, out_ref in enumerate(query_refs):
            copy = pltpu.make_async_copy(
                queries_held.at[cross ^ mask, where],
                out_ref.at[where],
                out_sems.at[plane + index * plane + mask],
            )
            copy.start()
            leaving.append(copy)
    total = jnp.concatenate(
        [squares[0:1, start : start + HEAD] for start in range(0, rows, HEAD)], axis=0
    )
    coarse = total.astype(jnp.bfloat16).astype(jnp.float32)
    both = jnp.concatenate([coarse, total - coarse], axis=0).astype(jnp.bfloat16)
    for index in range(plane):
        pairs_held[index, pl.ds(2 * block, both.shape[0]), :] = both
    outs = [(pairs_held.at[cross ^ mask], out_ref) for mask, out_ref in enumerate(pair_refs)]
    copy_all(outs, out_sems)
    for copy in leaving:
        copy.wait()


def added(refs, start, size):
    parts = [ref[pl.ds(start, size), :].astype(jnp.float32) for ref in refs]
    return sum(parts[1:], parts[0])


def row_scale(features, refs, lines):
    both = added(refs, refs[0].shape[0] - 2 * lines, 2 * lines)
    total = both[:lines, :] + both[lines:, :]
    return jnp.transpose(lax.rsqrt(total * (1.0 / features) + eps))


def pairs_kernel(features, lines, *refs):
    got_refs, pair_ref = refs[:-1], refs[-1]
    scale = row_scale(features, got_refs, lines)
    cross = lax.rem(seat()[0], len(got_refs))
    per_block = lines // len(got_refs)
    for line in range(per_block):
        mine = scale[:, line : line + 1]
        for index in range(1, len(got_refs)):
            column = index * per_block + line
            mine = jnp.where(cross == index, scale[:, column : column + 1], mine)
        for number in range(2):
            start = (number * per_block + line) * HEAD
            pair_ref[pl.ds(start, HEAD), :] = (added(got_refs, start, HEAD) * mine).astype(
                jnp.bfloat16
            )


def queries_kernel(features, plane, *refs):
    got_refs, pair_refs, (query_ref, queries) = refs[:plane], refs[plane:-2], refs[-2:]
    rows = query_ref.shape[0]
    lines = rows // HEAD
    shards = rows // CH_OWN
    layers = shards // plane
    scale = row_scale(features, pair_refs, lines)
    for line in range(lines):
        scaled = added(got_refs, line * HEAD, HEAD) * scale[:, line : line + 1]
        for start in range(0, HEAD, CH_OWN):
            index = (line * HEAD + start) // CH_OWN
            shard = (index % layers) * plane + index // layers
            queries[pl.ds(shard, CH_OWN, stride=shards), :] = scaled[start : start + CH_OWN, :]
    query_ref[...] = queries[...].astype(jnp.bfloat16)


def attend_kernel(plane, place_ref, query_ref, *refs):
    pair_refs, (out_ref, natural, keys, values, attended) = refs[:plane], refs[plane:]
    rows = query_ref.shape[0]
    window = out_ref.shape[1]
    part = rows // plane
    shards = rows // CH_OWN
    layers = shards // plane
    cross = lax.rem(seat()[0], plane)
    for number, held in enumerate((keys, values)):
        for mask, pair_ref in enumerate(pair_refs):
            for layer in range(layers):
                piece = pair_ref[pl.ds(number * part + layer * CH_OWN, CH_OWN), :]
                where = pl.ds(layer * plane + (cross ^ mask), CH_OWN, stride=shards)
                natural[where, :] = piece.astype(jnp.float32)
        held[...] = natural[...].astype(jnp.bfloat16)
    block = min(256, rows)
    score_scale = 1.0 / math.sqrt(HEAD)
    for start in range(0, rows, block):
        stop = start + block
        scores = lax.dot_general(
            query_ref[start:stop, :],
            keys[0:stop, :],
            (((1,), (1,)), ((), ())),
            preferred_element_type=jnp.float32,
        )
        spots = lax.broadcasted_iota(jnp.int32, scores.shape, 1)
        mine = lax.broadcasted_iota(jnp.int32, scores.shape, 0) + start
        scores = jnp.where(spots <= mine, scores * score_scale, masked)
        peak = jnp.max(scores, axis=1, keepdims=True)
        lifted = jnp.exp(scores - peak)
        denominator = jnp.sum(lifted, axis=1, keepdims=True)
        weighted = jnp.dot(
            lifted.astype(jnp.bfloat16), values[0:stop, :], preferred_element_type=jnp.float32
        )
        attended[start:stop, :] = (weighted / denominator).astype(jnp.bfloat16)
    attended[rows:, :] = jnp.zeros((attended.shape[0] - rows, HEAD), jnp.bfloat16)
    for shard in range(out_ref.shape[0]):
        first = place_ref[shard]
        out_ref[shard] = attended[pl.ds(pl.multiple_of(first * TILE, TILE), window), :]


def return_kernel(weight_ref, pieces_ref, own_ref, other_ref, attended):
    half = own_ref.shape[1]
    lane = seat()[1]
    for head in range(pieces_ref.shape[0]):
        attended[:, head * HEAD : (head + 1) * HEAD] = pieces_ref[head]
    other_ref[...] = jnp.dot(
        attended[...], weight_ref[:, lanes(1 - lane, half)], preferred_element_type=jnp.float32
    )
    own_ref[...] = jnp.dot(
        attended[...], weight_ref[:, lanes(lane, half)], preferred_element_type=jnp.float32
    )


def join_kernel(own_ref, other_ref, encoded_ref, spread_ref, out_ref):
    returned = (own_ref[...] + other_ref[...]).astype(jnp.bfloat16)
    results = jnp.dot(spread_ref[...], returned, preferred_element_type=jnp.float32)
    out_ref[...] = (encoded_ref[...].astype(jnp.float32) + results).astype(jnp.bfloat16)


def one_head_each(
    byte_states,
    outer_gain,
    mamba_input,
    mamba_step,
    decay_rate,
    mixer_weight,
    boundaries,
    span_counts,
    up_weight,
    up_bias,
    inner_gain,
    query_weight,
    key_weight,
    value_weight,
    return_weight,
):
    shards = lax.axis_size("seq")
    me = lax.axis_index("seq")
    lane = lax.axis_index("mp")
    plane = HEADS // KV_HEADS
    layers = shards // plane
    rows_here, width = byte_states.shape
    half = mamba_input.shape[1]
    capacity = boundaries.shape[1]
    window = capacity + TILE
    total_rows = CH_OWN * shards
    inner_width = inner_gain.shape[0]
    inner_half = up_bias.shape[0]
    weight_rows = query_weight.shape[0]
    f32, bf16 = jnp.float32, jnp.bfloat16
    layer, cross = me // plane, me % plane

    def over(value, mask):
        return lax.ppermute(value, "seq", [(i, i ^ mask) for i in range(shards)])

    def after(value, done):
        return lax.optimization_barrier((value, done))[0]

    own_bias = up_bias.reshape(layers // 2, plane, weight_rows)
    own_bias = lax.dynamic_index_in_dim(own_bias, cross, 1, keepdims=False).reshape(1, -1)
    own_gain = inner_gain.reshape(layers, plane, weight_rows)
    own_gain = lax.dynamic_index_in_dim(own_gain, cross, 1, keepdims=False).reshape(1, -1)

    seq_ids = jnp.arange(shards, dtype=jnp.int32)
    offsets = jnp.cumsum(span_counts) - span_counts
    own_offset = jnp.sum(jnp.where(seq_ids == me, offsets, 0))
    own_count = jnp.sum(jnp.where(seq_ids == me, span_counts, 0))
    place = offsets // TILE
    own_marks = boundaries[0]
    positions = jnp.arange(rows_here, dtype=jnp.int32)
    spans_here = jnp.arange(capacity, dtype=jnp.int32)
    live = spans_here < own_count
    slots = capacity // shards
    slot_ids = jnp.arange(slots, dtype=jnp.int32)
    owners = seq_ids.reshape(layers, plane).T
    local_span = slot_ids * shards + ((owners - own_offset) % shards)[:, :, None]
    is_span = spans_here[None, :] == local_span.reshape(-1)[:, None]
    byte_at = jnp.sum(jnp.where(is_span, jnp.minimum(own_marks, rows_here - 1)[None, :], 0), axis=1)
    pool_pick = (positions[None, :] == byte_at[:, None]).astype(bf16)
    near_owner = jnp.arange(layers, dtype=jnp.int32) * plane + cross
    near_spans = near_owner[:, None] + jnp.arange(CH_OWN, dtype=jnp.int32)[None, :] * shards
    origin = jnp.sum((offsets <= near_spans[:, :, None]).astype(jnp.int32), axis=2) - 1
    origin_offset = jnp.sum(jnp.where(seq_ids == origin[:, :, None], offsets, 0), axis=2)
    arrived_row = (
        origin * (layers * slots)
        + jnp.arange(layers, dtype=jnp.int32)[:, None] * slots
        + (near_spans - origin_offset) // shards
    ).reshape(-1)
    near_pick = (
        jnp.arange(shards * layers * slots, dtype=jnp.int32)[None, :] == arrived_row[:, None]
    ).astype(bf16)
    passed = jnp.sum(
        ((own_marks[None, :] <= positions[:, None]) & live[None, :]).astype(jnp.int32), axis=1
    )
    result_row = passed - 1 + own_offset % TILE
    spread = (jnp.arange(window, dtype=jnp.int32)[None, :] == result_row[:, None]).astype(bf16)

    up_half = inner_half // plane
    up_layers = [up_weight] + [over(up_weight, plane * step) for step in range(1, layers)]

    local, through, ends, *pair_cuts = pl.pallas_call(
        functools.partial(scan_kernel, plane, layers),
        out_shape=(
            jax.ShapeDtypeStruct((rows_here, half), f32),
            jax.ShapeDtypeStruct((rows_here, half), f32),
            jax.ShapeDtypeStruct((shards, 2, half), f32),
        )
        + (jax.ShapeDtypeStruct((weight_rows, (plane + 2) * HEAD), bf16),) * layers,
        in_specs=[in_hbm(), vmem(), in_hbm(), in_hbm(), vmem()] + [in_hbm()] * 3,
        out_specs=(vmem(),) * 3 + (in_place(),) * layers,
        scratch_shapes=[
            pltpu.VMEM(array.shape, bf16)
            for array in (
                byte_states,
                mamba_input,
                mamba_step,
                query_weight,
                key_weight,
                value_weight,
            )
        ]
        + [pltpu.SemaphoreType.DMA((6,)), pltpu.SemaphoreType.DMA((3 * layers,))],
        cost_estimate=brief(),
        compiler_params=params(56),
    )(
        byte_states,
        outer_gain[None, :],
        mamba_input,
        mamba_step,
        decay_rate[None, :],
        query_weight,
        key_weight,
        value_weight,
    )
    ends = lax.all_to_all(ends, "seq", 0, 0, tiled=True)
    ends, up_layers = lax.optimization_barrier((ends, up_layers))
    pieces = [pair_cuts[0]] + [over(pair_cuts[step], plane * step) for step in range(1, layers)]
    states, other_part = pl.pallas_call(
        states_kernel,
        out_shape=(
            jax.ShapeDtypeStruct((rows_here, half), bf16),
            jax.ShapeDtypeStruct((rows_here, half), f32),
        ),
        in_specs=[vmem()] * 4,
        out_specs=(vmem(),) * 2,
        cost_estimate=brief(),
        compiler_params=params(56),
    )(local, through, mixer_weight, ends)
    far_bias = swapped(own_bias)
    bias = jnp.where(
        lane == 0,
        jnp.concatenate([own_bias, far_bias], axis=1),
        jnp.concatenate([far_bias, own_bias], axis=1),
    )
    far_part, bias, own_gain, near_pick, pieces[1] = lax.optimization_barrier(
        (swapped(other_part), bias, own_gain, near_pick, pieces[1])
    )
    encoded, leaving = pl.pallas_call(
        functools.partial(pool_kernel, plane),
        out_shape=(
            jax.ShapeDtypeStruct((rows_here, half), bf16),
            jax.ShapeDtypeStruct((shards, layers * slots, half), bf16),
        ),
        in_specs=[vmem()] * 5,
        out_specs=(vmem(),) * 2,
        cost_estimate=brief(),
        compiler_params=params(56),
    )(states, mixer_weight, far_part, byte_states, pool_pick)
    arrived = lax.all_to_all(leaving, "seq", 0, 0, tiled=True)
    up_cuts = pl.pallas_call(
        functools.partial(cut_kernel, plane),
        out_shape=(jax.ShapeDtypeStruct((layers, up_weight.shape[0], up_half), bf16),) * plane,
        in_specs=[in_place()] * (1 + layers),
        out_specs=(in_place(),) * plane,
        scratch_shapes=[
            pltpu.VMEM((layers, *up_weight.shape), bf16),
            pltpu.SemaphoreType.DMA((layers,)),
            pltpu.SemaphoreType.DMA((plane * layers // 2,)),
        ],
        cost_estimate=brief(),
        compiler_params=params(56),
    )(leaving, *up_layers)
    up_own = [up_cuts[0]] + [over(up_cuts[mask], mask) for mask in range(1, plane)]
    arrived, pieces, up_own = lax.optimization_barrier((arrived, pieces, up_own))
    near_rows = pl.pallas_call(
        own_kernel,
        out_shape=jax.ShapeDtypeStruct((layers * CH_OWN, half), bf16),
        in_specs=[vmem()] * 2,
        out_specs=vmem(),
        cost_estimate=brief(),
        compiler_params=params(56),
    )(near_pick, arrived)
    near_rows, up_far = lax.optimization_barrier(
        (near_rows, [swapped(piece) for piece in up_own])
    )
    near = [near_rows] + [over(near_rows, mask) for mask in range(1, plane)]
    far = [swapped(piece) for piece in near]

    features = own_gain.shape[1]
    block = total_rows // plane
    lines = total_rows // HEAD
    pair_rows = 2 * block + 2 * lines
    partial_sums = pl.pallas_call(
        functools.partial(inner_kernel, plane, layers),
        out_shape=(jax.ShapeDtypeStruct((total_rows, HEAD), bf16),) * plane
        + (jax.ShapeDtypeStruct((pair_rows, HEAD), bf16),) * plane,
        in_specs=[vmem()] * 2 + [in_place()] * (4 * plane + layers),
        out_specs=(in_place(),) * (2 * plane),
        scratch_shapes=[
            pltpu.VMEM((total_rows, width), bf16),
            pltpu.VMEM((width, features), bf16),
            pltpu.VMEM((features, (plane + 2) * HEAD), bf16),
            pltpu.VMEM((8, total_rows), f32),
            pltpu.VMEM((plane, total_rows, HEAD), bf16),
            pltpu.VMEM((plane, pair_rows, HEAD), bf16),
            pltpu.SemaphoreType.DMA((2 * plane + 2 * shards + layers,)),
            pltpu.SemaphoreType.DMA((plane + plane * plane,)),
        ],
        cost_estimate=brief(),
        compiler_params=params(56),
    )(bias, own_gain, *near, *far, *up_own, *up_far, *pieces)
    query_sums, pair_sums = partial_sums[:plane], partial_sums[plane:]
    got_pairs = [pair_sums[0]] + [over(pair_sums[mask], mask) for mask in range(1, plane)]
    got_queries = [query_sums[0]] + [over(query_sums[mask], mask) for mask in range(1, plane)]
    pairs = pl.pallas_call(
        functools.partial(pairs_kernel, inner_width, lines),
        out_shape=jax.ShapeDtypeStruct((2 * block, HEAD), bf16),
        in_specs=[vmem()] * plane,
        out_specs=vmem(),
        cost_estimate=brief(),
        compiler_params=params(8),
    )(*got_pairs)
    whole_pairs = [pairs] + [over(pairs, mask) for mask in range(1, plane)]
    queries = pl.pallas_call(
        functools.partial(queries_kernel, inner_width, plane),
        out_shape=jax.ShapeDtypeStruct((total_rows, HEAD), bf16),
        in_specs=[vmem()] * (2 * plane),
        out_specs=vmem(),
        scratch_shapes=[pltpu.VMEM((total_rows, HEAD), f32)],
        cost_estimate=brief(),
        compiler_params=params(10),
    )(*got_queries, *got_pairs)
    leaving = pl.pallas_call(
        functools.partial(attend_kernel, plane),
        out_shape=jax.ShapeDtypeStruct((shards, window, HEAD), bf16),
        in_specs=[smem()] + [vmem()] * (1 + plane),
        out_specs=vmem(),
        scratch_shapes=[
            pltpu.VMEM((total_rows, HEAD), f32),
            pltpu.VMEM((total_rows, HEAD), bf16),
            pltpu.VMEM((total_rows, HEAD), bf16),
            pltpu.VMEM((total_rows + window, HEAD), bf16),
        ],
        cost_estimate=brief(),
        compiler_params=params(12),
    )(place, queries, *whole_pairs)
    pieces = lax.all_to_all(leaving, "seq", 0, 0, tiled=True)
    own_back, other_back = pl.pallas_call(
        return_kernel,
        out_shape=(jax.ShapeDtypeStruct((window, half), f32),) * 2,
        in_specs=[vmem()] * 2,
        out_specs=(vmem(),) * 2,
        scratch_shapes=[pltpu.VMEM((window, shards * HEAD), bf16)],
        cost_estimate=brief(),
        compiler_params=params(12),
    )(return_weight, pieces)
    return pl.pallas_call(
        join_kernel,
        out_shape=jax.ShapeDtypeStruct((rows_here, half), bf16),
        in_specs=[vmem()] * 4,
        out_specs=vmem(),
        cost_estimate=brief(),
        compiler_params=params(8),
    )(own_back, swapped(other_back), encoded, spread)


def prefix(value, axis, join, neutral):
    count, mine = (lax.axis_size(axis), lax.axis_index(axis))
    pieces = jax.tree.map(lambda part: lax.all_gather(part, axis), value)
    so_far = jax.tree.map(
        lambda part, zero: jnp.full_like(part, 0) + jnp.asarray(zero, part.dtype), value, neutral
    )

    def lap(position, so_far):
        longer = join(so_far, jax.tree.map(lambda part: part[position], pieces))
        return jax.tree.map(lambda new, old: jnp.where(position < mine, new, old), longer, so_far)

    return lax.fori_loop(0, count - 1, lap, so_far)


def rms_scale(values, gain):
    values = values.astype(jnp.float32)
    return values * lax.rsqrt(jnp.mean(values * values, axis=-1, keepdims=True) + eps) * gain


def combine_pairs(earlier, later):
    return (earlier[0] * later[0], later[0] * earlier[1] + later[1])


def pick_table(table, wanted, seq_ids):
    return jnp.sum(jnp.where(seq_ids[None, :] == wanted[:, None], table[None, :], 0), axis=1)


def block_size(piece_rows, shard_rows):
    limit = max(1, 1024 // shard_rows)
    pieces = max(1, piece_rows // shard_rows)
    best_size = 1
    for candidate in range(1, limit + 1):
        if pieces % candidate == 0:
            best_size = candidate
    return min(piece_rows, best_size * shard_rows)


def spread_heads(
    byte_states,
    outer_gain,
    mamba_input,
    mamba_step,
    decay_rate,
    mixer_weight,
    boundaries,
    span_counts,
    up_weight,
    up_bias,
    inner_gain,
    query_weight,
    key_weight,
    value_weight,
    return_weight,
):
    shards = lax.axis_size("seq")
    own_shard = lax.axis_index("seq")
    own_lane = lax.axis_index("mp")
    rows_here = byte_states.shape[0]
    capacity = boundaries.shape[1]
    column_count = mamba_input.shape[1]
    kv_local = key_weight.shape[1] // HEAD
    group_size = HEADS // KV_HEADS
    slot_count = capacity // shards
    offsets = jnp.cumsum(span_counts) - span_counts
    seq_ids = jnp.arange(shards, dtype=jnp.int32)
    own_offset = jnp.sum(jnp.where(seq_ids == own_shard, offsets, 0))
    own_count = jnp.sum(jnp.where(seq_ids == own_shard, span_counts, 0))
    normed = rms_scale(byte_states, outer_gain).astype(jnp.bfloat16)
    inputs = jnp.dot(normed, mamba_input, preferred_element_type=jnp.float32)
    step_sizes = jax.nn.softplus(jnp.dot(normed, mamba_step, preferred_element_type=jnp.float32))
    rate_steps = step_sizes * decay_rate
    decays = jnp.exp(-rate_steps)
    drives = jnp.sqrt(-jnp.expm1(-2.0 * rate_steps)) * inputs
    through, local_states = lax.associative_scan(combine_pairs, (decays, drives), axis=0)
    starting = (jnp.ones((column_count,), jnp.float32), jnp.zeros((column_count,), jnp.float32))
    arriving = prefix((through[-1], local_states[-1]), "seq", combine_pairs, starting)
    states = (local_states + through * arriving[1][None, :]).astype(jnp.bfloat16)
    partial_value = jnp.dot(states, mixer_weight, preferred_element_type=jnp.float32)
    mixed_sum = lax.psum(partial_value, "mp")
    encoded = (byte_states.astype(jnp.float32) + mixed_sum).astype(jnp.bfloat16)
    skip_part = lax.dynamic_slice_in_dim(encoded, own_lane * column_count, column_count, 1)
    own_marks = boundaries[0]
    pooled = encoded[jnp.minimum(own_marks, rows_here - 1)]
    row_width = pooled.shape[1]
    outgoing = jnp.roll(pooled.reshape(slot_count, shards, row_width), own_offset % shards, axis=1)
    incoming = lax.all_to_all(outgoing, "seq", split_axis=1, concat_axis=1, tiled=True)
    position = jnp.arange(CH_OWN, dtype=jnp.int32)
    span_index = own_shard + position * shards
    source = jnp.sum((offsets[None, :] <= span_index[:, None]).astype(jnp.int32), axis=1) - 1
    source_offset = pick_table(offsets, source, seq_ids)
    slot_index = (span_index - source_offset) // shards
    gathered_rows = incoming.reshape(slot_count * shards, row_width)[slot_index * shards + source]
    columns = gathered_rows
    widened_sum = jnp.dot(
        columns,
        lax.all_gather(up_weight, "seq", axis=0, tiled=True),
        preferred_element_type=jnp.float32,
    )
    widened_share = (widened_sum + up_bias[None, :]).astype(jnp.bfloat16)
    widened = lax.all_gather(widened_share, "mp", axis=1, tiled=True)
    inner_normed = rms_scale(widened, inner_gain).astype(jnp.bfloat16)
    columns = inner_normed
    query_part = jnp.dot(
        columns,
        lax.all_gather(query_weight, "seq", axis=0, tiled=True),
        preferred_element_type=jnp.float32,
    )
    key_part = jnp.dot(
        columns,
        lax.all_gather(key_weight, "seq", axis=0, tiled=True),
        preferred_element_type=jnp.float32,
    )
    value_part = jnp.dot(
        columns,
        lax.all_gather(value_weight, "seq", axis=0, tiled=True),
        preferred_element_type=jnp.float32,
    )
    queries = query_part.astype(jnp.bfloat16)
    key_rows = key_part.astype(jnp.bfloat16)
    value_rows = value_part.astype(jnp.bfloat16)
    query_count = queries.shape[0]
    grouped = (
        queries.reshape(query_count, kv_local, group_size, HEAD)
        .transpose(1, 0, 2, 3)
        .reshape(kv_local, query_count * group_size, HEAD)
    )
    row_index = jnp.repeat(span_index, group_size)
    shard_rows = key_rows.shape[0]
    score_scale = 1.0 / math.sqrt(HEAD)

    def key_index(whole_index):
        return whole_index // shard_rows + whole_index % shard_rows * shards

    def attend_block(running, key_block, value_block, index_block):
        row_peak, denominator, weighted = running
        scores = (
            jnp.einsum("hqd,khd->hqk", grouped, key_block, preferred_element_type=jnp.float32)
            * score_scale
        )
        scores = jnp.where(index_block[None, None, :] <= row_index[None, :, None], scores, masked)
        new_peak = jnp.maximum(row_peak, jnp.max(scores, axis=2))
        shrink = jnp.exp(row_peak - new_peak)
        lifted = jnp.exp(scores - new_peak[:, :, None])
        denominator = denominator * shrink + jnp.sum(lifted, axis=2)
        weighted = weighted * shrink[:, :, None] + jnp.einsum(
            "hqk,khd->hqd",
            lifted.astype(jnp.bfloat16),
            value_block,
            preferred_element_type=jnp.float32,
        )
        return (new_peak, denominator, weighted)

    query_total = query_count * group_size
    initial = (
        jnp.full((kv_local, query_total), masked, jnp.float32),
        jnp.zeros((kv_local, query_total), jnp.float32),
        jnp.zeros((kv_local, query_total, HEAD), jnp.float32),
    )
    key_piece = lax.all_gather(key_rows, "seq", axis=0, tiled=True)
    value_piece = lax.all_gather(value_rows, "seq", axis=0, tiled=True)
    piece_rows = key_piece.shape[0]
    block_rows = block_size(piece_rows, shard_rows)
    turn_count = piece_rows // block_rows
    key_blocks = key_piece.reshape(turn_count, block_rows, kv_local, HEAD)
    value_blocks = value_piece.reshape(turn_count, block_rows, kv_local, HEAD)

    def one_turn(turn_index, inner_running):
        whole_index = turn_index * block_rows + jnp.arange(block_rows, dtype=jnp.int32)
        return attend_block(
            inner_running, key_blocks[turn_index], value_blocks[turn_index], key_index(whole_index)
        )

    row_peak, denominator, weighted = lax.fori_loop(0, turn_count, one_turn, initial)
    attended = (weighted / denominator[:, :, None]).astype(jnp.bfloat16)
    attended = (
        attended.reshape(kv_local, query_count, group_size, HEAD)
        .transpose(1, 0, 2, 3)
        .reshape(query_count, kv_local * group_size * HEAD)
    )
    projected = jnp.dot(attended, return_weight, preferred_element_type=jnp.float32)
    returned = lax.psum_scatter(
        projected.astype(jnp.bfloat16), "mp", scatter_dimension=1, tiled=True
    )
    slot_ids = jnp.arange(slot_count, dtype=jnp.int32)
    lead_slot = (own_shard - offsets) % shards
    local_span = slot_ids[:, None] * shards + lead_slot[None, :]
    back_index = (offsets[None, :] + local_span - own_shard) // shards
    alive = local_span < span_counts[None, :]
    back_rows = jnp.where(
        alive[:, :, None],
        returned[jnp.clip(back_index, 0, CH_OWN - 1)],
        jnp.zeros((), jnp.bfloat16),
    )
    arrived = lax.all_to_all(back_rows, "seq", split_axis=1, concat_axis=1, tiled=True)
    span_results = jnp.roll(arrived, -(own_offset % shards), axis=1).reshape(capacity, column_count)
    positions = jnp.arange(rows_here, dtype=jnp.int32)
    live_slots = jnp.arange(capacity, dtype=jnp.int32) < own_count
    passed = jnp.sum(
        ((own_marks[None, :] <= positions[:, None]) & live_slots[None, :]).astype(jnp.int32), axis=1
    )
    return (skip_part.astype(jnp.float32) + span_results[passed - 1].astype(jnp.float32)).astype(
        jnp.bfloat16
    )


def solution(mesh):
    in_specs = (
        P("seq", None),
        P(),
        P(None, "mp"),
        P(None, "mp"),
        P("mp"),
        P("mp", None),
        P("seq", None),
        P(),
        P("seq", "mp"),
        P("mp"),
        P(),
        P("seq", "mp"),
        P("seq", "mp"),
        P("seq", "mp"),
        P("mp", None),
    )
    out_specs = P("seq", "mp")
    def on_device(*arrays):
        heads_here = arrays[11].shape[1] // HEAD
        fits = heads_here == mesh.shape["seq"] and mesh.shape["mp"] == 2
        return (one_head_each if fits else spread_heads)(*arrays)

    return jax.shard_map(
        on_device, mesh=mesh, in_specs=in_specs, out_specs=out_specs, check_vma=False
    )
```

```python
import functools
import math

import jax
import jax.numpy as jnp
from jax import lax
from jax.experimental import pallas as pl
from jax.experimental.pallas import tpu as pltpu
from jax.sharding import PartitionSpec as P

HEADS = 32
KV_HEADS = 8
HEAD = 128
CH_OWN = 64


eps = 1e-05
masked = -1e30
TILE = 16


def swapped(value):
    return lax.ppermute(value, "mp", [(0, 1), (1, 0)])


def vmem():
    return pl.BlockSpec(memory_space=pltpu.VMEM)


def smem():
    return pl.BlockSpec(memory_space=pltpu.SMEM)


def in_place():
    return pl.BlockSpec(memory_space=pl.ANY)


def in_hbm():
    return pl.BlockSpec(memory_space=pltpu.HBM)


def seat():
    return lax.axis_index("seq"), lax.axis_index("mp")


def params(mebibytes=24):
    return pltpu.CompilerParams(vmem_limit_bytes=mebibytes * 2**20)


def brief():
    return pl.CostEstimate(flops=1, bytes_accessed=1, transcendentals=0)


def lanes(which, size):
    return pl.ds(pl.multiple_of(which * size, size), size)


def rows_at(which, size):
    return pl.ds(pl.multiple_of(which * size, size), size)


def start_all(pairs, sems):
    copies = []
    for index, (from_ref, to_ref) in enumerate(pairs):
        copy = pltpu.make_async_copy(from_ref, to_ref, sems.at[index])
        copy.start()
        copies.append(copy)
    return copies


def copy_all(pairs, sems):
    for copy in start_all(pairs, sems):
        copy.wait()


def one_minus_exp(u):
    series = jnp.ones_like(u)
    for order in range(9, 1, -1):
        series = 1.0 - u * (1.0 / order) * series
    return jnp.where(u < 0.5, u * series, 1.0 - jnp.exp(-u))


def softplus(v):
    tail = jnp.exp(-jnp.abs(v))
    series = jnp.ones_like(tail)
    for order in range(6, 1, -1):
        series = 1.0 - tail * ((order - 1.0) / order) * series
    return jnp.maximum(v, 0.0) + jnp.where(tail < 0.03, tail * series, jnp.log(1.0 + tail))


def start_cuts(plane, query_ref, key_ref, value_ref, pair_outs, sems):
    layers = len(pair_outs)
    me, _ = seat()
    layer = me // plane
    group = plane * HEAD
    pairs = []
    for step, out_ref in enumerate(pair_outs):
        target = layer ^ step
        pairs.append((query_ref.at[:, lanes(target, group)], out_ref.at[:, pl.ds(0, group)]))
        pairs.append((key_ref.at[:, lanes(target, HEAD)], out_ref.at[:, pl.ds(group, HEAD)]))
        pairs.append(
            (value_ref.at[:, lanes(target, HEAD)], out_ref.at[:, pl.ds(group + HEAD, HEAD)])
        )
    return start_all(pairs, sems)


def scan_kernel(plane, layers, *refs):
    bytes_hbm, gain_ref, input_hbm, step_hbm, rate_ref = refs[:5]
    others, refs = refs[5:8], refs[8:]
    local_ref, through_ref, ends_ref = refs[:3]
    pair_outs, refs = refs[3 : 3 + layers], refs[3 + layers :]
    bytes_ref, input_ref, step_ref, *held, sems, cut_sems = refs
    fetches = start_all(
        [(bytes_hbm, bytes_ref), (step_hbm, step_ref), (input_hbm, input_ref), *zip(others, held)],
        sems,
    )
    fetches[0].wait()
    values = bytes_ref[...].astype(jnp.float32)
    scale = lax.rsqrt(jnp.mean(values * values, axis=1, keepdims=True) + eps)
    normed = (values * scale * gain_ref[...]).astype(jnp.bfloat16)
    fetches[1].wait()
    steps = softplus(jnp.dot(normed, step_ref[...], preferred_element_type=jnp.float32))
    rate_steps = steps * rate_ref[...]
    fetches[2].wait()
    inputs = jnp.dot(normed, input_ref[...], preferred_element_type=jnp.float32)
    for fetch in fetches[3:]:
        fetch.wait()
    cuts = start_cuts(plane, *held, pair_outs, cut_sems)
    decays = jnp.exp(-rate_steps)
    drives = jnp.sqrt(one_minus_exp(2.0 * rate_steps)) * inputs
    rows, width = decays.shape
    tile = 8
    decays = decays.reshape(rows // tile, tile, width)
    drives = drives.reshape(rows // tile, tile, width)
    place = lax.broadcasted_iota(jnp.int32, decays.shape, 1)
    for reach in (1, 2, 4):
        before_decays = pltpu.roll(decays, reach, 1)
        before_drives = pltpu.roll(drives, reach, 1)
        inside = place >= reach
        drives = jnp.where(inside, decays * before_drives + drives, drives)
        decays = jnp.where(inside, decays * before_decays, decays)
    state = jnp.zeros((1, width), jnp.float32)
    kept = jnp.ones((1, width), jnp.float32)
    for index in range(rows // tile):
        states = decays[index] * state + drives[index]
        passing = decays[index] * kept
        local_ref[pl.ds(index * tile, tile), :] = states
        through_ref[pl.ds(index * tile, tile), :] = passing
        state = states[tile - 1 :, :]
        kept = passing[tile - 1 :, :]
    for index in range(ends_ref.shape[0]):
        ends_ref[index, 0:1, :] = kept
        ends_ref[index, 1:2, :] = state
    for cut in cuts:
        cut.wait()


def states_kernel(local_ref, through_ref, mixer_ref, ends_ref, states_ref, other_ref):
    me, lane = seat()
    carry = jnp.zeros((1, local_ref.shape[1]), jnp.float32)
    for shard in range(ends_ref.shape[0]):
        later = ends_ref[shard, 0:1, :] * carry + ends_ref[shard, 1:2, :]
        carry = jnp.where(shard < me, later, carry)
    states = (local_ref[...] + through_ref[...] * carry).astype(jnp.bfloat16)
    states_ref[...] = states
    half = other_ref.shape[1]
    other_ref[...] = jnp.dot(
        states, mixer_ref[:, lanes(1 - lane, half)], preferred_element_type=jnp.float32
    )


def pool_kernel(
    plane, states_ref, mixer_ref, other_ref, bytes_ref, pick_ref, encoded_ref, out_ref
):
    half = other_ref.shape[1]
    columns = lanes(seat()[1], half)
    mixed = jnp.dot(states_ref[...], mixer_ref[:, columns], preferred_element_type=jnp.float32)
    skip = bytes_ref[:, columns].astype(jnp.float32)
    encoded = (skip + (mixed + other_ref[...])).astype(jnp.bfloat16)
    encoded_ref[...] = encoded
    picked = jnp.dot(pick_ref[...], encoded, preferred_element_type=jnp.float32)
    picked = picked.astype(jnp.bfloat16)
    size = out_ref.shape[1]
    for target in range(out_ref.shape[0]):
        start = target % plane * size
        out_ref[target] = picked[start : start + size, :]


def cut_kernel(plane, gate_ref, *refs):
    layers = len(refs) - plane - 3
    pieces, (*outs, held, sems, cut_sems) = refs[:layers], refs[layers:]
    copy_all([(piece, held.at[step]) for step, piece in enumerate(pieces)], sems)
    cross = lax.rem(seat()[0], plane)
    pairs = []
    for mask, out_ref in enumerate(outs):
        size = 2 * out_ref.shape[2] // layers
        for number in range(layers // 2):
            columns = lanes(number * plane + (cross ^ mask), size)
            pairs.append((held.at[:, :, columns], out_ref.at[:, :, pl.ds(number * size, size)]))
    copy_all(pairs, cut_sems)


def own_kernel(pick_ref, arrived_ref, out_ref):
    shards, slots, half = arrived_ref.shape
    rows = arrived_ref[...].reshape(shards * slots, half)
    own = jnp.dot(pick_ref[...], rows, preferred_element_type=jnp.float32)
    out_ref[...] = own.astype(jnp.bfloat16)


def inner_kernel(plane, layers, bias_ref, gain_ref, *refs):
    near, refs = refs[:plane], refs[plane:]
    far, refs = refs[:plane], refs[plane:]
    up_own, refs = refs[:plane], refs[plane:]
    up_far, refs = refs[:plane], refs[plane:]
    pieces, refs = refs[:layers], refs[layers:]
    query_refs, pair_refs, refs = refs[:plane], refs[plane : 2 * plane], refs[2 * plane :]
    pooled, up, weights, squares, queries_held, pairs_held, sems, out_sems = refs
    me, lane = seat()
    layer, cross = me // plane, lax.rem(me, plane)
    near_rows, half = near[0].shape
    up_rows, up_half = up_own[0].shape[1:]
    pairs = []
    for mask in range(plane):
        where = rows_at(cross ^ mask, near_rows)
        pairs.append((near[mask], pooled.at[where, lanes(lane, half)]))
        pairs.append((far[mask], pooled.at[where, lanes(1 - lane, half)]))
    for step in range(layers):
        for mask in range(plane):
            where = rows_at((layer ^ step) * plane + (cross ^ mask), up_rows)
            pairs.append((up_own[mask].at[step], up.at[where, lanes(lane, up_half)]))
            pairs.append((up_far[mask].at[step], up.at[where, lanes(1 - lane, up_half)]))
    for step, piece in enumerate(pieces):
        pairs.append((piece, weights.at[rows_at(layer ^ step, piece.shape[0]), :]))
    copies = start_all(pairs, sems)
    for copy in copies[:-layers]:
        copy.wait()
    rows = pooled.shape[0]
    block = rows // plane
    ones = jnp.ones((8, up.shape[1]), jnp.bfloat16)
    leaving = []
    for index in range(plane):
        where = pl.ds(index * block, block)
        widened = jnp.dot(pooled[where, :], up[...], preferred_element_type=jnp.float32)
        widened = (widened + bias_ref[...]).astype(jnp.bfloat16).astype(jnp.float32)
        inner = (widened * gain_ref[...]).astype(jnp.bfloat16)
        square = widened * widened
        coarse = square.astype(jnp.bfloat16)
        fine = (square - coarse.astype(jnp.float32)).astype(jnp.bfloat16)
        squares[:, where] = sum(
            lax.dot_general(
                ones, part, (((1,), (1,)), ((), ())), preferred_element_type=jnp.float32
            )
            for part in (coarse, fine)
        )
        if index == 0:
            for copy in copies[-layers:]:
                copy.wait()
        sums = jnp.dot(inner, weights[...], preferred_element_type=jnp.float32)
        sums = sums.astype(jnp.bfloat16)
        for head in range(plane):
            queries_held[head, where, :] = sums[:, head * HEAD : (head + 1) * HEAD]
        for number in range(2):
            start = (plane + number) * HEAD
            pairs_held[index, pl.ds(number * block, block), :] = sums[:, start : start + HEAD]
        for mask, out_ref in enumerate(query_refs):
            copy = pltpu.make_async_copy(
                queries_held.at[cross ^ mask, where],
                out_ref.at[where],
                out_sems.at[plane + index * plane + mask],
            )
            copy.start()
            leaving.append(copy)
    total = jnp.concatenate(
        [squares[0:1, start : start + HEAD] for start in range(0, rows, HEAD)], axis=0
    )
    coarse = total.astype(jnp.bfloat16).astype(jnp.float32)
    both = jnp.concatenate([coarse, total - coarse], axis=0).astype(jnp.bfloat16)
    for index in range(plane):
        pairs_held[index, pl.ds(2 * block, both.shape[0]), :] = both
    outs = [(pairs_held.at[cross ^ mask], out_ref) for mask, out_ref in enumerate(pair_refs)]
    copy_all(outs, out_sems)
    for copy in leaving:
        copy.wait()


def added(refs, start, size):
    parts = [ref[pl.ds(start, size), :].astype(jnp.float32) for ref in refs]
    return sum(parts[1:], parts[0])


def row_scale(features, refs, lines):
    both = added(refs, refs[0].shape[0] - 2 * lines, 2 * lines)
    total = both[:lines, :] + both[lines:, :]
    return jnp.transpose(lax.rsqrt(total * (1.0 / features) + eps))


def pairs_kernel(features, lines, *refs):
    got_refs, pair_ref = refs[:-1], refs[-1]
    scale = row_scale(features, got_refs, lines)
    cross = lax.rem(seat()[0], len(got_refs))
    per_block = lines // len(got_refs)
    for line in range(per_block):
        mine = scale[:, line : line + 1]
        for index in range(1, len(got_refs)):
            column = index * per_block + line
            mine = jnp.where(cross == index, scale[:, column : column + 1], mine)
        for number in range(2):
            start = (number * per_block + line) * HEAD
            pair_ref[pl.ds(start, HEAD), :] = (added(got_refs, start, HEAD) * mine).astype(
                jnp.bfloat16
            )


def queries_kernel(features, plane, *refs):
    got_refs, pair_refs, (query_ref, queries) = refs[:plane], refs[plane:-2], refs[-2:]
    rows = query_ref.shape[0]
    lines = rows // HEAD
    shards = rows // CH_OWN
    layers = shards // plane
    scale = row_scale(features, pair_refs, lines)
    for line in range(lines):
        scaled = added(got_refs, line * HEAD, HEAD) * scale[:, line : line + 1]
        for start in range(0, HEAD, CH_OWN):
            index = (line * HEAD + start) // CH_OWN
            shard = (index % layers) * plane + index // layers
            queries[pl.ds(shard, CH_OWN, stride=shards), :] = scaled[start : start + CH_OWN, :]
    query_ref[...] = queries[...].astype(jnp.bfloat16)


def attend_kernel(plane, place_ref, query_ref, *refs):
    pair_refs, (out_ref, natural, keys, values, attended) = refs[:plane], refs[plane:]
    rows = query_ref.shape[0]
    window = out_ref.shape[1]
    part = rows // plane
    shards = rows // CH_OWN
    layers = shards // plane
    cross = lax.rem(seat()[0], plane)
    for number, held in enumerate((keys, values)):
        for mask, pair_ref in enumerate(pair_refs):
            for layer in range(layers):
                piece = pair_ref[pl.ds(number * part + layer * CH_OWN, CH_OWN), :]
                where = pl.ds(layer * plane + (cross ^ mask), CH_OWN, stride=shards)
                natural[where, :] = piece.astype(jnp.float32)
        held[...] = natural[...].astype(jnp.bfloat16)
    block = min(256, rows)
    score_scale = 1.0 / math.sqrt(HEAD)
    for start in range(0, rows, block):
        stop = start + block
        scores = lax.dot_general(
            query_ref[start:stop, :],
            keys[0:stop, :],
            (((1,), (1,)), ((), ())),
            preferred_element_type=jnp.float32,
        )
        spots = lax.broadcasted_iota(jnp.int32, scores.shape, 1)
        mine = lax.broadcasted_iota(jnp.int32, scores.shape, 0) + start
        scores = jnp.where(spots <= mine, scores * score_scale, masked)
        peak = jnp.max(scores, axis=1, keepdims=True)
        lifted = jnp.exp(scores - peak)
        denominator = jnp.sum(lifted, axis=1, keepdims=True)
        weighted = jnp.dot(
            lifted.astype(jnp.bfloat16), values[0:stop, :], preferred_element_type=jnp.float32
        )
        attended[start:stop, :] = (weighted / denominator).astype(jnp.bfloat16)
    attended[rows:, :] = jnp.zeros((attended.shape[0] - rows, HEAD), jnp.bfloat16)
    for shard in range(out_ref.shape[0]):
        first = place_ref[shard]
        out_ref[shard] = attended[pl.ds(pl.multiple_of(first * TILE, TILE), window), :]


def return_kernel(weight_ref, pieces_ref, own_ref, other_ref, attended):
    half = own_ref.shape[1]
    lane = seat()[1]
    for head in range(pieces_ref.shape[0]):
        attended[:, head * HEAD : (head + 1) * HEAD] = pieces_ref[head]
    other_ref[...] = jnp.dot(
        attended[...], weight_ref[:, lanes(1 - lane, half)], preferred_element_type=jnp.float32
    )
    own_ref[...] = jnp.dot(
        attended[...], weight_ref[:, lanes(lane, half)], preferred_element_type=jnp.float32
    )


def join_kernel(own_ref, other_ref, encoded_ref, spread_ref, out_ref):
    returned = (own_ref[...] + other_ref[...]).astype(jnp.bfloat16)
    results = jnp.dot(spread_ref[...], returned, preferred_element_type=jnp.float32)
    out_ref[...] = (encoded_ref[...].astype(jnp.float32) + results).astype(jnp.bfloat16)


def one_head_each(
    byte_states,
    outer_gain,
    mamba_input,
    mamba_step,
    decay_rate,
    mixer_weight,
    boundaries,
    span_counts,
    up_weight,
    up_bias,
    inner_gain,
    query_weight,
    key_weight,
    value_weight,
    return_weight,
):
    shards = lax.axis_size("seq")
    me = lax.axis_index("seq")
    lane = lax.axis_index("mp")
    plane = HEADS // KV_HEADS
    layers = shards // plane
    rows_here, width = byte_states.shape
    half = mamba_input.shape[1]
    capacity = boundaries.shape[1]
    window = capacity + TILE
    total_rows = CH_OWN * shards
    inner_width = inner_gain.shape[0]
    inner_half = up_bias.shape[0]
    weight_rows = query_weight.shape[0]
    f32, bf16 = jnp.float32, jnp.bfloat16
    layer, cross = me // plane, me % plane

    def over(value, mask):
        return lax.ppermute(value, "seq", [(i, i ^ mask) for i in range(shards)])

    def after(value, done):
        return lax.optimization_barrier((value, done))[0]

    own_bias = up_bias.reshape(layers // 2, plane, weight_rows)
    own_bias = lax.dynamic_index_in_dim(own_bias, cross, 1, keepdims=False).reshape(1, -1)
    own_gain = inner_gain.reshape(layers, plane, weight_rows)
    own_gain = lax.dynamic_index_in_dim(own_gain, cross, 1, keepdims=False).reshape(1, -1)

    seq_ids = jnp.arange(shards, dtype=jnp.int32)
    offsets = jnp.cumsum(span_counts) - span_counts
    own_offset = jnp.sum(jnp.where(seq_ids == me, offsets, 0))
    own_count = jnp.sum(jnp.where(seq_ids == me, span_counts, 0))
    place = offsets // TILE
    own_marks = boundaries[0]
    positions = jnp.arange(rows_here, dtype=jnp.int32)
    spans_here = jnp.arange(capacity, dtype=jnp.int32)
    live = spans_here < own_count
    slots = capacity // shards
    slot_ids = jnp.arange(slots, dtype=jnp.int32)
    owners = seq_ids.reshape(layers, plane).T
    local_span = slot_ids * shards + ((owners - own_offset) % shards)[:, :, None]
    is_span = spans_here[None, :] == local_span.reshape(-1)[:, None]
    byte_at = jnp.sum(jnp.where(is_span, jnp.minimum(own_marks, rows_here - 1)[None, :], 0), axis=1)
    pool_pick = (positions[None, :] == byte_at[:, None]).astype(bf16)
    near_owner = jnp.arange(layers, dtype=jnp.int32) * plane + cross
    near_spans = near_owner[:, None] + jnp.arange(CH_OWN, dtype=jnp.int32)[None, :] * shards
    origin = jnp.sum((offsets <= near_spans[:, :, None]).astype(jnp.int32), axis=2) - 1
    origin_offset = jnp.sum(jnp.where(seq_ids == origin[:, :, None], offsets, 0), axis=2)
    arrived_row = (
        origin * (layers * slots)
        + jnp.arange(layers, dtype=jnp.int32)[:, None] * slots
        + (near_spans - origin_offset) // shards
    ).reshape(-1)
    near_pick = (
        jnp.arange(shards * layers * slots, dtype=jnp.int32)[None, :] == arrived_row[:, None]
    ).astype(bf16)
    passed = jnp.sum(
        ((own_marks[None, :] <= positions[:, None]) & live[None, :]).astype(jnp.int32), axis=1
    )
    result_row = passed - 1 + own_offset % TILE
    spread = (jnp.arange(window, dtype=jnp.int32)[None, :] == result_row[:, None]).astype(bf16)

    up_half = inner_half // plane
    up_layers = [up_weight] + [over(up_weight, plane * step) for step in range(1, layers)]

    local, through, ends, *pair_cuts = pl.pallas_call(
        functools.partial(scan_kernel, plane, layers),
        out_shape=(
            jax.ShapeDtypeStruct((rows_here, half), f32),
            jax.ShapeDtypeStruct((rows_here, half), f32),
            jax.ShapeDtypeStruct((shards, 2, half), f32),
        )
        + (jax.ShapeDtypeStruct((weight_rows, (plane + 2) * HEAD), bf16),) * layers,
        in_specs=[in_hbm(), vmem(), in_hbm(), in_hbm(), vmem()] + [in_hbm()] * 3,
        out_specs=(vmem(),) * 3 + (in_place(),) * layers,
        scratch_shapes=[
            pltpu.VMEM(array.shape, bf16)
            for array in (
                byte_states,
                mamba_input,
                mamba_step,
                query_weight,
                key_weight,
                value_weight,
            )
        ]
        + [pltpu.SemaphoreType.DMA((6,)), pltpu.SemaphoreType.DMA((3 * layers,))],
        cost_estimate=brief(),
        compiler_params=params(56),
    )(
        byte_states,
        outer_gain[None, :],
        mamba_input,
        mamba_step,
        decay_rate[None, :],
        query_weight,
        key_weight,
        value_weight,
    )
    ends = lax.all_to_all(ends, "seq", 0, 0, tiled=True)
    ends, up_layers = lax.optimization_barrier((ends, up_layers))
    pieces = [pair_cuts[0]] + [over(pair_cuts[step], plane * step) for step in range(1, layers)]
    states, other_part = pl.pallas_call(
        states_kernel,
        out_shape=(
            jax.ShapeDtypeStruct((rows_here, half), bf16),
            jax.ShapeDtypeStruct((rows_here, half), f32),
        ),
        in_specs=[vmem()] * 4,
        out_specs=(vmem(),) * 2,
        cost_estimate=brief(),
        compiler_params=params(56),
    )(local, through, mixer_weight, ends)
    far_bias = swapped(own_bias)
    bias = jnp.where(
        lane == 0,
        jnp.concatenate([own_bias, far_bias], axis=1),
        jnp.concatenate([far_bias, own_bias], axis=1),
    )
    far_part, bias, pieces[1] = lax.optimization_barrier((swapped(other_part), bias, pieces[1]))
    encoded, leaving = pl.pallas_call(
        functools.partial(pool_kernel, plane),
        out_shape=(
            jax.ShapeDtypeStruct((rows_here, half), bf16),
            jax.ShapeDtypeStruct((shards, layers * slots, half), bf16),
        ),
        in_specs=[vmem()] * 5,
        out_specs=(vmem(),) * 2,
        cost_estimate=brief(),
        compiler_params=params(56),
    )(states, mixer_weight, far_part, byte_states, pool_pick)
    arrived = lax.all_to_all(leaving, "seq", 0, 0, tiled=True)
    up_cuts = pl.pallas_call(
        functools.partial(cut_kernel, plane),
        out_shape=(jax.ShapeDtypeStruct((layers, up_weight.shape[0], up_half), bf16),) * plane,
        in_specs=[in_place()] * (1 + layers),
        out_specs=(in_place(),) * plane,
        scratch_shapes=[
            pltpu.VMEM((layers, *up_weight.shape), bf16),
            pltpu.SemaphoreType.DMA((layers,)),
            pltpu.SemaphoreType.DMA((plane * layers // 2,)),
        ],
        cost_estimate=brief(),
        compiler_params=params(56),
    )(leaving, *up_layers)
    up_own = [up_cuts[0]] + [over(up_cuts[mask], mask) for mask in range(1, plane)]
    arrived, pieces, up_own = lax.optimization_barrier((arrived, pieces, up_own))
    near_rows = pl.pallas_call(
        own_kernel,
        out_shape=jax.ShapeDtypeStruct((layers * CH_OWN, half), bf16),
        in_specs=[vmem()] * 2,
        out_specs=vmem(),
        cost_estimate=brief(),
        compiler_params=params(56),
    )(near_pick, arrived)
    near_rows, up_far = lax.optimization_barrier(
        (near_rows, [swapped(piece) for piece in up_own])
    )
    near = [near_rows] + [over(near_rows, mask) for mask in range(1, plane)]
    far = [swapped(piece) for piece in near]

    features = own_gain.shape[1]
    block = total_rows // plane
    lines = total_rows // HEAD
    pair_rows = 2 * block + 2 * lines
    partial_sums = pl.pallas_call(
        functools.partial(inner_kernel, plane, layers),
        out_shape=(jax.ShapeDtypeStruct((total_rows, HEAD), bf16),) * plane
        + (jax.ShapeDtypeStruct((pair_rows, HEAD), bf16),) * plane,
        in_specs=[vmem()] * 2 + [in_place()] * (4 * plane + layers),
        out_specs=(in_place(),) * (2 * plane),
        scratch_shapes=[
            pltpu.VMEM((total_rows, width), bf16),
            pltpu.VMEM((width, features), bf16),
            pltpu.VMEM((features, (plane + 2) * HEAD), bf16),
            pltpu.VMEM((8, total_rows), f32),
            pltpu.VMEM((plane, total_rows, HEAD), bf16),
            pltpu.VMEM((plane, pair_rows, HEAD), bf16),
            pltpu.SemaphoreType.DMA((2 * plane + 2 * shards + layers,)),
            pltpu.SemaphoreType.DMA((plane + plane * plane,)),
        ],
        cost_estimate=brief(),
        compiler_params=params(56),
    )(bias, own_gain, *near, *far, *up_own, *up_far, *pieces)
    query_sums, pair_sums = partial_sums[:plane], partial_sums[plane:]
    got_pairs = [pair_sums[0]] + [over(pair_sums[mask], mask) for mask in range(1, plane)]
    got_queries = [query_sums[0]] + [over(query_sums[mask], mask) for mask in range(1, plane)]
    pairs = pl.pallas_call(
        functools.partial(pairs_kernel, inner_width, lines),
        out_shape=jax.ShapeDtypeStruct((2 * block, HEAD), bf16),
        in_specs=[vmem()] * plane,
        out_specs=vmem(),
        cost_estimate=brief(),
        compiler_params=params(8),
    )(*got_pairs)
    whole_pairs = [pairs] + [over(pairs, mask) for mask in range(1, plane)]
    queries = pl.pallas_call(
        functools.partial(queries_kernel, inner_width, plane),
        out_shape=jax.ShapeDtypeStruct((total_rows, HEAD), bf16),
        in_specs=[vmem()] * (2 * plane),
        out_specs=vmem(),
        scratch_shapes=[pltpu.VMEM((total_rows, HEAD), f32)],
        cost_estimate=brief(),
        compiler_params=params(10),
    )(*got_queries, *got_pairs)
    leaving = pl.pallas_call(
        functools.partial(attend_kernel, plane),
        out_shape=jax.ShapeDtypeStruct((shards, window, HEAD), bf16),
        in_specs=[smem()] + [vmem()] * (1 + plane),
        out_specs=vmem(),
        scratch_shapes=[
            pltpu.VMEM((total_rows, HEAD), f32),
            pltpu.VMEM((total_rows, HEAD), bf16),
            pltpu.VMEM((total_rows, HEAD), bf16),
            pltpu.VMEM((total_rows + window, HEAD), bf16),
        ],
        cost_estimate=brief(),
        compiler_params=params(12),
    )(place, queries, *whole_pairs)
    pieces = lax.all_to_all(leaving, "seq", 0, 0, tiled=True)
    own_back, other_back = pl.pallas_call(
        return_kernel,
        out_shape=(jax.ShapeDtypeStruct((window, half), f32),) * 2,
        in_specs=[vmem()] * 2,
        out_specs=(vmem(),) * 2,
        scratch_shapes=[pltpu.VMEM((window, shards * HEAD), bf16)],
        cost_estimate=brief(),
        compiler_params=params(12),
    )(return_weight, pieces)
    return pl.pallas_call(
        join_kernel,
        out_shape=jax.ShapeDtypeStruct((rows_here, half), bf16),
        in_specs=[vmem()] * 4,
        out_specs=vmem(),
        cost_estimate=brief(),
        compiler_params=params(8),
    )(own_back, swapped(other_back), encoded, spread)


def prefix(value, axis, join, neutral):
    count, mine = (lax.axis_size(axis), lax.axis_index(axis))
    pieces = jax.tree.map(lambda part: lax.all_gather(part, axis), value)
    so_far = jax.tree.map(
        lambda part, zero: jnp.full_like(part, 0) + jnp.asarray(zero, part.dtype), value, neutral
    )

    def lap(position, so_far):
        longer = join(so_far, jax.tree.map(lambda part: part[position], pieces))
        return jax.tree.map(lambda new, old: jnp.where(position < mine, new, old), longer, so_far)

    return lax.fori_loop(0, count - 1, lap, so_far)


def rms_scale(values, gain):
    values = values.astype(jnp.float32)
    return values * lax.rsqrt(jnp.mean(values * values, axis=-1, keepdims=True) + eps) * gain


def combine_pairs(earlier, later):
    return (earlier[0] * later[0], later[0] * earlier[1] + later[1])


def pick_table(table, wanted, seq_ids):
    return jnp.sum(jnp.where(seq_ids[None, :] == wanted[:, None], table[None, :], 0), axis=1)


def block_size(piece_rows, shard_rows):
    limit = max(1, 1024 // shard_rows)
    pieces = max(1, piece_rows // shard_rows)
    best_size = 1
    for candidate in range(1, limit + 1):
        if pieces % candidate == 0:
            best_size = candidate
    return min(piece_rows, best_size * shard_rows)


def spread_heads(
    byte_states,
    outer_gain,
    mamba_input,
    mamba_step,
    decay_rate,
    mixer_weight,
    boundaries,
    span_counts,
    up_weight,
    up_bias,
    inner_gain,
    query_weight,
    key_weight,
    value_weight,
    return_weight,
):
    shards = lax.axis_size("seq")
    own_shard = lax.axis_index("seq")
    own_lane = lax.axis_index("mp")
    rows_here = byte_states.shape[0]
    capacity = boundaries.shape[1]
    column_count = mamba_input.shape[1]
    kv_local = key_weight.shape[1] // HEAD
    group_size = HEADS // KV_HEADS
    slot_count = capacity // shards
    offsets = jnp.cumsum(span_counts) - span_counts
    seq_ids = jnp.arange(shards, dtype=jnp.int32)
    own_offset = jnp.sum(jnp.where(seq_ids == own_shard, offsets, 0))
    own_count = jnp.sum(jnp.where(seq_ids == own_shard, span_counts, 0))
    normed = rms_scale(byte_states, outer_gain).astype(jnp.bfloat16)
    inputs = jnp.dot(normed, mamba_input, preferred_element_type=jnp.float32)
    step_sizes = jax.nn.softplus(jnp.dot(normed, mamba_step, preferred_element_type=jnp.float32))
    rate_steps = step_sizes * decay_rate
    decays = jnp.exp(-rate_steps)
    drives = jnp.sqrt(-jnp.expm1(-2.0 * rate_steps)) * inputs
    through, local_states = lax.associative_scan(combine_pairs, (decays, drives), axis=0)
    starting = (jnp.ones((column_count,), jnp.float32), jnp.zeros((column_count,), jnp.float32))
    arriving = prefix((through[-1], local_states[-1]), "seq", combine_pairs, starting)
    states = (local_states + through * arriving[1][None, :]).astype(jnp.bfloat16)
    partial_value = jnp.dot(states, mixer_weight, preferred_element_type=jnp.float32)
    mixed_sum = lax.psum(partial_value, "mp")
    encoded = (byte_states.astype(jnp.float32) + mixed_sum).astype(jnp.bfloat16)
    skip_part = lax.dynamic_slice_in_dim(encoded, own_lane * column_count, column_count, 1)
    own_marks = boundaries[0]
    pooled = encoded[jnp.minimum(own_marks, rows_here - 1)]
    row_width = pooled.shape[1]
    outgoing = jnp.roll(pooled.reshape(slot_count, shards, row_width), own_offset % shards, axis=1)
    incoming = lax.all_to_all(outgoing, "seq", split_axis=1, concat_axis=1, tiled=True)
    position = jnp.arange(CH_OWN, dtype=jnp.int32)
    span_index = own_shard + position * shards
    source = jnp.sum((offsets[None, :] <= span_index[:, None]).astype(jnp.int32), axis=1) - 1
    source_offset = pick_table(offsets, source, seq_ids)
    slot_index = (span_index - source_offset) // shards
    gathered_rows = incoming.reshape(slot_count * shards, row_width)[slot_index * shards + source]
    columns = gathered_rows
    widened_sum = jnp.dot(
        columns,
        lax.all_gather(up_weight, "seq", axis=0, tiled=True),
        preferred_element_type=jnp.float32,
    )
    widened_share = (widened_sum + up_bias[None, :]).astype(jnp.bfloat16)
    widened = lax.all_gather(widened_share, "mp", axis=1, tiled=True)
    inner_normed = rms_scale(widened, inner_gain).astype(jnp.bfloat16)
    columns = inner_normed
    query_part = jnp.dot(
        columns,
        lax.all_gather(query_weight, "seq", axis=0, tiled=True),
        preferred_element_type=jnp.float32,
    )
    key_part = jnp.dot(
        columns,
        lax.all_gather(key_weight, "seq", axis=0, tiled=True),
        preferred_element_type=jnp.float32,
    )
    value_part = jnp.dot(
        columns,
        lax.all_gather(value_weight, "seq", axis=0, tiled=True),
        preferred_element_type=jnp.float32,
    )
    queries = query_part.astype(jnp.bfloat16)
    key_rows = key_part.astype(jnp.bfloat16)
    value_rows = value_part.astype(jnp.bfloat16)
    query_count = queries.shape[0]
    grouped = (
        queries.reshape(query_count, kv_local, group_size, HEAD)
        .transpose(1, 0, 2, 3)
        .reshape(kv_local, query_count * group_size, HEAD)
    )
    row_index = jnp.repeat(span_index, group_size)
    shard_rows = key_rows.shape[0]
    score_scale = 1.0 / math.sqrt(HEAD)

    def key_index(whole_index):
        return whole_index // shard_rows + whole_index % shard_rows * shards

    def attend_block(running, key_block, value_block, index_block):
        row_peak, denominator, weighted = running
        scores = (
            jnp.einsum("hqd,khd->hqk", grouped, key_block, preferred_element_type=jnp.float32)
            * score_scale
        )
        scores = jnp.where(index_block[None, None, :] <= row_index[None, :, None], scores, masked)
        new_peak = jnp.maximum(row_peak, jnp.max(scores, axis=2))
        shrink = jnp.exp(row_peak - new_peak)
        lifted = jnp.exp(scores - new_peak[:, :, None])
        denominator = denominator * shrink + jnp.sum(lifted, axis=2)
        weighted = weighted * shrink[:, :, None] + jnp.einsum(
            "hqk,khd->hqd",
            lifted.astype(jnp.bfloat16),
            value_block,
            preferred_element_type=jnp.float32,
        )
        return (new_peak, denominator, weighted)

    query_total = query_count * group_size
    initial = (
        jnp.full((kv_local, query_total), masked, jnp.float32),
        jnp.zeros((kv_local, query_total), jnp.float32),
        jnp.zeros((kv_local, query_total, HEAD), jnp.float32),
    )
    key_piece = lax.all_gather(key_rows, "seq", axis=0, tiled=True)
    value_piece = lax.all_gather(value_rows, "seq", axis=0, tiled=True)
    piece_rows = key_piece.shape[0]
    block_rows = block_size(piece_rows, shard_rows)
    turn_count = piece_rows // block_rows
    key_blocks = key_piece.reshape(turn_count, block_rows, kv_local, HEAD)
    value_blocks = value_piece.reshape(turn_count, block_rows, kv_local, HEAD)

    def one_turn(turn_index, inner_running):
        whole_index = turn_index * block_rows + jnp.arange(block_rows, dtype=jnp.int32)
        return attend_block(
            inner_running, key_blocks[turn_index], value_blocks[turn_index], key_index(whole_index)
        )

    row_peak, denominator, weighted = lax.fori_loop(0, turn_count, one_turn, initial)
    attended = (weighted / denominator[:, :, None]).astype(jnp.bfloat16)
    attended = (
        attended.reshape(kv_local, query_count, group_size, HEAD)
        .transpose(1, 0, 2, 3)
        .reshape(query_count, kv_local * group_size * HEAD)
    )
    projected = jnp.dot(attended, return_weight, preferred_element_type=jnp.float32)
    returned = lax.psum_scatter(
        projected.astype(jnp.bfloat16), "mp", scatter_dimension=1, tiled=True
    )
    slot_ids = jnp.arange(slot_count, dtype=jnp.int32)
    lead_slot = (own_shard - offsets) % shards
    local_span = slot_ids[:, None] * shards + lead_slot[None, :]
    back_index = (offsets[None, :] + local_span - own_shard) // shards
    alive = local_span < span_counts[None, :]
    back_rows = jnp.where(
        alive[:, :, None],
        returned[jnp.clip(back_index, 0, CH_OWN - 1)],
        jnp.zeros((), jnp.bfloat16),
    )
    arrived = lax.all_to_all(back_rows, "seq", split_axis=1, concat_axis=1, tiled=True)
    span_results = jnp.roll(arrived, -(own_offset % shards), axis=1).reshape(capacity, column_count)
    positions = jnp.arange(rows_here, dtype=jnp.int32)
    live_slots = jnp.arange(capacity, dtype=jnp.int32) < own_count
    passed = jnp.sum(
        ((own_marks[None, :] <= positions[:, None]) & live_slots[None, :]).astype(jnp.int32), axis=1
    )
    return (skip_part.astype(jnp.float32) + span_results[passed - 1].astype(jnp.float32)).astype(
        jnp.bfloat16
    )


def solution(mesh):
    in_specs = (
        P("seq", None),
        P(),
        P(None, "mp"),
        P(None, "mp"),
        P("mp"),
        P("mp", None),
        P("seq", None),
        P(),
        P("seq", "mp"),
        P("mp"),
        P(),
        P("seq", "mp"),
        P("seq", "mp"),
        P("seq", "mp"),
        P("mp", None),
    )
    out_specs = P("seq", "mp")
    def on_device(*arrays):
        heads_here = arrays[11].shape[1] // HEAD
        fits = heads_here == mesh.shape["seq"] and mesh.shape["mp"] == 2
        return (one_head_each if fits else spread_heads)(*arrays)

    return jax.shard_map(
        on_device, mesh=mesh, in_specs=in_specs, out_specs=out_specs, check_vma=False
    )
```
